32 devices in a mesh: row: 4 (over y, x), col: 4 (over z), exp: 2 (over core).
Axes of the slice: x: 2, y: 2, z: 4, core: 2. Of those that a mesh axis runs over, the one named last changes fastest.
Arguments:
- hidden_in: bfloat16 [2, 2048, 2048], P('exp', ('row', 'col')), may hold values from -6 to 6
- out_grad: bfloat16 [2, 2048, 2048], P('exp', ('row', 'col')), may hold values from -6 to 6
- attn_gain: bfloat16 [2048], replicated, may hold values from 0.5 to 1.5
- w_qkv: bfloat16 [2048, 6144], P('row', 'col'), may hold values from -0.125 to 0.125
- q_gain: bfloat16 [2048], replicated, may hold values from 0.796875 to 1.796875
- k_gain: bfloat16 [2048], replicated, may hold values from 0.796875 to 1.796875
- w_out: bfloat16 [2048, 2048], P('col', 'row'), may hold values from -0.5 to 0.5
- moe_gain: bfloat16 [2048], replicated, may hold values from 0.5 to 1.5
- router: bfloat16 [2048, 16], replicated, may hold values from -0.0625 to 0.0625
- w_gate: bfloat16 [32, 2048, 512], P(('row', 'col', 'exp')), may hold values from -0.125 to 0.125
- w_up: bfloat16 [32, 2048, 512], P(('row', 'col', 'exp')), may hold values from -0.125 to 0.125
- w_down: bfloat16 [32, 512, 2048], P(('row', 'col', 'exp')), may hold values from -6 to 6
- routes: int32 [2, 2048, 8], P('exp', ('row', 'col')), may hold values from 0 to 15, all different within a row; in each aligned block of 128 rows (0 to 127, 128 to 255, ..., all dimensions but the last counted through in order) at most 128 rows name the same one
- doc_cuts: int32 [1, 2], replicated, may hold values from 1 to 4095, as said below
Outputs:
- out_hidden: bfloat16 [2, 2048, 2048], P('exp', ('row', 'col'))
- grad_hidden: float32 [2, 2048, 2048], P('exp', ('row', 'col'))
- grad_attn_gain: float32 [2048], replicated
- grad_qkv: float32 [2048, 6144], P('row', 'col')
- grad_q_gain: float32 [2048], replicated
- grad_k_gain: float32 [2048], replicated
- grad_w_out: float32 [2048, 2048], P('col', 'row')
- grad_moe_gain: float32 [2048], replicated
- grad_router: float32 [2048, 16], replicated
- grad_gate: float32 [32, 2048, 512], P(('row', 'col', 'exp'))
- grad_up: float32 [32, 2048, 512], P(('row', 'col', 'exp'))
- grad_down: float32 [32, 512, 2048], P(('row', 'col', 'exp'))
The draws below stay inside these ranges and needn't reach their ends.
Inputs may be any that keep to these rules, and one draw needn't show every extreme that they name: `routes`: each token names 8 different experts. In each aligned block of 128 tokens (the tokens of one device) no expert is named by more than 128 tokens, a bound that some block reaches. A sequence's documents are its tokens before doc_cuts[s, 0], those from doc_cuts[s, 0] up to doc_cuts[s, 1], and the rest; doc_cuts[s, 0] is at most 64 and doc_cuts[s, 1] at least 4032.
All inputs are finite; a program needn't handle non-finite values.
Results may differ from the reference program's by a relative error of at most 0.024.
Values may be sent and summed in bfloat16 or wider, within the bound.
A program may use at most 320 MiB of HBM per device.

```python
import math
import jax
import jax.numpy as jnp
import numpy as np
from jax import lax

D = 2048
H = 16
HD = 128
FF = 1024
TOPK = 8
TOK_DEV = 128
GROUPS = 2
GROUP_TOK = 2048
SEQS = 1
SEQ_TOK = 4096
TOKENS = 4096
EXPERTS = 16
HALF = 512
CAP = 128
DEVICES = 32


def draw_doc_cuts(key, part):
    key = jax.random.fold_in(key, 7)
    first_key, second_key = jax.random.split(key)
    first = jax.random.randint(first_key, (SEQS,), 1, TOK_DEV // 2 + 1)
    second = SEQ_TOK - jax.random.randint(second_key, (SEQS,), 1, TOK_DEV // 2 + 1)
    return jnp.stack([first, second], axis=1).astype(jnp.int32)


def levels(key, shape, cuts, least, high):
    level, own = 1.0, jax.random.fold_in(key, 6)
    for dim, blocks in cuts:
        draws = jnp.exp(jax.random.uniform(jax.random.fold_in(own, dim), (blocks,), jnp.float32, least / len(cuts), high / len(cuts)))
        level = level * jnp.repeat(draws, shape[dim] // blocks).reshape([-1 if axis == dim else 1 for axis in range(len(shape))])
    return level


def shared_out(stream_key, own, number, rows, amount, top, limit, lean):
    order = jax.random.permutation(stream_key, amount)
    heavy_load, usual = shares(amount, rows * top, limit, lean, True), shares(amount, rows * top, limit, lean, False)
    places = jnp.arange(amount)

    def named(lengths, rotation):
        used = int((lengths > 0).sum())
        fixed = max(1, used // 4)
        moved = fixed + (places - fixed + rotation * (used - fixed)) % max(1, amount - fixed)
        return jnp.zeros((amount,), jnp.int32).at[order[jnp.where(places < fixed, places, moved)]].set(jnp.asarray(lengths, jnp.int32))

    lengths = jnp.where(number % 4 == 0, named(heavy_load, number // 4), named(usual, number - number // 4 - 1))
    mixed = jax.random.permutation(jax.random.fold_in(own, 3), amount)
    donor, receiver = mixed[0:amount // 2 * 2:2], mixed[1:amount // 2 * 2:2]
    room = jnp.minimum(lengths[donor] - 1, limit - lengths[receiver]) // 2
    room = jnp.where((donor == order[0]) | (receiver == order[0]) | (lengths[receiver] == 0), 0, jnp.maximum(room, 0))
    moved = jax.random.randint(jax.random.fold_in(own, 4), (amount // 2,), 0, 1 << 20) % (room + 1)
    lengths = lengths.at[donor].add(-moved).at[receiver].add(moved)
    labels = jnp.searchsorted(jnp.cumsum(lengths), jnp.arange(rows * top), side="right").astype(jnp.int32)
    grid = labels.reshape(top, rows).T
    grid = grid[jax.random.permutation(jax.random.fold_in(own, 1), rows)]
    rotation = jax.random.randint(jax.random.fold_in(own, 2), (rows, 1), 0, top)
    return jnp.take_along_axis(grid, (jnp.arange(top)[None, :] + rotation) % top, axis=1)


def shares(count, total, most, lean, full):
    loads = [(1 << 20) // math.isqrt(standing ** lean) + 1 for standing in range(1, count + 1)]
    largest = most if full else min(most, max(-(-total // count), total * loads[0] // sum(loads)))
    least = 1 if total - largest >= count - 1 else 0
    counts, surplus = [largest] + [least] * (count - 1), total - largest - least * (count - 1)
    while surplus > 0:
        free = [i for i in range(1, count) if counts[i] < largest] or [i for i in range(1, count) if counts[i] < most]
        pool, left = sum([loads[i] for i in free]), surplus
        for i in free:
            extra = min(most - counts[i], max(1, left * loads[i] // pool), surplus)
            counts[i] = counts[i] + extra
            surplus = surplus - extra
    return np.array(counts)


def gaussian(key, dims, spread, bound, shards=(), kind=jnp.bfloat16):
    values = jax.random.normal(key, dims, jnp.float32) * spread
    if len(shards) > 0:
        values = levels(key, dims, shards, -0.22, 0.18) * values
    return jnp.clip(values, min=-bound, max=bound).astype(kind)


def setup_inputs(seed: int = 0) -> dict:
    key_list = jax.random.split(jax.random.key(seed), 15)
    hidden_in = gaussian(key_list[0], (GROUPS, GROUP_TOK, D), 1.0, 6.0, ((0, 2), (1, 16)))
    out_grad = gaussian(key_list[1], (GROUPS, GROUP_TOK, D), 1.0, 6.0, ((0, 2), (1, 16)))
    attn_gain = jnp.clip(1.0 + 0.1 * jax.random.normal(key_list[2], (D,), jnp.float32), 0.5, 1.5).astype(jnp.bfloat16)
    w_qkv = gaussian(key_list[3], (D, 3 * D), D ** -0.5, 0.125, ((0, 4), (1, 4)))
    q_gain = jnp.clip(jax.random.uniform(key_list[4], (D,), jnp.float32, 0.796875, 1.796875), 0.796875, 1.796875).astype(jnp.bfloat16)
    k_gain = jnp.clip(jax.random.uniform(key_list[5], (D,), jnp.float32, 0.796875, 1.796875), 0.796875, 1.796875).astype(jnp.bfloat16)
    w_out = gaussian(key_list[6], (D, D), (D // 16) ** -0.5, 0.5, ((0, 4), (1, 4)))
    moe_gain = jnp.clip(1.0 + 0.1 * jax.random.normal(key_list[7], (D,), jnp.float32), 0.5, 1.5).astype(jnp.bfloat16)
    router = gaussian(key_list[8], (D, EXPERTS), (4 * D) ** -0.5, 0.0625)
    w_gate = gaussian(key_list[9], (2 * EXPERTS, D, HALF), D ** -0.5, 0.125, ((0, 32),))
    w_up = gaussian(key_list[10], (2 * EXPERTS, D, HALF), D ** -0.5, 0.125, ((0, 32),))
    w_down = gaussian(key_list[11], (2 * EXPERTS, HALF, D), 1 ** -0.5, 6.0, ((0, 32),))
    routes_keys = jax.random.split(jax.random.fold_in(key_list[12], 1), GROUPS * GROUP_TOK // TOK_DEV)
    routes_turns = jax.random.permutation(jax.random.fold_in(key_list[12], 3), GROUPS * GROUP_TOK // TOK_DEV)
    routes = jax.vmap(lambda own, number: shared_out(jax.random.fold_in(key_list[12], 2), own, number, TOK_DEV, EXPERTS, TOPK, CAP, 1))(routes_keys, routes_turns).reshape((GROUPS, GROUP_TOK, TOPK))
    doc_cuts = draw_doc_cuts(jax.random.fold_in(key_list[14], 71), 0)
    return {"hidden_in": hidden_in, "out_grad": out_grad, "attn_gain": attn_gain, "w_qkv": w_qkv, "q_gain": q_gain, "k_gain": k_gain, "w_out": w_out, "moe_gain": moe_gain, "router": router, "w_gate": w_gate, "w_up": w_up, "w_down": w_down, "routes": routes, "doc_cuts": doc_cuts}


EPSILON = 1e-05
ROPE_BASE = 10000.0
MASKED = -1e+30
HIGHEST = lax.Precision.HIGHEST

@jax.custom_vjp
def low(v):
    return lax.optimization_barrier(v.astype(jnp.bfloat16)).astype(jnp.float32)

@jax.custom_vjp
def low_back(v):
    return v

def low_keep(v):
    return (low(v), None)

def low_pass(kept, grad):
    return (grad,)

def back_keep(v):
    return (v, None)

def back_low(kept, grad):
    return (low(grad),)
low.defvjp(low_keep, low_pass)
low_back.defvjp(back_keep, back_low)

def rms_scale(values):
    return lax.rsqrt(lax.optimization_barrier(jnp.mean(values * values, axis=-1, keepdims=True)) + EPSILON)

def rope_tables(position, width):
    frequency = ROPE_BASE ** (-jnp.arange(0, width, 2, dtype=jnp.float32) / width)
    angle = position.astype(jnp.float32)[:, None] * frequency[None, :]
    return (jnp.concatenate([jnp.cos(angle)] * 2, axis=-1), jnp.concatenate([jnp.sin(angle)] * 2, axis=-1))

def rotate(values, cosine, sine):
    half = values.shape[-1] // 2
    turned = jnp.concatenate([-values[..., half:], values[..., :half]], axis=-1)
    return values * cosine + turned * sine

def doc_positions(places, cuts):
    first = (places >= cuts[0]).astype(jnp.int32)
    second = (places >= cuts[1]).astype(jnp.int32)
    start = first * cuts[0] + second * (cuts[1] - cuts[0])
    return (first + second, places - start)

def run_experts(normed, probs, routes, w_gate, w_up, w_down):
    pairs = routes.reshape(-1)
    most = DEVICES * CAP
    gate_all = w_gate.reshape(EXPERTS, 2, D, HALF).transpose(0, 2, 1, 3).reshape(EXPERTS, D, FF)
    up_all = w_up.reshape(EXPERTS, 2, D, HALF).transpose(0, 2, 1, 3).reshape(EXPERTS, D, FF)
    down_all = w_down.reshape(EXPERTS, FF, D)

    def one_expert(carry, pieces):
        expert, gate_w, up_w, down_w = pieces
        hit = pairs == expert
        found = jnp.nonzero(hit, size=most, fill_value=0)[0].astype(jnp.int32)
        valid = (jnp.arange(most, dtype=jnp.int32) < jnp.sum(hit.astype(jnp.int32))).astype(jnp.float32)
        token = found // TOPK
        rows = normed[token]
        weight = probs[token, expert] * valid
        pre_gate = low_back(jnp.dot(rows, gate_w, precision=HIGHEST))
        pre_up = low_back(jnp.dot(rows, up_w, precision=HIGHEST))
        hidden = low(jax.nn.silu(pre_gate) * pre_up)
        result = low_back(jnp.dot(hidden, down_w, precision=HIGHEST))
        return (carry.at[token].add(weight[:, None] * result), None)
    start = jnp.zeros((TOKENS, D), jnp.float32)
    total, unused = lax.scan(jax.checkpoint(one_expert), start, (jnp.arange(EXPERTS, dtype=jnp.int32), gate_all, up_all, down_all))
    return total

def forward(hidden, attn_gain, w_qkv, q_gain, k_gain, w_out, moe_gain, router, w_gate, w_up, w_down, routes, doc_cuts):
    scale = HD ** (-0.5)

    def sequence_attention(pieces):
        tokens, cuts = pieces
        normed = low(tokens * rms_scale(tokens) * attn_gain)
        qkv = low_back(jnp.dot(normed, w_qkv, precision=HIGHEST)).reshape(SEQ_TOK, H, 3, HD)
        query_raw = qkv[:, :, 0, :].reshape(SEQ_TOK, D)
        key_raw = qkv[:, :, 1, :].reshape(SEQ_TOK, D)
        q_unit = (query_raw * rms_scale(query_raw) * q_gain).reshape(SEQ_TOK, H, HD)
        k_unit = (key_raw * rms_scale(key_raw) * k_gain).reshape(SEQ_TOK, H, HD)
        places = jnp.arange(SEQ_TOK, dtype=jnp.int32)
        document, position = doc_positions(places, cuts)
        cosine, sine = rope_tables(position, HD)
        query = low(rotate(q_unit, cosine[:, None, :], sine[:, None, :]))
        key = low(rotate(k_unit, cosine[:, None, :], sine[:, None, :]))
        value = low(qkv[:, :, 2, :])
        allowed = (document[:, None] == document[None, :]) & (places[None, :] <= places[:, None])

        def head_attention(parts):
            query_head, key_head, value_head = parts
            scores = jnp.dot(query_head, key_head.T, precision=HIGHEST) * scale
            scores = low_back(jnp.where(allowed, scores, MASKED))
            probs = low(jax.nn.softmax(scores, axis=-1))
            return low(low_back(jnp.dot(probs, value_head, precision=HIGHEST)))
        mixed = lax.map(jax.checkpoint(head_attention), (query.transpose(1, 0, 2), key.transpose(1, 0, 2), value.transpose(1, 0, 2)))
        mixed = mixed.transpose(1, 0, 2).reshape(SEQ_TOK, D)
        return low_back(jnp.dot(mixed, w_out, precision=HIGHEST))
    sequences = hidden.reshape(SEQS, SEQ_TOK, D)
    attn = lax.map(jax.checkpoint(sequence_attention), (sequences, doc_cuts))
    middle = (sequences + attn).reshape(TOKENS, D)
    normed_two = low(middle * rms_scale(middle) * moe_gain)
    logits = low_back(jnp.dot(normed_two, router, precision=HIGHEST))
    gates_all = jax.nn.softmax(logits, axis=-1)
    moe = run_experts(normed_two, gates_all, routes.reshape(TOKENS, TOPK), w_gate, w_up, w_down)
    return (middle + moe).reshape(GROUPS, GROUP_TOK, D)

def reference(hidden_in, out_grad, attn_gain, w_qkv, q_gain, k_gain, w_out, moe_gain, router, w_gate, w_up, w_down, routes, doc_cuts):
    floats = tuple((value.astype(jnp.float32) for value in (hidden_in, attn_gain, w_qkv, q_gain, k_gain, w_out, moe_gain, router, w_gate, w_up, w_down)))

    def wrapped(*values):
        return forward(*values, routes, doc_cuts)
    result, pullback = jax.vjp(wrapped, *floats)
    grads = pullback(out_grad.astype(jnp.float32))
    return (result.astype(jnp.bfloat16), grads[0], grads[1], grads[2], grads[3], grads[4], grads[5], grads[6], grads[7], grads[8], grads[9], grads[10])
```

```python
import math

import jax
import jax.numpy as jnp
from jax import lax
from jax.sharding import PartitionSpec as P

HD = 128
EPSILON = 1e-05
ROPE_BASE = 10000.0
MASKED = -1e30
BF16 = jnp.bfloat16
F32 = jnp.float32


def matmul(left, right):
    return jnp.dot(left, right, preferred_element_type=F32)


def contract_rows(left, right):
    return lax.dot_general(left, right, (((0,), (0,)), ((), ())), preferred_element_type=F32)


def contract_cols(left, right):
    return lax.dot_general(left, right, (((1,), (1,)), ((), ())), preferred_element_type=F32)


def rms_scale(values):
    return lax.rsqrt(jnp.mean(values * values, axis=-1, keepdims=True) + EPSILON)


def rope_tables(position, width):
    frequency = ROPE_BASE ** (-jnp.arange(0, width, 2, dtype=F32) / width)
    angle = position.astype(F32)[:, None] * frequency[None, :]
    return (
        jnp.concatenate([jnp.cos(angle)] * 2, axis=-1),
        jnp.concatenate([jnp.sin(angle)] * 2, axis=-1),
    )


def rotate(values, cosine, sine):
    half = values.shape[-1] // 2
    turned = jnp.concatenate([-values[..., half:], values[..., :half]], axis=-1)
    return values * cosine + turned * sine


def rotate_back(values, cosine, sine):
    half = values.shape[-1] // 2
    turned = values * sine
    return values * cosine + jnp.concatenate([turned[..., half:], -turned[..., :half]], axis=-1)


def doc_positions(places, cuts):
    first = (places >= cuts[0]).astype(jnp.int32)
    second = (places >= cuts[1]).astype(jnp.int32)
    start = first * cuts[0] + second * (cuts[1] - cuts[0])
    return (first + second, places - start)


def from_behind(value, axis, steps):
    count = lax.axis_size(axis)
    initial, last = (max(0, -steps), min(count, count - steps))
    return lax.ppermute(value, axis, [(source, source + steps) for source in range(initial, last)])


def rows_to_heads(values):
    count = lax.axis_size("row")
    rows, heads, width = values.shape
    moved = lax.all_to_all(values.transpose(1, 0, 2), "row", split_axis=0, concat_axis=0, tiled=True)
    return moved.reshape(count * rows, width)


def heads_to_rows(values):
    count = lax.axis_size("row")
    rows, width = values.shape
    moved = lax.all_to_all(
        values.reshape(count, rows // count, width), "row", split_axis=0, concat_axis=0, tiled=True
    )
    return moved.transpose(1, 0, 2)


def heads_to_tokens(values):
    row_count, col_count = lax.axis_size("row"), lax.axis_size("col")
    rows = values.shape[0] // (row_count * col_count)
    moved = lax.all_to_all(
        values.reshape(row_count * col_count, rows, HD),
        ("row", "col"),
        split_axis=0,
        concat_axis=0,
        tiled=True,
    )
    moved = moved.reshape(row_count, col_count, rows, HD).transpose(2, 1, 0, 3)
    return moved.reshape(rows, row_count * col_count * HD)


def tokens_to_heads(values):
    row_count, col_count = lax.axis_size("row"), lax.axis_size("col")
    rows = values.shape[0]
    parted = values.reshape(rows, col_count, row_count, HD).transpose(2, 1, 0, 3)
    moved = lax.all_to_all(
        parted.reshape(row_count * col_count, rows, HD),
        ("row", "col"),
        split_axis=0,
        concat_axis=0,
        tiled=True,
    )
    return moved.reshape(row_count * col_count * rows, HD)


def attention_forward(query, key_all, value_all, places, document, key_places, key_doc, scale):
    group_tok, head_size = query.shape
    block_rows = math.gcd(512, group_tok)
    block_count = group_tok // block_rows

    def forward_block(pieces):
        query_block, place_block, doc_block = pieces
        allowed = (doc_block[:, None] == key_doc[None, :]) & (
            key_places[None, :] <= place_block[:, None]
        )
        scores = jnp.where(allowed, contract_cols(query_block, key_all) * scale, MASKED)
        top_score = jnp.max(scores, axis=-1, keepdims=True)
        weights = jnp.exp(scores - top_score)
        total = jnp.sum(weights, axis=-1, keepdims=True)
        probs = (weights / total).astype(BF16)
        return (matmul(probs, value_all).astype(BF16), top_score + jnp.log(total))

    mixed, total = lax.map(
        forward_block,
        (
            query.reshape(block_count, block_rows, head_size),
            places.reshape(block_count, block_rows),
            document.reshape(block_count, block_rows),
        ),
    )
    return mixed.reshape(group_tok, head_size), total.reshape(group_tok, 1)


def attention_backward(
    query, key_all, value_all, d_mixed, total, places, document, key_places, key_doc, scale
):
    group_tok, head_size = query.shape
    block_rows = math.gcd(512, group_tok)
    block_count = group_tok // block_rows

    def backward_block(carry, pieces):
        acc_key, acc_value = carry
        query_block, place_block, doc_block, total_block, d_mixed_block = pieces
        allowed = (doc_block[:, None] == key_doc[None, :]) & (
            key_places[None, :] <= place_block[:, None]
        )
        scores = jnp.where(allowed, contract_cols(query_block, key_all) * scale, MASKED)
        recomputed = jnp.exp(scores - total_block)
        probs = recomputed.astype(BF16)
        d_probs = contract_cols(d_mixed_block, value_all)
        d_scores = (
            recomputed * (d_probs - jnp.sum(recomputed * d_probs, axis=-1, keepdims=True))
        ).astype(BF16)
        d_query_block = matmul(d_scores, key_all) * scale
        acc_key = acc_key + contract_rows(d_scores, query_block) * scale
        acc_value = acc_value + contract_rows(probs, d_mixed_block)
        return ((acc_key, acc_value), d_query_block)

    zeros = jnp.zeros((key_all.shape[0], head_size), F32)
    (acc_key, acc_value), d_query = lax.scan(
        backward_block,
        (zeros, zeros),
        (
            query.reshape(block_count, block_rows, head_size),
            places.reshape(block_count, block_rows),
            document.reshape(block_count, block_rows),
            total.reshape(block_count, block_rows, 1),
            d_mixed.reshape(block_count, block_rows, head_size),
        ),
    )
    return d_query.reshape(group_tok, head_size), acc_key, acc_value


ALL = ("row", "col", "exp")


def expert_rows(rows, grads, gate, gate_w, up_w, down_w):
    pre_gate = matmul(rows, gate_w)
    pre_up = matmul(rows, up_w)
    back = contract_cols(grads, down_w)
    sigmoid_gate = jax.nn.sigmoid(pre_gate)
    silu_gate = pre_gate * sigmoid_gate
    hidden = (silu_gate * pre_up).astype(BF16)
    inner = jnp.sum(hidden.astype(F32) * back, axis=-1)
    weighted = (hidden.astype(F32) * gate).astype(BF16)
    d_hid = back * gate
    d_pregate = (d_hid * pre_up * (sigmoid_gate + silu_gate * (1.0 - sigmoid_gate))).astype(BF16)
    d_preup = (d_hid * silu_gate).astype(BF16)
    outputs = matmul(weighted, down_w).astype(BF16)
    d_rows = (contract_cols(d_pregate, gate_w) + contract_cols(d_preup, up_w)).astype(BF16)
    return (
        outputs,
        d_rows,
        inner,
        contract_rows(rows, d_pregate),
        contract_rows(rows, d_preup),
        contract_rows(weighted, grads),
    )


def experts(normed, grads, dense_gates, gate_w, up_w, down_w):
    rows_dev, width = normed.shape
    devices = math.prod(lax.axis_size(axis) for axis in ALL)
    expert_count = dense_gates.shape[1]
    expert = lax.axis_index(ALL) // 2
    parts = max(1, lax.axis_size("exp") // 2)
    step = rows_dev // parts

    def one_part(sums, piece):
        rows, grad_rows, gates = piece
        rows_all = lax.all_gather(rows, ALL, axis=0, tiled=True)
        grads_all = lax.all_gather(grad_rows, ALL, axis=0, tiled=True)
        gates_all = lax.all_gather(gates, ALL, axis=0, tiled=True)
        gate = lax.dynamic_slice_in_dim(gates_all, expert, 1, 1)
        got = expert_rows(rows_all, grads_all, gate, gate_w, up_w, down_w)
        outputs = lax.psum_scatter(got[0], ALL, scatter_dimension=0, tiled=True)
        d_rows = lax.psum_scatter(got[1], ALL, scatter_dimension=0, tiled=True)
        inner = lax.all_to_all(
            got[2].reshape(devices, step), ALL, split_axis=0, concat_axis=0, tiled=True
        )
        inner = inner.reshape(expert_count, 2, step).sum(axis=1).T
        sums = got[3:] if sums is None else tuple(a + b for a, b in zip(sums, got[3:]))
        return sums, (outputs, d_rows, inner)

    if parts == 1:
        sums, (outputs, d_rows, inner) = one_part(None, (normed, grads, dense_gates))
    else:
        start = tuple(jnp.zeros(w.shape, F32) for w in (gate_w, up_w, down_w))
        pieces = tuple(v.reshape(parts, step, -1) for v in (normed, grads, dense_gates))
        sums, got = lax.scan(one_part, start, pieces)
        outputs, d_rows, inner = (v.reshape(rows_dev, -1) for v in got)
    return outputs.astype(F32), d_rows.astype(F32), inner, sums


def shards(
    hidden_in,
    out_grad,
    attn_gain,
    w_qkv,
    q_gain,
    k_gain,
    w_out,
    moe_gain,
    router,
    w_gate,
    w_up,
    w_down,
    routes,
    doc_cuts,
):
    row_count, col_count = lax.axis_size("row"), lax.axis_size("col")
    tokens = hidden_in[0].astype(F32)
    rows_dev, width = tokens.shape
    heads = w_qkv.shape[1] // (3 * HD)
    plane = heads * HD
    scale = HD ** (-0.5)
    side = lax.axis_index("exp") % 2
    row_tok = rows_dev * col_count
    group_tok = row_tok * row_count
    cuts = lax.dynamic_index_in_dim(doc_cuts, lax.axis_index("exp") // 2, 0, keepdims=False)

    gain_one = attn_gain.astype(F32)
    scale_one = rms_scale(tokens)
    normed_one = (tokens * scale_one * gain_one).astype(BF16)
    normed_row = lax.all_gather(normed_one, "col", axis=0, tiled=True)
    qkv_w = lax.all_gather(w_qkv, "row", axis=0, tiled=True)
    out_w = lax.all_gather(lax.all_gather(w_out, "row", axis=1, tiled=True), "col", axis=0, tiled=True)
    qkv = matmul(normed_row, qkv_w).reshape(row_tok, heads, 3, HD)
    query_raw, key_raw, value_raw = qkv[:, :, 0], qkv[:, :, 1], qkv[:, :, 2]
    total_q, total_k = lax.psum(
        (jnp.sum(query_raw * query_raw, axis=(1, 2)), jnp.sum(key_raw * key_raw, axis=(1, 2))), "col"
    )
    scale_q = lax.rsqrt(total_q / width + EPSILON)[:, None, None]
    scale_k = lax.rsqrt(total_k / width + EPSILON)[:, None, None]
    head_start = lax.axis_index("col") * plane
    gain_q = lax.dynamic_slice_in_dim(q_gain, head_start, plane, 0).astype(F32).reshape(heads, HD)
    gain_k = lax.dynamic_slice_in_dim(k_gain, head_start, plane, 0).astype(F32).reshape(heads, HD)
    row_places = side * group_tok + lax.axis_index("row") * row_tok + jnp.arange(row_tok, dtype=jnp.int32)
    unused_doc, position = doc_positions(row_places, cuts)
    cosine, sine = rope_tables(position, HD)
    cosine, sine = cosine[:, None, :], sine[:, None, :]
    query = rotate(query_raw * scale_q * gain_q, cosine, sine).astype(BF16)
    key = rotate(key_raw * scale_k * gain_k, cosine, sine).astype(BF16)
    moved = rows_to_heads(jnp.concatenate([query, key, value_raw.astype(BF16)], axis=-1))

    query, own_pair = moved[:, :HD], moved[:, HD:]
    earlier_pair = from_behind(own_pair, "exp", 1)
    lower_pair = jnp.where(side == 0, own_pair, earlier_pair)
    upper_pair = jnp.where(side == 0, jnp.zeros_like(own_pair), own_pair)
    key_value = jnp.concatenate([lower_pair, upper_pair], axis=0)
    key_all, value_all = key_value[:, :HD], key_value[:, HD:]
    key_places = jnp.arange(2 * group_tok, dtype=jnp.int32)
    places = side * group_tok + jnp.arange(group_tok, dtype=jnp.int32)
    document, unused_pos = doc_positions(places, cuts)
    key_doc, unused_pos = doc_positions(key_places, cuts)
    mixed, total = attention_forward(
        query, key_all, value_all, places, document, key_places, key_doc, scale
    )
    mixed_row = heads_to_rows(mixed).reshape(row_tok, plane)
    middle = tokens + matmul(heads_to_tokens(mixed), out_w)

    gain_two = moe_gain.astype(F32)
    scale_two = rms_scale(middle)
    normed_two = (middle * scale_two * gain_two).astype(BF16)
    gates_all = jax.nn.softmax(matmul(normed_two, router), axis=-1)
    picks = routes[0]
    chosen = jnp.any(
        picks[:, :, None] == jnp.arange(router.shape[1], dtype=jnp.int32)[None, None, :], axis=1
    )
    dense_gates = jnp.where(chosen, gates_all, 0.0)
    grad_out = out_grad[0].astype(F32)
    mixture, d_normed_two, inner, weight_grads = experts(
        normed_two, out_grad[0], dense_gates, w_gate[0], w_up[0], w_down[0]
    )
    final = middle + mixture
    dense = jnp.where(chosen, inner, 0.0)
    d_logits = (gates_all * (dense - jnp.sum(gates_all * dense, axis=-1, keepdims=True))).astype(BF16)
    grad_router = contract_rows(normed_two, d_logits)
    d_normed_two = d_normed_two + contract_cols(d_logits, router)
    grad_moe_gain = jnp.sum(d_normed_two * middle * scale_two, axis=0)
    weighted_two = d_normed_two * gain_two
    d_middle = (
        grad_out
        + scale_two * weighted_two
        - middle * scale_two**3 * jnp.mean(weighted_two * middle, axis=-1, keepdims=True)
    )

    d_attn = d_middle.astype(BF16)
    d_mixed = tokens_to_heads(contract_cols(d_attn, out_w).astype(BF16))
    d_attn_row = lax.all_gather(d_attn, "col", axis=0, tiled=True)
    grad_w_out = lax.psum_scatter(
        contract_rows(mixed_row, d_attn_row).astype(BF16), "row", scatter_dimension=1, tiled=True
    )
    d_query, acc_key, acc_value = attention_backward(
        query, key_all, value_all, d_mixed, total, places, document, key_places, key_doc, scale
    )
    accumulated = jnp.concatenate([acc_key, acc_value], axis=1)
    lower_acc, upper_acc = accumulated[:group_tok], accumulated[group_tok:]
    kept_acc = jnp.where(side == 0, lower_acc, upper_acc)
    later_acc = from_behind(lower_acc.astype(BF16), "exp", -1).astype(F32)
    summed_pair = kept_acc + jnp.where(side == 0, later_acc, jnp.zeros_like(later_acc))
    d_heads = heads_to_rows(jnp.concatenate([d_query, summed_pair], axis=1).astype(BF16)).astype(F32)
    d_q_unit = rotate_back(d_heads[:, :, :HD], cosine, sine)
    d_k_unit = rotate_back(d_heads[:, :, HD : 2 * HD], cosine, sine)
    d_value = d_heads[:, :, 2 * HD :]
    weighted_q = d_q_unit * gain_q
    weighted_k = d_k_unit * gain_k
    sum_q, sum_k = lax.psum(
        (jnp.sum(weighted_q * query_raw, axis=(1, 2)), jnp.sum(weighted_k * key_raw, axis=(1, 2))),
        "col",
    )
    d_query_raw = scale_q * weighted_q - query_raw * scale_q**3 * (sum_q / width)[:, None, None]
    d_key_raw = scale_k * weighted_k - key_raw * scale_k**3 * (sum_k / width)[:, None, None]
    grad_q_part = jnp.sum(d_q_unit * query_raw * scale_q, axis=0).reshape(plane)
    grad_k_part = jnp.sum(d_k_unit * key_raw * scale_k, axis=0).reshape(plane)
    d_qkv = jnp.concatenate([d_query_raw, d_key_raw, d_value], axis=2).astype(BF16)
    d_qkv = d_qkv.reshape(row_tok, heads * 3 * HD)
    d_normed_one = lax.psum_scatter(
        contract_cols(d_qkv, qkv_w).astype(BF16), "col", scatter_dimension=0, tiled=True
    ).astype(F32)
    grad_qkv = lax.psum_scatter(
        contract_rows(normed_row, d_qkv).astype(BF16), "row", scatter_dimension=0, tiled=True
    )
    grad_attn_gain = jnp.sum(d_normed_one * tokens * scale_one, axis=0)
    weighted_one = d_normed_one * gain_one
    grad_hidden = (
        d_middle
        + scale_one * weighted_one
        - tokens * scale_one**3 * jnp.mean(weighted_one * tokens, axis=-1, keepdims=True)
    )
    grad_qkv, grad_w_out = (
        lax.psum(grad_qkv, "exp").astype(F32),
        lax.psum(grad_w_out, "exp").astype(F32),
    )
    empty = jnp.zeros((width,), F32)
    grad_q_full = lax.dynamic_update_slice_in_dim(empty, grad_q_part, head_start, 0)
    grad_k_full = lax.dynamic_update_slice_in_dim(empty, grad_k_part, head_start, 0)
    summed = lax.psum((grad_attn_gain, grad_q_full, grad_k_full, grad_moe_gain, grad_router), ALL)
    return (
        final.astype(BF16)[None],
        grad_hidden[None],
        summed[0],
        grad_qkv,
        summed[1],
        summed[2],
        grad_w_out,
        summed[3],
        summed[4],
        weight_grads[0][None],
        weight_grads[1][None],
        weight_grads[2][None],
    )


def solution(mesh):
    token_spec = P("exp", ("row", "col"), None)
    expert_spec = P(("row", "col", "exp"), None, None)
    in_specs = (
        token_spec,
        token_spec,
        P(),
        P("row", "col"),
        P(),
        P(),
        P("col", "row"),
        P(),
        P(),
        expert_spec,
        expert_spec,
        expert_spec,
        token_spec,
        P(),
    )
    out_specs = (
        token_spec,
        token_spec,
        P(),
        P("row", "col"),
        P(),
        P(),
        P("col", "row"),
        P(),
        P(),
        expert_spec,
        expert_spec,
        expert_spec,
    )
    return jax.shard_map(shards, mesh=mesh, in_specs=in_specs, out_specs=out_specs, check_vma=False)
```

```python
import functools
import math

import jax
import jax.numpy as jnp
from jax import lax
from jax.experimental import pallas as pl
from jax.experimental.pallas import tpu as pltpu
from jax.sharding import PartitionSpec as P

HD = 128
EPSILON = 1e-05
ROPE_BASE = 10000.0
MASKED = -1e30
BF16 = jnp.bfloat16
F32 = jnp.float32


def matmul(left, right):
    return jnp.dot(left, right, preferred_element_type=F32)


def contract_rows(left, right):
    return lax.dot_general(left, right, (((0,), (0,)), ((), ())), preferred_element_type=F32)


def contract_cols(left, right):
    return lax.dot_general(left, right, (((1,), (1,)), ((), ())), preferred_element_type=F32)


def rms_scale(values):
    return lax.rsqrt(jnp.mean(values * values, axis=-1, keepdims=True) + EPSILON)


def rope_tables(position, width):
    frequency = ROPE_BASE ** (-jnp.arange(0, width, 2, dtype=F32) / width)
    angle = position.astype(F32)[:, None] * frequency[None, :]
    return (
        jnp.concatenate([jnp.cos(angle)] * 2, axis=-1),
        jnp.concatenate([jnp.sin(angle)] * 2, axis=-1),
    )


def rotate(values, cosine, sine):
    half = values.shape[-1] // 2
    turned = jnp.concatenate([-values[..., half:], values[..., :half]], axis=-1)
    return values * cosine + turned * sine


def rotate_back(values, cosine, sine):
    half = values.shape[-1] // 2
    turned = values * sine
    return values * cosine + jnp.concatenate([turned[..., half:], -turned[..., :half]], axis=-1)


def doc_positions(places, cuts):
    first = (places >= cuts[0]).astype(jnp.int32)
    second = (places >= cuts[1]).astype(jnp.int32)
    start = first * cuts[0] + second * (cuts[1] - cuts[0])
    return (first + second, places - start)


def from_behind(value, axis, steps):
    count = lax.axis_size(axis)
    initial, last = (max(0, -steps), min(count, count - steps))
    return lax.ppermute(value, axis, [(source, source + steps) for source in range(initial, last)])


def rows_to_heads(values):
    count = lax.axis_size("row")
    rows, heads, width = values.shape
    moved = lax.all_to_all(values.transpose(1, 0, 2), "row", split_axis=0, concat_axis=0, tiled=True)
    return moved.reshape(count * rows, width)


def heads_to_rows(values):
    count = lax.axis_size("row")
    rows, width = values.shape
    moved = lax.all_to_all(
        values.reshape(count, rows // count, width), "row", split_axis=0, concat_axis=0, tiled=True
    )
    return moved.transpose(1, 0, 2)


def heads_to_tokens(values):
    row_count, col_count = lax.axis_size("row"), lax.axis_size("col")
    rows = values.shape[0] // (row_count * col_count)
    moved = lax.all_to_all(
        values.reshape(row_count * col_count, rows, HD),
        ("row", "col"),
        split_axis=0,
        concat_axis=0,
        tiled=True,
    )
    moved = moved.reshape(row_count, col_count, rows, HD).transpose(2, 1, 0, 3)
    return moved.reshape(rows, row_count * col_count * HD)


def tokens_to_heads(values):
    row_count, col_count = lax.axis_size("row"), lax.axis_size("col")
    rows = values.shape[0]
    parted = values.reshape(rows, col_count, row_count, HD).transpose(2, 1, 0, 3)
    moved = lax.all_to_all(
        parted.reshape(row_count * col_count, rows, HD),
        ("row", "col"),
        split_axis=0,
        concat_axis=0,
        tiled=True,
    )
    return moved.reshape(row_count * col_count * rows, HD)


def doc_start(places, cuts):
    return jnp.where(places >= cuts[1], cuts[1], jnp.where(places >= cuts[0], cuts[0], 0))


def key_blocks(cuts, first_query, rows, scores_of, block_fn):
    def scan(index, carry):
        start = pl.multiple_of(index * rows, rows)
        free = (start >= doc_start(first_query + rows - 1, cuts)) & (start + rows <= first_query + 1)

        @pl.when(free)
        def _():
            block_fn(start, scores_of(start))

        @pl.when(jnp.logical_not(free))
        def _():
            key_place = start + lax.broadcasted_iota(jnp.int32, (rows, rows), 0)
            place = first_query + lax.broadcasted_iota(jnp.int32, (1, rows), 1)
            allowed = (key_place <= place) & (key_place >= doc_start(place, cuts))
            block_fn(start, jnp.where(allowed, scores_of(start), MASKED))

        return carry

    lax.fori_loop(doc_start(first_query, cuts) // rows, first_query // rows + 1, scan, 0)


def attend_kernel(scale, group_tok, cuts, query, keys, values_t, mixed, total, top, summed, acc):
    rows = query.shape[0]
    side = lax.axis_index("exp") % 2
    first_query = side * group_tok + pl.program_id(0) * rows
    top[...] = jnp.full_like(top, MASKED)
    summed[...] = jnp.zeros_like(summed)
    acc[...] = jnp.zeros_like(acc)
    cut = (cuts[0, 0], cuts[0, 1])

    def scores_of(start):
        return contract_cols(keys[pl.ds(start, rows)], query[...]) * scale

    def block_fn(start, scores):
        old = top[...]
        new = jnp.maximum(old, jnp.max(scores, axis=0, keepdims=True))
        weights = jnp.exp(scores - new)
        decay = jnp.exp(old - new)
        top[...] = new
        summed[...] = summed[...] * decay + jnp.sum(weights, axis=0, keepdims=True)
        acc[...] = acc[...] * decay + matmul(values_t[:, pl.ds(start, rows)], weights.astype(BF16))

    key_blocks(cut, first_query, rows, scores_of, block_fn)
    mixed[...] = (acc[...] / summed[...]).T
    total[...] = top[...] + jnp.log(summed[...])


def attend(query, keys, values, cuts, scale, rows=512):
    group_tok, head_size = query.shape
    whole = lambda shape: pl.BlockSpec(shape, lambda i: (0, 0))
    return pl.pallas_call(
        functools.partial(attend_kernel, scale, group_tok),
        grid=(group_tok // rows,),
        in_specs=[
            pl.BlockSpec(memory_space=pltpu.SMEM),
            pl.BlockSpec((rows, head_size), lambda i: (i, 0)),
            whole(keys.shape),
            whole(values.shape[::-1]),
        ],
        out_specs=[
            pl.BlockSpec((rows, head_size), lambda i: (i, 0)),
            pl.BlockSpec((1, rows), lambda i: (0, i)),
        ],
        out_shape=[
            jax.ShapeDtypeStruct((group_tok, head_size), F32),
            jax.ShapeDtypeStruct((1, group_tok), F32),
        ],
        scratch_shapes=[
            pltpu.VMEM((1, rows), F32),
            pltpu.VMEM((1, rows), F32),
            pltpu.VMEM((head_size, rows), F32),
        ],
        compiler_params=pltpu.CompilerParams(vmem_limit_bytes=40 * 2**20),
        cost_estimate=pl.CostEstimate(
            flops=4 * 7 * 2**20 * head_size, bytes_accessed=2**23, transcendentals=7 * 2**20
        ),
    )(cuts[None], query, keys, values.T)


def attend_back_kernel(
    scale, group_tok, cuts, query, keys, keys_t, values, d_mixed, total, delta,
    d_query, d_keys, d_values, acc,
):
    rows = query.shape[0]
    side = lax.axis_index("exp") % 2
    first_query = side * group_tok + pl.program_id(0) * rows
    cut = (cuts[0, 0], cuts[0, 1])

    @pl.when(pl.program_id(0) == 0)
    def _():
        d_keys[...] = jnp.zeros_like(d_keys)
        d_values[...] = jnp.zeros_like(d_values)

    acc[...] = jnp.zeros_like(acc)

    def scores_of(start):
        return contract_cols(keys[pl.ds(start, rows)], query[...]) * scale

    def block_fn(start, scores):
        part = pl.ds(start, rows)
        weights = jnp.exp(scores - total[...])
        d_weights = contract_cols(values[part], d_mixed[...])
        d_scores = (weights * (d_weights - delta[...])).astype(BF16)
        d_values[part] += matmul(weights.astype(BF16), d_mixed[...])
        d_keys[part] += matmul(d_scores, query[...]) * scale
        acc[...] += matmul(keys_t[:, part], d_scores)

    key_blocks(cut, first_query, rows, scores_of, block_fn)
    d_query[...] = (acc[...] * scale).T


def attend_back(query, keys, values, d_mixed, mixed, total, cuts, scale, rows=512):
    group_tok, head_size = query.shape
    delta = jnp.sum(d_mixed.astype(F32) * mixed, axis=1)[None]
    whole = lambda shape: pl.BlockSpec(shape, lambda i: (0, 0))
    block = pl.BlockSpec((rows, head_size), lambda i: (i, 0))
    line = pl.BlockSpec((1, rows), lambda i: (0, i))
    return pl.pallas_call(
        functools.partial(attend_back_kernel, scale, group_tok),
        grid=(group_tok // rows,),
        in_specs=[
            pl.BlockSpec(memory_space=pltpu.SMEM),
            block,
            whole(keys.shape),
            whole(keys.shape[::-1]),
            whole(keys.shape),
            block,
            line,
            line,
        ],
        out_specs=[block, whole(keys.shape), whole(keys.shape)],
        out_shape=[
            jax.ShapeDtypeStruct((group_tok, head_size), F32),
            jax.ShapeDtypeStruct(keys.shape, F32),
            jax.ShapeDtypeStruct(keys.shape, F32),
        ],
        scratch_shapes=[pltpu.VMEM((head_size, rows), F32)],
        compiler_params=pltpu.CompilerParams(vmem_limit_bytes=48 * 2**20),
        cost_estimate=pl.CostEstimate(
            flops=10 * 7 * 2**20 * head_size, bytes_accessed=2**23, transcendentals=7 * 2**20
        ),
    )(cuts[None], query, keys, keys.T, values, d_mixed, total, delta)


ALL = ("row", "col", "exp")
MESH = pl.DeviceIdType.MESH


def places_of():
    row, col, core = (lax.axis_index(axis) for axis in ALL)
    across = row + 1 - 2 * (row % 2)
    along = (row + 2) % 4
    return row, col, core, across, along


def near_first(col):
    half = col // 2
    return [col, 1 + col % 2, 2 - col - col % 2 + 3 * half, 3 - 3 * half]


def greet(row, col, core, across, along):
    barrier = pltpu.get_barrier_semaphore()

    def signal(target):
        pl.semaphore_signal(barrier, inc=1, device_id=target, device_id_type=MESH)

    signal((row, col, 1 - core))
    signal((across, col, core))
    signal((along, col, core))

    @pl.when(col > 0)
    def _():
        signal((row, col - 1, core))

    @pl.when(col < 3)
    def _():
        signal((row, col + 1, core))

    pl.semaphore_wait(barrier, 3 + (col + 3) // 4 + (6 - col) // 4)


def remote(source, target, send, recv, device):
    return pltpu.make_async_remote_copy(
        src_ref=source,
        dst_ref=target,
        send_sem=send,
        recv_sem=recv,
        device_id=device,
        device_id_type=MESH,
    )


def gather_kernel(own, out, kept, *sems):
    (
        up_send, down_send, line_recv,
        across_send, across_recv, along_send, along_recv,
        corner_one_send, corner_one_recv, corner_two_send, corner_two_recv,
        core_send, core_recv,
    ) = sems
    row, col, core, across, along = places_of()
    opposite = 3 - row
    half = own.shape[0] // 2
    order = near_first(col)

    def block(of_row, of_col, of_core):
        return out.at[(of_row * 4 + of_col) * 2 + of_core]

    greet(row, col, core, across, along)
    keep = pltpu.make_async_copy(own, block(row, col, core), kept)
    keep.start()

    def up(place, source):
        return remote(
            source, block(row, place, core), up_send.at[place], line_recv.at[place], (row, col + 1, core)
        )

    def down(place, source):
        return remote(
            source, block(row, place, core), down_send.at[place], line_recv.at[place], (row, col - 1, core)
        )

    def to_across(place, source):
        return remote(
            source, block(row, place, core), across_send.at[place], across_recv.at[place], (across, col, core)
        )

    def to_along(place, source):
        return remote(
            source, block(row, place, core), along_send.at[place], along_recv.at[place], (along, col, core)
        )

    def corner_one(place):
        part = block(across, place, core).at[pl.ds(0, half)]
        return remote(part, part, corner_one_send.at[place], corner_one_recv.at[place], (along, col, core))

    def corner_two(place):
        part = block(along, place, core).at[pl.ds(half, half)]
        return remote(part, part, corner_two_send.at[place], corner_two_recv.at[place], (across, col, core))

    def to_core(which, of_row, place, source):
        return remote(
            source,
            block(of_row, place, core),
            core_send.at[which, place],
            core_recv.at[which, place],
            (row, col, 1 - core),
        )

    def arrived(target, recv):
        pltpu.make_async_copy(target, target, recv).wait()

    def line_step(step):
        place = order[step]
        source = own if step == 0 else block(row, place, core)
        if step > 0:
            arrived(source, line_recv.at[place])

        @pl.when((place <= col) & (col < 3))
        def _():
            up(place, source).start()

        @pl.when((place >= col) & (col > 0))
        def _():
            down(place, source).start()

        to_across(place, source).start()
        to_along(place, source).start()
        to_core(0, row, place, source).start()

    def plane_step(step):
        place = order[step]
        arrived(block(across, place, core), across_recv.at[place])
        corner_one(place).start()
        to_core(1, across, place, block(across, place, core)).start()
        arrived(block(along, place, core), along_recv.at[place])
        corner_two(place).start()
        to_core(2, along, place, block(along, place, core)).start()

    def corner_step(step):
        place = order[step]
        target = block(opposite, place, core)
        arrived(target.at[pl.ds(0, half)], corner_one_recv.at[place])
        arrived(target.at[pl.ds(half, half)], corner_two_recv.at[place])
        to_core(3, opposite, place, target).start()

    for step in range(6):
        if step < 4:
            line_step(step)
        if 0 <= step - 1 < 4:
            plane_step(step - 1)
        if 0 <= step - 2 < 4:
            corner_step(step - 2)
    keep.wait()
    for step in range(4):
        place = order[step]
        source = own if step == 0 else block(row, place, core)

        @pl.when((place <= col) & (col < 3))
        def _():
            up(place, source).wait_send()

        @pl.when((place >= col) & (col > 0))
        def _():
            down(place, source).wait_send()

        to_across(place, source).wait_send()
        to_along(place, source).wait_send()
        corner_one(place).wait_send()
        corner_two(place).wait_send()
        for which, of_row in enumerate((row, across, along, opposite)):
            to_core(which, of_row, place, block(of_row, place, core)).wait_send()
            arrived(block(of_row, place, 1 - core), core_recv.at[which, place])


def gather_rows(values, collective_id):
    return pl.pallas_call(
        gather_kernel,
        out_shape=jax.ShapeDtypeStruct((32,) + values.shape, values.dtype),
        in_specs=[pl.BlockSpec(memory_space=pl.ANY)],
        out_specs=pl.BlockSpec(memory_space=pl.ANY),
        scratch_shapes=[pltpu.SemaphoreType.DMA]
        + [pltpu.SemaphoreType.DMA((4,))] * 11
        + [pltpu.SemaphoreType.DMA((4, 4))] * 2,
        compiler_params=pltpu.CompilerParams(collective_id=collective_id, has_side_effects=True),
    )(values)


def reduce_kernel(values, total, mine, other, corner_one, corner_two, from_across, from_along, line, *sems):
    (
        mine_sem, other_send, other_recv,
        corner_one_send, corner_one_recv, corner_two_send, corner_two_recv,
        across_send, across_recv, along_send, along_recv,
        up_send, down_send, line_recv,
    ) = sems
    row, col, core, across, along = places_of()
    rows = (row, across, along, 3 - row)
    half = total.shape[0] // 2
    order = near_first(col)[::-1]
    first, second = pl.ds(0, half), pl.ds(half, half)

    def block(of_row, of_col, of_core):
        return values.at[(of_row * 4 + of_col) * 2 + of_core]

    def load(which, place):
        return pltpu.make_async_copy(
            block(rows[which], place, core), mine.at[which, place], mine_sem.at[which, place]
        )

    def to_core(which, place):
        return remote(
            block(rows[which], place, 1 - core),
            other.at[which, place],
            other_send.at[which, place],
            other_recv.at[which, place],
            (row, col, 1 - core),
        )

    def give_one(place):
        return remote(
            mine.at[3, place, first], corner_one.at[place],
            corner_one_send.at[place], corner_one_recv.at[place], (across, col, core),
        )

    def give_two(place):
        return remote(
            mine.at[3, place, second], corner_two.at[place],
            corner_two_send.at[place], corner_two_recv.at[place], (along, col, core),
        )

    def give_across(place, part):
        return remote(
            mine.at[1, place, (first, second)[part]], from_across.at[place, (first, second)[part]],
            across_send.at[part, place], across_recv.at[part, place], (across, col, core),
        )

    def give_along(place, part):
        return remote(
            mine.at[2, place, (first, second)[part]], from_along.at[place, (first, second)[part]],
            along_send.at[part, place], along_recv.at[part, place], (along, col, core),
        )

    def give_up(place):
        return remote(
            mine.at[0, place], line.at[place], up_send.at[place], line_recv.at[place], (row, col + 1, core)
        )

    def give_down(place, slot):
        return remote(
            mine.at[0, place], line.at[slot], down_send.at[place], line_recv.at[slot], (row, col - 1, core)
        )

    def add(target, *terms):
        step = 16

        @pl.loop(0, target.shape[0] // step)
        def _(index):
            part = pl.ds(pl.multiple_of(index * step, step), step)
            value = target[part].astype(F32)
            for term in terms:
                value = value + term[part].astype(F32)
            target[part] = value.astype(target.dtype)

    def own_sum(which, place):
        load(which, place).wait()
        to_core(which, place).wait_recv()
        add(mine.at[which, place], other.at[which, place])

    greet(row, col, core, across, along)
    for place in order:
        for which in (3, 1, 2, 0):
            to_core(which, place).start()
            load(which, place).start()

    def start_step(place):
        own_sum(3, place)
        give_one(place).start()
        give_two(place).start()
        own_sum(1, place)
        give_across(place, 0).start()
        own_sum(2, place)
        give_along(place, 1).start()

    def corner_step(place):
        give_two(place).wait_recv()
        add(mine.at[1, place, second], corner_two.at[place])
        give_across(place, 1).start()
        give_one(place).wait_recv()
        add(mine.at[2, place, first], corner_one.at[place])
        give_along(place, 0).start()

    def line_step(place):
        own_sum(0, place)
        for part in range(2):
            give_across(place, part).wait_recv()
            give_along(place, part).wait_recv()
        add(mine.at[0, place], from_across.at[place], from_along.at[place])

        @pl.when((place > col) & (col > 0))
        def _():
            give_up(place).wait_recv()
            add(mine.at[0, place], line.at[place])

        @pl.when((place < col) & (col < 3))
        def _():
            give_down(place, place).wait_recv()
            add(mine.at[0, place], line.at[place])

        @pl.when(place > col)
        def _():
            give_up(place).start()

        @pl.when((place < col) & (place < col - 1))
        def _():
            give_down(place, place).start()

        @pl.when((place < col) & (place == col - 1))
        def _():
            give_down(place, 4).start()

    for step in range(6):
        if step < 4:
            start_step(order[step])
        if 0 <= step - 1 < 4:
            corner_step(order[step - 1])
        if 0 <= step - 2 < 4:
            line_step(order[step - 2])

    @pl.when(col > 0)
    def _():
        give_up(col).wait_recv()
        add(mine.at[0, col], line.at[col])

    @pl.when(col < 3)
    def _():
        give_down(col, 4).wait_recv()
        add(mine.at[0, col], line.at[4])

    total[...] = mine[0, col]
    for place in order:
        for which in range(4):
            to_core(which, place).wait_send()
        give_one(place).wait_send()
        give_two(place).wait_send()
        for part in range(2):
            give_across(place, part).wait_send()
            give_along(place, part).wait_send()

        @pl.when(place > col)
        def _():
            give_up(place).wait_send()

        @pl.when(place < col)
        def _():
            give_down(place, place).wait_send()


def reduce_rows(values, collective_id):
    unused, rows, width = values.shape
    dtype = values.dtype
    return pl.pallas_call(
        reduce_kernel,
        out_shape=jax.ShapeDtypeStruct((rows, width), dtype),
        in_specs=[pl.BlockSpec(memory_space=pl.ANY)],
        out_specs=pl.BlockSpec(memory_space=pltpu.VMEM),
        scratch_shapes=[
            pltpu.VMEM((4, 4, rows, width), dtype),
            pltpu.VMEM((4, 4, rows, width), dtype),
            pltpu.VMEM((4, rows // 2, width), dtype),
            pltpu.VMEM((4, rows // 2, width), dtype),
            pltpu.VMEM((4, rows, width), dtype),
            pltpu.VMEM((4, rows, width), dtype),
            pltpu.VMEM((5, rows, width), dtype),
        ]
        + [pltpu.SemaphoreType.DMA((4, 4))] * 3
        + [pltpu.SemaphoreType.DMA((4,))] * 4
        + [pltpu.SemaphoreType.DMA((2, 4))] * 4
        + [pltpu.SemaphoreType.DMA((4,))] * 2
        + [pltpu.SemaphoreType.DMA((5,))],
        compiler_params=pltpu.CompilerParams(
            collective_id=collective_id, has_side_effects=True, vmem_limit_bytes=48 * 2**20
        ),
    )(values)


def transposed_product(left, right):
    return jnp.dot(left.T, right, preferred_element_type=F32)


def expert_kernel(
    expert_count, rows, grads, routed, gate_w, up_w, down_w, router,
    outputs, d_rows, inner, grad_gate, grad_up, grad_down, sum_gate, sum_up,
):
    step, last = pl.program_id(0), pl.num_programs(0) - 1
    row, col, core = (lax.axis_index(axis) for axis in ALL)
    expert = row * lax.axis_size("col") + col
    x, dy = rows[...], grads[...]
    lane = lax.broadcasted_iota(jnp.int32, (x.shape[0], router.shape[1]), 1)
    logits = jnp.where(lane < expert_count, matmul(x, router[...]), MASKED)
    raised = jnp.exp(logits - jnp.max(logits, axis=1, keepdims=True))
    picked = jnp.sum(jnp.where(lane == expert, raised, 0.0), axis=1, keepdims=True)
    gate = picked / jnp.sum(raised, axis=1, keepdims=True) * routed[...]
    pre_gate = matmul(x, gate_w[...])
    pre_up = matmul(x, up_w[...])
    back = contract_cols(dy, down_w[...])
    sigmoid_gate = 1.0 / (1.0 + jnp.exp(-pre_gate))
    silu_gate = pre_gate * sigmoid_gate
    hidden = (silu_gate * pre_up).astype(BF16).astype(F32)
    inner[...] = jnp.sum(hidden * back, axis=1, keepdims=True)
    weighted = (hidden * gate).astype(BF16)
    d_hid = back * gate
    d_gate = (d_hid * pre_up * (sigmoid_gate + silu_gate * (1.0 - sigmoid_gate))).astype(BF16)
    d_up = (d_hid * silu_gate).astype(BF16)
    outputs[...] = matmul(weighted, down_w[...]).astype(BF16)
    d_rows[...] = (contract_cols(d_gate, gate_w[...]) + contract_cols(d_up, up_w[...])).astype(BF16)

    @pl.when(step == 0)
    def _():
        grad_down[...] = transposed_product(weighted, dy)
        sum_gate[...] = transposed_product(d_gate, x)
        sum_up[...] = transposed_product(d_up, x)

    @pl.when(step > 0)
    def _():
        grad_down[...] += transposed_product(weighted, dy)
        sum_gate[...] += transposed_product(d_gate, x)
        sum_up[...] += transposed_product(d_up, x)

    @pl.when(step == last)
    def _():
        grad_gate[...] = sum_gate[...].T
        grad_up[...] = sum_up[...].T


def expert_products(rows, grads, routed, gate_w, up_w, down_w, router, chunk=512):
    count, width = rows.shape
    hidden = gate_w.shape[1]
    expert_count = router.shape[1]
    router = jnp.pad(router, ((0, 0), (0, 128 - expert_count)))

    def whole(shape):
        return pl.BlockSpec(shape, lambda i: (0, 0), pipeline_mode=pl.Buffered(1))

    def part(columns):
        return pl.BlockSpec((chunk, columns), lambda i: (i, 0))

    return pl.pallas_call(
        functools.partial(expert_kernel, expert_count),
        grid=(count // chunk,),
        in_specs=[part(width), part(width), part(1)]
        + [whole(w.shape) for w in (gate_w, up_w, down_w, router)],
        out_specs=[part(width), part(width), part(1)]
        + [whole(w.shape) for w in (gate_w, up_w, down_w)],
        out_shape=[
            jax.ShapeDtypeStruct((count, width), BF16),
            jax.ShapeDtypeStruct((count, width), BF16),
            jax.ShapeDtypeStruct((count, 1), F32),
            jax.ShapeDtypeStruct((width, hidden), F32),
            jax.ShapeDtypeStruct((width, hidden), F32),
            jax.ShapeDtypeStruct((hidden, width), F32),
        ],
        scratch_shapes=[pltpu.VMEM((hidden, width), F32), pltpu.VMEM((hidden, width), F32)],
        compiler_params=pltpu.CompilerParams(vmem_limit_bytes=60 * 2**20),
        cost_estimate=pl.CostEstimate(
            flops=18 * count * width * hidden,
            bytes_accessed=8 * count * width + 18 * width * hidden,
            transcendentals=count * hidden,
        ),
    )(rows, grads, routed, gate_w, up_w, down_w, router)


def expert_rows(rows, grads, gate, gate_w, up_w, down_w):
    pre_gate = matmul(rows, gate_w)
    pre_up = matmul(rows, up_w)
    back = contract_cols(grads, down_w)
    sigmoid_gate = jax.nn.sigmoid(pre_gate)
    silu_gate = pre_gate * sigmoid_gate
    hidden = (silu_gate * pre_up).astype(BF16)
    inner = jnp.sum(hidden.astype(F32) * back, axis=-1)
    weighted = (hidden.astype(F32) * gate).astype(BF16)
    d_hid = back * gate
    d_pregate = (d_hid * pre_up * (sigmoid_gate + silu_gate * (1.0 - sigmoid_gate))).astype(BF16)
    d_preup = (d_hid * silu_gate).astype(BF16)
    outputs = matmul(weighted, down_w).astype(BF16)
    d_rows = (contract_cols(d_pregate, gate_w) + contract_cols(d_preup, up_w)).astype(BF16)
    return (
        outputs,
        d_rows,
        inner,
        contract_rows(rows, d_pregate),
        contract_rows(rows, d_preup),
        contract_rows(weighted, grads),
    )


def experts(normed, grads, dense_gates, gate_w, up_w, down_w):
    rows_dev, width = normed.shape
    devices = math.prod(lax.axis_size(axis) for axis in ALL)
    expert_count = dense_gates.shape[1]
    expert = lax.axis_index(ALL) // 2
    parts = max(1, lax.axis_size("exp") // 2)
    step = rows_dev // parts

    def one_part(sums, piece):
        rows, grad_rows, gates = piece
        rows_all = lax.all_gather(rows, ALL, axis=0, tiled=True)
        grads_all = lax.all_gather(grad_rows, ALL, axis=0, tiled=True)
        gates_all = lax.all_gather(gates, ALL, axis=0, tiled=True)
        gate = lax.dynamic_slice_in_dim(gates_all, expert, 1, 1)
        got = expert_rows(rows_all, grads_all, gate, gate_w, up_w, down_w)
        outputs = lax.psum_scatter(got[0], ALL, scatter_dimension=0, tiled=True)
        d_rows = lax.psum_scatter(got[1], ALL, scatter_dimension=0, tiled=True)
        inner = lax.all_to_all(
            got[2].reshape(devices, step), ALL, split_axis=0, concat_axis=0, tiled=True
        )
        inner = inner.reshape(expert_count, 2, step).sum(axis=1).T
        sums = got[3:] if sums is None else tuple(a + b for a, b in zip(sums, got[3:]))
        return sums, (outputs, d_rows, inner)

    if parts == 1:
        sums, (outputs, d_rows, inner) = one_part(None, (normed, grads, dense_gates))
    else:
        start = tuple(jnp.zeros(w.shape, F32) for w in (gate_w, up_w, down_w))
        pieces = tuple(v.reshape(parts, step, -1) for v in (normed, grads, dense_gates))
        sums, got = lax.scan(one_part, start, pieces)
        outputs, d_rows, inner = (v.reshape(rows_dev, -1) for v in got)
    return outputs.astype(F32), d_rows.astype(F32), inner, sums


def experts_here(normed, gathered_grads, routes_all, router, gate_w, up_w, down_w):
    rows_dev, width = normed.shape
    devices = gathered_grads.shape[0]
    expert_count = router.shape[1]
    expert = lax.axis_index(ALL) // 2
    rows_all = gather_rows(normed, 1).reshape(-1, width)
    routed = jnp.any(routes_all == expert, axis=1, keepdims=True).astype(F32)
    got = expert_products(
        rows_all, gathered_grads.reshape(-1, width), routed, gate_w, up_w, down_w, router
    )
    d_rows = reduce_rows(got[1].reshape(devices, rows_dev, width), 2)
    outputs = reduce_rows(got[0].reshape(devices, rows_dev, width), 3)
    inner = lax.all_to_all(
        got[2].reshape(devices, rows_dev), ALL, split_axis=0, concat_axis=0, tiled=True
    )
    inner = inner.reshape(expert_count, 2, rows_dev).sum(axis=1).T
    return outputs.astype(F32), d_rows.astype(F32), inner, got[3:]


def shards(
    hidden_in,
    out_grad,
    attn_gain,
    w_qkv,
    q_gain,
    k_gain,
    w_out,
    moe_gain,
    router,
    w_gate,
    w_up,
    w_down,
    routes,
    doc_cuts,
):
    row_count, col_count = lax.axis_size("row"), lax.axis_size("col")
    tokens = hidden_in[0].astype(F32)
    rows_dev, width = tokens.shape
    heads = w_qkv.shape[1] // (3 * HD)
    plane = heads * HD
    scale = HD ** (-0.5)
    side = lax.axis_index("exp") % 2
    row_tok = rows_dev * col_count
    group_tok = row_tok * row_count
    here = (row_count, col_count, lax.axis_size("exp")) == (4, 4, 2)
    if here:
        gathered_grads = gather_rows(out_grad[0], 0)
        routes_all = lax.all_gather(routes[0], ALL, axis=0, tiled=True)
    cuts = lax.dynamic_index_in_dim(doc_cuts, lax.axis_index("exp") // 2, 0, keepdims=False)

    gain_one = attn_gain.astype(F32)
    scale_one = rms_scale(tokens)
    normed_one = (tokens * scale_one * gain_one).astype(BF16)
    normed_row = lax.all_gather(normed_one, "col", axis=0, tiled=True)
    qkv_w = lax.all_gather(w_qkv, "row", axis=0, tiled=True)
    out_w = lax.all_gather(lax.all_gather(w_out, "row", axis=1, tiled=True), "col", axis=0, tiled=True)
    qkv = matmul(normed_row, qkv_w).reshape(row_tok, heads, 3, HD)
    query_raw, key_raw, value_raw = qkv[:, :, 0], qkv[:, :, 1], qkv[:, :, 2]
    total_q, total_k = lax.psum(
        (jnp.sum(query_raw * query_raw, axis=(1, 2)), jnp.sum(key_raw * key_raw, axis=(1, 2))), "col"
    )
    scale_q = lax.rsqrt(total_q / width + EPSILON)[:, None, None]
    scale_k = lax.rsqrt(total_k / width + EPSILON)[:, None, None]
    head_start = lax.axis_index("col") * plane
    gain_q = lax.dynamic_slice_in_dim(q_gain, head_start, plane, 0).astype(F32).reshape(heads, HD)
    gain_k = lax.dynamic_slice_in_dim(k_gain, head_start, plane, 0).astype(F32).reshape(heads, HD)
    row_places = side * group_tok + lax.axis_index("row") * row_tok + jnp.arange(row_tok, dtype=jnp.int32)
    unused_doc, position = doc_positions(row_places, cuts)
    cosine, sine = rope_tables(position, HD)
    cosine, sine = cosine[:, None, :], sine[:, None, :]
    query = rotate(query_raw * scale_q * gain_q, cosine, sine).astype(BF16)
    key = rotate(key_raw * scale_k * gain_k, cosine, sine).astype(BF16)
    moved = rows_to_heads(jnp.concatenate([query, key, value_raw.astype(BF16)], axis=-1))

    query, own_pair = moved[:, :HD], moved[:, HD:]
    earlier_pair = from_behind(own_pair, "exp", 1)
    lower_pair = jnp.where(side == 0, own_pair, earlier_pair)
    upper_pair = jnp.where(side == 0, jnp.zeros_like(own_pair), own_pair)
    key_value = jnp.concatenate([lower_pair, upper_pair], axis=0)
    key_all, value_all = key_value[:, :HD], key_value[:, HD:]
    mixed_wide, total = attend(query, key_all, value_all, cuts, scale)
    mixed = mixed_wide.astype(BF16)
    mixed_row = heads_to_rows(mixed).reshape(row_tok, plane)
    middle = tokens + matmul(heads_to_tokens(mixed), out_w)

    gain_two = moe_gain.astype(F32)
    scale_two = rms_scale(middle)
    normed_two = (middle * scale_two * gain_two).astype(BF16)
    gates_all = jax.nn.softmax(matmul(normed_two, router), axis=-1)
    picks = routes[0]
    chosen = jnp.any(
        picks[:, :, None] == jnp.arange(router.shape[1], dtype=jnp.int32)[None, None, :], axis=1
    )
    grad_out = out_grad[0].astype(F32)
    expert_w = (w_gate[0], w_up[0], w_down[0])
    if here:
        mixture, d_normed_two, inner, weight_grads = experts_here(
            normed_two, gathered_grads, routes_all, router, *expert_w
        )
    else:
        dense_gates = jnp.where(chosen, gates_all, 0.0)
        mixture, d_normed_two, inner, weight_grads = experts(
            normed_two, out_grad[0], dense_gates, *expert_w
        )
    final = middle + mixture
    dense = jnp.where(chosen, inner, 0.0)
    d_logits = (gates_all * (dense - jnp.sum(gates_all * dense, axis=-1, keepdims=True))).astype(BF16)
    grad_router = contract_rows(normed_two, d_logits)
    d_normed_two = d_normed_two + contract_cols(d_logits, router)
    grad_moe_gain = jnp.sum(d_normed_two * middle * scale_two, axis=0)
    weighted_two = d_normed_two * gain_two
    d_middle = (
        grad_out
        + scale_two * weighted_two
        - middle * scale_two**3 * jnp.mean(weighted_two * middle, axis=-1, keepdims=True)
    )

    d_attn = d_middle.astype(BF16)
    d_mixed = tokens_to_heads(contract_cols(d_attn, out_w).astype(BF16))
    d_attn_row = lax.all_gather(d_attn, "col", axis=0, tiled=True)
    grad_w_out = lax.psum_scatter(
        contract_rows(mixed_row, d_attn_row).astype(BF16), "row", scatter_dimension=1, tiled=True
    )
    d_query, acc_key, acc_value = attend_back(
        query, key_all, value_all, d_mixed, mixed_wide, total, cuts, scale
    )
    accumulated = jnp.concatenate([acc_key, acc_value], axis=1)
    lower_acc, upper_acc = accumulated[:group_tok], accumulated[group_tok:]
    kept_acc = jnp.where(side == 0, lower_acc, upper_acc)
    later_acc = from_behind(lower_acc.astype(BF16), "exp", -1).astype(F32)
    summed_pair = kept_acc + jnp.where(side == 0, later_acc, jnp.zeros_like(later_acc))
    d_heads = heads_to_rows(jnp.concatenate([d_query, summed_pair], axis=1).astype(BF16)).astype(F32)
    d_q_unit = rotate_back(d_heads[:, :, :HD], cosine, sine)
    d_k_unit = rotate_back(d_heads[:, :, HD : 2 * HD], cosine, sine)
    d_value = d_heads[:, :, 2 * HD :]
    weighted_q = d_q_unit * gain_q
    weighted_k = d_k_unit * gain_k
    sum_q, sum_k = lax.psum(
        (jnp.sum(weighted_q * query_raw, axis=(1, 2)), jnp.sum(weighted_k * key_raw, axis=(1, 2))),
        "col",
    )
    d_query_raw = scale_q * weighted_q - query_raw * scale_q**3 * (sum_q / width)[:, None, None]
    d_key_raw = scale_k * weighted_k - key_raw * scale_k**3 * (sum_k / width)[:, None, None]
    grad_q_part = jnp.sum(d_q_unit * query_raw * scale_q, axis=0).reshape(plane)
    grad_k_part = jnp.sum(d_k_unit * key_raw * scale_k, axis=0).reshape(plane)
    d_qkv = jnp.concatenate([d_query_raw, d_key_raw, d_value], axis=2).astype(BF16)
    d_qkv = d_qkv.reshape(row_tok, heads * 3 * HD)
    d_normed_one = lax.psum_scatter(
        contract_cols(d_qkv, qkv_w).astype(BF16), "col", scatter_dimension=0, tiled=True
    ).astype(F32)
    grad_qkv = lax.psum_scatter(
        contract_rows(normed_row, d_qkv).astype(BF16), "row", scatter_dimension=0, tiled=True
    )
    grad_attn_gain = jnp.sum(d_normed_one * tokens * scale_one, axis=0)
    weighted_one = d_normed_one * gain_one
    grad_hidden = (
        d_middle
        + scale_one * weighted_one
        - tokens * scale_one**3 * jnp.mean(weighted_one * tokens, axis=-1, keepdims=True)
    )
    grad_qkv, grad_w_out = (
        lax.psum(grad_qkv, "exp").astype(F32),
        lax.psum(grad_w_out, "exp").astype(F32),
    )
    empty = jnp.zeros((width,), F32)
    grad_q_full = lax.dynamic_update_slice_in_dim(empty, grad_q_part, head_start, 0)
    grad_k_full = lax.dynamic_update_slice_in_dim(empty, grad_k_part, head_start, 0)
    summed = lax.psum((grad_attn_gain, grad_q_full, grad_k_full, grad_moe_gain, grad_router), ALL)
    return (
        final.astype(BF16)[None],
        grad_hidden[None],
        summed[0],
        grad_qkv,
        summed[1],
        summed[2],
        grad_w_out,
        summed[3],
        summed[4],
        weight_grads[0][None],
        weight_grads[1][None],
        weight_grads[2][None],
    )


def solution(mesh):
    token_spec = P("exp", ("row", "col"), None)
    expert_spec = P(("row", "col", "exp"), None, None)
    in_specs = (
        token_spec,
        token_spec,
        P(),
        P("row", "col"),
        P(),
        P(),
        P("col", "row"),
        P(),
        P(),
        expert_spec,
        expert_spec,
        expert_spec,
        token_spec,
        P(),
    )
    out_specs = (
        token_spec,
        token_spec,
        P(),
        P("row", "col"),
        P(),
        P(),
        P("col", "row"),
        P(),
        P(),
        expert_spec,
        expert_spec,
        expert_spec,
    )
    return jax.shard_map(shards, mesh=mesh, in_specs=in_specs, out_specs=out_specs, check_vma=False)
```

```python
import functools
import math

import jax
import jax.numpy as jnp
from jax import lax
from jax.experimental import pallas as pl
from jax.experimental.pallas import tpu as pltpu
from jax.sharding import PartitionSpec as P

HD = 128
EPSILON = 1e-05
ROPE_BASE = 10000.0
MASKED = -1e30
BF16 = jnp.bfloat16
F32 = jnp.float32


def matmul(left, right):
    return jnp.dot(left, right, preferred_element_type=F32)


def contract_rows(left, right):
    return lax.dot_general(left, right, (((0,), (0,)), ((), ())), preferred_element_type=F32)


def contract_cols(left, right):
    return lax.dot_general(left, right, (((1,), (1,)), ((), ())), preferred_element_type=F32)


def rms_scale(values):
    return lax.rsqrt(jnp.mean(values * values, axis=-1, keepdims=True) + EPSILON)


def rope_tables(position, width):
    frequency = ROPE_BASE ** (-jnp.arange(0, width, 2, dtype=F32) / width)
    angle = position.astype(F32)[:, None] * frequency[None, :]
    return (
        jnp.concatenate([jnp.cos(angle)] * 2, axis=-1),
        jnp.concatenate([jnp.sin(angle)] * 2, axis=-1),
    )


def rotate(values, cosine, sine):
    half = values.shape[-1] // 2
    turned = jnp.concatenate([-values[..., half:], values[..., :half]], axis=-1)
    return values * cosine + turned * sine


def rotate_back(values, cosine, sine):
    half = values.shape[-1] // 2
    turned = values * sine
    return values * cosine + jnp.concatenate([turned[..., half:], -turned[..., :half]], axis=-1)


def doc_positions(places, cuts):
    first = (places >= cuts[0]).astype(jnp.int32)
    second = (places >= cuts[1]).astype(jnp.int32)
    start = first * cuts[0] + second * (cuts[1] - cuts[0])
    return (first + second, places - start)


def from_behind(value, axis, steps):
    count = lax.axis_size(axis)
    initial, last = (max(0, -steps), min(count, count - steps))
    return lax.ppermute(value, axis, [(source, source + steps) for source in range(initial, last)])


def rows_to_heads(values):
    count = lax.axis_size("row")
    rows, heads, width = values.shape
    moved = lax.all_to_all(values.transpose(1, 0, 2), "row", split_axis=0, concat_axis=0, tiled=True)
    return moved.reshape(count * rows, width)


def heads_to_rows(values):
    count = lax.axis_size("row")
    rows, width = values.shape
    moved = lax.all_to_all(
        values.reshape(count, rows // count, width), "row", split_axis=0, concat_axis=0, tiled=True
    )
    return moved.transpose(1, 0, 2)


def heads_to_tokens(values):
    row_count, col_count = lax.axis_size("row"), lax.axis_size("col")
    rows = values.shape[0] // (row_count * col_count)
    moved = lax.all_to_all(
        values.reshape(row_count * col_count, rows, HD),
        ("row", "col"),
        split_axis=0,
        concat_axis=0,
        tiled=True,
    )
    moved = moved.reshape(row_count, col_count, rows, HD).transpose(2, 1, 0, 3)
    return moved.reshape(rows, row_count * col_count * HD)


def tokens_to_heads(values):
    row_count, col_count = lax.axis_size("row"), lax.axis_size("col")
    rows = values.shape[0]
    parted = values.reshape(rows, col_count, row_count, HD).transpose(2, 1, 0, 3)
    moved = lax.all_to_all(
        parted.reshape(row_count * col_count, rows, HD),
        ("row", "col"),
        split_axis=0,
        concat_axis=0,
        tiled=True,
    )
    return moved.reshape(row_count * col_count * rows, HD)


MESH = pl.DeviceIdType.MESH
ALL = ("row", "col", "exp")


class Here:
    def __init__(self):
        self.row, self.col, self.core = (lax.axis_index(axis) for axis in ALL)
        self.across = self.row + 1 - 2 * (self.row % 2)
        self.along = (self.row + 2) % 4
        self.opposite = 3 - self.row
        self.rows = (self.row, self.across, self.along, self.opposite)
        half = self.col // 2
        self.near_first = [
            self.col,
            1 + self.col % 2,
            2 - self.col - self.col % 2 + 3 * half,
            3 - 3 * half,
        ]

    def at_row(self, row):
        return (row, self.col, self.core)

    def at_col(self, col):
        return (self.row, col, self.core)

    def other_core(self):
        return (self.row, self.col, 1 - self.core)

    def line_peers(self):
        return [self.at_col((self.col + step) % 4) for step in (1, 2, 3)]

    def plane_peers(self):
        return [self.at_row(row) for row in self.rows[1:]]


def greet(peers):
    barrier = pltpu.get_barrier_semaphore()
    for peer in peers:
        pl.semaphore_signal(barrier, inc=1, device_id=peer, device_id_type=MESH)
    pl.semaphore_wait(barrier, len(peers))


def greet_near(here):
    barrier = pltpu.get_barrier_semaphore()
    col = here.col

    def signal(peer):
        pl.semaphore_signal(barrier, inc=1, device_id=peer, device_id_type=MESH)

    for peer in (here.other_core(), here.at_row(here.across), here.at_row(here.along)):
        signal(peer)

    @pl.when(col > 0)
    def _():
        signal(here.at_col(col - 1))

    @pl.when(col < 3)
    def _():
        signal(here.at_col(col + 1))

    pl.semaphore_wait(barrier, 3 + (col + 3) // 4 + (6 - col) // 4)


def remote(source, target, send, recv, device):
    return pltpu.make_async_remote_copy(
        src_ref=source,
        dst_ref=target,
        send_sem=send,
        recv_sem=recv,
        device_id=device,
        device_id_type=MESH,
    )


def arrived(target, recv):
    pltpu.make_async_copy(target, target, recv).wait()


def add_into(target, *terms):
    step = 16

    @pl.loop(0, target.shape[0] // step)
    def _(index):
        part = pl.ds(pl.multiple_of(index * step, step), step)
        value = target[part].astype(F32)
        for term in terms:
            value = value + term[part].astype(F32)
        target[part] = value.astype(target.dtype)


SPREAD_SEMS = [pltpu.SemaphoreType.DMA((4,))] * 11 + [pltpu.SemaphoreType.DMA((4, 4))] * 2


class Spread:
    def __init__(self, here, own, block, rows, sems, line=True, plane=True):
        self.here, self.own, self.block, self.line, self.plane = here, own, block, line, plane
        (
            self.up_send, self.down_send, self.line_recv,
            self.across_send, self.across_recv, self.along_send, self.along_recv,
            self.one_send, self.one_recv, self.two_send, self.two_recv,
            self.core_send, self.core_recv,
        ) = sems
        self.first, self.second = pl.ds(0, rows // 2), pl.ds(rows // 2, rows // 2)
        self.order = here.near_first if line else [0]
        self.steps = len(self.order)

    def held(self, step):
        here = self.here
        return self.own if step == 0 else self.block(here.row, self.order[step], here.core)

    def up(self, step):
        here, place = self.here, self.order[step]
        target = self.block(here.row, place, here.core)
        recv = self.line_recv.at[place]
        return remote(self.held(step), target, self.up_send.at[place], recv, here.at_col(here.col + 1))

    def down(self, step):
        here, place = self.here, self.order[step]
        target = self.block(here.row, place, here.core)
        recv = self.line_recv.at[place]
        return remote(self.held(step), target, self.down_send.at[place], recv, here.at_col(here.col - 1))

    def to_across(self, step):
        here, place = self.here, self.order[step]
        target = self.block(here.row, place, here.core)
        sems = self.across_send.at[place], self.across_recv.at[place]
        return remote(self.held(step), target, *sems, here.at_row(here.across))

    def to_along(self, step):
        here, place = self.here, self.order[step]
        target = self.block(here.row, place, here.core)
        sems = self.along_send.at[place], self.along_recv.at[place]
        return remote(self.held(step), target, *sems, here.at_row(here.along))

    def corner_one(self, step):
        here, place = self.here, self.order[step]
        part = self.block(here.across, place, here.core).at[self.first]
        sems = self.one_send.at[place], self.one_recv.at[place]
        return remote(part, part, *sems, here.at_row(here.along))

    def corner_two(self, step):
        here, place = self.here, self.order[step]
        part = self.block(here.along, place, here.core).at[self.second]
        sems = self.two_send.at[place], self.two_recv.at[place]
        return remote(part, part, *sems, here.at_row(here.across))

    def to_core(self, which, step):
        here, place = self.here, self.order[step]
        target = self.block(here.rows[which], place, here.core)
        source = self.held(step) if which == 0 else target
        sems = self.core_send.at[which, place], self.core_recv.at[which, place]
        return remote(source, target, *sems, here.other_core())

    def line_step(self, step):
        here, place = self.here, self.order[step]
        if step > 0:
            arrived(self.held(step), self.line_recv.at[place])
        if self.line:

            @pl.when((place <= here.col) & (here.col < 3))
            def _():
                self.up(step).start()

            @pl.when((place >= here.col) & (here.col > 0))
            def _():
                self.down(step).start()

        if self.plane:
            self.to_across(step).start()
            self.to_along(step).start()
            self.to_core(0, step).start()

    def plane_step(self, step):
        here, place = self.here, self.order[step]
        arrived(self.block(here.across, place, here.core), self.across_recv.at[place])
        self.corner_one(step).start()
        self.to_core(1, step).start()
        arrived(self.block(here.along, place, here.core), self.along_recv.at[place])
        self.corner_two(step).start()
        self.to_core(2, step).start()

    def corner_step(self, step):
        here, place = self.here, self.order[step]
        target = self.block(here.opposite, place, here.core)
        arrived(target.at[self.first], self.one_recv.at[place])
        arrived(target.at[self.second], self.two_recv.at[place])
        self.to_core(3, step).start()

    def step(self, index):
        if index < self.steps:
            self.line_step(index)
        if self.plane and 0 <= index - 1 < self.steps:
            self.plane_step(index - 1)
        if self.plane and 0 <= index - 2 < self.steps:
            self.corner_step(index - 2)

    def core_arrived(self, which, step):
        here, place = self.here, self.order[step]
        target = self.block(here.rows[which], place, 1 - here.core)
        arrived(target, self.core_recv.at[which, place])

    def finish(self, arrivals=True):
        here = self.here
        for step in range(self.steps):
            place = self.order[step]
            if self.line:

                @pl.when((place <= here.col) & (here.col < 3))
                def _():
                    self.up(step).wait_send()

                @pl.when((place >= here.col) & (here.col > 0))
                def _():
                    self.down(step).wait_send()

            if self.plane:
                self.to_across(step).wait_send()
                self.to_along(step).wait_send()
                self.corner_one(step).wait_send()
                self.corner_two(step).wait_send()
                for which in range(4):
                    self.to_core(which, step).wait_send()
                    if arrivals:
                        self.core_arrived(which, step)


def gather_kernel(own, out, kept, *sems):
    here = Here()

    def block(row, col, core):
        return out.at[(row * 4 + col) * 2 + core]

    greet_near(here)
    keep = pltpu.make_async_copy(own, block(here.row, here.col, here.core), kept)
    keep.start()
    spread = Spread(here, own, block, own.shape[0], sems)
    for index in range(6):
        spread.step(index)
    keep.wait()
    spread.finish()


def gather_rows(values, collective_id):
    return pl.pallas_call(
        gather_kernel,
        out_shape=jax.ShapeDtypeStruct((32,) + values.shape, values.dtype),
        in_specs=[pl.BlockSpec(memory_space=pl.ANY)],
        out_specs=pl.BlockSpec(memory_space=pl.ANY),
        scratch_shapes=[pltpu.SemaphoreType.DMA] + SPREAD_SEMS,
        compiler_params=pltpu.CompilerParams(collective_id=collective_id, has_side_effects=True),
    )(values)


def reduce_kernel(values, total, mine, other, corner_one, corner_two, from_across, from_along, line, *sems):
    (
        mine_sem, other_send, other_recv,
        corner_one_send, corner_one_recv, corner_two_send, corner_two_recv,
        across_send, across_recv, along_send, along_recv,
        up_send, down_send, line_recv,
    ) = sems
    here = Here()
    row, col, core, across, along = here.row, here.col, here.core, here.across, here.along
    rows = here.rows
    half = total.shape[0] // 2
    order = here.near_first[::-1]
    first, second = pl.ds(0, half), pl.ds(half, half)

    def block(of_row, of_col, of_core):
        return values.at[(of_row * 4 + of_col) * 2 + of_core]

    def load(which, place):
        return pltpu.make_async_copy(
            block(rows[which], place, core), mine.at[which, place], mine_sem.at[which, place]
        )

    def to_core(which, place):
        return remote(
            block(rows[which], place, 1 - core),
            other.at[which, place],
            other_send.at[which, place],
            other_recv.at[which, place],
            (row, col, 1 - core),
        )

    def give_one(place):
        return remote(
            mine.at[3, place, first], corner_one.at[place],
            corner_one_send.at[place], corner_one_recv.at[place], (across, col, core),
        )

    def give_two(place):
        return remote(
            mine.at[3, place, second], corner_two.at[place],
            corner_two_send.at[place], corner_two_recv.at[place], (along, col, core),
        )

    def give_across(place, part):
        return remote(
            mine.at[1, place, (first, second)[part]], from_across.at[place, (first, second)[part]],
            across_send.at[part, place], across_recv.at[part, place], (across, col, core),
        )

    def give_along(place, part):
        return remote(
            mine.at[2, place, (first, second)[part]], from_along.at[place, (first, second)[part]],
            along_send.at[part, place], along_recv.at[part, place], (along, col, core),
        )

    def give_up(place):
        return remote(
            mine.at[0, place], line.at[place], up_send.at[place], line_recv.at[place], (row, col + 1, core)
        )

    def give_down(place, slot):
        return remote(
            mine.at[0, place], line.at[slot], down_send.at[place], line_recv.at[slot], (row, col - 1, core)
        )

    def own_sum(which, place):
        load(which, place).wait()
        to_core(which, place).wait_recv()
        add_into(mine.at[which, place], other.at[which, place])

    greet_near(here)
    for place in order:
        for which in (3, 1, 2, 0):
            to_core(which, place).start()
            load(which, place).start()

    def start_step(place):
        own_sum(3, place)
        give_one(place).start()
        give_two(place).start()
        own_sum(1, place)
        give_across(place, 0).start()
        own_sum(2, place)
        give_along(place, 1).start()

    def corner_step(place):
        give_two(place).wait_recv()
        add_into(mine.at[1, place, second], corner_two.at[place])
        give_across(place, 1).start()
        give_one(place).wait_recv()
        add_into(mine.at[2, place, first], corner_one.at[place])
        give_along(place, 0).start()

    def line_step(place):
        own_sum(0, place)
        for part in range(2):
            give_across(place, part).wait_recv()
            give_along(place, part).wait_recv()
        add_into(mine.at[0, place], from_across.at[place], from_along.at[place])

        @pl.when((place > col) & (col > 0))
        def _():
            give_up(place).wait_recv()
            add_into(mine.at[0, place], line.at[place])

        @pl.when((place < col) & (col < 3))
        def _():
            give_down(place, place).wait_recv()
            add_into(mine.at[0, place], line.at[place])

        @pl.when(place > col)
        def _():
            give_up(place).start()

        @pl.when((place < col) & (place < col - 1))
        def _():
            give_down(place, place).start()

        @pl.when((place < col) & (place == col - 1))
        def _():
            give_down(place, 4).start()

    for step in range(6):
        if step < 4:
            start_step(order[step])
        if 0 <= step - 1 < 4:
            corner_step(order[step - 1])
        if 0 <= step - 2 < 4:
            line_step(order[step - 2])

    @pl.when(col > 0)
    def _():
        give_up(col).wait_recv()
        add_into(mine.at[0, col], line.at[col])

    @pl.when(col < 3)
    def _():
        give_down(col, 4).wait_recv()
        add_into(mine.at[0, col], line.at[4])

    total[...] = mine[0, col]
    for place in order:
        for which in range(4):
            to_core(which, place).wait_send()
        give_one(place).wait_send()
        give_two(place).wait_send()
        for part in range(2):
            give_across(place, part).wait_send()
            give_along(place, part).wait_send()

        @pl.when(place > col)
        def _():
            give_up(place).wait_send()

        @pl.when(place < col)
        def _():
            give_down(place, place).wait_send()


def reduce_rows(values, collective_id):
    unused, rows, width = values.shape
    dtype = values.dtype
    return pl.pallas_call(
        reduce_kernel,
        out_shape=jax.ShapeDtypeStruct((rows, width), dtype),
        in_specs=[pl.BlockSpec(memory_space=pl.ANY)],
        out_specs=pl.BlockSpec(memory_space=pltpu.VMEM),
        scratch_shapes=[
            pltpu.VMEM((4, 4, rows, width), dtype),
            pltpu.VMEM((4, 4, rows, width), dtype),
            pltpu.VMEM((4, rows // 2, width), dtype),
            pltpu.VMEM((4, rows // 2, width), dtype),
            pltpu.VMEM((4, rows, width), dtype),
            pltpu.VMEM((4, rows, width), dtype),
            pltpu.VMEM((5, rows, width), dtype),
        ]
        + [pltpu.SemaphoreType.DMA((4, 4))] * 3
        + [pltpu.SemaphoreType.DMA((4,))] * 4
        + [pltpu.SemaphoreType.DMA((2, 4))] * 4
        + [pltpu.SemaphoreType.DMA((4,))] * 2
        + [pltpu.SemaphoreType.DMA((5,))],
        compiler_params=pltpu.CompilerParams(
            collective_id=collective_id, has_side_effects=True, vmem_limit_bytes=48 * 2**20
        ),
    )(values)


def doc_start(places, cuts):
    return jnp.where(places >= cuts[1], cuts[1], jnp.where(places >= cuts[0], cuts[0], 0))


def key_blocks(cuts, first_query, rows, scores_of, block_fn):
    def scan(index, carry):
        start = pl.multiple_of(index * rows, rows)
        free = (start >= doc_start(first_query + rows - 1, cuts)) & (start + rows <= first_query + 1)

        @pl.when(free)
        def _():
            block_fn(start, scores_of(start))

        @pl.when(jnp.logical_not(free))
        def _():
            key_place = start + lax.broadcasted_iota(jnp.int32, (rows, rows), 0)
            place = first_query + lax.broadcasted_iota(jnp.int32, (1, rows), 1)
            allowed = (key_place <= place) & (key_place >= doc_start(place, cuts))
            block_fn(start, jnp.where(allowed, scores_of(start), MASKED))

        return carry

    lax.fori_loop(doc_start(first_query, cuts) // rows, first_query // rows + 1, scan, 0)


def attend_kernel(scale, group_tok, cuts, query, keys, values_t, mixed, total, top, summed, acc):
    rows = query.shape[0]
    side = lax.axis_index("exp") % 2
    first_query = side * group_tok + pl.program_id(0) * rows
    top[...] = jnp.full_like(top, MASKED)
    summed[...] = jnp.zeros_like(summed)
    acc[...] = jnp.zeros_like(acc)
    cut = (cuts[0, 0], cuts[0, 1])

    def scores_of(start):
        return contract_cols(keys[pl.ds(start, rows)], query[...]) * scale

    def block_fn(start, scores):
        old = top[...]
        new = jnp.maximum(old, jnp.max(scores, axis=0, keepdims=True))
        weights = jnp.exp(scores - new)
        decay = jnp.exp(old - new)
        top[...] = new
        summed[...] = summed[...] * decay + jnp.sum(weights, axis=0, keepdims=True)
        acc[...] = acc[...] * decay + matmul(values_t[:, pl.ds(start, rows)], weights.astype(BF16))

    key_blocks(cut, first_query, rows, scores_of, block_fn)
    mixed[...] = (acc[...] / summed[...]).T
    total[...] = top[...] + jnp.log(summed[...])


def attend(query, keys, values, cuts, scale, rows=512):
    group_tok, head_size = query.shape
    whole = lambda shape: pl.BlockSpec(shape, lambda i: (0, 0))
    return pl.pallas_call(
        functools.partial(attend_kernel, scale, group_tok),
        grid=(group_tok // rows,),
        in_specs=[
            pl.BlockSpec(memory_space=pltpu.SMEM),
            pl.BlockSpec((rows, head_size), lambda i: (i, 0)),
            whole(keys.shape),
            whole(values.shape[::-1]),
        ],
        out_specs=[
            pl.BlockSpec((rows, head_size), lambda i: (i, 0)),
            pl.BlockSpec((1, rows), lambda i: (0, i)),
        ],
        out_shape=[
            jax.ShapeDtypeStruct((group_tok, head_size), F32),
            jax.ShapeDtypeStruct((1, group_tok), F32),
        ],
        scratch_shapes=[
            pltpu.VMEM((1, rows), F32),
            pltpu.VMEM((1, rows), F32),
            pltpu.VMEM((head_size, rows), F32),
        ],
        compiler_params=pltpu.CompilerParams(vmem_limit_bytes=40 * 2**20),
        cost_estimate=pl.CostEstimate(
            flops=4 * 7 * 2**20 * head_size, bytes_accessed=2**23, transcendentals=7 * 2**20
        ),
    )(cuts[None], query, keys, values.T)


def attend_back_kernel(
    scale, group_tok, cuts, query, keys, keys_t, values, d_mixed, total, delta,
    d_query, d_keys, d_values, acc,
):
    rows = query.shape[0]
    side = lax.axis_index("exp") % 2
    first_query = side * group_tok + pl.program_id(0) * rows
    cut = (cuts[0, 0], cuts[0, 1])

    @pl.when(pl.program_id(0) == 0)
    def _():
        d_keys[...] = jnp.zeros_like(d_keys)
        d_values[...] = jnp.zeros_like(d_values)

    acc[...] = jnp.zeros_like(acc)

    def scores_of(start):
        return contract_cols(keys[pl.ds(start, rows)], query[...]) * scale

    def block_fn(start, scores):
        part = pl.ds(start, rows)
        weights = jnp.exp(scores - total[...])
        d_weights = contract_cols(values[part], d_mixed[...])
        d_scores = (weights * (d_weights - delta[...])).astype(BF16)
        d_values[part] += matmul(weights.astype(BF16), d_mixed[...])
        d_keys[part] += matmul(d_scores, query[...]) * scale
        acc[...] += matmul(keys_t[:, part], d_scores)

    key_blocks(cut, first_query, rows, scores_of, block_fn)
    d_query[...] = (acc[...] * scale).T


def attend_back(query, keys, values, d_mixed, mixed, total, cuts, scale, rows=512):
    group_tok, head_size = query.shape
    delta = jnp.sum(d_mixed.astype(F32) * mixed, axis=1)[None]
    whole = lambda shape: pl.BlockSpec(shape, lambda i: (0, 0))
    block = pl.BlockSpec((rows, head_size), lambda i: (i, 0))
    line = pl.BlockSpec((1, rows), lambda i: (0, i))
    return pl.pallas_call(
        functools.partial(attend_back_kernel, scale, group_tok),
        grid=(group_tok // rows,),
        in_specs=[
            pl.BlockSpec(memory_space=pltpu.SMEM),
            block,
            whole(keys.shape),
            whole(keys.shape[::-1]),
            whole(keys.shape),
            block,
            line,
            line,
        ],
        out_specs=[block, whole(keys.shape), whole(keys.shape)],
        out_shape=[
            jax.ShapeDtypeStruct((group_tok, head_size), F32),
            jax.ShapeDtypeStruct(keys.shape, F32),
            jax.ShapeDtypeStruct(keys.shape, F32),
        ],
        scratch_shapes=[pltpu.VMEM((head_size, rows), F32)],
        compiler_params=pltpu.CompilerParams(vmem_limit_bytes=48 * 2**20),
        cost_estimate=pl.CostEstimate(
            flops=10 * 7 * 2**20 * head_size, bytes_accessed=2**23, transcendentals=7 * 2**20
        ),
    )(cuts[None], query, keys, keys.T, values, d_mixed, total, delta)


def transposed_product(left, right):
    return jnp.dot(left.T, right, preferred_element_type=F32)


def expert_kernel(
    expert_count, rows, grads, routed, gate_w, up_w, down_w, router,
    outputs, d_rows, inner, grad_gate, grad_up, grad_down, sum_gate, sum_up,
):
    step, last = pl.program_id(0), pl.num_programs(0) - 1
    row, col, core = (lax.axis_index(axis) for axis in ALL)
    expert = row * lax.axis_size("col") + col
    x, dy = rows[...], grads[...]
    lane = lax.broadcasted_iota(jnp.int32, (x.shape[0], router.shape[1]), 1)
    logits = jnp.where(lane < expert_count, matmul(x, router[...]), MASKED)
    raised = jnp.exp(logits - jnp.max(logits, axis=1, keepdims=True))
    picked = jnp.sum(jnp.where(lane == expert, raised, 0.0), axis=1, keepdims=True)
    gate = picked / jnp.sum(raised, axis=1, keepdims=True) * routed[...]
    pre_gate = matmul(x, gate_w[...])
    pre_up = matmul(x, up_w[...])
    back = contract_cols(dy, down_w[...])
    sigmoid_gate = 1.0 / (1.0 + jnp.exp(-pre_gate))
    silu_gate = pre_gate * sigmoid_gate
    hidden = (silu_gate * pre_up).astype(BF16).astype(F32)
    inner[...] = jnp.sum(hidden * back, axis=1, keepdims=True)
    weighted = (hidden * gate).astype(BF16)
    d_hid = back * gate
    d_gate = (d_hid * pre_up * (sigmoid_gate + silu_gate * (1.0 - sigmoid_gate))).astype(BF16)
    d_up = (d_hid * silu_gate).astype(BF16)
    outputs[...] = matmul(weighted, down_w[...]).astype(BF16)
    d_rows[...] = (contract_cols(d_gate, gate_w[...]) + contract_cols(d_up, up_w[...])).astype(BF16)

    @pl.when(step == 0)
    def _():
        grad_down[...] = transposed_product(weighted, dy)
        sum_gate[...] = transposed_product(d_gate, x)
        sum_up[...] = transposed_product(d_up, x)

    @pl.when(step > 0)
    def _():
        grad_down[...] += transposed_product(weighted, dy)
        sum_gate[...] += transposed_product(d_gate, x)
        sum_up[...] += transposed_product(d_up, x)

    @pl.when(step == last)
    def _():
        grad_gate[...] = sum_gate[...].T
        grad_up[...] = sum_up[...].T


def expert_products(rows, grads, routed, gate_w, up_w, down_w, router, chunk=512):
    count, width = rows.shape
    hidden = gate_w.shape[1]
    expert_count = router.shape[1]
    router = jnp.pad(router, ((0, 0), (0, 128 - expert_count)))

    def whole(shape):
        return pl.BlockSpec(shape, lambda i: (0, 0), pipeline_mode=pl.Buffered(1))

    def part(columns):
        return pl.BlockSpec((chunk, columns), lambda i: (i, 0))

    return pl.pallas_call(
        functools.partial(expert_kernel, expert_count),
        grid=(count // chunk,),
        in_specs=[part(width), part(width), part(1)]
        + [whole(w.shape) for w in (gate_w, up_w, down_w, router)],
        out_specs=[part(width), part(width), part(1)]
        + [whole(w.shape) for w in (gate_w, up_w, down_w)],
        out_shape=[
            jax.ShapeDtypeStruct((count, width), BF16),
            jax.ShapeDtypeStruct((count, width), BF16),
            jax.ShapeDtypeStruct((count, 1), F32),
            jax.ShapeDtypeStruct((width, hidden), F32),
            jax.ShapeDtypeStruct((width, hidden), F32),
            jax.ShapeDtypeStruct((hidden, width), F32),
        ],
        scratch_shapes=[pltpu.VMEM((hidden, width), F32), pltpu.VMEM((hidden, width), F32)],
        compiler_params=pltpu.CompilerParams(vmem_limit_bytes=60 * 2**20),
        cost_estimate=pl.CostEstimate(
            flops=18 * count * width * hidden,
            bytes_accessed=8 * count * width + 18 * width * hidden,
            transcendentals=count * hidden,
        ),
    )(rows, grads, routed, gate_w, up_w, down_w, router)


def project_kernel(
    hidden, gain, weights, out_weights, q_gain, k_gain, cosine, sine,
    normed, all_weights, all_out, qkv, totals, query, keys, values,
    heads, stat, scale_q, scale_k, kept_sem, kept_out_sem, kept_kv_sem,
    stat_send, stat_recv, head_send, head_recv, pair_send, pair_recv, *sems,
):
    here = Here()
    row, col, core = here.row, here.col, here.core
    count = len(SPREAD_SEMS)
    rows, width = hidden.shape
    depth = weights.shape[0]
    part, side = depth // 2, out_weights.shape[0]

    def weight_block(of_row, unused_place, of_core):
        return all_weights.at[pl.ds(pl.multiple_of(of_row * depth + of_core * part, part), part)]

    def out_block(of_row, place, of_core):
        start = pl.multiple_of(place * side + of_core * (side // 2), side // 2)
        return all_out.at[pl.ds(start, side // 2), pl.ds(pl.multiple_of(of_row * side, side), side)]

    def normed_block(unused_row, place, unused_core):
        return normed.at[pl.ds(pl.multiple_of(place * rows, rows), rows)]

    own_weight = weights.at[pl.ds(pl.multiple_of(core * part, part), part)]
    own_out = out_weights.at[pl.ds(pl.multiple_of(core * (side // 2), side // 2), side // 2)]
    spread_w = Spread(here, own_weight, weight_block, part, sems[:count], line=False)
    spread_n = Spread(
        here, normed_block(row, col, core), normed_block, rows, sems[count : 2 * count], plane=False
    )
    spread_o = Spread(here, own_out, out_block, side // 2, sems[2 * count :])
    greet(here.plane_peers() + here.line_peers() + [here.other_core()])
    spread_w.step(0)
    keep = pltpu.make_async_copy(own_weight, weight_block(row, 0, core), kept_sem)
    keep.start()
    keep_out = pltpu.make_async_copy(own_out, out_block(row, col, core), kept_out_sem)
    keep_out.start()

    values_in = hidden[...].astype(F32)
    scale_one = lax.rsqrt(jnp.mean(values_in * values_in, axis=1, keepdims=True) + EPSILON)
    own_rows = pl.ds(pl.multiple_of(col * rows, rows), rows)
    normed[own_rows] = (values_in * scale_one * gain[...].astype(F32)).astype(BF16)
    spread_n.step(0)
    spread_o.step(0)
    spread_w.step(1)
    spread_n.step(1)
    spread_w.step(2)
    spread_n.step(2)
    spread_n.step(3)
    keep.wait()
    for which in range(4):
        spread_w.core_arrived(which, 0)

    columns = 256

    @pl.loop(0, qkv.shape[1] // columns)
    def _(index):
        at = pl.ds(pl.multiple_of(index * columns, columns), columns)
        qkv[:, at] = matmul(normed[...], all_weights[:, at])

    plane = qkv.shape[1] // (3 * HD)
    for kind in range(2):
        square = jnp.zeros((qkv.shape[0], HD), F32)
        for head in range(plane):
            start = (head * 3 + kind) * HD
            raw = qkv[:, start : start + HD]
            square = square + raw * raw
        stat[col, kind : kind + 1] = jnp.sum(square.T, axis=0, keepdims=True)

    def give_stat(step):
        peer = here.line_peers()[step]
        return remote(stat.at[col], stat.at[col], stat_send.at[step], stat_recv.at[col], peer)

    for step in range(3):
        give_stat(step).start()
    spread_o.step(1)
    for step in range(3):
        place = (col + step + 1) % 4
        arrived(stat.at[place], stat_recv.at[place])
    total = stat[0] + stat[1] + stat[2] + stat[3]
    totals[...] = total
    for kind, target in enumerate((scale_q, scale_k)):
        line = lax.rsqrt(total[kind : kind + 1] / width + EPSILON)
        target[...] = jnp.broadcast_to(line, (HD, line.shape[1])).T

    chunk = 64

    @pl.loop(0, qkv.shape[0] // chunk)
    def _(index):
        at = pl.ds(pl.multiple_of(index * chunk, chunk), chunk)
        for head in range(plane):
            for kind, (scales, gains) in enumerate(((scale_q, q_gain), (scale_k, k_gain))):
                raw = qkv[at, pl.ds((head * 3 + kind) * HD, HD)]
                unit = raw * scales[at] * gains[:, head * HD : (head + 1) * HD]
                turned = pltpu.roll(unit, HD // 2, 1)
                heads[head, kind, at] = (unit * cosine[at] + turned * sine[at]).astype(BF16)
            heads[head, 2, at] = qkv[at, pl.ds((head * 3 + 2) * HD, HD)].astype(BF16)

    targets = (query.at[row], keys.at[1, row], values.at[1, row])

    def give_head(step, kind):
        dest = here.rows[step + 1]
        sems = head_send.at[step, kind], head_recv.at[kind, row]
        return remote(heads.at[dest, kind], targets[kind], *sems, here.at_row(dest))

    for kind in (1, 2, 0):
        for step in range(3):
            give_head(step, kind).start()

    def give_pair(source, kind):
        array = (keys, values)[kind]
        sems = pair_send.at[kind, source], pair_recv.at[kind, source]
        return remote(array.at[1, source], array.at[0, source], *sems, here.other_core())

    def keep_pair(source, kind):
        array = (keys, values)[kind]
        return pltpu.make_async_copy(
            array.at[1, source], array.at[0, source], kept_kv_sem.at[kind, source]
        )

    def pair_from(source):
        @pl.when(core == 0)
        def _():
            for kind in range(2):
                give_pair(source, kind).start()
                keep_pair(source, kind).start()

    for kind, array in ((1, keys), (2, values)):
        array[1, row] = heads[row, kind]
    query[row] = heads[row, 0]
    pair_from(row)
    spread_o.step(2)
    for source in here.rows[1:]:
        arrived(keys.at[1, source], head_recv.at[1, source])
        arrived(values.at[1, source], head_recv.at[2, source])
        pair_from(source)
    spread_o.step(3)
    for source in here.rows[1:]:
        arrived(query.at[source], head_recv.at[0, source])
    spread_o.step(4)
    spread_o.step(5)

    @pl.when(core == 0)
    def _():
        for source in range(4):
            for kind in range(2):
                give_pair(source, kind).wait_send()
                keep_pair(source, kind).wait()

    @pl.when(core == 1)
    def _():
        for source in range(4):
            for kind in range(2):
                give_pair(source, kind).wait_recv()

    for step in range(3):
        give_stat(step).wait_send()
        for kind in range(3):
            give_head(step, kind).wait_send()
    keep_out.wait()
    spread_w.finish(arrivals=False)
    spread_n.finish()
    spread_o.finish()


def project(hidden, gain, weights, out_weights, q_gain, k_gain, cosine, sine, collective_id):
    rows, width = hidden.shape
    depth, columns = weights.shape
    row_tok = 4 * rows
    plane = columns // (3 * HD)
    vmem = pl.BlockSpec(memory_space=pltpu.VMEM)
    hbm = pl.BlockSpec(memory_space=pl.ANY)
    return pl.pallas_call(
        project_kernel,
        in_specs=[vmem, vmem, hbm, hbm, vmem, vmem, vmem, vmem],
        out_specs=[vmem, vmem, hbm, vmem, vmem, vmem, vmem, vmem],
        out_shape=[
            jax.ShapeDtypeStruct((row_tok, width), BF16),
            jax.ShapeDtypeStruct((4 * depth, columns), BF16),
            jax.ShapeDtypeStruct((width, width), BF16),
            jax.ShapeDtypeStruct((row_tok, columns), F32),
            jax.ShapeDtypeStruct((8, row_tok), F32),
            jax.ShapeDtypeStruct((4, row_tok, HD), BF16),
            jax.ShapeDtypeStruct((2, 4, row_tok, HD), BF16),
            jax.ShapeDtypeStruct((2, 4, row_tok, HD), BF16),
        ],
        scratch_shapes=[
            pltpu.VMEM((plane, 3, row_tok, HD), BF16),
            pltpu.VMEM((4, 8, row_tok), F32),
            pltpu.VMEM((row_tok, HD), F32),
            pltpu.VMEM((row_tok, HD), F32),
            pltpu.SemaphoreType.DMA,
            pltpu.SemaphoreType.DMA,
            pltpu.SemaphoreType.DMA((2, 4)),
            pltpu.SemaphoreType.DMA((3,)),
            pltpu.SemaphoreType.DMA((4,)),
            pltpu.SemaphoreType.DMA((3, 3)),
            pltpu.SemaphoreType.DMA((3, 4)),
            pltpu.SemaphoreType.DMA((2, 4)),
            pltpu.SemaphoreType.DMA((2, 4)),
        ]
        + SPREAD_SEMS * 3,
        compiler_params=pltpu.CompilerParams(
            collective_id=collective_id, has_side_effects=True, vmem_limit_bytes=56 * 2**20
        ),
    )(hidden, gain[None], weights, out_weights, q_gain, k_gain, cosine, sine)


def tail_kernel(
    d_qkv, weights, normed, mixed, d_attn,
    d_normed, grads,
    line, line_in, whole, give, other, plane, corner_one, corner_two, from_across, from_along,
    up_send, down_send, line_recv, other_send, other_recv,
    one_send, one_recv, two_send, two_recv, across_send, across_recv, along_send, along_recv,
    back_send, back_recv,
):
    here = Here()
    row, col, core = here.row, here.col, here.core
    rows = d_normed.shape[0]
    depth, columns = grads.shape
    part = depth // 2
    first, second = pl.ds(0, part // 2), pl.ds(part // 2, part // 2)
    order = here.near_first[::-1]
    qkv_columns = d_qkv.shape[1]
    tile = 512

    def line_rows(place):
        return pl.ds(pl.multiple_of(place * rows, rows), rows)

    def line_product(place):
        gradient = d_qkv[line_rows(place)]

        @pl.loop(0, weights.shape[0] // tile)
        def _(index):
            at = pl.ds(pl.multiple_of(index * tile, tile), tile)
            line[place, :, at] = contract_cols(gradient, weights[at]).astype(BF16)

    def give_up(place):
        sems = up_send.at[place], line_recv.at[place]
        return remote(line.at[place], line_in.at[place], *sems, here.at_col(col + 1))

    def give_down(place, slot):
        sems = down_send.at[place], line_recv.at[slot]
        return remote(line.at[place], line_in.at[slot], *sems, here.at_col(col - 1))

    def line_step(place):
        @pl.when((place > col) & (col > 0))
        def _():
            give_up(place).wait_recv()
            add_into(line.at[place], line_in.at[place])

        @pl.when((place < col) & (col < 3))
        def _():
            give_down(place, place).wait_recv()
            add_into(line.at[place], line_in.at[place])

        @pl.when(place > col)
        def _():
            give_up(place).start()

        @pl.when(place < col - 1)
        def _():
            give_down(place, place).start()

        @pl.when(place == col - 1)
        def _():
            give_down(place, 4).start()

    def row_product(which):
        of_row = here.rows[which]
        at = pl.ds(pl.multiple_of(of_row * depth, depth), depth)
        whole[:, pl.ds(0, qkv_columns)] = transposed_product(normed[:, at], d_qkv[...]).astype(BF16)
        whole[:, pl.ds(qkv_columns, columns - qkv_columns)] = transposed_product(
            mixed[...], d_attn[:, at]
        ).astype(BF16)
        plane[which] = whole[pl.ds(pl.multiple_of(core * part, part), part)]
        give[which] = whole[pl.ds(pl.multiple_of((1 - core) * part, part), part)]
        to_core(which).start()

    def to_core(which):
        sems = other_send.at[which], other_recv.at[which]
        return remote(give.at[which], other.at[which], *sems, here.other_core())

    def own_sum(which):
        to_core(which).wait_recv()
        add_into(plane.at[which], other.at[which])

    give_one = remote(
        plane.at[3, first], corner_one, one_send, one_recv, here.at_row(here.across)
    )
    give_two = remote(
        plane.at[3, second], corner_two, two_send, two_recv, here.at_row(here.along)
    )

    def give_across(index):
        at = (first, second)[index]
        sems = across_send.at[index], across_recv.at[index]
        return remote(plane.at[1, at], from_across.at[at], *sems, here.at_row(here.across))

    def give_along(index):
        at = (first, second)[index]
        sems = along_send.at[index], along_recv.at[index]
        return remote(plane.at[2, at], from_along.at[at], *sems, here.at_row(here.along))

    greet(here.plane_peers() + here.line_peers() + [here.other_core()])
    line_product(order[0])
    line_step(order[0])
    row_product(3)
    line_product(order[1])
    line_step(order[1])
    row_product(1)
    own_sum(3)
    give_one.start()
    give_two.start()
    row_product(2)
    own_sum(1)
    give_across(0).start()
    own_sum(2)
    give_along(1).start()
    line_product(order[2])
    line_step(order[2])
    row_product(0)
    line_product(order[3])
    give_two.wait_recv()
    add_into(plane.at[1, second], corner_two)
    give_across(1).start()
    give_one.wait_recv()
    add_into(plane.at[2, first], corner_one)
    give_along(0).start()
    own_sum(0)

    @pl.when(col > 0)
    def _():
        give_up(col).wait_recv()
        add_into(line.at[col], line_in.at[col])

    @pl.when(col < 3)
    def _():
        give_down(col, 4).wait_recv()
        add_into(line.at[col], line_in.at[4])

    d_normed[...] = line[col]
    for index in range(2):
        give_across(index).wait_recv()
        give_along(index).wait_recv()
    add_into(plane.at[0], from_across, from_along)
    own_half = pl.ds(pl.multiple_of(core * part, part), part)
    give_back = remote(
        plane.at[0], grads.at[own_half], back_send, back_recv, here.other_core()
    )
    give_back.start()
    grads[own_half] = plane[0]
    other_half = grads.at[pl.ds(pl.multiple_of((1 - core) * part, part), part)]
    arrived(other_half, back_recv)
    give_back.wait_send()
    give_one.wait_send()
    give_two.wait_send()
    for index in range(2):
        give_across(index).wait_send()
        give_along(index).wait_send()
    for which in range(4):
        to_core(which).wait_send()
    for place in order:

        @pl.when(place > col)
        def _():
            give_up(place).wait_send()

        @pl.when(place < col)
        def _():
            give_down(place, place).wait_send()


def tail(d_qkv, weights, normed, mixed, d_attn, collective_id):
    row_tok, qkv_columns = d_qkv.shape
    width = weights.shape[0]
    rows, depth = row_tok // 4, width // 4
    columns = qkv_columns + d_attn.shape[1] // 4
    part = depth // 2
    vmem = pl.BlockSpec(memory_space=pltpu.VMEM)
    one, four = pltpu.SemaphoreType.DMA, pltpu.SemaphoreType.DMA((4,))
    two, five = pltpu.SemaphoreType.DMA((2,)), pltpu.SemaphoreType.DMA((5,))
    return pl.pallas_call(
        tail_kernel,
        in_specs=[vmem] * 5,
        out_specs=[vmem] * 2,
        out_shape=[
            jax.ShapeDtypeStruct((rows, width), BF16),
            jax.ShapeDtypeStruct((depth, columns), BF16),
        ],
        scratch_shapes=[
            pltpu.VMEM((4, rows, width), BF16),
            pltpu.VMEM((5, rows, width), BF16),
            pltpu.VMEM((depth, columns), BF16),
            pltpu.VMEM((4, part, columns), BF16),
            pltpu.VMEM((4, part, columns), BF16),
            pltpu.VMEM((4, part, columns), BF16),
            pltpu.VMEM((part // 2, columns), BF16),
            pltpu.VMEM((part // 2, columns), BF16),
            pltpu.VMEM((part, columns), BF16),
            pltpu.VMEM((part, columns), BF16),
            four, four, five, four, four,
            one, one, one, one, two, two, two, two,
            one, one,
        ],
        compiler_params=pltpu.CompilerParams(
            collective_id=collective_id, has_side_effects=True, vmem_limit_bytes=56 * 2**20
        ),
    )(d_qkv, weights, normed, mixed, d_attn)


def sum_kernel(values, out, held, got, send, recv):
    here = Here()
    core, col = here.core, here.col
    half = values.shape[0] // 2
    peers = [
        here.at_row(here.across),
        here.at_row(here.along),
        here.at_col(col + 1 - 2 * (col % 2)),
        here.at_col((col + 2) % 4),
    ]
    greet(peers + [here.other_core()])
    own = pl.ds(pl.multiple_of(core * half, half), half)
    others = pl.ds(pl.multiple_of((1 - core) * half, half), half)
    copies = [remote(values.at[others], got.at[0], send.at[0], recv.at[0], here.other_core())]
    copies[0].start()
    copies[0].wait_recv()
    held[0] = values[own] + got[0]
    for step, peer in enumerate(peers):
        copy = remote(held.at[step], got.at[step + 1], send.at[step + 1], recv.at[step + 1], peer)
        copy.start()
        copy.wait_recv()
        held[step + 1] = held[step] + got[step + 1]
        copies.append(copy)
    out[own] = held[4]
    back = remote(held.at[4], out.at[own], send.at[5], recv.at[5], here.other_core())
    back.start()
    arrived(out.at[others], recv.at[5])
    for copy in copies + [back]:
        copy.wait_send()


def sum_everywhere(values, collective_id):
    half = (values.shape[0] // 2, values.shape[1])
    vmem = pl.BlockSpec(memory_space=pltpu.VMEM)
    return pl.pallas_call(
        sum_kernel,
        in_specs=[vmem],
        out_specs=vmem,
        out_shape=jax.ShapeDtypeStruct(values.shape, F32),
        scratch_shapes=[
            pltpu.VMEM((5,) + half, F32),
            pltpu.VMEM((5,) + half, F32),
            pltpu.SemaphoreType.DMA((6,)),
            pltpu.SemaphoreType.DMA((6,)),
        ],
        compiler_params=pltpu.CompilerParams(collective_id=collective_id, has_side_effects=True),
    )(values)


def expert_rows(rows, grads, gate, gate_w, up_w, down_w):
    pre_gate = matmul(rows, gate_w)
    pre_up = matmul(rows, up_w)
    back = contract_cols(grads, down_w)
    sigmoid_gate = jax.nn.sigmoid(pre_gate)
    silu_gate = pre_gate * sigmoid_gate
    hidden = (silu_gate * pre_up).astype(BF16)
    inner = jnp.sum(hidden.astype(F32) * back, axis=-1)
    weighted = (hidden.astype(F32) * gate).astype(BF16)
    d_hid = back * gate
    d_pregate = (d_hid * pre_up * (sigmoid_gate + silu_gate * (1.0 - sigmoid_gate))).astype(BF16)
    d_preup = (d_hid * silu_gate).astype(BF16)
    outputs = matmul(weighted, down_w).astype(BF16)
    d_rows = (contract_cols(d_pregate, gate_w) + contract_cols(d_preup, up_w)).astype(BF16)
    return (
        outputs,
        d_rows,
        inner,
        contract_rows(rows, d_pregate),
        contract_rows(rows, d_preup),
        contract_rows(weighted, grads),
    )


def experts(normed, grads, dense_gates, gate_w, up_w, down_w):
    rows_dev, width = normed.shape
    devices = math.prod(lax.axis_size(axis) for axis in ALL)
    expert_count = dense_gates.shape[1]
    expert = lax.axis_index(ALL) // 2
    parts = max(1, lax.axis_size("exp") // 2)
    step = rows_dev // parts

    def one_part(sums, piece):
        rows, grad_rows, gates = piece
        rows_all = lax.all_gather(rows, ALL, axis=0, tiled=True)
        grads_all = lax.all_gather(grad_rows, ALL, axis=0, tiled=True)
        gates_all = lax.all_gather(gates, ALL, axis=0, tiled=True)
        gate = lax.dynamic_slice_in_dim(gates_all, expert, 1, 1)
        got = expert_rows(rows_all, grads_all, gate, gate_w, up_w, down_w)
        outputs = lax.psum_scatter(got[0], ALL, scatter_dimension=0, tiled=True)
        d_rows = lax.psum_scatter(got[1], ALL, scatter_dimension=0, tiled=True)
        inner = lax.all_to_all(
            got[2].reshape(devices, step), ALL, split_axis=0, concat_axis=0, tiled=True
        )
        inner = inner.reshape(expert_count, 2, step).sum(axis=1).T
        sums = got[3:] if sums is None else tuple(a + b for a, b in zip(sums, got[3:]))
        return sums, (outputs, d_rows, inner)

    if parts == 1:
        sums, (outputs, d_rows, inner) = one_part(None, (normed, grads, dense_gates))
    else:
        start = tuple(jnp.zeros(w.shape, F32) for w in (gate_w, up_w, down_w))
        pieces = tuple(v.reshape(parts, step, -1) for v in (normed, grads, dense_gates))
        sums, got = lax.scan(one_part, start, pieces)
        outputs, d_rows, inner = (v.reshape(rows_dev, -1) for v in got)
    return outputs.astype(F32), d_rows.astype(F32), inner, sums


def experts_here(normed, gathered_grads, routes_all, router, gate_w, up_w, down_w):
    rows_dev, width = normed.shape
    devices = gathered_grads.shape[0]
    expert_count = router.shape[1]
    expert = lax.axis_index(ALL) // 2
    rows_all = gather_rows(normed, 2).reshape(-1, width)
    routed = jnp.any(routes_all == expert, axis=1, keepdims=True).astype(F32)
    got = expert_products(
        rows_all, gathered_grads.reshape(-1, width), routed, gate_w, up_w, down_w, router
    )
    d_rows = reduce_rows(got[1].reshape(devices, rows_dev, width), 3)
    outputs = reduce_rows(got[0].reshape(devices, rows_dev, width), 4)
    inner = lax.all_to_all(
        got[2].reshape(devices, rows_dev), ALL, split_axis=0, concat_axis=0, tiled=True
    )
    inner = inner.reshape(expert_count, 2, rows_dev).sum(axis=1).T
    return outputs.astype(F32), d_rows.astype(F32), inner, got[3:]


def shards(
    hidden_in,
    out_grad,
    attn_gain,
    w_qkv,
    q_gain,
    k_gain,
    w_out,
    moe_gain,
    router,
    w_gate,
    w_up,
    w_down,
    routes,
    doc_cuts,
):
    row_count, col_count = lax.axis_size("row"), lax.axis_size("col")
    tokens = hidden_in[0].astype(F32)
    rows_dev, width = tokens.shape
    heads = w_qkv.shape[1] // (3 * HD)
    plane = heads * HD
    scale = HD ** (-0.5)
    side = lax.axis_index("exp") % 2
    row_tok = rows_dev * col_count
    group_tok = row_tok * row_count
    cuts = lax.dynamic_index_in_dim(doc_cuts, lax.axis_index("exp") // 2, 0, keepdims=False)

    here = (row_count, col_count, lax.axis_size("exp")) == (4, 4, 2)
    if here:
        routes_all = lax.all_gather(routes[0], ALL, axis=0, tiled=True)

    gain_one = attn_gain.astype(F32)
    scale_one = rms_scale(tokens)
    head_start = lax.axis_index("col") * plane
    gain_q = lax.dynamic_slice_in_dim(q_gain, head_start, plane, 0).astype(F32)
    gain_k = lax.dynamic_slice_in_dim(k_gain, head_start, plane, 0).astype(F32)
    row_places = side * group_tok + lax.axis_index("row") * row_tok + jnp.arange(row_tok, dtype=jnp.int32)
    unused_doc, position = doc_positions(row_places, cuts)
    cosine, sine = rope_tables(position, HD)
    if here:
        signed = jnp.concatenate([-sine[:, : HD // 2], sine[:, HD // 2 :]], axis=1)
        normed_row, qkv_w, out_w, qkv, totals, query, keys, values = project(
            hidden_in[0], attn_gain, w_qkv, w_out, gain_q[None], gain_k[None], cosine, signed, 0
        )
        total_q, total_k = totals[0], totals[1]
        query = query.reshape(group_tok, HD)
        key_all, value_all = keys.reshape(-1, HD), values.reshape(-1, HD)
    else:
        normed_one = (tokens * scale_one * gain_one).astype(BF16)
        normed_row = lax.all_gather(normed_one, "col", axis=0, tiled=True)
        qkv_w = lax.all_gather(w_qkv, "row", axis=0, tiled=True)
        out_w = lax.all_gather(
            lax.all_gather(w_out, "row", axis=1, tiled=True), "col", axis=0, tiled=True
        )
        qkv = matmul(normed_row, qkv_w)
    qkv = qkv.reshape(row_tok, heads, 3, HD)
    query_raw, key_raw, value_raw = qkv[:, :, 0], qkv[:, :, 1], qkv[:, :, 2]
    if not here:
        total_q, total_k = lax.psum(
            (jnp.sum(query_raw * query_raw, axis=(1, 2)), jnp.sum(key_raw * key_raw, axis=(1, 2))),
            "col",
        )
    scale_q = lax.rsqrt(total_q / width + EPSILON)[:, None, None]
    scale_k = lax.rsqrt(total_k / width + EPSILON)[:, None, None]
    gain_q, gain_k = gain_q.reshape(heads, HD), gain_k.reshape(heads, HD)
    cosine, sine = cosine[:, None, :], sine[:, None, :]
    if not here:
        query = rotate(query_raw * scale_q * gain_q, cosine, sine).astype(BF16)
        key = rotate(key_raw * scale_k * gain_k, cosine, sine).astype(BF16)
        moved = rows_to_heads(jnp.concatenate([query, key, value_raw.astype(BF16)], axis=-1))
        query, own_pair = moved[:, :HD], moved[:, HD:]
        earlier_pair = from_behind(own_pair, "exp", 1)
        lower_pair = jnp.where(side == 0, own_pair, earlier_pair)
        upper_pair = jnp.where(side == 0, jnp.zeros_like(own_pair), own_pair)
        key_value = jnp.concatenate([lower_pair, upper_pair], axis=0)
        key_all, value_all = key_value[:, :HD], key_value[:, HD:]

    mixed_wide, total = attend(query, key_all, value_all, cuts, scale)
    mixed = mixed_wide.astype(BF16)
    mixed_row = heads_to_rows(mixed).reshape(row_tok, plane)
    middle = tokens + matmul(heads_to_tokens(mixed), out_w)

    gain_two = moe_gain.astype(F32)
    scale_two = rms_scale(middle)
    normed_two = (middle * scale_two * gain_two).astype(BF16)
    gates_all = jax.nn.softmax(matmul(normed_two, router), axis=-1)
    picks = routes[0]
    chosen = jnp.any(
        picks[:, :, None] == jnp.arange(router.shape[1], dtype=jnp.int32)[None, None, :], axis=1
    )
    grad_out = out_grad[0].astype(F32)
    expert_w = (w_gate[0], w_up[0], w_down[0])
    if here:
        mixture, d_normed_two, inner, weight_grads = experts_here(
            normed_two, gather_rows(out_grad[0], 1), routes_all, router, *expert_w
        )
    else:
        dense_gates = jnp.where(chosen, gates_all, 0.0)
        mixture, d_normed_two, inner, weight_grads = experts(
            normed_two, out_grad[0], dense_gates, *expert_w
        )
    final = middle + mixture
    dense = jnp.where(chosen, inner, 0.0)
    d_logits = (gates_all * (dense - jnp.sum(gates_all * dense, axis=-1, keepdims=True))).astype(BF16)
    grad_router = contract_rows(normed_two, d_logits)
    d_normed_two = d_normed_two + contract_cols(d_logits, router)
    grad_moe_gain = jnp.sum(d_normed_two * middle * scale_two, axis=0)
    weighted_two = d_normed_two * gain_two
    d_middle = (
        grad_out
        + scale_two * weighted_two
        - middle * scale_two**3 * jnp.mean(weighted_two * middle, axis=-1, keepdims=True)
    )

    d_attn = d_middle.astype(BF16)
    d_mixed = tokens_to_heads(contract_cols(d_attn, out_w).astype(BF16))
    d_attn_row = lax.all_gather(d_attn, "col", axis=0, tiled=True)
    d_query, acc_key, acc_value = attend_back(
        query, key_all, value_all, d_mixed, mixed_wide, total, cuts, scale
    )
    accumulated = jnp.concatenate([acc_key, acc_value], axis=1)
    lower_acc, upper_acc = accumulated[:group_tok], accumulated[group_tok:]
    kept_acc = jnp.where(side == 0, lower_acc, upper_acc)
    later_acc = from_behind(lower_acc.astype(BF16), "exp", -1).astype(F32)
    summed_pair = kept_acc + jnp.where(side == 0, later_acc, jnp.zeros_like(later_acc))
    d_heads = heads_to_rows(jnp.concatenate([d_query, summed_pair], axis=1).astype(BF16)).astype(F32)
    d_q_unit = rotate_back(d_heads[:, :, :HD], cosine, sine)
    d_k_unit = rotate_back(d_heads[:, :, HD : 2 * HD], cosine, sine)
    d_value = d_heads[:, :, 2 * HD :]
    weighted_q = d_q_unit * gain_q
    weighted_k = d_k_unit * gain_k
    sum_q, sum_k = lax.psum(
        (jnp.sum(weighted_q * query_raw, axis=(1, 2)), jnp.sum(weighted_k * key_raw, axis=(1, 2))),
        "col",
    )
    d_query_raw = scale_q * weighted_q - query_raw * scale_q**3 * (sum_q / width)[:, None, None]
    d_key_raw = scale_k * weighted_k - key_raw * scale_k**3 * (sum_k / width)[:, None, None]
    grad_q_part = jnp.sum(d_q_unit * query_raw * scale_q, axis=0).reshape(plane)
    grad_k_part = jnp.sum(d_k_unit * key_raw * scale_k, axis=0).reshape(plane)
    d_qkv = jnp.concatenate([d_query_raw, d_key_raw, d_value], axis=2).astype(BF16)
    d_qkv = d_qkv.reshape(row_tok, heads * 3 * HD)
    if here:
        d_normed_one, grads = tail(d_qkv, qkv_w, normed_row, mixed_row, d_attn_row, 5)
        d_normed_one, grads = d_normed_one.astype(F32), grads.astype(F32)
        grad_qkv, grad_w_out = grads[:, : d_qkv.shape[1]], grads[:, d_qkv.shape[1] :]
    else:
        d_normed_one = lax.psum_scatter(
            contract_cols(d_qkv, qkv_w).astype(BF16), "col", scatter_dimension=0, tiled=True
        ).astype(F32)
        grad_qkv = lax.psum_scatter(
            contract_rows(normed_row, d_qkv).astype(BF16), "row", scatter_dimension=0, tiled=True
        )
        grad_w_out = lax.psum_scatter(
            contract_rows(mixed_row, d_attn_row).astype(BF16), "row", scatter_dimension=1, tiled=True
        )
        grad_qkv = lax.psum(grad_qkv, "exp").astype(F32)
        grad_w_out = lax.psum(grad_w_out, "exp").astype(F32)
    grad_attn_gain = jnp.sum(d_normed_one * tokens * scale_one, axis=0)
    weighted_one = d_normed_one * gain_one
    grad_hidden = (
        d_middle
        + scale_one * weighted_one
        - tokens * scale_one**3 * jnp.mean(weighted_one * tokens, axis=-1, keepdims=True)
    )
    empty = jnp.zeros((width,), F32)
    grad_q_full = lax.dynamic_update_slice_in_dim(empty, grad_q_part, head_start, 0)
    grad_k_full = lax.dynamic_update_slice_in_dim(empty, grad_k_part, head_start, 0)
    parts = (grad_attn_gain, grad_q_full, grad_k_full, grad_moe_gain)
    if here:
        packed = jnp.concatenate(parts + (grad_router.T.reshape(-1),)).reshape(-1, 128)
        packed = sum_everywhere(packed, 6).reshape(-1)
        summed = [packed[i * width : (i + 1) * width] for i in range(4)]
        summed.append(packed[4 * width :].reshape(-1, width).T)
    else:
        summed = lax.psum(parts + (grad_router,), ALL)
    return (
        final.astype(BF16)[None],
        grad_hidden[None],
        summed[0],
        grad_qkv,
        summed[1],
        summed[2],
        grad_w_out,
        summed[3],
        summed[4],
        weight_grads[0][None],
        weight_grads[1][None],
        weight_grads[2][None],
    )


def solution(mesh):
    token_spec = P("exp", ("row", "col"), None)
    expert_spec = P(("row", "col", "exp"), None, None)
    in_specs = (
        token_spec,
        token_spec,
        P(),
        P("row", "col"),
        P(),
        P(),
        P("col", "row"),
        P(),
        P(),
        expert_spec,
        expert_spec,
        expert_spec,
        token_spec,
        P(),
    )
    out_specs = (
        token_spec,
        token_spec,
        P(),
        P("row", "col"),
        P(),
        P(),
        P("col", "row"),
        P(),
        P(),
        expert_spec,
        expert_spec,
        expert_spec,
    )
    return jax.shard_map(shards, mesh=mesh, in_specs=in_specs, out_specs=out_specs, check_vma=False)
```

```python
import functools
import math

import jax
import jax.numpy as jnp
from jax import lax
from jax.experimental import pallas as pl
from jax.experimental.pallas import tpu as pltpu
from jax.sharding import PartitionSpec as P

HD = 128
EPSILON = 1e-05
ROPE_BASE = 10000.0
MASKED = -1e30
BF16 = jnp.bfloat16
F32 = jnp.float32


def matmul(left, right):
    return jnp.dot(left, right, preferred_element_type=F32)


def contract_rows(left, right):
    return lax.dot_general(left, right, (((0,), (0,)), ((), ())), preferred_element_type=F32)


def contract_cols(left, right):
    return lax.dot_general(left, right, (((1,), (1,)), ((), ())), preferred_element_type=F32)


def rms_scale(values):
    return lax.rsqrt(jnp.mean(values * values, axis=-1, keepdims=True) + EPSILON)


def rope_tables(position, width):
    frequency = ROPE_BASE ** (-jnp.arange(0, width, 2, dtype=F32) / width)
    angle = position.astype(F32)[:, None] * frequency[None, :]
    return (
        jnp.concatenate([jnp.cos(angle)] * 2, axis=-1),
        jnp.concatenate([jnp.sin(angle)] * 2, axis=-1),
    )


def rotate(values, cosine, sine):
    half = values.shape[-1] // 2
    turned = jnp.concatenate([-values[..., half:], values[..., :half]], axis=-1)
    return values * cosine + turned * sine


def rotate_back(values, cosine, sine):
    half = values.shape[-1] // 2
    turned = values * sine
    return values * cosine + jnp.concatenate([turned[..., half:], -turned[..., :half]], axis=-1)


def doc_positions(places, cuts):
    first = (places >= cuts[0]).astype(jnp.int32)
    second = (places >= cuts[1]).astype(jnp.int32)
    start = first * cuts[0] + second * (cuts[1] - cuts[0])
    return (first + second, places - start)


def from_behind(value, axis, steps):
    count = lax.axis_size(axis)
    initial, last = (max(0, -steps), min(count, count - steps))
    return lax.ppermute(value, axis, [(source, source + steps) for source in range(initial, last)])


def rows_to_heads(values):
    count = lax.axis_size("row")
    rows, heads, width = values.shape
    moved = lax.all_to_all(values.transpose(1, 0, 2), "row", split_axis=0, concat_axis=0, tiled=True)
    return moved.reshape(count * rows, width)


def heads_to_rows(values):
    count = lax.axis_size("row")
    rows, width = values.shape
    moved = lax.all_to_all(
        values.reshape(count, rows // count, width), "row", split_axis=0, concat_axis=0, tiled=True
    )
    return moved.transpose(1, 0, 2)


def heads_to_tokens(values):
    row_count, col_count = lax.axis_size("row"), lax.axis_size("col")
    rows = values.shape[0] // (row_count * col_count)
    moved = lax.all_to_all(
        values.reshape(row_count * col_count, rows, HD),
        ("row", "col"),
        split_axis=0,
        concat_axis=0,
        tiled=True,
    )
    moved = moved.reshape(row_count, col_count, rows, HD).transpose(2, 1, 0, 3)
    return moved.reshape(rows, row_count * col_count * HD)


def tokens_to_heads(values):
    row_count, col_count = lax.axis_size("row"), lax.axis_size("col")
    rows = values.shape[0]
    parted = values.reshape(rows, col_count, row_count, HD).transpose(2, 1, 0, 3)
    moved = lax.all_to_all(
        parted.reshape(row_count * col_count, rows, HD),
        ("row", "col"),
        split_axis=0,
        concat_axis=0,
        tiled=True,
    )
    return moved.reshape(row_count * col_count * rows, HD)


MESH = pl.DeviceIdType.MESH
ALL = ("row", "col", "exp")


class Here:
    def __init__(self):
        self.row, self.col, self.core = (lax.axis_index(axis) for axis in ALL)
        self.across = self.row + 1 - 2 * (self.row % 2)
        self.along = (self.row + 2) % 4
        self.opposite = 3 - self.row
        self.rows = (self.row, self.across, self.along, self.opposite)
        half = self.col // 2
        self.near_first = [
            self.col,
            1 + self.col % 2,
            2 - self.col - self.col % 2 + 3 * half,
            3 - 3 * half,
        ]

    def at_row(self, row):
        return (row, self.col, self.core)

    def at_col(self, col):
        return (self.row, col, self.core)

    def other_core(self):
        return (self.row, self.col, 1 - self.core)

    def line_peers(self):
        return [self.at_col((self.col + step) % 4) for step in (1, 2, 3)]

    def plane_peers(self):
        return [self.at_row(row) for row in self.rows[1:]]


def greet(peers):
    barrier = pltpu.get_barrier_semaphore()
    for peer in peers:
        pl.semaphore_signal(barrier, inc=1, device_id=peer, device_id_type=MESH)
    pl.semaphore_wait(barrier, len(peers))


def greet_near(here):
    barrier = pltpu.get_barrier_semaphore()
    col = here.col

    def signal(peer):
        pl.semaphore_signal(barrier, inc=1, device_id=peer, device_id_type=MESH)

    for peer in (here.other_core(), here.at_row(here.across), here.at_row(here.along)):
        signal(peer)

    @pl.when(col > 0)
    def _():
        signal(here.at_col(col - 1))

    @pl.when(col < 3)
    def _():
        signal(here.at_col(col + 1))

    pl.semaphore_wait(barrier, 3 + (col + 3) // 4 + (6 - col) // 4)


def remote(source, target, send, recv, device):
    return pltpu.make_async_remote_copy(
        src_ref=source,
        dst_ref=target,
        send_sem=send,
        recv_sem=recv,
        device_id=device,
        device_id_type=MESH,
    )


def arrived(target, recv):
    pltpu.make_async_copy(target, target, recv).wait()


def add_into(target, *terms):
    step = 16

    @pl.loop(0, target.shape[0] // step)
    def _(index):
        part = pl.ds(pl.multiple_of(index * step, step), step)
        value = target[part].astype(F32)
        for term in terms:
            value = value + term[part].astype(F32)
        target[part] = value.astype(target.dtype)


SPREAD_SEMS = [pltpu.SemaphoreType.DMA((4,))] * 11 + [pltpu.SemaphoreType.DMA((4, 4))] * 2


class Spread:
    def __init__(self, here, own, block, rows, sems, line=True, plane=True, core=True):
        self.here, self.own, self.block = here, own, block
        self.line, self.plane, self.core = line, plane, core
        (
            self.up_send, self.down_send, self.line_recv,
            self.across_send, self.across_recv, self.along_send, self.along_recv,
            self.one_send, self.one_recv, self.two_send, self.two_recv,
            self.core_send, self.core_recv,
        ) = sems
        self.first, self.second = pl.ds(0, rows // 2), pl.ds(rows // 2, rows // 2)
        self.order = here.near_first if line else [0]
        self.steps = len(self.order)

    def held(self, step):
        here = self.here
        return self.own if step == 0 else self.block(here.row, self.order[step], here.core)

    def up(self, step):
        here, place = self.here, self.order[step]
        target = self.block(here.row, place, here.core)
        recv = self.line_recv.at[place]
        return remote(self.held(step), target, self.up_send.at[place], recv, here.at_col(here.col + 1))

    def down(self, step):
        here, place = self.here, self.order[step]
        target = self.block(here.row, place, here.core)
        recv = self.line_recv.at[place]
        return remote(self.held(step), target, self.down_send.at[place], recv, here.at_col(here.col - 1))

    def to_across(self, step):
        here, place = self.here, self.order[step]
        target = self.block(here.row, place, here.core)
        sems = self.across_send.at[place], self.across_recv.at[place]
        return remote(self.held(step), target, *sems, here.at_row(here.across))

    def to_along(self, step):
        here, place = self.here, self.order[step]
        target = self.block(here.row, place, here.core)
        sems = self.along_send.at[place], self.along_recv.at[place]
        return remote(self.held(step), target, *sems, here.at_row(here.along))

    def corner_one(self, step):
        here, place = self.here, self.order[step]
        part = self.block(here.across, place, here.core).at[self.first]
        sems = self.one_send.at[place], self.one_recv.at[place]
        return remote(part, part, *sems, here.at_row(here.along))

    def corner_two(self, step):
        here, place = self.here, self.order[step]
        part = self.block(here.along, place, here.core).at[self.second]
        sems = self.two_send.at[place], self.two_recv.at[place]
        return remote(part, part, *sems, here.at_row(here.across))

    def to_core(self, which, step):
        here, place = self.here, self.order[step]
        target = self.block(here.rows[which], place, here.core)
        source = self.held(step) if which == 0 else target
        sems = self.core_send.at[which, place], self.core_recv.at[which, place]
        return remote(source, target, *sems, here.other_core())

    def line_step(self, step):
        here, place = self.here, self.order[step]
        if step > 0:
            arrived(self.held(step), self.line_recv.at[place])
        if self.line:

            @pl.when((place <= here.col) & (here.col < 3))
            def _():
                self.up(step).start()

            @pl.when((place >= here.col) & (here.col > 0))
            def _():
                self.down(step).start()

        if self.plane:
            self.to_across(step).start()
            self.to_along(step).start()
            if self.core:
                self.to_core(0, step).start()

    def plane_step(self, step):
        here, place = self.here, self.order[step]
        arrived(self.block(here.across, place, here.core), self.across_recv.at[place])
        self.corner_one(step).start()
        if self.core:
            self.to_core(1, step).start()
        arrived(self.block(here.along, place, here.core), self.along_recv.at[place])
        self.corner_two(step).start()
        if self.core:
            self.to_core(2, step).start()

    def corner_step(self, step):
        here, place = self.here, self.order[step]
        target = self.block(here.opposite, place, here.core)
        arrived(target.at[self.first], self.one_recv.at[place])
        arrived(target.at[self.second], self.two_recv.at[place])
        if self.core:
            self.to_core(3, step).start()

    def step(self, index):
        if index < self.steps:
            self.line_step(index)
        if self.plane and 0 <= index - 1 < self.steps:
            self.plane_step(index - 1)
        if self.plane and 0 <= index - 2 < self.steps:
            self.corner_step(index - 2)

    def core_arrived(self, which, step):
        here, place = self.here, self.order[step]
        target = self.block(here.rows[which], place, 1 - here.core)
        arrived(target, self.core_recv.at[which, place])

    def finish(self, arrivals=True):
        here = self.here
        for step in range(self.steps):
            place = self.order[step]
            if self.line:

                @pl.when((place <= here.col) & (here.col < 3))
                def _():
                    self.up(step).wait_send()

                @pl.when((place >= here.col) & (here.col > 0))
                def _():
                    self.down(step).wait_send()

            if self.plane:
                self.to_across(step).wait_send()
                self.to_along(step).wait_send()
                self.corner_one(step).wait_send()
                self.corner_two(step).wait_send()
                for which in range(4 if self.core else 0):
                    self.to_core(which, step).wait_send()
                    if arrivals:
                        self.core_arrived(which, step)


COLLECT_SEMS = (
    [pltpu.SemaphoreType.DMA((4,))] * 4
    + [pltpu.SemaphoreType.DMA((2, 4))] * 4
    + [pltpu.SemaphoreType.DMA((4,))] * 2
    + [pltpu.SemaphoreType.DMA((5,))]
)


def collect_buffers(rows, width):
    return [
        pltpu.VMEM((4, 4, rows, width), BF16),
        pltpu.VMEM((4, rows // 2, width), BF16),
        pltpu.VMEM((4, rows // 2, width), BF16),
        pltpu.VMEM((4, rows, width), BF16),
        pltpu.VMEM((4, rows, width), BF16),
        pltpu.VMEM((5, rows, width), BF16),
    ]


class Collect:
    def __init__(self, here, buffers, sems):
        self.here = here
        self.mine, self.one, self.two, self.from_across, self.from_along, self.line = buffers
        (
            self.one_send, self.one_recv, self.two_send, self.two_recv,
            self.across_send, self.across_recv, self.along_send, self.along_recv,
            self.up_send, self.down_send, self.line_recv,
        ) = sems
        half = self.mine.shape[2] // 2
        self.halves = (pl.ds(0, half), pl.ds(half, half))

    def give_one(self, place):
        here = self.here
        return remote(
            self.mine.at[3, place, self.halves[0]], self.one.at[place],
            self.one_send.at[place], self.one_recv.at[place], here.at_row(here.across),
        )

    def give_two(self, place):
        here = self.here
        return remote(
            self.mine.at[3, place, self.halves[1]], self.two.at[place],
            self.two_send.at[place], self.two_recv.at[place], here.at_row(here.along),
        )

    def give_across(self, place, half):
        here, part = self.here, self.halves[half]
        return remote(
            self.mine.at[1, place, part], self.from_across.at[place, part],
            self.across_send.at[half, place], self.across_recv.at[half, place], here.at_row(here.across),
        )

    def give_along(self, place, half):
        here, part = self.here, self.halves[half]
        return remote(
            self.mine.at[2, place, part], self.from_along.at[place, part],
            self.along_send.at[half, place], self.along_recv.at[half, place], here.at_row(here.along),
        )

    def give_up(self, place):
        here = self.here
        sems = self.up_send.at[place], self.line_recv.at[place]
        return remote(self.mine.at[0, place], self.line.at[place], *sems, here.at_col(here.col + 1))

    def give_down(self, place, slot):
        here = self.here
        sems = self.down_send.at[place], self.line_recv.at[slot]
        return remote(self.mine.at[0, place], self.line.at[slot], *sems, here.at_col(here.col - 1))

    def start_far(self, place):
        self.give_one(place).start()
        self.give_two(place).start()
        self.give_along(place, 1).start()

    def start_near(self, place):
        self.give_across(place, 0).start()

    def corner_step(self, place):
        self.give_two(place).wait_recv()
        add_into(self.mine.at[1, place, self.halves[1]], self.two.at[place])
        self.give_across(place, 1).start()
        self.give_one(place).wait_recv()
        add_into(self.mine.at[2, place, self.halves[0]], self.one.at[place])
        self.give_along(place, 0).start()

    def plane_step(self, place):
        for half in range(2):
            self.give_across(place, half).wait_recv()
            self.give_along(place, half).wait_recv()
        add_into(self.mine.at[0, place], self.from_across.at[place], self.from_along.at[place])

    def line_step(self, place):
        col = self.here.col

        @pl.when((place > col) & (col > 0))
        def _():
            self.give_up(place).wait_recv()
            add_into(self.mine.at[0, place], self.line.at[place])

        @pl.when((place < col) & (col < 3))
        def _():
            self.give_down(place, place).wait_recv()
            add_into(self.mine.at[0, place], self.line.at[place])

        @pl.when(place > col)
        def _():
            self.give_up(place).start()

        @pl.when(place < col - 1)
        def _():
            self.give_down(place, place).start()

        @pl.when(place == col - 1)
        def _():
            self.give_down(place, 4).start()

    def own_step(self):
        col = self.here.col

        @pl.when(col > 0)
        def _():
            self.give_up(col).wait_recv()
            add_into(self.mine.at[0, col], self.line.at[col])

        @pl.when(col < 3)
        def _():
            self.give_down(col, 4).wait_recv()
            add_into(self.mine.at[0, col], self.line.at[4])

    def finish(self):
        col = self.here.col
        for place in range(4):
            self.give_one(place).wait_send()
            self.give_two(place).wait_send()
            for half in range(2):
                self.give_across(place, half).wait_send()
                self.give_along(place, half).wait_send()

            @pl.when(place > col)
            def _():
                self.give_up(place).wait_send()

            @pl.when(place < col)
            def _():
                self.give_down(place, place).wait_send()


def reduce_kernel(values, total, *rest):
    here = Here()
    collect = Collect(here, rest[:6], rest[6 : 6 + len(COLLECT_SEMS)])
    load_sem = rest[-1]
    order = here.near_first[::-1]

    def load(which, place):
        return pltpu.make_async_copy(
            values.at[which, place], collect.mine.at[which, place], load_sem.at[which, place]
        )

    for place in order:
        for which in (3, 2, 1, 0):
            load(which, place).start()
    greet_near(here)
    for step in range(6):
        if step < 4:
            place = order[step]
            load(3, place).wait()
            load(2, place).wait()
            collect.start_far(place)
            load(1, place).wait()
            collect.start_near(place)
        if 0 <= step - 1 < 4:
            collect.corner_step(order[step - 1])
        if 0 <= step - 2 < 4:
            place = order[step - 2]
            load(0, place).wait()
            collect.plane_step(place)
            collect.line_step(place)
    collect.own_step()
    total[...] = collect.mine[0, here.col]
    collect.finish()


def reduce_rows(values, collective_id):
    rows, width = values.shape[2:]
    return pl.pallas_call(
        reduce_kernel,
        out_shape=jax.ShapeDtypeStruct((rows, width), BF16),
        in_specs=[pl.BlockSpec(memory_space=pl.ANY)],
        out_specs=pl.BlockSpec(memory_space=pltpu.VMEM),
        scratch_shapes=collect_buffers(rows, width)
        + COLLECT_SEMS
        + [pltpu.SemaphoreType.DMA((4, 4))],
        compiler_params=pltpu.CompilerParams(
            collective_id=collective_id, has_side_effects=True, vmem_limit_bytes=40 * 2**20
        ),
    )(values)


def doc_start(places, cuts):
    return jnp.where(places >= cuts[1], cuts[1], jnp.where(places >= cuts[0], cuts[0], 0))


def key_blocks(cuts, first_query, rows, scores_of, block_fn):
    def scan(index, carry):
        start = pl.multiple_of(index * rows, rows)
        free = (start >= doc_start(first_query + rows - 1, cuts)) & (start + rows <= first_query + 1)

        @pl.when(free)
        def _():
            block_fn(start, scores_of(start))

        @pl.when(jnp.logical_not(free))
        def _():
            key_place = start + lax.broadcasted_iota(jnp.int32, (rows, rows), 0)
            place = first_query + lax.broadcasted_iota(jnp.int32, (1, rows), 1)
            allowed = (key_place <= place) & (key_place >= doc_start(place, cuts))
            block_fn(start, jnp.where(allowed, scores_of(start), MASKED))

        return carry

    lax.fori_loop(doc_start(first_query, cuts) // rows, first_query // rows + 1, scan, 0)


def attend_kernel(scale, group_tok, cuts, query, keys, values_t, mixed, total, top, summed, acc):
    rows = query.shape[0]
    side = lax.axis_index("exp") % 2
    first_query = side * group_tok + pl.program_id(0) * rows
    top[...] = jnp.full_like(top, MASKED)
    summed[...] = jnp.zeros_like(summed)
    acc[...] = jnp.zeros_like(acc)
    cut = (cuts[0, 0], cuts[0, 1])

    def scores_of(start):
        return contract_cols(keys[pl.ds(start, rows)], query[...]) * scale

    def block_fn(start, scores):
        old = top[...]
        new = jnp.maximum(old, jnp.max(scores, axis=0, keepdims=True))
        weights = jnp.exp(scores - new)
        decay = jnp.exp(old - new)
        top[...] = new
        summed[...] = summed[...] * decay + jnp.sum(weights, axis=0, keepdims=True)
        acc[...] = acc[...] * decay + matmul(values_t[:, pl.ds(start, rows)], weights.astype(BF16))

    key_blocks(cut, first_query, rows, scores_of, block_fn)
    mixed[...] = (acc[...] / summed[...]).T
    total[...] = top[...] + jnp.log(summed[...])


def attend(query, keys, values, cuts, scale, rows=512):
    group_tok, head_size = query.shape
    whole = lambda shape: pl.BlockSpec(shape, lambda i: (0, 0))
    return pl.pallas_call(
        functools.partial(attend_kernel, scale, group_tok),
        grid=(group_tok // rows,),
        in_specs=[
            pl.BlockSpec(memory_space=pltpu.SMEM),
            pl.BlockSpec((rows, head_size), lambda i: (i, 0)),
            whole(keys.shape),
            whole(values.shape[::-1]),
        ],
        out_specs=[
            pl.BlockSpec((rows, head_size), lambda i: (i, 0)),
            pl.BlockSpec((1, rows), lambda i: (0, i)),
        ],
        out_shape=[
            jax.ShapeDtypeStruct((group_tok, head_size), F32),
            jax.ShapeDtypeStruct((1, group_tok), F32),
        ],
        scratch_shapes=[
            pltpu.VMEM((1, rows), F32),
            pltpu.VMEM((1, rows), F32),
            pltpu.VMEM((head_size, rows), F32),
        ],
        compiler_params=pltpu.CompilerParams(vmem_limit_bytes=40 * 2**20),
        cost_estimate=pl.CostEstimate(
            flops=4 * 7 * 2**20 * head_size, bytes_accessed=2**23, transcendentals=7 * 2**20
        ),
    )(cuts[None], query, keys, values.T)


def attend_back_kernel(
    scale, group_tok, cuts, query, keys, keys_t, values, d_mixed, total, delta,
    d_query, d_keys, d_values, acc,
):
    rows = query.shape[0]
    side = lax.axis_index("exp") % 2
    first_query = side * group_tok + pl.program_id(0) * rows
    cut = (cuts[0, 0], cuts[0, 1])

    @pl.when(pl.program_id(0) == 0)
    def _():
        d_keys[...] = jnp.zeros_like(d_keys)
        d_values[...] = jnp.zeros_like(d_values)

    acc[...] = jnp.zeros_like(acc)

    def scores_of(start):
        return contract_cols(keys[pl.ds(start, rows)], query[...]) * scale

    def block_fn(start, scores):
        part = pl.ds(start, rows)
        weights = jnp.exp(scores - total[...])
        d_weights = contract_cols(values[part], d_mixed[...])
        d_scores = (weights * (d_weights - delta[...])).astype(BF16)
        d_values[part] += matmul(weights.astype(BF16), d_mixed[...])
        d_keys[part] += matmul(d_scores, query[...]) * scale
        acc[...] += matmul(keys_t[:, part], d_scores)

    key_blocks(cut, first_query, rows, scores_of, block_fn)
    d_query[...] = (acc[...] * scale).T


def attend_back(query, keys, values, d_mixed, mixed, total, cuts, scale, rows=512):
    group_tok, head_size = query.shape
    delta = jnp.sum(d_mixed.astype(F32) * mixed, axis=1)[None]
    whole = lambda shape: pl.BlockSpec(shape, lambda i: (0, 0))
    block = pl.BlockSpec((rows, head_size), lambda i: (i, 0))
    line = pl.BlockSpec((1, rows), lambda i: (0, i))
    return pl.pallas_call(
        functools.partial(attend_back_kernel, scale, group_tok),
        grid=(group_tok // rows,),
        in_specs=[
            pl.BlockSpec(memory_space=pltpu.SMEM),
            block,
            whole(keys.shape),
            whole(keys.shape[::-1]),
            whole(keys.shape),
            block,
            line,
            line,
        ],
        out_specs=[block, whole(keys.shape), whole(keys.shape)],
        out_shape=[
            jax.ShapeDtypeStruct((group_tok, head_size), F32),
            jax.ShapeDtypeStruct(keys.shape, F32),
            jax.ShapeDtypeStruct(keys.shape, F32),
        ],
        scratch_shapes=[pltpu.VMEM((head_size, rows), F32)],
        compiler_params=pltpu.CompilerParams(vmem_limit_bytes=48 * 2**20),
        cost_estimate=pl.CostEstimate(
            flops=10 * 7 * 2**20 * head_size, bytes_accessed=2**23, transcendentals=7 * 2**20
        ),
    )(cuts[None], query, keys, keys.T, values, d_mixed, total, delta)


def transposed_product(left, right):
    return jnp.dot(left.T, right, preferred_element_type=F32)


def column_of(line):
    return jnp.broadcast_to(line, (128, 128)).T[:, :1]


def line_of(column):
    return jnp.broadcast_to(column, (128, 128)).T[:1]


def expert_kernel(
    expert_count, normed, grads, mask, gate_half, up_half, down_half, router,
    rows_all, grads_all, out_parts, total, inner, grad_gate, grad_up, grad_down,
    their_gate, their_up, their_down,
    gate_w, up_w, down_w, masks, x_buf, d_buf, d_gates, d_ups, weighteds, out_buf,
    tile_buf, give_buf, give_down, their_buf, their_down_buf, sum_buf, sum_down, *rest,
):
    here = Here()
    row, col, core = here.row, here.col, here.core
    rows, width = normed.shape
    half = gate_half.shape[1]
    expert = row * 4 + col
    count = len(SPREAD_SEMS)
    collect = Collect(here, rest[:6], rest[6 : 6 + len(COLLECT_SEMS)])
    rest = rest[6 + len(COLLECT_SEMS) :]
    (
        kept_sem, weight_sem, weight_send, weight_recv, load_sem, store_sem,
        tile_sem, give_send, give_recv, their_sem, sum_sem,
    ) = rest[:11]
    sems = rest[11:]

    def x_block(of_row, place, unused_core):
        return rows_all.at[of_row, place]

    def d_block(of_row, place, unused_core):
        return grads_all.at[of_row, place]

    def m_block(of_row, place, unused_core):
        return masks.at[of_row, place]

    spread_x = Spread(here, normed, x_block, rows, sems[:count], core=False)
    spread_d = Spread(here, grads, d_block, rows, sems[count : 2 * count], core=False)
    spread_m = Spread(here, mask, m_block, mask.shape[0], sems[2 * count :], core=False)
    order = here.near_first

    own_half = pl.ds(pl.multiple_of(core * half, half), half)
    other_half = pl.ds(pl.multiple_of((1 - core) * half, half), half)
    halves = (
        (gate_half, gate_w.at[:, own_half], gate_w.at[:, other_half]),
        (up_half, up_w.at[:, own_half], up_w.at[:, other_half]),
        (down_half, down_w.at[own_half], down_w.at[other_half]),
    )
    keeps = [
        pltpu.make_async_copy(source, target, weight_sem.at[index])
        for index, (source, target, unused) in enumerate(halves)
    ] + [
        pltpu.make_async_copy(source, target, kept_sem.at[index])
        for index, (source, target) in enumerate(
            ((normed, x_block(row, col, 0)), (grads, d_block(row, col, 0)), (mask, m_block(row, col, 0)))
        )
    ]
    for keep in keeps:
        keep.start()
    greet_near(here)
    swaps = [
        remote(source, target, weight_send.at[index], weight_recv.at[index], here.other_core())
        for index, (source, target, unused) in enumerate(halves)
    ]
    spread_x.step(0)
    spread_m.step(0)
    for swap in swaps:
        swap.start()
    spread_d.step(0)

    pairs = ((3, 2), (1, 0))

    def loads(step, pair):
        place, slot = order[step], pair
        made = []
        for index, which in enumerate(pairs[pair]):
            part = pl.ds(index * rows, rows)
            for array, (source, target) in enumerate(((x_block, x_buf), (d_block, d_buf))):
                made.append(
                    pltpu.make_async_copy(
                        source(here.rows[which], place, 0),
                        target.at[slot, part],
                        load_sem.at[slot, index, array],
                    )
                )
        return made

    def stores(step, pair):
        return [
            pltpu.make_async_copy(
                out_buf.at[pair, pl.ds(index * rows, rows)],
                out_parts.at[which, order[step]],
                store_sem.at[pair, index],
            )
            for index, which in enumerate(pairs[pair])
        ]

    def act_rows(which, place):
        start = (here.rows[which] * 4 + place) * rows
        return pl.ds(pl.multiple_of(start, rows), rows)

    tile = 256

    def first_products(step, pair):
        place = order[step]
        x, dy = x_buf[pair], d_buf[pair]
        lane = lax.broadcasted_iota(jnp.int32, (x.shape[0], router.shape[1]), 1)
        logits = jnp.where(lane < expert_count, matmul(x, router[...]), MASKED)
        raised = jnp.exp(logits - jnp.max(logits, axis=1, keepdims=True))
        picked = jnp.sum(jnp.where(lane == expert, raised, 0.0), axis=1, keepdims=True)
        routed = jnp.concatenate(
            [column_of(masks[here.rows[which], place, pl.ds(expert, 1)]) for which in pairs[pair]]
        )
        gate = picked / jnp.sum(raised, axis=1, keepdims=True) * routed
        ats = [act_rows(which, place) for which in pairs[pair]]

        def tile_step(index, inner_sum):
            at = pl.ds(pl.multiple_of(index * tile, tile), tile)
            pre_gate = matmul(x_buf[pair], gate_w[:, at])
            pre_up = matmul(x_buf[pair], up_w[:, at])
            back = contract_cols(d_buf[pair], down_w[at])
            sigmoid_gate = 1.0 / (1.0 + jnp.exp(-pre_gate))
            silu_gate = pre_gate * sigmoid_gate
            hidden = (silu_gate * pre_up).astype(BF16).astype(F32)
            d_hid = back * gate
            d_gate = (d_hid * pre_up * (sigmoid_gate + silu_gate * (1.0 - sigmoid_gate))).astype(BF16)
            d_up = (d_hid * silu_gate).astype(BF16)
            weighted = (hidden * gate).astype(BF16)
            for position, act in enumerate(ats):
                part = slice(position * rows, (position + 1) * rows)
                d_gates[act, at] = d_gate[part]
                d_ups[act, at] = d_up[part]
                weighteds[act, at] = weighted[part]
            return inner_sum + jnp.sum(hidden * back, axis=1, keepdims=True)

        start = jnp.zeros((x.shape[0], 1), F32)
        inner_sum = lax.fori_loop(0, gate_w.shape[1] // tile, tile_step, start)
        for position, which in enumerate(pairs[pair]):
            part = slice(position * rows, (position + 1) * rows)
            inner[here.rows[which], place, 0:1] = line_of(inner_sum[part])

    def second_products(step, pair):
        place = order[step]
        ats = [act_rows(which, place) for which in pairs[pair]]

        @pl.loop(0, width // tile)
        def _(index):
            at = pl.ds(pl.multiple_of(index * tile, tile), tile)

            def both(act):
                return jnp.concatenate([act[part] for part in ats])

            out_buf[pair, :, at] = matmul(both(weighteds), down_w[:, at]).astype(BF16)
            d_x = contract_cols(both(d_gates), gate_w[at]) + contract_cols(both(d_ups), up_w[at])
            d_x = d_x.astype(BF16)
            for position, which in enumerate(pairs[pair]):
                part = slice(position * rows, (position + 1) * rows)
                collect.mine[which, place, :, at] = d_x[part]

    for index in (1, 2):
        spread_x.step(index)
        spread_m.step(index)
        spread_d.step(index)
    for keep in keeps:
        keep.wait()
    for copy in loads(0, 0):
        copy.start()
    for swap in swaps:
        swap.wait_recv()
    for step in range(4):
        for copy in loads(step, 0):
            copy.wait()
        for copy in loads(step, 1):
            copy.start()
        first_products(step, 0)
        if step < 3:
            spread_x.step(step + 3)
        if step > 0:
            for copy in stores(step - 1, 0):
                copy.wait()
        second_products(step, 0)
        for copy in stores(step, 0):
            copy.start()
        collect.start_far(order[step])
        if step > 0:
            collect.corner_step(order[step - 1])
        for copy in loads(step, 1):
            copy.wait()
        first_products(step, 1)
        if step < 3:
            spread_m.step(step + 3)
            spread_d.step(step + 3)
            for copy in loads(step + 1, 0):
                copy.start()
        if step > 0:
            for copy in stores(step - 1, 1):
                copy.wait()
        second_products(step, 1)
        for copy in stores(step, 1):
            copy.start()
        collect.start_near(order[step])
        if step > 0:
            collect.plane_step(order[step - 1])

    acts = (d_gates, d_ups, weighteds)
    theirs = (their_gate, their_up, their_down)
    results = (grad_gate, grad_up, grad_down)
    tiles = width // tile

    def tile_at(index):
        return pl.ds(pl.multiple_of(index * tile, tile), tile)

    def tile_of(arrays, kind, index):
        return arrays[kind].at[tile_at(index)] if kind < 2 else arrays[kind].at[:, tile_at(index)]

    def slot_of(pair, kind, slot):
        return pair[0].at[slot, kind] if kind < 2 else pair[1].at[slot]

    def tile_load(source, index, slot):
        return pltpu.make_async_copy(
            source.at[:, :, :, tile_at(index)], tile_buf.at[slot], tile_sem.at[slot]
        )

    def give(kind, index, slot):
        sems = give_send.at[slot, kind], give_recv.at[kind, index]
        source = slot_of((give_buf, give_down), kind, slot)
        return remote(source, tile_of(theirs, kind, index), *sems, here.other_core())

    def their_load(kind, index, slot):
        return pltpu.make_async_copy(
            tile_of(theirs, kind, index),
            slot_of((their_buf, their_down_buf), kind, slot),
            their_sem.at[slot, kind],
        )

    def sum_store(kind, index, slot):
        return pltpu.make_async_copy(
            slot_of((sum_buf, sum_down), kind, slot),
            tile_of(results, kind, index),
            sum_sem.at[slot, kind],
        )

    def product_of(kind, turned, part):
        product = matmul(turned, acts[kind][:, part])
        return product if kind < 2 else product.T

    def give_gradients(source, kinds):
        tile_load(source, 0, 0).start()

        @pl.loop(0, tiles)
        def _(index):
            slot = index % 2

            @pl.when(index + 1 < tiles)
            def _():
                tile_load(source, index + 1, 1 - slot).start()

            tile_load(source, index, slot).wait()
            turned = tile_buf[slot].reshape(-1, tile).T
            for kind in kinds:
                product = product_of(kind, turned, other_half)

                @pl.when(index >= 2)
                def _():
                    give(kind, index - 2, slot).wait_send()

                slot_of((give_buf, give_down), kind, slot)[...] = product.astype(BF16)
                give(kind, index, slot).start()

    def keep_gradients(source, kinds):
        tile_load(source, 0, 0).start()
        for kind in kinds:
            give(kind, 0, 0).wait_recv()
            their_load(kind, 0, 0).start()

        @pl.loop(0, tiles)
        def _(index):
            slot = index % 2

            @pl.when(index + 1 < tiles)
            def _():
                tile_load(source, index + 1, 1 - slot).start()
                for kind in kinds:
                    give(kind, index + 1, 1 - slot).wait_recv()
                    their_load(kind, index + 1, 1 - slot).start()

            tile_load(source, index, slot).wait()
            turned = tile_buf[slot].reshape(-1, tile).T
            for kind in kinds:
                product = product_of(kind, turned, own_half)
                their_load(kind, index, slot).wait()

                @pl.when(index >= 2)
                def _():
                    sum_store(kind, index - 2, slot).wait()

                term = slot_of((their_buf, their_down_buf), kind, slot)[...].astype(F32)
                slot_of((sum_buf, sum_down), kind, slot)[...] = product + term
                sum_store(kind, index, slot).start()

    collect.line_step(1)
    collect.line_step(2)
    give_gradients(rows_all, (0, 1))
    collect.corner_step(order[3])
    give_gradients(grads_all, (2,))
    collect.plane_step(order[3])
    collect.line_step(0)
    collect.line_step(3)
    keep_gradients(rows_all, (0, 1))
    keep_gradients(grads_all, (2,))
    collect.own_step()
    total[...] = collect.mine[0, col]

    for kind in range(3):
        for slot in range(2):
            give(kind, tiles - 2 + slot, slot).wait_send()
            sum_store(kind, tiles - 2 + slot, slot).wait()
    for pair in range(2):
        for copy in stores(3, pair):
            copy.wait()
    for swap in swaps:
        swap.wait_send()
    spread_x.finish()
    spread_d.finish()
    spread_m.finish()
    collect.finish()


def expert_stage(normed, grads, mask, gate_half, up_half, down_half, router, collective_id):
    rows, width = normed.shape
    half = gate_half.shape[1]
    expert_count = router.shape[1]
    router = jnp.pad(router, ((0, 0), (0, 128 - expert_count)))
    tokens = 16 * rows
    tile = 256
    vmem = pl.BlockSpec(memory_space=pltpu.VMEM)
    hbm = pl.BlockSpec(memory_space=pl.ANY)
    dma = pltpu.SemaphoreType.DMA
    blocks = jax.ShapeDtypeStruct((4, 4, rows, width), BF16)
    got = pl.pallas_call(
        functools.partial(expert_kernel, expert_count),
        in_specs=[hbm] * 6 + [vmem],
        out_specs=[hbm] * 3 + [vmem] * 2 + [hbm] * 6,
        out_shape=[
            blocks,
            blocks,
            blocks,
            jax.ShapeDtypeStruct((rows, width), BF16),
            jax.ShapeDtypeStruct((4, 4, 8, rows), F32),
            jax.ShapeDtypeStruct((width, half), F32),
            jax.ShapeDtypeStruct((width, half), F32),
            jax.ShapeDtypeStruct((half, width), F32),
            jax.ShapeDtypeStruct((width, half), BF16),
            jax.ShapeDtypeStruct((width, half), BF16),
            jax.ShapeDtypeStruct((half, width), BF16),
        ],
        scratch_shapes=[
            pltpu.VMEM((width, 2 * half), BF16),
            pltpu.VMEM((width, 2 * half), BF16),
            pltpu.VMEM((2 * half, width), BF16),
            pltpu.VMEM((4, 4) + mask.shape, F32),
            pltpu.VMEM((2, 2 * rows, width), BF16),
            pltpu.VMEM((2, 2 * rows, width), BF16),
            pltpu.VMEM((tokens, 2 * half), BF16),
            pltpu.VMEM((tokens, 2 * half), BF16),
            pltpu.VMEM((tokens, 2 * half), BF16),
            pltpu.VMEM((2, 2 * rows, width), BF16),
            pltpu.VMEM((2, 4, 4, rows, tile), BF16),
            pltpu.VMEM((2, 2, tile, half), BF16),
            pltpu.VMEM((2, half, tile), BF16),
            pltpu.VMEM((2, 2, tile, half), BF16),
            pltpu.VMEM((2, half, tile), BF16),
            pltpu.VMEM((2, 2, tile, half), F32),
            pltpu.VMEM((2, half, tile), F32),
        ]
        + collect_buffers(rows, width)
        + COLLECT_SEMS
        + [
            dma((3,)), dma((3,)), dma((3,)), dma((3,)), dma((2, 2, 2)), dma((2, 2)),
            dma((2,)), dma((2, 3)), dma((3, width // tile)), dma((2, 3)), dma((2, 3)),
        ]
        + SPREAD_SEMS * 3,
        compiler_params=pltpu.CompilerParams(
            collective_id=collective_id, has_side_effects=True, vmem_limit_bytes=61 * 2**20
        ),
        cost_estimate=pl.CostEstimate(
            flops=18 * 2 * tokens * width * half,
            bytes_accessed=2**26,
            transcendentals=2 * tokens * half,
        ),
    )(normed, grads, mask, gate_half, up_half, down_half, router)
    return got[2], got[3], got[4], got[5:8]


def project_kernel(
    hidden, gain, weights, out_weights, q_gain, k_gain, cosine, sine,
    normed, all_weights, all_out, qkv, totals, query, keys, values,
    heads, stat, scale_q, scale_k, kept_sem, kept_out_sem, kept_kv_sem,
    stat_send, stat_recv, head_send, head_recv, pair_send, pair_recv, *sems,
):
    here = Here()
    row, col, core = here.row, here.col, here.core
    count = len(SPREAD_SEMS)
    rows, width = hidden.shape
    depth = weights.shape[0]
    part, side = depth // 2, out_weights.shape[0]

    def weight_block(of_row, unused_place, of_core):
        return all_weights.at[pl.ds(pl.multiple_of(of_row * depth + of_core * part, part), part)]

    def out_block(of_row, place, of_core):
        start = pl.multiple_of(place * side + of_core * (side // 2), side // 2)
        return all_out.at[pl.ds(start, side // 2), pl.ds(pl.multiple_of(of_row * side, side), side)]

    def normed_block(unused_row, place, unused_core):
        return normed.at[pl.ds(pl.multiple_of(place * rows, rows), rows)]

    own_weight = weights.at[pl.ds(pl.multiple_of(core * part, part), part)]
    own_out = out_weights.at[pl.ds(pl.multiple_of(core * (side // 2), side // 2), side // 2)]
    spread_w = Spread(here, own_weight, weight_block, part, sems[:count], line=False)
    spread_n = Spread(
        here, normed_block(row, col, core), normed_block, rows, sems[count : 2 * count], plane=False
    )
    spread_o = Spread(here, own_out, out_block, side // 2, sems[2 * count :])
    greet(here.plane_peers() + here.line_peers() + [here.other_core()])
    spread_w.step(0)
    keep = pltpu.make_async_copy(own_weight, weight_block(row, 0, core), kept_sem)
    keep.start()
    keep_out = pltpu.make_async_copy(own_out, out_block(row, col, core), kept_out_sem)
    keep_out.start()

    values_in = hidden[...].astype(F32)
    scale_one = lax.rsqrt(jnp.mean(values_in * values_in, axis=1, keepdims=True) + EPSILON)
    own_rows = pl.ds(pl.multiple_of(col * rows, rows), rows)
    normed[own_rows] = (values_in * scale_one * gain[...].astype(F32)).astype(BF16)
    spread_n.step(0)
    spread_o.step(0)
    spread_w.step(1)
    spread_n.step(1)
    spread_w.step(2)
    spread_n.step(2)
    spread_n.step(3)
    keep.wait()
    for which in range(4):
        spread_w.core_arrived(which, 0)

    columns = 256

    @pl.loop(0, qkv.shape[1] // columns)
    def _(index):
        at = pl.ds(pl.multiple_of(index * columns, columns), columns)
        qkv[:, at] = matmul(normed[...], all_weights[:, at])

    plane = qkv.shape[1] // (3 * HD)
    for kind in range(2):
        square = jnp.zeros((qkv.shape[0], HD), F32)
        for head in range(plane):
            start = (head * 3 + kind) * HD
            raw = qkv[:, start : start + HD]
            square = square + raw * raw
        stat[col, kind : kind + 1] = jnp.sum(square.T, axis=0, keepdims=True)

    def give_stat(step):
        peer = here.line_peers()[step]
        return remote(stat.at[col], stat.at[col], stat_send.at[step], stat_recv.at[col], peer)

    for step in range(3):
        give_stat(step).start()
    spread_o.step(1)
    for step in range(3):
        place = (col + step + 1) % 4
        arrived(stat.at[place], stat_recv.at[place])
    total = stat[0] + stat[1] + stat[2] + stat[3]
    totals[...] = total
    for kind, target in enumerate((scale_q, scale_k)):
        line = lax.rsqrt(total[kind : kind + 1] / width + EPSILON)
        target[...] = jnp.broadcast_to(line, (HD, line.shape[1])).T

    chunk = 64

    @pl.loop(0, qkv.shape[0] // chunk)
    def _(index):
        at = pl.ds(pl.multiple_of(index * chunk, chunk), chunk)
        for head in range(plane):
            for kind, (scales, gains) in enumerate(((scale_q, q_gain), (scale_k, k_gain))):
                raw = qkv[at, pl.ds((head * 3 + kind) * HD, HD)]
                unit = raw * scales[at] * gains[:, head * HD : (head + 1) * HD]
                turned = pltpu.roll(unit, HD // 2, 1)
                heads[head, kind, at] = (unit * cosine[at] + turned * sine[at]).astype(BF16)
            heads[head, 2, at] = qkv[at, pl.ds((head * 3 + 2) * HD, HD)].astype(BF16)

    targets = (query.at[row], keys.at[1, row], values.at[1, row])

    def give_head(step, kind):
        dest = here.rows[step + 1]
        sems = head_send.at[step, kind], head_recv.at[kind, row]
        return remote(heads.at[dest, kind], targets[kind], *sems, here.at_row(dest))

    for kind in (1, 2, 0):
        for step in range(3):
            give_head(step, kind).start()

    def give_pair(source, kind):
        array = (keys, values)[kind]
        sems = pair_send.at[kind, source], pair_recv.at[kind, source]
        return remote(array.at[1, source], array.at[0, source], *sems, here.other_core())

    def keep_pair(source, kind):
        array = (keys, values)[kind]
        return pltpu.make_async_copy(
            array.at[1, source], array.at[0, source], kept_kv_sem.at[kind, source]
        )

    def pair_from(source):
        @pl.when(core == 0)
        def _():
            for kind in range(2):
                give_pair(source, kind).start()
                keep_pair(source, kind).start()

    for kind, array in ((1, keys), (2, values)):
        array[1, row] = heads[row, kind]
    query[row] = heads[row, 0]
    pair_from(row)
    spread_o.step(2)
    for source in here.rows[1:]:
        arrived(keys.at[1, source], head_recv.at[1, source])
        arrived(values.at[1, source], head_recv.at[2, source])
        pair_from(source)
    spread_o.step(3)
    for source in here.rows[1:]:
        arrived(query.at[source], head_recv.at[0, source])
    spread_o.step(4)
    spread_o.step(5)

    @pl.when(core == 0)
    def _():
        for source in range(4):
            for kind in range(2):
                give_pair(source, kind).wait_send()
                keep_pair(source, kind).wait()

    @pl.when(core == 1)
    def _():
        for source in range(4):
            for kind in range(2):
                give_pair(source, kind).wait_recv()

    for step in range(3):
        give_stat(step).wait_send()
        for kind in range(3):
            give_head(step, kind).wait_send()
    keep_out.wait()
    spread_w.finish(arrivals=False)
    spread_n.finish()
    spread_o.finish()


def project(hidden, gain, weights, out_weights, q_gain, k_gain, cosine, sine, collective_id):
    rows, width = hidden.shape
    depth, columns = weights.shape
    row_tok = 4 * rows
    plane = columns // (3 * HD)
    vmem = pl.BlockSpec(memory_space=pltpu.VMEM)
    hbm = pl.BlockSpec(memory_space=pl.ANY)
    return pl.pallas_call(
        project_kernel,
        in_specs=[vmem, vmem, hbm, hbm, vmem, vmem, vmem, vmem],
        out_specs=[vmem, vmem, hbm, vmem, vmem, vmem, vmem, vmem],
        out_shape=[
            jax.ShapeDtypeStruct((row_tok, width), BF16),
            jax.ShapeDtypeStruct((4 * depth, columns), BF16),
            jax.ShapeDtypeStruct((width, width), BF16),
            jax.ShapeDtypeStruct((row_tok, columns), F32),
            jax.ShapeDtypeStruct((8, row_tok), F32),
            jax.ShapeDtypeStruct((4, row_tok, HD), BF16),
            jax.ShapeDtypeStruct((2, 4, row_tok, HD), BF16),
            jax.ShapeDtypeStruct((2, 4, row_tok, HD), BF16),
        ],
        scratch_shapes=[
            pltpu.VMEM((plane, 3, row_tok, HD), BF16),
            pltpu.VMEM((4, 8, row_tok), F32),
            pltpu.VMEM((row_tok, HD), F32),
            pltpu.VMEM((row_tok, HD), F32),
            pltpu.SemaphoreType.DMA,
            pltpu.SemaphoreType.DMA,
            pltpu.SemaphoreType.DMA((2, 4)),
            pltpu.SemaphoreType.DMA((3,)),
            pltpu.SemaphoreType.DMA((4,)),
            pltpu.SemaphoreType.DMA((3, 3)),
            pltpu.SemaphoreType.DMA((3, 4)),
            pltpu.SemaphoreType.DMA((2, 4)),
            pltpu.SemaphoreType.DMA((2, 4)),
        ]
        + SPREAD_SEMS * 3,
        compiler_params=pltpu.CompilerParams(
            collective_id=collective_id, has_side_effects=True, vmem_limit_bytes=56 * 2**20
        ),
    )(hidden, gain[None], weights, out_weights, q_gain, k_gain, cosine, sine)


def tail_kernel(
    d_qkv, weights, normed, mixed, d_attn,
    d_normed, grads,
    line, line_in, whole, give, other, plane, corner_one, corner_two, from_across, from_along,
    up_send, down_send, line_recv, other_send, other_recv,
    one_send, one_recv, two_send, two_recv, across_send, across_recv, along_send, along_recv,
    back_send, back_recv,
):
    here = Here()
    row, col, core = here.row, here.col, here.core
    rows = d_normed.shape[0]
    depth, columns = grads.shape
    part = depth // 2
    first, second = pl.ds(0, part // 2), pl.ds(part // 2, part // 2)
    order = here.near_first[::-1]
    qkv_columns = d_qkv.shape[1]
    tile = 512

    def line_rows(place):
        return pl.ds(pl.multiple_of(place * rows, rows), rows)

    def line_product(place):
        gradient = d_qkv[line_rows(place)]

        @pl.loop(0, weights.shape[0] // tile)
        def _(index):
            at = pl.ds(pl.multiple_of(index * tile, tile), tile)
            line[place, :, at] = contract_cols(gradient, weights[at]).astype(BF16)

    def give_up(place):
        sems = up_send.at[place], line_recv.at[place]
        return remote(line.at[place], line_in.at[place], *sems, here.at_col(col + 1))

    def give_down(place, slot):
        sems = down_send.at[place], line_recv.at[slot]
        return remote(line.at[place], line_in.at[slot], *sems, here.at_col(col - 1))

    def line_step(place):
        @pl.when((place > col) & (col > 0))
        def _():
            give_up(place).wait_recv()
            add_into(line.at[place], line_in.at[place])

        @pl.when((place < col) & (col < 3))
        def _():
            give_down(place, place).wait_recv()
            add_into(line.at[place], line_in.at[place])

        @pl.when(place > col)
        def _():
            give_up(place).start()

        @pl.when(place < col - 1)
        def _():
            give_down(place, place).start()

        @pl.when(place == col - 1)
        def _():
            give_down(place, 4).start()

    def row_product(which):
        of_row = here.rows[which]
        at = pl.ds(pl.multiple_of(of_row * depth, depth), depth)
        whole[:, pl.ds(0, qkv_columns)] = transposed_product(normed[:, at], d_qkv[...]).astype(BF16)
        whole[:, pl.ds(qkv_columns, columns - qkv_columns)] = transposed_product(
            mixed[...], d_attn[:, at]
        ).astype(BF16)
        plane[which] = whole[pl.ds(pl.multiple_of(core * part, part), part)]
        give[which] = whole[pl.ds(pl.multiple_of((1 - core) * part, part), part)]
        to_core(which).start()

    def to_core(which):
        sems = other_send.at[which], other_recv.at[which]
        return remote(give.at[which], other.at[which], *sems, here.other_core())

    def own_sum(which):
        to_core(which).wait_recv()
        add_into(plane.at[which], other.at[which])

    give_one = remote(
        plane.at[3, first], corner_one, one_send, one_recv, here.at_row(here.across)
    )
    give_two = remote(
        plane.at[3, second], corner_two, two_send, two_recv, here.at_row(here.along)
    )

    def give_across(index):
        at = (first, second)[index]
        sems = across_send.at[index], across_recv.at[index]
        return remote(plane.at[1, at], from_across.at[at], *sems, here.at_row(here.across))

    def give_along(index):
        at = (first, second)[index]
        sems = along_send.at[index], along_recv.at[index]
        return remote(plane.at[2, at], from_along.at[at], *sems, here.at_row(here.along))

    greet(here.plane_peers() + here.line_peers() + [here.other_core()])
    line_product(order[0])
    line_step(order[0])
    row_product(3)
    line_product(order[1])
    line_step(order[1])
    row_product(1)
    own_sum(3)
    give_one.start()
    give_two.start()
    row_product(2)
    own_sum(1)
    give_across(0).start()
    own_sum(2)
    give_along(1).start()
    line_product(order[2])
    line_step(order[2])
    row_product(0)
    line_product(order[3])
    give_two.wait_recv()
    add_into(plane.at[1, second], corner_two)
    give_across(1).start()
    give_one.wait_recv()
    add_into(plane.at[2, first], corner_one)
    give_along(0).start()
    own_sum(0)

    @pl.when(col > 0)
    def _():
        give_up(col).wait_recv()
        add_into(line.at[col], line_in.at[col])

    @pl.when(col < 3)
    def _():
        give_down(col, 4).wait_recv()
        add_into(line.at[col], line_in.at[4])

    d_normed[...] = line[col]
    for index in range(2):
        give_across(index).wait_recv()
        give_along(index).wait_recv()
    add_into(plane.at[0], from_across, from_along)
    own_half = pl.ds(pl.multiple_of(core * part, part), part)
    give_back = remote(
        plane.at[0], grads.at[own_half], back_send, back_recv, here.other_core()
    )
    give_back.start()
    grads[own_half] = plane[0]
    other_half = grads.at[pl.ds(pl.multiple_of((1 - core) * part, part), part)]
    arrived(other_half, back_recv)
    give_back.wait_send()
    give_one.wait_send()
    give_two.wait_send()
    for index in range(2):
        give_across(index).wait_send()
        give_along(index).wait_send()
    for which in range(4):
        to_core(which).wait_send()
    for place in order:

        @pl.when(place > col)
        def _():
            give_up(place).wait_send()

        @pl.when(place < col)
        def _():
            give_down(place, place).wait_send()


def tail(d_qkv, weights, normed, mixed, d_attn, collective_id):
    row_tok, qkv_columns = d_qkv.shape
    width = weights.shape[0]
    rows, depth = row_tok // 4, width // 4
    columns = qkv_columns + d_attn.shape[1] // 4
    part = depth // 2
    vmem = pl.BlockSpec(memory_space=pltpu.VMEM)
    one, four = pltpu.SemaphoreType.DMA, pltpu.SemaphoreType.DMA((4,))
    two, five = pltpu.SemaphoreType.DMA((2,)), pltpu.SemaphoreType.DMA((5,))
    return pl.pallas_call(
        tail_kernel,
        in_specs=[vmem] * 5,
        out_specs=[vmem] * 2,
        out_shape=[
            jax.ShapeDtypeStruct((rows, width), BF16),
            jax.ShapeDtypeStruct((depth, columns), BF16),
        ],
        scratch_shapes=[
            pltpu.VMEM((4, rows, width), BF16),
            pltpu.VMEM((5, rows, width), BF16),
            pltpu.VMEM((depth, columns), BF16),
            pltpu.VMEM((4, part, columns), BF16),
            pltpu.VMEM((4, part, columns), BF16),
            pltpu.VMEM((4, part, columns), BF16),
            pltpu.VMEM((part // 2, columns), BF16),
            pltpu.VMEM((part // 2, columns), BF16),
            pltpu.VMEM((part, columns), BF16),
            pltpu.VMEM((part, columns), BF16),
            four, four, five, four, four,
            one, one, one, one, two, two, two, two,
            one, one,
        ],
        compiler_params=pltpu.CompilerParams(
            collective_id=collective_id, has_side_effects=True, vmem_limit_bytes=56 * 2**20
        ),
    )(d_qkv, weights, normed, mixed, d_attn)


def sum_kernel(values, out, held, got, send, recv):
    here = Here()
    core, col = here.core, here.col
    half = values.shape[0] // 2
    peers = [
        here.at_row(here.across),
        here.at_row(here.along),
        here.at_col(col + 1 - 2 * (col % 2)),
        here.at_col((col + 2) % 4),
    ]
    greet(peers + [here.other_core()])
    own = pl.ds(pl.multiple_of(core * half, half), half)
    others = pl.ds(pl.multiple_of((1 - core) * half, half), half)
    copies = [remote(values.at[others], got.at[0], send.at[0], recv.at[0], here.other_core())]
    copies[0].start()
    copies[0].wait_recv()
    held[0] = values[own] + got[0]
    for step, peer in enumerate(peers):
        copy = remote(held.at[step], got.at[step + 1], send.at[step + 1], recv.at[step + 1], peer)
        copy.start()
        copy.wait_recv()
        held[step + 1] = held[step] + got[step + 1]
        copies.append(copy)
    out[own] = held[4]
    back = remote(held.at[4], out.at[own], send.at[5], recv.at[5], here.other_core())
    back.start()
    arrived(out.at[others], recv.at[5])
    for copy in copies + [back]:
        copy.wait_send()


def sum_everywhere(values, collective_id):
    half = (values.shape[0] // 2, values.shape[1])
    vmem = pl.BlockSpec(memory_space=pltpu.VMEM)
    return pl.pallas_call(
        sum_kernel,
        in_specs=[vmem],
        out_specs=vmem,
        out_shape=jax.ShapeDtypeStruct(values.shape, F32),
        scratch_shapes=[
            pltpu.VMEM((5,) + half, F32),
            pltpu.VMEM((5,) + half, F32),
            pltpu.SemaphoreType.DMA((6,)),
            pltpu.SemaphoreType.DMA((6,)),
        ],
        compiler_params=pltpu.CompilerParams(collective_id=collective_id, has_side_effects=True),
    )(values)


def expert_rows(rows, grads, gate, gate_w, up_w, down_w):
    pre_gate = matmul(rows, gate_w)
    pre_up = matmul(rows, up_w)
    back = contract_cols(grads, down_w)
    sigmoid_gate = jax.nn.sigmoid(pre_gate)
    silu_gate = pre_gate * sigmoid_gate
    hidden = (silu_gate * pre_up).astype(BF16)
    inner = jnp.sum(hidden.astype(F32) * back, axis=-1)
    weighted = (hidden.astype(F32) * gate).astype(BF16)
    d_hid = back * gate
    d_pregate = (d_hid * pre_up * (sigmoid_gate + silu_gate * (1.0 - sigmoid_gate))).astype(BF16)
    d_preup = (d_hid * silu_gate).astype(BF16)
    outputs = matmul(weighted, down_w).astype(BF16)
    d_rows = (contract_cols(d_pregate, gate_w) + contract_cols(d_preup, up_w)).astype(BF16)
    return (
        outputs,
        d_rows,
        inner,
        contract_rows(rows, d_pregate),
        contract_rows(rows, d_preup),
        contract_rows(weighted, grads),
    )


def experts(normed, grads, dense_gates, gate_w, up_w, down_w):
    rows_dev, width = normed.shape
    devices = math.prod(lax.axis_size(axis) for axis in ALL)
    expert_count = dense_gates.shape[1]
    expert = lax.axis_index(ALL) // 2
    parts = max(1, lax.axis_size("exp") // 2)
    step = rows_dev // parts

    def one_part(sums, piece):
        rows, grad_rows, gates = piece
        rows_all = lax.all_gather(rows, ALL, axis=0, tiled=True)
        grads_all = lax.all_gather(grad_rows, ALL, axis=0, tiled=True)
        gates_all = lax.all_gather(gates, ALL, axis=0, tiled=True)
        gate = lax.dynamic_slice_in_dim(gates_all, expert, 1, 1)
        got = expert_rows(rows_all, grads_all, gate, gate_w, up_w, down_w)
        outputs = lax.psum_scatter(got[0], ALL, scatter_dimension=0, tiled=True)
        d_rows = lax.psum_scatter(got[1], ALL, scatter_dimension=0, tiled=True)
        inner = lax.all_to_all(
            got[2].reshape(devices, step), ALL, split_axis=0, concat_axis=0, tiled=True
        )
        inner = inner.reshape(expert_count, 2, step).sum(axis=1).T
        sums = got[3:] if sums is None else tuple(a + b for a, b in zip(sums, got[3:]))
        return sums, (outputs, d_rows, inner)

    if parts == 1:
        sums, (outputs, d_rows, inner) = one_part(None, (normed, grads, dense_gates))
    else:
        start = tuple(jnp.zeros(w.shape, F32) for w in (gate_w, up_w, down_w))
        pieces = tuple(v.reshape(parts, step, -1) for v in (normed, grads, dense_gates))
        sums, got = lax.scan(one_part, start, pieces)
        outputs, d_rows, inner = (v.reshape(rows_dev, -1) for v in got)
    return outputs.astype(F32), d_rows.astype(F32), inner, sums


def experts_here(normed, grads, picks, router, gate_w, up_w, down_w):
    rows_dev, width = normed.shape
    numbers = jnp.arange(router.shape[1], dtype=jnp.int32)
    mask = jnp.any(picks.T[None] == numbers[:, None, None], axis=1).astype(F32)
    out_parts, d_rows, inner, weights = expert_stage(
        normed, grads, mask, gate_w, up_w, down_w, router, 1
    )
    outputs = reduce_rows(out_parts, 2)
    inner = inner[:, :, 0].reshape(-1, rows_dev)
    inner = lax.all_to_all(inner, ("row", "col"), split_axis=0, concat_axis=0, tiled=True).T
    return outputs.astype(F32), d_rows.astype(F32), inner, weights


def shards(
    hidden_in,
    out_grad,
    attn_gain,
    w_qkv,
    q_gain,
    k_gain,
    w_out,
    moe_gain,
    router,
    w_gate,
    w_up,
    w_down,
    routes,
    doc_cuts,
):
    row_count, col_count = lax.axis_size("row"), lax.axis_size("col")
    tokens = hidden_in[0].astype(F32)
    rows_dev, width = tokens.shape
    heads = w_qkv.shape[1] // (3 * HD)
    plane = heads * HD
    scale = HD ** (-0.5)
    side = lax.axis_index("exp") % 2
    row_tok = rows_dev * col_count
    group_tok = row_tok * row_count
    cuts = lax.dynamic_index_in_dim(doc_cuts, lax.axis_index("exp") // 2, 0, keepdims=False)

    here = (row_count, col_count, lax.axis_size("exp")) == (4, 4, 2)

    gain_one = attn_gain.astype(F32)
    scale_one = rms_scale(tokens)
    head_start = lax.axis_index("col") * plane
    gain_q = lax.dynamic_slice_in_dim(q_gain, head_start, plane, 0).astype(F32)
    gain_k = lax.dynamic_slice_in_dim(k_gain, head_start, plane, 0).astype(F32)
    row_places = side * group_tok + lax.axis_index("row") * row_tok + jnp.arange(row_tok, dtype=jnp.int32)
    unused_doc, position = doc_positions(row_places, cuts)
    cosine, sine = rope_tables(position, HD)
    if here:
        signed = jnp.concatenate([-sine[:, : HD // 2], sine[:, HD // 2 :]], axis=1)
        normed_row, qkv_w, out_w, qkv, totals, query, keys, values = project(
            hidden_in[0], attn_gain, w_qkv, w_out, gain_q[None], gain_k[None], cosine, signed, 0
        )
        total_q, total_k = totals[0], totals[1]
        query = query.reshape(group_tok, HD)
        key_all, value_all = keys.reshape(-1, HD), values.reshape(-1, HD)
    else:
        normed_one = (tokens * scale_one * gain_one).astype(BF16)
        normed_row = lax.all_gather(normed_one, "col", axis=0, tiled=True)
        qkv_w = lax.all_gather(w_qkv, "row", axis=0, tiled=True)
        out_w = lax.all_gather(
            lax.all_gather(w_out, "row", axis=1, tiled=True), "col", axis=0, tiled=True
        )
        qkv = matmul(normed_row, qkv_w)
    qkv = qkv.reshape(row_tok, heads, 3, HD)
    query_raw, key_raw, value_raw = qkv[:, :, 0], qkv[:, :, 1], qkv[:, :, 2]
    if not here:
        total_q, total_k = lax.psum(
            (jnp.sum(query_raw * query_raw, axis=(1, 2)), jnp.sum(key_raw * key_raw, axis=(1, 2))),
            "col",
        )
    scale_q = lax.rsqrt(total_q / width + EPSILON)[:, None, None]
    scale_k = lax.rsqrt(total_k / width + EPSILON)[:, None, None]
    gain_q, gain_k = gain_q.reshape(heads, HD), gain_k.reshape(heads, HD)
    cosine, sine = cosine[:, None, :], sine[:, None, :]
    if not here:
        query = rotate(query_raw * scale_q * gain_q, cosine, sine).astype(BF16)
        key = rotate(key_raw * scale_k * gain_k, cosine, sine).astype(BF16)
        moved = rows_to_heads(jnp.concatenate([query, key, value_raw.astype(BF16)], axis=-1))
        query, own_pair = moved[:, :HD], moved[:, HD:]
        earlier_pair = from_behind(own_pair, "exp", 1)
        lower_pair = jnp.where(side == 0, own_pair, earlier_pair)
        upper_pair = jnp.where(side == 0, jnp.zeros_like(own_pair), own_pair)
        key_value = jnp.concatenate([lower_pair, upper_pair], axis=0)
        key_all, value_all = key_value[:, :HD], key_value[:, HD:]

    mixed_wide, total = attend(query, key_all, value_all, cuts, scale)
    mixed = mixed_wide.astype(BF16)
    mixed_row = heads_to_rows(mixed).reshape(row_tok, plane)
    middle = tokens + matmul(heads_to_tokens(mixed), out_w)

    gain_two = moe_gain.astype(F32)
    scale_two = rms_scale(middle)
    normed_two = (middle * scale_two * gain_two).astype(BF16)
    gates_all = jax.nn.softmax(matmul(normed_two, router), axis=-1)
    picks = routes[0]
    chosen = jnp.any(
        picks[:, :, None] == jnp.arange(router.shape[1], dtype=jnp.int32)[None, None, :], axis=1
    )
    grad_out = out_grad[0].astype(F32)
    expert_w = (w_gate[0], w_up[0], w_down[0])
    if here:
        mixture, d_normed_two, inner, weight_grads = experts_here(
            normed_two, out_grad[0], picks, router, *expert_w
        )
    else:
        dense_gates = jnp.where(chosen, gates_all, 0.0)
        mixture, d_normed_two, inner, weight_grads = experts(
            normed_two, out_grad[0], dense_gates, *expert_w
        )
    final = middle + mixture
    dense = jnp.where(chosen, inner, 0.0)
    d_logits = (gates_all * (dense - jnp.sum(gates_all * dense, axis=-1, keepdims=True))).astype(BF16)
    grad_router = contract_rows(normed_two, d_logits)
    d_normed_two = d_normed_two + contract_cols(d_logits, router)
    grad_moe_gain = jnp.sum(d_normed_two * middle * scale_two, axis=0)
    weighted_two = d_normed_two * gain_two
    d_middle = (
        grad_out
        + scale_two * weighted_two
        - middle * scale_two**3 * jnp.mean(weighted_two * middle, axis=-1, keepdims=True)
    )

    d_attn = d_middle.astype(BF16)
    d_mixed = tokens_to_heads(contract_cols(d_attn, out_w).astype(BF16))
    d_attn_row = lax.all_gather(d_attn, "col", axis=0, tiled=True)
    d_query, acc_key, acc_value = attend_back(
        query, key_all, value_all, d_mixed, mixed_wide, total, cuts, scale
    )
    accumulated = jnp.concatenate([acc_key, acc_value], axis=1)
    lower_acc, upper_acc = accumulated[:group_tok], accumulated[group_tok:]
    kept_acc = jnp.where(side == 0, lower_acc, upper_acc)
    later_acc = from_behind(lower_acc.astype(BF16), "exp", -1).astype(F32)
    summed_pair = kept_acc + jnp.where(side == 0, later_acc, jnp.zeros_like(later_acc))
    d_heads = heads_to_rows(jnp.concatenate([d_query, summed_pair], axis=1).astype(BF16)).astype(F32)
    d_q_unit = rotate_back(d_heads[:, :, :HD], cosine, sine)
    d_k_unit = rotate_back(d_heads[:, :, HD : 2 * HD], cosine, sine)
    d_value = d_heads[:, :, 2 * HD :]
    weighted_q = d_q_unit * gain_q
    weighted_k = d_k_unit * gain_k
    sum_q, sum_k = lax.psum(
        (jnp.sum(weighted_q * query_raw, axis=(1, 2)), jnp.sum(weighted_k * key_raw, axis=(1, 2))),
        "col",
    )
    d_query_raw = scale_q * weighted_q - query_raw * scale_q**3 * (sum_q / width)[:, None, None]
    d_key_raw = scale_k * weighted_k - key_raw * scale_k**3 * (sum_k / width)[:, None, None]
    grad_q_part = jnp.sum(d_q_unit * query_raw * scale_q, axis=0).reshape(plane)
    grad_k_part = jnp.sum(d_k_unit * key_raw * scale_k, axis=0).reshape(plane)
    d_qkv = jnp.concatenate([d_query_raw, d_key_raw, d_value], axis=2).astype(BF16)
    d_qkv = d_qkv.reshape(row_tok, heads * 3 * HD)
    if here:
        d_normed_one, grads = tail(d_qkv, qkv_w, normed_row, mixed_row, d_attn_row, 5)
        d_normed_one, grads = d_normed_one.astype(F32), grads.astype(F32)
        grad_qkv, grad_w_out = grads[:, : d_qkv.shape[1]], grads[:, d_qkv.shape[1] :]
    else:
        d_normed_one = lax.psum_scatter(
            contract_cols(d_qkv, qkv_w).astype(BF16), "col", scatter_dimension=0, tiled=True
        ).astype(F32)
        grad_qkv = lax.psum_scatter(
            contract_rows(normed_row, d_qkv).astype(BF16), "row", scatter_dimension=0, tiled=True
        )
        grad_w_out = lax.psum_scatter(
            contract_rows(mixed_row, d_attn_row).astype(BF16), "row", scatter_dimension=1, tiled=True
        )
        grad_qkv = lax.psum(grad_qkv, "exp").astype(F32)
        grad_w_out = lax.psum(grad_w_out, "exp").astype(F32)
    grad_attn_gain = jnp.sum(d_normed_one * tokens * scale_one, axis=0)
    weighted_one = d_normed_one * gain_one
    grad_hidden = (
        d_middle
        + scale_one * weighted_one
        - tokens * scale_one**3 * jnp.mean(weighted_one * tokens, axis=-1, keepdims=True)
    )
    empty = jnp.zeros((width,), F32)
    grad_q_full = lax.dynamic_update_slice_in_dim(empty, grad_q_part, head_start, 0)
    grad_k_full = lax.dynamic_update_slice_in_dim(empty, grad_k_part, head_start, 0)
    parts = (grad_attn_gain, grad_q_full, grad_k_full, grad_moe_gain)
    if here:
        packed = jnp.concatenate(parts + (grad_router.T.reshape(-1),)).reshape(-1, 128)
        packed = sum_everywhere(packed, 6).reshape(-1)
        summed = [packed[i * width : (i + 1) * width] for i in range(4)]
        summed.append(packed[4 * width :].reshape(-1, width).T)
    else:
        summed = lax.psum(parts + (grad_router,), ALL)
    return (
        final.astype(BF16)[None],
        grad_hidden[None],
        summed[0],
        grad_qkv,
        summed[1],
        summed[2],
        grad_w_out,
        summed[3],
        summed[4],
        weight_grads[0][None],
        weight_grads[1][None],
        weight_grads[2][None],
    )


def solution(mesh):
    token_spec = P("exp", ("row", "col"), None)
    expert_spec = P(("row", "col", "exp"), None, None)
    in_specs = (
        token_spec,
        token_spec,
        P(),
        P("row", "col"),
        P(),
        P(),
        P("col", "row"),
        P(),
        P(),
        expert_spec,
        expert_spec,
        expert_spec,
        token_spec,
        P(),
    )
    out_specs = (
        token_spec,
        token_spec,
        P(),
        P("row", "col"),
        P(),
        P(),
        P("col", "row"),
        P(),
        P(),
        expert_spec,
        expert_spec,
        expert_spec,
    )
    return jax.shard_map(shards, mesh=mesh, in_specs=in_specs, out_specs=out_specs, check_vma=False)
```

```python
import functools
import math

import jax
import jax.numpy as jnp
from jax import lax
from jax.experimental import pallas as pl
from jax.experimental.pallas import tpu as pltpu
from jax.sharding import PartitionSpec as P

HD = 128
EPSILON = 1e-05
ROPE_BASE = 10000.0
MASKED = -1e30
BF16 = jnp.bfloat16
F32 = jnp.float32


def matmul(left, right):
    return jnp.dot(left, right, preferred_element_type=F32)


def contract_rows(left, right):
    return lax.dot_general(left, right, (((0,), (0,)), ((), ())), preferred_element_type=F32)


def contract_cols(left, right):
    return lax.dot_general(left, right, (((1,), (1,)), ((), ())), preferred_element_type=F32)


def rms_scale(values):
    return lax.rsqrt(jnp.mean(values * values, axis=-1, keepdims=True) + EPSILON)


def rope_tables(position, width):
    frequency = ROPE_BASE ** (-jnp.arange(0, width, 2, dtype=F32) / width)
    angle = position.astype(F32)[:, None] * frequency[None, :]
    return (
        jnp.concatenate([jnp.cos(angle)] * 2, axis=-1),
        jnp.concatenate([jnp.sin(angle)] * 2, axis=-1),
    )


def rotate(values, cosine, sine):
    half = values.shape[-1] // 2
    turned = jnp.concatenate([-values[..., half:], values[..., :half]], axis=-1)
    return values * cosine + turned * sine


def rotate_back(values, cosine, sine):
    half = values.shape[-1] // 2
    turned = values * sine
    return values * cosine + jnp.concatenate([turned[..., half:], -turned[..., :half]], axis=-1)


def doc_positions(places, cuts):
    first = (places >= cuts[0]).astype(jnp.int32)
    second = (places >= cuts[1]).astype(jnp.int32)
    start = first * cuts[0] + second * (cuts[1] - cuts[0])
    return (first + second, places - start)


def from_behind(value, axis, steps):
    count = lax.axis_size(axis)
    initial, last = (max(0, -steps), min(count, count - steps))
    return lax.ppermute(value, axis, [(source, source + steps) for source in range(initial, last)])


def rows_to_heads(values):
    count = lax.axis_size("row")
    rows, heads, width = values.shape
    moved = lax.all_to_all(values.transpose(1, 0, 2), "row", split_axis=0, concat_axis=0, tiled=True)
    return moved.reshape(count * rows, width)


def heads_to_rows(values):
    count = lax.axis_size("row")
    rows, width = values.shape
    moved = lax.all_to_all(
        values.reshape(count, rows // count, width), "row", split_axis=0, concat_axis=0, tiled=True
    )
    return moved.transpose(1, 0, 2)


def heads_to_tokens(values):
    row_count, col_count = lax.axis_size("row"), lax.axis_size("col")
    rows = values.shape[0] // (row_count * col_count)
    moved = lax.all_to_all(
        values.reshape(row_count * col_count, rows, HD),
        ("row", "col"),
        split_axis=0,
        concat_axis=0,
        tiled=True,
    )
    moved = moved.reshape(row_count, col_count, rows, HD).transpose(2, 1, 0, 3)
    return moved.reshape(rows, row_count * col_count * HD)


def tokens_to_heads(values):
    row_count, col_count = lax.axis_size("row"), lax.axis_size("col")
    rows = values.shape[0]
    parted = values.reshape(rows, col_count, row_count, HD).transpose(2, 1, 0, 3)
    moved = lax.all_to_all(
        parted.reshape(row_count * col_count, rows, HD),
        ("row", "col"),
        split_axis=0,
        concat_axis=0,
        tiled=True,
    )
    return moved.reshape(row_count * col_count * rows, HD)


MESH = pl.DeviceIdType.MESH
ALL = ("row", "col", "exp")


class Here:
    def __init__(self):
        self.row, self.col, self.core = (lax.axis_index(axis) for axis in ALL)
        self.across = self.row + 1 - 2 * (self.row % 2)
        self.along = (self.row + 2) % 4
        self.opposite = 3 - self.row
        self.rows = (self.row, self.across, self.along, self.opposite)
        half = self.col // 2
        self.near_first = [
            self.col,
            1 + self.col % 2,
            2 - self.col - self.col % 2 + 3 * half,
            3 - 3 * half,
        ]

    def at_row(self, row):
        return (row, self.col, self.core)

    def at_col(self, col):
        return (self.row, col, self.core)

    def other_core(self):
        return (self.row, self.col, 1 - self.core)

    def line_peers(self):
        return [self.at_col((self.col + step) % 4) for step in (1, 2, 3)]

    def group_peers(self):
        steps = range(1, 16)
        return [((self.row + s // 4) % 4, (self.col + s) % 4, self.core) for s in steps]

    def plane_peers(self):
        return [self.at_row(row) for row in self.rows[1:]]


def greet(peers):
    barrier = pltpu.get_barrier_semaphore()
    for peer in peers:
        pl.semaphore_signal(barrier, inc=1, device_id=peer, device_id_type=MESH)
    pl.semaphore_wait(barrier, len(peers))


def greet_near(here):
    barrier = pltpu.get_barrier_semaphore()
    col = here.col

    def signal(peer):
        pl.semaphore_signal(barrier, inc=1, device_id=peer, device_id_type=MESH)

    for peer in (here.other_core(), here.at_row(here.across), here.at_row(here.along)):
        signal(peer)

    @pl.when(col > 0)
    def _():
        signal(here.at_col(col - 1))

    @pl.when(col < 3)
    def _():
        signal(here.at_col(col + 1))

    pl.semaphore_wait(barrier, 3 + (col + 3) // 4 + (6 - col) // 4)


def remote(source, target, send, recv, device):
    return pltpu.make_async_remote_copy(
        src_ref=source,
        dst_ref=target,
        send_sem=send,
        recv_sem=recv,
        device_id=device,
        device_id_type=MESH,
    )


def arrived(target, recv):
    pltpu.make_async_copy(target, target, recv).wait()


def add_into(target, *terms):
    step = 16

    @pl.loop(0, target.shape[0] // step)
    def _(index):
        part = pl.ds(pl.multiple_of(index * step, step), step)
        value = target[part].astype(F32)
        for term in terms:
            value = value + term[part].astype(F32)
        target[part] = value.astype(target.dtype)


SPREAD_SEMS = [pltpu.SemaphoreType.DMA((4,))] * 11 + [pltpu.SemaphoreType.DMA((4, 4))] * 2


class Spread:
    def __init__(self, here, own, block, rows, sems, line=True, plane=True, core=True):
        self.here, self.own, self.block = here, own, block
        self.line, self.plane, self.core = line, plane, core
        (
            self.up_send, self.down_send, self.line_recv,
            self.across_send, self.across_recv, self.along_send, self.along_recv,
            self.one_send, self.one_recv, self.two_send, self.two_recv,
            self.core_send, self.core_recv,
        ) = sems
        self.first, self.second = pl.ds(0, rows // 2), pl.ds(rows // 2, rows // 2)
        self.order = here.near_first if line else [0]
        self.steps = len(self.order)

    def held(self, step):
        here = self.here
        return self.own if step == 0 else self.block(here.row, self.order[step], here.core)

    def up(self, step):
        here, place = self.here, self.order[step]
        target = self.block(here.row, place, here.core)
        recv = self.line_recv.at[place]
        return remote(self.held(step), target, self.up_send.at[place], recv, here.at_col(here.col + 1))

    def down(self, step):
        here, place = self.here, self.order[step]
        target = self.block(here.row, place, here.core)
        recv = self.line_recv.at[place]
        return remote(self.held(step), target, self.down_send.at[place], recv, here.at_col(here.col - 1))

    def to_across(self, step):
        here, place = self.here, self.order[step]
        target = self.block(here.row, place, here.core)
        sems = self.across_send.at[place], self.across_recv.at[place]
        return remote(self.held(step), target, *sems, here.at_row(here.across))

    def to_along(self, step):
        here, place = self.here, self.order[step]
        target = self.block(here.row, place, here.core)
        sems = self.along_send.at[place], self.along_recv.at[place]
        return remote(self.held(step), target, *sems, here.at_row(here.along))

    def corner_one(self, step):
        here, place = self.here, self.order[step]
        part = self.block(here.across, place, here.core).at[self.first]
        sems = self.one_send.at[place], self.one_recv.at[place]
        return remote(part, part, *sems, here.at_row(here.along))

    def corner_two(self, step):
        here, place = self.here, self.order[step]
        part = self.block(here.along, place, here.core).at[self.second]
        sems = self.two_send.at[place], self.two_recv.at[place]
        return remote(part, part, *sems, here.at_row(here.across))

    def to_core(self, which, step):
        here, place = self.here, self.order[step]
        target = self.block(here.rows[which], place, here.core)
        source = self.held(step) if which == 0 else target
        sems = self.core_send.at[which, place], self.core_recv.at[which, place]
        return remote(source, target, *sems, here.other_core())

    def line_step(self, step):
        here, place = self.here, self.order[step]
        if step > 0:
            arrived(self.held(step), self.line_recv.at[place])
        if self.line:

            @pl.when((place <= here.col) & (here.col < 3))
            def _():
                self.up(step).start()

            @pl.when((place >= here.col) & (here.col > 0))
            def _():
                self.down(step).start()

        if self.plane:
            self.to_across(step).start()
            self.to_along(step).start()
            if self.core:
                self.to_core(0, step).start()

    def plane_step(self, step):
        here, place = self.here, self.order[step]
        arrived(self.block(here.across, place, here.core), self.across_recv.at[place])
        self.corner_one(step).start()
        if self.core:
            self.to_core(1, step).start()
        arrived(self.block(here.along, place, here.core), self.along_recv.at[place])
        self.corner_two(step).start()
        if self.core:
            self.to_core(2, step).start()

    def corner_step(self, step):
        here, place = self.here, self.order[step]
        target = self.block(here.opposite, place, here.core)
        arrived(target.at[self.first], self.one_recv.at[place])
        arrived(target.at[self.second], self.two_recv.at[place])
        if self.core:
            self.to_core(3, step).start()

    def step(self, index):
        if index < self.steps:
            self.line_step(index)
        if self.plane and 0 <= index - 1 < self.steps:
            self.plane_step(index - 1)
        if self.plane and 0 <= index - 2 < self.steps:
            self.corner_step(index - 2)

    def core_arrived(self, which, step):
        here, place = self.here, self.order[step]
        target = self.block(here.rows[which], place, 1 - here.core)
        arrived(target, self.core_recv.at[which, place])

    def finish(self, arrivals=True):
        here = self.here
        for step in range(self.steps):
            place = self.order[step]
            if self.line:

                @pl.when((place <= here.col) & (here.col < 3))
                def _():
                    self.up(step).wait_send()

                @pl.when((place >= here.col) & (here.col > 0))
                def _():
                    self.down(step).wait_send()

            if self.plane:
                self.to_across(step).wait_send()
                self.to_along(step).wait_send()
                self.corner_one(step).wait_send()
                self.corner_two(step).wait_send()
                for which in range(4 if self.core else 0):
                    self.to_core(which, step).wait_send()
                    if arrivals:
                        self.core_arrived(which, step)


COLLECT_SEMS = (
    [pltpu.SemaphoreType.DMA((4,))] * 4
    + [pltpu.SemaphoreType.DMA((2, 4))] * 4
    + [pltpu.SemaphoreType.DMA((4,))] * 2
    + [pltpu.SemaphoreType.DMA((5,))]
)


def collect_buffers(rows, width):
    return [
        pltpu.VMEM((4, 4, rows, width), BF16),
        pltpu.VMEM((4, rows // 2, width), BF16),
        pltpu.VMEM((4, rows // 2, width), BF16),
        pltpu.VMEM((4, rows, width), BF16),
        pltpu.VMEM((4, rows, width), BF16),
        pltpu.VMEM((5, rows, width), BF16),
    ]


class Collect:
    def __init__(self, here, buffers, sems):
        self.here = here
        self.mine, self.one, self.two, self.from_across, self.from_along, self.line = buffers
        (
            self.one_send, self.one_recv, self.two_send, self.two_recv,
            self.across_send, self.across_recv, self.along_send, self.along_recv,
            self.up_send, self.down_send, self.line_recv,
        ) = sems
        half = self.mine.shape[2] // 2
        self.halves = (pl.ds(0, half), pl.ds(half, half))

    def give_one(self, place):
        here = self.here
        return remote(
            self.mine.at[3, place, self.halves[0]], self.one.at[place],
            self.one_send.at[place], self.one_recv.at[place], here.at_row(here.across),
        )

    def give_two(self, place):
        here = self.here
        return remote(
            self.mine.at[3, place, self.halves[1]], self.two.at[place],
            self.two_send.at[place], self.two_recv.at[place], here.at_row(here.along),
        )

    def give_across(self, place, half):
        here, part = self.here, self.halves[half]
        return remote(
            self.mine.at[1, place, part], self.from_across.at[place, part],
            self.across_send.at[half, place], self.across_recv.at[half, place], here.at_row(here.across),
        )

    def give_along(self, place, half):
        here, part = self.here, self.halves[half]
        return remote(
            self.mine.at[2, place, part], self.from_along.at[place, part],
            self.along_send.at[half, place], self.along_recv.at[half, place], here.at_row(here.along),
        )

    def give_up(self, place):
        here = self.here
        sems = self.up_send.at[place], self.line_recv.at[place]
        return remote(self.mine.at[0, place], self.line.at[place], *sems, here.at_col(here.col + 1))

    def give_down(self, place, slot):
        here = self.here
        sems = self.down_send.at[place], self.line_recv.at[slot]
        return remote(self.mine.at[0, place], self.line.at[slot], *sems, here.at_col(here.col - 1))

    def start_far(self, place):
        self.give_one(place).start()
        self.give_two(place).start()
        self.give_along(place, 1).start()

    def start_near(self, place):
        self.give_across(place, 0).start()

    def corner_step(self, place):
        self.give_two(place).wait_recv()
        add_into(self.mine.at[1, place, self.halves[1]], self.two.at[place])
        self.give_across(place, 1).start()
        self.give_one(place).wait_recv()
        add_into(self.mine.at[2, place, self.halves[0]], self.one.at[place])
        self.give_along(place, 0).start()

    def plane_step(self, place):
        for half in range(2):
            self.give_across(place, half).wait_recv()
            self.give_along(place, half).wait_recv()
        add_into(self.mine.at[0, place], self.from_across.at[place], self.from_along.at[place])

    def line_step(self, place):
        col = self.here.col

        @pl.when((place > col) & (col > 0))
        def _():
            self.give_up(place).wait_recv()
            add_into(self.mine.at[0, place], self.line.at[place])

        @pl.when((place < col) & (col < 3))
        def _():
            self.give_down(place, place).wait_recv()
            add_into(self.mine.at[0, place], self.line.at[place])

        @pl.when(place > col)
        def _():
            self.give_up(place).start()

        @pl.when(place < col - 1)
        def _():
            self.give_down(place, place).start()

        @pl.when(place == col - 1)
        def _():
            self.give_down(place, 4).start()

    def own_step(self):
        col = self.here.col

        @pl.when(col > 0)
        def _():
            self.give_up(col).wait_recv()
            add_into(self.mine.at[0, col], self.line.at[col])

        @pl.when(col < 3)
        def _():
            self.give_down(col, 4).wait_recv()
            add_into(self.mine.at[0, col], self.line.at[4])

    def finish(self):
        col = self.here.col
        for place in range(4):
            self.give_one(place).wait_send()
            self.give_two(place).wait_send()
            for half in range(2):
                self.give_across(place, half).wait_send()
                self.give_along(place, half).wait_send()

            @pl.when(place > col)
            def _():
                self.give_up(place).wait_send()

            @pl.when(place < col)
            def _():
                self.give_down(place, place).wait_send()


def reduce_kernel(values, total, *rest):
    here = Here()
    collect = Collect(here, rest[:6], rest[6 : 6 + len(COLLECT_SEMS)])
    load_sem = rest[-1]
    order = here.near_first[::-1]

    def load(which, place):
        return pltpu.make_async_copy(
            values.at[which, place], collect.mine.at[which, place], load_sem.at[which, place]
        )

    for place in order:
        for which in (3, 2, 1, 0):
            load(which, place).start()
    greet_near(here)
    for step in range(6):
        if step < 4:
            place = order[step]
            load(3, place).wait()
            load(2, place).wait()
            collect.start_far(place)
            load(1, place).wait()
            collect.start_near(place)
        if 0 <= step - 1 < 4:
            collect.corner_step(order[step - 1])
        if 0 <= step - 2 < 4:
            place = order[step - 2]
            load(0, place).wait()
            collect.plane_step(place)
            collect.line_step(place)
    collect.own_step()
    total[...] = collect.mine[0, here.col]
    collect.finish()


def reduce_rows(values, collective_id):
    rows, width = values.shape[2:]
    return pl.pallas_call(
        reduce_kernel,
        out_shape=jax.ShapeDtypeStruct((rows, width), BF16),
        in_specs=[pl.BlockSpec(memory_space=pl.ANY)],
        out_specs=pl.BlockSpec(memory_space=pltpu.VMEM),
        scratch_shapes=collect_buffers(rows, width)
        + COLLECT_SEMS
        + [pltpu.SemaphoreType.DMA((4, 4))],
        compiler_params=pltpu.CompilerParams(
            collective_id=collective_id, has_side_effects=True, vmem_limit_bytes=40 * 2**20
        ),
    )(values)


def doc_start(places, cuts):
    return jnp.where(places >= cuts[1], cuts[1], jnp.where(places >= cuts[0], cuts[0], 0))


def key_blocks(cuts, first_query, rows, scores_of, block_fn):
    def scan(index, carry):
        start = pl.multiple_of(index * rows, rows)
        free = (start >= doc_start(first_query + rows - 1, cuts)) & (start + rows <= first_query + 1)

        @pl.when(free)
        def _():
            block_fn(start, scores_of(start))

        @pl.when(jnp.logical_not(free))
        def _():
            key_place = start + lax.broadcasted_iota(jnp.int32, (rows, rows), 0)
            place = first_query + lax.broadcasted_iota(jnp.int32, (1, rows), 1)
            allowed = (key_place <= place) & (key_place >= doc_start(place, cuts))
            block_fn(start, jnp.where(allowed, scores_of(start), MASKED))

        return carry

    lax.fori_loop(doc_start(first_query, cuts) // rows, first_query // rows + 1, scan, 0)


def attend_kernel(scale, group_tok, cuts, query, keys, values_t, mixed, total, top, summed, acc):
    rows = query.shape[0]
    side = lax.axis_index("exp") % 2
    first_query = side * group_tok + pl.program_id(0) * rows
    top[...] = jnp.full_like(top, MASKED)
    summed[...] = jnp.zeros_like(summed)
    acc[...] = jnp.zeros_like(acc)
    cut = (cuts[0, 0], cuts[0, 1])

    def scores_of(start):
        return contract_cols(keys[pl.ds(start, rows)], query[...]) * scale

    def block_fn(start, scores):
        old = top[...]
        new = jnp.maximum(old, jnp.max(scores, axis=0, keepdims=True))
        weights = jnp.exp(scores - new)
        decay = jnp.exp(old - new)
        top[...] = new
        summed[...] = summed[...] * decay + jnp.sum(weights, axis=0, keepdims=True)
        acc[...] = acc[...] * decay + matmul(values_t[:, pl.ds(start, rows)], weights.astype(BF16))

    key_blocks(cut, first_query, rows, scores_of, block_fn)
    mixed[...] = (acc[...] / summed[...]).T
    total[...] = top[...] + jnp.log(summed[...])


def attend(query, keys, values, cuts, scale, rows=512):
    group_tok, head_size = query.shape
    whole = lambda shape: pl.BlockSpec(shape, lambda i: (0, 0))
    return pl.pallas_call(
        functools.partial(attend_kernel, scale, group_tok),
        grid=(group_tok // rows,),
        in_specs=[
            pl.BlockSpec(memory_space=pltpu.SMEM),
            pl.BlockSpec((rows, head_size), lambda i: (i, 0)),
            whole(keys.shape),
            whole(values.shape[::-1]),
        ],
        out_specs=[
            pl.BlockSpec((rows, head_size), lambda i: (i, 0)),
            pl.BlockSpec((1, rows), lambda i: (0, i)),
        ],
        out_shape=[
            jax.ShapeDtypeStruct((group_tok, head_size), F32),
            jax.ShapeDtypeStruct((1, group_tok), F32),
        ],
        scratch_shapes=[
            pltpu.VMEM((1, rows), F32),
            pltpu.VMEM((1, rows), F32),
            pltpu.VMEM((head_size, rows), F32),
        ],
        compiler_params=pltpu.CompilerParams(vmem_limit_bytes=40 * 2**20),
        cost_estimate=pl.CostEstimate(
            flops=4 * 7 * 2**20 * head_size, bytes_accessed=2**23, transcendentals=7 * 2**20
        ),
    )(cuts[None], query, keys, values.T)


def attend_back_kernel(
    scale, group_tok, cuts, query, keys, keys_t, values, d_mixed, total, delta,
    d_query, d_keys, d_values, acc,
):
    rows = query.shape[0]
    side = lax.axis_index("exp") % 2
    first_query = side * group_tok + pl.program_id(0) * rows
    cut = (cuts[0, 0], cuts[0, 1])

    @pl.when(pl.program_id(0) == 0)
    def _():
        d_keys[...] = jnp.zeros_like(d_keys)
        d_values[...] = jnp.zeros_like(d_values)

    acc[...] = jnp.zeros_like(acc)

    def scores_of(start):
        return contract_cols(keys[pl.ds(start, rows)], query[...]) * scale

    def block_fn(start, scores):
        part = pl.ds(start, rows)
        weights = jnp.exp(scores - total[...])
        d_weights = contract_cols(values[part], d_mixed[...])
        d_scores = (weights * (d_weights - delta[...])).astype(BF16)
        d_values[part] += matmul(weights.astype(BF16), d_mixed[...])
        d_keys[part] += matmul(d_scores, query[...]) * scale
        acc[...] += matmul(keys_t[:, part], d_scores)

    key_blocks(cut, first_query, rows, scores_of, block_fn)
    d_query[...] = (acc[...] * scale).T


def attend_back(query, keys, values, d_mixed, mixed, total, cuts, scale, rows=512):
    group_tok, head_size = query.shape
    delta = jnp.sum(d_mixed.astype(F32) * mixed, axis=1)[None]
    whole = lambda shape: pl.BlockSpec(shape, lambda i: (0, 0))
    block = pl.BlockSpec((rows, head_size), lambda i: (i, 0))
    line = pl.BlockSpec((1, rows), lambda i: (0, i))
    return pl.pallas_call(
        functools.partial(attend_back_kernel, scale, group_tok),
        grid=(group_tok // rows,),
        in_specs=[
            pl.BlockSpec(memory_space=pltpu.SMEM),
            block,
            whole(keys.shape),
            whole(keys.shape[::-1]),
            whole(keys.shape),
            block,
            line,
            line,
        ],
        out_specs=[block, whole(keys.shape), whole(keys.shape)],
        out_shape=[
            jax.ShapeDtypeStruct((group_tok, head_size), F32),
            jax.ShapeDtypeStruct(keys.shape, F32),
            jax.ShapeDtypeStruct(keys.shape, F32),
        ],
        scratch_shapes=[pltpu.VMEM((head_size, rows), F32)],
        compiler_params=pltpu.CompilerParams(vmem_limit_bytes=48 * 2**20),
        cost_estimate=pl.CostEstimate(
            flops=10 * 7 * 2**20 * head_size, bytes_accessed=2**23, transcendentals=7 * 2**20
        ),
    )(cuts[None], query, keys, keys.T, values, d_mixed, total, delta)


def transposed_product(left, right):
    return jnp.dot(left.T, right, preferred_element_type=F32)


def column_of(line):
    return jnp.broadcast_to(line, (128, 128)).T[:, :1]


def line_of(column):
    return jnp.broadcast_to(column, (128, 128)).T[:1]


def expert_kernel(
    expert_count, normed, grads_all, mask, gate_half, up_half, down_half, router,
    rows_all, out_parts, total, inner_in, grad_gate, grad_up, grad_down,
    their_gate, their_up, their_down,
    gate_w, up_w, down_w, masks, x_buf, d_buf, d_gates, d_ups, weighteds, out_buf,
    inner, tile_buf, give_buf, give_down, their_buf, their_down_buf, sum_buf, sum_down, *rest,
):
    here = Here()
    row, col, core = here.row, here.col, here.core
    rows, width = normed.shape
    half = gate_half.shape[1]
    expert = row * 4 + col
    count = len(SPREAD_SEMS)
    collect = Collect(here, rest[:6], rest[6 : 6 + len(COLLECT_SEMS)])
    rest = rest[6 + len(COLLECT_SEMS) :]
    (
        kept_sem, weight_sem, weight_send, weight_recv, load_sem, store_sem,
        tile_sem, give_send, give_recv, their_sem, sum_sem,
        inner_send, inner_recv,
    ) = rest[:13]
    sems = rest[13:]

    def x_block(of_row, place, unused_core):
        return rows_all.at[of_row, place]

    def d_block(of_row, place, unused_core):
        return grads_all.at[of_row, place]

    def m_block(of_row, place, unused_core):
        return masks.at[of_row, place]

    spread_x = Spread(here, normed, x_block, rows, sems[:count], core=False)
    spread_m = Spread(here, mask, m_block, mask.shape[0], sems[count:], core=False)
    order = here.near_first

    own_half = pl.ds(pl.multiple_of(core * half, half), half)
    other_half = pl.ds(pl.multiple_of((1 - core) * half, half), half)
    halves = (
        (gate_half, gate_w.at[:, own_half], gate_w.at[:, other_half]),
        (up_half, up_w.at[:, own_half], up_w.at[:, other_half]),
        (down_half, down_w.at[own_half], down_w.at[other_half]),
    )
    keeps = [
        pltpu.make_async_copy(source, target, weight_sem.at[index])
        for index, (source, target, unused) in enumerate(halves)
    ] + [
        pltpu.make_async_copy(source, target, kept_sem.at[index])
        for index, (source, target) in enumerate(
            ((normed, x_block(row, col, 0)), (mask, m_block(row, col, 0)))
        )
    ]
    for keep in keeps:
        keep.start()
    greet(here.group_peers() + [here.other_core()])
    swaps = [
        remote(source, target, weight_send.at[index], weight_recv.at[index], here.other_core())
        for index, (source, target, unused) in enumerate(halves)
    ]
    spread_x.step(0)
    spread_m.step(0)
    for swap in swaps:
        swap.start()

    pairs = ((3, 2), (1, 0))

    def loads(step, pair):
        place, slot = order[step], pair
        made = []
        for index, which in enumerate(pairs[pair]):
            part = pl.ds(index * rows, rows)
            for array, (source, target) in enumerate(((x_block, x_buf), (d_block, d_buf))):
                made.append(
                    pltpu.make_async_copy(
                        source(here.rows[which], place, 0),
                        target.at[slot, part],
                        load_sem.at[slot, index, array],
                    )
                )
        return made

    def stores(step, pair):
        return [
            pltpu.make_async_copy(
                out_buf.at[pair, pl.ds(index * rows, rows)],
                out_parts.at[which, order[step]],
                store_sem.at[pair, index],
            )
            for index, which in enumerate(pairs[pair])
        ]

    def act_rows(which, place):
        start = (here.rows[which] * 4 + place) * rows
        return pl.ds(pl.multiple_of(start, rows), rows)

    tile = 256

    def first_products(step, pair):
        place = order[step]
        x, dy = x_buf[pair], d_buf[pair]
        lane = lax.broadcasted_iota(jnp.int32, (x.shape[0], router.shape[1]), 1)
        logits = jnp.where(lane < expert_count, matmul(x, router[...]), MASKED)
        raised = jnp.exp(logits - jnp.max(logits, axis=1, keepdims=True))
        picked = jnp.sum(jnp.where(lane == expert, raised, 0.0), axis=1, keepdims=True)
        routed = jnp.concatenate(
            [column_of(masks[here.rows[which], place, pl.ds(expert, 1)]) for which in pairs[pair]]
        )
        gate = picked / jnp.sum(raised, axis=1, keepdims=True) * routed
        ats = [act_rows(which, place) for which in pairs[pair]]

        def tile_step(index, inner_sum):
            at = pl.ds(pl.multiple_of(index * tile, tile), tile)
            pre_gate = matmul(x_buf[pair], gate_w[:, at])
            pre_up = matmul(x_buf[pair], up_w[:, at])
            back = contract_cols(d_buf[pair], down_w[at])
            sigmoid_gate = 1.0 / (1.0 + jnp.exp(-pre_gate))
            silu_gate = pre_gate * sigmoid_gate
            hidden = (silu_gate * pre_up).astype(BF16).astype(F32)
            d_hid = back * gate
            d_gate = (d_hid * pre_up * (sigmoid_gate + silu_gate * (1.0 - sigmoid_gate))).astype(BF16)
            d_up = (d_hid * silu_gate).astype(BF16)
            weighted = (hidden * gate).astype(BF16)
            for position, act in enumerate(ats):
                part = slice(position * rows, (position + 1) * rows)
                d_gates[act, at] = d_gate[part]
                d_ups[act, at] = d_up[part]
                weighteds[act, at] = weighted[part]
            return inner_sum + jnp.sum(hidden * back, axis=1, keepdims=True)

        start = jnp.zeros((x.shape[0], 1), F32)
        inner_sum = lax.fori_loop(0, gate_w.shape[1] // tile, tile_step, start)
        for position, which in enumerate(pairs[pair]):
            part = slice(position * rows, (position + 1) * rows)
            inner[here.rows[which], place, 0:1] = line_of(inner_sum[part])

    def second_products(step, pair):
        place = order[step]
        ats = [act_rows(which, place) for which in pairs[pair]]

        @pl.loop(0, width // tile)
        def _(index):
            at = pl.ds(pl.multiple_of(index * tile, tile), tile)

            def both(act):
                return jnp.concatenate([act[part] for part in ats])

            out_buf[pair, :, at] = matmul(both(weighteds), down_w[:, at]).astype(BF16)
            d_x = contract_cols(both(d_gates), gate_w[at]) + contract_cols(both(d_ups), up_w[at])
            d_x = d_x.astype(BF16)
            for position, which in enumerate(pairs[pair]):
                part = slice(position * rows, (position + 1) * rows)
                collect.mine[which, place, :, at] = d_x[part]

    for index in (1, 2):
        spread_x.step(index)
        spread_m.step(index)
    for keep in keeps:
        keep.wait()
    for copy in loads(0, 0):
        copy.start()
    for swap in swaps:
        swap.wait_recv()
    for step in range(4):
        for copy in loads(step, 0):
            copy.wait()
        for copy in loads(step, 1):
            copy.start()
        first_products(step, 0)
        if step < 3:
            spread_x.step(step + 3)
        if step > 0:
            for copy in stores(step - 1, 0):
                copy.wait()
        second_products(step, 0)
        for copy in stores(step, 0):
            copy.start()
        collect.start_far(order[step])
        if step > 0:
            collect.corner_step(order[step - 1])
        for copy in loads(step, 1):
            copy.wait()
        first_products(step, 1)
        if step < 3:
            spread_m.step(step + 3)
            for copy in loads(step + 1, 0):
                copy.start()
        if step > 0:
            for copy in stores(step - 1, 1):
                copy.wait()
        second_products(step, 1)
        for copy in stores(step, 1):
            copy.start()
        collect.start_near(order[step])
        if step > 0:
            collect.plane_step(order[step - 1])

    acts = (d_gates, d_ups, weighteds)
    theirs = (their_gate, their_up, their_down)
    results = (grad_gate, grad_up, grad_down)
    tiles = width // tile

    def tile_at(index):
        return pl.ds(pl.multiple_of(index * tile, tile), tile)

    def tile_of(arrays, kind, index):
        return arrays[kind].at[tile_at(index)] if kind < 2 else arrays[kind].at[:, tile_at(index)]

    def slot_of(pair, kind, slot):
        return pair[0].at[slot, kind] if kind < 2 else pair[1].at[slot]

    def tile_load(source, index, slot):
        return pltpu.make_async_copy(
            source.at[:, :, :, tile_at(index)], tile_buf.at[slot], tile_sem.at[slot]
        )

    def give(kind, index, slot):
        sems = give_send.at[slot, kind], give_recv.at[kind, index]
        source = slot_of((give_buf, give_down), kind, slot)
        return remote(source, tile_of(theirs, kind, index), *sems, here.other_core())

    def their_load(kind, index, slot):
        return pltpu.make_async_copy(
            tile_of(theirs, kind, index),
            slot_of((their_buf, their_down_buf), kind, slot),
            their_sem.at[slot, kind],
        )

    def sum_store(kind, index, slot):
        return pltpu.make_async_copy(
            slot_of((sum_buf, sum_down), kind, slot),
            tile_of(results, kind, index),
            sum_sem.at[slot, kind],
        )

    def product_of(kind, turned, part):
        product = matmul(turned, acts[kind][:, part])
        return product if kind < 2 else product.T

    def give_gradients(source, kinds):
        tile_load(source, 0, 0).start()

        @pl.loop(0, tiles)
        def _(index):
            slot = index % 2

            @pl.when(index + 1 < tiles)
            def _():
                tile_load(source, index + 1, 1 - slot).start()

            tile_load(source, index, slot).wait()
            turned = tile_buf[slot].reshape(-1, tile).T
            for kind in kinds:
                product = product_of(kind, turned, other_half)

                @pl.when(index >= 2)
                def _():
                    give(kind, index - 2, slot).wait_send()

                slot_of((give_buf, give_down), kind, slot)[...] = product.astype(BF16)
                give(kind, index, slot).start()

    def keep_gradients(source, kinds):
        tile_load(source, 0, 0).start()
        for kind in kinds:
            give(kind, 0, 0).wait_recv()
            their_load(kind, 0, 0).start()

        @pl.loop(0, tiles)
        def _(index):
            slot = index % 2

            @pl.when(index + 1 < tiles)
            def _():
                tile_load(source, index + 1, 1 - slot).start()
                for kind in kinds:
                    give(kind, index + 1, 1 - slot).wait_recv()
                    their_load(kind, index + 1, 1 - slot).start()

            tile_load(source, index, slot).wait()
            turned = tile_buf[slot].reshape(-1, tile).T
            for kind in kinds:
                product = product_of(kind, turned, own_half)
                their_load(kind, index, slot).wait()

                @pl.when(index >= 2)
                def _():
                    sum_store(kind, index - 2, slot).wait()

                term = slot_of((their_buf, their_down_buf), kind, slot)[...].astype(F32)
                slot_of((sum_buf, sum_down), kind, slot)[...] = product + term
                sum_store(kind, index, slot).start()

    def give_inner(index):
        step = index + 1
        to_row, to_col = (row + step // 4) % 4, (col + step) % 4
        return remote(
            inner.at[to_row, to_col],
            inner_in.at[row, col],
            inner_send.at[index],
            inner_recv.at[row, col],
            (to_row, to_col, core),
        )

    for index in range(15):
        give_inner(index).start()
    inner_in[row, col] = inner[row, col]
    collect.line_step(1)
    collect.line_step(2)
    give_gradients(rows_all, (0, 1))
    collect.corner_step(order[3])
    give_gradients(grads_all, (2,))
    collect.plane_step(order[3])
    collect.line_step(0)
    collect.line_step(3)
    keep_gradients(rows_all, (0, 1))
    keep_gradients(grads_all, (2,))
    collect.own_step()
    total[...] = collect.mine[0, col]

    for index in range(15):
        give_inner(index).wait_send()
        step = index + 1
        from_row, from_col = (row + 4 - step // 4) % 4, (col + 4 - step % 4) % 4
        arrived(inner_in.at[from_row, from_col], inner_recv.at[from_row, from_col])
    for kind in range(3):
        for slot in range(2):
            give(kind, tiles - 2 + slot, slot).wait_send()
            sum_store(kind, tiles - 2 + slot, slot).wait()
    for pair in range(2):
        for copy in stores(3, pair):
            copy.wait()
    for swap in swaps:
        swap.wait_send()
    spread_x.finish()
    spread_m.finish()
    collect.finish()


def expert_stage(normed, grads_all, mask, gate_half, up_half, down_half, router, collective_id):
    rows, width = normed.shape
    half = gate_half.shape[1]
    expert_count = router.shape[1]
    router = jnp.pad(router, ((0, 0), (0, 128 - expert_count)))
    tokens = 16 * rows
    tile = 256
    vmem = pl.BlockSpec(memory_space=pltpu.VMEM)
    hbm = pl.BlockSpec(memory_space=pl.ANY)
    dma = pltpu.SemaphoreType.DMA
    blocks = jax.ShapeDtypeStruct((4, 4, rows, width), BF16)
    got = pl.pallas_call(
        functools.partial(expert_kernel, expert_count),
        in_specs=[hbm] * 6 + [vmem],
        out_specs=[hbm] * 2 + [vmem] * 2 + [hbm] * 6,
        out_shape=[
            blocks,
            blocks,
            jax.ShapeDtypeStruct((rows, width), BF16),
            jax.ShapeDtypeStruct((4, 4, 8, rows), F32),
            jax.ShapeDtypeStruct((width, half), F32),
            jax.ShapeDtypeStruct((width, half), F32),
            jax.ShapeDtypeStruct((half, width), F32),
            jax.ShapeDtypeStruct((width, half), BF16),
            jax.ShapeDtypeStruct((width, half), BF16),
            jax.ShapeDtypeStruct((half, width), BF16),
        ],
        scratch_shapes=[
            pltpu.VMEM((width, 2 * half), BF16),
            pltpu.VMEM((width, 2 * half), BF16),
            pltpu.VMEM((2 * half, width), BF16),
            pltpu.VMEM((4, 4) + mask.shape, F32),
            pltpu.VMEM((2, 2 * rows, width), BF16),
            pltpu.VMEM((2, 2 * rows, width), BF16),
            pltpu.VMEM((tokens, 2 * half), BF16),
            pltpu.VMEM((tokens, 2 * half), BF16),
            pltpu.VMEM((tokens, 2 * half), BF16),
            pltpu.VMEM((2, 2 * rows, width), BF16),
            pltpu.VMEM((4, 4, 8, rows), F32),
            pltpu.VMEM((2, 4, 4, rows, tile), BF16),
            pltpu.VMEM((2, 2, tile, half), BF16),
            pltpu.VMEM((2, half, tile), BF16),
            pltpu.VMEM((2, 2, tile, half), BF16),
            pltpu.VMEM((2, half, tile), BF16),
            pltpu.VMEM((2, 2, tile, half), F32),
            pltpu.VMEM((2, half, tile), F32),
        ]
        + collect_buffers(rows, width)
        + COLLECT_SEMS
        + [
            dma((3,)), dma((3,)), dma((3,)), dma((3,)), dma((2, 2, 2)), dma((2, 2)),
            dma((2,)), dma((2, 3)), dma((3, width // tile)), dma((2, 3)), dma((2, 3)),
            dma((15,)), dma((4, 4)),
        ]
        + SPREAD_SEMS * 2,
        compiler_params=pltpu.CompilerParams(
            collective_id=collective_id, has_side_effects=True, vmem_limit_bytes=61 * 2**20
        ),
        cost_estimate=pl.CostEstimate(
            flops=18 * 2 * tokens * width * half,
            bytes_accessed=2**26,
            transcendentals=2 * tokens * half,
        ),
    )(normed, grads_all, mask, gate_half, up_half, down_half, router)
    return got[1], got[2], got[3], got[4:7]


def project_kernel(
    hidden, gain, weights, out_weights, q_gain, k_gain, cosine, sine,
    normed, all_weights, all_out, qkv, totals, query, keys, values,
    heads, stat, scale_q, scale_k, kept_sem, kept_out_sem, kept_kv_sem,
    stat_send, stat_recv, head_send, head_recv, pair_send, pair_recv, *sems,
):
    here = Here()
    row, col, core = here.row, here.col, here.core
    count = len(SPREAD_SEMS)
    rows, width = hidden.shape
    depth = weights.shape[0]
    part, side = depth // 2, out_weights.shape[0]

    def weight_block(of_row, unused_place, of_core):
        return all_weights.at[pl.ds(pl.multiple_of(of_row * depth + of_core * part, part), part)]

    def out_block(of_row, place, of_core):
        start = pl.multiple_of(place * side + of_core * (side // 2), side // 2)
        return all_out.at[pl.ds(start, side // 2), pl.ds(pl.multiple_of(of_row * side, side), side)]

    def normed_block(unused_row, place, unused_core):
        return normed.at[pl.ds(pl.multiple_of(place * rows, rows), rows)]

    own_weight = weights.at[pl.ds(pl.multiple_of(core * part, part), part)]
    own_out = out_weights.at[pl.ds(pl.multiple_of(core * (side // 2), side // 2), side // 2)]
    spread_w = Spread(here, own_weight, weight_block, part, sems[:count], line=False)
    spread_n = Spread(
        here, normed_block(row, col, core), normed_block, rows, sems[count : 2 * count], plane=False
    )
    spread_o = Spread(here, own_out, out_block, side // 2, sems[2 * count :])
    greet(here.plane_peers() + here.line_peers() + [here.other_core()])
    spread_w.step(0)
    keep = pltpu.make_async_copy(own_weight, weight_block(row, 0, core), kept_sem)
    keep.start()
    keep_out = pltpu.make_async_copy(own_out, out_block(row, col, core), kept_out_sem)
    keep_out.start()

    values_in = hidden[...].astype(F32)
    scale_one = lax.rsqrt(jnp.mean(values_in * values_in, axis=1, keepdims=True) + EPSILON)
    own_rows = pl.ds(pl.multiple_of(col * rows, rows), rows)
    normed[own_rows] = (values_in * scale_one * gain[...].astype(F32)).astype(BF16)
    spread_n.step(0)
    spread_o.step(0)
    spread_w.step(1)
    spread_n.step(1)
    spread_w.step(2)
    spread_n.step(2)
    spread_n.step(3)
    keep.wait()
    for which in range(4):
        spread_w.core_arrived(which, 0)

    columns = 256

    @pl.loop(0, qkv.shape[1] // columns)
    def _(index):
        at = pl.ds(pl.multiple_of(index * columns, columns), columns)
        qkv[:, at] = matmul(normed[...], all_weights[:, at])

    plane = qkv.shape[1] // (3 * HD)
    for kind in range(2):
        square = jnp.zeros((qkv.shape[0], HD), F32)
        for head in range(plane):
            start = (head * 3 + kind) * HD
            raw = qkv[:, start : start + HD]
            square = square + raw * raw
        stat[col, kind : kind + 1] = jnp.sum(square.T, axis=0, keepdims=True)

    def give_stat(step):
        peer = here.line_peers()[step]
        return remote(stat.at[col], stat.at[col], stat_send.at[step], stat_recv.at[col], peer)

    for step in range(3):
        give_stat(step).start()
    spread_o.step(1)
    for step in range(3):
        place = (col + step + 1) % 4
        arrived(stat.at[place], stat_recv.at[place])
    total = stat[0] + stat[1] + stat[2] + stat[3]
    totals[...] = total
    for kind, target in enumerate((scale_q, scale_k)):
        line = lax.rsqrt(total[kind : kind + 1] / width + EPSILON)
        target[...] = jnp.broadcast_to(line, (HD, line.shape[1])).T

    chunk = 64

    @pl.loop(0, qkv.shape[0] // chunk)
    def _(index):
        at = pl.ds(pl.multiple_of(index * chunk, chunk), chunk)
        for head in range(plane):
            for kind, (scales, gains) in enumerate(((scale_q, q_gain), (scale_k, k_gain))):
                raw = qkv[at, pl.ds((head * 3 + kind) * HD, HD)]
                unit = raw * scales[at] * gains[:, head * HD : (head + 1) * HD]
                turned = pltpu.roll(unit, HD // 2, 1)
                heads[head, kind, at] = (unit * cosine[at] + turned * sine[at]).astype(BF16)
            heads[head, 2, at] = qkv[at, pl.ds((head * 3 + 2) * HD, HD)].astype(BF16)

    targets = (query.at[row], keys.at[1, row], values.at[1, row])

    def give_head(step, kind):
        dest = here.rows[step + 1]
        sems = head_send.at[step, kind], head_recv.at[kind, row]
        return remote(heads.at[dest, kind], targets[kind], *sems, here.at_row(dest))

    for kind in (1, 2, 0):
        for step in range(3):
            give_head(step, kind).start()

    def give_pair(source, kind):
        array = (keys, values)[kind]
        sems = pair_send.at[kind, source], pair_recv.at[kind, source]
        return remote(array.at[1, source], array.at[0, source], *sems, here.other_core())

    def keep_pair(source, kind):
        array = (keys, values)[kind]
        return pltpu.make_async_copy(
            array.at[1, source], array.at[0, source], kept_kv_sem.at[kind, source]
        )

    def pair_from(source):
        @pl.when(core == 0)
        def _():
            for kind in range(2):
                give_pair(source, kind).start()
                keep_pair(source, kind).start()

    for kind, array in ((1, keys), (2, values)):
        array[1, row] = heads[row, kind]
    query[row] = heads[row, 0]
    pair_from(row)
    spread_o.step(2)
    for source in here.rows[1:]:
        arrived(keys.at[1, source], head_recv.at[1, source])
        arrived(values.at[1, source], head_recv.at[2, source])
        pair_from(source)
    spread_o.step(3)
    for source in here.rows[1:]:
        arrived(query.at[source], head_recv.at[0, source])
    spread_o.step(4)
    spread_o.step(5)

    @pl.when(core == 0)
    def _():
        for source in range(4):
            for kind in range(2):
                give_pair(source, kind).wait_send()
                keep_pair(source, kind).wait()

    @pl.when(core == 1)
    def _():
        for source in range(4):
            for kind in range(2):
                give_pair(source, kind).wait_recv()

    for step in range(3):
        give_stat(step).wait_send()
        for kind in range(3):
            give_head(step, kind).wait_send()
    keep_out.wait()
    spread_w.finish(arrivals=False)
    spread_n.finish()
    spread_o.finish()


def project(hidden, gain, weights, out_weights, q_gain, k_gain, cosine, sine, collective_id):
    rows, width = hidden.shape
    depth, columns = weights.shape
    row_tok = 4 * rows
    plane = columns // (3 * HD)
    vmem = pl.BlockSpec(memory_space=pltpu.VMEM)
    hbm = pl.BlockSpec(memory_space=pl.ANY)
    return pl.pallas_call(
        project_kernel,
        in_specs=[vmem, vmem, hbm, hbm, vmem, vmem, vmem, vmem],
        out_specs=[vmem, vmem, hbm, vmem, vmem, vmem, vmem, vmem],
        out_shape=[
            jax.ShapeDtypeStruct((row_tok, width), BF16),
            jax.ShapeDtypeStruct((4 * depth, columns), BF16),
            jax.ShapeDtypeStruct((width, width), BF16),
            jax.ShapeDtypeStruct((row_tok, columns), F32),
            jax.ShapeDtypeStruct((8, row_tok), F32),
            jax.ShapeDtypeStruct((4, row_tok, HD), BF16),
            jax.ShapeDtypeStruct((2, 4, row_tok, HD), BF16),
            jax.ShapeDtypeStruct((2, 4, row_tok, HD), BF16),
        ],
        scratch_shapes=[
            pltpu.VMEM((plane, 3, row_tok, HD), BF16),
            pltpu.VMEM((4, 8, row_tok), F32),
            pltpu.VMEM((row_tok, HD), F32),
            pltpu.VMEM((row_tok, HD), F32),
            pltpu.SemaphoreType.DMA,
            pltpu.SemaphoreType.DMA,
            pltpu.SemaphoreType.DMA((2, 4)),
            pltpu.SemaphoreType.DMA((3,)),
            pltpu.SemaphoreType.DMA((4,)),
            pltpu.SemaphoreType.DMA((3, 3)),
            pltpu.SemaphoreType.DMA((3, 4)),
            pltpu.SemaphoreType.DMA((2, 4)),
            pltpu.SemaphoreType.DMA((2, 4)),
        ]
        + SPREAD_SEMS * 3,
        compiler_params=pltpu.CompilerParams(
            collective_id=collective_id, has_side_effects=True, vmem_limit_bytes=56 * 2**20
        ),
    )(hidden, gain[None], weights, out_weights, q_gain, k_gain, cosine, sine)


def tail_kernel(
    d_qkv, weights, normed, mixed, d_attn,
    d_normed, grads,
    line, line_in, whole, give, other, plane, corner_one, corner_two, from_across, from_along,
    up_send, down_send, line_recv, other_send, other_recv,
    one_send, one_recv, two_send, two_recv, across_send, across_recv, along_send, along_recv,
    back_send, back_recv,
):
    here = Here()
    row, col, core = here.row, here.col, here.core
    rows = d_normed.shape[0]
    depth, columns = grads.shape
    part = depth // 2
    first, second = pl.ds(0, part // 2), pl.ds(part // 2, part // 2)
    order = here.near_first[::-1]
    qkv_columns = d_qkv.shape[1]
    tile = 512

    def line_rows(place):
        return pl.ds(pl.multiple_of(place * rows, rows), rows)

    def line_product(place):
        gradient = d_qkv[line_rows(place)]

        @pl.loop(0, weights.shape[0] // tile)
        def _(index):
            at = pl.ds(pl.multiple_of(index * tile, tile), tile)
            line[place, :, at] = contract_cols(gradient, weights[at]).astype(BF16)

    def give_up(place):
        sems = up_send.at[place], line_recv.at[place]
        return remote(line.at[place], line_in.at[place], *sems, here.at_col(col + 1))

    def give_down(place, slot):
        sems = down_send.at[place], line_recv.at[slot]
        return remote(line.at[place], line_in.at[slot], *sems, here.at_col(col - 1))

    def line_step(place):
        @pl.when((place > col) & (col > 0))
        def _():
            give_up(place).wait_recv()
            add_into(line.at[place], line_in.at[place])

        @pl.when((place < col) & (col < 3))
        def _():
            give_down(place, place).wait_recv()
            add_into(line.at[place], line_in.at[place])

        @pl.when(place > col)
        def _():
            give_up(place).start()

        @pl.when(place < col - 1)
        def _():
            give_down(place, place).start()

        @pl.when(place == col - 1)
        def _():
            give_down(place, 4).start()

    def row_product(which):
        of_row = here.rows[which]
        at = pl.ds(pl.multiple_of(of_row * depth, depth), depth)
        whole[:, pl.ds(0, qkv_columns)] = transposed_product(normed[:, at], d_qkv[...]).astype(BF16)
        whole[:, pl.ds(qkv_columns, columns - qkv_columns)] = transposed_product(
            mixed[...], d_attn[:, at]
        ).astype(BF16)
        plane[which] = whole[pl.ds(pl.multiple_of(core * part, part), part)]
        give[which] = whole[pl.ds(pl.multiple_of((1 - core) * part, part), part)]
        to_core(which).start()

    def to_core(which):
        sems = other_send.at[which], other_recv.at[which]
        return remote(give.at[which], other.at[which], *sems, here.other_core())

    def own_sum(which):
        to_core(which).wait_recv()
        add_into(plane.at[which], other.at[which])

    give_one = remote(
        plane.at[3, first], corner_one, one_send, one_recv, here.at_row(here.across)
    )
    give_two = remote(
        plane.at[3, second], corner_two, two_send, two_recv, here.at_row(here.along)
    )

    def give_across(index):
        at = (first, second)[index]
        sems = across_send.at[index], across_recv.at[index]
        return remote(plane.at[1, at], from_across.at[at], *sems, here.at_row(here.across))

    def give_along(index):
        at = (first, second)[index]
        sems = along_send.at[index], along_recv.at[index]
        return remote(plane.at[2, at], from_along.at[at], *sems, here.at_row(here.along))

    greet(here.plane_peers() + here.line_peers() + [here.other_core()])
    line_product(order[0])
    line_step(order[0])
    row_product(3)
    line_product(order[1])
    line_step(order[1])
    row_product(1)
    own_sum(3)
    give_one.start()
    give_two.start()
    row_product(2)
    own_sum(1)
    give_across(0).start()
    own_sum(2)
    give_along(1).start()
    line_product(order[2])
    line_step(order[2])
    row_product(0)
    line_product(order[3])
    give_two.wait_recv()
    add_into(plane.at[1, second], corner_two)
    give_across(1).start()
    give_one.wait_recv()
    add_into(plane.at[2, first], corner_one)
    give_along(0).start()
    own_sum(0)

    @pl.when(col > 0)
    def _():
        give_up(col).wait_recv()
        add_into(line.at[col], line_in.at[col])

    @pl.when(col < 3)
    def _():
        give_down(col, 4).wait_recv()
        add_into(line.at[col], line_in.at[4])

    d_normed[...] = line[col]
    for index in range(2):
        give_across(index).wait_recv()
        give_along(index).wait_recv()
    add_into(plane.at[0], from_across, from_along)
    own_half = pl.ds(pl.multiple_of(core * part, part), part)
    give_back = remote(
        plane.at[0], grads.at[own_half], back_send, back_recv, here.other_core()
    )
    give_back.start()
    grads[own_half] = plane[0]
    other_half = grads.at[pl.ds(pl.multiple_of((1 - core) * part, part), part)]
    arrived(other_half, back_recv)
    give_back.wait_send()
    give_one.wait_send()
    give_two.wait_send()
    for index in range(2):
        give_across(index).wait_send()
        give_along(index).wait_send()
    for which in range(4):
        to_core(which).wait_send()
    for place in order:

        @pl.when(place > col)
        def _():
            give_up(place).wait_send()

        @pl.when(place < col)
        def _():
            give_down(place, place).wait_send()


def tail(d_qkv, weights, normed, mixed, d_attn, collective_id):
    row_tok, qkv_columns = d_qkv.shape
    width = weights.shape[0]
    rows, depth = row_tok // 4, width // 4
    columns = qkv_columns + d_attn.shape[1] // 4
    part = depth // 2
    vmem = pl.BlockSpec(memory_space=pltpu.VMEM)
    one, four = pltpu.SemaphoreType.DMA, pltpu.SemaphoreType.DMA((4,))
    two, five = pltpu.SemaphoreType.DMA((2,)), pltpu.SemaphoreType.DMA((5,))
    return pl.pallas_call(
        tail_kernel,
        in_specs=[vmem] * 5,
        out_specs=[vmem] * 2,
        out_shape=[
            jax.ShapeDtypeStruct((rows, width), BF16),
            jax.ShapeDtypeStruct((depth, columns), BF16),
        ],
        scratch_shapes=[
            pltpu.VMEM((4, rows, width), BF16),
            pltpu.VMEM((5, rows, width), BF16),
            pltpu.VMEM((depth, columns), BF16),
            pltpu.VMEM((4, part, columns), BF16),
            pltpu.VMEM((4, part, columns), BF16),
            pltpu.VMEM((4, part, columns), BF16),
            pltpu.VMEM((part // 2, columns), BF16),
            pltpu.VMEM((part // 2, columns), BF16),
            pltpu.VMEM((part, columns), BF16),
            pltpu.VMEM((part, columns), BF16),
            four, four, five, four, four,
            one, one, one, one, two, two, two, two,
            one, one,
        ],
        compiler_params=pltpu.CompilerParams(
            collective_id=collective_id, has_side_effects=True, vmem_limit_bytes=56 * 2**20
        ),
    )(d_qkv, weights, normed, mixed, d_attn)


def sum_kernel(values, out, held, got, send, recv):
    here = Here()
    core, col = here.core, here.col
    half = values.shape[0] // 2
    peers = [
        here.at_row(here.across),
        here.at_row(here.along),
        here.at_col(col + 1 - 2 * (col % 2)),
        here.at_col((col + 2) % 4),
    ]
    greet(peers + [here.other_core()])
    own = pl.ds(pl.multiple_of(core * half, half), half)
    others = pl.ds(pl.multiple_of((1 - core) * half, half), half)
    copies = [remote(values.at[others], got.at[0], send.at[0], recv.at[0], here.other_core())]
    copies[0].start()
    copies[0].wait_recv()
    held[0] = values[own] + got[0]
    for step, peer in enumerate(peers):
        copy = remote(held.at[step], got.at[step + 1], send.at[step + 1], recv.at[step + 1], peer)
        copy.start()
        copy.wait_recv()
        held[step + 1] = held[step] + got[step + 1]
        copies.append(copy)
    out[own] = held[4]
    back = remote(held.at[4], out.at[own], send.at[5], recv.at[5], here.other_core())
    back.start()
    arrived(out.at[others], recv.at[5])
    for copy in copies + [back]:
        copy.wait_send()


def sum_everywhere(values, collective_id):
    half = (values.shape[0] // 2, values.shape[1])
    vmem = pl.BlockSpec(memory_space=pltpu.VMEM)
    return pl.pallas_call(
        sum_kernel,
        in_specs=[vmem],
        out_specs=vmem,
        out_shape=jax.ShapeDtypeStruct(values.shape, F32),
        scratch_shapes=[
            pltpu.VMEM((5,) + half, F32),
            pltpu.VMEM((5,) + half, F32),
            pltpu.SemaphoreType.DMA((6,)),
            pltpu.SemaphoreType.DMA((6,)),
        ],
        compiler_params=pltpu.CompilerParams(collective_id=collective_id, has_side_effects=True),
    )(values)


def expert_rows(rows, grads, gate, gate_w, up_w, down_w):
    pre_gate = matmul(rows, gate_w)
    pre_up = matmul(rows, up_w)
    back = contract_cols(grads, down_w)
    sigmoid_gate = jax.nn.sigmoid(pre_gate)
    silu_gate = pre_gate * sigmoid_gate
    hidden = (silu_gate * pre_up).astype(BF16)
    inner = jnp.sum(hidden.astype(F32) * back, axis=-1)
    weighted = (hidden.astype(F32) * gate).astype(BF16)
    d_hid = back * gate
    d_pregate = (d_hid * pre_up * (sigmoid_gate + silu_gate * (1.0 - sigmoid_gate))).astype(BF16)
    d_preup = (d_hid * silu_gate).astype(BF16)
    outputs = matmul(weighted, down_w).astype(BF16)
    d_rows = (contract_cols(d_pregate, gate_w) + contract_cols(d_preup, up_w)).astype(BF16)
    return (
        outputs,
        d_rows,
        inner,
        contract_rows(rows, d_pregate),
        contract_rows(rows, d_preup),
        contract_rows(weighted, grads),
    )


def experts(normed, grads, dense_gates, gate_w, up_w, down_w):
    rows_dev, width = normed.shape
    devices = math.prod(lax.axis_size(axis) for axis in ALL)
    expert_count = dense_gates.shape[1]
    expert = lax.axis_index(ALL) // 2
    parts = max(1, lax.axis_size("exp") // 2)
    step = rows_dev // parts

    def one_part(sums, piece):
        rows, grad_rows, gates = piece
        rows_all = lax.all_gather(rows, ALL, axis=0, tiled=True)
        grads_all = lax.all_gather(grad_rows, ALL, axis=0, tiled=True)
        gates_all = lax.all_gather(gates, ALL, axis=0, tiled=True)
        gate = lax.dynamic_slice_in_dim(gates_all, expert, 1, 1)
        got = expert_rows(rows_all, grads_all, gate, gate_w, up_w, down_w)
        outputs = lax.psum_scatter(got[0], ALL, scatter_dimension=0, tiled=True)
        d_rows = lax.psum_scatter(got[1], ALL, scatter_dimension=0, tiled=True)
        inner = lax.all_to_all(
            got[2].reshape(devices, step), ALL, split_axis=0, concat_axis=0, tiled=True
        )
        inner = inner.reshape(expert_count, 2, step).sum(axis=1).T
        sums = got[3:] if sums is None else tuple(a + b for a, b in zip(sums, got[3:]))
        return sums, (outputs, d_rows, inner)

    if parts == 1:
        sums, (outputs, d_rows, inner) = one_part(None, (normed, grads, dense_gates))
    else:
        start = tuple(jnp.zeros(w.shape, F32) for w in (gate_w, up_w, down_w))
        pieces = tuple(v.reshape(parts, step, -1) for v in (normed, grads, dense_gates))
        sums, got = lax.scan(one_part, start, pieces)
        outputs, d_rows, inner = (v.reshape(rows_dev, -1) for v in got)
    return outputs.astype(F32), d_rows.astype(F32), inner, sums


def experts_here(normed, grads_all, picks, router, gate_w, up_w, down_w):
    numbers = jnp.arange(router.shape[1], dtype=jnp.int32)
    mask = jnp.any(picks.T[None] == numbers[:, None, None], axis=1).astype(F32)
    out_parts, d_rows, inner, weights = expert_stage(
        normed, grads_all, mask, gate_w, up_w, down_w, router, 1
    )
    outputs = reduce_rows(out_parts, 2)
    inner = inner[:, :, 0].reshape(router.shape[1], -1).T
    return outputs.astype(F32), d_rows.astype(F32), inner, weights


def shards(
    hidden_in,
    out_grad,
    attn_gain,
    w_qkv,
    q_gain,
    k_gain,
    w_out,
    moe_gain,
    router,
    w_gate,
    w_up,
    w_down,
    routes,
    doc_cuts,
):
    row_count, col_count = lax.axis_size("row"), lax.axis_size("col")
    tokens = hidden_in[0].astype(F32)
    rows_dev, width = tokens.shape
    heads = w_qkv.shape[1] // (3 * HD)
    plane = heads * HD
    scale = HD ** (-0.5)
    side = lax.axis_index("exp") % 2
    row_tok = rows_dev * col_count
    group_tok = row_tok * row_count
    cuts = lax.dynamic_index_in_dim(doc_cuts, lax.axis_index("exp") // 2, 0, keepdims=False)

    here = (row_count, col_count, lax.axis_size("exp")) == (4, 4, 2)

    if here:
        grads_all = lax.all_gather(out_grad[0], ("row", "col"), axis=0)
        grads_all = grads_all.reshape(row_count, col_count, rows_dev, width)

    gain_one = attn_gain.astype(F32)
    scale_one = rms_scale(tokens)
    head_start = lax.axis_index("col") * plane
    gain_q = lax.dynamic_slice_in_dim(q_gain, head_start, plane, 0).astype(F32)
    gain_k = lax.dynamic_slice_in_dim(k_gain, head_start, plane, 0).astype(F32)
    row_places = side * group_tok + lax.axis_index("row") * row_tok + jnp.arange(row_tok, dtype=jnp.int32)
    unused_doc, position = doc_positions(row_places, cuts)
    cosine, sine = rope_tables(position, HD)
    if here:
        signed = jnp.concatenate([-sine[:, : HD // 2], sine[:, HD // 2 :]], axis=1)
        normed_row, qkv_w, out_w, qkv, totals, query, keys, values = project(
            hidden_in[0], attn_gain, w_qkv, w_out, gain_q[None], gain_k[None], cosine, signed, 0
        )
        total_q, total_k = totals[0], totals[1]
        query = query.reshape(group_tok, HD)
        key_all, value_all = keys.reshape(-1, HD), values.reshape(-1, HD)
    else:
        normed_one = (tokens * scale_one * gain_one).astype(BF16)
        normed_row = lax.all_gather(normed_one, "col", axis=0, tiled=True)
        qkv_w = lax.all_gather(w_qkv, "row", axis=0, tiled=True)
        out_w = lax.all_gather(
            lax.all_gather(w_out, "row", axis=1, tiled=True), "col", axis=0, tiled=True
        )
        qkv = matmul(normed_row, qkv_w)
    qkv = qkv.reshape(row_tok, heads, 3, HD)
    query_raw, key_raw, value_raw = qkv[:, :, 0], qkv[:, :, 1], qkv[:, :, 2]
    if not here:
        total_q, total_k = lax.psum(
            (jnp.sum(query_raw * query_raw, axis=(1, 2)), jnp.sum(key_raw * key_raw, axis=(1, 2))),
            "col",
        )
    scale_q = lax.rsqrt(total_q / width + EPSILON)[:, None, None]
    scale_k = lax.rsqrt(total_k / width + EPSILON)[:, None, None]
    gain_q, gain_k = gain_q.reshape(heads, HD), gain_k.reshape(heads, HD)
    cosine, sine = cosine[:, None, :], sine[:, None, :]
    if not here:
        query = rotate(query_raw * scale_q * gain_q, cosine, sine).astype(BF16)
        key = rotate(key_raw * scale_k * gain_k, cosine, sine).astype(BF16)
        moved = rows_to_heads(jnp.concatenate([query, key, value_raw.astype(BF16)], axis=-1))
        query, own_pair = moved[:, :HD], moved[:, HD:]
        earlier_pair = from_behind(own_pair, "exp", 1)
        lower_pair = jnp.where(side == 0, own_pair, earlier_pair)
        upper_pair = jnp.where(side == 0, jnp.zeros_like(own_pair), own_pair)
        key_value = jnp.concatenate([lower_pair, upper_pair], axis=0)
        key_all, value_all = key_value[:, :HD], key_value[:, HD:]

    mixed_wide, total = attend(query, key_all, value_all, cuts, scale)
    mixed = mixed_wide.astype(BF16)
    mixed_row = heads_to_rows(mixed).reshape(row_tok, plane)
    middle = tokens + matmul(heads_to_tokens(mixed), out_w)

    gain_two = moe_gain.astype(F32)
    scale_two = rms_scale(middle)
    normed_two = (middle * scale_two * gain_two).astype(BF16)
    gates_all = jax.nn.softmax(matmul(normed_two, router), axis=-1)
    picks = routes[0]
    chosen = jnp.any(
        picks[:, :, None] == jnp.arange(router.shape[1], dtype=jnp.int32)[None, None, :], axis=1
    )
    grad_out = out_grad[0].astype(F32)
    expert_w = (w_gate[0], w_up[0], w_down[0])
    if here:
        mixture, d_normed_two, inner, weight_grads = experts_here(
            normed_two, grads_all, picks, router, *expert_w
        )
    else:
        dense_gates = jnp.where(chosen, gates_all, 0.0)
        mixture, d_normed_two, inner, weight_grads = experts(
            normed_two, out_grad[0], dense_gates, *expert_w
        )
    final = middle + mixture
    dense = jnp.where(chosen, inner, 0.0)
    d_logits = (gates_all * (dense - jnp.sum(gates_all * dense, axis=-1, keepdims=True))).astype(BF16)
    grad_router = contract_rows(normed_two, d_logits)
    d_normed_two = d_normed_two + contract_cols(d_logits, router)
    grad_moe_gain = jnp.sum(d_normed_two * middle * scale_two, axis=0)
    weighted_two = d_normed_two * gain_two
    d_middle = (
        grad_out
        + scale_two * weighted_two
        - middle * scale_two**3 * jnp.mean(weighted_two * middle, axis=-1, keepdims=True)
    )

    d_attn = d_middle.astype(BF16)
    d_mixed = tokens_to_heads(contract_cols(d_attn, out_w).astype(BF16))
    d_attn_row = lax.all_gather(d_attn, "col", axis=0, tiled=True)
    d_query, acc_key, acc_value = attend_back(
        query, key_all, value_all, d_mixed, mixed_wide, total, cuts, scale
    )
    accumulated = jnp.concatenate([acc_key, acc_value], axis=1)
    lower_acc, upper_acc = accumulated[:group_tok], accumulated[group_tok:]
    kept_acc = jnp.where(side == 0, lower_acc, upper_acc)
    later_acc = from_behind(lower_acc.astype(BF16), "exp", -1).astype(F32)
    summed_pair = kept_acc + jnp.where(side == 0, later_acc, jnp.zeros_like(later_acc))
    d_heads = heads_to_rows(jnp.concatenate([d_query, summed_pair], axis=1).astype(BF16)).astype(F32)
    d_q_unit = rotate_back(d_heads[:, :, :HD], cosine, sine)
    d_k_unit = rotate_back(d_heads[:, :, HD : 2 * HD], cosine, sine)
    d_value = d_heads[:, :, 2 * HD :]
    weighted_q = d_q_unit * gain_q
    weighted_k = d_k_unit * gain_k
    sum_q, sum_k = lax.psum(
        (jnp.sum(weighted_q * query_raw, axis=(1, 2)), jnp.sum(weighted_k * key_raw, axis=(1, 2))),
        "col",
    )
    d_query_raw = scale_q * weighted_q - query_raw * scale_q**3 * (sum_q / width)[:, None, None]
    d_key_raw = scale_k * weighted_k - key_raw * scale_k**3 * (sum_k / width)[:, None, None]
    grad_q_part = jnp.sum(d_q_unit * query_raw * scale_q, axis=0).reshape(plane)
    grad_k_part = jnp.sum(d_k_unit * key_raw * scale_k, axis=0).reshape(plane)
    d_qkv = jnp.concatenate([d_query_raw, d_key_raw, d_value], axis=2).astype(BF16)
    d_qkv = d_qkv.reshape(row_tok, heads * 3 * HD)
    if here:
        d_normed_one, grads = tail(d_qkv, qkv_w, normed_row, mixed_row, d_attn_row, 5)
        d_normed_one, grads = d_normed_one.astype(F32), grads.astype(F32)
        grad_qkv, grad_w_out = grads[:, : d_qkv.shape[1]], grads[:, d_qkv.shape[1] :]
    else:
        d_normed_one = lax.psum_scatter(
            contract_cols(d_qkv, qkv_w).astype(BF16), "col", scatter_dimension=0, tiled=True
        ).astype(F32)
        grad_qkv = lax.psum_scatter(
            contract_rows(normed_row, d_qkv).astype(BF16), "row", scatter_dimension=0, tiled=True
        )
        grad_w_out = lax.psum_scatter(
            contract_rows(mixed_row, d_attn_row).astype(BF16), "row", scatter_dimension=1, tiled=True
        )
        grad_qkv = lax.psum(grad_qkv, "exp").astype(F32)
        grad_w_out = lax.psum(grad_w_out, "exp").astype(F32)
    grad_attn_gain = jnp.sum(d_normed_one * tokens * scale_one, axis=0)
    weighted_one = d_normed_one * gain_one
    grad_hidden = (
        d_middle
        + scale_one * weighted_one
        - tokens * scale_one**3 * jnp.mean(weighted_one * tokens, axis=-1, keepdims=True)
    )
    empty = jnp.zeros((width,), F32)
    grad_q_full = lax.dynamic_update_slice_in_dim(empty, grad_q_part, head_start, 0)
    grad_k_full = lax.dynamic_update_slice_in_dim(empty, grad_k_part, head_start, 0)
    parts = (grad_attn_gain, grad_q_full, grad_k_full, grad_moe_gain)
    if here:
        packed = jnp.concatenate(parts + (grad_router.T.reshape(-1),)).reshape(-1, 128)
        packed = sum_everywhere(packed, 6).reshape(-1)
        summed = [packed[i * width : (i + 1) * width] for i in range(4)]
        summed.append(packed[4 * width :].reshape(-1, width).T)
    else:
        summed = lax.psum(parts + (grad_router,), ALL)
    return (
        final.astype(BF16)[None],
        grad_hidden[None],
        summed[0],
        grad_qkv,
        summed[1],
        summed[2],
        grad_w_out,
        summed[3],
        summed[4],
        weight_grads[0][None],
        weight_grads[1][None],
        weight_grads[2][None],
    )


def solution(mesh):
    token_spec = P("exp", ("row", "col"), None)
    expert_spec = P(("row", "col", "exp"), None, None)
    in_specs = (
        token_spec,
        token_spec,
        P(),
        P("row", "col"),
        P(),
        P(),
        P("col", "row"),
        P(),
        P(),
        expert_spec,
        expert_spec,
        expert_spec,
        token_spec,
        P(),
    )
    out_specs = (
        token_spec,
        token_spec,
        P(),
        P("row", "col"),
        P(),
        P(),
        P("col", "row"),
        P(),
        P(),
        expert_spec,
        expert_spec,
        expert_spec,
    )
    return jax.shard_map(shards, mesh=mesh, in_specs=in_specs, out_specs=out_specs, check_vma=False)
```

```python
import functools
import math

import jax
import jax.numpy as jnp
from jax import lax
from jax.experimental import pallas as pl
from jax.experimental.pallas import tpu as pltpu
from jax.sharding import PartitionSpec as P

HD = 128
EPSILON = 1e-05
ROPE_BASE = 10000.0
MASKED = -1e30
BF16 = jnp.bfloat16
F32 = jnp.float32


def matmul(left, right):
    return jnp.dot(left, right, preferred_element_type=F32)


def contract_rows(left, right):
    return lax.dot_general(left, right, (((0,), (0,)), ((), ())), preferred_element_type=F32)


def contract_cols(left, right):
    return lax.dot_general(left, right, (((1,), (1,)), ((), ())), preferred_element_type=F32)


def rms_scale(values):
    return lax.rsqrt(jnp.mean(values * values, axis=-1, keepdims=True) + EPSILON)


def rope_tables(position, width):
    frequency = ROPE_BASE ** (-jnp.arange(0, width, 2, dtype=F32) / width)
    angle = position.astype(F32)[:, None] * frequency[None, :]
    return (
        jnp.concatenate([jnp.cos(angle)] * 2, axis=-1),
        jnp.concatenate([jnp.sin(angle)] * 2, axis=-1),
    )


def rotate(values, cosine, sine):
    half = values.shape[-1] // 2
    turned = jnp.concatenate([-values[..., half:], values[..., :half]], axis=-1)
    return values * cosine + turned * sine


def rotate_back(values, cosine, sine):
    half = values.shape[-1] // 2
    turned = values * sine
    return values * cosine + jnp.concatenate([turned[..., half:], -turned[..., :half]], axis=-1)


def doc_positions(places, cuts):
    first = (places >= cuts[0]).astype(jnp.int32)
    second = (places >= cuts[1]).astype(jnp.int32)
    start = first * cuts[0] + second * (cuts[1] - cuts[0])
    return (first + second, places - start)


def from_behind(value, axis, steps):
    count = lax.axis_size(axis)
    initial, last = (max(0, -steps), min(count, count - steps))
    return lax.ppermute(value, axis, [(source, source + steps) for source in range(initial, last)])


def rows_to_heads(values):
    count = lax.axis_size("row")
    rows, heads, width = values.shape
    moved = lax.all_to_all(values.transpose(1, 0, 2), "row", split_axis=0, concat_axis=0, tiled=True)
    return moved.reshape(count * rows, width)


def heads_to_rows(values):
    count = lax.axis_size("row")
    rows, width = values.shape
    moved = lax.all_to_all(
        values.reshape(count, rows // count, width), "row", split_axis=0, concat_axis=0, tiled=True
    )
    return moved.transpose(1, 0, 2)


def heads_to_tokens(values):
    row_count, col_count = lax.axis_size("row"), lax.axis_size("col")
    rows = values.shape[0] // (row_count * col_count)
    moved = lax.all_to_all(
        values.reshape(row_count * col_count, rows, HD),
        ("row", "col"),
        split_axis=0,
        concat_axis=0,
        tiled=True,
    )
    moved = moved.reshape(row_count, col_count, rows, HD).transpose(2, 1, 0, 3)
    return moved.reshape(rows, row_count * col_count * HD)


def tokens_to_heads(values):
    row_count, col_count = lax.axis_size("row"), lax.axis_size("col")
    rows = values.shape[0]
    parted = values.reshape(rows, col_count, row_count, HD).transpose(2, 1, 0, 3)
    moved = lax.all_to_all(
        parted.reshape(row_count * col_count, rows, HD),
        ("row", "col"),
        split_axis=0,
        concat_axis=0,
        tiled=True,
    )
    return moved.reshape(row_count * col_count * rows, HD)


MESH = pl.DeviceIdType.MESH
ALL = ("row", "col", "exp")


class Here:
    def __init__(self):
        self.row, self.col, self.core = (lax.axis_index(axis) for axis in ALL)
        self.across = self.row + 1 - 2 * (self.row % 2)
        self.along = (self.row + 2) % 4
        self.opposite = 3 - self.row
        self.rows = (self.row, self.across, self.along, self.opposite)
        half = self.col // 2
        self.near_first = [
            self.col,
            1 + self.col % 2,
            2 - self.col - self.col % 2 + 3 * half,
            3 - 3 * half,
        ]

    def at_row(self, row):
        return (row, self.col, self.core)

    def at_col(self, col):
        return (self.row, col, self.core)

    def other_core(self):
        return (self.row, self.col, 1 - self.core)

    def line_peers(self):
        return [self.at_col((self.col + step) % 4) for step in (1, 2, 3)]

    def group_peers(self):
        steps = range(1, 16)
        return [((self.row + s // 4) % 4, (self.col + s) % 4, self.core) for s in steps]

    def plane_peers(self):
        return [self.at_row(row) for row in self.rows[1:]]


def greet(peers):
    barrier = pltpu.get_barrier_semaphore()
    for peer in peers:
        pl.semaphore_signal(barrier, inc=1, device_id=peer, device_id_type=MESH)
    pl.semaphore_wait(barrier, len(peers))


def greet_near(here):
    barrier = pltpu.get_barrier_semaphore()
    col = here.col

    def signal(peer):
        pl.semaphore_signal(barrier, inc=1, device_id=peer, device_id_type=MESH)

    for peer in (here.other_core(), here.at_row(here.across), here.at_row(here.along)):
        signal(peer)

    @pl.when(col > 0)
    def _():
        signal(here.at_col(col - 1))

    @pl.when(col < 3)
    def _():
        signal(here.at_col(col + 1))

    pl.semaphore_wait(barrier, 3 + (col + 3) // 4 + (6 - col) // 4)


def remote(source, target, send, recv, device):
    return pltpu.make_async_remote_copy(
        src_ref=source,
        dst_ref=target,
        send_sem=send,
        recv_sem=recv,
        device_id=device,
        device_id_type=MESH,
    )


def arrived(target, recv):
    pltpu.make_async_copy(target, target, recv).wait()


def add_into(target, *terms):
    step = 16

    @pl.loop(0, target.shape[0] // step)
    def _(index):
        part = pl.ds(pl.multiple_of(index * step, step), step)
        value = target[part].astype(F32)
        for term in terms:
            value = value + term[part].astype(F32)
        target[part] = value.astype(target.dtype)


SPREAD_SEMS = [pltpu.SemaphoreType.DMA((4,))] * 11 + [pltpu.SemaphoreType.DMA((4, 4))] * 2


class Spread:
    def __init__(self, here, own, block, rows, sems, line=True, plane=True, core=True):
        self.here, self.own, self.block = here, own, block
        self.line, self.plane, self.core = line, plane, core
        (
            self.up_send, self.down_send, self.line_recv,
            self.across_send, self.across_recv, self.along_send, self.along_recv,
            self.one_send, self.one_recv, self.two_send, self.two_recv,
            self.core_send, self.core_recv,
        ) = sems
        self.first, self.second = pl.ds(0, rows // 2), pl.ds(rows // 2, rows // 2)
        self.order = here.near_first if line else [0]
        self.steps = len(self.order)

    def held(self, step):
        here = self.here
        return self.own if step == 0 else self.block(here.row, self.order[step], here.core)

    def up(self, step):
        here, place = self.here, self.order[step]
        target = self.block(here.row, place, here.core)
        recv = self.line_recv.at[place]
        return remote(self.held(step), target, self.up_send.at[place], recv, here.at_col(here.col + 1))

    def down(self, step):
        here, place = self.here, self.order[step]
        target = self.block(here.row, place, here.core)
        recv = self.line_recv.at[place]
        return remote(self.held(step), target, self.down_send.at[place], recv, here.at_col(here.col - 1))

    def to_across(self, step):
        here, place = self.here, self.order[step]
        target = self.block(here.row, place, here.core)
        sems = self.across_send.at[place], self.across_recv.at[place]
        return remote(self.held(step), target, *sems, here.at_row(here.across))

    def to_along(self, step):
        here, place = self.here, self.order[step]
        target = self.block(here.row, place, here.core)
        sems = self.along_send.at[place], self.along_recv.at[place]
        return remote(self.held(step), target, *sems, here.at_row(here.along))

    def corner_one(self, step):
        here, place = self.here, self.order[step]
        part = self.block(here.across, place, here.core).at[self.first]
        sems = self.one_send.at[place], self.one_recv.at[place]
        return remote(part, part, *sems, here.at_row(here.along))

    def corner_two(self, step):
        here, place = self.here, self.order[step]
        part = self.block(here.along, place, here.core).at[self.second]
        sems = self.two_send.at[place], self.two_recv.at[place]
        return remote(part, part, *sems, here.at_row(here.across))

    def to_core(self, which, step):
        here, place = self.here, self.order[step]
        target = self.block(here.rows[which], place, here.core)
        source = self.held(step) if which == 0 else target
        sems = self.core_send.at[which, place], self.core_recv.at[which, place]
        return remote(source, target, *sems, here.other_core())

    def line_step(self, step):
        here, place = self.here, self.order[step]
        if step > 0:
            arrived(self.held(step), self.line_recv.at[place])
        if self.line:

            @pl.when((place <= here.col) & (here.col < 3))
            def _():
                self.up(step).start()

            @pl.when((place >= here.col) & (here.col > 0))
            def _():
                self.down(step).start()

        if self.plane:
            self.to_across(step).start()
            self.to_along(step).start()
            if self.core:
                self.to_core(0, step).start()

    def plane_step(self, step):
        here, place = self.here, self.order[step]
        arrived(self.block(here.across, place, here.core), self.across_recv.at[place])
        self.corner_one(step).start()
        if self.core:
            self.to_core(1, step).start()
        arrived(self.block(here.along, place, here.core), self.along_recv.at[place])
        self.corner_two(step).start()
        if self.core:
            self.to_core(2, step).start()

    def corner_step(self, step):
        here, place = self.here, self.order[step]
        target = self.block(here.opposite, place, here.core)
        arrived(target.at[self.first], self.one_recv.at[place])
        arrived(target.at[self.second], self.two_recv.at[place])
        if self.core:
            self.to_core(3, step).start()

    def step(self, index):
        if index < self.steps:
            self.line_step(index)
        if self.plane and 0 <= index - 1 < self.steps:
            self.plane_step(index - 1)
        if self.plane and 0 <= index - 2 < self.steps:
            self.corner_step(index - 2)

    def core_arrived(self, which, step):
        here, place = self.here, self.order[step]
        target = self.block(here.rows[which], place, 1 - here.core)
        arrived(target, self.core_recv.at[which, place])

    def finish(self, arrivals=True):
        here = self.here
        for step in range(self.steps):
            place = self.order[step]
            if self.line:

                @pl.when((place <= here.col) & (here.col < 3))
                def _():
                    self.up(step).wait_send()

                @pl.when((place >= here.col) & (here.col > 0))
                def _():
                    self.down(step).wait_send()

            if self.plane:
                self.to_across(step).wait_send()
                self.to_along(step).wait_send()
                self.corner_one(step).wait_send()
                self.corner_two(step).wait_send()
                for which in range(4 if self.core else 0):
                    self.to_core(which, step).wait_send()
                    if arrivals:
                        self.core_arrived(which, step)


COLLECT_SEMS = (
    [pltpu.SemaphoreType.DMA((4,))] * 4
    + [pltpu.SemaphoreType.DMA((2, 4))] * 4
    + [pltpu.SemaphoreType.DMA((4,))] * 2
    + [pltpu.SemaphoreType.DMA((5,))]
)


def collect_buffers(rows, width):
    return [
        pltpu.VMEM((4, 4, rows, width), BF16),
        pltpu.VMEM((4, rows // 2, width), BF16),
        pltpu.VMEM((4, rows // 2, width), BF16),
        pltpu.VMEM((4, rows, width), BF16),
        pltpu.VMEM((4, rows, width), BF16),
        pltpu.VMEM((5, rows, width), BF16),
    ]


class Collect:
    def __init__(self, here, buffers, sems):
        self.here = here
        self.mine, self.one, self.two, self.from_across, self.from_along, self.line = buffers
        (
            self.one_send, self.one_recv, self.two_send, self.two_recv,
            self.across_send, self.across_recv, self.along_send, self.along_recv,
            self.up_send, self.down_send, self.line_recv,
        ) = sems
        half = self.mine.shape[2] // 2
        self.halves = (pl.ds(0, half), pl.ds(half, half))

    def give_one(self, place):
        here = self.here
        return remote(
            self.mine.at[3, place, self.halves[0]], self.one.at[place],
            self.one_send.at[place], self.one_recv.at[place], here.at_row(here.across),
        )

    def give_two(self, place):
        here = self.here
        return remote(
            self.mine.at[3, place, self.halves[1]], self.two.at[place],
            self.two_send.at[place], self.two_recv.at[place], here.at_row(here.along),
        )

    def give_across(self, place, half):
        here, part = self.here, self.halves[half]
        return remote(
            self.mine.at[1, place, part], self.from_across.at[place, part],
            self.across_send.at[half, place], self.across_recv.at[half, place], here.at_row(here.across),
        )

    def give_along(self, place, half):
        here, part = self.here, self.halves[half]
        return remote(
            self.mine.at[2, place, part], self.from_along.at[place, part],
            self.along_send.at[half, place], self.along_recv.at[half, place], here.at_row(here.along),
        )

    def give_up(self, place):
        here = self.here
        sems = self.up_send.at[place], self.line_recv.at[place]
        return remote(self.mine.at[0, place], self.line.at[place], *sems, here.at_col(here.col + 1))

    def give_down(self, place, slot):
        here = self.here
        sems = self.down_send.at[place], self.line_recv.at[slot]
        return remote(self.mine.at[0, place], self.line.at[slot], *sems, here.at_col(here.col - 1))

    def start_far(self, place):
        self.give_one(place).start()
        self.give_two(place).start()
        self.give_along(place, 1).start()

    def start_near(self, place):
        self.give_across(place, 0).start()

    def corner_step(self, place):
        self.give_two(place).wait_recv()
        add_into(self.mine.at[1, place, self.halves[1]], self.two.at[place])
        self.give_across(place, 1).start()
        self.give_one(place).wait_recv()
        add_into(self.mine.at[2, place, self.halves[0]], self.one.at[place])
        self.give_along(place, 0).start()

    def plane_step(self, place):
        for half in range(2):
            self.give_across(place, half).wait_recv()
            self.give_along(place, half).wait_recv()
        add_into(self.mine.at[0, place], self.from_across.at[place], self.from_along.at[place])

    def line_step(self, place):
        col = self.here.col

        @pl.when((place > col) & (col > 0))
        def _():
            self.give_up(place).wait_recv()
            add_into(self.mine.at[0, place], self.line.at[place])

        @pl.when((place < col) & (col < 3))
        def _():
            self.give_down(place, place).wait_recv()
            add_into(self.mine.at[0, place], self.line.at[place])

        @pl.when(place > col)
        def _():
            self.give_up(place).start()

        @pl.when(place < col - 1)
        def _():
            self.give_down(place, place).start()

        @pl.when(place == col - 1)
        def _():
            self.give_down(place, 4).start()

    def own_step(self):
        col = self.here.col

        @pl.when(col > 0)
        def _():
            self.give_up(col).wait_recv()
            add_into(self.mine.at[0, col], self.line.at[col])

        @pl.when(col < 3)
        def _():
            self.give_down(col, 4).wait_recv()
            add_into(self.mine.at[0, col], self.line.at[4])

    def finish(self):
        col = self.here.col
        for place in range(4):
            self.give_one(place).wait_send()
            self.give_two(place).wait_send()
            for half in range(2):
                self.give_across(place, half).wait_send()
                self.give_along(place, half).wait_send()

            @pl.when(place > col)
            def _():
                self.give_up(place).wait_send()

            @pl.when(place < col)
            def _():
                self.give_down(place, place).wait_send()


def reduce_kernel(values, total, *rest):
    here = Here()
    collect = Collect(here, rest[:6], rest[6 : 6 + len(COLLECT_SEMS)])
    load_sem = rest[-1]
    order = here.near_first[::-1]

    def load(which, place):
        return pltpu.make_async_copy(
            values.at[which, place], collect.mine.at[which, place], load_sem.at[which, place]
        )

    for place in order:
        for which in (3, 2, 1, 0):
            load(which, place).start()
    greet_near(here)
    for step in range(6):
        if step < 4:
            place = order[step]
            load(3, place).wait()
            load(2, place).wait()
            collect.start_far(place)
            load(1, place).wait()
            collect.start_near(place)
        if 0 <= step - 1 < 4:
            collect.corner_step(order[step - 1])
        if 0 <= step - 2 < 4:
            place = order[step - 2]
            load(0, place).wait()
            collect.plane_step(place)
            collect.line_step(place)
    collect.own_step()
    total[...] = collect.mine[0, here.col]
    collect.finish()


def reduce_rows(values, collective_id):
    rows, width = values.shape[2:]
    return pl.pallas_call(
        reduce_kernel,
        out_shape=jax.ShapeDtypeStruct((rows, width), BF16),
        in_specs=[pl.BlockSpec(memory_space=pl.ANY)],
        out_specs=pl.BlockSpec(memory_space=pltpu.VMEM),
        scratch_shapes=collect_buffers(rows, width)
        + COLLECT_SEMS
        + [pltpu.SemaphoreType.DMA((4, 4))],
        compiler_params=pltpu.CompilerParams(
            collective_id=collective_id, has_side_effects=True, vmem_limit_bytes=40 * 2**20
        ),
    )(values)


def doc_start(places, cuts):
    return jnp.where(places >= cuts[1], cuts[1], jnp.where(places >= cuts[0], cuts[0], 0))


def key_blocks(cuts, first_query, rows, scores_of, block_fn):
    def scan(index, carry):
        start = pl.multiple_of(index * rows, rows)
        free = (start >= doc_start(first_query + rows - 1, cuts)) & (start + rows <= first_query + 1)

        @pl.when(free)
        def _():
            block_fn(start, scores_of(start))

        @pl.when(jnp.logical_not(free))
        def _():
            key_place = start + lax.broadcasted_iota(jnp.int32, (rows, rows), 0)
            place = first_query + lax.broadcasted_iota(jnp.int32, (1, rows), 1)
            allowed = (key_place <= place) & (key_place >= doc_start(place, cuts))
            block_fn(start, jnp.where(allowed, scores_of(start), MASKED))

        return carry

    lax.fori_loop(doc_start(first_query, cuts) // rows, first_query // rows + 1, scan, 0)


def attend_kernel(scale, group_tok, cuts, query, keys, values_t, mixed, total, top, summed, acc):
    rows = query.shape[0]
    side = lax.axis_index("exp") % 2
    first_query = side * group_tok + pl.program_id(0) * rows
    top[...] = jnp.full_like(top, MASKED)
    summed[...] = jnp.zeros_like(summed)
    acc[...] = jnp.zeros_like(acc)
    cut = (cuts[0, 0], cuts[0, 1])

    def scores_of(start):
        return contract_cols(keys[pl.ds(start, rows)], query[...]) * scale

    def block_fn(start, scores):
        old = top[...]
        new = jnp.maximum(old, jnp.max(scores, axis=0, keepdims=True))
        weights = jnp.exp(scores - new)
        decay = jnp.exp(old - new)
        top[...] = new
        summed[...] = summed[...] * decay + jnp.sum(weights, axis=0, keepdims=True)
        acc[...] = acc[...] * decay + matmul(values_t[:, pl.ds(start, rows)], weights.astype(BF16))

    key_blocks(cut, first_query, rows, scores_of, block_fn)
    mixed[...] = (acc[...] / summed[...]).T
    total[...] = top[...] + jnp.log(summed[...])


def attend(query, keys, values, cuts, scale, rows=512):
    group_tok, head_size = query.shape
    whole = lambda shape: pl.BlockSpec(shape, lambda i: (0, 0))
    return pl.pallas_call(
        functools.partial(attend_kernel, scale, group_tok),
        grid=(group_tok // rows,),
        in_specs=[
            pl.BlockSpec(memory_space=pltpu.SMEM),
            pl.BlockSpec((rows, head_size), lambda i: (i, 0)),
            whole(keys.shape),
            whole(values.shape[::-1]),
        ],
        out_specs=[
            pl.BlockSpec((rows, head_size), lambda i: (i, 0)),
            pl.BlockSpec((1, rows), lambda i: (0, i)),
        ],
        out_shape=[
            jax.ShapeDtypeStruct((group_tok, head_size), F32),
            jax.ShapeDtypeStruct((1, group_tok), F32),
        ],
        scratch_shapes=[
            pltpu.VMEM((1, rows), F32),
            pltpu.VMEM((1, rows), F32),
            pltpu.VMEM((head_size, rows), F32),
        ],
        compiler_params=pltpu.CompilerParams(vmem_limit_bytes=40 * 2**20),
        cost_estimate=pl.CostEstimate(
            flops=4 * 7 * 2**20 * head_size, bytes_accessed=2**23, transcendentals=7 * 2**20
        ),
    )(cuts[None], query, keys, values.T)


def attend_back_kernel(
    scale, group_tok, cuts, query, keys, keys_t, values, d_mixed, total, delta,
    d_query, d_keys, d_values, acc,
):
    rows = query.shape[0]
    side = lax.axis_index("exp") % 2
    first_query = side * group_tok + pl.program_id(0) * rows
    cut = (cuts[0, 0], cuts[0, 1])

    @pl.when(pl.program_id(0) == 0)
    def _():
        d_keys[...] = jnp.zeros_like(d_keys)
        d_values[...] = jnp.zeros_like(d_values)

    acc[...] = jnp.zeros_like(acc)

    def scores_of(start):
        return contract_cols(keys[pl.ds(start, rows)], query[...]) * scale

    def block_fn(start, scores):
        part = pl.ds(start, rows)
        weights = jnp.exp(scores - total[...])
        d_weights = contract_cols(values[part], d_mixed[...])
        d_scores = (weights * (d_weights - delta[...])).astype(BF16)
        d_values[part] += matmul(weights.astype(BF16), d_mixed[...])
        d_keys[part] += matmul(d_scores, query[...]) * scale
        acc[...] += matmul(keys_t[:, part], d_scores)

    key_blocks(cut, first_query, rows, scores_of, block_fn)
    d_query[...] = (acc[...] * scale).T


def attend_back(query, keys, values, d_mixed, mixed, total, cuts, scale, rows=512):
    group_tok, head_size = query.shape
    delta = jnp.sum(d_mixed.astype(F32) * mixed, axis=1)[None]
    whole = lambda shape: pl.BlockSpec(shape, lambda i: (0, 0))
    block = pl.BlockSpec((rows, head_size), lambda i: (i, 0))
    line = pl.BlockSpec((1, rows), lambda i: (0, i))
    return pl.pallas_call(
        functools.partial(attend_back_kernel, scale, group_tok),
        grid=(group_tok // rows,),
        in_specs=[
            pl.BlockSpec(memory_space=pltpu.SMEM),
            block,
            whole(keys.shape),
            whole(keys.shape[::-1]),
            whole(keys.shape),
            block,
            line,
            line,
        ],
        out_specs=[block, whole(keys.shape), whole(keys.shape)],
        out_shape=[
            jax.ShapeDtypeStruct((group_tok, head_size), F32),
            jax.ShapeDtypeStruct(keys.shape, F32),
            jax.ShapeDtypeStruct(keys.shape, F32),
        ],
        scratch_shapes=[pltpu.VMEM((head_size, rows), F32)],
        compiler_params=pltpu.CompilerParams(vmem_limit_bytes=48 * 2**20),
        cost_estimate=pl.CostEstimate(
            flops=10 * 7 * 2**20 * head_size, bytes_accessed=2**23, transcendentals=7 * 2**20
        ),
    )(cuts[None], query, keys, keys.T, values, d_mixed, total, delta)


def transposed_product(left, right):
    return jnp.dot(left.T, right, preferred_element_type=F32)


def column_of(line):
    return jnp.broadcast_to(line, (128, 128)).T[:, :1]


def line_of(column):
    return jnp.broadcast_to(column, (128, 128)).T[:1]


def expert_kernel(
    expert_count, normed, grads_all, mask, gate_half, up_half, down_half, router,
    rows_all, out_parts, total, inner_in, grad_gate, grad_up, grad_down,
    their_gates, their_down,
    gate_w, up_w, down_w, masks, x_buf, d_buf, gates_t, weighteds_t, d_gates, d_ups, weighteds, out_buf,
    inner, sum_buf, sum_down, *rest,
):
    here = Here()
    row, col, core = here.row, here.col, here.core
    rows, width = normed.shape
    half = gate_half.shape[1]
    expert = row * 4 + col
    count = len(SPREAD_SEMS)
    collect = Collect(here, rest[:6], rest[6 : 6 + len(COLLECT_SEMS)])
    rest = rest[6 + len(COLLECT_SEMS) :]
    (
        kept_sem, weight_sem, weight_send, weight_recv, load_sem, store_sem,
        tile_sem, give_send, give_recv, their_sem, sum_sem,
        inner_send, inner_recv,
    ) = rest[:13]
    sems = rest[13:]

    def x_block(of_row, place, unused_core):
        return rows_all.at[pl.ds(pl.multiple_of((of_row * 4 + place) * rows, rows), rows)]

    def d_block(of_row, place, unused_core):
        return grads_all.at[pl.ds(pl.multiple_of((of_row * 4 + place) * rows, rows), rows)]

    def m_block(of_row, place, unused_core):
        return masks.at[of_row, place]

    spread_x = Spread(here, normed, x_block, rows, sems[:count], core=False)
    spread_m = Spread(here, mask, m_block, mask.shape[0], sems[count:], core=False)
    order = here.near_first

    own_half = pl.ds(pl.multiple_of(core * half, half), half)
    other_half = pl.ds(pl.multiple_of((1 - core) * half, half), half)
    halves = (
        (gate_half, gate_w.at[:, own_half], gate_w.at[:, other_half]),
        (up_half, up_w.at[:, own_half], up_w.at[:, other_half]),
        (down_half, down_w.at[own_half], down_w.at[other_half]),
    )
    keeps = [
        pltpu.make_async_copy(source, target, weight_sem.at[index])
        for index, (source, target, unused) in enumerate(halves)
    ] + [
        pltpu.make_async_copy(source, target, kept_sem.at[index])
        for index, (source, target) in enumerate(
            ((normed, x_block(row, col, 0)), (mask, m_block(row, col, 0)))
        )
    ]
    for keep in keeps:
        keep.start()
    greet(here.group_peers() + [here.other_core()])
    swaps = [
        remote(source, target, weight_send.at[index], weight_recv.at[index], here.other_core())
        for index, (source, target, unused) in enumerate(halves)
    ]
    spread_x.step(0)
    spread_m.step(0)
    for swap in swaps:
        swap.start()

    turns = (3, 2, 1, 0)

    def loads(step):
        return [
            pltpu.make_async_copy(
                source(here.rows[which], order[step], 0),
                target.at[pl.ds(position * rows, rows)],
                load_sem.at[position, array],
            )
            for position, which in enumerate(turns)
            for array, (source, target) in enumerate(((x_block, x_buf), (d_block, d_buf)))
        ]

    def stores(step):
        return [
            pltpu.make_async_copy(
                out_buf.at[pl.ds(position * rows, rows)],
                out_parts.at[which, order[step]],
                store_sem.at[position],
            )
            for position, which in enumerate(turns)
        ]

    tile = 256

    def first_products(step):
        place = order[step]
        x = x_buf[...]
        lane = lax.broadcasted_iota(jnp.int32, (x.shape[0], router.shape[1]), 1)
        logits = jnp.where(lane < expert_count, matmul(x, router[...]), MASKED)
        raised = jnp.exp(logits - jnp.max(logits, axis=1, keepdims=True))
        picked = jnp.sum(jnp.where(lane == expert, raised, 0.0), axis=1, keepdims=True)
        routed = jnp.concatenate(
            [column_of(masks[here.rows[which], place, pl.ds(expert, 1)]) for which in turns]
        )
        gate = picked / jnp.sum(raised, axis=1, keepdims=True) * routed
        columns = [
            pl.ds(pl.multiple_of((here.rows[which] * 4 + place) * rows, rows), rows) for which in turns
        ]

        def tile_step(index, inner_sum):
            at = pl.ds(pl.multiple_of(index * tile, tile), tile)
            pre_gate = matmul(x_buf[...], gate_w[:, at])
            pre_up = matmul(x_buf[...], up_w[:, at])
            back = contract_cols(d_buf[...], down_w[at])
            sigmoid_gate = 1.0 / (1.0 + jnp.exp(-pre_gate))
            silu_gate = pre_gate * sigmoid_gate
            hidden = (silu_gate * pre_up).astype(BF16).astype(F32)
            d_hid = back * gate
            d_gate = (d_hid * pre_up * (sigmoid_gate + silu_gate * (1.0 - sigmoid_gate))).astype(BF16)
            d_up = (d_hid * silu_gate).astype(BF16)
            weight = (hidden * gate).astype(BF16)
            d_gates[:, at] = d_gate
            d_ups[:, at] = d_up
            weighteds[:, at] = weight
            side = index // (half // tile)
            first = pl.multiple_of(index % (half // tile) * tile, tile)
            for values, target in (
                (d_gate, gates_t.at[side, pl.ds(first, tile)]),
                (d_up, gates_t.at[side, pl.ds(first + half, tile)]),
                (weight, weighteds_t.at[at]),
            ):
                turned = values.T
                for position, column in enumerate(columns):
                    target[:, column] = turned[:, position * rows : (position + 1) * rows]
            return inner_sum + jnp.sum(hidden * back, axis=1, keepdims=True)

        start = jnp.zeros((x.shape[0], 1), F32)
        inner_sum = lax.fori_loop(0, gate_w.shape[1] // tile, tile_step, start)
        for position, which in enumerate(turns):
            part = slice(position * rows, (position + 1) * rows)
            inner[here.rows[which], place, 0:1] = line_of(inner_sum[part])

    def second_products(step):
        place = order[step]

        @pl.loop(0, width // tile)
        def _(index):
            at = pl.ds(pl.multiple_of(index * tile, tile), tile)
            out_buf[:, at] = matmul(weighteds[...], down_w[:, at]).astype(BF16)
            d_x = contract_cols(d_gates[...], gate_w[at]) + contract_cols(d_ups[...], up_w[at])
            d_x = d_x.astype(BF16)
            for position, which in enumerate(turns):
                collect.mine[which, place, :, at] = d_x[position * rows : (position + 1) * rows]

    for index in (1, 2):
        spread_x.step(index)
        spread_m.step(index)
    for keep in keeps:
        keep.wait()
    for copy in loads(0):
        copy.start()
    for swap in swaps:
        swap.wait_recv()
    for step in range(4):
        for copy in loads(step):
            copy.wait()
        first_products(step)
        if step < 3:
            spread_x.step(step + 3)
            spread_m.step(step + 3)
            for copy in loads(step + 1):
                copy.start()
        if step > 0:
            for copy in stores(step - 1):
                copy.wait()
            collect.corner_step(order[step - 1])
        second_products(step)
        for copy in stores(step):
            copy.start()
        collect.start_far(order[step])
        collect.start_near(order[step])
        if step > 0:
            collect.plane_step(order[step - 1])

    tiles = width // tile

    def tile_at(index):
        return pl.ds(pl.multiple_of(index * tile, tile), tile)

    def acts_of(kind, side):
        if kind == 0:
            return gates_t[side]
        return weighteds_t[pl.ds(pl.multiple_of(side * half, half), half)]

    counts = (2 * half, half)

    def slot_at(slot):
        return pl.ds(pl.multiple_of(slot * tile, tile), tile)

    def tile_buf(slot):
        return gate_w.at[:, slot_at(slot)]

    def give_buf(kind, slot):
        return up_w.at[pl.ds(0, counts[kind]), slot_at(slot)]

    def their_buf(kind, slot):
        return up_w.at[pl.ds(width // 2, counts[kind]), slot_at(slot)]

    theirs = (their_gates, their_down)

    def tile_load(source, index, slot):
        return pltpu.make_async_copy(
            source.at[:, tile_at(index)], tile_buf(slot), tile_sem.at[slot]
        )

    def give(kind, index, slot):
        sems = give_send.at[slot, kind], give_recv.at[kind, index]
        return remote(give_buf(kind, slot), theirs[kind].at[:, tile_at(index)], *sems, here.other_core())

    def their_load(kind, index, slot):
        return pltpu.make_async_copy(
            theirs[kind].at[:, tile_at(index)],
            their_buf(kind, slot),
            their_sem.at[slot, kind],
        )

    def sum_stores(kind, index, slot):
        if kind == 1:
            target = grad_down.at[:, tile_at(index)]
            return [pltpu.make_async_copy(sum_down, target, sum_sem.at[0, 2])]
        return [
            pltpu.make_async_copy(
                sum_buf.at[slot, part], target.at[tile_at(index)], sum_sem.at[slot, part]
            )
            for part, target in enumerate((grad_gate, grad_up))
        ]

    def give_gradients(source, kind):
        tile_load(source, 0, 0).start()

        @pl.loop(0, tiles)
        def _(index):
            slot = index % 2

            @pl.when(index + 1 < tiles)
            def _():
                tile_load(source, index + 1, 1 - slot).start()

            tile_load(source, index, slot).wait()
            product = matmul(acts_of(kind, 1 - core), tile_buf(slot)[...])

            @pl.when(index >= 2)
            def _():
                give(kind, index - 2, slot).wait_send()

            give_buf(kind, slot)[...] = product.astype(BF16)
            give(kind, index, slot).start()

        for slot in range(2):
            give(kind, tiles - 2 + slot, slot).wait_send()

    def keep_gradients(source, kind):
        tile_load(source, 0, 0).start()
        give(kind, 0, 0).wait_recv()
        their_load(kind, 0, 0).start()

        @pl.loop(0, tiles)
        def _(index):
            slot = index % 2

            @pl.when(index + 1 < tiles)
            def _():
                tile_load(source, index + 1, 1 - slot).start()
                give(kind, index + 1, 1 - slot).wait_recv()
                their_load(kind, index + 1, 1 - slot).start()

            tile_load(source, index, slot).wait()
            product = matmul(acts_of(kind, core), tile_buf(slot)[...])
            their_load(kind, index, slot).wait()
            product = product + their_buf(kind, slot)[...].astype(F32)

            held = 2 - kind

            @pl.when(index >= held)
            def _():
                for copy in sum_stores(kind, index - held, slot):
                    copy.wait()

            if kind == 1:
                sum_down[...] = product
            else:
                sum_buf[slot, 0] = product[:half].T
                sum_buf[slot, 1] = product[half:].T
            for copy in sum_stores(kind, index, slot):
                copy.start()

        for slot in range(2 - kind):
            for copy in sum_stores(kind, tiles - 2 + kind + slot, slot):
                copy.wait()

    def give_inner(index):
        step = index + 1
        to_row, to_col = (row + step // 4) % 4, (col + step) % 4
        return remote(
            inner.at[to_row, to_col],
            inner_in.at[row, col],
            inner_send.at[index],
            inner_recv.at[row, col],
            (to_row, to_col, core),
        )

    for index in range(15):
        give_inner(index).start()
    inner_in[row, col] = inner[row, col]
    collect.line_step(1)
    collect.line_step(2)
    give_gradients(rows_all, 0)
    collect.corner_step(order[3])
    give_gradients(grads_all, 1)
    collect.plane_step(order[3])
    collect.line_step(0)
    collect.line_step(3)
    keep_gradients(rows_all, 0)
    keep_gradients(grads_all, 1)
    collect.own_step()
    total[...] = collect.mine[0, col]

    for index in range(15):
        give_inner(index).wait_send()
        step = index + 1
        from_row, from_col = (row + 4 - step // 4) % 4, (col + 4 - step % 4) % 4
        arrived(inner_in.at[from_row, from_col], inner_recv.at[from_row, from_col])
    for copy in stores(3):
        copy.wait()
    for swap in swaps:
        swap.wait_send()
    spread_x.finish()
    spread_m.finish()
    collect.finish()


def expert_stage(normed, grads_all, mask, gate_half, up_half, down_half, router, collective_id):
    rows, width = normed.shape
    half = gate_half.shape[1]
    expert_count = router.shape[1]
    router = jnp.pad(router, ((0, 0), (0, 128 - expert_count)))
    tokens = 16 * rows
    tile = 256
    vmem = pl.BlockSpec(memory_space=pltpu.VMEM)
    hbm = pl.BlockSpec(memory_space=pl.ANY)
    dma = pltpu.SemaphoreType.DMA
    blocks = jax.ShapeDtypeStruct((4, 4, rows, width), BF16)
    got = pl.pallas_call(
        functools.partial(expert_kernel, expert_count),
        in_specs=[hbm] * 6 + [vmem],
        out_specs=[hbm] * 2 + [vmem] * 2 + [hbm] * 5,
        out_shape=[
            jax.ShapeDtypeStruct((tokens, width), BF16),
            blocks,
            jax.ShapeDtypeStruct((rows, width), BF16),
            jax.ShapeDtypeStruct((4, 4, 8, rows), F32),
            jax.ShapeDtypeStruct((width, half), F32),
            jax.ShapeDtypeStruct((width, half), F32),
            jax.ShapeDtypeStruct((half, width), F32),
            jax.ShapeDtypeStruct((2 * half, width), BF16),
            jax.ShapeDtypeStruct((half, width), BF16),
        ],
        scratch_shapes=[
            pltpu.VMEM((width, 2 * half), BF16),
            pltpu.VMEM((width, 2 * half), BF16),
            pltpu.VMEM((2 * half, width), BF16),
            pltpu.VMEM((4, 4) + mask.shape, F32),
            pltpu.VMEM((4 * rows, width), BF16),
            pltpu.VMEM((4 * rows, width), BF16),
            pltpu.VMEM((2, 2 * half, tokens), BF16),
            pltpu.VMEM((2 * half, tokens), BF16),
            pltpu.VMEM((4 * rows, 2 * half), BF16),
            pltpu.VMEM((4 * rows, 2 * half), BF16),
            pltpu.VMEM((4 * rows, 2 * half), BF16),
            pltpu.VMEM((4 * rows, width), BF16),
            pltpu.VMEM((4, 4, 8, rows), F32),
            pltpu.VMEM((2, 2, tile, half), F32),
            pltpu.VMEM((half, tile), F32),
        ]
        + collect_buffers(rows, width)
        + COLLECT_SEMS
        + [
            dma((3,)), dma((3,)), dma((3,)), dma((3,)), dma((4, 2)), dma((4,)),
            dma((2,)), dma((2, 2)), dma((2, width // tile)), dma((2, 2)), dma((2, 3)),
            dma((15,)), dma((4, 4)),
        ]
        + SPREAD_SEMS * 2,
        compiler_params=pltpu.CompilerParams(
            collective_id=collective_id, has_side_effects=True, vmem_limit_bytes=61 * 2**20
        ),
        cost_estimate=pl.CostEstimate(
            flops=18 * 2 * tokens * width * half,
            bytes_accessed=2**26,
            transcendentals=2 * tokens * half,
        ),
    )(normed, grads_all, mask, gate_half, up_half, down_half, router)
    return got[1], got[2], got[3], got[4:7]


def project_kernel(
    hidden, gain, weights, out_weights, q_gain, k_gain, cosine, sine,
    normed, all_weights, all_out, qkv, totals, query, keys, values,
    heads, stat, scale_q, scale_k, kept_sem, kept_out_sem, kept_kv_sem,
    stat_send, stat_recv, head_send, head_recv, pair_send, pair_recv, *sems,
):
    here = Here()
    row, col, core = here.row, here.col, here.core
    count = len(SPREAD_SEMS)
    rows, width = hidden.shape
    depth = weights.shape[0]
    part, side = depth // 2, out_weights.shape[0]

    def weight_block(of_row, unused_place, of_core):
        return all_weights.at[pl.ds(pl.multiple_of(of_row * depth + of_core * part, part), part)]

    def out_block(of_row, place, of_core):
        start = pl.multiple_of(place * side + of_core * (side // 2), side // 2)
        return all_out.at[pl.ds(start, side // 2), pl.ds(pl.multiple_of(of_row * side, side), side)]

    def normed_block(unused_row, place, unused_core):
        return normed.at[pl.ds(pl.multiple_of(place * rows, rows), rows)]

    own_weight = weights.at[pl.ds(pl.multiple_of(core * part, part), part)]
    own_out = out_weights.at[pl.ds(pl.multiple_of(core * (side // 2), side // 2), side // 2)]
    spread_w = Spread(here, own_weight, weight_block, part, sems[:count], line=False)
    spread_n = Spread(
        here, normed_block(row, col, core), normed_block, rows, sems[count : 2 * count], plane=False
    )
    spread_o = Spread(here, own_out, out_block, side // 2, sems[2 * count :])
    greet(here.plane_peers() + here.line_peers() + [here.other_core()])
    spread_w.step(0)
    keep = pltpu.make_async_copy(own_weight, weight_block(row, 0, core), kept_sem)
    keep.start()
    keep_out = pltpu.make_async_copy(own_out, out_block(row, col, core), kept_out_sem)
    keep_out.start()

    values_in = hidden[...].astype(F32)
    scale_one = lax.rsqrt(jnp.mean(values_in * values_in, axis=1, keepdims=True) + EPSILON)
    own_rows = pl.ds(pl.multiple_of(col * rows, rows), rows)
    normed[own_rows] = (values_in * scale_one * gain[...].astype(F32)).astype(BF16)
    spread_n.step(0)
    spread_o.step(0)
    spread_w.step(1)
    spread_n.step(1)
    spread_w.step(2)
    spread_n.step(2)
    spread_n.step(3)
    keep.wait()
    for which in range(4):
        spread_w.core_arrived(which, 0)

    columns = 256

    @pl.loop(0, qkv.shape[1] // columns)
    def _(index):
        at = pl.ds(pl.multiple_of(index * columns, columns), columns)
        qkv[:, at] = matmul(normed[...], all_weights[:, at])

    plane = qkv.shape[1] // (3 * HD)
    for kind in range(2):
        square = jnp.zeros((qkv.shape[0], HD), F32)
        for head in range(plane):
            start = (head * 3 + kind) * HD
            raw = qkv[:, start : start + HD]
            square = square + raw * raw
        stat[col, kind : kind + 1] = jnp.sum(square.T, axis=0, keepdims=True)

    def give_stat(step):
        peer = here.line_peers()[step]
        return remote(stat.at[col], stat.at[col], stat_send.at[step], stat_recv.at[col], peer)

    for step in range(3):
        give_stat(step).start()
    spread_o.step(1)
    for step in range(3):
        place = (col + step + 1) % 4
        arrived(stat.at[place], stat_recv.at[place])
    total = stat[0] + stat[1] + stat[2] + stat[3]
    totals[...] = total
    for kind, target in enumerate((scale_q, scale_k)):
        line = lax.rsqrt(total[kind : kind + 1] / width + EPSILON)
        target[...] = jnp.broadcast_to(line, (HD, line.shape[1])).T

    chunk = 64

    @pl.loop(0, qkv.shape[0] // chunk)
    def _(index):
        at = pl.ds(pl.multiple_of(index * chunk, chunk), chunk)
        for head in range(plane):
            for kind, (scales, gains) in enumerate(((scale_q, q_gain), (scale_k, k_gain))):
                raw = qkv[at, pl.ds((head * 3 + kind) * HD, HD)]
                unit = raw * scales[at] * gains[:, head * HD : (head + 1) * HD]
                turned = pltpu.roll(unit, HD // 2, 1)
                heads[head, kind, at] = (unit * cosine[at] + turned * sine[at]).astype(BF16)
            heads[head, 2, at] = qkv[at, pl.ds((head * 3 + 2) * HD, HD)].astype(BF16)

    targets = (query.at[row], keys.at[1, row], values.at[1, row])

    def give_head(step, kind):
        dest = here.rows[step + 1]
        sems = head_send.at[step, kind], head_recv.at[kind, row]
        return remote(heads.at[dest, kind], targets[kind], *sems, here.at_row(dest))

    for kind in (1, 2, 0):
        for step in range(3):
            give_head(step, kind).start()

    def give_pair(source, kind):
        array = (keys, values)[kind]
        sems = pair_send.at[kind, source], pair_recv.at[kind, source]
        return remote(array.at[1, source], array.at[0, source], *sems, here.other_core())

    def keep_pair(source, kind):
        array = (keys, values)[kind]
        return pltpu.make_async_copy(
            array.at[1, source], array.at[0, source], kept_kv_sem.at[kind, source]
        )

    def pair_from(source):
        @pl.when(core == 0)
        def _():
            for kind in range(2):
                give_pair(source, kind).start()
                keep_pair(source, kind).start()

    for kind, array in ((1, keys), (2, values)):
        array[1, row] = heads[row, kind]
    query[row] = heads[row, 0]
    pair_from(row)
    spread_o.step(2)
    for source in here.rows[1:]:
        arrived(keys.at[1, source], head_recv.at[1, source])
        arrived(values.at[1, source], head_recv.at[2, source])
        pair_from(source)
    spread_o.step(3)
    for source in here.rows[1:]:
        arrived(query.at[source], head_recv.at[0, source])
    spread_o.step(4)
    spread_o.step(5)

    @pl.when(core == 0)
    def _():
        for source in range(4):
            for kind in range(2):
                give_pair(source, kind).wait_send()
                keep_pair(source, kind).wait()

    @pl.when(core == 1)
    def _():
        for source in range(4):
            for kind in range(2):
                give_pair(source, kind).wait_recv()

    for step in range(3):
        give_stat(step).wait_send()
        for kind in range(3):
            give_head(step, kind).wait_send()
    keep_out.wait()
    spread_w.finish(arrivals=False)
    spread_n.finish()
    spread_o.finish()


def project(hidden, gain, weights, out_weights, q_gain, k_gain, cosine, sine, collective_id):
    rows, width = hidden.shape
    depth, columns = weights.shape
    row_tok = 4 * rows
    plane = columns // (3 * HD)
    vmem = pl.BlockSpec(memory_space=pltpu.VMEM)
    hbm = pl.BlockSpec(memory_space=pl.ANY)
    return pl.pallas_call(
        project_kernel,
        in_specs=[vmem, vmem, hbm, hbm, vmem, vmem, vmem, vmem],
        out_specs=[vmem, vmem, hbm, vmem, vmem, vmem, vmem, vmem],
        out_shape=[
            jax.ShapeDtypeStruct((row_tok, width), BF16),
            jax.ShapeDtypeStruct((4 * depth, columns), BF16),
            jax.ShapeDtypeStruct((width, width), BF16),
            jax.ShapeDtypeStruct((row_tok, columns), F32),
            jax.ShapeDtypeStruct((8, row_tok), F32),
            jax.ShapeDtypeStruct((4, row_tok, HD), BF16),
            jax.ShapeDtypeStruct((2, 4, row_tok, HD), BF16),
            jax.ShapeDtypeStruct((2, 4, row_tok, HD), BF16),
        ],
        scratch_shapes=[
            pltpu.VMEM((plane, 3, row_tok, HD), BF16),
            pltpu.VMEM((4, 8, row_tok), F32),
            pltpu.VMEM((row_tok, HD), F32),
            pltpu.VMEM((row_tok, HD), F32),
            pltpu.SemaphoreType.DMA,
            pltpu.SemaphoreType.DMA,
            pltpu.SemaphoreType.DMA((2, 4)),
            pltpu.SemaphoreType.DMA((3,)),
            pltpu.SemaphoreType.DMA((4,)),
            pltpu.SemaphoreType.DMA((3, 3)),
            pltpu.SemaphoreType.DMA((3, 4)),
            pltpu.SemaphoreType.DMA((2, 4)),
            pltpu.SemaphoreType.DMA((2, 4)),
        ]
        + SPREAD_SEMS * 3,
        compiler_params=pltpu.CompilerParams(
            collective_id=collective_id, has_side_effects=True, vmem_limit_bytes=56 * 2**20
        ),
    )(hidden, gain[None], weights, out_weights, q_gain, k_gain, cosine, sine)


def tail_kernel(
    d_qkv, weights, normed, mixed, d_attn,
    d_normed, grads,
    line, line_in, whole, give, other, plane, corner_one, corner_two, from_across, from_along,
    up_send, down_send, line_recv, other_send, other_recv,
    one_send, one_recv, two_send, two_recv, across_send, across_recv, along_send, along_recv,
    back_send, back_recv,
):
    here = Here()
    row, col, core = here.row, here.col, here.core
    rows = d_normed.shape[0]
    depth, columns = grads.shape
    part = depth // 2
    first, second = pl.ds(0, part // 2), pl.ds(part // 2, part // 2)
    order = here.near_first[::-1]
    qkv_columns = d_qkv.shape[1]
    tile = 512

    def line_rows(place):
        return pl.ds(pl.multiple_of(place * rows, rows), rows)

    def line_product(place):
        gradient = d_qkv[line_rows(place)]

        @pl.loop(0, weights.shape[0] // tile)
        def _(index):
            at = pl.ds(pl.multiple_of(index * tile, tile), tile)
            line[place, :, at] = contract_cols(gradient, weights[at]).astype(BF16)

    def give_up(place):
        sems = up_send.at[place], line_recv.at[place]
        return remote(line.at[place], line_in.at[place], *sems, here.at_col(col + 1))

    def give_down(place, slot):
        sems = down_send.at[place], line_recv.at[slot]
        return remote(line.at[place], line_in.at[slot], *sems, here.at_col(col - 1))

    def line_step(place):
        @pl.when((place > col) & (col > 0))
        def _():
            give_up(place).wait_recv()
            add_into(line.at[place], line_in.at[place])

        @pl.when((place < col) & (col < 3))
        def _():
            give_down(place, place).wait_recv()
            add_into(line.at[place], line_in.at[place])

        @pl.when(place > col)
        def _():
            give_up(place).start()

        @pl.when(place < col - 1)
        def _():
            give_down(place, place).start()

        @pl.when(place == col - 1)
        def _():
            give_down(place, 4).start()

    def row_product(which):
        of_row = here.rows[which]
        at = pl.ds(pl.multiple_of(of_row * depth, depth), depth)
        whole[:, pl.ds(0, qkv_columns)] = transposed_product(normed[:, at], d_qkv[...]).astype(BF16)
        whole[:, pl.ds(qkv_columns, columns - qkv_columns)] = transposed_product(
            mixed[...], d_attn[:, at]
        ).astype(BF16)
        plane[which] = whole[pl.ds(pl.multiple_of(core * part, part), part)]
        give[which] = whole[pl.ds(pl.multiple_of((1 - core) * part, part), part)]
        to_core(which).start()

    def to_core(which):
        sems = other_send.at[which], other_recv.at[which]
        return remote(give.at[which], other.at[which], *sems, here.other_core())

    def own_sum(which):
        to_core(which).wait_recv()
        add_into(plane.at[which], other.at[which])

    give_one = remote(
        plane.at[3, first], corner_one, one_send, one_recv, here.at_row(here.across)
    )
    give_two = remote(
        plane.at[3, second], corner_two, two_send, two_recv, here.at_row(here.along)
    )

    def give_across(index):
        at = (first, second)[index]
        sems = across_send.at[index], across_recv.at[index]
        return remote(plane.at[1, at], from_across.at[at], *sems, here.at_row(here.across))

    def give_along(index):
        at = (first, second)[index]
        sems = along_send.at[index], along_recv.at[index]
        return remote(plane.at[2, at], from_along.at[at], *sems, here.at_row(here.along))

    greet(here.plane_peers() + here.line_peers() + [here.other_core()])
    line_product(order[0])
    line_step(order[0])
    row_product(3)
    line_product(order[1])
    line_step(order[1])
    row_product(1)
    own_sum(3)
    give_one.start()
    give_two.start()
    row_product(2)
    own_sum(1)
    give_across(0).start()
    own_sum(2)
    give_along(1).start()
    line_product(order[2])
    line_step(order[2])
    row_product(0)
    line_product(order[3])
    give_two.wait_recv()
    add_into(plane.at[1, second], corner_two)
    give_across(1).start()
    give_one.wait_recv()
    add_into(plane.at[2, first], corner_one)
    give_along(0).start()
    own_sum(0)

    @pl.when(col > 0)
    def _():
        give_up(col).wait_recv()
        add_into(line.at[col], line_in.at[col])

    @pl.when(col < 3)
    def _():
        give_down(col, 4).wait_recv()
        add_into(line.at[col], line_in.at[4])

    d_normed[...] = line[col]
    for index in range(2):
        give_across(index).wait_recv()
        give_along(index).wait_recv()
    add_into(plane.at[0], from_across, from_along)
    own_half = pl.ds(pl.multiple_of(core * part, part), part)
    give_back = remote(
        plane.at[0], grads.at[own_half], back_send, back_recv, here.other_core()
    )
    give_back.start()
    grads[own_half] = plane[0]
    other_half = grads.at[pl.ds(pl.multiple_of((1 - core) * part, part), part)]
    arrived(other_half, back_recv)
    give_back.wait_send()
    give_one.wait_send()
    give_two.wait_send()
    for index in range(2):
        give_across(index).wait_send()
        give_along(index).wait_send()
    for which in range(4):
        to_core(which).wait_send()
    for place in order:

        @pl.when(place > col)
        def _():
            give_up(place).wait_send()

        @pl.when(place < col)
        def _():
            give_down(place, place).wait_send()


def tail(d_qkv, weights, normed, mixed, d_attn, collective_id):
    row_tok, qkv_columns = d_qkv.shape
    width = weights.shape[0]
    rows, depth = row_tok // 4, width // 4
    columns = qkv_columns + d_attn.shape[1] // 4
    part = depth // 2
    vmem = pl.BlockSpec(memory_space=pltpu.VMEM)
    one, four = pltpu.SemaphoreType.DMA, pltpu.SemaphoreType.DMA((4,))
    two, five = pltpu.SemaphoreType.DMA((2,)), pltpu.SemaphoreType.DMA((5,))
    return pl.pallas_call(
        tail_kernel,
        in_specs=[vmem] * 5,
        out_specs=[vmem] * 2,
        out_shape=[
            jax.ShapeDtypeStruct((rows, width), BF16),
            jax.ShapeDtypeStruct((depth, columns), BF16),
        ],
        scratch_shapes=[
            pltpu.VMEM((4, rows, width), BF16),
            pltpu.VMEM((5, rows, width), BF16),
            pltpu.VMEM((depth, columns), BF16),
            pltpu.VMEM((4, part, columns), BF16),
            pltpu.VMEM((4, part, columns), BF16),
            pltpu.VMEM((4, part, columns), BF16),
            pltpu.VMEM((part // 2, columns), BF16),
            pltpu.VMEM((part // 2, columns), BF16),
            pltpu.VMEM((part, columns), BF16),
            pltpu.VMEM((part, columns), BF16),
            four, four, five, four, four,
            one, one, one, one, two, two, two, two,
            one, one,
        ],
        compiler_params=pltpu.CompilerParams(
            collective_id=collective_id, has_side_effects=True, vmem_limit_bytes=56 * 2**20
        ),
    )(d_qkv, weights, normed, mixed, d_attn)


def sum_kernel(values, out, held, got, send, recv):
    here = Here()
    core, col = here.core, here.col
    half = values.shape[0] // 2
    peers = [
        here.at_row(here.across),
        here.at_row(here.along),
        here.at_col(col + 1 - 2 * (col % 2)),
        here.at_col((col + 2) % 4),
    ]
    greet(peers + [here.other_core()])
    own = pl.ds(pl.multiple_of(core * half, half), half)
    others = pl.ds(pl.multiple_of((1 - core) * half, half), half)
    copies = [remote(values.at[others], got.at[0], send.at[0], recv.at[0], here.other_core())]
    copies[0].start()
    copies[0].wait_recv()
    held[0] = values[own] + got[0]
    for step, peer in enumerate(peers):
        copy = remote(held.at[step], got.at[step + 1], send.at[step + 1], recv.at[step + 1], peer)
        copy.start()
        copy.wait_recv()
        held[step + 1] = held[step] + got[step + 1]
        copies.append(copy)
    out[own] = held[4]
    back = remote(held.at[4], out.at[own], send.at[5], recv.at[5], here.other_core())
    back.start()
    arrived(out.at[others], recv.at[5])
    for copy in copies + [back]:
        copy.wait_send()


def sum_everywhere(values, collective_id):
    half = (values.shape[0] // 2, values.shape[1])
    vmem = pl.BlockSpec(memory_space=pltpu.VMEM)
    return pl.pallas_call(
        sum_kernel,
        in_specs=[vmem],
        out_specs=vmem,
        out_shape=jax.ShapeDtypeStruct(values.shape, F32),
        scratch_shapes=[
            pltpu.VMEM((5,) + half, F32),
            pltpu.VMEM((5,) + half, F32),
            pltpu.SemaphoreType.DMA((6,)),
            pltpu.SemaphoreType.DMA((6,)),
        ],
        compiler_params=pltpu.CompilerParams(collective_id=collective_id, has_side_effects=True),
    )(values)


def expert_rows(rows, grads, gate, gate_w, up_w, down_w):
    pre_gate = matmul(rows, gate_w)
    pre_up = matmul(rows, up_w)
    back = contract_cols(grads, down_w)
    sigmoid_gate = jax.nn.sigmoid(pre_gate)
    silu_gate = pre_gate * sigmoid_gate
    hidden = (silu_gate * pre_up).astype(BF16)
    inner = jnp.sum(hidden.astype(F32) * back, axis=-1)
    weighted = (hidden.astype(F32) * gate).astype(BF16)
    d_hid = back * gate
    d_pregate = (d_hid * pre_up * (sigmoid_gate + silu_gate * (1.0 - sigmoid_gate))).astype(BF16)
    d_preup = (d_hid * silu_gate).astype(BF16)
    outputs = matmul(weighted, down_w).astype(BF16)
    d_rows = (contract_cols(d_pregate, gate_w) + contract_cols(d_preup, up_w)).astype(BF16)
    return (
        outputs,
        d_rows,
        inner,
        contract_rows(rows, d_pregate),
        contract_rows(rows, d_preup),
        contract_rows(weighted, grads),
    )


def experts(normed, grads, dense_gates, gate_w, up_w, down_w):
    rows_dev, width = normed.shape
    devices = math.prod(lax.axis_size(axis) for axis in ALL)
    expert_count = dense_gates.shape[1]
    expert = lax.axis_index(ALL) // 2
    parts = max(1, lax.axis_size("exp") // 2)
    step = rows_dev // parts

    def one_part(sums, piece):
        rows, grad_rows, gates = piece
        rows_all = lax.all_gather(rows, ALL, axis=0, tiled=True)
        grads_all = lax.all_gather(grad_rows, ALL, axis=0, tiled=True)
        gates_all = lax.all_gather(gates, ALL, axis=0, tiled=True)
        gate = lax.dynamic_slice_in_dim(gates_all, expert, 1, 1)
        got = expert_rows(rows_all, grads_all, gate, gate_w, up_w, down_w)
        outputs = lax.psum_scatter(got[0], ALL, scatter_dimension=0, tiled=True)
        d_rows = lax.psum_scatter(got[1], ALL, scatter_dimension=0, tiled=True)
        inner = lax.all_to_all(
            got[2].reshape(devices, step), ALL, split_axis=0, concat_axis=0, tiled=True
        )
        inner = inner.reshape(expert_count, 2, step).sum(axis=1).T
        sums = got[3:] if sums is None else tuple(a + b for a, b in zip(sums, got[3:]))
        return sums, (outputs, d_rows, inner)

    if parts == 1:
        sums, (outputs, d_rows, inner) = one_part(None, (normed, grads, dense_gates))
    else:
        start = tuple(jnp.zeros(w.shape, F32) for w in (gate_w, up_w, down_w))
        pieces = tuple(v.reshape(parts, step, -1) for v in (normed, grads, dense_gates))
        sums, got = lax.scan(one_part, start, pieces)
        outputs, d_rows, inner = (v.reshape(rows_dev, -1) for v in got)
    return outputs.astype(F32), d_rows.astype(F32), inner, sums


def experts_here(normed, grads_all, picks, router, gate_w, up_w, down_w):
    numbers = jnp.arange(router.shape[1], dtype=jnp.int32)
    mask = jnp.any(picks.T[None] == numbers[:, None, None], axis=1).astype(F32)
    out_parts, d_rows, inner, weights = expert_stage(
        normed, grads_all, mask, gate_w, up_w, down_w, router, 1
    )
    outputs = reduce_rows(out_parts, 2)
    inner = inner[:, :, 0].reshape(router.shape[1], -1).T
    return outputs.astype(F32), d_rows.astype(F32), inner, weights


def shards(
    hidden_in,
    out_grad,
    attn_gain,
    w_qkv,
    q_gain,
    k_gain,
    w_out,
    moe_gain,
    router,
    w_gate,
    w_up,
    w_down,
    routes,
    doc_cuts,
):
    row_count, col_count = lax.axis_size("row"), lax.axis_size("col")
    tokens = hidden_in[0].astype(F32)
    rows_dev, width = tokens.shape
    heads = w_qkv.shape[1] // (3 * HD)
    plane = heads * HD
    scale = HD ** (-0.5)
    side = lax.axis_index("exp") % 2
    row_tok = rows_dev * col_count
    group_tok = row_tok * row_count
    cuts = lax.dynamic_index_in_dim(doc_cuts, lax.axis_index("exp") // 2, 0, keepdims=False)

    here = (row_count, col_count, lax.axis_size("exp")) == (4, 4, 2)

    if here:
        grads_all = lax.all_gather(out_grad[0], ("row", "col"), axis=0, tiled=True)

    gain_one = attn_gain.astype(F32)
    scale_one = rms_scale(tokens)
    head_start = lax.axis_index("col") * plane
    gain_q = lax.dynamic_slice_in_dim(q_gain, head_start, plane, 0).astype(F32)
    gain_k = lax.dynamic_slice_in_dim(k_gain, head_start, plane, 0).astype(F32)
    row_places = side * group_tok + lax.axis_index("row") * row_tok + jnp.arange(row_tok, dtype=jnp.int32)
    unused_doc, position = doc_positions(row_places, cuts)
    cosine, sine = rope_tables(position, HD)
    if here:
        signed = jnp.concatenate([-sine[:, : HD // 2], sine[:, HD // 2 :]], axis=1)
        normed_row, qkv_w, out_w, qkv, totals, query, keys, values = project(
            hidden_in[0], attn_gain, w_qkv, w_out, gain_q[None], gain_k[None], cosine, signed, 0
        )
        total_q, total_k = totals[0], totals[1]
        query = query.reshape(group_tok, HD)
        key_all, value_all = keys.reshape(-1, HD), values.reshape(-1, HD)
    else:
        normed_one = (tokens * scale_one * gain_one).astype(BF16)
        normed_row = lax.all_gather(normed_one, "col", axis=0, tiled=True)
        qkv_w = lax.all_gather(w_qkv, "row", axis=0, tiled=True)
        out_w = lax.all_gather(
            lax.all_gather(w_out, "row", axis=1, tiled=True), "col", axis=0, tiled=True
        )
        qkv = matmul(normed_row, qkv_w)
    qkv = qkv.reshape(row_tok, heads, 3, HD)
    query_raw, key_raw, value_raw = qkv[:, :, 0], qkv[:, :, 1], qkv[:, :, 2]
    if not here:
        total_q, total_k = lax.psum(
            (jnp.sum(query_raw * query_raw, axis=(1, 2)), jnp.sum(key_raw * key_raw, axis=(1, 2))),
            "col",
        )
    scale_q = lax.rsqrt(total_q / width + EPSILON)[:, None, None]
    scale_k = lax.rsqrt(total_k / width + EPSILON)[:, None, None]
    gain_q, gain_k = gain_q.reshape(heads, HD), gain_k.reshape(heads, HD)
    cosine, sine = cosine[:, None, :], sine[:, None, :]
    if not here:
        query = rotate(query_raw * scale_q * gain_q, cosine, sine).astype(BF16)
        key = rotate(key_raw * scale_k * gain_k, cosine, sine).astype(BF16)
        moved = rows_to_heads(jnp.concatenate([query, key, value_raw.astype(BF16)], axis=-1))
        query, own_pair = moved[:, :HD], moved[:, HD:]
        earlier_pair = from_behind(own_pair, "exp", 1)
        lower_pair = jnp.where(side == 0, own_pair, earlier_pair)
        upper_pair = jnp.where(side == 0, jnp.zeros_like(own_pair), own_pair)
        key_value = jnp.concatenate([lower_pair, upper_pair], axis=0)
        key_all, value_all = key_value[:, :HD], key_value[:, HD:]

    mixed_wide, total = attend(query, key_all, value_all, cuts, scale)
    mixed = mixed_wide.astype(BF16)
    mixed_row = heads_to_rows(mixed).reshape(row_tok, plane)
    middle = tokens + matmul(heads_to_tokens(mixed), out_w)

    gain_two = moe_gain.astype(F32)
    scale_two = rms_scale(middle)
    normed_two = (middle * scale_two * gain_two).astype(BF16)
    gates_all = jax.nn.softmax(matmul(normed_two, router), axis=-1)
    picks = routes[0]
    chosen = jnp.any(
        picks[:, :, None] == jnp.arange(router.shape[1], dtype=jnp.int32)[None, None, :], axis=1
    )
    grad_out = out_grad[0].astype(F32)
    expert_w = (w_gate[0], w_up[0], w_down[0])
    if here:
        mixture, d_normed_two, inner, weight_grads = experts_here(
            normed_two, grads_all, picks, router, *expert_w
        )
    else:
        dense_gates = jnp.where(chosen, gates_all, 0.0)
        mixture, d_normed_two, inner, weight_grads = experts(
            normed_two, out_grad[0], dense_gates, *expert_w
        )
    final = middle + mixture
    dense = jnp.where(chosen, inner, 0.0)
    d_logits = (gates_all * (dense - jnp.sum(gates_all * dense, axis=-1, keepdims=True))).astype(BF16)
    grad_router = contract_rows(normed_two, d_logits)
    d_normed_two = d_normed_two + contract_cols(d_logits, router)
    grad_moe_gain = jnp.sum(d_normed_two * middle * scale_two, axis=0)
    weighted_two = d_normed_two * gain_two
    d_middle = (
        grad_out
        + scale_two * weighted_two
        - middle * scale_two**3 * jnp.mean(weighted_two * middle, axis=-1, keepdims=True)
    )

    d_attn = d_middle.astype(BF16)
    d_mixed = tokens_to_heads(contract_cols(d_attn, out_w).astype(BF16))
    d_attn_row = lax.all_gather(d_attn, "col", axis=0, tiled=True)
    d_query, acc_key, acc_value = attend_back(
        query, key_all, value_all, d_mixed, mixed_wide, total, cuts, scale
    )
    accumulated = jnp.concatenate([acc_key, acc_value], axis=1)
    lower_acc, upper_acc = accumulated[:group_tok], accumulated[group_tok:]
    kept_acc = jnp.where(side == 0, lower_acc, upper_acc)
    later_acc = from_behind(lower_acc.astype(BF16), "exp", -1).astype(F32)
    summed_pair = kept_acc + jnp.where(side == 0, later_acc, jnp.zeros_like(later_acc))
    d_heads = heads_to_rows(jnp.concatenate([d_query, summed_pair], axis=1).astype(BF16)).astype(F32)
    d_q_unit = rotate_back(d_heads[:, :, :HD], cosine, sine)
    d_k_unit = rotate_back(d_heads[:, :, HD : 2 * HD], cosine, sine)
    d_value = d_heads[:, :, 2 * HD :]
    weighted_q = d_q_unit * gain_q
    weighted_k = d_k_unit * gain_k
    sum_q, sum_k = lax.psum(
        (jnp.sum(weighted_q * query_raw, axis=(1, 2)), jnp.sum(weighted_k * key_raw, axis=(1, 2))),
        "col",
    )
    d_query_raw = scale_q * weighted_q - query_raw * scale_q**3 * (sum_q / width)[:, None, None]
    d_key_raw = scale_k * weighted_k - key_raw * scale_k**3 * (sum_k / width)[:, None, None]
    grad_q_part = jnp.sum(d_q_unit * query_raw * scale_q, axis=0).reshape(plane)
    grad_k_part = jnp.sum(d_k_unit * key_raw * scale_k, axis=0).reshape(plane)
    d_qkv = jnp.concatenate([d_query_raw, d_key_raw, d_value], axis=2).astype(BF16)
    d_qkv = d_qkv.reshape(row_tok, heads * 3 * HD)
    if here:
        d_normed_one, grads = tail(d_qkv, qkv_w, normed_row, mixed_row, d_attn_row, 5)
        d_normed_one, grads = d_normed_one.astype(F32), grads.astype(F32)
        grad_qkv, grad_w_out = grads[:, : d_qkv.shape[1]], grads[:, d_qkv.shape[1] :]
    else:
        d_normed_one = lax.psum_scatter(
            contract_cols(d_qkv, qkv_w).astype(BF16), "col", scatter_dimension=0, tiled=True
        ).astype(F32)
        grad_qkv = lax.psum_scatter(
            contract_rows(normed_row, d_qkv).astype(BF16), "row", scatter_dimension=0, tiled=True
        )
        grad_w_out = lax.psum_scatter(
            contract_rows(mixed_row, d_attn_row).astype(BF16), "row", scatter_dimension=1, tiled=True
        )
        grad_qkv = lax.psum(grad_qkv, "exp").astype(F32)
        grad_w_out = lax.psum(grad_w_out, "exp").astype(F32)
    grad_attn_gain = jnp.sum(d_normed_one * tokens * scale_one, axis=0)
    weighted_one = d_normed_one * gain_one
    grad_hidden = (
        d_middle
        + scale_one * weighted_one
        - tokens * scale_one**3 * jnp.mean(weighted_one * tokens, axis=-1, keepdims=True)
    )
    empty = jnp.zeros((width,), F32)
    grad_q_full = lax.dynamic_update_slice_in_dim(empty, grad_q_part, head_start, 0)
    grad_k_full = lax.dynamic_update_slice_in_dim(empty, grad_k_part, head_start, 0)
    parts = (grad_attn_gain, grad_q_full, grad_k_full, grad_moe_gain)
    if here:
        packed = jnp.concatenate(parts + (grad_router.T.reshape(-1),)).reshape(-1, 128)
        packed = sum_everywhere(packed, 6).reshape(-1)
        summed = [packed[i * width : (i + 1) * width] for i in range(4)]
        summed.append(packed[4 * width :].reshape(-1, width).T)
    else:
        summed = lax.psum(parts + (grad_router,), ALL)
    return (
        final.astype(BF16)[None],
        grad_hidden[None],
        summed[0],
        grad_qkv,
        summed[1],
        summed[2],
        grad_w_out,
        summed[3],
        summed[4],
        weight_grads[0][None],
        weight_grads[1][None],
        weight_grads[2][None],
    )


def solution(mesh):
    token_spec = P("exp", ("row", "col"), None)
    expert_spec = P(("row", "col", "exp"), None, None)
    in_specs = (
        token_spec,
        token_spec,
        P(),
        P("row", "col"),
        P(),
        P(),
        P("col", "row"),
        P(),
        P(),
        expert_spec,
        expert_spec,
        expert_spec,
        token_spec,
        P(),
    )
    out_specs = (
        token_spec,
        token_spec,
        P(),
        P("row", "col"),
        P(),
        P(),
        P("col", "row"),
        P(),
        P(),
        expert_spec,
        expert_spec,
        expert_spec,
    )
    return jax.shard_map(shards, mesh=mesh, in_specs=in_specs, out_specs=out_specs, check_vma=False)
```

```python
import functools
import math

import jax
import jax.numpy as jnp
from jax import lax
from jax.experimental import pallas as pl
from jax.experimental.pallas import tpu as pltpu
from jax.sharding import PartitionSpec as P

HD = 128
EPSILON = 1e-05
ROPE_BASE = 10000.0
MASKED = -1e30
BF16 = jnp.bfloat16
F32 = jnp.float32


def matmul(left, right):
    return jnp.dot(left, right, preferred_element_type=F32)


def contract_rows(left, right):
    return lax.dot_general(left, right, (((0,), (0,)), ((), ())), preferred_element_type=F32)


def contract_cols(left, right):
    return lax.dot_general(left, right, (((1,), (1,)), ((), ())), preferred_element_type=F32)


def rms_scale(values):
    return lax.rsqrt(jnp.mean(values * values, axis=-1, keepdims=True) + EPSILON)


def rope_tables(position, width):
    frequency = ROPE_BASE ** (-jnp.arange(0, width, 2, dtype=F32) / width)
    angle = position.astype(F32)[:, None] * frequency[None, :]
    return (
        jnp.concatenate([jnp.cos(angle)] * 2, axis=-1),
        jnp.concatenate([jnp.sin(angle)] * 2, axis=-1),
    )


def rotate(values, cosine, sine):
    half = values.shape[-1] // 2
    turned = jnp.concatenate([-values[..., half:], values[..., :half]], axis=-1)
    return values * cosine + turned * sine


def rotate_back(values, cosine, sine):
    half = values.shape[-1] // 2
    turned = values * sine
    return values * cosine + jnp.concatenate([turned[..., half:], -turned[..., :half]], axis=-1)


def doc_positions(places, cuts):
    first = (places >= cuts[0]).astype(jnp.int32)
    second = (places >= cuts[1]).astype(jnp.int32)
    start = first * cuts[0] + second * (cuts[1] - cuts[0])
    return (first + second, places - start)


def from_behind(value, axis, steps):
    count = lax.axis_size(axis)
    initial, last = (max(0, -steps), min(count, count - steps))
    return lax.ppermute(value, axis, [(source, source + steps) for source in range(initial, last)])


def rows_to_heads(values):
    count = lax.axis_size("row")
    rows, heads, width = values.shape
    moved = lax.all_to_all(values.transpose(1, 0, 2), "row", split_axis=0, concat_axis=0, tiled=True)
    return moved.reshape(count * rows, width)


def heads_to_rows(values):
    count = lax.axis_size("row")
    rows, width = values.shape
    moved = lax.all_to_all(
        values.reshape(count, rows // count, width), "row", split_axis=0, concat_axis=0, tiled=True
    )
    return moved.transpose(1, 0, 2)


def heads_to_tokens(values):
    row_count, col_count = lax.axis_size("row"), lax.axis_size("col")
    rows = values.shape[0] // (row_count * col_count)
    moved = lax.all_to_all(
        values.reshape(row_count * col_count, rows, HD),
        ("row", "col"),
        split_axis=0,
        concat_axis=0,
        tiled=True,
    )
    moved = moved.reshape(row_count, col_count, rows, HD).transpose(2, 1, 0, 3)
    return moved.reshape(rows, row_count * col_count * HD)


def tokens_to_heads(values):
    row_count, col_count = lax.axis_size("row"), lax.axis_size("col")
    rows = values.shape[0]
    parted = values.reshape(rows, col_count, row_count, HD).transpose(2, 1, 0, 3)
    moved = lax.all_to_all(
        parted.reshape(row_count * col_count, rows, HD),
        ("row", "col"),
        split_axis=0,
        concat_axis=0,
        tiled=True,
    )
    return moved.reshape(row_count * col_count * rows, HD)


MESH = pl.DeviceIdType.MESH
ALL = ("row", "col", "exp")


class Here:
    def __init__(self):
        self.row, self.col, self.core = (lax.axis_index(axis) for axis in ALL)
        self.across = self.row + 1 - 2 * (self.row % 2)
        self.along = (self.row + 2) % 4
        self.opposite = 3 - self.row
        self.rows = (self.row, self.across, self.along, self.opposite)
        half = self.col // 2
        self.near_first = [
            self.col,
            1 + self.col % 2,
            2 - self.col - self.col % 2 + 3 * half,
            3 - 3 * half,
        ]

    def at_row(self, row):
        return (row, self.col, self.core)

    def at_col(self, col):
        return (self.row, col, self.core)

    def other_core(self):
        return (self.row, self.col, 1 - self.core)

    def line_peers(self):
        return [self.at_col((self.col + step) % 4) for step in (1, 2, 3)]

    def group_peers(self):
        steps = range(1, 16)
        return [((self.row + s // 4) % 4, (self.col + s) % 4, self.core) for s in steps]

    def plane_peers(self):
        return [self.at_row(row) for row in self.rows[1:]]


def greet(peers):
    barrier = pltpu.get_barrier_semaphore()
    for peer in peers:
        pl.semaphore_signal(barrier, inc=1, device_id=peer, device_id_type=MESH)
    pl.semaphore_wait(barrier, len(peers))


def greet_near(here):
    barrier = pltpu.get_barrier_semaphore()
    col = here.col

    def signal(peer):
        pl.semaphore_signal(barrier, inc=1, device_id=peer, device_id_type=MESH)

    for peer in (here.other_core(), here.at_row(here.across), here.at_row(here.along)):
        signal(peer)

    @pl.when(col > 0)
    def _():
        signal(here.at_col(col - 1))

    @pl.when(col < 3)
    def _():
        signal(here.at_col(col + 1))

    pl.semaphore_wait(barrier, 3 + (col + 3) // 4 + (6 - col) // 4)


def remote(source, target, send, recv, device):
    return pltpu.make_async_remote_copy(
        src_ref=source,
        dst_ref=target,
        send_sem=send,
        recv_sem=recv,
        device_id=device,
        device_id_type=MESH,
    )


def arrived(target, recv):
    pltpu.make_async_copy(target, target, recv).wait()


def add_into(target, *terms):
    step = 16

    @pl.loop(0, target.shape[0] // step)
    def _(index):
        part = pl.ds(pl.multiple_of(index * step, step), step)
        value = target[part].astype(F32)
        for term in terms:
            value = value + term[part].astype(F32)
        target[part] = value.astype(target.dtype)


SPREAD_SEMS = [pltpu.SemaphoreType.DMA((4,))] * 11 + [pltpu.SemaphoreType.DMA((4, 4))] * 2


class Spread:
    def __init__(self, here, own, block, rows, sems, line=True, plane=True, core=True):
        self.here, self.own, self.block = here, own, block
        self.line, self.plane, self.core = line, plane, core
        (
            self.up_send, self.down_send, self.line_recv,
            self.across_send, self.across_recv, self.along_send, self.along_recv,
            self.one_send, self.one_recv, self.two_send, self.two_recv,
            self.core_send, self.core_recv,
        ) = sems
        self.first, self.second = pl.ds(0, rows // 2), pl.ds(rows // 2, rows // 2)
        self.order = here.near_first if line else [0]
        self.steps = len(self.order)

    def held(self, step):
        here = self.here
        return self.own if step == 0 else self.block(here.row, self.order[step], here.core)

    def up(self, step):
        here, place = self.here, self.order[step]
        target = self.block(here.row, place, here.core)
        recv = self.line_recv.at[place]
        return remote(self.held(step), target, self.up_send.at[place], recv, here.at_col(here.col + 1))

    def down(self, step):
        here, place = self.here, self.order[step]
        target = self.block(here.row, place, here.core)
        recv = self.line_recv.at[place]
        return remote(self.held(step), target, self.down_send.at[place], recv, here.at_col(here.col - 1))

    def to_across(self, step):
        here, place = self.here, self.order[step]
        target = self.block(here.row, place, here.core)
        sems = self.across_send.at[place], self.across_recv.at[place]
        return remote(self.held(step), target, *sems, here.at_row(here.across))

    def to_along(self, step):
        here, place = self.here, self.order[step]
        target = self.block(here.row, place, here.core)
        sems = self.along_send.at[place], self.along_recv.at[place]
        return remote(self.held(step), target, *sems, here.at_row(here.along))

    def corner_one(self, step):
        here, place = self.here, self.order[step]
        part = self.block(here.across, place, here.core).at[self.first]
        sems = self.one_send.at[place], self.one_recv.at[place]
        return remote(part, part, *sems, here.at_row(here.along))

    def corner_two(self, step):
        here, place = self.here, self.order[step]
        part = self.block(here.along, place, here.core).at[self.second]
        sems = self.two_send.at[place], self.two_recv.at[place]
        return remote(part, part, *sems, here.at_row(here.across))

    def to_core(self, which, step):
        here, place = self.here, self.order[step]
        target = self.block(here.rows[which], place, here.core)
        source = self.held(step) if which == 0 else target
        sems = self.core_send.at[which, place], self.core_recv.at[which, place]
        return remote(source, target, *sems, here.other_core())

    def line_step(self, step):
        here, place = self.here, self.order[step]
        if step > 0:
            arrived(self.held(step), self.line_recv.at[place])
        if self.line:

            @pl.when((place <= here.col) & (here.col < 3))
            def _():
                self.up(step).start()

            @pl.when((place >= here.col) & (here.col > 0))
            def _():
                self.down(step).start()

        if self.plane:
            self.to_across(step).start()
            self.to_along(step).start()
            if self.core:
                self.to_core(0, step).start()

    def plane_step(self, step):
        here, place = self.here, self.order[step]
        arrived(self.block(here.across, place, here.core), self.across_recv.at[place])
        self.corner_one(step).start()
        if self.core:
            self.to_core(1, step).start()
        arrived(self.block(here.along, place, here.core), self.along_recv.at[place])
        self.corner_two(step).start()
        if self.core:
            self.to_core(2, step).start()

    def corner_step(self, step):
        here, place = self.here, self.order[step]
        target = self.block(here.opposite, place, here.core)
        arrived(target.at[self.first], self.one_recv.at[place])
        arrived(target.at[self.second], self.two_recv.at[place])
        if self.core:
            self.to_core(3, step).start()

    def step(self, index):
        if index < self.steps:
            self.line_step(index)
        if self.plane and 0 <= index - 1 < self.steps:
            self.plane_step(index - 1)
        if self.plane and 0 <= index - 2 < self.steps:
            self.corner_step(index - 2)

    def core_arrived(self, which, step):
        here, place = self.here, self.order[step]
        target = self.block(here.rows[which], place, 1 - here.core)
        arrived(target, self.core_recv.at[which, place])

    def finish(self, arrivals=True):
        here = self.here
        for step in range(self.steps):
            place = self.order[step]
            if self.line:

                @pl.when((place <= here.col) & (here.col < 3))
                def _():
                    self.up(step).wait_send()

                @pl.when((place >= here.col) & (here.col > 0))
                def _():
                    self.down(step).wait_send()

            if self.plane:
                self.to_across(step).wait_send()
                self.to_along(step).wait_send()
                self.corner_one(step).wait_send()
                self.corner_two(step).wait_send()
                for which in range(4 if self.core else 0):
                    self.to_core(which, step).wait_send()
                    if arrivals:
                        self.core_arrived(which, step)


COLLECT_SEMS = (
    [pltpu.SemaphoreType.DMA((4,))] * 4
    + [pltpu.SemaphoreType.DMA((2, 4))] * 4
    + [pltpu.SemaphoreType.DMA((4,))] * 2
    + [pltpu.SemaphoreType.DMA((5,))]
)


def collect_buffers(rows, width):
    return [
        pltpu.VMEM((4, 4, rows, width), BF16),
        pltpu.VMEM((4, rows // 2, width), BF16),
        pltpu.VMEM((4, rows // 2, width), BF16),
        pltpu.VMEM((4, rows, width), BF16),
        pltpu.VMEM((4, rows, width), BF16),
        pltpu.VMEM((5, rows, width), BF16),
    ]


class Collect:
    def __init__(self, here, buffers, sems):
        self.here = here
        self.mine, self.one, self.two, self.from_across, self.from_along, self.line = buffers
        (
            self.one_send, self.one_recv, self.two_send, self.two_recv,
            self.across_send, self.across_recv, self.along_send, self.along_recv,
            self.up_send, self.down_send, self.line_recv,
        ) = sems
        half = self.mine.shape[2] // 2
        self.halves = (pl.ds(0, half), pl.ds(half, half))

    def give_one(self, place):
        here = self.here
        return remote(
            self.mine.at[3, place, self.halves[0]], self.one.at[place],
            self.one_send.at[place], self.one_recv.at[place], here.at_row(here.across),
        )

    def give_two(self, place):
        here = self.here
        return remote(
            self.mine.at[3, place, self.halves[1]], self.two.at[place],
            self.two_send.at[place], self.two_recv.at[place], here.at_row(here.along),
        )

    def give_across(self, place, half):
        here, part = self.here, self.halves[half]
        return remote(
            self.mine.at[1, place, part], self.from_across.at[place, part],
            self.across_send.at[half, place], self.across_recv.at[half, place], here.at_row(here.across),
        )

    def give_along(self, place, half):
        here, part = self.here, self.halves[half]
        return remote(
            self.mine.at[2, place, part], self.from_along.at[place, part],
            self.along_send.at[half, place], self.along_recv.at[half, place], here.at_row(here.along),
        )

    def give_up(self, place):
        here = self.here
        sems = self.up_send.at[place], self.line_recv.at[place]
        return remote(self.mine.at[0, place], self.line.at[place], *sems, here.at_col(here.col + 1))

    def give_down(self, place, slot):
        here = self.here
        sems = self.down_send.at[place], self.line_recv.at[slot]
        return remote(self.mine.at[0, place], self.line.at[slot], *sems, here.at_col(here.col - 1))

    def start_far(self, place):
        self.give_one(place).start()
        self.give_two(place).start()
        self.give_along(place, 1).start()

    def start_near(self, place):
        self.give_across(place, 0).start()

    def corner_step(self, place):
        self.give_two(place).wait_recv()
        add_into(self.mine.at[1, place, self.halves[1]], self.two.at[place])
        self.give_across(place, 1).start()
        self.give_one(place).wait_recv()
        add_into(self.mine.at[2, place, self.halves[0]], self.one.at[place])
        self.give_along(place, 0).start()

    def plane_step(self, place):
        for half in range(2):
            self.give_across(place, half).wait_recv()
            self.give_along(place, half).wait_recv()
        add_into(self.mine.at[0, place], self.from_across.at[place], self.from_along.at[place])

    def line_step(self, place):
        col = self.here.col

        @pl.when((place > col) & (col > 0))
        def _():
            self.give_up(place).wait_recv()
            add_into(self.mine.at[0, place], self.line.at[place])

        @pl.when((place < col) & (col < 3))
        def _():
            self.give_down(place, place).wait_recv()
            add_into(self.mine.at[0, place], self.line.at[place])

        @pl.when(place > col)
        def _():
            self.give_up(place).start()

        @pl.when(place < col - 1)
        def _():
            self.give_down(place, place).start()

        @pl.when(place == col - 1)
        def _():
            self.give_down(place, 4).start()

    def own_step(self):
        col = self.here.col

        @pl.when(col > 0)
        def _():
            self.give_up(col).wait_recv()
            add_into(self.mine.at[0, col], self.line.at[col])

        @pl.when(col < 3)
        def _():
            self.give_down(col, 4).wait_recv()
            add_into(self.mine.at[0, col], self.line.at[4])

    def finish(self):
        col = self.here.col
        for place in range(4):
            self.give_one(place).wait_send()
            self.give_two(place).wait_send()
            for half in range(2):
                self.give_across(place, half).wait_send()
                self.give_along(place, half).wait_send()

            @pl.when(place > col)
            def _():
                self.give_up(place).wait_send()

            @pl.when(place < col)
            def _():
                self.give_down(place, place).wait_send()


def doc_start(places, cuts):
    return jnp.where(places >= cuts[1], cuts[1], jnp.where(places >= cuts[0], cuts[0], 0))


def key_blocks(cuts, first_query, rows, scores_of, block_fn):
    def scan(index, carry):
        start = pl.multiple_of(index * rows, rows)
        free = (start >= doc_start(first_query + rows - 1, cuts)) & (start + rows <= first_query + 1)

        @pl.when(free)
        def _():
            block_fn(start, scores_of(start))

        @pl.when(jnp.logical_not(free))
        def _():
            key_place = start + lax.broadcasted_iota(jnp.int32, (rows, rows), 0)
            place = first_query + lax.broadcasted_iota(jnp.int32, (1, rows), 1)
            allowed = (key_place <= place) & (key_place >= doc_start(place, cuts))
            block_fn(start, jnp.where(allowed, scores_of(start), MASKED))

        return carry

    lax.fori_loop(doc_start(first_query, cuts) // rows, first_query // rows + 1, scan, 0)


def attend_kernel(scale, group_tok, cuts, query, keys, values_t, mixed, total, top, summed, acc):
    rows = query.shape[0]
    side = lax.axis_index("exp") % 2
    first_query = side * group_tok + pl.program_id(0) * rows
    top[...] = jnp.full_like(top, MASKED)
    summed[...] = jnp.zeros_like(summed)
    acc[...] = jnp.zeros_like(acc)
    cut = (cuts[0, 0], cuts[0, 1])

    def scores_of(start):
        return contract_cols(keys[pl.ds(start, rows)], query[...]) * scale

    def block_fn(start, scores):
        old = top[...]
        new = jnp.maximum(old, jnp.max(scores, axis=0, keepdims=True))
        weights = jnp.exp(scores - new)
        decay = jnp.exp(old - new)
        top[...] = new
        summed[...] = summed[...] * decay + jnp.sum(weights, axis=0, keepdims=True)
        acc[...] = acc[...] * decay + matmul(values_t[:, pl.ds(start, rows)], weights.astype(BF16))

    key_blocks(cut, first_query, rows, scores_of, block_fn)
    mixed[...] = (acc[...] / summed[...]).T
    total[...] = top[...] + jnp.log(summed[...])


def attend(query, keys, values, cuts, scale, rows=512):
    group_tok, head_size = query.shape
    whole = lambda shape: pl.BlockSpec(shape, lambda i: (0, 0))
    return pl.pallas_call(
        functools.partial(attend_kernel, scale, group_tok),
        grid=(group_tok // rows,),
        in_specs=[
            pl.BlockSpec(memory_space=pltpu.SMEM),
            pl.BlockSpec((rows, head_size), lambda i: (i, 0)),
            whole(keys.shape),
            whole(values.shape[::-1]),
        ],
        out_specs=[
            pl.BlockSpec((rows, head_size), lambda i: (i, 0)),
            pl.BlockSpec((1, rows), lambda i: (0, i)),
        ],
        out_shape=[
            jax.ShapeDtypeStruct((group_tok, head_size), F32),
            jax.ShapeDtypeStruct((1, group_tok), F32),
        ],
        scratch_shapes=[
            pltpu.VMEM((1, rows), F32),
            pltpu.VMEM((1, rows), F32),
            pltpu.VMEM((head_size, rows), F32),
        ],
        compiler_params=pltpu.CompilerParams(vmem_limit_bytes=40 * 2**20),
        cost_estimate=pl.CostEstimate(
            flops=4 * 7 * 2**20 * head_size, bytes_accessed=2**23, transcendentals=7 * 2**20
        ),
    )(cuts[None], query, keys, values.T)


def attend_back_kernel(
    scale, group_tok, cuts, query, keys, keys_t, values, d_mixed, total, delta,
    d_query, d_keys, d_values, acc,
):
    rows = query.shape[0]
    side = lax.axis_index("exp") % 2
    first_query = side * group_tok + pl.program_id(0) * rows
    cut = (cuts[0, 0], cuts[0, 1])

    @pl.when(pl.program_id(0) == 0)
    def _():
        d_keys[...] = jnp.zeros_like(d_keys)
        d_values[...] = jnp.zeros_like(d_values)

    acc[...] = jnp.zeros_like(acc)

    def scores_of(start):
        return contract_cols(keys[pl.ds(start, rows)], query[...]) * scale

    def block_fn(start, scores):
        part = pl.ds(start, rows)
        weights = jnp.exp(scores - total[...])
        d_weights = contract_cols(values[part], d_mixed[...])
        d_scores = (weights * (d_weights - delta[...])).astype(BF16)
        d_values[part] += matmul(weights.astype(BF16), d_mixed[...])
        d_keys[part] += matmul(d_scores, query[...]) * scale
        acc[...] += matmul(keys_t[:, part], d_scores)

    key_blocks(cut, first_query, rows, scores_of, block_fn)
    d_query[...] = (acc[...] * scale).T


def attend_back(query, keys, values, d_mixed, mixed, total, cuts, scale, rows=512):
    group_tok, head_size = query.shape
    delta = jnp.sum(d_mixed.astype(F32) * mixed, axis=1)[None]
    whole = lambda shape: pl.BlockSpec(shape, lambda i: (0, 0))
    block = pl.BlockSpec((rows, head_size), lambda i: (i, 0))
    line = pl.BlockSpec((1, rows), lambda i: (0, i))
    return pl.pallas_call(
        functools.partial(attend_back_kernel, scale, group_tok),
        grid=(group_tok // rows,),
        in_specs=[
            pl.BlockSpec(memory_space=pltpu.SMEM),
            block,
            whole(keys.shape),
            whole(keys.shape[::-1]),
            whole(keys.shape),
            block,
            line,
            line,
        ],
        out_specs=[block, whole(keys.shape), whole(keys.shape)],
        out_shape=[
            jax.ShapeDtypeStruct((group_tok, head_size), F32),
            jax.ShapeDtypeStruct(keys.shape, F32),
            jax.ShapeDtypeStruct(keys.shape, F32),
        ],
        scratch_shapes=[pltpu.VMEM((head_size, rows), F32)],
        compiler_params=pltpu.CompilerParams(vmem_limit_bytes=48 * 2**20),
        cost_estimate=pl.CostEstimate(
            flops=10 * 7 * 2**20 * head_size, bytes_accessed=2**23, transcendentals=7 * 2**20
        ),
    )(cuts[None], query, keys, keys.T, values, d_mixed, total, delta)


def transposed_product(left, right):
    return jnp.dot(left.T, right, preferred_element_type=F32)


def column_of(line):
    return jnp.broadcast_to(line, (128, 128)).T[:, :1]


def line_of(column):
    return jnp.broadcast_to(column, (128, 128)).T[:1]


def expert_kernel(
    expert_count, normed, grads_all, mask, gate_half, up_half, down_half, router,
    rows_all, out_parts, total, inner_in, grad_gate, grad_up, grad_down,
    their_gates, their_down,
    gate_w, up_w, down_w, masks, x_buf, d_buf, gates_t, weighteds_t, d_gates, d_ups, weighteds, out_buf,
    inner, sum_buf, sum_down, *rest,
):
    here = Here()
    row, col, core = here.row, here.col, here.core
    rows, width = normed.shape
    half = gate_half.shape[1]
    expert = row * 4 + col
    count = len(SPREAD_SEMS)
    collect = Collect(here, rest[:6], rest[6 : 6 + len(COLLECT_SEMS)])
    rest = rest[6 + len(COLLECT_SEMS) :]
    (
        kept_sem, weight_sem, weight_send, weight_recv, load_sem, store_sem,
        tile_sem, give_send, give_recv, their_sem, sum_sem,
        inner_send, inner_recv,
    ) = rest[:13]
    sems = rest[13:]

    def x_block(of_row, place, unused_core):
        return rows_all.at[pl.ds(pl.multiple_of((of_row * 4 + place) * rows, rows), rows)]

    def d_block(of_row, place, unused_core):
        return grads_all.at[pl.ds(pl.multiple_of((of_row * 4 + place) * rows, rows), rows)]

    def m_block(of_row, place, unused_core):
        return masks.at[of_row, place]

    spread_x = Spread(here, normed, x_block, rows, sems[:count], core=False)
    spread_m = Spread(here, mask, m_block, mask.shape[0], sems[count:], core=False)
    order = here.near_first

    own_half = pl.ds(pl.multiple_of(core * half, half), half)
    other_half = pl.ds(pl.multiple_of((1 - core) * half, half), half)
    halves = (
        (gate_half, gate_w.at[:, own_half], gate_w.at[:, other_half]),
        (up_half, up_w.at[:, own_half], up_w.at[:, other_half]),
        (down_half, down_w.at[own_half], down_w.at[other_half]),
    )
    keeps = [
        pltpu.make_async_copy(source, target, weight_sem.at[index])
        for index, (source, target, unused) in enumerate(halves)
    ] + [
        pltpu.make_async_copy(source, target, kept_sem.at[index])
        for index, (source, target) in enumerate(
            ((normed, x_block(row, col, 0)), (mask, m_block(row, col, 0)))
        )
    ]
    for keep in keeps:
        keep.start()
    greet(here.group_peers() + [here.other_core()])
    swaps = [
        remote(source, target, weight_send.at[index], weight_recv.at[index], here.other_core())
        for index, (source, target, unused) in enumerate(halves)
    ]
    spread_x.step(0)
    spread_m.step(0)
    for swap in swaps:
        swap.start()

    turns = (3, 2, 1, 0)

    def loads(step):
        return [
            pltpu.make_async_copy(
                source(here.rows[which], order[step], 0),
                target.at[pl.ds(position * rows, rows)],
                load_sem.at[position, array],
            )
            for position, which in enumerate(turns)
            for array, (source, target) in enumerate(((x_block, x_buf), (d_block, d_buf)))
        ]

    def stores(step):
        return [
            pltpu.make_async_copy(
                out_buf.at[pl.ds(position * rows, rows)],
                out_parts.at[which, order[step]],
                store_sem.at[position],
            )
            for position, which in enumerate(turns)
        ]

    tile = 256

    def first_products(step):
        place = order[step]
        x = x_buf[...]
        lane = lax.broadcasted_iota(jnp.int32, (x.shape[0], router.shape[1]), 1)
        logits = jnp.where(lane < expert_count, matmul(x, router[...]), MASKED)
        raised = jnp.exp(logits - jnp.max(logits, axis=1, keepdims=True))
        picked = jnp.sum(jnp.where(lane == expert, raised, 0.0), axis=1, keepdims=True)
        routed = jnp.concatenate(
            [column_of(masks[here.rows[which], place, pl.ds(expert, 1)]) for which in turns]
        )
        gate = picked / jnp.sum(raised, axis=1, keepdims=True) * routed
        columns = [
            pl.ds(pl.multiple_of((here.rows[which] * 4 + place) * rows, rows), rows) for which in turns
        ]

        def tile_step(index, inner_sum):
            at = pl.ds(pl.multiple_of(index * tile, tile), tile)
            pre_gate = matmul(x_buf[...], gate_w[:, at])
            pre_up = matmul(x_buf[...], up_w[:, at])
            back = contract_cols(d_buf[...], down_w[at])
            sigmoid_gate = 1.0 / (1.0 + jnp.exp(-pre_gate))
            silu_gate = pre_gate * sigmoid_gate
            hidden = (silu_gate * pre_up).astype(BF16).astype(F32)
            d_hid = back * gate
            d_gate = (d_hid * pre_up * (sigmoid_gate + silu_gate * (1.0 - sigmoid_gate))).astype(BF16)
            d_up = (d_hid * silu_gate).astype(BF16)
            weight = (hidden * gate).astype(BF16)
            d_gates[:, at] = d_gate
            d_ups[:, at] = d_up
            weighteds[:, at] = weight
            side = index // (half // tile)
            first = pl.multiple_of(index % (half // tile) * tile, tile)
            for values, target in (
                (d_gate, gates_t.at[side, pl.ds(first, tile)]),
                (d_up, gates_t.at[side, pl.ds(first + half, tile)]),
                (weight, weighteds_t.at[at]),
            ):
                turned = values.T
                for position, column in enumerate(columns):
                    target[:, column] = turned[:, position * rows : (position + 1) * rows]
            return inner_sum + jnp.sum(hidden * back, axis=1, keepdims=True)

        start = jnp.zeros((x.shape[0], 1), F32)
        inner_sum = lax.fori_loop(0, gate_w.shape[1] // tile, tile_step, start)
        for position, which in enumerate(turns):
            part = slice(position * rows, (position + 1) * rows)
            inner[here.rows[which], place, 0:1] = line_of(inner_sum[part])

    def second_products(step):
        place = order[step]

        @pl.loop(0, width // tile)
        def _(index):
            at = pl.ds(pl.multiple_of(index * tile, tile), tile)
            out_buf[:, at] = matmul(weighteds[...], down_w[:, at]).astype(BF16)
            d_x = contract_cols(d_gates[...], gate_w[at]) + contract_cols(d_ups[...], up_w[at])
            d_x = d_x.astype(BF16)
            for position, which in enumerate(turns):
                collect.mine[which, place, :, at] = d_x[position * rows : (position + 1) * rows]

    for index in (1, 2):
        spread_x.step(index)
        spread_m.step(index)
    for keep in keeps:
        keep.wait()
    for copy in loads(0):
        copy.start()
    for swap in swaps:
        swap.wait_recv()
    for step in range(4):
        for copy in loads(step):
            copy.wait()
        first_products(step)
        if step < 3:
            spread_x.step(step + 3)
            spread_m.step(step + 3)
            for copy in loads(step + 1):
                copy.start()
        if step > 0:
            for copy in stores(step - 1):
                copy.wait()
            collect.corner_step(order[step - 1])
        second_products(step)
        for copy in stores(step):
            copy.start()
        collect.start_far(order[step])
        collect.start_near(order[step])
        if step > 0:
            collect.plane_step(order[step - 1])

    tiles = width // tile

    def tile_at(index):
        return pl.ds(pl.multiple_of(index * tile, tile), tile)

    def acts_of(kind, side):
        if kind == 0:
            return gates_t[side]
        return weighteds_t[pl.ds(pl.multiple_of(side * half, half), half)]

    counts = (2 * half, half)

    def slot_at(slot):
        return pl.ds(pl.multiple_of(slot * tile, tile), tile)

    def tile_buf(slot):
        return gate_w.at[:, slot_at(slot)]

    def give_buf(kind, slot):
        return up_w.at[pl.ds(0, counts[kind]), slot_at(slot)]

    def their_buf(kind, slot):
        return up_w.at[pl.ds(width // 2, counts[kind]), slot_at(slot)]

    theirs = (their_gates, their_down)

    def tile_load(source, index, slot):
        return pltpu.make_async_copy(
            source.at[:, tile_at(index)], tile_buf(slot), tile_sem.at[slot]
        )

    def give(kind, index, slot):
        sems = give_send.at[slot, kind], give_recv.at[kind, index]
        return remote(give_buf(kind, slot), theirs[kind].at[:, tile_at(index)], *sems, here.other_core())

    def their_load(kind, index, slot):
        return pltpu.make_async_copy(
            theirs[kind].at[:, tile_at(index)],
            their_buf(kind, slot),
            their_sem.at[slot, kind],
        )

    def sum_stores(kind, index, slot):
        if kind == 1:
            target = grad_down.at[:, tile_at(index)]
            return [pltpu.make_async_copy(sum_down, target, sum_sem.at[0, 2])]
        return [
            pltpu.make_async_copy(
                sum_buf.at[slot, part], target.at[tile_at(index)], sum_sem.at[slot, part]
            )
            for part, target in enumerate((grad_gate, grad_up))
        ]

    def give_gradients(source, kind):
        tile_load(source, 0, 0).start()

        @pl.loop(0, tiles)
        def _(index):
            slot = index % 2

            @pl.when(index + 1 < tiles)
            def _():
                tile_load(source, index + 1, 1 - slot).start()

            tile_load(source, index, slot).wait()
            product = matmul(acts_of(kind, 1 - core), tile_buf(slot)[...])

            @pl.when(index >= 2)
            def _():
                give(kind, index - 2, slot).wait_send()

            give_buf(kind, slot)[...] = product.astype(BF16)
            give(kind, index, slot).start()

        for slot in range(2):
            give(kind, tiles - 2 + slot, slot).wait_send()

    def keep_gradients(source, kind):
        tile_load(source, 0, 0).start()
        give(kind, 0, 0).wait_recv()
        their_load(kind, 0, 0).start()

        @pl.loop(0, tiles)
        def _(index):
            slot = index % 2

            @pl.when(index + 1 < tiles)
            def _():
                tile_load(source, index + 1, 1 - slot).start()
                give(kind, index + 1, 1 - slot).wait_recv()
                their_load(kind, index + 1, 1 - slot).start()

            tile_load(source, index, slot).wait()
            product = matmul(acts_of(kind, core), tile_buf(slot)[...])
            their_load(kind, index, slot).wait()
            product = product + their_buf(kind, slot)[...].astype(F32)

            held = 2 - kind

            @pl.when(index >= held)
            def _():
                for copy in sum_stores(kind, index - held, slot):
                    copy.wait()

            if kind == 1:
                sum_down[...] = product
            else:
                sum_buf[slot, 0] = product[:half].T
                sum_buf[slot, 1] = product[half:].T
            for copy in sum_stores(kind, index, slot):
                copy.start()

        for slot in range(2 - kind):
            for copy in sum_stores(kind, tiles - 2 + kind + slot, slot):
                copy.wait()

    def give_inner(index):
        step = index + 1
        to_row, to_col = (row + step // 4) % 4, (col + step) % 4
        return remote(
            inner.at[to_row, to_col],
            inner_in.at[row, col],
            inner_send.at[index],
            inner_recv.at[row, col],
            (to_row, to_col, core),
        )

    for index in range(15):
        give_inner(index).start()
    inner_in[row, col] = inner[row, col]
    collect.line_step(1)
    collect.line_step(2)
    give_gradients(rows_all, 0)
    collect.corner_step(order[3])
    give_gradients(grads_all, 1)
    collect.plane_step(order[3])
    collect.line_step(0)
    collect.line_step(3)
    keep_gradients(rows_all, 0)
    keep_gradients(grads_all, 1)
    collect.own_step()
    total[...] = collect.mine[0, col]

    for index in range(15):
        give_inner(index).wait_send()
        step = index + 1
        from_row, from_col = (row + 4 - step // 4) % 4, (col + 4 - step % 4) % 4
        arrived(inner_in.at[from_row, from_col], inner_recv.at[from_row, from_col])
    for copy in stores(3):
        copy.wait()
    for swap in swaps:
        swap.wait_send()
    spread_x.finish()
    spread_m.finish()
    collect.finish()


def expert_stage(normed, grads_all, mask, gate_half, up_half, down_half, router, collective_id):
    rows, width = normed.shape
    half = gate_half.shape[1]
    expert_count = router.shape[1]
    router = jnp.pad(router, ((0, 0), (0, 128 - expert_count)))
    tokens = 16 * rows
    tile = 256
    vmem = pl.BlockSpec(memory_space=pltpu.VMEM)
    hbm = pl.BlockSpec(memory_space=pl.ANY)
    dma = pltpu.SemaphoreType.DMA
    blocks = jax.ShapeDtypeStruct((4, 4, rows, width), BF16)
    got = pl.pallas_call(
        functools.partial(expert_kernel, expert_count),
        in_specs=[hbm] * 6 + [vmem],
        out_specs=[hbm] * 2 + [vmem] * 2 + [hbm] * 5,
        out_shape=[
            jax.ShapeDtypeStruct((tokens, width), BF16),
            blocks,
            jax.ShapeDtypeStruct((rows, width), BF16),
            jax.ShapeDtypeStruct((4, 4, 8, rows), F32),
            jax.ShapeDtypeStruct((width, half), F32),
            jax.ShapeDtypeStruct((width, half), F32),
            jax.ShapeDtypeStruct((half, width), F32),
            jax.ShapeDtypeStruct((2 * half, width), BF16),
            jax.ShapeDtypeStruct((half, width), BF16),
        ],
        scratch_shapes=[
            pltpu.VMEM((width, 2 * half), BF16),
            pltpu.VMEM((width, 2 * half), BF16),
            pltpu.VMEM((2 * half, width), BF16),
            pltpu.VMEM((4, 4) + mask.shape, F32),
            pltpu.VMEM((4 * rows, width), BF16),
            pltpu.VMEM((4 * rows, width), BF16),
            pltpu.VMEM((2, 2 * half, tokens), BF16),
            pltpu.VMEM((2 * half, tokens), BF16),
            pltpu.VMEM((4 * rows, 2 * half), BF16),
            pltpu.VMEM((4 * rows, 2 * half), BF16),
            pltpu.VMEM((4 * rows, 2 * half), BF16),
            pltpu.VMEM((4 * rows, width), BF16),
            pltpu.VMEM((4, 4, 8, rows), F32),
            pltpu.VMEM((2, 2, tile, half), F32),
            pltpu.VMEM((half, tile), F32),
        ]
        + collect_buffers(rows, width)
        + COLLECT_SEMS
        + [
            dma((3,)), dma((3,)), dma((3,)), dma((3,)), dma((4, 2)), dma((4,)),
            dma((2,)), dma((2, 2)), dma((2, width // tile)), dma((2, 2)), dma((2, 3)),
            dma((15,)), dma((4, 4)),
        ]
        + SPREAD_SEMS * 2,
        compiler_params=pltpu.CompilerParams(
            collective_id=collective_id, has_side_effects=True, vmem_limit_bytes=61 * 2**20
        ),
        cost_estimate=pl.CostEstimate(
            flops=18 * 2 * tokens * width * half,
            bytes_accessed=2**26,
            transcendentals=2 * tokens * half,
        ),
    )(normed, grads_all, mask, gate_half, up_half, down_half, router)
    return got[1], got[2], got[3], got[4:7]


def project_kernel(
    hidden, gain, weights, out_weights, q_gain, k_gain, cosine, sine,
    normed, all_weights, all_out, qkv, totals, query, keys, values,
    heads, stat, scale_q, scale_k, kept_sem, kept_out_sem, kept_kv_sem,
    stat_send, stat_recv, head_send, head_recv, pair_send, pair_recv, *sems,
):
    here = Here()
    row, col, core = here.row, here.col, here.core
    count = len(SPREAD_SEMS)
    rows, width = hidden.shape
    depth = weights.shape[0]
    part, side = depth // 2, out_weights.shape[0]

    def weight_block(of_row, unused_place, of_core):
        return all_weights.at[pl.ds(pl.multiple_of(of_row * depth + of_core * part, part), part)]

    def out_block(of_row, place, of_core):
        start = pl.multiple_of(place * side + of_core * (side // 2), side // 2)
        return all_out.at[pl.ds(start, side // 2), pl.ds(pl.multiple_of(of_row * side, side), side)]

    def normed_block(unused_row, place, unused_core):
        return normed.at[pl.ds(pl.multiple_of(place * rows, rows), rows)]

    own_weight = weights.at[pl.ds(pl.multiple_of(core * part, part), part)]
    own_out = out_weights.at[pl.ds(pl.multiple_of(core * (side // 2), side // 2), side // 2)]
    spread_w = Spread(here, own_weight, weight_block, part, sems[:count], line=False)
    spread_n = Spread(
        here, normed_block(row, col, core), normed_block, rows, sems[count : 2 * count], plane=False
    )
    spread_o = Spread(here, own_out, out_block, side // 2, sems[2 * count :])
    greet(here.plane_peers() + here.line_peers() + [here.other_core()])
    spread_w.step(0)
    keep = pltpu.make_async_copy(own_weight, weight_block(row, 0, core), kept_sem)
    keep.start()
    keep_out = pltpu.make_async_copy(own_out, out_block(row, col, core), kept_out_sem)
    keep_out.start()

    values_in = hidden[...].astype(F32)
    scale_one = lax.rsqrt(jnp.mean(values_in * values_in, axis=1, keepdims=True) + EPSILON)
    own_rows = pl.ds(pl.multiple_of(col * rows, rows), rows)
    normed[own_rows] = (values_in * scale_one * gain[...].astype(F32)).astype(BF16)
    spread_n.step(0)
    spread_o.step(0)
    spread_w.step(1)
    spread_n.step(1)
    spread_w.step(2)
    spread_n.step(2)
    spread_n.step(3)
    keep.wait()
    for which in range(4):
        spread_w.core_arrived(which, 0)

    columns = 256

    @pl.loop(0, qkv.shape[1] // columns)
    def _(index):
        at = pl.ds(pl.multiple_of(index * columns, columns), columns)
        qkv[:, at] = matmul(normed[...], all_weights[:, at])

    plane = qkv.shape[1] // (3 * HD)
    for kind in range(2):
        square = jnp.zeros((qkv.shape[0], HD), F32)
        for head in range(plane):
            start = (head * 3 + kind) * HD
            raw = qkv[:, start : start + HD]
            square = square + raw * raw
        stat[col, kind : kind + 1] = jnp.sum(square.T, axis=0, keepdims=True)

    def give_stat(step):
        peer = here.line_peers()[step]
        return remote(stat.at[col], stat.at[col], stat_send.at[step], stat_recv.at[col], peer)

    for step in range(3):
        give_stat(step).start()
    spread_o.step(1)
    for step in range(3):
        place = (col + step + 1) % 4
        arrived(stat.at[place], stat_recv.at[place])
    total = stat[0] + stat[1] + stat[2] + stat[3]
    totals[...] = total
    for kind, target in enumerate((scale_q, scale_k)):
        line = lax.rsqrt(total[kind : kind + 1] / width + EPSILON)
        target[...] = jnp.broadcast_to(line, (HD, line.shape[1])).T

    chunk = 64

    @pl.loop(0, qkv.shape[0] // chunk)
    def _(index):
        at = pl.ds(pl.multiple_of(index * chunk, chunk), chunk)
        for head in range(plane):
            for kind, (scales, gains) in enumerate(((scale_q, q_gain), (scale_k, k_gain))):
                raw = qkv[at, pl.ds((head * 3 + kind) * HD, HD)]
                unit = raw * scales[at] * gains[:, head * HD : (head + 1) * HD]
                turned = pltpu.roll(unit, HD // 2, 1)
                heads[head, kind, at] = (unit * cosine[at] + turned * sine[at]).astype(BF16)
            heads[head, 2, at] = qkv[at, pl.ds((head * 3 + 2) * HD, HD)].astype(BF16)

    targets = (query.at[row], keys.at[1, row], values.at[1, row])

    def give_head(step, kind):
        dest = here.rows[step + 1]
        sems = head_send.at[step, kind], head_recv.at[kind, row]
        return remote(heads.at[dest, kind], targets[kind], *sems, here.at_row(dest))

    for kind in (1, 2, 0):
        for step in range(3):
            give_head(step, kind).start()

    def give_pair(source, kind):
        array = (keys, values)[kind]
        sems = pair_send.at[kind, source], pair_recv.at[kind, source]
        return remote(array.at[1, source], array.at[0, source], *sems, here.other_core())

    def keep_pair(source, kind):
        array = (keys, values)[kind]
        return pltpu.make_async_copy(
            array.at[1, source], array.at[0, source], kept_kv_sem.at[kind, source]
        )

    def pair_from(source):
        @pl.when(core == 0)
        def _():
            for kind in range(2):
                give_pair(source, kind).start()
                keep_pair(source, kind).start()

    for kind, array in ((1, keys), (2, values)):
        array[1, row] = heads[row, kind]
    query[row] = heads[row, 0]
    pair_from(row)
    spread_o.step(2)
    for source in here.rows[1:]:
        arrived(keys.at[1, source], head_recv.at[1, source])
        arrived(values.at[1, source], head_recv.at[2, source])
        pair_from(source)
    spread_o.step(3)
    for source in here.rows[1:]:
        arrived(query.at[source], head_recv.at[0, source])
    spread_o.step(4)
    spread_o.step(5)

    @pl.when(core == 0)
    def _():
        for source in range(4):
            for kind in range(2):
                give_pair(source, kind).wait_send()
                keep_pair(source, kind).wait()

    @pl.when(core == 1)
    def _():
        for source in range(4):
            for kind in range(2):
                give_pair(source, kind).wait_recv()

    for step in range(3):
        give_stat(step).wait_send()
        for kind in range(3):
            give_head(step, kind).wait_send()
    keep_out.wait()
    spread_w.finish(arrivals=False)
    spread_n.finish()
    spread_o.finish()


def project(hidden, gain, weights, out_weights, q_gain, k_gain, cosine, sine, collective_id):
    rows, width = hidden.shape
    depth, columns = weights.shape
    row_tok = 4 * rows
    plane = columns // (3 * HD)
    vmem = pl.BlockSpec(memory_space=pltpu.VMEM)
    hbm = pl.BlockSpec(memory_space=pl.ANY)
    return pl.pallas_call(
        project_kernel,
        in_specs=[vmem, vmem, hbm, hbm, vmem, vmem, vmem, vmem],
        out_specs=[vmem, vmem, hbm, vmem, vmem, vmem, vmem, vmem],
        out_shape=[
            jax.ShapeDtypeStruct((row_tok, width), BF16),
            jax.ShapeDtypeStruct((4 * depth, columns), BF16),
            jax.ShapeDtypeStruct((width, width), BF16),
            jax.ShapeDtypeStruct((row_tok, columns), F32),
            jax.ShapeDtypeStruct((8, row_tok), F32),
            jax.ShapeDtypeStruct((4, row_tok, HD), BF16),
            jax.ShapeDtypeStruct((2, 4, row_tok, HD), BF16),
            jax.ShapeDtypeStruct((2, 4, row_tok, HD), BF16),
        ],
        scratch_shapes=[
            pltpu.VMEM((plane, 3, row_tok, HD), BF16),
            pltpu.VMEM((4, 8, row_tok), F32),
            pltpu.VMEM((row_tok, HD), F32),
            pltpu.VMEM((row_tok, HD), F32),
            pltpu.SemaphoreType.DMA,
            pltpu.SemaphoreType.DMA,
            pltpu.SemaphoreType.DMA((2, 4)),
            pltpu.SemaphoreType.DMA((3,)),
            pltpu.SemaphoreType.DMA((4,)),
            pltpu.SemaphoreType.DMA((3, 3)),
            pltpu.SemaphoreType.DMA((3, 4)),
            pltpu.SemaphoreType.DMA((2, 4)),
            pltpu.SemaphoreType.DMA((2, 4)),
        ]
        + SPREAD_SEMS * 3,
        compiler_params=pltpu.CompilerParams(
            collective_id=collective_id, has_side_effects=True, vmem_limit_bytes=56 * 2**20
        ),
    )(hidden, gain[None], weights, out_weights, q_gain, k_gain, cosine, sine)


class PairSum:
    def __init__(self, here, values, out, held, got, send, recv):
        self.here, self.values, self.out, self.held, self.got = here, values, out, held, got
        self.send, self.recv = send, recv
        col, half = here.col, values.shape[1] // 2
        self.own = pl.ds(pl.multiple_of(here.core * half, half), half)
        self.others = pl.ds(pl.multiple_of((1 - here.core) * half, half), half)
        self.peers = [
            here.at_row(here.across),
            here.at_row(here.along),
            here.at_col(col + 1 - 2 * (col % 2)),
            here.at_col((col + 2) % 4),
        ]

    def copy(self, step):
        here, sems = self.here, (self.send.at[step], self.recv.at[step])
        if step == 0:
            return remote(self.values.at[:, self.others], self.got.at[0], *sems, here.other_core())
        if step == 5:
            return remote(self.held.at[4], self.out.at[:, self.own], *sems, here.other_core())
        return remote(self.held.at[step - 1], self.got.at[step], *sems, self.peers[step - 1])

    def begin(self):
        self.copy(0).start()

    def step(self, index):
        if index == 5:
            arrived(self.out.at[:, self.others], self.recv.at[5])
            return
        self.copy(index).wait_recv()
        before = self.values[:, self.own] if index == 0 else self.held[index - 1]
        self.held[index] = before + self.got[index]
        if index == 4:
            self.out[:, self.own] = self.held[4]
        self.copy(index + 1).start()

    def finish(self):
        for index in range(6):
            self.copy(index).wait_send()


def pair_sum_buffers(rows, width):
    return [
        pltpu.VMEM((5, rows, width // 2), F32),
        pltpu.VMEM((5, rows, width // 2), F32),
        pltpu.SemaphoreType.DMA((6,)),
        pltpu.SemaphoreType.DMA((6,)),
    ]


def back_kernel(
    scale, cuts, d_attn, query, keys, keys_t, values, mixed, total, out_weights, out_parts, early,
    d_attn_row, d_heads, mixed_rows, out_total, early_sum,
    weights, d_mixed_give, d_mixed_row, d_mixed, mixed_low, d_keys, d_values, acc, pair_out, pair_in,
    head_give, sum_held, sum_got, sum_send, sum_recv, weight_sem, load_sem,
    near_send, near_recv, head_send, head_recv, mixed_send, mixed_recv, back_send, back_recv,
    pair_send, pair_recv, *rest,
):
    here = Here()
    row, col, core = here.row, here.col, here.core
    rows = d_attn.shape[0]
    row_tok = 4 * rows
    group_tok = 4 * row_tok
    plane = 4 * HD
    order = here.near_first[::-1]
    collect = Collect(here, rest[:6], rest[6 : 6 + len(COLLECT_SEMS)])
    sems = rest[6 + len(COLLECT_SEMS) :]

    def row_block(unused_row, place, unused_core):
        return d_attn_row.at[pl.ds(pl.multiple_of(place * rows, rows), rows)]

    spread = Spread(here, row_block(row, col, core), row_block, rows, sems, plane=False)
    pair_sum = PairSum(here, early, early_sum, sum_held, sum_got, sum_send, sum_recv)

    def load(which, place):
        return pltpu.make_async_copy(
            out_parts.at[which, place], collect.mine.at[which, place], load_sem.at[which, place]
        )

    load_weights = pltpu.make_async_copy(out_weights, weights, weight_sem)
    load_weights.start()
    for place in order:
        for which in (3, 2, 1, 0):
            load(which, place).start()
    mixed_low[...] = mixed[...].astype(BF16)
    d_attn_row[pl.ds(pl.multiple_of(col * rows, rows), rows)] = d_attn[...]
    greet(here.plane_peers() + here.line_peers() + [here.other_core()])

    def give_near(step):
        place = (col + step) % 4
        sems_of = near_send.at[step], near_recv.at[col]
        return remote(d_mixed_give.at[place], d_mixed_row.at[col], *sems_of, here.at_col(place))

    def give_head(step):
        dest = here.rows[step]
        part = pl.ds(pl.multiple_of(dest * HD, HD), HD)
        sems_of = head_send.at[step], head_recv.at[row]
        return remote(d_mixed_row.at[:, :, part], d_mixed.at[row], *sems_of, here.at_row(dest))

    def give_mixed(step):
        dest = here.rows[step]
        part = pl.ds(pl.multiple_of(dest * row_tok, row_tok), row_tok)
        sems_of = mixed_send.at[step], mixed_recv.at[row]
        return remote(mixed_low.at[part], mixed_rows.at[row], *sems_of, here.at_row(dest))

    pair_sum.begin()
    load_weights.wait()
    for step in (1, 2, 3, 0):
        place = (col + step) % 4
        part = pl.ds(pl.multiple_of(place * plane, plane), plane)
        product = contract_cols(d_attn[...], weights[part]).astype(BF16)
        if step == 0:
            d_mixed_row[col] = product
        else:
            d_mixed_give[place] = product
            give_near(step).start()
    spread.step(0)
    for which in (3, 2, 1):
        load(which, order[0]).wait()
    collect.start_far(order[0])
    collect.start_near(order[0])
    pair_sum.step(0)
    for step in range(1, 4):
        place = (col + 4 - step) % 4
        arrived(d_mixed_row.at[place], near_recv.at[place])
    for step in range(1, 4):
        give_head(step).start()
    d_mixed[row] = d_mixed_row[:, :, pl.ds(pl.multiple_of(row * HD, HD), HD)]
    for step in range(1, 4):
        give_mixed(step).start()
    mixed_rows[row] = mixed_low[pl.ds(pl.multiple_of(row * row_tok, row_tok), row_tok)]
    for place in order[1:]:
        for which in (3, 2, 1):
            load(which, place).wait()
        collect.start_far(place)
        collect.start_near(place)
    pair_sum.step(1)
    spread.step(1)
    d_keys[...] = jnp.zeros_like(d_keys)
    d_values[...] = jnp.zeros_like(d_values)
    for source in here.rows[1:]:
        arrived(d_mixed.at[source], head_recv.at[source])

    cut = (cuts[0, 0], cuts[0, 1])
    last_query = 2 * group_tok - row_tok

    def queries(start, stop):
        @pl.loop(start, stop)
        def _(index):
            at = pl.ds(pl.multiple_of(index * row_tok, row_tok), row_tok)
            first_query = core * group_tok + index * row_tok
            gradient = d_mixed[index].reshape(row_tok, HD)
            delta = jnp.sum((gradient.astype(F32) * mixed[at]).T, axis=0, keepdims=True)
            sums = total[:, at]
            acc[...] = jnp.zeros_like(acc)

            def block_fn(part, scores):
                weight = jnp.exp(scores - sums)
                d_weight = contract_cols(values[part], gradient)
                d_scores = (weight * (d_weight - delta)).astype(BF16)
                d_values[part] += matmul(weight.astype(BF16), gradient)
                d_keys[part] += matmul(d_scores, query[at]) * scale
                acc[...] += matmul(keys_t[:, part], d_scores)

            def scan(block, carry):
                first_key = block * row_tok
                part = pl.ds(pl.multiple_of(first_key, row_tok), row_tok)
                masked = (block == 0) | (first_key == first_query) | (first_query == last_query)

                @pl.when(jnp.logical_not(masked))
                def _():
                    block_fn(part, contract_cols(keys[part], query[at]) * scale)

                @pl.when(masked)
                def _():
                    key_place = first_key + lax.broadcasted_iota(jnp.int32, (row_tok, row_tok), 0)
                    place = first_query + lax.broadcasted_iota(jnp.int32, (1, row_tok), 1)
                    allowed = (key_place <= place) & (key_place >= doc_start(place, cut))
                    scores = contract_cols(keys[part], query[at]) * scale
                    block_fn(part, jnp.where(allowed, scores, MASKED))

                return carry

            lax.fori_loop(0, core * 4 + index + 1, scan, 0)
            head_give[0, index] = (acc[...] * scale).T.astype(BF16)

    queries(0, 2)
    pair_sum.step(2)
    spread.step(2)
    collect.corner_step(order[0])
    queries(2, 4)

    def give_back(step, kind):
        dest = here.rows[step]
        sems_of = back_send.at[step, kind], back_recv.at[kind, row]
        return remote(head_give.at[kind, dest], d_heads.at[row, kind], *sems_of, here.at_row(dest))

    def give_pair(kind):
        sems_of = pair_send.at[kind], pair_recv.at[kind]
        return remote(pair_out.at[kind], pair_in.at[kind], *sems_of, here.other_core())

    for step in range(1, 4):
        give_back(step, 0).start()
    d_heads[row, 0] = head_give[0, row]

    @pl.when(core == 1)
    def _():
        for kind, gradient in enumerate((d_keys, d_values)):
            pair_out[kind] = gradient[pl.ds(0, group_tok)].astype(BF16)
            give_pair(kind).start()
        for kind, gradient in enumerate((d_keys, d_values)):
            for part in range(4):
                at = pl.ds(group_tok + part * row_tok, row_tok)
                head_give[kind + 1, part] = gradient[at].astype(BF16)

    collect.corner_step(order[1])

    @pl.when(core == 0)
    def _():
        for kind, gradient in enumerate((d_keys, d_values)):
            give_pair(kind).wait_recv()
            for part in range(4):
                at = pl.ds(part * row_tok, row_tok)
                summed = gradient[at] + pair_in[kind, at].astype(F32)
                head_give[kind + 1, part] = summed.astype(BF16)

    for kind in (1, 2):
        for step in range(1, 4):
            give_back(step, kind).start()
        d_heads[row, kind] = head_give[kind, row]
    pair_sum.step(3)
    spread.step(3)

    def line_part(place):
        load(0, place).wait()
        collect.plane_step(place)
        collect.line_step(place)

    line_part(order[0])
    collect.corner_step(order[2])
    pair_sum.step(4)
    line_part(order[1])
    collect.corner_step(order[3])
    line_part(order[2])
    line_part(order[3])
    pair_sum.step(5)
    collect.own_step()
    out_total[...] = collect.mine[0, col]
    for source in here.rows[1:]:
        arrived(mixed_rows.at[source], mixed_recv.at[source])
        for kind in range(3):
            arrived(d_heads.at[source, kind], back_recv.at[kind, source])
    for step in range(1, 4):
        give_near(step).wait_send()
        give_head(step).wait_send()
        give_mixed(step).wait_send()
        for kind in range(3):
            give_back(step, kind).wait_send()

    @pl.when(core == 1)
    def _():
        for kind in range(2):
            give_pair(kind).wait_send()

    pair_sum.finish()
    spread.finish()
    collect.finish()


def attend_back_stage(
    d_attn, query, keys, values, mixed, total, cuts, out_weights, out_parts, early, scale, collective_id
):
    rows, width = d_attn.shape
    row_tok, group_tok = 4 * rows, 16 * rows
    vmem, hbm = pl.BlockSpec(memory_space=pltpu.VMEM), pl.BlockSpec(memory_space=pl.ANY)
    dma = pltpu.SemaphoreType.DMA
    return pl.pallas_call(
        functools.partial(back_kernel, scale),
        in_specs=[pl.BlockSpec(memory_space=pltpu.SMEM)] + [vmem] * 7 + [hbm] * 2 + [vmem],
        out_specs=[vmem] * 5,
        out_shape=[
            jax.ShapeDtypeStruct((row_tok, width), BF16),
            jax.ShapeDtypeStruct((4, 3, row_tok, HD), BF16),
            jax.ShapeDtypeStruct((4, row_tok, HD), BF16),
            jax.ShapeDtypeStruct((rows, width), BF16),
            jax.ShapeDtypeStruct(early.shape, F32),
        ],
        scratch_shapes=[
            pltpu.VMEM((width, width), BF16),
            pltpu.VMEM((4, rows, 4 * HD), BF16),
            pltpu.VMEM((4, rows, 4 * HD), BF16),
            pltpu.VMEM((4, 4, rows, HD), BF16),
            pltpu.VMEM((group_tok, HD), BF16),
            pltpu.VMEM((2 * group_tok, HD), F32),
            pltpu.VMEM((2 * group_tok, HD), F32),
            pltpu.VMEM((HD, row_tok), F32),
            pltpu.VMEM((2, group_tok, HD), BF16),
            pltpu.VMEM((2, group_tok, HD), BF16),
            pltpu.VMEM((3, 4, row_tok, HD), BF16),
        ]
        + pair_sum_buffers(*early.shape)
        + [
            dma, dma((4, 4)), dma((4,)), dma((4,)), dma((4,)), dma((4,)), dma((4,)), dma((4,)),
            dma((4, 3)), dma((3, 4)), dma((2,)), dma((2,)),
        ]
        + collect_buffers(rows, width)
        + COLLECT_SEMS
        + SPREAD_SEMS,
        compiler_params=pltpu.CompilerParams(
            collective_id=collective_id, has_side_effects=True, vmem_limit_bytes=58 * 2**20
        ),
    )(cuts[None], d_attn, query, keys, keys.T, values, mixed, total, out_weights, out_parts, early)


def tail_kernel(
    d_heads, qkv, totals, q_gain, k_gain, cosine, sine, weights, normed, mixed_rows, d_attn,
    hidden, gain, d_middle,
    grad_hidden, grad_qkv, grad_out, late_sum,
    d_qkv, late, grads, mixed, units, stat, scales, sums, sum_held, sum_got, sum_send, sum_recv,
    stat_send, stat_recv,
    line, line_in, whole, give, other, plane, corner_one, corner_two, from_across, from_along,
    up_send, down_send, line_recv, other_send, other_recv,
    one_send, one_recv, two_send, two_recv, across_send, across_recv, along_send, along_recv,
    back_send, back_recv,
):
    here = Here()
    row, col, core = here.row, here.col, here.core
    rows = hidden.shape[0]
    depth, columns = grads.shape
    part = depth // 2
    first, second = pl.ds(0, part // 2), pl.ds(part // 2, part // 2)
    order = here.near_first[::-1]
    qkv_columns = d_qkv.shape[1]
    tile = 512

    def line_products():
        @pl.loop(0, weights.shape[0] // tile)
        def _(index):
            at = pl.ds(pl.multiple_of(index * tile, tile), tile)
            product = contract_cols(d_qkv[...], weights[at]).astype(BF16)
            line[:, :, at] = product.reshape(4, rows, tile)

    def give_up(place):
        sems = up_send.at[place], line_recv.at[place]
        return remote(line.at[place], line_in.at[place], *sems, here.at_col(col + 1))

    def give_down(place, slot):
        sems = down_send.at[place], line_recv.at[slot]
        return remote(line.at[place], line_in.at[slot], *sems, here.at_col(col - 1))

    def line_step(place):
        @pl.when((place > col) & (col > 0))
        def _():
            give_up(place).wait_recv()
            add_into(line.at[place], line_in.at[place])

        @pl.when((place < col) & (col < 3))
        def _():
            give_down(place, place).wait_recv()
            add_into(line.at[place], line_in.at[place])

        @pl.when(place > col)
        def _():
            give_up(place).start()

        @pl.when(place < col - 1)
        def _():
            give_down(place, place).start()

        @pl.when(place == col - 1)
        def _():
            give_down(place, 4).start()

    def row_product(which):
        of_row = here.rows[which]
        at = pl.ds(pl.multiple_of(of_row * depth, depth), depth)
        whole[:, pl.ds(0, qkv_columns)] = transposed_product(normed[:, at], d_qkv[...]).astype(BF16)
        whole[:, pl.ds(qkv_columns, columns - qkv_columns)] = transposed_product(
            mixed[...], d_attn[:, at]
        ).astype(BF16)
        plane[which] = whole[pl.ds(pl.multiple_of(core * part, part), part)]
        give[which] = whole[pl.ds(pl.multiple_of((1 - core) * part, part), part)]
        to_core(which).start()

    def to_core(which):
        sems = other_send.at[which], other_recv.at[which]
        return remote(give.at[which], other.at[which], *sems, here.other_core())

    def own_sum(which):
        to_core(which).wait_recv()
        add_into(plane.at[which], other.at[which])

    give_one = remote(
        plane.at[3, first], corner_one, one_send, one_recv, here.at_row(here.across)
    )
    give_two = remote(
        plane.at[3, second], corner_two, two_send, two_recv, here.at_row(here.along)
    )

    def give_across(index):
        at = (first, second)[index]
        sems = across_send.at[index], across_recv.at[index]
        return remote(plane.at[1, at], from_across.at[at], *sems, here.at_row(here.across))

    def give_along(index):
        at = (first, second)[index]
        sems = along_send.at[index], along_recv.at[index]
        return remote(plane.at[2, at], from_along.at[at], *sems, here.at_row(here.along))

    pair_sum = PairSum(here, late, late_sum, sum_held, sum_got, sum_send, sum_recv)
    greet(here.plane_peers() + here.line_peers() + [here.other_core()])

    width = hidden.shape[1]
    heads = d_heads.shape[0]
    row_tok = d_qkv.shape[0]
    late[...] = jnp.zeros_like(late)
    for kind in range(2):
        root = lax.rsqrt(totals[kind : kind + 1] / width + EPSILON)
        scales[kind] = jnp.broadcast_to(root, (HD, row_tok)).T
        square = jnp.zeros((row_tok, HD), F32)
        for head in range(heads):
            start = (head * 3 + kind) * HD
            raw = qkv[:, start : start + HD]
            given = d_heads[head, kind].astype(F32)
            unit = given * cosine[...] + pltpu.roll(given * sine[...], HD // 2, 1)
            gains = (q_gain, k_gain)[kind][:, head * HD : (head + 1) * HD]
            gain_sum = jnp.sum(unit * raw * scales[kind], axis=0, keepdims=True)
            place = pl.ds(pl.multiple_of((col * heads + head) * HD, HD), HD)
            late[kind + 1 : kind + 2, place] = gain_sum
            weighted = unit * gains
            square = square + weighted * raw
            units[kind, head] = weighted
        stat[col, kind : kind + 1] = jnp.sum(square.T, axis=0, keepdims=True)

    def give_stat(step):
        peer = here.line_peers()[step]
        return remote(stat.at[col], stat.at[col], stat_send.at[step], stat_recv.at[col], peer)

    for step in range(3):
        give_stat(step).start()
    for head in range(heads):
        d_qkv[:, (head * 3 + 2) * HD : (head * 3 + 3) * HD] = d_heads[head, 2]
        mixed[:, head * HD : (head + 1) * HD] = mixed_rows[head]
    for step in range(3):
        place = (col + step + 1) % 4
        arrived(stat.at[place], stat_recv.at[place])
    total = stat[0] + stat[1] + stat[2] + stat[3]
    for kind in range(2):
        sums[...] = jnp.broadcast_to(total[kind : kind + 1] / width, (HD, row_tok)).T
        for head in range(heads):
            start = (head * 3 + kind) * HD
            raw = qkv[:, start : start + HD]
            root = scales[kind]
            d_raw = root * units[kind, head] - raw * (root * root * root) * sums[...]
            d_qkv[:, start : start + HD] = d_raw.astype(BF16)
    ends = (col == 0) | (col == 3)
    line_products()

    @pl.when(ends)
    def _():
        for place in order[:3]:
            line_step(place)

    def inner_step(place):
        @pl.when(jnp.logical_not(ends))
        def _():
            line_step(place)

    row_product(3)
    row_product(1)
    inner_step(order[0])
    own_sum(3)
    give_one.start()
    give_two.start()
    row_product(2)
    own_sum(1)
    give_across(0).start()
    own_sum(2)
    give_along(1).start()
    inner_step(order[1])
    row_product(0)
    inner_step(order[2])
    give_two.wait_recv()
    add_into(plane.at[1, second], corner_two)
    give_across(1).start()
    give_one.wait_recv()
    add_into(plane.at[2, first], corner_one)
    give_along(0).start()
    own_sum(0)

    @pl.when(col > 0)
    def _():
        give_up(col).wait_recv()
        add_into(line.at[col], line_in.at[col])

    @pl.when(col < 3)
    def _():
        give_down(col, 4).wait_recv()
        add_into(line.at[col], line_in.at[4])

    given = line[col].astype(F32)
    tokens = hidden[...].astype(F32)
    root = lax.rsqrt(jnp.mean(tokens * tokens, axis=1, keepdims=True) + EPSILON)
    late[0:1] = jnp.sum(given * tokens * root, axis=0, keepdims=True)
    pair_sum.begin()
    weighted = given * gain[...].astype(F32)
    inner = jnp.mean(weighted * tokens, axis=1, keepdims=True)
    grad_hidden[...] = d_middle[...] + root * weighted - tokens * (root * root * root) * inner
    pair_sum.step(0)
    for index in range(2):
        give_across(index).wait_recv()
        give_along(index).wait_recv()
    add_into(plane.at[0], from_across, from_along)
    pair_sum.step(1)
    own_half = pl.ds(pl.multiple_of(core * part, part), part)
    give_back = remote(
        plane.at[0], grads.at[own_half], back_send, back_recv, here.other_core()
    )
    give_back.start()
    grads[own_half] = plane[0]
    other_half = grads.at[pl.ds(pl.multiple_of((1 - core) * part, part), part)]
    pair_sum.step(2)
    arrived(other_half, back_recv)
    grad_qkv[...] = grads[:, pl.ds(0, qkv_columns)].astype(F32)
    grad_out[...] = grads[:, pl.ds(qkv_columns, columns - qkv_columns)].astype(F32)
    for index in (3, 4, 5):
        pair_sum.step(index)
    pair_sum.finish()
    for step in range(3):
        give_stat(step).wait_send()
    give_back.wait_send()
    give_one.wait_send()
    give_two.wait_send()
    for index in range(2):
        give_across(index).wait_send()
        give_along(index).wait_send()
    for which in range(4):
        to_core(which).wait_send()
    for place in order:

        @pl.when(place > col)
        def _():
            give_up(place).wait_send()

        @pl.when(place < col)
        def _():
            give_down(place, place).wait_send()


def tail_stage(
    d_heads, qkv, totals, q_gain, k_gain, cosine, sine, weights, normed, mixed_rows, d_attn,
    hidden, gain, d_middle, collective_id,
):
    row_tok, qkv_columns = qkv.shape
    rows, width = hidden.shape
    depth = width // 4
    out_columns = width // 4
    columns = qkv_columns + out_columns
    part = depth // 2
    heads = d_heads.shape[0]
    vmem = pl.BlockSpec(memory_space=pltpu.VMEM)
    one, four = pltpu.SemaphoreType.DMA, pltpu.SemaphoreType.DMA((4,))
    two, five = pltpu.SemaphoreType.DMA((2,)), pltpu.SemaphoreType.DMA((5,))
    three = pltpu.SemaphoreType.DMA((3,))
    return pl.pallas_call(
        tail_kernel,
        in_specs=[vmem] * 14,
        out_specs=[vmem] * 4,
        out_shape=[
            jax.ShapeDtypeStruct((rows, width), F32),
            jax.ShapeDtypeStruct((depth, qkv_columns), F32),
            jax.ShapeDtypeStruct((depth, out_columns), F32),
            jax.ShapeDtypeStruct((8, width), F32),
        ],
        scratch_shapes=[
            pltpu.VMEM((row_tok, qkv_columns), BF16),
            pltpu.VMEM((8, width), F32),
            pltpu.VMEM((depth, columns), BF16),
            pltpu.VMEM((row_tok, heads * HD), BF16),
            pltpu.VMEM((2, heads, row_tok, HD), F32),
            pltpu.VMEM((4, 8, row_tok), F32),
            pltpu.VMEM((2, row_tok, HD), F32),
            pltpu.VMEM((row_tok, HD), F32),
        ]
        + pair_sum_buffers(8, width)
        + [
            three, four,
            pltpu.VMEM((4, rows, width), BF16),
            pltpu.VMEM((5, rows, width), BF16),
            pltpu.VMEM((depth, columns), BF16),
            pltpu.VMEM((4, part, columns), BF16),
            pltpu.VMEM((4, part, columns), BF16),
            pltpu.VMEM((4, part, columns), BF16),
            pltpu.VMEM((part // 2, columns), BF16),
            pltpu.VMEM((part // 2, columns), BF16),
            pltpu.VMEM((part, columns), BF16),
            pltpu.VMEM((part, columns), BF16),
            four, four, five, four, four,
            one, one, one, one, two, two, two, two,
            one, one,
        ],
        compiler_params=pltpu.CompilerParams(
            collective_id=collective_id, has_side_effects=True, vmem_limit_bytes=58 * 2**20
        ),
    )(
        d_heads, qkv, totals, q_gain, k_gain, cosine, sine, weights, normed, mixed_rows, d_attn,
        hidden, gain[None], d_middle,
    )


def expert_rows(rows, grads, gate, gate_w, up_w, down_w):
    pre_gate = matmul(rows, gate_w)
    pre_up = matmul(rows, up_w)
    back = contract_cols(grads, down_w)
    sigmoid_gate = jax.nn.sigmoid(pre_gate)
    silu_gate = pre_gate * sigmoid_gate
    hidden = (silu_gate * pre_up).astype(BF16)
    inner = jnp.sum(hidden.astype(F32) * back, axis=-1)
    weighted = (hidden.astype(F32) * gate).astype(BF16)
    d_hid = back * gate
    d_pregate = (d_hid * pre_up * (sigmoid_gate + silu_gate * (1.0 - sigmoid_gate))).astype(BF16)
    d_preup = (d_hid * silu_gate).astype(BF16)
    outputs = matmul(weighted, down_w).astype(BF16)
    d_rows = (contract_cols(d_pregate, gate_w) + contract_cols(d_preup, up_w)).astype(BF16)
    return (
        outputs,
        d_rows,
        inner,
        contract_rows(rows, d_pregate),
        contract_rows(rows, d_preup),
        contract_rows(weighted, grads),
    )


def experts(normed, grads, dense_gates, gate_w, up_w, down_w):
    rows_dev, width = normed.shape
    devices = math.prod(lax.axis_size(axis) for axis in ALL)
    expert_count = dense_gates.shape[1]
    expert = lax.axis_index(ALL) // 2
    parts = max(1, lax.axis_size("exp") // 2)
    step = rows_dev // parts

    def one_part(sums, piece):
        rows, grad_rows, gates = piece
        rows_all = lax.all_gather(rows, ALL, axis=0, tiled=True)
        grads_all = lax.all_gather(grad_rows, ALL, axis=0, tiled=True)
        gates_all = lax.all_gather(gates, ALL, axis=0, tiled=True)
        gate = lax.dynamic_slice_in_dim(gates_all, expert, 1, 1)
        got = expert_rows(rows_all, grads_all, gate, gate_w, up_w, down_w)
        outputs = lax.psum_scatter(got[0], ALL, scatter_dimension=0, tiled=True)
        d_rows = lax.psum_scatter(got[1], ALL, scatter_dimension=0, tiled=True)
        inner = lax.all_to_all(
            got[2].reshape(devices, step), ALL, split_axis=0, concat_axis=0, tiled=True
        )
        inner = inner.reshape(expert_count, 2, step).sum(axis=1).T
        sums = got[3:] if sums is None else tuple(a + b for a, b in zip(sums, got[3:]))
        return sums, (outputs, d_rows, inner)

    if parts == 1:
        sums, (outputs, d_rows, inner) = one_part(None, (normed, grads, dense_gates))
    else:
        start = tuple(jnp.zeros(w.shape, F32) for w in (gate_w, up_w, down_w))
        pieces = tuple(v.reshape(parts, step, -1) for v in (normed, grads, dense_gates))
        sums, got = lax.scan(one_part, start, pieces)
        outputs, d_rows, inner = (v.reshape(rows_dev, -1) for v in got)
    return outputs.astype(F32), d_rows.astype(F32), inner, sums


def experts_here(normed, grads_all, picks, router, gate_w, up_w, down_w):
    numbers = jnp.arange(router.shape[1], dtype=jnp.int32)
    mask = jnp.any(picks.T[None] == numbers[:, None, None], axis=1).astype(F32)
    out_parts, d_rows, inner, weights = expert_stage(
        normed, grads_all, mask, gate_w, up_w, down_w, router, 1
    )
    inner = inner[:, :, 0].reshape(router.shape[1], -1).T
    return out_parts, d_rows.astype(F32), inner, weights


def shards(
    hidden_in,
    out_grad,
    attn_gain,
    w_qkv,
    q_gain,
    k_gain,
    w_out,
    moe_gain,
    router,
    w_gate,
    w_up,
    w_down,
    routes,
    doc_cuts,
):
    row_count, col_count = lax.axis_size("row"), lax.axis_size("col")
    tokens = hidden_in[0].astype(F32)
    rows_dev, width = tokens.shape
    heads = w_qkv.shape[1] // (3 * HD)
    plane = heads * HD
    scale = HD ** (-0.5)
    side = lax.axis_index("exp") % 2
    row_tok = rows_dev * col_count
    group_tok = row_tok * row_count
    cuts = lax.dynamic_index_in_dim(doc_cuts, lax.axis_index("exp") // 2, 0, keepdims=False)

    here = (row_count, col_count, lax.axis_size("exp")) == (4, 4, 2)

    if here:
        grads_all = lax.all_gather(out_grad[0], ("row", "col"), axis=0, tiled=True)

    gain_one = attn_gain.astype(F32)
    scale_one = rms_scale(tokens)
    head_start = lax.axis_index("col") * plane
    gain_q = lax.dynamic_slice_in_dim(q_gain, head_start, plane, 0).astype(F32)
    gain_k = lax.dynamic_slice_in_dim(k_gain, head_start, plane, 0).astype(F32)
    row_places = side * group_tok + lax.axis_index("row") * row_tok + jnp.arange(row_tok, dtype=jnp.int32)
    unused_doc, position = doc_positions(row_places, cuts)
    cosine, sine = rope_tables(position, HD)
    if here:
        signed = jnp.concatenate([-sine[:, : HD // 2], sine[:, HD // 2 :]], axis=1)
        normed_row, qkv_w, out_w, qkv, totals, query, keys, values = project(
            hidden_in[0], attn_gain, w_qkv, w_out, gain_q[None], gain_k[None], cosine, signed, 0
        )
        total_q, total_k = totals[0], totals[1]
        query = query.reshape(group_tok, HD)
        key_all, value_all = keys.reshape(-1, HD), values.reshape(-1, HD)
    else:
        normed_one = (tokens * scale_one * gain_one).astype(BF16)
        normed_row = lax.all_gather(normed_one, "col", axis=0, tiled=True)
        qkv_w = lax.all_gather(w_qkv, "row", axis=0, tiled=True)
        out_w = lax.all_gather(
            lax.all_gather(w_out, "row", axis=1, tiled=True), "col", axis=0, tiled=True
        )
        qkv = matmul(normed_row, qkv_w)
    qkv = qkv.reshape(row_tok, heads, 3, HD)
    query_raw, key_raw, value_raw = qkv[:, :, 0], qkv[:, :, 1], qkv[:, :, 2]
    if not here:
        total_q, total_k = lax.psum(
            (jnp.sum(query_raw * query_raw, axis=(1, 2)), jnp.sum(key_raw * key_raw, axis=(1, 2))),
            "col",
        )
    scale_q = lax.rsqrt(total_q / width + EPSILON)[:, None, None]
    scale_k = lax.rsqrt(total_k / width + EPSILON)[:, None, None]
    gain_q, gain_k = gain_q.reshape(heads, HD), gain_k.reshape(heads, HD)
    cosine, sine = cosine[:, None, :], sine[:, None, :]
    if not here:
        query = rotate(query_raw * scale_q * gain_q, cosine, sine).astype(BF16)
        key = rotate(key_raw * scale_k * gain_k, cosine, sine).astype(BF16)
        moved = rows_to_heads(jnp.concatenate([query, key, value_raw.astype(BF16)], axis=-1))
        query, own_pair = moved[:, :HD], moved[:, HD:]
        earlier_pair = from_behind(own_pair, "exp", 1)
        lower_pair = jnp.where(side == 0, own_pair, earlier_pair)
        upper_pair = jnp.where(side == 0, jnp.zeros_like(own_pair), own_pair)
        key_value = jnp.concatenate([lower_pair, upper_pair], axis=0)
        key_all, value_all = key_value[:, :HD], key_value[:, HD:]

    mixed_wide, total = attend(query, key_all, value_all, cuts, scale)
    mixed = mixed_wide.astype(BF16)
    middle = tokens + matmul(heads_to_tokens(mixed), out_w)

    gain_two = moe_gain.astype(F32)
    scale_two = rms_scale(middle)
    normed_two = (middle * scale_two * gain_two).astype(BF16)
    gates_all = jax.nn.softmax(matmul(normed_two, router), axis=-1)
    picks = routes[0]
    chosen = jnp.any(
        picks[:, :, None] == jnp.arange(router.shape[1], dtype=jnp.int32)[None, None, :], axis=1
    )
    grad_out = out_grad[0].astype(F32)
    expert_w = (w_gate[0], w_up[0], w_down[0])
    if here:
        out_parts, d_normed_two, inner, weight_grads = experts_here(
            normed_two, grads_all, picks, router, *expert_w
        )
    else:
        dense_gates = jnp.where(chosen, gates_all, 0.0)
        mixture, d_normed_two, inner, weight_grads = experts(
            normed_two, out_grad[0], dense_gates, *expert_w
        )
    dense = jnp.where(chosen, inner, 0.0)
    d_logits = (gates_all * (dense - jnp.sum(gates_all * dense, axis=-1, keepdims=True))).astype(BF16)
    grad_router = contract_rows(d_logits, normed_two)
    d_normed_two = d_normed_two + contract_cols(d_logits, router)
    grad_moe_gain = jnp.sum(d_normed_two * middle * scale_two, axis=0)
    weighted_two = d_normed_two * gain_two
    d_middle = (
        grad_out
        + scale_two * weighted_two
        - middle * scale_two**3 * jnp.mean(weighted_two * middle, axis=-1, keepdims=True)
    )

    d_attn = d_middle.astype(BF16)
    if here:
        early = jnp.concatenate([grad_moe_gain[None], jnp.zeros((7, width), F32), grad_router])
        d_attn_row, d_heads, mixed_rows, mixture, early = attend_back_stage(
            d_attn, query, key_all, value_all, mixed_wide, total, cuts, out_w, out_parts, early, scale, 2
        )
        grad_hidden, grad_qkv, grad_w_out, late = tail_stage(
            d_heads, qkv.reshape(row_tok, -1), totals, gain_q.reshape(1, -1), gain_k.reshape(1, -1),
            cosine[:, 0], signed, qkv_w, normed_row, mixed_rows, d_attn_row,
            hidden_in[0], attn_gain, d_middle, 3,
        )
        final = middle + mixture.astype(F32)
        summed = (late[0], late[1], late[2], early[0], early[8:])
    else:
        final = middle + mixture
        mixed_row = heads_to_rows(mixed).reshape(row_tok, plane)
        d_mixed = tokens_to_heads(contract_cols(d_attn, out_w).astype(BF16))
        d_attn_row = lax.all_gather(d_attn, "col", axis=0, tiled=True)
        d_query, acc_key, acc_value = attend_back(
            query, key_all, value_all, d_mixed, mixed_wide, total, cuts, scale
        )
        accumulated = jnp.concatenate([acc_key, acc_value], axis=1)
        lower_acc, upper_acc = accumulated[:group_tok], accumulated[group_tok:]
        kept_acc = jnp.where(side == 0, lower_acc, upper_acc)
        later_acc = from_behind(lower_acc.astype(BF16), "exp", -1).astype(F32)
        summed_pair = kept_acc + jnp.where(side == 0, later_acc, jnp.zeros_like(later_acc))
        d_heads = heads_to_rows(jnp.concatenate([d_query, summed_pair], axis=1).astype(BF16)).astype(F32)
        d_q_unit = rotate_back(d_heads[:, :, :HD], cosine, sine)
        d_k_unit = rotate_back(d_heads[:, :, HD : 2 * HD], cosine, sine)
        d_value = d_heads[:, :, 2 * HD :]
        weighted_q = d_q_unit * gain_q
        weighted_k = d_k_unit * gain_k
        sum_q, sum_k = lax.psum(
            (jnp.sum(weighted_q * query_raw, axis=(1, 2)), jnp.sum(weighted_k * key_raw, axis=(1, 2))),
            "col",
        )
        d_query_raw = scale_q * weighted_q - query_raw * scale_q**3 * (sum_q / width)[:, None, None]
        d_key_raw = scale_k * weighted_k - key_raw * scale_k**3 * (sum_k / width)[:, None, None]
        grad_q_part = jnp.sum(d_q_unit * query_raw * scale_q, axis=0).reshape(plane)
        grad_k_part = jnp.sum(d_k_unit * key_raw * scale_k, axis=0).reshape(plane)
        d_qkv = jnp.concatenate([d_query_raw, d_key_raw, d_value], axis=2).astype(BF16)
        d_qkv = d_qkv.reshape(row_tok, heads * 3 * HD)
        d_normed_one = lax.psum_scatter(
            contract_cols(d_qkv, qkv_w).astype(BF16), "col", scatter_dimension=0, tiled=True
        ).astype(F32)
        grad_qkv = lax.psum_scatter(
            contract_rows(normed_row, d_qkv).astype(BF16), "row", scatter_dimension=0, tiled=True
        )
        grad_w_out = lax.psum_scatter(
            contract_rows(mixed_row, d_attn_row).astype(BF16), "row", scatter_dimension=1, tiled=True
        )
        grad_qkv = lax.psum(grad_qkv, "exp").astype(F32)
        grad_w_out = lax.psum(grad_w_out, "exp").astype(F32)
        grad_attn_gain = jnp.sum(d_normed_one * tokens * scale_one, axis=0)
        weighted_one = d_normed_one * gain_one
        grad_hidden = (
            d_middle
            + scale_one * weighted_one
            - tokens * scale_one**3 * jnp.mean(weighted_one * tokens, axis=-1, keepdims=True)
        )
        empty = jnp.zeros((width,), F32)
        grad_q_full = lax.dynamic_update_slice_in_dim(empty, grad_q_part, head_start, 0)
        grad_k_full = lax.dynamic_update_slice_in_dim(empty, grad_k_part, head_start, 0)
        parts = (grad_attn_gain, grad_q_full, grad_k_full, grad_moe_gain)
        summed = lax.psum(parts + (grad_router,), ALL)
    return (
        final.astype(BF16)[None],
        grad_hidden[None],
        summed[0],
        grad_qkv,
        summed[1],
        summed[2],
        grad_w_out,
        summed[3],
        summed[4].T,
        weight_grads[0][None],
        weight_grads[1][None],
        weight_grads[2][None],
    )


def solution(mesh):
    token_spec = P("exp", ("row", "col"), None)
    expert_spec = P(("row", "col", "exp"), None, None)
    in_specs = (
        token_spec,
        token_spec,
        P(),
        P("row", "col"),
        P(),
        P(),
        P("col", "row"),
        P(),
        P(),
        expert_spec,
        expert_spec,
        expert_spec,
        token_spec,
        P(),
    )
    out_specs = (
        token_spec,
        token_spec,
        P(),
        P("row", "col"),
        P(),
        P(),
        P("col", "row"),
        P(),
        P(),
        expert_spec,
        expert_spec,
        expert_spec,
    )
    return jax.shard_map(shards, mesh=mesh, in_specs=in_specs, out_specs=out_specs, check_vma=False)
```

```python
import functools
import math

import jax
import jax.numpy as jnp
from jax import lax
from jax.experimental import pallas as pl
from jax.experimental.pallas import tpu as pltpu
from jax.sharding import PartitionSpec as P

HD = 128
EPSILON = 1e-05
ROPE_BASE = 10000.0
MASKED = -1e30
BF16 = jnp.bfloat16
F32 = jnp.float32


def matmul(left, right):
    return jnp.dot(left, right, preferred_element_type=F32)


def contract_rows(left, right):
    return lax.dot_general(left, right, (((0,), (0,)), ((), ())), preferred_element_type=F32)


def contract_cols(left, right):
    return lax.dot_general(left, right, (((1,), (1,)), ((), ())), preferred_element_type=F32)


def rms_scale(values):
    return lax.rsqrt(jnp.mean(values * values, axis=-1, keepdims=True) + EPSILON)


def rope_tables(position, width):
    frequency = ROPE_BASE ** (-jnp.arange(0, width, 2, dtype=F32) / width)
    angle = position.astype(F32)[:, None] * frequency[None, :]
    return (
        jnp.concatenate([jnp.cos(angle)] * 2, axis=-1),
        jnp.concatenate([jnp.sin(angle)] * 2, axis=-1),
    )


def rotate(values, cosine, sine):
    half = values.shape[-1] // 2
    turned = jnp.concatenate([-values[..., half:], values[..., :half]], axis=-1)
    return values * cosine + turned * sine


def rotate_back(values, cosine, sine):
    half = values.shape[-1] // 2
    turned = values * sine
    return values * cosine + jnp.concatenate([turned[..., half:], -turned[..., :half]], axis=-1)


def doc_positions(places, cuts):
    first = (places >= cuts[0]).astype(jnp.int32)
    second = (places >= cuts[1]).astype(jnp.int32)
    start = first * cuts[0] + second * (cuts[1] - cuts[0])
    return (first + second, places - start)


def from_behind(value, axis, steps):
    count = lax.axis_size(axis)
    initial, last = (max(0, -steps), min(count, count - steps))
    return lax.ppermute(value, axis, [(source, source + steps) for source in range(initial, last)])


def rows_to_heads(values):
    count = lax.axis_size("row")
    rows, heads, width = values.shape
    moved = lax.all_to_all(values.transpose(1, 0, 2), "row", split_axis=0, concat_axis=0, tiled=True)
    return moved.reshape(count * rows, width)


def heads_to_rows(values):
    count = lax.axis_size("row")
    rows, width = values.shape
    moved = lax.all_to_all(
        values.reshape(count, rows // count, width), "row", split_axis=0, concat_axis=0, tiled=True
    )
    return moved.transpose(1, 0, 2)


def heads_to_tokens(values):
    row_count, col_count = lax.axis_size("row"), lax.axis_size("col")
    rows = values.shape[0] // (row_count * col_count)
    moved = lax.all_to_all(
        values.reshape(row_count * col_count, rows, HD),
        ("row", "col"),
        split_axis=0,
        concat_axis=0,
        tiled=True,
    )
    moved = moved.reshape(row_count, col_count, rows, HD).transpose(2, 1, 0, 3)
    return moved.reshape(rows, row_count * col_count * HD)


def tokens_to_heads(values):
    row_count, col_count = lax.axis_size("row"), lax.axis_size("col")
    rows = values.shape[0]
    parted = values.reshape(rows, col_count, row_count, HD).transpose(2, 1, 0, 3)
    moved = lax.all_to_all(
        parted.reshape(row_count * col_count, rows, HD),
        ("row", "col"),
        split_axis=0,
        concat_axis=0,
        tiled=True,
    )
    return moved.reshape(row_count * col_count * rows, HD)


MESH = pl.DeviceIdType.MESH
ALL = ("row", "col", "exp")


class Here:
    def __init__(self):
        self.row, self.col, self.core = (lax.axis_index(axis) for axis in ALL)
        self.across = self.row + 1 - 2 * (self.row % 2)
        self.along = (self.row + 2) % 4
        self.opposite = 3 - self.row
        self.rows = (self.row, self.across, self.along, self.opposite)
        half = self.col // 2
        self.near_first = [
            self.col,
            1 + self.col % 2,
            2 - self.col - self.col % 2 + 3 * half,
            3 - 3 * half,
        ]

    def at_row(self, row):
        return (row, self.col, self.core)

    def at_col(self, col):
        return (self.row, col, self.core)

    def other_core(self):
        return (self.row, self.col, 1 - self.core)

    def line_peers(self):
        return [self.at_col((self.col + step) % 4) for step in (1, 2, 3)]

    def group_peers(self):
        steps = range(1, 16)
        return [((self.row + s // 4) % 4, (self.col + s) % 4, self.core) for s in steps]

    def plane_peers(self):
        return [self.at_row(row) for row in self.rows[1:]]


def greet(peers):
    barrier = pltpu.get_barrier_semaphore()
    for peer in peers:
        pl.semaphore_signal(barrier, inc=1, device_id=peer, device_id_type=MESH)
    pl.semaphore_wait(barrier, len(peers))


def greet_near(here):
    barrier = pltpu.get_barrier_semaphore()
    col = here.col

    def signal(peer):
        pl.semaphore_signal(barrier, inc=1, device_id=peer, device_id_type=MESH)

    for peer in (here.other_core(), here.at_row(here.across), here.at_row(here.along)):
        signal(peer)

    @pl.when(col > 0)
    def _():
        signal(here.at_col(col - 1))

    @pl.when(col < 3)
    def _():
        signal(here.at_col(col + 1))

    pl.semaphore_wait(barrier, 3 + (col + 3) // 4 + (6 - col) // 4)


def remote(source, target, send, recv, device):
    return pltpu.make_async_remote_copy(
        src_ref=source,
        dst_ref=target,
        send_sem=send,
        recv_sem=recv,
        device_id=device,
        device_id_type=MESH,
    )


def arrived(target, recv):
    pltpu.make_async_copy(target, target, recv).wait()


def add_into(target, *terms):
    step = 16

    @pl.loop(0, target.shape[0] // step)
    def _(index):
        part = pl.ds(pl.multiple_of(index * step, step), step)
        value = target[part].astype(F32)
        for term in terms:
            value = value + term[part].astype(F32)
        target[part] = value.astype(target.dtype)


SPREAD_SEMS = [pltpu.SemaphoreType.DMA((4,))] * 11 + [pltpu.SemaphoreType.DMA((4, 4))] * 2


class Spread:
    def __init__(self, here, own, block, rows, sems, line=True, plane=True, core=True):
        self.here, self.own, self.block = here, own, block
        self.line, self.plane, self.core = line, plane, core
        (
            self.up_send, self.down_send, self.line_recv,
            self.across_send, self.across_recv, self.along_send, self.along_recv,
            self.one_send, self.one_recv, self.two_send, self.two_recv,
            self.core_send, self.core_recv,
        ) = sems
        self.first, self.second = pl.ds(0, rows // 2), pl.ds(rows // 2, rows // 2)
        self.order = here.near_first if line else [0]
        self.steps = len(self.order)

    def held(self, step):
        here = self.here
        return self.own if step == 0 else self.block(here.row, self.order[step], here.core)

    def up(self, step):
        here, place = self.here, self.order[step]
        target = self.block(here.row, place, here.core)
        recv = self.line_recv.at[place]
        return remote(self.held(step), target, self.up_send.at[place], recv, here.at_col(here.col + 1))

    def down(self, step):
        here, place = self.here, self.order[step]
        target = self.block(here.row, place, here.core)
        recv = self.line_recv.at[place]
        return remote(self.held(step), target, self.down_send.at[place], recv, here.at_col(here.col - 1))

    def to_across(self, step):
        here, place = self.here, self.order[step]
        target = self.block(here.row, place, here.core)
        sems = self.across_send.at[place], self.across_recv.at[place]
        return remote(self.held(step), target, *sems, here.at_row(here.across))

    def to_along(self, step):
        here, place = self.here, self.order[step]
        target = self.block(here.row, place, here.core)
        sems = self.along_send.at[place], self.along_recv.at[place]
        return remote(self.held(step), target, *sems, here.at_row(here.along))

    def corner_one(self, step):
        here, place = self.here, self.order[step]
        part = self.block(here.across, place, here.core).at[self.first]
        sems = self.one_send.at[place], self.one_recv.at[place]
        return remote(part, part, *sems, here.at_row(here.along))

    def corner_two(self, step):
        here, place = self.here, self.order[step]
        part = self.block(here.along, place, here.core).at[self.second]
        sems = self.two_send.at[place], self.two_recv.at[place]
        return remote(part, part, *sems, here.at_row(here.across))

    def to_core(self, which, step):
        here, place = self.here, self.order[step]
        target = self.block(here.rows[which], place, here.core)
        source = self.held(step) if which == 0 else target
        sems = self.core_send.at[which, place], self.core_recv.at[which, place]
        return remote(source, target, *sems, here.other_core())

    def line_step(self, step):
        here, place = self.here, self.order[step]
        if step > 0:
            arrived(self.held(step), self.line_recv.at[place])
        if self.line:

            @pl.when((place <= here.col) & (here.col < 3))
            def _():
                self.up(step).start()

            @pl.when((place >= here.col) & (here.col > 0))
            def _():
                self.down(step).start()

        if self.plane:
            self.to_across(step).start()
            self.to_along(step).start()
            if self.core:
                self.to_core(0, step).start()

    def plane_step(self, step):
        here, place = self.here, self.order[step]
        arrived(self.block(here.across, place, here.core), self.across_recv.at[place])
        self.corner_one(step).start()
        if self.core:
            self.to_core(1, step).start()
        arrived(self.block(here.along, place, here.core), self.along_recv.at[place])
        self.corner_two(step).start()
        if self.core:
            self.to_core(2, step).start()

    def corner_step(self, step):
        here, place = self.here, self.order[step]
        target = self.block(here.opposite, place, here.core)
        arrived(target.at[self.first], self.one_recv.at[place])
        arrived(target.at[self.second], self.two_recv.at[place])
        if self.core:
            self.to_core(3, step).start()

    def step(self, index):
        if index < self.steps:
            self.line_step(index)
        if self.plane and 0 <= index - 1 < self.steps:
            self.plane_step(index - 1)
        if self.plane and 0 <= index - 2 < self.steps:
            self.corner_step(index - 2)

    def core_arrived(self, which, step):
        here, place = self.here, self.order[step]
        target = self.block(here.rows[which], place, 1 - here.core)
        arrived(target, self.core_recv.at[which, place])

    def finish(self, arrivals=True):
        here = self.here
        for step in range(self.steps):
            place = self.order[step]
            if self.line:

                @pl.when((place <= here.col) & (here.col < 3))
                def _():
                    self.up(step).wait_send()

                @pl.when((place >= here.col) & (here.col > 0))
                def _():
                    self.down(step).wait_send()

            if self.plane:
                self.to_across(step).wait_send()
                self.to_along(step).wait_send()
                self.corner_one(step).wait_send()
                self.corner_two(step).wait_send()
                for which in range(4 if self.core else 0):
                    self.to_core(which, step).wait_send()
                    if arrivals:
                        self.core_arrived(which, step)


COLLECT_SEMS = (
    [pltpu.SemaphoreType.DMA((4,))] * 4
    + [pltpu.SemaphoreType.DMA((2, 4))] * 4
    + [pltpu.SemaphoreType.DMA((4,))] * 2
    + [pltpu.SemaphoreType.DMA((5,))]
)


def collect_buffers(rows, width):
    return [
        pltpu.VMEM((4, 4, rows, width), BF16),
        pltpu.VMEM((4, rows // 2, width), BF16),
        pltpu.VMEM((4, rows // 2, width), BF16),
        pltpu.VMEM((4, rows, width), BF16),
        pltpu.VMEM((4, rows, width), BF16),
        pltpu.VMEM((5, rows, width), BF16),
    ]


class Collect:
    def __init__(self, here, buffers, sems):
        self.here = here
        self.mine, self.one, self.two, self.from_across, self.from_along, self.line = buffers
        (
            self.one_send, self.one_recv, self.two_send, self.two_recv,
            self.across_send, self.across_recv, self.along_send, self.along_recv,
            self.up_send, self.down_send, self.line_recv,
        ) = sems
        half = self.mine.shape[2] // 2
        self.halves = (pl.ds(0, half), pl.ds(half, half))

    def give_one(self, place):
        here = self.here
        return remote(
            self.mine.at[3, place, self.halves[0]], self.one.at[place],
            self.one_send.at[place], self.one_recv.at[place], here.at_row(here.across),
        )

    def give_two(self, place):
        here = self.here
        return remote(
            self.mine.at[3, place, self.halves[1]], self.two.at[place],
            self.two_send.at[place], self.two_recv.at[place], here.at_row(here.along),
        )

    def give_across(self, place, half):
        here, part = self.here, self.halves[half]
        return remote(
            self.mine.at[1, place, part], self.from_across.at[place, part],
            self.across_send.at[half, place], self.across_recv.at[half, place], here.at_row(here.across),
        )

    def give_along(self, place, half):
        here, part = self.here, self.halves[half]
        return remote(
            self.mine.at[2, place, part], self.from_along.at[place, part],
            self.along_send.at[half, place], self.along_recv.at[half, place], here.at_row(here.along),
        )

    def give_up(self, place):
        here = self.here
        sems = self.up_send.at[place], self.line_recv.at[place]
        return remote(self.mine.at[0, place], self.line.at[place], *sems, here.at_col(here.col + 1))

    def give_down(self, place, slot):
        here = self.here
        sems = self.down_send.at[place], self.line_recv.at[slot]
        return remote(self.mine.at[0, place], self.line.at[slot], *sems, here.at_col(here.col - 1))

    def start_far(self, place):
        self.give_one(place).start()
        self.give_two(place).start()
        self.give_along(place, 1).start()

    def start_near(self, place):
        self.give_across(place, 0).start()

    def corner_step(self, place):
        self.give_two(place).wait_recv()
        add_into(self.mine.at[1, place, self.halves[1]], self.two.at[place])
        self.give_across(place, 1).start()
        self.give_one(place).wait_recv()
        add_into(self.mine.at[2, place, self.halves[0]], self.one.at[place])
        self.give_along(place, 0).start()

    def plane_step(self, place):
        for half in range(2):
            self.give_across(place, half).wait_recv()
            self.give_along(place, half).wait_recv()
        add_into(self.mine.at[0, place], self.from_across.at[place], self.from_along.at[place])

    def line_step(self, place):
        col = self.here.col

        @pl.when((place > col) & (col > 0))
        def _():
            self.give_up(place).wait_recv()
            add_into(self.mine.at[0, place], self.line.at[place])

        @pl.when((place < col) & (col < 3))
        def _():
            self.give_down(place, place).wait_recv()
            add_into(self.mine.at[0, place], self.line.at[place])

        @pl.when(place > col)
        def _():
            self.give_up(place).start()

        @pl.when(place < col - 1)
        def _():
            self.give_down(place, place).start()

        @pl.when(place == col - 1)
        def _():
            self.give_down(place, 4).start()

    def own_step(self):
        col = self.here.col

        @pl.when(col > 0)
        def _():
            self.give_up(col).wait_recv()
            add_into(self.mine.at[0, col], self.line.at[col])

        @pl.when(col < 3)
        def _():
            self.give_down(col, 4).wait_recv()
            add_into(self.mine.at[0, col], self.line.at[4])

    def finish(self):
        col = self.here.col
        for place in range(4):
            self.give_one(place).wait_send()
            self.give_two(place).wait_send()
            for half in range(2):
                self.give_across(place, half).wait_send()
                self.give_along(place, half).wait_send()

            @pl.when(place > col)
            def _():
                self.give_up(place).wait_send()

            @pl.when(place < col)
            def _():
                self.give_down(place, place).wait_send()


def doc_start(places, cuts):
    return jnp.where(places >= cuts[1], cuts[1], jnp.where(places >= cuts[0], cuts[0], 0))


def key_blocks(cuts, first_query, rows, scores_of, block_fn):
    def scan(index, carry):
        start = pl.multiple_of(index * rows, rows)
        free = (start >= doc_start(first_query + rows - 1, cuts)) & (start + rows <= first_query + 1)

        @pl.when(free)
        def _():
            block_fn(start, scores_of(start))

        @pl.when(jnp.logical_not(free))
        def _():
            key_place = start + lax.broadcasted_iota(jnp.int32, (rows, rows), 0)
            place = first_query + lax.broadcasted_iota(jnp.int32, (1, rows), 1)
            allowed = (key_place <= place) & (key_place >= doc_start(place, cuts))
            block_fn(start, jnp.where(allowed, scores_of(start), MASKED))

        return carry

    lax.fori_loop(doc_start(first_query, cuts) // rows, first_query // rows + 1, scan, 0)


def attend_kernel(scale, group_tok, cuts, query, keys, values_t, mixed, total, top, summed, acc):
    rows = query.shape[0]
    side = lax.axis_index("exp") % 2
    first_query = side * group_tok + pl.program_id(0) * rows
    top[...] = jnp.full_like(top, MASKED)
    summed[...] = jnp.zeros_like(summed)
    acc[...] = jnp.zeros_like(acc)
    cut = (cuts[0, 0], cuts[0, 1])

    def scores_of(start):
        return contract_cols(keys[pl.ds(start, rows)], query[...]) * scale

    def block_fn(start, scores):
        old = top[...]
        new = jnp.maximum(old, jnp.max(scores, axis=0, keepdims=True))
        weights = jnp.exp(scores - new)
        decay = jnp.exp(old - new)
        top[...] = new
        summed[...] = summed[...] * decay + jnp.sum(weights, axis=0, keepdims=True)
        acc[...] = acc[...] * decay + matmul(values_t[:, pl.ds(start, rows)], weights.astype(BF16))

    key_blocks(cut, first_query, rows, scores_of, block_fn)
    mixed[...] = (acc[...] / summed[...]).T
    total[...] = top[...] + jnp.log(summed[...])


def attend(query, keys, values, cuts, scale, rows=512):
    group_tok, head_size = query.shape
    whole = lambda shape: pl.BlockSpec(shape, lambda i: (0, 0))
    return pl.pallas_call(
        functools.partial(attend_kernel, scale, group_tok),
        grid=(group_tok // rows,),
        in_specs=[
            pl.BlockSpec(memory_space=pltpu.SMEM),
            pl.BlockSpec((rows, head_size), lambda i: (i, 0)),
            whole(keys.shape),
            whole(values.shape[::-1]),
        ],
        out_specs=[
            pl.BlockSpec((rows, head_size), lambda i: (i, 0)),
            pl.BlockSpec((1, rows), lambda i: (0, i)),
        ],
        out_shape=[
            jax.ShapeDtypeStruct((group_tok, head_size), F32),
            jax.ShapeDtypeStruct((1, group_tok), F32),
        ],
        scratch_shapes=[
            pltpu.VMEM((1, rows), F32),
            pltpu.VMEM((1, rows), F32),
            pltpu.VMEM((head_size, rows), F32),
        ],
        compiler_params=pltpu.CompilerParams(vmem_limit_bytes=40 * 2**20),
        cost_estimate=pl.CostEstimate(
            flops=4 * 7 * 2**20 * head_size, bytes_accessed=2**23, transcendentals=7 * 2**20
        ),
    )(cuts[None], query, keys, values.T)


def attend_back_kernel(
    scale, group_tok, cuts, query, keys, keys_t, values, d_mixed, total, delta,
    d_query, d_keys, d_values, acc,
):
    rows = query.shape[0]
    side = lax.axis_index("exp") % 2
    first_query = side * group_tok + pl.program_id(0) * rows
    cut = (cuts[0, 0], cuts[0, 1])

    @pl.when(pl.program_id(0) == 0)
    def _():
        d_keys[...] = jnp.zeros_like(d_keys)
        d_values[...] = jnp.zeros_like(d_values)

    acc[...] = jnp.zeros_like(acc)

    def scores_of(start):
        return contract_cols(keys[pl.ds(start, rows)], query[...]) * scale

    def block_fn(start, scores):
        part = pl.ds(start, rows)
        weights = jnp.exp(scores - total[...])
        d_weights = contract_cols(values[part], d_mixed[...])
        d_scores = (weights * (d_weights - delta[...])).astype(BF16)
        d_values[part] += matmul(weights.astype(BF16), d_mixed[...])
        d_keys[part] += matmul(d_scores, query[...]) * scale
        acc[...] += matmul(keys_t[:, part], d_scores)

    key_blocks(cut, first_query, rows, scores_of, block_fn)
    d_query[...] = (acc[...] * scale).T


def attend_back(query, keys, values, d_mixed, mixed, total, cuts, scale, rows=512):
    group_tok, head_size = query.shape
    delta = jnp.sum(d_mixed.astype(F32) * mixed, axis=1)[None]
    whole = lambda shape: pl.BlockSpec(shape, lambda i: (0, 0))
    block = pl.BlockSpec((rows, head_size), lambda i: (i, 0))
    line = pl.BlockSpec((1, rows), lambda i: (0, i))
    return pl.pallas_call(
        functools.partial(attend_back_kernel, scale, group_tok),
        grid=(group_tok // rows,),
        in_specs=[
            pl.BlockSpec(memory_space=pltpu.SMEM),
            block,
            whole(keys.shape),
            whole(keys.shape[::-1]),
            whole(keys.shape),
            block,
            line,
            line,
        ],
        out_specs=[block, whole(keys.shape), whole(keys.shape)],
        out_shape=[
            jax.ShapeDtypeStruct((group_tok, head_size), F32),
            jax.ShapeDtypeStruct(keys.shape, F32),
            jax.ShapeDtypeStruct(keys.shape, F32),
        ],
        scratch_shapes=[pltpu.VMEM((head_size, rows), F32)],
        compiler_params=pltpu.CompilerParams(vmem_limit_bytes=48 * 2**20),
        cost_estimate=pl.CostEstimate(
            flops=10 * 7 * 2**20 * head_size, bytes_accessed=2**23, transcendentals=7 * 2**20
        ),
    )(cuts[None], query, keys, keys.T, values, d_mixed, total, delta)


def transposed_product(left, right):
    return jnp.dot(left.T, right, preferred_element_type=F32)


def column_of(line):
    return jnp.broadcast_to(line, (128, 128)).T[:, :1]


def line_of(column):
    return jnp.broadcast_to(column, (128, 128)).T[:1]


def expert_kernel(
    expert_count, normed, grads_all, mask, gate_half, up_half, down_half,
    gate_other, up_other, down_other, router,
    rows_all, out_parts, total, inner_in, grad_gate, grad_up, grad_down,
    their_gates, their_down,
    gate_w, up_w, down_w, masks, x_buf, d_buf, gates_t, weighteds_t, d_gates, d_ups, weighteds, out_buf,
    inner, sum_buf, sum_down, *rest,
):
    here = Here()
    row, col, core = here.row, here.col, here.core
    rows, width = normed.shape
    half = gate_half.shape[1]
    expert = row * 4 + col
    count = len(SPREAD_SEMS)
    collect = Collect(here, rest[:6], rest[6 : 6 + len(COLLECT_SEMS)])
    rest = rest[6 + len(COLLECT_SEMS) :]
    (
        weight_sem, load_sem, store_sem, tile_sem, give_send, give_recv, their_sem, sum_sem,
        inner_send, inner_recv,
    ) = rest[:10]
    sems = rest[10:]

    def x_block(of_row, place, unused_core):
        return rows_all.at[pl.ds(pl.multiple_of((of_row * 4 + place) * rows, rows), rows)]

    def d_block(of_row, place, unused_core):
        return grads_all.at[pl.ds(pl.multiple_of((of_row * 4 + place) * rows, rows), rows)]

    def m_block(of_row, place, unused_core):
        return masks.at[of_row, place]

    spread_x = Spread(here, normed, x_block, rows, sems[:count], core=False)
    spread_m = Spread(here, mask, m_block, mask.shape[0], sems[count:], core=False)
    order = here.near_first

    own_half = pl.ds(pl.multiple_of(core * half, half), half)
    other_half = pl.ds(pl.multiple_of((1 - core) * half, half), half)
    keeps = [
        pltpu.make_async_copy(source, target, weight_sem.at[index])
        for index, (source, target) in enumerate(
            (
                (normed, x_block(row, col, 0)),
                (mask, m_block(row, col, 0)),
                (gate_half, gate_w.at[:, own_half]),
                (up_half, up_w.at[:, own_half]),
                (down_half, down_w.at[own_half]),
                (gate_other, gate_w.at[:, other_half]),
                (up_other, up_w.at[:, other_half]),
                (down_other, down_w.at[other_half]),
            )
        )
    ]
    greet(here.group_peers() + [here.other_core()])
    spread_x.step(0)
    spread_m.step(0)
    for keep in keeps:
        keep.start()

    turns = (3, 2, 1, 0)

    def loads(step):
        return [
            pltpu.make_async_copy(
                source(here.rows[which], order[step], 0),
                target.at[pl.ds(position * rows, rows)],
                load_sem.at[position, array],
            )
            for position, which in enumerate(turns)
            for array, (source, target) in enumerate(((x_block, x_buf), (d_block, d_buf)))
        ]

    def stores(step):
        return [
            pltpu.make_async_copy(
                out_buf.at[pl.ds(position * rows, rows)],
                out_parts.at[which, order[step]],
                store_sem.at[position],
            )
            for position, which in enumerate(turns)
        ]

    tile = 256

    def first_products(step):
        place = order[step]
        x = x_buf[...]
        lane = lax.broadcasted_iota(jnp.int32, (x.shape[0], router.shape[1]), 1)
        logits = jnp.where(lane < expert_count, matmul(x, router[...]), MASKED)
        raised = jnp.exp(logits - jnp.max(logits, axis=1, keepdims=True))
        picked = jnp.sum(jnp.where(lane == expert, raised, 0.0), axis=1, keepdims=True)
        routed = jnp.concatenate(
            [column_of(masks[here.rows[which], place, pl.ds(expert, 1)]) for which in turns]
        )
        gate = picked / jnp.sum(raised, axis=1, keepdims=True) * routed
        columns = [
            pl.ds(pl.multiple_of((here.rows[which] * 4 + place) * rows, rows), rows) for which in turns
        ]

        def tile_step(index, inner_sum):
            at = pl.ds(pl.multiple_of(index * tile, tile), tile)
            pre_gate = matmul(x_buf[...], gate_w[:, at])
            pre_up = matmul(x_buf[...], up_w[:, at])
            back = contract_cols(d_buf[...], down_w[at])
            sigmoid_gate = 1.0 / (1.0 + jnp.exp(-pre_gate))
            silu_gate = pre_gate * sigmoid_gate
            hidden = (silu_gate * pre_up).astype(BF16).astype(F32)
            d_hid = back * gate
            d_gate = (d_hid * pre_up * (sigmoid_gate + silu_gate * (1.0 - sigmoid_gate))).astype(BF16)
            d_up = (d_hid * silu_gate).astype(BF16)
            weight = (hidden * gate).astype(BF16)
            d_gates[:, at] = d_gate
            d_ups[:, at] = d_up
            weighteds[:, at] = weight
            side = index // (half // tile)
            first = pl.multiple_of(index % (half // tile) * tile, tile)
            for values, target in (
                (d_gate, gates_t.at[side, pl.ds(first, tile)]),
                (d_up, gates_t.at[side, pl.ds(first + half, tile)]),
                (weight, weighteds_t.at[at]),
            ):
                turned = values.T
                for position, column in enumerate(columns):
                    target[:, column] = turned[:, position * rows : (position + 1) * rows]
            return inner_sum + jnp.sum(hidden * back, axis=1, keepdims=True)

        start = jnp.zeros((x.shape[0], 1), F32)
        inner_sum = lax.fori_loop(0, gate_w.shape[1] // tile, tile_step, start)
        for position, which in enumerate(turns):
            part = slice(position * rows, (position + 1) * rows)
            inner[here.rows[which], place, 0:1] = line_of(inner_sum[part])

    def second_products(step):
        place = order[step]

        @pl.loop(0, width // tile)
        def _(index):
            at = pl.ds(pl.multiple_of(index * tile, tile), tile)
            out_buf[:, at] = matmul(weighteds[...], down_w[:, at]).astype(BF16)
            d_x = contract_cols(d_gates[...], gate_w[at]) + contract_cols(d_ups[...], up_w[at])
            d_x = d_x.astype(BF16)
            for position, which in enumerate(turns):
                collect.mine[which, place, :, at] = d_x[position * rows : (position + 1) * rows]

    for index in (1, 2):
        spread_x.step(index)
        spread_m.step(index)
    for keep in keeps:
        keep.wait()
    for copy in loads(0):
        copy.start()
    turn_order = (0, 1, 3, 2)
    ends = (col == 0) | (col == 3)

    def from_ends(step):
        @pl.when(ends)
        def _():
            collect.line_step(order[step])

    def from_inside(step):
        @pl.when(jnp.logical_not(ends))
        def _():
            collect.line_step(order[step])

    for turn, step in enumerate(turn_order):
        for copy in loads(step):
            copy.wait()
        first_products(step)
        if turn < 2:
            spread_x.step(turn + 3)
            spread_m.step(turn + 3)
        if turn in (0, 2):
            for copy in loads(turn_order[turn + 1]):
                copy.start()
        if turn > 0:
            for copy in stores(turn_order[turn - 1]):
                copy.wait()
            collect.corner_step(order[turn_order[turn - 1]])
        second_products(step)
        for copy in stores(step):
            copy.start()
        collect.start_far(order[step])
        collect.start_near(order[step])
        if turn == 1:
            spread_x.step(5)
            spread_m.step(5)
            for copy in loads(turn_order[2]):
                copy.start()
        if turn > 0:
            collect.plane_step(order[turn_order[turn - 1]])
        if turn > 1:
            from_ends(turn_order[turn - 1])

    tiles = width // tile

    def tile_at(index):
        return pl.ds(pl.multiple_of(index * tile, tile), tile)

    def acts_of(kind, side):
        if kind == 0:
            return gates_t[side]
        return weighteds_t[pl.ds(pl.multiple_of(side * half, half), half)]

    counts = (2 * half, half)

    def slot_at(kind, slot):
        return pl.ds(pl.multiple_of((2 * kind + slot) * tile, tile), tile)

    def tile_buf(kind, slot):
        return gate_w.at[:, slot_at(kind, slot)]

    def give_buf(kind, slot):
        return up_w.at[pl.ds(0, counts[kind]), slot_at(kind, slot)]

    def their_buf(kind, slot):
        return up_w.at[pl.ds(width // 2, counts[kind]), slot_at(kind, slot)]

    theirs = (their_gates, their_down)

    def tile_load(kind, index, slot):
        source = (rows_all, grads_all)[kind]
        return pltpu.make_async_copy(
            source.at[:, tile_at(index)], tile_buf(kind, slot), tile_sem.at[slot]
        )

    def give(kind, index, slot):
        sems = give_send.at[slot, kind], give_recv.at[kind, index]
        return remote(give_buf(kind, slot), theirs[kind].at[:, tile_at(index)], *sems, here.other_core())

    def their_load(kind, index, slot):
        return pltpu.make_async_copy(
            theirs[kind].at[:, tile_at(index)],
            their_buf(kind, slot),
            their_sem.at[slot, kind],
        )

    def sum_stores(kind, index, slot):
        if kind == 1:
            target = grad_down.at[:, tile_at(index)]
            return [pltpu.make_async_copy(sum_down, target, sum_sem.at[0, 2])]
        return [
            pltpu.make_async_copy(
                sum_buf.at[slot, part], target.at[tile_at(index)], sum_sem.at[slot, part]
            )
            for part, target in enumerate((grad_gate, grad_up))
        ]

    def give_gradients(kind, start, stop):
        tile_load(kind, start, 0).start()

        @pl.loop(start, stop)
        def _(index):
            slot = index % 2

            @pl.when(index + 1 < stop)
            def _():
                tile_load(kind, index + 1, 1 - slot).start()

            tile_load(kind, index, slot).wait()
            product = matmul(acts_of(kind, 1 - core), tile_buf(kind, slot)[...])

            @pl.when(index >= 2)
            def _():
                give(kind, index - 2, slot).wait_send()

            give_buf(kind, slot)[...] = product.astype(BF16)
            give(kind, index, slot).start()

    def keep_gradients(kind, start, stop):
        tile_load(kind, start, 0).start()
        give(kind, start, 0).wait_recv()
        their_load(kind, start, 0).start()

        @pl.loop(start, stop)
        def _(index):
            slot = index % 2

            @pl.when(index + 1 < stop)
            def _():
                tile_load(kind, index + 1, 1 - slot).start()
                give(kind, index + 1, 1 - slot).wait_recv()
                their_load(kind, index + 1, 1 - slot).start()

            tile_load(kind, index, slot).wait()
            product = matmul(acts_of(kind, core), tile_buf(kind, slot)[...])
            their_load(kind, index, slot).wait()
            product = product + their_buf(kind, slot)[...].astype(F32)
            held = 2 - kind

            @pl.when(index >= held)
            def _():
                for copy in sum_stores(kind, index - held, slot):
                    copy.wait()

            if kind == 1:
                sum_down[...] = product
            else:
                sum_buf[slot, 0] = product[:half].T
                sum_buf[slot, 1] = product[half:].T
            for copy in sum_stores(kind, index, slot):
                copy.start()

    def give_inner(index):
        step = index + 1
        to_row, to_col = (row + step // 4) % 4, (col + step) % 4
        return remote(
            inner.at[to_row, to_col],
            inner_in.at[row, col],
            inner_send.at[index],
            inner_recv.at[row, col],
            (to_row, to_col, core),
        )

    for index in range(15):
        give_inner(index).start()
    inner_in[row, col] = inner[row, col]
    give_gradients(0, 0, tiles // 2)
    from_inside(3)
    collect.corner_step(order[2])
    give_gradients(0, tiles // 2, tiles)
    collect.plane_step(order[2])
    from_ends(2)
    give_gradients(1, 0, tiles)
    from_inside(2)
    keep_gradients(0, 0, tiles // 2)
    from_inside(1)
    keep_gradients(0, tiles // 2, tiles)
    keep_gradients(1, 0, tiles)
    collect.own_step()
    total[...] = collect.mine[0, col]

    for index in range(15):
        give_inner(index).wait_send()
        step = index + 1
        from_row, from_col = (row + 4 - step // 4) % 4, (col + 4 - step % 4) % 4
        arrived(inner_in.at[from_row, from_col], inner_recv.at[from_row, from_col])
    for copy in stores(turn_order[3]):
        copy.wait()
    for kind in range(2):
        for slot in range(2):
            give(kind, tiles - 2 + slot, slot).wait_send()
        for slot in range(2 - kind):
            for copy in sum_stores(kind, tiles - 2 + kind + slot, slot):
                copy.wait()
    spread_x.finish()
    spread_m.finish()
    collect.finish()


def expert_stage(normed, grads_all, mask, halves, others, router, collective_id):
    rows, width = normed.shape
    half = halves[0].shape[1]
    expert_count = router.shape[1]
    router = jnp.pad(router, ((0, 0), (0, 128 - expert_count)))
    tokens = 16 * rows
    tile = 256
    vmem = pl.BlockSpec(memory_space=pltpu.VMEM)
    hbm = pl.BlockSpec(memory_space=pl.ANY)
    dma = pltpu.SemaphoreType.DMA
    blocks = jax.ShapeDtypeStruct((4, 4, rows, width), BF16)
    got = pl.pallas_call(
        functools.partial(expert_kernel, expert_count),
        in_specs=[hbm] * 9 + [vmem],
        out_specs=[hbm] * 2 + [vmem] * 2 + [hbm] * 5,
        out_shape=[
            jax.ShapeDtypeStruct((tokens, width), BF16),
            blocks,
            jax.ShapeDtypeStruct((rows, width), BF16),
            jax.ShapeDtypeStruct((4, 4, 8, rows), F32),
            jax.ShapeDtypeStruct((width, half), F32),
            jax.ShapeDtypeStruct((width, half), F32),
            jax.ShapeDtypeStruct((half, width), F32),
            jax.ShapeDtypeStruct((2 * half, width), BF16),
            jax.ShapeDtypeStruct((half, width), BF16),
        ],
        scratch_shapes=[
            pltpu.VMEM((width, 2 * half), BF16),
            pltpu.VMEM((width, 2 * half), BF16),
            pltpu.VMEM((2 * half, width), BF16),
            pltpu.VMEM((4, 4) + mask.shape, F32),
            pltpu.VMEM((4 * rows, width), BF16),
            pltpu.VMEM((4 * rows, width), BF16),
            pltpu.VMEM((2, 2 * half, tokens), BF16),
            pltpu.VMEM((2 * half, tokens), BF16),
            pltpu.VMEM((4 * rows, 2 * half), BF16),
            pltpu.VMEM((4 * rows, 2 * half), BF16),
            pltpu.VMEM((4 * rows, 2 * half), BF16),
            pltpu.VMEM((4 * rows, width), BF16),
            pltpu.VMEM((4, 4, 8, rows), F32),
            pltpu.VMEM((2, 2, tile, half), F32),
            pltpu.VMEM((half, tile), F32),
        ]
        + collect_buffers(rows, width)
        + COLLECT_SEMS
        + [
            dma((8,)), dma((4, 2)), dma((4,)),
            dma((2,)), dma((2, 2)), dma((2, width // tile)), dma((2, 2)), dma((2, 3)),
            dma((15,)), dma((4, 4)),
        ]
        + SPREAD_SEMS * 2,
        compiler_params=pltpu.CompilerParams(
            collective_id=collective_id, has_side_effects=True, vmem_limit_bytes=61 * 2**20
        ),
        cost_estimate=pl.CostEstimate(
            flops=18 * 2 * tokens * width * half,
            bytes_accessed=2**26,
            transcendentals=2 * tokens * half,
        ),
    )(normed, grads_all, mask, *halves, *others, router)
    return got[1], got[2], got[3], got[4:7]


def project_kernel(
    hidden, gain, weights, out_weights, q_gain, k_gain, cosine, sine,
    normed, all_weights, all_out, qkv, totals, query, keys, values,
    heads, stat, scale_q, scale_k, kept_sem, kept_out_sem, kept_kv_sem,
    stat_send, stat_recv, head_send, head_recv, pair_send, pair_recv, *sems,
):
    here = Here()
    row, col, core = here.row, here.col, here.core
    count = len(SPREAD_SEMS)
    rows, width = hidden.shape
    depth = weights.shape[0]
    part, side = depth // 2, out_weights.shape[0]

    def weight_block(of_row, unused_place, of_core):
        return all_weights.at[pl.ds(pl.multiple_of(of_row * depth + of_core * part, part), part)]

    def out_block(of_row, place, of_core):
        start = pl.multiple_of(place * side + of_core * (side // 2), side // 2)
        return all_out.at[pl.ds(start, side // 2), pl.ds(pl.multiple_of(of_row * side, side), side)]

    def normed_block(unused_row, place, unused_core):
        return normed.at[pl.ds(pl.multiple_of(place * rows, rows), rows)]

    own_weight = weights.at[pl.ds(pl.multiple_of(core * part, part), part)]
    own_out = out_weights.at[pl.ds(pl.multiple_of(core * (side // 2), side // 2), side // 2)]
    spread_w = Spread(here, own_weight, weight_block, part, sems[:count], line=False)
    spread_n = Spread(
        here, normed_block(row, col, core), normed_block, rows, sems[count : 2 * count], plane=False
    )
    spread_o = Spread(here, own_out, out_block, side // 2, sems[2 * count :])
    greet(here.plane_peers() + here.line_peers() + [here.other_core()])
    spread_w.step(0)
    keep = pltpu.make_async_copy(own_weight, weight_block(row, 0, core), kept_sem)
    keep.start()
    keep_out = pltpu.make_async_copy(own_out, out_block(row, col, core), kept_out_sem)
    keep_out.start()

    values_in = hidden[...].astype(F32)
    scale_one = lax.rsqrt(jnp.mean(values_in * values_in, axis=1, keepdims=True) + EPSILON)
    own_rows = pl.ds(pl.multiple_of(col * rows, rows), rows)
    normed[own_rows] = (values_in * scale_one * gain[...].astype(F32)).astype(BF16)
    spread_n.step(0)
    spread_o.step(0)
    spread_w.step(1)
    spread_n.step(1)
    spread_w.step(2)
    spread_n.step(2)
    spread_n.step(3)
    keep.wait()
    for which in range(4):
        spread_w.core_arrived(which, 0)

    columns = 256

    @pl.loop(0, qkv.shape[1] // columns)
    def _(index):
        at = pl.ds(pl.multiple_of(index * columns, columns), columns)
        qkv[:, at] = matmul(normed[...], all_weights[:, at])

    plane = qkv.shape[1] // (3 * HD)
    for kind in range(2):
        square = jnp.zeros((qkv.shape[0], HD), F32)
        for head in range(plane):
            start = (head * 3 + kind) * HD
            raw = qkv[:, start : start + HD]
            square = square + raw * raw
        stat[col, kind : kind + 1] = jnp.sum(square.T, axis=0, keepdims=True)

    def give_stat(step):
        peer = here.line_peers()[step]
        return remote(stat.at[col], stat.at[col], stat_send.at[step], stat_recv.at[col], peer)

    for step in range(3):
        give_stat(step).start()
    spread_o.step(1)
    for step in range(3):
        place = (col + step + 1) % 4
        arrived(stat.at[place], stat_recv.at[place])
    total = stat[0] + stat[1] + stat[2] + stat[3]
    totals[...] = total
    for kind, target in enumerate((scale_q, scale_k)):
        line = lax.rsqrt(total[kind : kind + 1] / width + EPSILON)
        target[...] = jnp.broadcast_to(line, (HD, line.shape[1])).T

    chunk = 64

    @pl.loop(0, qkv.shape[0] // chunk)
    def _(index):
        at = pl.ds(pl.multiple_of(index * chunk, chunk), chunk)
        for head in range(plane):
            for kind, (scales, gains) in enumerate(((scale_q, q_gain), (scale_k, k_gain))):
                raw = qkv[at, pl.ds((head * 3 + kind) * HD, HD)]
                unit = raw * scales[at] * gains[:, head * HD : (head + 1) * HD]
                turned = pltpu.roll(unit, HD // 2, 1)
                heads[head, kind, at] = (unit * cosine[at] + turned * sine[at]).astype(BF16)
            heads[head, 2, at] = qkv[at, pl.ds((head * 3 + 2) * HD, HD)].astype(BF16)

    targets = (query.at[row], keys.at[1, row], values.at[1, row])

    def give_head(step, kind):
        dest = here.rows[step + 1]
        sems = head_send.at[step, kind], head_recv.at[kind, row]
        return remote(heads.at[dest, kind], targets[kind], *sems, here.at_row(dest))

    for kind in (1, 2, 0):
        for step in range(3):
            give_head(step, kind).start()

    def give_pair(source, kind):
        array = (keys, values)[kind]
        sems = pair_send.at[kind, source], pair_recv.at[kind, source]
        return remote(array.at[1, source], array.at[0, source], *sems, here.other_core())

    def keep_pair(source, kind):
        array = (keys, values)[kind]
        return pltpu.make_async_copy(
            array.at[1, source], array.at[0, source], kept_kv_sem.at[kind, source]
        )

    def pair_from(source):
        @pl.when(core == 0)
        def _():
            for kind in range(2):
                give_pair(source, kind).start()
                keep_pair(source, kind).start()

    for kind, array in ((1, keys), (2, values)):
        array[1, row] = heads[row, kind]
    query[row] = heads[row, 0]
    pair_from(row)
    spread_o.step(2)
    for source in here.rows[1:]:
        arrived(keys.at[1, source], head_recv.at[1, source])
        arrived(values.at[1, source], head_recv.at[2, source])
        pair_from(source)
    spread_o.step(3)
    for source in here.rows[1:]:
        arrived(query.at[source], head_recv.at[0, source])
    spread_o.step(4)
    spread_o.step(5)

    @pl.when(core == 0)
    def _():
        for source in range(4):
            for kind in range(2):
                give_pair(source, kind).wait_send()
                keep_pair(source, kind).wait()

    @pl.when(core == 1)
    def _():
        for source in range(4):
            for kind in range(2):
                give_pair(source, kind).wait_recv()

    for step in range(3):
        give_stat(step).wait_send()
        for kind in range(3):
            give_head(step, kind).wait_send()
    keep_out.wait()
    spread_w.finish(arrivals=False)
    spread_n.finish()
    spread_o.finish()


def project(hidden, gain, weights, out_weights, q_gain, k_gain, cosine, sine, collective_id):
    rows, width = hidden.shape
    depth, columns = weights.shape
    row_tok = 4 * rows
    plane = columns // (3 * HD)
    vmem = pl.BlockSpec(memory_space=pltpu.VMEM)
    hbm = pl.BlockSpec(memory_space=pl.ANY)
    return pl.pallas_call(
        project_kernel,
        in_specs=[vmem, vmem, hbm, hbm, vmem, vmem, vmem, vmem],
        out_specs=[vmem, vmem, hbm, vmem, vmem, vmem, vmem, vmem],
        out_shape=[
            jax.ShapeDtypeStruct((row_tok, width), BF16),
            jax.ShapeDtypeStruct((4 * depth, columns), BF16),
            jax.ShapeDtypeStruct((width, width), BF16),
            jax.ShapeDtypeStruct((row_tok, columns), F32),
            jax.ShapeDtypeStruct((8, row_tok), F32),
            jax.ShapeDtypeStruct((4, row_tok, HD), BF16),
            jax.ShapeDtypeStruct((2, 4, row_tok, HD), BF16),
            jax.ShapeDtypeStruct((2, 4, row_tok, HD), BF16),
        ],
        scratch_shapes=[
            pltpu.VMEM((plane, 3, row_tok, HD), BF16),
            pltpu.VMEM((4, 8, row_tok), F32),
            pltpu.VMEM((row_tok, HD), F32),
            pltpu.VMEM((row_tok, HD), F32),
            pltpu.SemaphoreType.DMA,
            pltpu.SemaphoreType.DMA,
            pltpu.SemaphoreType.DMA((2, 4)),
            pltpu.SemaphoreType.DMA((3,)),
            pltpu.SemaphoreType.DMA((4,)),
            pltpu.SemaphoreType.DMA((3, 3)),
            pltpu.SemaphoreType.DMA((3, 4)),
            pltpu.SemaphoreType.DMA((2, 4)),
            pltpu.SemaphoreType.DMA((2, 4)),
        ]
        + SPREAD_SEMS * 3,
        compiler_params=pltpu.CompilerParams(
            collective_id=collective_id, has_side_effects=True, vmem_limit_bytes=56 * 2**20
        ),
    )(hidden, gain[None], weights, out_weights, q_gain, k_gain, cosine, sine)


class PairSum:
    def __init__(self, here, values, out, held, got, send, recv):
        self.here, self.values, self.out, self.held, self.got = here, values, out, held, got
        self.send, self.recv = send, recv
        col, half = here.col, values.shape[1] // 2
        self.own = pl.ds(pl.multiple_of(here.core * half, half), half)
        self.others = pl.ds(pl.multiple_of((1 - here.core) * half, half), half)
        self.peers = [
            here.at_row(here.across),
            here.at_row(here.along),
            here.at_col(col + 1 - 2 * (col % 2)),
            here.at_col((col + 2) % 4),
        ]

    def copy(self, step):
        here, sems = self.here, (self.send.at[step], self.recv.at[step])
        if step == 0:
            return remote(self.values.at[:, self.others], self.got.at[0], *sems, here.other_core())
        if step == 5:
            return remote(self.held.at[4], self.out.at[:, self.own], *sems, here.other_core())
        return remote(self.held.at[step - 1], self.got.at[step], *sems, self.peers[step - 1])

    def begin(self):
        self.copy(0).start()

    def step(self, index):
        if index == 5:
            arrived(self.out.at[:, self.others], self.recv.at[5])
            return
        self.copy(index).wait_recv()
        before = self.values[:, self.own] if index == 0 else self.held[index - 1]
        self.held[index] = before + self.got[index]
        if index == 4:
            self.out[:, self.own] = self.held[4]
        self.copy(index + 1).start()

    def finish(self):
        for index in range(6):
            self.copy(index).wait_send()


def pair_sum_buffers(rows, width):
    return [
        pltpu.VMEM((5, rows, width // 2), F32),
        pltpu.VMEM((5, rows, width // 2), F32),
        pltpu.SemaphoreType.DMA((6,)),
        pltpu.SemaphoreType.DMA((6,)),
    ]


def back_kernel(
    scale, cuts, d_attn, query, keys, keys_t, values, mixed, total, out_weights, out_parts, early,
    d_attn_row, d_heads, mixed_rows, out_total, early_sum,
    weights, d_mixed_give, d_mixed_row, d_mixed, mixed_low, d_keys, d_values, acc, pair_out, pair_in,
    head_give, sum_held, sum_got, sum_send, sum_recv, weight_sem, load_sem,
    near_send, near_recv, head_send, head_recv, mixed_send, mixed_recv, back_send, back_recv,
    pair_send, pair_recv, *rest,
):
    here = Here()
    row, col, core = here.row, here.col, here.core
    rows = d_attn.shape[0]
    row_tok = 4 * rows
    group_tok = 4 * row_tok
    plane = 4 * HD
    order = here.near_first[::-1]
    collect = Collect(here, rest[:6], rest[6 : 6 + len(COLLECT_SEMS)])
    sems = rest[6 + len(COLLECT_SEMS) :]

    def row_block(unused_row, place, unused_core):
        return d_attn_row.at[pl.ds(pl.multiple_of(place * rows, rows), rows)]

    spread = Spread(here, row_block(row, col, core), row_block, rows, sems, plane=False)
    pair_sum = PairSum(here, early, early_sum, sum_held, sum_got, sum_send, sum_recv)

    def load(which, place):
        return pltpu.make_async_copy(
            out_parts.at[which, place], collect.mine.at[which, place], load_sem.at[which, place]
        )

    load_weights = pltpu.make_async_copy(out_weights, weights, weight_sem)
    load_weights.start()
    for place in order:
        for which in (3, 2, 1, 0):
            load(which, place).start()
    mixed_low[...] = mixed[...].astype(BF16)
    d_attn_row[pl.ds(pl.multiple_of(col * rows, rows), rows)] = d_attn[...]
    greet(here.plane_peers() + here.line_peers() + [here.other_core()])

    def give_near(step):
        place = (col + step) % 4
        sems_of = near_send.at[step], near_recv.at[col]
        return remote(d_mixed_give.at[place], d_mixed_row.at[col], *sems_of, here.at_col(place))

    def give_head(step):
        dest = here.rows[step]
        part = pl.ds(pl.multiple_of(dest * HD, HD), HD)
        sems_of = head_send.at[step], head_recv.at[row]
        return remote(d_mixed_row.at[:, :, part], d_mixed.at[row], *sems_of, here.at_row(dest))

    def give_mixed(step):
        dest = here.rows[step]
        part = pl.ds(pl.multiple_of(dest * row_tok, row_tok), row_tok)
        sems_of = mixed_send.at[step], mixed_recv.at[row]
        return remote(mixed_low.at[part], mixed_rows.at[row], *sems_of, here.at_row(dest))

    def start(index):
        for which in (3, 2, 1):
            load(which, order[index]).wait()
        collect.start_far(order[index])
        collect.start_near(order[index])

    ends = (col == 0) | (col == 3)

    def from_ends(index):
        @pl.when(ends)
        def _():
            collect.line_step(order[index])

    def from_inside(index):
        @pl.when(jnp.logical_not(ends))
        def _():
            collect.line_step(order[index])

    def plane_part(index):
        load(0, order[index]).wait()
        collect.plane_step(order[index])

    start(0)
    pair_sum.begin()
    load_weights.wait()
    for step in (1, 2, 3, 0):
        place = (col + step) % 4
        part = pl.ds(pl.multiple_of(place * plane, plane), plane)
        product = contract_cols(d_attn[...], weights[part]).astype(BF16)
        if step == 0:
            d_mixed_row[col] = product
        else:
            d_mixed_give[place] = product
            give_near(step).start()
    spread.step(0)
    pair_sum.step(0)
    d_keys[...] = jnp.zeros_like(d_keys)
    d_values[...] = jnp.zeros_like(d_values)
    for step in range(1, 4):
        place = (col + 4 - step) % 4
        arrived(d_mixed_row.at[place], near_recv.at[place])
    for step in range(1, 4):
        give_head(step).start()
    d_mixed[row] = d_mixed_row[:, :, pl.ds(pl.multiple_of(row * HD, HD), HD)]
    collect.corner_step(order[0])
    start(1)
    for step in range(1, 4):
        give_mixed(step).start()
    mixed_rows[row] = mixed_low[pl.ds(pl.multiple_of(row * row_tok, row_tok), row_tok)]
    pair_sum.step(1)
    spread.step(1)
    for source in here.rows[1:]:
        arrived(d_mixed.at[source], head_recv.at[source])

    cut = (cuts[0, 0], cuts[0, 1])
    last_query = 2 * group_tok - row_tok

    def queries(index):
        at = pl.ds(index * row_tok, row_tok)
        first_query = core * group_tok + index * row_tok
        gradient = d_mixed[index].reshape(row_tok, HD)
        delta = jnp.sum((gradient.astype(F32) * mixed[at]).T, axis=0, keepdims=True)
        sums = total[:, at]
        acc[...] = jnp.zeros_like(acc)

        def block_fn(part, scores):
            weight = jnp.exp(scores - sums)
            d_weight = contract_cols(values[part], gradient)
            d_scores = (weight * (d_weight - delta)).astype(BF16)
            d_values[part] += matmul(weight.astype(BF16), gradient)
            d_keys[part] += matmul(d_scores, query[at]) * scale
            acc[...] += matmul(keys_t[:, part], d_scores)

        def scan(block, carry):
            first_key = block * row_tok
            part = pl.ds(pl.multiple_of(first_key, row_tok), row_tok)
            masked = (block == 0) | (first_key == first_query) | (first_query == last_query)

            @pl.when(jnp.logical_not(masked))
            def _():
                block_fn(part, contract_cols(keys[part], query[at]) * scale)

            @pl.when(masked)
            def _():
                key_place = first_key + lax.broadcasted_iota(jnp.int32, (row_tok, row_tok), 0)
                place = first_query + lax.broadcasted_iota(jnp.int32, (1, row_tok), 1)
                allowed = (key_place <= place) & (key_place >= doc_start(place, cut))
                scores = contract_cols(keys[part], query[at]) * scale
                block_fn(part, jnp.where(allowed, scores, MASKED))

            return carry

        lax.fori_loop(0, core * 4 + index + 1, scan, 0)
        head_give[0, index] = (acc[...] * scale).T.astype(BF16)

    queries(0)
    plane_part(0)
    from_ends(0)
    collect.corner_step(order[1])
    start(2)
    spread.step(2)
    queries(1)
    from_inside(0)
    plane_part(1)
    from_ends(1)
    collect.corner_step(order[2])
    start(3)
    pair_sum.step(2)
    queries(2)
    from_inside(1)
    plane_part(2)
    from_ends(2)
    collect.corner_step(order[3])
    spread.step(3)
    queries(3)

    def give_back(step, kind):
        dest = here.rows[step]
        sems_of = back_send.at[step, kind], back_recv.at[kind, row]
        return remote(head_give.at[kind, dest], d_heads.at[row, kind], *sems_of, here.at_row(dest))

    def give_pair(kind):
        sems_of = pair_send.at[kind], pair_recv.at[kind]
        return remote(pair_out.at[kind], pair_in.at[kind], *sems_of, here.other_core())

    for step in range(1, 4):
        give_back(step, 0).start()
    d_heads[row, 0] = head_give[0, row]

    @pl.when(core == 1)
    def _():
        for kind, gradient in enumerate((d_keys, d_values)):
            pair_out[kind] = gradient[pl.ds(0, group_tok)].astype(BF16)
            give_pair(kind).start()
        for kind, gradient in enumerate((d_keys, d_values)):
            for part in range(4):
                at = pl.ds(group_tok + part * row_tok, row_tok)
                head_give[kind + 1, part] = gradient[at].astype(BF16)

    from_inside(2)
    plane_part(3)
    pair_sum.step(3)

    @pl.when(core == 0)
    def _():
        for kind, gradient in enumerate((d_keys, d_values)):
            give_pair(kind).wait_recv()
            for part in range(4):
                at = pl.ds(part * row_tok, row_tok)
                summed = gradient[at] + pair_in[kind, at].astype(F32)
                head_give[kind + 1, part] = summed.astype(BF16)

    for kind in (1, 2):
        for step in range(1, 4):
            give_back(step, kind).start()
        d_heads[row, kind] = head_give[kind, row]
    pair_sum.step(4)
    pair_sum.step(5)
    collect.own_step()
    out_total[...] = collect.mine[0, col]
    for source in here.rows[1:]:
        arrived(mixed_rows.at[source], mixed_recv.at[source])
        for kind in range(3):
            arrived(d_heads.at[source, kind], back_recv.at[kind, source])
    for step in range(1, 4):
        give_near(step).wait_send()
        give_head(step).wait_send()
        give_mixed(step).wait_send()
        for kind in range(3):
            give_back(step, kind).wait_send()

    @pl.when(core == 1)
    def _():
        for kind in range(2):
            give_pair(kind).wait_send()

    pair_sum.finish()
    spread.finish()
    collect.finish()


def attend_back_stage(
    d_attn, query, keys, values, mixed, total, cuts, out_weights, out_parts, early, scale, collective_id
):
    rows, width = d_attn.shape
    row_tok, group_tok = 4 * rows, 16 * rows
    vmem, hbm = pl.BlockSpec(memory_space=pltpu.VMEM), pl.BlockSpec(memory_space=pl.ANY)
    dma = pltpu.SemaphoreType.DMA
    return pl.pallas_call(
        functools.partial(back_kernel, scale),
        in_specs=[pl.BlockSpec(memory_space=pltpu.SMEM)] + [vmem] * 7 + [hbm] * 2 + [vmem],
        out_specs=[vmem] * 5,
        out_shape=[
            jax.ShapeDtypeStruct((row_tok, width), BF16),
            jax.ShapeDtypeStruct((4, 3, row_tok, HD), BF16),
            jax.ShapeDtypeStruct((4, row_tok, HD), BF16),
            jax.ShapeDtypeStruct((rows, width), BF16),
            jax.ShapeDtypeStruct(early.shape, F32),
        ],
        scratch_shapes=[
            pltpu.VMEM((width, width), BF16),
            pltpu.VMEM((4, rows, 4 * HD), BF16),
            pltpu.VMEM((4, rows, 4 * HD), BF16),
            pltpu.VMEM((4, 4, rows, HD), BF16),
            pltpu.VMEM((group_tok, HD), BF16),
            pltpu.VMEM((2 * group_tok, HD), F32),
            pltpu.VMEM((2 * group_tok, HD), F32),
            pltpu.VMEM((HD, row_tok), F32),
            pltpu.VMEM((2, group_tok, HD), BF16),
            pltpu.VMEM((2, group_tok, HD), BF16),
            pltpu.VMEM((3, 4, row_tok, HD), BF16),
        ]
        + pair_sum_buffers(*early.shape)
        + [
            dma, dma((4, 4)), dma((4,)), dma((4,)), dma((4,)), dma((4,)), dma((4,)), dma((4,)),
            dma((4, 3)), dma((3, 4)), dma((2,)), dma((2,)),
        ]
        + collect_buffers(rows, width)
        + COLLECT_SEMS
        + SPREAD_SEMS,
        compiler_params=pltpu.CompilerParams(
            collective_id=collective_id, has_side_effects=True, vmem_limit_bytes=58 * 2**20
        ),
    )(cuts[None], d_attn, query, keys, keys.T, values, mixed, total, out_weights, out_parts, early)


def tail_kernel(
    d_heads, qkv, totals, q_gain, k_gain, cosine, sine, weights, normed, mixed_rows, d_attn,
    hidden, gain, d_middle,
    grad_hidden, grad_qkv, grad_out, late_sum,
    d_qkv, late, grads, mixed, units, stat, scales, sums, sum_held, sum_got, sum_send, sum_recv,
    stat_send, stat_recv,
    line, line_in, whole, give, other, plane, corner_one, corner_two, from_across, from_along,
    up_send, down_send, line_recv, other_send, other_recv,
    one_send, one_recv, two_send, two_recv, across_send, across_recv, along_send, along_recv,
    back_send, back_recv,
):
    here = Here()
    row, col, core = here.row, here.col, here.core
    rows = hidden.shape[0]
    depth, columns = grads.shape
    part = depth // 2
    first, second = pl.ds(0, part // 2), pl.ds(part // 2, part // 2)
    order = here.near_first[::-1]
    qkv_columns = d_qkv.shape[1]
    tile = 512

    def line_products():
        @pl.loop(0, weights.shape[0] // tile)
        def _(index):
            at = pl.ds(pl.multiple_of(index * tile, tile), tile)
            product = contract_cols(d_qkv[...], weights[at]).astype(BF16)
            line[:, :, at] = product.reshape(4, rows, tile)

    def give_up(place):
        sems = up_send.at[place], line_recv.at[place]
        return remote(line.at[place], line_in.at[place], *sems, here.at_col(col + 1))

    def give_down(place, slot):
        sems = down_send.at[place], line_recv.at[slot]
        return remote(line.at[place], line_in.at[slot], *sems, here.at_col(col - 1))

    def line_step(place):
        @pl.when((place > col) & (col > 0))
        def _():
            give_up(place).wait_recv()
            add_into(line.at[place], line_in.at[place])

        @pl.when((place < col) & (col < 3))
        def _():
            give_down(place, place).wait_recv()
            add_into(line.at[place], line_in.at[place])

        @pl.when(place > col)
        def _():
            give_up(place).start()

        @pl.when(place < col - 1)
        def _():
            give_down(place, place).start()

        @pl.when(place == col - 1)
        def _():
            give_down(place, 4).start()

    def row_product(which):
        of_row = here.rows[which]
        at = pl.ds(pl.multiple_of(of_row * depth, depth), depth)
        whole[:, pl.ds(0, qkv_columns)] = transposed_product(normed[:, at], d_qkv[...]).astype(BF16)
        whole[:, pl.ds(qkv_columns, columns - qkv_columns)] = transposed_product(
            mixed[...], d_attn[:, at]
        ).astype(BF16)
        plane[which] = whole[pl.ds(pl.multiple_of(core * part, part), part)]
        give[which] = whole[pl.ds(pl.multiple_of((1 - core) * part, part), part)]
        to_core(which).start()

    def to_core(which):
        sems = other_send.at[which], other_recv.at[which]
        return remote(give.at[which], other.at[which], *sems, here.other_core())

    def own_sum(which):
        to_core(which).wait_recv()
        add_into(plane.at[which], other.at[which])

    give_one = remote(
        plane.at[3, first], corner_one, one_send, one_recv, here.at_row(here.across)
    )
    give_two = remote(
        plane.at[3, second], corner_two, two_send, two_recv, here.at_row(here.along)
    )

    def give_across(index):
        at = (first, second)[index]
        sems = across_send.at[index], across_recv.at[index]
        return remote(plane.at[1, at], from_across.at[at], *sems, here.at_row(here.across))

    def give_along(index):
        at = (first, second)[index]
        sems = along_send.at[index], along_recv.at[index]
        return remote(plane.at[2, at], from_along.at[at], *sems, here.at_row(here.along))

    pair_sum = PairSum(here, late, late_sum, sum_held, sum_got, sum_send, sum_recv)
    greet(here.plane_peers() + here.line_peers() + [here.other_core()])

    width = hidden.shape[1]
    heads = d_heads.shape[0]
    row_tok = d_qkv.shape[0]
    late[...] = jnp.zeros_like(late)
    for kind in range(2):
        root = lax.rsqrt(totals[kind : kind + 1] / width + EPSILON)
        scales[kind] = jnp.broadcast_to(root, (HD, row_tok)).T
        square = jnp.zeros((row_tok, HD), F32)
        for head in range(heads):
            start = (head * 3 + kind) * HD
            raw = qkv[:, start : start + HD]
            given = d_heads[head, kind].astype(F32)
            unit = given * cosine[...] + pltpu.roll(given * sine[...], HD // 2, 1)
            gains = (q_gain, k_gain)[kind][:, head * HD : (head + 1) * HD]
            gain_sum = jnp.sum(unit * raw * scales[kind], axis=0, keepdims=True)
            place = pl.ds(pl.multiple_of((col * heads + head) * HD, HD), HD)
            late[kind + 1 : kind + 2, place] = gain_sum
            weighted = unit * gains
            square = square + weighted * raw
            units[kind, head] = weighted
        stat[col, kind : kind + 1] = jnp.sum(square.T, axis=0, keepdims=True)

    def give_stat(step):
        peer = here.line_peers()[step]
        return remote(stat.at[col], stat.at[col], stat_send.at[step], stat_recv.at[col], peer)

    for step in range(3):
        give_stat(step).start()
    for head in range(heads):
        d_qkv[:, (head * 3 + 2) * HD : (head * 3 + 3) * HD] = d_heads[head, 2]
        mixed[:, head * HD : (head + 1) * HD] = mixed_rows[head]
    for step in range(3):
        place = (col + step + 1) % 4
        arrived(stat.at[place], stat_recv.at[place])
    total = stat[0] + stat[1] + stat[2] + stat[3]
    for kind in range(2):
        sums[...] = jnp.broadcast_to(total[kind : kind + 1] / width, (HD, row_tok)).T
        for head in range(heads):
            start = (head * 3 + kind) * HD
            raw = qkv[:, start : start + HD]
            root = scales[kind]
            d_raw = root * units[kind, head] - raw * (root * root * root) * sums[...]
            d_qkv[:, start : start + HD] = d_raw.astype(BF16)
    ends = (col == 0) | (col == 3)
    line_products()

    @pl.when(ends)
    def _():
        for place in order[:3]:
            line_step(place)

    def inner_step(place):
        @pl.when(jnp.logical_not(ends))
        def _():
            line_step(place)

    row_product(3)
    row_product(1)
    inner_step(order[0])
    own_sum(3)
    give_one.start()
    give_two.start()
    row_product(2)
    own_sum(1)
    give_across(0).start()
    own_sum(2)
    give_along(1).start()
    inner_step(order[1])
    row_product(0)
    inner_step(order[2])
    give_two.wait_recv()
    add_into(plane.at[1, second], corner_two)
    give_across(1).start()
    give_one.wait_recv()
    add_into(plane.at[2, first], corner_one)
    give_along(0).start()
    own_sum(0)

    @pl.when(col > 0)
    def _():
        give_up(col).wait_recv()
        add_into(line.at[col], line_in.at[col])

    @pl.when(col < 3)
    def _():
        give_down(col, 4).wait_recv()
        add_into(line.at[col], line_in.at[4])

    given = line[col].astype(F32)
    tokens = hidden[...].astype(F32)
    root = lax.rsqrt(jnp.mean(tokens * tokens, axis=1, keepdims=True) + EPSILON)
    late[0:1] = jnp.sum(given * tokens * root, axis=0, keepdims=True)
    pair_sum.begin()
    weighted = given * gain[...].astype(F32)
    inner = jnp.mean(weighted * tokens, axis=1, keepdims=True)
    grad_hidden[...] = d_middle[...] + root * weighted - tokens * (root * root * root) * inner
    pair_sum.step(0)
    for index in range(2):
        give_across(index).wait_recv()
        give_along(index).wait_recv()
    add_into(plane.at[0], from_across, from_along)
    pair_sum.step(1)
    own_half = pl.ds(pl.multiple_of(core * part, part), part)
    give_back = remote(
        plane.at[0], grads.at[own_half], back_send, back_recv, here.other_core()
    )
    give_back.start()
    grads[own_half] = plane[0]
    other_half = grads.at[pl.ds(pl.multiple_of((1 - core) * part, part), part)]
    pair_sum.step(2)
    arrived(other_half, back_recv)
    grad_qkv[...] = grads[:, pl.ds(0, qkv_columns)].astype(F32)
    grad_out[...] = grads[:, pl.ds(qkv_columns, columns - qkv_columns)].astype(F32)
    for index in (3, 4, 5):
        pair_sum.step(index)
    pair_sum.finish()
    for step in range(3):
        give_stat(step).wait_send()
    give_back.wait_send()
    give_one.wait_send()
    give_two.wait_send()
    for index in range(2):
        give_across(index).wait_send()
        give_along(index).wait_send()
    for which in range(4):
        to_core(which).wait_send()
    for place in order:

        @pl.when(place > col)
        def _():
            give_up(place).wait_send()

        @pl.when(place < col)
        def _():
            give_down(place, place).wait_send()


def tail_stage(
    d_heads, qkv, totals, q_gain, k_gain, cosine, sine, weights, normed, mixed_rows, d_attn,
    hidden, gain, d_middle, collective_id,
):
    row_tok, qkv_columns = qkv.shape
    rows, width = hidden.shape
    depth = width // 4
    out_columns = width // 4
    columns = qkv_columns + out_columns
    part = depth // 2
    heads = d_heads.shape[0]
    vmem = pl.BlockSpec(memory_space=pltpu.VMEM)
    one, four = pltpu.SemaphoreType.DMA, pltpu.SemaphoreType.DMA((4,))
    two, five = pltpu.SemaphoreType.DMA((2,)), pltpu.SemaphoreType.DMA((5,))
    three = pltpu.SemaphoreType.DMA((3,))
    return pl.pallas_call(
        tail_kernel,
        in_specs=[vmem] * 14,
        out_specs=[vmem] * 4,
        out_shape=[
            jax.ShapeDtypeStruct((rows, width), F32),
            jax.ShapeDtypeStruct((depth, qkv_columns), F32),
            jax.ShapeDtypeStruct((depth, out_columns), F32),
            jax.ShapeDtypeStruct((8, width), F32),
        ],
        scratch_shapes=[
            pltpu.VMEM((row_tok, qkv_columns), BF16),
            pltpu.VMEM((8, width), F32),
            pltpu.VMEM((depth, columns), BF16),
            pltpu.VMEM((row_tok, heads * HD), BF16),
            pltpu.VMEM((2, heads, row_tok, HD), F32),
            pltpu.VMEM((4, 8, row_tok), F32),
            pltpu.VMEM((2, row_tok, HD), F32),
            pltpu.VMEM((row_tok, HD), F32),
        ]
        + pair_sum_buffers(8, width)
        + [
            three, four,
            pltpu.VMEM((4, rows, width), BF16),
            pltpu.VMEM((5, rows, width), BF16),
            pltpu.VMEM((depth, columns), BF16),
            pltpu.VMEM((4, part, columns), BF16),
            pltpu.VMEM((4, part, columns), BF16),
            pltpu.VMEM((4, part, columns), BF16),
            pltpu.VMEM((part // 2, columns), BF16),
            pltpu.VMEM((part // 2, columns), BF16),
            pltpu.VMEM((part, columns), BF16),
            pltpu.VMEM((part, columns), BF16),
            four, four, five, four, four,
            one, one, one, one, two, two, two, two,
            one, one,
        ],
        compiler_params=pltpu.CompilerParams(
            collective_id=collective_id, has_side_effects=True, vmem_limit_bytes=58 * 2**20
        ),
    )(
        d_heads, qkv, totals, q_gain, k_gain, cosine, sine, weights, normed, mixed_rows, d_attn,
        hidden, gain[None], d_middle,
    )


def expert_rows(rows, grads, gate, gate_w, up_w, down_w):
    pre_gate = matmul(rows, gate_w)
    pre_up = matmul(rows, up_w)
    back = contract_cols(grads, down_w)
    sigmoid_gate = jax.nn.sigmoid(pre_gate)
    silu_gate = pre_gate * sigmoid_gate
    hidden = (silu_gate * pre_up).astype(BF16)
    inner = jnp.sum(hidden.astype(F32) * back, axis=-1)
    weighted = (hidden.astype(F32) * gate).astype(BF16)
    d_hid = back * gate
    d_pregate = (d_hid * pre_up * (sigmoid_gate + silu_gate * (1.0 - sigmoid_gate))).astype(BF16)
    d_preup = (d_hid * silu_gate).astype(BF16)
    outputs = matmul(weighted, down_w).astype(BF16)
    d_rows = (contract_cols(d_pregate, gate_w) + contract_cols(d_preup, up_w)).astype(BF16)
    return (
        outputs,
        d_rows,
        inner,
        contract_rows(rows, d_pregate),
        contract_rows(rows, d_preup),
        contract_rows(weighted, grads),
    )


def experts(normed, grads, dense_gates, gate_w, up_w, down_w):
    rows_dev, width = normed.shape
    devices = math.prod(lax.axis_size(axis) for axis in ALL)
    expert_count = dense_gates.shape[1]
    expert = lax.axis_index(ALL) // 2
    parts = max(1, lax.axis_size("exp") // 2)
    step = rows_dev // parts

    def one_part(sums, piece):
        rows, grad_rows, gates = piece
        rows_all = lax.all_gather(rows, ALL, axis=0, tiled=True)
        grads_all = lax.all_gather(grad_rows, ALL, axis=0, tiled=True)
        gates_all = lax.all_gather(gates, ALL, axis=0, tiled=True)
        gate = lax.dynamic_slice_in_dim(gates_all, expert, 1, 1)
        got = expert_rows(rows_all, grads_all, gate, gate_w, up_w, down_w)
        outputs = lax.psum_scatter(got[0], ALL, scatter_dimension=0, tiled=True)
        d_rows = lax.psum_scatter(got[1], ALL, scatter_dimension=0, tiled=True)
        inner = lax.all_to_all(
            got[2].reshape(devices, step), ALL, split_axis=0, concat_axis=0, tiled=True
        )
        inner = inner.reshape(expert_count, 2, step).sum(axis=1).T
        sums = got[3:] if sums is None else tuple(a + b for a, b in zip(sums, got[3:]))
        return sums, (outputs, d_rows, inner)

    if parts == 1:
        sums, (outputs, d_rows, inner) = one_part(None, (normed, grads, dense_gates))
    else:
        start = tuple(jnp.zeros(w.shape, F32) for w in (gate_w, up_w, down_w))
        pieces = tuple(v.reshape(parts, step, -1) for v in (normed, grads, dense_gates))
        sums, got = lax.scan(one_part, start, pieces)
        outputs, d_rows, inner = (v.reshape(rows_dev, -1) for v in got)
    return outputs.astype(F32), d_rows.astype(F32), inner, sums


def experts_here(normed, grads_all, picks, router, halves, others):
    numbers = jnp.arange(router.shape[1], dtype=jnp.int32)
    mask = jnp.any(picks.T[None] == numbers[:, None, None], axis=1).astype(F32)
    out_parts, d_rows, inner, weights = expert_stage(
        normed, grads_all, mask, halves, others, router, 1
    )
    inner = inner[:, :, 0].reshape(router.shape[1], -1).T
    return out_parts, d_rows.astype(F32), inner, weights


def shards(
    hidden_in,
    out_grad,
    attn_gain,
    w_qkv,
    q_gain,
    k_gain,
    w_out,
    moe_gain,
    router,
    w_gate,
    w_up,
    w_down,
    routes,
    doc_cuts,
):
    row_count, col_count = lax.axis_size("row"), lax.axis_size("col")
    tokens = hidden_in[0].astype(F32)
    rows_dev, width = tokens.shape
    heads = w_qkv.shape[1] // (3 * HD)
    plane = heads * HD
    scale = HD ** (-0.5)
    side = lax.axis_index("exp") % 2
    row_tok = rows_dev * col_count
    group_tok = row_tok * row_count
    cuts = lax.dynamic_index_in_dim(doc_cuts, lax.axis_index("exp") // 2, 0, keepdims=False)

    here = (row_count, col_count, lax.axis_size("exp")) == (4, 4, 2)

    if here:
        grads_all = lax.all_gather(out_grad[0], ("row", "col"), axis=0, tiled=True)
        other_w = [lax.ppermute(w[0], "exp", [(0, 1), (1, 0)]) for w in (w_gate, w_up, w_down)]

    gain_one = attn_gain.astype(F32)
    scale_one = rms_scale(tokens)
    head_start = lax.axis_index("col") * plane
    gain_q = lax.dynamic_slice_in_dim(q_gain, head_start, plane, 0).astype(F32)
    gain_k = lax.dynamic_slice_in_dim(k_gain, head_start, plane, 0).astype(F32)
    row_places = side * group_tok + lax.axis_index("row") * row_tok + jnp.arange(row_tok, dtype=jnp.int32)
    unused_doc, position = doc_positions(row_places, cuts)
    cosine, sine = rope_tables(position, HD)
    if here:
        signed = jnp.concatenate([-sine[:, : HD // 2], sine[:, HD // 2 :]], axis=1)
        normed_row, qkv_w, out_w, qkv, totals, query, keys, values = project(
            hidden_in[0], attn_gain, w_qkv, w_out, gain_q[None], gain_k[None], cosine, signed, 0
        )
        total_q, total_k = totals[0], totals[1]
        query = query.reshape(group_tok, HD)
        key_all, value_all = keys.reshape(-1, HD), values.reshape(-1, HD)
    else:
        normed_one = (tokens * scale_one * gain_one).astype(BF16)
        normed_row = lax.all_gather(normed_one, "col", axis=0, tiled=True)
        qkv_w = lax.all_gather(w_qkv, "row", axis=0, tiled=True)
        out_w = lax.all_gather(
            lax.all_gather(w_out, "row", axis=1, tiled=True), "col", axis=0, tiled=True
        )
        qkv = matmul(normed_row, qkv_w)
    qkv = qkv.reshape(row_tok, heads, 3, HD)
    query_raw, key_raw, value_raw = qkv[:, :, 0], qkv[:, :, 1], qkv[:, :, 2]
    if not here:
        total_q, total_k = lax.psum(
            (jnp.sum(query_raw * query_raw, axis=(1, 2)), jnp.sum(key_raw * key_raw, axis=(1, 2))),
            "col",
        )
    scale_q = lax.rsqrt(total_q / width + EPSILON)[:, None, None]
    scale_k = lax.rsqrt(total_k / width + EPSILON)[:, None, None]
    gain_q, gain_k = gain_q.reshape(heads, HD), gain_k.reshape(heads, HD)
    cosine, sine = cosine[:, None, :], sine[:, None, :]
    if not here:
        query = rotate(query_raw * scale_q * gain_q, cosine, sine).astype(BF16)
        key = rotate(key_raw * scale_k * gain_k, cosine, sine).astype(BF16)
        moved = rows_to_heads(jnp.concatenate([query, key, value_raw.astype(BF16)], axis=-1))
        query, own_pair = moved[:, :HD], moved[:, HD:]
        earlier_pair = from_behind(own_pair, "exp", 1)
        lower_pair = jnp.where(side == 0, own_pair, earlier_pair)
        upper_pair = jnp.where(side == 0, jnp.zeros_like(own_pair), own_pair)
        key_value = jnp.concatenate([lower_pair, upper_pair], axis=0)
        key_all, value_all = key_value[:, :HD], key_value[:, HD:]

    mixed_wide, total = attend(query, key_all, value_all, cuts, scale)
    mixed = mixed_wide.astype(BF16)
    middle = tokens + matmul(heads_to_tokens(mixed), out_w)

    gain_two = moe_gain.astype(F32)
    scale_two = rms_scale(middle)
    normed_two = (middle * scale_two * gain_two).astype(BF16)
    gates_all = jax.nn.softmax(matmul(normed_two, router), axis=-1)
    picks = routes[0]
    chosen = jnp.any(
        picks[:, :, None] == jnp.arange(router.shape[1], dtype=jnp.int32)[None, None, :], axis=1
    )
    grad_out = out_grad[0].astype(F32)
    expert_w = (w_gate[0], w_up[0], w_down[0])
    if here:
        out_parts, d_normed_two, inner, weight_grads = experts_here(
            normed_two, grads_all, picks, router, expert_w, other_w
        )
    else:
        dense_gates = jnp.where(chosen, gates_all, 0.0)
        mixture, d_normed_two, inner, weight_grads = experts(
            normed_two, out_grad[0], dense_gates, *expert_w
        )
    dense = jnp.where(chosen, inner, 0.0)
    d_logits = (gates_all * (dense - jnp.sum(gates_all * dense, axis=-1, keepdims=True))).astype(BF16)
    grad_router = contract_rows(d_logits, normed_two)
    d_normed_two = d_normed_two + contract_cols(d_logits, router)
    grad_moe_gain = jnp.sum(d_normed_two * middle * scale_two, axis=0)
    weighted_two = d_normed_two * gain_two
    d_middle = (
        grad_out
        + scale_two * weighted_two
        - middle * scale_two**3 * jnp.mean(weighted_two * middle, axis=-1, keepdims=True)
    )

    d_attn = d_middle.astype(BF16)
    if here:
        early = jnp.concatenate([grad_moe_gain[None], jnp.zeros((7, width), F32), grad_router])
        d_attn_row, d_heads, mixed_rows, mixture, early = attend_back_stage(
            d_attn, query, key_all, value_all, mixed_wide, total, cuts, out_w, out_parts, early, scale, 2
        )
        grad_hidden, grad_qkv, grad_w_out, late = tail_stage(
            d_heads, qkv.reshape(row_tok, -1), totals, gain_q.reshape(1, -1), gain_k.reshape(1, -1),
            cosine[:, 0], signed, qkv_w, normed_row, mixed_rows, d_attn_row,
            hidden_in[0], attn_gain, d_middle, 3,
        )
        final = middle + mixture.astype(F32)
        summed = (late[0], late[1], late[2], early[0], early[8:])
    else:
        final = middle + mixture
        mixed_row = heads_to_rows(mixed).reshape(row_tok, plane)
        d_mixed = tokens_to_heads(contract_cols(d_attn, out_w).astype(BF16))
        d_attn_row = lax.all_gather(d_attn, "col", axis=0, tiled=True)
        d_query, acc_key, acc_value = attend_back(
            query, key_all, value_all, d_mixed, mixed_wide, total, cuts, scale
        )
        accumulated = jnp.concatenate([acc_key, acc_value], axis=1)
        lower_acc, upper_acc = accumulated[:group_tok], accumulated[group_tok:]
        kept_acc = jnp.where(side == 0, lower_acc, upper_acc)
        later_acc = from_behind(lower_acc.astype(BF16), "exp", -1).astype(F32)
        summed_pair = kept_acc + jnp.where(side == 0, later_acc, jnp.zeros_like(later_acc))
        d_heads = heads_to_rows(jnp.concatenate([d_query, summed_pair], axis=1).astype(BF16)).astype(F32)
        d_q_unit = rotate_back(d_heads[:, :, :HD], cosine, sine)
        d_k_unit = rotate_back(d_heads[:, :, HD : 2 * HD], cosine, sine)
        d_value = d_heads[:, :, 2 * HD :]
        weighted_q = d_q_unit * gain_q
        weighted_k = d_k_unit * gain_k
        sum_q, sum_k = lax.psum(
            (jnp.sum(weighted_q * query_raw, axis=(1, 2)), jnp.sum(weighted_k * key_raw, axis=(1, 2))),
            "col",
        )
        d_query_raw = scale_q * weighted_q - query_raw * scale_q**3 * (sum_q / width)[:, None, None]
        d_key_raw = scale_k * weighted_k - key_raw * scale_k**3 * (sum_k / width)[:, None, None]
        grad_q_part = jnp.sum(d_q_unit * query_raw * scale_q, axis=0).reshape(plane)
        grad_k_part = jnp.sum(d_k_unit * key_raw * scale_k, axis=0).reshape(plane)
        d_qkv = jnp.concatenate([d_query_raw, d_key_raw, d_value], axis=2).astype(BF16)
        d_qkv = d_qkv.reshape(row_tok, heads * 3 * HD)
        d_normed_one = lax.psum_scatter(
            contract_cols(d_qkv, qkv_w).astype(BF16), "col", scatter_dimension=0, tiled=True
        ).astype(F32)
        grad_qkv = lax.psum_scatter(
            contract_rows(normed_row, d_qkv).astype(BF16), "row", scatter_dimension=0, tiled=True
        )
        grad_w_out = lax.psum_scatter(
            contract_rows(mixed_row, d_attn_row).astype(BF16), "row", scatter_dimension=1, tiled=True
        )
        grad_qkv = lax.psum(grad_qkv, "exp").astype(F32)
        grad_w_out = lax.psum(grad_w_out, "exp").astype(F32)
        grad_attn_gain = jnp.sum(d_normed_one * tokens * scale_one, axis=0)
        weighted_one = d_normed_one * gain_one
        grad_hidden = (
            d_middle
            + scale_one * weighted_one
            - tokens * scale_one**3 * jnp.mean(weighted_one * tokens, axis=-1, keepdims=True)
        )
        empty = jnp.zeros((width,), F32)
        grad_q_full = lax.dynamic_update_slice_in_dim(empty, grad_q_part, head_start, 0)
        grad_k_full = lax.dynamic_update_slice_in_dim(empty, grad_k_part, head_start, 0)
        parts = (grad_attn_gain, grad_q_full, grad_k_full, grad_moe_gain)
        summed = lax.psum(parts + (grad_router,), ALL)
    return (
        final.astype(BF16)[None],
        grad_hidden[None],
        summed[0],
        grad_qkv,
        summed[1],
        summed[2],
        grad_w_out,
        summed[3],
        summed[4].T,
        weight_grads[0][None],
        weight_grads[1][None],
        weight_grads[2][None],
    )


def solution(mesh):
    token_spec = P("exp", ("row", "col"), None)
    expert_spec = P(("row", "col", "exp"), None, None)
    in_specs = (
        token_spec,
        token_spec,
        P(),
        P("row", "col"),
        P(),
        P(),
        P("col", "row"),
        P(),
        P(),
        expert_spec,
        expert_spec,
        expert_spec,
        token_spec,
        P(),
    )
    out_specs = (
        token_spec,
        token_spec,
        P(),
        P("row", "col"),
        P(),
        P(),
        P("col", "row"),
        P(),
        P(),
        expert_spec,
        expert_spec,
        expert_spec,
    )
    return jax.shard_map(shards, mesh=mesh, in_specs=in_specs, out_specs=out_specs, check_vma=False)
```

```python
import functools
import math

import jax
import jax.numpy as jnp
from jax import lax
from jax.experimental import pallas as pl
from jax.experimental.pallas import tpu as pltpu
from jax.sharding import PartitionSpec as P

HD = 128
EPSILON = 1e-05
ROPE_BASE = 10000.0
MASKED = -1e30
BF16 = jnp.bfloat16
F32 = jnp.float32


def matmul(left, right):
    return jnp.dot(left, right, preferred_element_type=F32)


def contract_rows(left, right):
    return lax.dot_general(left, right, (((0,), (0,)), ((), ())), preferred_element_type=F32)


def contract_cols(left, right):
    return lax.dot_general(left, right, (((1,), (1,)), ((), ())), preferred_element_type=F32)


def rms_scale(values):
    return lax.rsqrt(jnp.mean(values * values, axis=-1, keepdims=True) + EPSILON)


def rope_tables(position, width):
    frequency = ROPE_BASE ** (-jnp.arange(0, width, 2, dtype=F32) / width)
    angle = position.astype(F32)[:, None] * frequency[None, :]
    return (
        jnp.concatenate([jnp.cos(angle)] * 2, axis=-1),
        jnp.concatenate([jnp.sin(angle)] * 2, axis=-1),
    )


def rotate(values, cosine, sine):
    half = values.shape[-1] // 2
    turned = jnp.concatenate([-values[..., half:], values[..., :half]], axis=-1)
    return values * cosine + turned * sine


def rotate_back(values, cosine, sine):
    half = values.shape[-1] // 2
    turned = values * sine
    return values * cosine + jnp.concatenate([turned[..., half:], -turned[..., :half]], axis=-1)


def doc_positions(places, cuts):
    first = (places >= cuts[0]).astype(jnp.int32)
    second = (places >= cuts[1]).astype(jnp.int32)
    start = first * cuts[0] + second * (cuts[1] - cuts[0])
    return (first + second, places - start)


def from_behind(value, axis, steps):
    count = lax.axis_size(axis)
    initial, last = (max(0, -steps), min(count, count - steps))
    return lax.ppermute(value, axis, [(source, source + steps) for source in range(initial, last)])


def rows_to_heads(values):
    count = lax.axis_size("row")
    rows, heads, width = values.shape
    moved = lax.all_to_all(values.transpose(1, 0, 2), "row", split_axis=0, concat_axis=0, tiled=True)
    return moved.reshape(count * rows, width)


def heads_to_rows(values):
    count = lax.axis_size("row")
    rows, width = values.shape
    moved = lax.all_to_all(
        values.reshape(count, rows // count, width), "row", split_axis=0, concat_axis=0, tiled=True
    )
    return moved.transpose(1, 0, 2)


def heads_to_tokens(values):
    row_count, col_count = lax.axis_size("row"), lax.axis_size("col")
    rows = values.shape[0] // (row_count * col_count)
    moved = lax.all_to_all(
        values.reshape(row_count * col_count, rows, HD),
        ("row", "col"),
        split_axis=0,
        concat_axis=0,
        tiled=True,
    )
    moved = moved.reshape(row_count, col_count, rows, HD).transpose(2, 1, 0, 3)
    return moved.reshape(rows, row_count * col_count * HD)


def tokens_to_heads(values):
    row_count, col_count = lax.axis_size("row"), lax.axis_size("col")
    rows = values.shape[0]
    parted = values.reshape(rows, col_count, row_count, HD).transpose(2, 1, 0, 3)
    moved = lax.all_to_all(
        parted.reshape(row_count * col_count, rows, HD),
        ("row", "col"),
        split_axis=0,
        concat_axis=0,
        tiled=True,
    )
    return moved.reshape(row_count * col_count * rows, HD)


MESH = pl.DeviceIdType.MESH
ALL = ("row", "col", "exp")


class Here:
    def __init__(self):
        self.row, self.col, self.core = (lax.axis_index(axis) for axis in ALL)
        self.across = self.row + 1 - 2 * (self.row % 2)
        self.along = (self.row + 2) % 4
        self.opposite = 3 - self.row
        self.rows = (self.row, self.across, self.along, self.opposite)
        half = self.col // 2
        self.near_first = [
            self.col,
            1 + self.col % 2,
            2 - self.col - self.col % 2 + 3 * half,
            3 - 3 * half,
        ]

    def at_row(self, row):
        return (row, self.col, self.core)

    def at_col(self, col):
        return (self.row, col, self.core)

    def other_core(self):
        return (self.row, self.col, 1 - self.core)

    def line_peers(self):
        return [self.at_col((self.col + step) % 4) for step in (1, 2, 3)]

    def group_peers(self):
        steps = range(1, 16)
        return [((self.row + s // 4) % 4, (self.col + s) % 4, self.core) for s in steps]

    def plane_peers(self):
        return [self.at_row(row) for row in self.rows[1:]]


def greet(peers):
    barrier = pltpu.get_barrier_semaphore()
    for peer in peers:
        pl.semaphore_signal(barrier, inc=1, device_id=peer, device_id_type=MESH)
    pl.semaphore_wait(barrier, len(peers))


def greet_near(here):
    barrier = pltpu.get_barrier_semaphore()
    col = here.col

    def signal(peer):
        pl.semaphore_signal(barrier, inc=1, device_id=peer, device_id_type=MESH)

    for peer in (here.other_core(), here.at_row(here.across), here.at_row(here.along)):
        signal(peer)

    @pl.when(col > 0)
    def _():
        signal(here.at_col(col - 1))

    @pl.when(col < 3)
    def _():
        signal(here.at_col(col + 1))

    pl.semaphore_wait(barrier, 3 + (col + 3) // 4 + (6 - col) // 4)


def remote(source, target, send, recv, device):
    return pltpu.make_async_remote_copy(
        src_ref=source,
        dst_ref=target,
        send_sem=send,
        recv_sem=recv,
        device_id=device,
        device_id_type=MESH,
    )


def arrived(target, recv):
    pltpu.make_async_copy(target, target, recv).wait()


def add_into(target, *terms):
    step = 16

    @pl.loop(0, target.shape[0] // step)
    def _(index):
        part = pl.ds(pl.multiple_of(index * step, step), step)
        value = target[part].astype(F32)
        for term in terms:
            value = value + term[part].astype(F32)
        target[part] = value.astype(target.dtype)


SPREAD_SEMS = [pltpu.SemaphoreType.DMA((4,))] * 11 + [pltpu.SemaphoreType.DMA((4, 4))] * 2


class Spread:
    def __init__(self, here, own, block, rows, sems, line=True, plane=True, core=True):
        self.here, self.own, self.block = here, own, block
        self.line, self.plane, self.core = line, plane, core
        (
            self.up_send, self.down_send, self.line_recv,
            self.across_send, self.across_recv, self.along_send, self.along_recv,
            self.one_send, self.one_recv, self.two_send, self.two_recv,
            self.core_send, self.core_recv,
        ) = sems
        self.first, self.second = pl.ds(0, rows // 2), pl.ds(rows // 2, rows // 2)
        self.order = here.near_first if line else [0]
        self.steps = len(self.order)

    def held(self, step):
        here = self.here
        return self.own if step == 0 else self.block(here.row, self.order[step], here.core)

    def up(self, step):
        here, place = self.here, self.order[step]
        target = self.block(here.row, place, here.core)
        recv = self.line_recv.at[place]
        return remote(self.held(step), target, self.up_send.at[place], recv, here.at_col(here.col + 1))

    def down(self, step):
        here, place = self.here, self.order[step]
        target = self.block(here.row, place, here.core)
        recv = self.line_recv.at[place]
        return remote(self.held(step), target, self.down_send.at[place], recv, here.at_col(here.col - 1))

    def to_across(self, step):
        here, place = self.here, self.order[step]
        target = self.block(here.row, place, here.core)
        sems = self.across_send.at[place], self.across_recv.at[place]
        return remote(self.held(step), target, *sems, here.at_row(here.across))

    def to_along(self, step):
        here, place = self.here, self.order[step]
        target = self.block(here.row, place, here.core)
        sems = self.along_send.at[place], self.along_recv.at[place]
        return remote(self.held(step), target, *sems, here.at_row(here.along))

    def corner_one(self, step):
        here, place = self.here, self.order[step]
        part = self.block(here.across, place, here.core).at[self.first]
        sems = self.one_send.at[place], self.one_recv.at[place]
        return remote(part, part, *sems, here.at_row(here.along))

    def corner_two(self, step):
        here, place = self.here, self.order[step]
        part = self.block(here.along, place, here.core).at[self.second]
        sems = self.two_send.at[place], self.two_recv.at[place]
        return remote(part, part, *sems, here.at_row(here.across))

    def to_core(self, which, step):
        here, place = self.here, self.order[step]
        target = self.block(here.rows[which], place, here.core)
        source = self.held(step) if which == 0 else target
        sems = self.core_send.at[which, place], self.core_recv.at[which, place]
        return remote(source, target, *sems, here.other_core())

    def line_step(self, step):
        here, place = self.here, self.order[step]
        if step > 0:
            arrived(self.held(step), self.line_recv.at[place])
        if self.line:

            @pl.when((place <= here.col) & (here.col < 3))
            def _():
                self.up(step).start()

            @pl.when((place >= here.col) & (here.col > 0))
            def _():
                self.down(step).start()

        if self.plane:
            self.to_across(step).start()
            self.to_along(step).start()
            if self.core:
                self.to_core(0, step).start()

    def plane_step(self, step):
        here, place = self.here, self.order[step]
        arrived(self.block(here.across, place, here.core), self.across_recv.at[place])
        self.corner_one(step).start()
        if self.core:
            self.to_core(1, step).start()
        arrived(self.block(here.along, place, here.core), self.along_recv.at[place])
        self.corner_two(step).start()
        if self.core:
            self.to_core(2, step).start()

    def corner_step(self, step):
        here, place = self.here, self.order[step]
        target = self.block(here.opposite, place, here.core)
        arrived(target.at[self.first], self.one_recv.at[place])
        arrived(target.at[self.second], self.two_recv.at[place])
        if self.core:
            self.to_core(3, step).start()

    def step(self, index):
        if index < self.steps:
            self.line_step(index)
        if self.plane and 0 <= index - 1 < self.steps:
            self.plane_step(index - 1)
        if self.plane and 0 <= index - 2 < self.steps:
            self.corner_step(index - 2)

    def core_arrived(self, which, step):
        here, place = self.here, self.order[step]
        target = self.block(here.rows[which], place, 1 - here.core)
        arrived(target, self.core_recv.at[which, place])

    def finish(self, arrivals=True):
        here = self.here
        for step in range(self.steps):
            place = self.order[step]
            if self.line:

                @pl.when((place <= here.col) & (here.col < 3))
                def _():
                    self.up(step).wait_send()

                @pl.when((place >= here.col) & (here.col > 0))
                def _():
                    self.down(step).wait_send()

            if self.plane:
                self.to_across(step).wait_send()
                self.to_along(step).wait_send()
                self.corner_one(step).wait_send()
                self.corner_two(step).wait_send()
                for which in range(4 if self.core else 0):
                    self.to_core(which, step).wait_send()
                    if arrivals:
                        self.core_arrived(which, step)


COLLECT_SEMS = (
    [pltpu.SemaphoreType.DMA((4,))] * 4
    + [pltpu.SemaphoreType.DMA((2, 4))] * 4
    + [pltpu.SemaphoreType.DMA((4,))] * 2
    + [pltpu.SemaphoreType.DMA((5,))]
)


def collect_buffers(rows, width):
    return [
        pltpu.VMEM((4, 4, rows, width), BF16),
        pltpu.VMEM((4, rows // 2, width), BF16),
        pltpu.VMEM((4, rows // 2, width), BF16),
        pltpu.VMEM((4, rows, width), BF16),
        pltpu.VMEM((4, rows, width), BF16),
        pltpu.VMEM((5, rows, width), BF16),
    ]


class Collect:
    def __init__(self, here, buffers, sems):
        self.here = here
        self.mine, self.one, self.two, self.from_across, self.from_along, self.line = buffers
        (
            self.one_send, self.one_recv, self.two_send, self.two_recv,
            self.across_send, self.across_recv, self.along_send, self.along_recv,
            self.up_send, self.down_send, self.line_recv,
        ) = sems
        half = self.mine.shape[2] // 2
        self.halves = (pl.ds(0, half), pl.ds(half, half))

    def give_one(self, place):
        here = self.here
        return remote(
            self.mine.at[3, place, self.halves[0]], self.one.at[place],
            self.one_send.at[place], self.one_recv.at[place], here.at_row(here.across),
        )

    def give_two(self, place):
        here = self.here
        return remote(
            self.mine.at[3, place, self.halves[1]], self.two.at[place],
            self.two_send.at[place], self.two_recv.at[place], here.at_row(here.along),
        )

    def give_across(self, place, half):
        here, part = self.here, self.halves[half]
        return remote(
            self.mine.at[1, place, part], self.from_across.at[place, part],
            self.across_send.at[half, place], self.across_recv.at[half, place], here.at_row(here.across),
        )

    def give_along(self, place, half):
        here, part = self.here, self.halves[half]
        return remote(
            self.mine.at[2, place, part], self.from_along.at[place, part],
            self.along_send.at[half, place], self.along_recv.at[half, place], here.at_row(here.along),
        )

    def give_up(self, place):
        here = self.here
        sems = self.up_send.at[place], self.line_recv.at[place]
        return remote(self.mine.at[0, place], self.line.at[place], *sems, here.at_col(here.col + 1))

    def give_down(self, place, slot):
        here = self.here
        sems = self.down_send.at[place], self.line_recv.at[slot]
        return remote(self.mine.at[0, place], self.line.at[slot], *sems, here.at_col(here.col - 1))

    def start_far(self, place):
        self.give_one(place).start()
        self.give_two(place).start()
        self.give_along(place, 1).start()

    def start_near(self, place):
        self.give_across(place, 0).start()

    def corner_step(self, place):
        self.give_two(place).wait_recv()
        add_into(self.mine.at[1, place, self.halves[1]], self.two.at[place])
        self.give_across(place, 1).start()
        self.give_one(place).wait_recv()
        add_into(self.mine.at[2, place, self.halves[0]], self.one.at[place])
        self.give_along(place, 0).start()

    def plane_step(self, place):
        for half in range(2):
            self.give_across(place, half).wait_recv()
            self.give_along(place, half).wait_recv()
        add_into(self.mine.at[0, place], self.from_across.at[place], self.from_along.at[place])

    def line_step(self, place):
        col = self.here.col

        @pl.when((place > col) & (col > 0))
        def _():
            self.give_up(place).wait_recv()
            add_into(self.mine.at[0, place], self.line.at[place])

        @pl.when((place < col) & (col < 3))
        def _():
            self.give_down(place, place).wait_recv()
            add_into(self.mine.at[0, place], self.line.at[place])

        @pl.when(place > col)
        def _():
            self.give_up(place).start()

        @pl.when(place < col - 1)
        def _():
            self.give_down(place, place).start()

        @pl.when(place == col - 1)
        def _():
            self.give_down(place, 4).start()

    def own_step(self):
        col = self.here.col

        @pl.when(col > 0)
        def _():
            self.give_up(col).wait_recv()
            add_into(self.mine.at[0, col], self.line.at[col])

        @pl.when(col < 3)
        def _():
            self.give_down(col, 4).wait_recv()
            add_into(self.mine.at[0, col], self.line.at[4])

    def finish(self):
        col = self.here.col
        for place in range(4):
            self.give_one(place).wait_send()
            self.give_two(place).wait_send()
            for half in range(2):
                self.give_across(place, half).wait_send()
                self.give_along(place, half).wait_send()

            @pl.when(place > col)
            def _():
                self.give_up(place).wait_send()

            @pl.when(place < col)
            def _():
                self.give_down(place, place).wait_send()


def doc_start(places, cuts):
    return jnp.where(places >= cuts[1], cuts[1], jnp.where(places >= cuts[0], cuts[0], 0))


def key_blocks(cuts, first_query, rows, scores_of, block_fn):
    def scan(index, carry):
        start = pl.multiple_of(index * rows, rows)
        free = (start >= doc_start(first_query + rows - 1, cuts)) & (start + rows <= first_query + 1)

        @pl.when(free)
        def _():
            block_fn(start, scores_of(start))

        @pl.when(jnp.logical_not(free))
        def _():
            key_place = start + lax.broadcasted_iota(jnp.int32, (rows, rows), 0)
            place = first_query + lax.broadcasted_iota(jnp.int32, (1, rows), 1)
            allowed = (key_place <= place) & (key_place >= doc_start(place, cuts))
            block_fn(start, jnp.where(allowed, scores_of(start), MASKED))

        return carry

    lax.fori_loop(doc_start(first_query, cuts) // rows, first_query // rows + 1, scan, 0)


def attend_kernel(scale, group_tok, cuts, query, keys, values_t, mixed, total, top, summed, acc):
    rows = query.shape[0]
    side = lax.axis_index("exp") % 2
    first_query = side * group_tok + pl.program_id(0) * rows
    top[...] = jnp.full_like(top, MASKED)
    summed[...] = jnp.zeros_like(summed)
    acc[...] = jnp.zeros_like(acc)
    cut = (cuts[0, 0], cuts[0, 1])

    def scores_of(start):
        return contract_cols(keys[pl.ds(start, rows)], query[...]) * scale

    def block_fn(start, scores):
        old = top[...]
        new = jnp.maximum(old, jnp.max(scores, axis=0, keepdims=True))
        weights = jnp.exp(scores - new)
        decay = jnp.exp(old - new)
        top[...] = new
        summed[...] = summed[...] * decay + jnp.sum(weights, axis=0, keepdims=True)
        acc[...] = acc[...] * decay + matmul(values_t[:, pl.ds(start, rows)], weights.astype(BF16))

    key_blocks(cut, first_query, rows, scores_of, block_fn)
    mixed[...] = (acc[...] / summed[...]).T
    total[...] = top[...] + jnp.log(summed[...])


def attend(query, keys, values, cuts, scale, rows=512):
    group_tok, head_size = query.shape
    whole = lambda shape: pl.BlockSpec(shape, lambda i: (0, 0))
    return pl.pallas_call(
        functools.partial(attend_kernel, scale, group_tok),
        grid=(group_tok // rows,),
        in_specs=[
            pl.BlockSpec(memory_space=pltpu.SMEM),
            pl.BlockSpec((rows, head_size), lambda i: (i, 0)),
            whole(keys.shape),
            whole(values.shape[::-1]),
        ],
        out_specs=[
            pl.BlockSpec((rows, head_size), lambda i: (i, 0)),
            pl.BlockSpec((1, rows), lambda i: (0, i)),
        ],
        out_shape=[
            jax.ShapeDtypeStruct((group_tok, head_size), F32),
            jax.ShapeDtypeStruct((1, group_tok), F32),
        ],
        scratch_shapes=[
            pltpu.VMEM((1, rows), F32),
            pltpu.VMEM((1, rows), F32),
            pltpu.VMEM((head_size, rows), F32),
        ],
        compiler_params=pltpu.CompilerParams(vmem_limit_bytes=40 * 2**20),
        cost_estimate=pl.CostEstimate(
            flops=4 * 7 * 2**20 * head_size, bytes_accessed=2**23, transcendentals=7 * 2**20
        ),
    )(cuts[None], query, keys, values.T)


def attend_back_kernel(
    scale, group_tok, cuts, query, keys, keys_t, values, d_mixed, total, delta,
    d_query, d_keys, d_values, acc,
):
    rows = query.shape[0]
    side = lax.axis_index("exp") % 2
    first_query = side * group_tok + pl.program_id(0) * rows
    cut = (cuts[0, 0], cuts[0, 1])

    @pl.when(pl.program_id(0) == 0)
    def _():
        d_keys[...] = jnp.zeros_like(d_keys)
        d_values[...] = jnp.zeros_like(d_values)

    acc[...] = jnp.zeros_like(acc)

    def scores_of(start):
        return contract_cols(keys[pl.ds(start, rows)], query[...]) * scale

    def block_fn(start, scores):
        part = pl.ds(start, rows)
        weights = jnp.exp(scores - total[...])
        d_weights = contract_cols(values[part], d_mixed[...])
        d_scores = (weights * (d_weights - delta[...])).astype(BF16)
        d_values[part] += matmul(weights.astype(BF16), d_mixed[...])
        d_keys[part] += matmul(d_scores, query[...]) * scale
        acc[...] += matmul(keys_t[:, part], d_scores)

    key_blocks(cut, first_query, rows, scores_of, block_fn)
    d_query[...] = (acc[...] * scale).T


def attend_back(query, keys, values, d_mixed, mixed, total, cuts, scale, rows=512):
    group_tok, head_size = query.shape
    delta = jnp.sum(d_mixed.astype(F32) * mixed, axis=1)[None]
    whole = lambda shape: pl.BlockSpec(shape, lambda i: (0, 0))
    block = pl.BlockSpec((rows, head_size), lambda i: (i, 0))
    line = pl.BlockSpec((1, rows), lambda i: (0, i))
    return pl.pallas_call(
        functools.partial(attend_back_kernel, scale, group_tok),
        grid=(group_tok // rows,),
        in_specs=[
            pl.BlockSpec(memory_space=pltpu.SMEM),
            block,
            whole(keys.shape),
            whole(keys.shape[::-1]),
            whole(keys.shape),
            block,
            line,
            line,
        ],
        out_specs=[block, whole(keys.shape), whole(keys.shape)],
        out_shape=[
            jax.ShapeDtypeStruct((group_tok, head_size), F32),
            jax.ShapeDtypeStruct(keys.shape, F32),
            jax.ShapeDtypeStruct(keys.shape, F32),
        ],
        scratch_shapes=[pltpu.VMEM((head_size, rows), F32)],
        compiler_params=pltpu.CompilerParams(vmem_limit_bytes=48 * 2**20),
        cost_estimate=pl.CostEstimate(
            flops=10 * 7 * 2**20 * head_size, bytes_accessed=2**23, transcendentals=7 * 2**20
        ),
    )(cuts[None], query, keys, keys.T, values, d_mixed, total, delta)


def transposed_product(left, right):
    return jnp.dot(left.T, right, preferred_element_type=F32)


def column_of(line):
    return jnp.broadcast_to(line, (128, 128)).T[:, :1]


def line_of(column):
    return jnp.broadcast_to(column, (128, 128)).T[:1]


def expert_kernel(
    expert_count, normed, grads_all, mask, gate_half, up_half, down_half,
    gate_other, up_other, down_other, router,
    rows_all, out_parts, total, inner_in, grad_gate, grad_up, grad_down,
    their_gates, their_down,
    gate_w, up_w, down_w, masks, x_buf, d_buf, gates_t, weighteds_t, d_gates, d_ups, weighteds, out_buf,
    inner, sum_buf, sum_down, *rest,
):
    here = Here()
    row, col, core = here.row, here.col, here.core
    rows, width = normed.shape
    half = gate_half.shape[1]
    expert = row * 4 + col
    count = len(SPREAD_SEMS)
    collect = Collect(here, rest[:6], rest[6 : 6 + len(COLLECT_SEMS)])
    rest = rest[6 + len(COLLECT_SEMS) :]
    (
        weight_sem, load_sem, store_sem, tile_sem, give_send, give_recv, their_sem, sum_sem,
        inner_send, inner_recv,
    ) = rest[:10]
    sems = rest[10:]

    def x_block(of_row, place, unused_core):
        return rows_all.at[pl.ds(pl.multiple_of((of_row * 4 + place) * rows, rows), rows)]

    def d_block(of_row, place, unused_core):
        return grads_all.at[pl.ds(pl.multiple_of((of_row * 4 + place) * rows, rows), rows)]

    def m_block(of_row, place, unused_core):
        return masks.at[of_row, place]

    spread_x = Spread(here, normed, x_block, rows, sems[:count], core=False)
    spread_m = Spread(here, mask, m_block, mask.shape[0], sems[count:], core=False)
    order = here.near_first

    own_half = pl.ds(pl.multiple_of(core * half, half), half)
    other_half = pl.ds(pl.multiple_of((1 - core) * half, half), half)
    keeps = [
        pltpu.make_async_copy(source, target, weight_sem.at[index])
        for index, (source, target) in enumerate(
            (
                (normed, x_block(row, col, 0)),
                (mask, m_block(row, col, 0)),
                (gate_half, gate_w.at[:, own_half]),
                (up_half, up_w.at[:, own_half]),
                (down_half, down_w.at[own_half]),
                (gate_other, gate_w.at[:, other_half]),
                (up_other, up_w.at[:, other_half]),
                (down_other, down_w.at[other_half]),
            )
        )
    ]
    greet(here.group_peers() + [here.other_core()])
    spread_x.step(0)
    spread_m.step(0)
    for keep in keeps:
        keep.start()

    turns = (3, 2, 1, 0)

    def loads(step):
        return [
            pltpu.make_async_copy(
                source(here.rows[which], order[step], 0),
                target.at[pl.ds(position * rows, rows)],
                load_sem.at[position, array],
            )
            for position, which in enumerate(turns)
            for array, (source, target) in enumerate(((x_block, x_buf), (d_block, d_buf)))
        ]

    def stores(step):
        return [
            pltpu.make_async_copy(
                out_buf.at[pl.ds(position * rows, rows)],
                out_parts.at[which, order[step]],
                store_sem.at[position],
            )
            for position, which in enumerate(turns)
        ]

    tile = 256

    def first_products(step):
        place = order[step]
        x = x_buf[...]
        lane = lax.broadcasted_iota(jnp.int32, (x.shape[0], router.shape[1]), 1)
        logits = jnp.where(lane < expert_count, matmul(x, router[...]), MASKED)
        raised = jnp.exp(logits - jnp.max(logits, axis=1, keepdims=True))
        picked = jnp.sum(jnp.where(lane == expert, raised, 0.0), axis=1, keepdims=True)
        routed = jnp.concatenate(
            [column_of(masks[here.rows[which], place, pl.ds(expert, 1)]) for which in turns]
        )
        gate = picked / jnp.sum(raised, axis=1, keepdims=True) * routed
        columns = [
            pl.ds(pl.multiple_of((here.rows[which] * 4 + place) * rows, rows), rows) for which in turns
        ]

        def tile_step(index, inner_sum):
            at = pl.ds(pl.multiple_of(index * tile, tile), tile)
            pre_gate = matmul(x_buf[...], gate_w[:, at])
            pre_up = matmul(x_buf[...], up_w[:, at])
            back = contract_cols(d_buf[...], down_w[at])
            sigmoid_gate = 1.0 / (1.0 + jnp.exp(-pre_gate))
            silu_gate = pre_gate * sigmoid_gate
            hidden = (silu_gate * pre_up).astype(BF16).astype(F32)
            d_hid = back * gate
            d_gate = (d_hid * pre_up * (sigmoid_gate + silu_gate * (1.0 - sigmoid_gate))).astype(BF16)
            d_up = (d_hid * silu_gate).astype(BF16)
            weight = (hidden * gate).astype(BF16)
            d_gates[:, at] = d_gate
            d_ups[:, at] = d_up
            weighteds[:, at] = weight
            side = index // (half // tile)
            first = pl.multiple_of(index % (half // tile) * tile, tile)
            for values, target in (
                (d_gate, gates_t.at[side, pl.ds(first, tile)]),
                (d_up, gates_t.at[side, pl.ds(first + half, tile)]),
                (weight, weighteds_t.at[at]),
            ):
                turned = values.T
                for position, column in enumerate(columns):
                    target[:, column] = turned[:, position * rows : (position + 1) * rows]
            return inner_sum + jnp.sum(hidden * back, axis=1, keepdims=True)

        start = jnp.zeros((x.shape[0], 1), F32)
        inner_sum = lax.fori_loop(0, gate_w.shape[1] // tile, tile_step, start)
        for position, which in enumerate(turns):
            part = slice(position * rows, (position + 1) * rows)
            inner[here.rows[which], place, 0:1] = line_of(inner_sum[part])

    def second_products(step):
        place = order[step]

        @pl.loop(0, width // tile)
        def _(index):
            at = pl.ds(pl.multiple_of(index * tile, tile), tile)
            out_buf[:, at] = matmul(weighteds[...], down_w[:, at]).astype(BF16)
            d_x = contract_cols(d_gates[...], gate_w[at]) + contract_cols(d_ups[...], up_w[at])
            d_x = d_x.astype(BF16)
            for position, which in enumerate(turns):
                collect.mine[which, place, :, at] = d_x[position * rows : (position + 1) * rows]

    for index in (1, 2):
        spread_x.step(index)
        spread_m.step(index)
    for keep in keeps:
        keep.wait()
    for copy in loads(0):
        copy.start()
    turn_order = (0, 1, 3, 2)
    ends = (col == 0) | (col == 3)

    def from_ends(step):
        @pl.when(ends)
        def _():
            collect.line_step(order[step])

    def from_inside(step):
        @pl.when(jnp.logical_not(ends))
        def _():
            collect.line_step(order[step])

    for turn, step in enumerate(turn_order):
        for copy in loads(step):
            copy.wait()
        first_products(step)
        if turn < 2:
            spread_x.step(turn + 3)
            spread_m.step(turn + 3)
        if turn in (0, 2):
            for copy in loads(turn_order[turn + 1]):
                copy.start()
        if turn > 0:
            for copy in stores(turn_order[turn - 1]):
                copy.wait()
            collect.corner_step(order[turn_order[turn - 1]])
        second_products(step)
        for copy in stores(step):
            copy.start()
        collect.start_far(order[step])
        collect.start_near(order[step])
        if turn == 1:
            spread_x.step(5)
            spread_m.step(5)
            for copy in loads(turn_order[2]):
                copy.start()
        if turn > 0:
            collect.plane_step(order[turn_order[turn - 1]])
        if turn > 1:
            from_ends(turn_order[turn - 1])

    tiles = width // tile

    def tile_at(index):
        return pl.ds(pl.multiple_of(index * tile, tile), tile)

    def acts_of(kind, side):
        if kind == 0:
            return gates_t[side]
        return weighteds_t[pl.ds(pl.multiple_of(side * half, half), half)]

    counts = (2 * half, half)

    def slot_at(kind, slot):
        return pl.ds(pl.multiple_of((2 * kind + slot) * tile, tile), tile)

    def tile_buf(kind, slot):
        return gate_w.at[:, slot_at(kind, slot)]

    def give_buf(kind, slot):
        return up_w.at[pl.ds(0, counts[kind]), slot_at(kind, slot)]

    def their_buf(kind, slot):
        return up_w.at[pl.ds(width // 2, counts[kind]), slot_at(kind, slot)]

    theirs = (their_gates, their_down)

    def tile_load(kind, index, slot):
        source = (rows_all, grads_all)[kind]
        return pltpu.make_async_copy(
            source.at[:, tile_at(index)], tile_buf(kind, slot), tile_sem.at[slot]
        )

    def give(kind, index, slot):
        sems = give_send.at[slot, kind], give_recv.at[kind, index]
        return remote(give_buf(kind, slot), theirs[kind].at[:, tile_at(index)], *sems, here.other_core())

    def their_load(kind, index, slot):
        return pltpu.make_async_copy(
            theirs[kind].at[:, tile_at(index)],
            their_buf(kind, slot),
            their_sem.at[slot, kind],
        )

    def sum_stores(kind, index, slot):
        if kind == 1:
            target = grad_down.at[:, tile_at(index)]
            return [pltpu.make_async_copy(sum_down, target, sum_sem.at[0, 2])]
        return [
            pltpu.make_async_copy(
                sum_buf.at[slot, part], target.at[tile_at(index)], sum_sem.at[slot, part]
            )
            for part, target in enumerate((grad_gate, grad_up))
        ]

    def give_gradients(kind, start, stop):
        tile_load(kind, start, 0).start()

        @pl.loop(start, stop)
        def _(index):
            slot = index % 2

            @pl.when(index + 1 < stop)
            def _():
                tile_load(kind, index + 1, 1 - slot).start()

            tile_load(kind, index, slot).wait()
            product = matmul(acts_of(kind, 1 - core), tile_buf(kind, slot)[...])

            @pl.when(index >= 2)
            def _():
                give(kind, index - 2, slot).wait_send()

            give_buf(kind, slot)[...] = product.astype(BF16)
            give(kind, index, slot).start()

    def keep_gradients(kind, start, stop):
        tile_load(kind, start, 0).start()
        give(kind, start, 0).wait_recv()
        their_load(kind, start, 0).start()

        @pl.loop(start, stop)
        def _(index):
            slot = index % 2

            @pl.when(index + 1 < stop)
            def _():
                tile_load(kind, index + 1, 1 - slot).start()
                give(kind, index + 1, 1 - slot).wait_recv()
                their_load(kind, index + 1, 1 - slot).start()

            tile_load(kind, index, slot).wait()
            product = matmul(acts_of(kind, core), tile_buf(kind, slot)[...])
            their_load(kind, index, slot).wait()
            product = product + their_buf(kind, slot)[...].astype(F32)
            held = 2 - kind

            @pl.when(index >= held)
            def _():
                for copy in sum_stores(kind, index - held, slot):
                    copy.wait()

            if kind == 1:
                sum_down[...] = product
            else:
                sum_buf[slot, 0] = product[:half].T
                sum_buf[slot, 1] = product[half:].T
            for copy in sum_stores(kind, index, slot):
                copy.start()

    def give_inner(index):
        step = index + 1
        to_row, to_col = (row + step // 4) % 4, (col + step) % 4
        return remote(
            inner.at[to_row, to_col],
            inner_in.at[row, col],
            inner_send.at[index],
            inner_recv.at[row, col],
            (to_row, to_col, core),
        )

    for index in range(15):
        give_inner(index).start()
    inner_in[row, col] = inner[row, col]
    give_gradients(0, 0, tiles // 2)
    from_inside(3)
    collect.corner_step(order[2])
    give_gradients(0, tiles // 2, tiles)
    collect.plane_step(order[2])
    from_ends(2)
    give_gradients(1, 0, tiles)
    from_inside(2)
    keep_gradients(0, 0, tiles // 2)
    from_inside(1)
    keep_gradients(0, tiles // 2, tiles)
    keep_gradients(1, 0, tiles)
    collect.own_step()
    total[...] = collect.mine[0, col]

    for index in range(15):
        give_inner(index).wait_send()
        step = index + 1
        from_row, from_col = (row + 4 - step // 4) % 4, (col + 4 - step % 4) % 4
        arrived(inner_in.at[from_row, from_col], inner_recv.at[from_row, from_col])
    for copy in stores(turn_order[3]):
        copy.wait()
    for kind in range(2):
        for slot in range(2):
            give(kind, tiles - 2 + slot, slot).wait_send()
        for slot in range(2 - kind):
            for copy in sum_stores(kind, tiles - 2 + kind + slot, slot):
                copy.wait()
    spread_x.finish()
    spread_m.finish()
    collect.finish()


def expert_stage(normed, grads_all, mask, halves, others, router, collective_id):
    rows, width = normed.shape
    half = halves[0].shape[1]
    expert_count = router.shape[1]
    router = jnp.pad(router, ((0, 0), (0, 128 - expert_count)))
    tokens = 16 * rows
    tile = 256
    vmem = pl.BlockSpec(memory_space=pltpu.VMEM)
    hbm = pl.BlockSpec(memory_space=pl.ANY)
    dma = pltpu.SemaphoreType.DMA
    blocks = jax.ShapeDtypeStruct((4, 4, rows, width), BF16)
    got = pl.pallas_call(
        functools.partial(expert_kernel, expert_count),
        in_specs=[hbm] * 9 + [vmem],
        out_specs=[hbm] * 2 + [vmem] * 2 + [hbm] * 5,
        out_shape=[
            jax.ShapeDtypeStruct((tokens, width), BF16),
            blocks,
            jax.ShapeDtypeStruct((rows, width), BF16),
            jax.ShapeDtypeStruct((4, 4, 8, rows), F32),
            jax.ShapeDtypeStruct((width, half), F32),
            jax.ShapeDtypeStruct((width, half), F32),
            jax.ShapeDtypeStruct((half, width), F32),
            jax.ShapeDtypeStruct((2 * half, width), BF16),
            jax.ShapeDtypeStruct((half, width), BF16),
        ],
        scratch_shapes=[
            pltpu.VMEM((width, 2 * half), BF16),
            pltpu.VMEM((width, 2 * half), BF16),
            pltpu.VMEM((2 * half, width), BF16),
            pltpu.VMEM((4, 4) + mask.shape, F32),
            pltpu.VMEM((4 * rows, width), BF16),
            pltpu.VMEM((4 * rows, width), BF16),
            pltpu.VMEM((2, 2 * half, tokens), BF16),
            pltpu.VMEM((2 * half, tokens), BF16),
            pltpu.VMEM((4 * rows, 2 * half), BF16),
            pltpu.VMEM((4 * rows, 2 * half), BF16),
            pltpu.VMEM((4 * rows, 2 * half), BF16),
            pltpu.VMEM((4 * rows, width), BF16),
            pltpu.VMEM((4, 4, 8, rows), F32),
            pltpu.VMEM((2, 2, tile, half), F32),
            pltpu.VMEM((half, tile), F32),
        ]
        + collect_buffers(rows, width)
        + COLLECT_SEMS
        + [
            dma((8,)), dma((4, 2)), dma((4,)),
            dma((2,)), dma((2, 2)), dma((2, width // tile)), dma((2, 2)), dma((2, 3)),
            dma((15,)), dma((4, 4)),
        ]
        + SPREAD_SEMS * 2,
        compiler_params=pltpu.CompilerParams(
            collective_id=collective_id, has_side_effects=True, vmem_limit_bytes=61 * 2**20
        ),
        cost_estimate=pl.CostEstimate(
            flops=18 * 2 * tokens * width * half,
            bytes_accessed=2**26,
            transcendentals=2 * tokens * half,
        ),
    )(normed, grads_all, mask, *halves, *others, router)
    return got[1], got[2], got[3], got[4:7]


def project_kernel(
    hidden, gain, weights, q_gain, k_gain, cosine, sine,
    normed, all_weights, qkv, totals, query, keys, values,
    heads, stat, scale_q, scale_k, kept_sem, kept_kv_sem,
    stat_send, stat_recv, head_send, head_recv, pair_send, pair_recv, *sems,
):
    here = Here()
    row, col, core = here.row, here.col, here.core
    count = len(SPREAD_SEMS)
    rows, width = hidden.shape
    depth = weights.shape[0]
    part = depth // 2

    def weight_block(of_row, unused_place, of_core):
        return all_weights.at[pl.ds(pl.multiple_of(of_row * depth + of_core * part, part), part)]

    def normed_block(unused_row, place, unused_core):
        return normed.at[pl.ds(pl.multiple_of(place * rows, rows), rows)]

    own_weight = weights.at[pl.ds(pl.multiple_of(core * part, part), part)]
    spread_w = Spread(here, own_weight, weight_block, part, sems[:count], line=False)
    spread_n = Spread(
        here, normed_block(row, col, core), normed_block, rows, sems[count:], plane=False
    )
    greet(here.plane_peers() + here.line_peers() + [here.other_core()])
    spread_w.step(0)
    keep = pltpu.make_async_copy(own_weight, weight_block(row, 0, core), kept_sem)
    keep.start()

    values_in = hidden[...].astype(F32)
    scale_one = lax.rsqrt(jnp.mean(values_in * values_in, axis=1, keepdims=True) + EPSILON)
    own_rows = pl.ds(pl.multiple_of(col * rows, rows), rows)
    normed[own_rows] = (values_in * scale_one * gain[...].astype(F32)).astype(BF16)
    spread_n.step(0)
    spread_w.step(1)
    spread_n.step(1)
    spread_w.step(2)
    spread_n.step(2)
    spread_n.step(3)
    keep.wait()
    for which in range(4):
        spread_w.core_arrived(which, 0)

    columns = 256

    @pl.loop(0, qkv.shape[1] // columns)
    def _(index):
        at = pl.ds(pl.multiple_of(index * columns, columns), columns)
        qkv[:, at] = matmul(normed[...], all_weights[:, at])

    plane = qkv.shape[1] // (3 * HD)
    for kind in range(2):
        square = jnp.zeros((qkv.shape[0], HD), F32)
        for head in range(plane):
            start = (head * 3 + kind) * HD
            raw = qkv[:, start : start + HD]
            square = square + raw * raw
        stat[col, kind : kind + 1] = jnp.sum(square.T, axis=0, keepdims=True)

    def give_stat(step):
        peer = here.line_peers()[step]
        return remote(stat.at[col], stat.at[col], stat_send.at[step], stat_recv.at[col], peer)

    for step in range(3):
        give_stat(step).start()
    for step in range(3):
        place = (col + step + 1) % 4
        arrived(stat.at[place], stat_recv.at[place])
    total = stat[0] + stat[1] + stat[2] + stat[3]
    totals[...] = total
    for kind, target in enumerate((scale_q, scale_k)):
        line = lax.rsqrt(total[kind : kind + 1] / width + EPSILON)
        target[...] = jnp.broadcast_to(line, (HD, line.shape[1])).T

    chunk = 64

    @pl.loop(0, qkv.shape[0] // chunk)
    def _(index):
        at = pl.ds(pl.multiple_of(index * chunk, chunk), chunk)
        for head in range(plane):
            for kind, (scales, gains) in enumerate(((scale_q, q_gain), (scale_k, k_gain))):
                raw = qkv[at, pl.ds((head * 3 + kind) * HD, HD)]
                unit = raw * scales[at] * gains[:, head * HD : (head + 1) * HD]
                turned = pltpu.roll(unit, HD // 2, 1)
                heads[head, kind, at] = (unit * cosine[at] + turned * sine[at]).astype(BF16)
            heads[head, 2, at] = qkv[at, pl.ds((head * 3 + 2) * HD, HD)].astype(BF16)

    targets = (query.at[row], keys.at[1, row], values.at[1, row])

    def give_head(step, kind):
        dest = here.rows[step + 1]
        sems = head_send.at[step, kind], head_recv.at[kind, row]
        return remote(heads.at[dest, kind], targets[kind], *sems, here.at_row(dest))

    for kind in (1, 2, 0):
        for step in range(3):
            give_head(step, kind).start()

    def give_pair(source, kind):
        array = (keys, values)[kind]
        sems = pair_send.at[kind, source], pair_recv.at[kind, source]
        return remote(array.at[1, source], array.at[0, source], *sems, here.other_core())

    def keep_pair(source, kind):
        array = (keys, values)[kind]
        return pltpu.make_async_copy(
            array.at[1, source], array.at[0, source], kept_kv_sem.at[kind, source]
        )

    def pair_from(source):
        @pl.when(core == 0)
        def _():
            for kind in range(2):
                give_pair(source, kind).start()
                keep_pair(source, kind).start()

    for kind, array in ((1, keys), (2, values)):
        array[1, row] = heads[row, kind]
    query[row] = heads[row, 0]
    pair_from(row)
    for source in here.rows[1:]:
        arrived(keys.at[1, source], head_recv.at[1, source])
        arrived(values.at[1, source], head_recv.at[2, source])
        pair_from(source)
    for source in here.rows[1:]:
        arrived(query.at[source], head_recv.at[0, source])

    @pl.when(core == 0)
    def _():
        for source in range(4):
            for kind in range(2):
                give_pair(source, kind).wait_send()
                keep_pair(source, kind).wait()

    @pl.when(core == 1)
    def _():
        for source in range(4):
            for kind in range(2):
                give_pair(source, kind).wait_recv()

    for step in range(3):
        give_stat(step).wait_send()
        for kind in range(3):
            give_head(step, kind).wait_send()
    spread_w.finish(arrivals=False)
    spread_n.finish()


def project(hidden, gain, weights, q_gain, k_gain, cosine, sine, collective_id):
    rows, width = hidden.shape
    depth, columns = weights.shape
    row_tok = 4 * rows
    plane = columns // (3 * HD)
    vmem = pl.BlockSpec(memory_space=pltpu.VMEM)
    hbm = pl.BlockSpec(memory_space=pl.ANY)
    return pl.pallas_call(
        project_kernel,
        in_specs=[vmem, vmem, hbm, vmem, vmem, vmem, vmem],
        out_specs=[vmem, vmem, vmem, vmem, vmem, vmem, vmem],
        out_shape=[
            jax.ShapeDtypeStruct((row_tok, width), BF16),
            jax.ShapeDtypeStruct((4 * depth, columns), BF16),
            jax.ShapeDtypeStruct((row_tok, columns), F32),
            jax.ShapeDtypeStruct((8, row_tok), F32),
            jax.ShapeDtypeStruct((4, row_tok, HD), BF16),
            jax.ShapeDtypeStruct((2, 4, row_tok, HD), BF16),
            jax.ShapeDtypeStruct((2, 4, row_tok, HD), BF16),
        ],
        scratch_shapes=[
            pltpu.VMEM((plane, 3, row_tok, HD), BF16),
            pltpu.VMEM((4, 8, row_tok), F32),
            pltpu.VMEM((row_tok, HD), F32),
            pltpu.VMEM((row_tok, HD), F32),
            pltpu.SemaphoreType.DMA,
            pltpu.SemaphoreType.DMA((2, 4)),
            pltpu.SemaphoreType.DMA((3,)),
            pltpu.SemaphoreType.DMA((4,)),
            pltpu.SemaphoreType.DMA((3, 3)),
            pltpu.SemaphoreType.DMA((3, 4)),
            pltpu.SemaphoreType.DMA((2, 4)),
            pltpu.SemaphoreType.DMA((2, 4)),
        ]
        + SPREAD_SEMS * 2,
        compiler_params=pltpu.CompilerParams(
            collective_id=collective_id, has_side_effects=True, vmem_limit_bytes=56 * 2**20
        ),
    )(hidden, gain[None], weights, q_gain, k_gain, cosine, sine)


def attention_kernel(
    scale, cuts, query, keys, values, out_weights, hidden, gain,
    mixed, total, all_out, mixed_rows, middle, normed,
    values_t, top, summed, acc, mixed_low, mixed_tok, kept_sem,
    row_send, row_recv, token_send, token_recv, *sems,
):
    here = Here()
    row, col, core = here.row, here.col, here.core
    rows = hidden.shape[0]
    row_tok = 4 * rows
    group_tok = 4 * row_tok
    side = out_weights.shape[0]

    def out_block(of_row, place, of_core):
        start = pl.multiple_of(place * side + of_core * (side // 2), side // 2)
        return all_out.at[pl.ds(start, side // 2), pl.ds(pl.multiple_of(of_row * side, side), side)]

    own_out = out_weights.at[pl.ds(pl.multiple_of(core * (side // 2), side // 2), side // 2)]
    spread = Spread(here, own_out, out_block, side // 2, sems)
    keep = pltpu.make_async_copy(own_out, out_block(row, col, core), kept_sem)
    keep.start()
    values_t[...] = values[...].T
    greet(here.plane_peers() + here.line_peers() + [here.other_core()])
    spread.step(0)
    cut = (cuts[0, 0], cuts[0, 1])
    last_query = 2 * group_tok - row_tok

    def queries(index):
        at = pl.ds(index * row_tok, row_tok)
        first_query = core * group_tok + index * row_tok
        top[...] = jnp.full_like(top, MASKED)
        summed[...] = jnp.zeros_like(summed)
        acc[...] = jnp.zeros_like(acc)

        def block_fn(part, scores):
            old = top[...]
            new = jnp.maximum(old, jnp.max(scores, axis=0, keepdims=True))
            weight = jnp.exp(scores - new)
            decay = jnp.exp(old - new)
            top[...] = new
            summed[...] = summed[...] * decay + jnp.sum(weight, axis=0, keepdims=True)
            acc[...] = acc[...] * decay + matmul(values_t[:, part], weight.astype(BF16))

        def scan(block, carry):
            first_key = block * row_tok
            part = pl.ds(pl.multiple_of(first_key, row_tok), row_tok)
            masked = (block == 0) | (first_key == first_query) | (first_query == last_query)

            @pl.when(jnp.logical_not(masked))
            def _():
                block_fn(part, contract_cols(keys[part], query[at]) * scale)

            @pl.when(masked)
            def _():
                key_place = first_key + lax.broadcasted_iota(jnp.int32, (row_tok, row_tok), 0)
                place = first_query + lax.broadcasted_iota(jnp.int32, (1, row_tok), 1)
                allowed = (key_place <= place) & (key_place >= doc_start(place, cut))
                scores = contract_cols(keys[part], query[at]) * scale
                block_fn(part, jnp.where(allowed, scores, MASKED))

            return carry

        lax.fori_loop(0, core * 4 + index + 1, scan, 0)
        got = (acc[...] / summed[...]).T
        mixed[at] = got
        mixed_low[index] = got.astype(BF16)
        total[:, at] = top[...] + jnp.log(summed[...])

        @pl.when(row != index)
        def _():
            give_row(index).start()

        @pl.when(row == index)
        def _():
            mixed_rows[row] = mixed_low[index]

    def give_row(index):
        sems_of = row_send.at[index], row_recv.at[row]
        return remote(mixed_low.at[index], mixed_rows.at[row], *sems_of, here.at_row(index))

    def give_token(step):
        place = (col + step) % 4
        part = pl.ds(pl.multiple_of(place * rows, rows), rows)
        sems_of = token_send.at[step], token_recv.at[col]
        return remote(mixed_rows.at[:, part], mixed_tok.at[col], *sems_of, here.at_col(place))

    for index in range(4):
        queries(index)
        spread.step(index + 1)
    for source in here.rows[1:]:
        arrived(mixed_rows.at[source], row_recv.at[source])
    for step in range(1, 4):
        give_token(step).start()
    mixed_tok[col] = mixed_rows[:, pl.ds(pl.multiple_of(col * rows, rows), rows)]
    spread.step(5)
    keep.wait()
    spread.finish()
    for step in range(1, 4):
        place = (col + 4 - step) % 4
        arrived(mixed_tok.at[place], token_recv.at[place])
    own = jnp.concatenate([mixed_tok[place, head] for place in range(4) for head in range(4)], axis=1)
    tile = 512

    @pl.loop(0, all_out.shape[1] // tile)
    def _(index):
        at = pl.ds(pl.multiple_of(index * tile, tile), tile)
        middle[:, at] = hidden[:, at].astype(F32) + matmul(own, all_out[:, at])

    values_in = middle[...]
    root = lax.rsqrt(jnp.mean(values_in * values_in, axis=1, keepdims=True) + EPSILON)
    normed[...] = (values_in * root * gain[...].astype(F32)).astype(BF16)
    for index in range(4):

        @pl.when(row != index)
        def _():
            give_row(index).wait_send()

    for step in range(1, 4):
        give_token(step).wait_send()


def attention_stage(query, keys, values, cuts, out_weights, hidden, gain, scale, collective_id):
    rows, width = hidden.shape
    row_tok, group_tok = 4 * rows, 16 * rows
    vmem, hbm = pl.BlockSpec(memory_space=pltpu.VMEM), pl.BlockSpec(memory_space=pl.ANY)
    dma = pltpu.SemaphoreType.DMA
    return pl.pallas_call(
        functools.partial(attention_kernel, scale),
        in_specs=[pl.BlockSpec(memory_space=pltpu.SMEM)] + [vmem] * 3 + [hbm] + [vmem] * 2,
        out_specs=[vmem] * 6,
        out_shape=[
            jax.ShapeDtypeStruct((group_tok, HD), F32),
            jax.ShapeDtypeStruct((1, group_tok), F32),
            jax.ShapeDtypeStruct((width, width), BF16),
            jax.ShapeDtypeStruct((4, row_tok, HD), BF16),
            jax.ShapeDtypeStruct((rows, width), F32),
            jax.ShapeDtypeStruct((rows, width), BF16),
        ],
        scratch_shapes=[
            pltpu.VMEM((HD, 2 * group_tok), BF16),
            pltpu.VMEM((1, row_tok), F32),
            pltpu.VMEM((1, row_tok), F32),
            pltpu.VMEM((HD, row_tok), F32),
            pltpu.VMEM((4, row_tok, HD), BF16),
            pltpu.VMEM((4, 4, rows, HD), BF16),
            dma, dma((4,)), dma((4,)), dma((4,)), dma((4,)),
        ]
        + SPREAD_SEMS,
        compiler_params=pltpu.CompilerParams(
            collective_id=collective_id, has_side_effects=True, vmem_limit_bytes=40 * 2**20
        ),
    )(cuts[None], query, keys, values, out_weights, hidden, gain[None])


class PairSum:
    def __init__(self, here, values, out, held, got, send, recv):
        self.here, self.values, self.out, self.held, self.got = here, values, out, held, got
        self.send, self.recv = send, recv
        col, half = here.col, values.shape[1] // 2
        self.own = pl.ds(pl.multiple_of(here.core * half, half), half)
        self.others = pl.ds(pl.multiple_of((1 - here.core) * half, half), half)
        self.peers = [
            here.at_row(here.across),
            here.at_row(here.along),
            here.at_col(col + 1 - 2 * (col % 2)),
            here.at_col((col + 2) % 4),
        ]

    def copy(self, step):
        here, sems = self.here, (self.send.at[step], self.recv.at[step])
        if step == 0:
            return remote(self.values.at[:, self.others], self.got.at[0], *sems, here.other_core())
        if step == 5:
            return remote(self.held.at[4], self.out.at[:, self.own], *sems, here.other_core())
        return remote(self.held.at[step - 1], self.got.at[step], *sems, self.peers[step - 1])

    def begin(self):
        self.copy(0).start()

    def step(self, index):
        if index == 5:
            arrived(self.out.at[:, self.others], self.recv.at[5])
            return
        self.copy(index).wait_recv()
        before = self.values[:, self.own] if index == 0 else self.held[index - 1]
        self.held[index] = before + self.got[index]
        if index == 4:
            self.out[:, self.own] = self.held[4]
        self.copy(index + 1).start()

    def finish(self):
        for index in range(6):
            self.copy(index).wait_send()


def pair_sum_buffers(rows, width):
    return [
        pltpu.VMEM((5, rows, width // 2), F32),
        pltpu.VMEM((5, rows, width // 2), F32),
        pltpu.SemaphoreType.DMA((6,)),
        pltpu.SemaphoreType.DMA((6,)),
    ]


def back_kernel(
    scale, cuts, d_attn, query, keys, values, mixed, total, out_weights, out_parts, early,
    d_attn_row, d_heads, out_total, early_sum,
    weights, d_mixed_give, d_mixed_row, d_mixed, keys_t, d_keys, d_values, acc, pair_out, pair_in,
    head_give, sum_held, sum_got, sum_send, sum_recv, weight_sem, load_sem,
    near_send, near_recv, head_send, head_recv, back_send, back_recv,
    pair_send, pair_recv, *rest,
):
    here = Here()
    row, col, core = here.row, here.col, here.core
    rows = d_attn.shape[0]
    row_tok = 4 * rows
    group_tok = 4 * row_tok
    plane = 4 * HD
    order = here.near_first[::-1]
    collect = Collect(here, rest[:6], rest[6 : 6 + len(COLLECT_SEMS)])
    sems = rest[6 + len(COLLECT_SEMS) :]

    def row_block(unused_row, place, unused_core):
        return d_attn_row.at[pl.ds(pl.multiple_of(place * rows, rows), rows)]

    spread = Spread(here, row_block(row, col, core), row_block, rows, sems, plane=False)
    pair_sum = PairSum(here, early, early_sum, sum_held, sum_got, sum_send, sum_recv)

    def load(which, place):
        return pltpu.make_async_copy(
            out_parts.at[which, place], collect.mine.at[which, place], load_sem.at[which, place]
        )

    load_weights = pltpu.make_async_copy(out_weights, weights, weight_sem)
    load_weights.start()
    for place in order:
        for which in (3, 2, 1, 0):
            load(which, place).start()
    keys_t[...] = keys[...].T
    d_attn_row[pl.ds(pl.multiple_of(col * rows, rows), rows)] = d_attn[...]
    greet(here.plane_peers() + here.line_peers() + [here.other_core()])

    def give_near(step):
        place = (col + step) % 4
        sems_of = near_send.at[step], near_recv.at[col]
        return remote(d_mixed_give.at[place], d_mixed_row.at[col], *sems_of, here.at_col(place))

    def give_head(step):
        dest = here.rows[step]
        part = pl.ds(pl.multiple_of(dest * HD, HD), HD)
        sems_of = head_send.at[step], head_recv.at[row]
        return remote(d_mixed_row.at[:, :, part], d_mixed.at[row], *sems_of, here.at_row(dest))

    def start(index):
        for which in (3, 2, 1):
            load(which, order[index]).wait()
        collect.start_far(order[index])
        collect.start_near(order[index])

    ends = (col == 0) | (col == 3)

    def from_ends(index):
        @pl.when(ends)
        def _():
            collect.line_step(order[index])

    def from_inside(index):
        @pl.when(jnp.logical_not(ends))
        def _():
            collect.line_step(order[index])

    def plane_part(index):
        load(0, order[index]).wait()
        collect.plane_step(order[index])

    start(0)
    pair_sum.begin()
    load_weights.wait()
    for step in (1, 2, 3, 0):
        place = (col + step) % 4
        part = pl.ds(pl.multiple_of(place * plane, plane), plane)
        product = contract_cols(d_attn[...], weights[part]).astype(BF16)
        if step == 0:
            d_mixed_row[col] = product
        else:
            d_mixed_give[place] = product
            give_near(step).start()
    spread.step(0)
    pair_sum.step(0)
    d_keys[...] = jnp.zeros_like(d_keys)
    d_values[...] = jnp.zeros_like(d_values)
    for step in range(1, 4):
        place = (col + 4 - step) % 4
        arrived(d_mixed_row.at[place], near_recv.at[place])
    for step in range(1, 4):
        give_head(step).start()
    d_mixed[row] = d_mixed_row[:, :, pl.ds(pl.multiple_of(row * HD, HD), HD)]
    collect.corner_step(order[0])
    start(1)
    pair_sum.step(1)
    spread.step(1)
    for source in here.rows[1:]:
        arrived(d_mixed.at[source], head_recv.at[source])

    cut = (cuts[0, 0], cuts[0, 1])
    last_query = 2 * group_tok - row_tok

    def queries(index):
        at = pl.ds(index * row_tok, row_tok)
        first_query = core * group_tok + index * row_tok
        gradient = d_mixed[index].reshape(row_tok, HD)
        delta = jnp.sum((gradient.astype(F32) * mixed[at]).T, axis=0, keepdims=True)
        sums = total[:, at]
        acc[...] = jnp.zeros_like(acc)

        def block_fn(part, scores):
            weight = jnp.exp(scores - sums)
            d_weight = contract_cols(values[part], gradient)
            d_scores = (weight * (d_weight - delta)).astype(BF16)
            d_values[part] += matmul(weight.astype(BF16), gradient)
            d_keys[part] += matmul(d_scores, query[at]) * scale
            acc[...] += matmul(keys_t[:, part], d_scores)

        def scan(block, carry):
            first_key = block * row_tok
            part = pl.ds(pl.multiple_of(first_key, row_tok), row_tok)
            masked = (block == 0) | (first_key == first_query) | (first_query == last_query)

            @pl.when(jnp.logical_not(masked))
            def _():
                block_fn(part, contract_cols(keys[part], query[at]) * scale)

            @pl.when(masked)
            def _():
                key_place = first_key + lax.broadcasted_iota(jnp.int32, (row_tok, row_tok), 0)
                place = first_query + lax.broadcasted_iota(jnp.int32, (1, row_tok), 1)
                allowed = (key_place <= place) & (key_place >= doc_start(place, cut))
                scores = contract_cols(keys[part], query[at]) * scale
                block_fn(part, jnp.where(allowed, scores, MASKED))

            return carry

        lax.fori_loop(0, core * 4 + index + 1, scan, 0)
        head_give[0, index] = (acc[...] * scale).T.astype(BF16)

    queries(0)
    plane_part(0)
    from_ends(0)
    collect.corner_step(order[1])
    start(2)
    spread.step(2)
    queries(1)
    from_inside(0)
    plane_part(1)
    from_ends(1)
    collect.corner_step(order[2])
    start(3)
    pair_sum.step(2)
    queries(2)
    from_inside(1)
    plane_part(2)
    from_ends(2)
    collect.corner_step(order[3])
    spread.step(3)
    queries(3)

    def give_back(step, kind):
        dest = here.rows[step]
        sems_of = back_send.at[step, kind], back_recv.at[kind, row]
        return remote(head_give.at[kind, dest], d_heads.at[row, kind], *sems_of, here.at_row(dest))

    def give_pair(kind):
        sems_of = pair_send.at[kind], pair_recv.at[kind]
        return remote(pair_out.at[kind], pair_in.at[kind], *sems_of, here.other_core())

    for step in range(1, 4):
        give_back(step, 0).start()
    d_heads[row, 0] = head_give[0, row]

    @pl.when(core == 1)
    def _():
        for kind, gradient in enumerate((d_keys, d_values)):
            pair_out[kind] = gradient[pl.ds(0, group_tok)].astype(BF16)
            give_pair(kind).start()
        for kind, gradient in enumerate((d_keys, d_values)):
            for part in range(4):
                at = pl.ds(group_tok + part * row_tok, row_tok)
                head_give[kind + 1, part] = gradient[at].astype(BF16)

    from_inside(2)
    plane_part(3)
    pair_sum.step(3)

    @pl.when(core == 0)
    def _():
        for kind, gradient in enumerate((d_keys, d_values)):
            give_pair(kind).wait_recv()
            for part in range(4):
                at = pl.ds(part * row_tok, row_tok)
                summed = gradient[at] + pair_in[kind, at].astype(F32)
                head_give[kind + 1, part] = summed.astype(BF16)

    for kind in (1, 2):
        for step in range(1, 4):
            give_back(step, kind).start()
        d_heads[row, kind] = head_give[kind, row]
    pair_sum.step(4)
    pair_sum.step(5)
    collect.own_step()
    out_total[...] = collect.mine[0, col]
    for source in here.rows[1:]:
        for kind in range(3):
            arrived(d_heads.at[source, kind], back_recv.at[kind, source])
    for step in range(1, 4):
        give_near(step).wait_send()
        give_head(step).wait_send()
        for kind in range(3):
            give_back(step, kind).wait_send()

    @pl.when(core == 1)
    def _():
        for kind in range(2):
            give_pair(kind).wait_send()

    pair_sum.finish()
    spread.finish()
    collect.finish()


def attend_back_stage(
    d_attn, query, keys, values, mixed, total, cuts, out_weights, out_parts, early, scale, collective_id
):
    rows, width = d_attn.shape
    row_tok, group_tok = 4 * rows, 16 * rows
    vmem, hbm = pl.BlockSpec(memory_space=pltpu.VMEM), pl.BlockSpec(memory_space=pl.ANY)
    dma = pltpu.SemaphoreType.DMA
    return pl.pallas_call(
        functools.partial(back_kernel, scale),
        in_specs=[pl.BlockSpec(memory_space=pltpu.SMEM)] + [vmem] * 6 + [hbm] * 2 + [vmem],
        out_specs=[vmem] * 4,
        out_shape=[
            jax.ShapeDtypeStruct((row_tok, width), BF16),
            jax.ShapeDtypeStruct((4, 3, row_tok, HD), BF16),
            jax.ShapeDtypeStruct((rows, width), BF16),
            jax.ShapeDtypeStruct(early.shape, F32),
        ],
        scratch_shapes=[
            pltpu.VMEM((width, width), BF16),
            pltpu.VMEM((4, rows, 4 * HD), BF16),
            pltpu.VMEM((4, rows, 4 * HD), BF16),
            pltpu.VMEM((4, 4, rows, HD), BF16),
            pltpu.VMEM((HD, 2 * group_tok), BF16),
            pltpu.VMEM((2 * group_tok, HD), F32),
            pltpu.VMEM((2 * group_tok, HD), F32),
            pltpu.VMEM((HD, row_tok), F32),
            pltpu.VMEM((2, group_tok, HD), BF16),
            pltpu.VMEM((2, group_tok, HD), BF16),
            pltpu.VMEM((3, 4, row_tok, HD), BF16),
        ]
        + pair_sum_buffers(*early.shape)
        + [
            dma, dma((4, 4)), dma((4,)), dma((4,)), dma((4,)), dma((4,)),
            dma((4, 3)), dma((3, 4)), dma((2,)), dma((2,)),
        ]
        + collect_buffers(rows, width)
        + COLLECT_SEMS
        + SPREAD_SEMS,
        compiler_params=pltpu.CompilerParams(
            collective_id=collective_id, has_side_effects=True, vmem_limit_bytes=58 * 2**20
        ),
    )(cuts[None], d_attn, query, keys, values, mixed, total, out_weights, out_parts, early)


def tail_kernel(
    d_heads, qkv, totals, q_gain, k_gain, cosine, sine, weights, normed, mixed_rows, d_attn,
    hidden, gain, d_middle,
    grad_hidden, grad_qkv, grad_out, late_sum,
    d_qkv, late, grads, mixed, units, stat, scales, sums, sum_held, sum_got, sum_send, sum_recv,
    stat_send, stat_recv,
    line, line_in, whole, give, other, plane, corner_one, corner_two, from_across, from_along,
    up_send, down_send, line_recv, other_send, other_recv,
    one_send, one_recv, two_send, two_recv, across_send, across_recv, along_send, along_recv,
    back_send, back_recv,
):
    here = Here()
    row, col, core = here.row, here.col, here.core
    rows = hidden.shape[0]
    depth, columns = grads.shape
    part = depth // 2
    first, second = pl.ds(0, part // 2), pl.ds(part // 2, part // 2)
    order = here.near_first[::-1]
    qkv_columns = d_qkv.shape[1]
    tile = 512

    def line_products():
        @pl.loop(0, weights.shape[0] // tile)
        def _(index):
            at = pl.ds(pl.multiple_of(index * tile, tile), tile)
            product = contract_cols(d_qkv[...], weights[at]).astype(BF16)
            line[:, :, at] = product.reshape(4, rows, tile)

    def give_up(place):
        sems = up_send.at[place], line_recv.at[place]
        return remote(line.at[place], line_in.at[place], *sems, here.at_col(col + 1))

    def give_down(place, slot):
        sems = down_send.at[place], line_recv.at[slot]
        return remote(line.at[place], line_in.at[slot], *sems, here.at_col(col - 1))

    def line_step(place):
        @pl.when((place > col) & (col > 0))
        def _():
            give_up(place).wait_recv()
            add_into(line.at[place], line_in.at[place])

        @pl.when((place < col) & (col < 3))
        def _():
            give_down(place, place).wait_recv()
            add_into(line.at[place], line_in.at[place])

        @pl.when(place > col)
        def _():
            give_up(place).start()

        @pl.when(place < col - 1)
        def _():
            give_down(place, place).start()

        @pl.when(place == col - 1)
        def _():
            give_down(place, 4).start()

    def row_product(which):
        of_row = here.rows[which]
        at = pl.ds(pl.multiple_of(of_row * depth, depth), depth)
        whole[:, pl.ds(0, qkv_columns)] = transposed_product(normed[:, at], d_qkv[...]).astype(BF16)
        whole[:, pl.ds(qkv_columns, columns - qkv_columns)] = transposed_product(
            mixed[...], d_attn[:, at]
        ).astype(BF16)
        plane[which] = whole[pl.ds(pl.multiple_of(core * part, part), part)]
        give[which] = whole[pl.ds(pl.multiple_of((1 - core) * part, part), part)]
        to_core(which).start()

    def to_core(which):
        sems = other_send.at[which], other_recv.at[which]
        return remote(give.at[which], other.at[which], *sems, here.other_core())

    def own_sum(which):
        to_core(which).wait_recv()
        add_into(plane.at[which], other.at[which])

    give_one = remote(
        plane.at[3, first], corner_one, one_send, one_recv, here.at_row(here.across)
    )
    give_two = remote(
        plane.at[3, second], corner_two, two_send, two_recv, here.at_row(here.along)
    )

    def give_across(index):
        at = (first, second)[index]
        sems = across_send.at[index], across_recv.at[index]
        return remote(plane.at[1, at], from_across.at[at], *sems, here.at_row(here.across))

    def give_along(index):
        at = (first, second)[index]
        sems = along_send.at[index], along_recv.at[index]
        return remote(plane.at[2, at], from_along.at[at], *sems, here.at_row(here.along))

    pair_sum = PairSum(here, late, late_sum, sum_held, sum_got, sum_send, sum_recv)
    greet(here.plane_peers() + here.line_peers() + [here.other_core()])

    width = hidden.shape[1]
    heads = d_heads.shape[0]
    row_tok = d_qkv.shape[0]
    late[...] = jnp.zeros_like(late)
    for kind in range(2):
        root = lax.rsqrt(totals[kind : kind + 1] / width + EPSILON)
        scales[kind] = jnp.broadcast_to(root, (HD, row_tok)).T
        square = jnp.zeros((row_tok, HD), F32)
        for head in range(heads):
            start = (head * 3 + kind) * HD
            raw = qkv[:, start : start + HD]
            given = d_heads[head, kind].astype(F32)
            unit = given * cosine[...] + pltpu.roll(given * sine[...], HD // 2, 1)
            gains = (q_gain, k_gain)[kind][:, head * HD : (head + 1) * HD]
            gain_sum = jnp.sum(unit * raw * scales[kind], axis=0, keepdims=True)
            place = pl.ds(pl.multiple_of((col * heads + head) * HD, HD), HD)
            late[kind + 1 : kind + 2, place] = gain_sum
            weighted = unit * gains
            square = square + weighted * raw
            units[kind, head] = weighted
        stat[col, kind : kind + 1] = jnp.sum(square.T, axis=0, keepdims=True)

    def give_stat(step):
        peer = here.line_peers()[step]
        return remote(stat.at[col], stat.at[col], stat_send.at[step], stat_recv.at[col], peer)

    for step in range(3):
        give_stat(step).start()
    for head in range(heads):
        d_qkv[:, (head * 3 + 2) * HD : (head * 3 + 3) * HD] = d_heads[head, 2]
        mixed[:, head * HD : (head + 1) * HD] = mixed_rows[head]
    for step in range(3):
        place = (col + step + 1) % 4
        arrived(stat.at[place], stat_recv.at[place])
    total = stat[0] + stat[1] + stat[2] + stat[3]
    for kind in range(2):
        sums[...] = jnp.broadcast_to(total[kind : kind + 1] / width, (HD, row_tok)).T
        for head in range(heads):
            start = (head * 3 + kind) * HD
            raw = qkv[:, start : start + HD]
            root = scales[kind]
            d_raw = root * units[kind, head] - raw * (root * root * root) * sums[...]
            d_qkv[:, start : start + HD] = d_raw.astype(BF16)
    ends = (col == 0) | (col == 3)
    line_products()

    @pl.when(ends)
    def _():
        for place in order[:3]:
            line_step(place)

    def inner_step(place):
        @pl.when(jnp.logical_not(ends))
        def _():
            line_step(place)

    row_product(3)
    row_product(1)
    inner_step(order[0])
    own_sum(3)
    give_one.start()
    give_two.start()
    row_product(2)
    own_sum(1)
    give_across(0).start()
    own_sum(2)
    give_along(1).start()
    inner_step(order[1])
    row_product(0)
    inner_step(order[2])
    give_two.wait_recv()
    add_into(plane.at[1, second], corner_two)
    give_across(1).start()
    give_one.wait_recv()
    add_into(plane.at[2, first], corner_one)
    give_along(0).start()
    own_sum(0)

    @pl.when(col > 0)
    def _():
        give_up(col).wait_recv()
        add_into(line.at[col], line_in.at[col])

    @pl.when(col < 3)
    def _():
        give_down(col, 4).wait_recv()
        add_into(line.at[col], line_in.at[4])

    given = line[col].astype(F32)
    tokens = hidden[...].astype(F32)
    root = lax.rsqrt(jnp.mean(tokens * tokens, axis=1, keepdims=True) + EPSILON)
    late[0:1] = jnp.sum(given * tokens * root, axis=0, keepdims=True)
    pair_sum.begin()
    weighted = given * gain[...].astype(F32)
    inner = jnp.mean(weighted * tokens, axis=1, keepdims=True)
    grad_hidden[...] = d_middle[...] + root * weighted - tokens * (root * root * root) * inner
    pair_sum.step(0)
    for index in range(2):
        give_across(index).wait_recv()
        give_along(index).wait_recv()
    add_into(plane.at[0], from_across, from_along)
    pair_sum.step(1)
    own_half = pl.ds(pl.multiple_of(core * part, part), part)
    give_back = remote(
        plane.at[0], grads.at[own_half], back_send, back_recv, here.other_core()
    )
    give_back.start()
    grads[own_half] = plane[0]
    other_half = grads.at[pl.ds(pl.multiple_of((1 - core) * part, part), part)]
    pair_sum.step(2)
    arrived(other_half, back_recv)
    grad_qkv[...] = grads[:, pl.ds(0, qkv_columns)].astype(F32)
    grad_out[...] = grads[:, pl.ds(qkv_columns, columns - qkv_columns)].astype(F32)
    for index in (3, 4, 5):
        pair_sum.step(index)
    pair_sum.finish()
    for step in range(3):
        give_stat(step).wait_send()
    give_back.wait_send()
    give_one.wait_send()
    give_two.wait_send()
    for index in range(2):
        give_across(index).wait_send()
        give_along(index).wait_send()
    for which in range(4):
        to_core(which).wait_send()
    for place in order:

        @pl.when(place > col)
        def _():
            give_up(place).wait_send()

        @pl.when(place < col)
        def _():
            give_down(place, place).wait_send()


def tail_stage(
    d_heads, qkv, totals, q_gain, k_gain, cosine, sine, weights, normed, mixed_rows, d_attn,
    hidden, gain, d_middle, collective_id,
):
    row_tok, qkv_columns = qkv.shape
    rows, width = hidden.shape
    depth = width // 4
    out_columns = width // 4
    columns = qkv_columns + out_columns
    part = depth // 2
    heads = d_heads.shape[0]
    vmem = pl.BlockSpec(memory_space=pltpu.VMEM)
    one, four = pltpu.SemaphoreType.DMA, pltpu.SemaphoreType.DMA((4,))
    two, five = pltpu.SemaphoreType.DMA((2,)), pltpu.SemaphoreType.DMA((5,))
    three = pltpu.SemaphoreType.DMA((3,))
    return pl.pallas_call(
        tail_kernel,
        in_specs=[vmem] * 14,
        out_specs=[vmem] * 4,
        out_shape=[
            jax.ShapeDtypeStruct((rows, width), F32),
            jax.ShapeDtypeStruct((depth, qkv_columns), F32),
            jax.ShapeDtypeStruct((depth, out_columns), F32),
            jax.ShapeDtypeStruct((8, width), F32),
        ],
        scratch_shapes=[
            pltpu.VMEM((row_tok, qkv_columns), BF16),
            pltpu.VMEM((8, width), F32),
            pltpu.VMEM((depth, columns), BF16),
            pltpu.VMEM((row_tok, heads * HD), BF16),
            pltpu.VMEM((2, heads, row_tok, HD), F32),
            pltpu.VMEM((4, 8, row_tok), F32),
            pltpu.VMEM((2, row_tok, HD), F32),
            pltpu.VMEM((row_tok, HD), F32),
        ]
        + pair_sum_buffers(8, width)
        + [
            three, four,
            pltpu.VMEM((4, rows, width), BF16),
            pltpu.VMEM((5, rows, width), BF16),
            pltpu.VMEM((depth, columns), BF16),
            pltpu.VMEM((4, part, columns), BF16),
            pltpu.VMEM((4, part, columns), BF16),
            pltpu.VMEM((4, part, columns), BF16),
            pltpu.VMEM((part // 2, columns), BF16),
            pltpu.VMEM((part // 2, columns), BF16),
            pltpu.VMEM((part, columns), BF16),
            pltpu.VMEM((part, columns), BF16),
            four, four, five, four, four,
            one, one, one, one, two, two, two, two,
            one, one,
        ],
        compiler_params=pltpu.CompilerParams(
            collective_id=collective_id, has_side_effects=True, vmem_limit_bytes=58 * 2**20
        ),
    )(
        d_heads, qkv, totals, q_gain, k_gain, cosine, sine, weights, normed, mixed_rows, d_attn,
        hidden, gain[None], d_middle,
    )


def expert_rows(rows, grads, gate, gate_w, up_w, down_w):
    pre_gate = matmul(rows, gate_w)
    pre_up = matmul(rows, up_w)
    back = contract_cols(grads, down_w)
    sigmoid_gate = jax.nn.sigmoid(pre_gate)
    silu_gate = pre_gate * sigmoid_gate
    hidden = (silu_gate * pre_up).astype(BF16)
    inner = jnp.sum(hidden.astype(F32) * back, axis=-1)
    weighted = (hidden.astype(F32) * gate).astype(BF16)
    d_hid = back * gate
    d_pregate = (d_hid * pre_up * (sigmoid_gate + silu_gate * (1.0 - sigmoid_gate))).astype(BF16)
    d_preup = (d_hid * silu_gate).astype(BF16)
    outputs = matmul(weighted, down_w).astype(BF16)
    d_rows = (contract_cols(d_pregate, gate_w) + contract_cols(d_preup, up_w)).astype(BF16)
    return (
        outputs,
        d_rows,
        inner,
        contract_rows(rows, d_pregate),
        contract_rows(rows, d_preup),
        contract_rows(weighted, grads),
    )


def experts(normed, grads, dense_gates, gate_w, up_w, down_w):
    rows_dev, width = normed.shape
    devices = math.prod(lax.axis_size(axis) for axis in ALL)
    expert_count = dense_gates.shape[1]
    expert = lax.axis_index(ALL) // 2
    parts = max(1, lax.axis_size("exp") // 2)
    step = rows_dev // parts

    def one_part(sums, piece):
        rows, grad_rows, gates = piece
        rows_all = lax.all_gather(rows, ALL, axis=0, tiled=True)
        grads_all = lax.all_gather(grad_rows, ALL, axis=0, tiled=True)
        gates_all = lax.all_gather(gates, ALL, axis=0, tiled=True)
        gate = lax.dynamic_slice_in_dim(gates_all, expert, 1, 1)
        got = expert_rows(rows_all, grads_all, gate, gate_w, up_w, down_w)
        outputs = lax.psum_scatter(got[0], ALL, scatter_dimension=0, tiled=True)
        d_rows = lax.psum_scatter(got[1], ALL, scatter_dimension=0, tiled=True)
        inner = lax.all_to_all(
            got[2].reshape(devices, step), ALL, split_axis=0, concat_axis=0, tiled=True
        )
        inner = inner.reshape(expert_count, 2, step).sum(axis=1).T
        sums = got[3:] if sums is None else tuple(a + b for a, b in zip(sums, got[3:]))
        return sums, (outputs, d_rows, inner)

    if parts == 1:
        sums, (outputs, d_rows, inner) = one_part(None, (normed, grads, dense_gates))
    else:
        start = tuple(jnp.zeros(w.shape, F32) for w in (gate_w, up_w, down_w))
        pieces = tuple(v.reshape(parts, step, -1) for v in (normed, grads, dense_gates))
        sums, got = lax.scan(one_part, start, pieces)
        outputs, d_rows, inner = (v.reshape(rows_dev, -1) for v in got)
    return outputs.astype(F32), d_rows.astype(F32), inner, sums


def experts_here(normed, grads_all, picks, router, halves, others):
    numbers = jnp.arange(router.shape[1], dtype=jnp.int32)
    mask = jnp.any(picks.T[None] == numbers[:, None, None], axis=1).astype(F32)
    out_parts, d_rows, inner, weights = expert_stage(
        normed, grads_all, mask, halves, others, router, 1
    )
    inner = inner[:, :, 0].reshape(router.shape[1], -1).T
    return out_parts, d_rows.astype(F32), inner, weights


def shards(
    hidden_in,
    out_grad,
    attn_gain,
    w_qkv,
    q_gain,
    k_gain,
    w_out,
    moe_gain,
    router,
    w_gate,
    w_up,
    w_down,
    routes,
    doc_cuts,
):
    row_count, col_count = lax.axis_size("row"), lax.axis_size("col")
    tokens = hidden_in[0].astype(F32)
    rows_dev, width = tokens.shape
    heads = w_qkv.shape[1] // (3 * HD)
    plane = heads * HD
    scale = HD ** (-0.5)
    side = lax.axis_index("exp") % 2
    row_tok = rows_dev * col_count
    group_tok = row_tok * row_count
    cuts = lax.dynamic_index_in_dim(doc_cuts, lax.axis_index("exp") // 2, 0, keepdims=False)

    here = (row_count, col_count, lax.axis_size("exp")) == (4, 4, 2)

    if here:
        grads_all = lax.all_gather(out_grad[0], ("row", "col"), axis=0, tiled=True)
        other_w = [lax.ppermute(w[0], "exp", [(0, 1), (1, 0)]) for w in (w_gate, w_up, w_down)]

    gain_one = attn_gain.astype(F32)
    scale_one = rms_scale(tokens)
    head_start = lax.axis_index("col") * plane
    gain_q = lax.dynamic_slice_in_dim(q_gain, head_start, plane, 0).astype(F32)
    gain_k = lax.dynamic_slice_in_dim(k_gain, head_start, plane, 0).astype(F32)
    row_places = side * group_tok + lax.axis_index("row") * row_tok + jnp.arange(row_tok, dtype=jnp.int32)
    unused_doc, position = doc_positions(row_places, cuts)
    cosine, sine = rope_tables(position, HD)
    if here:
        signed = jnp.concatenate([-sine[:, : HD // 2], sine[:, HD // 2 :]], axis=1)
        normed_row, qkv_w, qkv, totals, query, keys, values = project(
            hidden_in[0], attn_gain, w_qkv, gain_q[None], gain_k[None], cosine, signed, 0
        )
        total_q, total_k = totals[0], totals[1]
        query = query.reshape(group_tok, HD)
        key_all, value_all = keys.reshape(-1, HD), values.reshape(-1, HD)
    else:
        normed_one = (tokens * scale_one * gain_one).astype(BF16)
        normed_row = lax.all_gather(normed_one, "col", axis=0, tiled=True)
        qkv_w = lax.all_gather(w_qkv, "row", axis=0, tiled=True)
        out_w = lax.all_gather(
            lax.all_gather(w_out, "row", axis=1, tiled=True), "col", axis=0, tiled=True
        )
        qkv = matmul(normed_row, qkv_w)
    qkv = qkv.reshape(row_tok, heads, 3, HD)
    query_raw, key_raw, value_raw = qkv[:, :, 0], qkv[:, :, 1], qkv[:, :, 2]
    if not here:
        total_q, total_k = lax.psum(
            (jnp.sum(query_raw * query_raw, axis=(1, 2)), jnp.sum(key_raw * key_raw, axis=(1, 2))),
            "col",
        )
    scale_q = lax.rsqrt(total_q / width + EPSILON)[:, None, None]
    scale_k = lax.rsqrt(total_k / width + EPSILON)[:, None, None]
    gain_q, gain_k = gain_q.reshape(heads, HD), gain_k.reshape(heads, HD)
    cosine, sine = cosine[:, None, :], sine[:, None, :]
    if not here:
        query = rotate(query_raw * scale_q * gain_q, cosine, sine).astype(BF16)
        key = rotate(key_raw * scale_k * gain_k, cosine, sine).astype(BF16)
        moved = rows_to_heads(jnp.concatenate([query, key, value_raw.astype(BF16)], axis=-1))
        query, own_pair = moved[:, :HD], moved[:, HD:]
        earlier_pair = from_behind(own_pair, "exp", 1)
        lower_pair = jnp.where(side == 0, own_pair, earlier_pair)
        upper_pair = jnp.where(side == 0, jnp.zeros_like(own_pair), own_pair)
        key_value = jnp.concatenate([lower_pair, upper_pair], axis=0)
        key_all, value_all = key_value[:, :HD], key_value[:, HD:]

    if here:
        mixed_wide, total, out_w, mixed_rows, middle, normed_two = attention_stage(
            query, key_all, value_all, cuts, w_out, hidden_in[0], moe_gain, scale, 4
        )
    else:
        mixed_wide, total = attend(query, key_all, value_all, cuts, scale)
        mixed = mixed_wide.astype(BF16)
        middle = tokens + matmul(heads_to_tokens(mixed), out_w)

    gain_two = moe_gain.astype(F32)
    scale_two = rms_scale(middle)
    if not here:
        normed_two = (middle * scale_two * gain_two).astype(BF16)
    gates_all = jax.nn.softmax(matmul(normed_two, router), axis=-1)
    picks = routes[0]
    chosen = jnp.any(
        picks[:, :, None] == jnp.arange(router.shape[1], dtype=jnp.int32)[None, None, :], axis=1
    )
    grad_out = out_grad[0].astype(F32)
    expert_w = (w_gate[0], w_up[0], w_down[0])
    if here:
        out_parts, d_normed_two, inner, weight_grads = experts_here(
            normed_two, grads_all, picks, router, expert_w, other_w
        )
    else:
        dense_gates = jnp.where(chosen, gates_all, 0.0)
        mixture, d_normed_two, inner, weight_grads = experts(
            normed_two, out_grad[0], dense_gates, *expert_w
        )
    dense = jnp.where(chosen, inner, 0.0)
    d_logits = (gates_all * (dense - jnp.sum(gates_all * dense, axis=-1, keepdims=True))).astype(BF16)
    grad_router = contract_rows(d_logits, normed_two)
    d_normed_two = d_normed_two + contract_cols(d_logits, router)
    grad_moe_gain = jnp.sum(d_normed_two * middle * scale_two, axis=0)
    weighted_two = d_normed_two * gain_two
    d_middle = (
        grad_out
        + scale_two * weighted_two
        - middle * scale_two**3 * jnp.mean(weighted_two * middle, axis=-1, keepdims=True)
    )

    d_attn = d_middle.astype(BF16)
    if here:
        early = jnp.concatenate([grad_moe_gain[None], jnp.zeros((7, width), F32), grad_router])
        d_attn_row, d_heads, mixture, early = attend_back_stage(
            d_attn, query, key_all, value_all, mixed_wide, total, cuts, out_w, out_parts, early, scale, 2
        )
        grad_hidden, grad_qkv, grad_w_out, late = tail_stage(
            d_heads, qkv.reshape(row_tok, -1), totals, gain_q.reshape(1, -1), gain_k.reshape(1, -1),
            cosine[:, 0], signed, qkv_w, normed_row, mixed_rows, d_attn_row,
            hidden_in[0], attn_gain, d_middle, 3,
        )
        final = middle + mixture.astype(F32)
        summed = (late[0], late[1], late[2], early[0], early[8:])
    else:
        final = middle + mixture
        mixed_row = heads_to_rows(mixed).reshape(row_tok, plane)
        d_mixed = tokens_to_heads(contract_cols(d_attn, out_w).astype(BF16))
        d_attn_row = lax.all_gather(d_attn, "col", axis=0, tiled=True)
        d_query, acc_key, acc_value = attend_back(
            query, key_all, value_all, d_mixed, mixed_wide, total, cuts, scale
        )
        accumulated = jnp.concatenate([acc_key, acc_value], axis=1)
        lower_acc, upper_acc = accumulated[:group_tok], accumulated[group_tok:]
        kept_acc = jnp.where(side == 0, lower_acc, upper_acc)
        later_acc = from_behind(lower_acc.astype(BF16), "exp", -1).astype(F32)
        summed_pair = kept_acc + jnp.where(side == 0, later_acc, jnp.zeros_like(later_acc))
        d_heads = heads_to_rows(jnp.concatenate([d_query, summed_pair], axis=1).astype(BF16)).astype(F32)
        d_q_unit = rotate_back(d_heads[:, :, :HD], cosine, sine)
        d_k_unit = rotate_back(d_heads[:, :, HD : 2 * HD], cosine, sine)
        d_value = d_heads[:, :, 2 * HD :]
        weighted_q = d_q_unit * gain_q
        weighted_k = d_k_unit * gain_k
        sum_q, sum_k = lax.psum(
            (jnp.sum(weighted_q * query_raw, axis=(1, 2)), jnp.sum(weighted_k * key_raw, axis=(1, 2))),
            "col",
        )
        d_query_raw = scale_q * weighted_q - query_raw * scale_q**3 * (sum_q / width)[:, None, None]
        d_key_raw = scale_k * weighted_k - key_raw * scale_k**3 * (sum_k / width)[:, None, None]
        grad_q_part = jnp.sum(d_q_unit * query_raw * scale_q, axis=0).reshape(plane)
        grad_k_part = jnp.sum(d_k_unit * key_raw * scale_k, axis=0).reshape(plane)
        d_qkv = jnp.concatenate([d_query_raw, d_key_raw, d_value], axis=2).astype(BF16)
        d_qkv = d_qkv.reshape(row_tok, heads * 3 * HD)
        d_normed_one = lax.psum_scatter(
            contract_cols(d_qkv, qkv_w).astype(BF16), "col", scatter_dimension=0, tiled=True
        ).astype(F32)
        grad_qkv = lax.psum_scatter(
            contract_rows(normed_row, d_qkv).astype(BF16), "row", scatter_dimension=0, tiled=True
        )
        grad_w_out = lax.psum_scatter(
            contract_rows(mixed_row, d_attn_row).astype(BF16), "row", scatter_dimension=1, tiled=True
        )
        grad_qkv = lax.psum(grad_qkv, "exp").astype(F32)
        grad_w_out = lax.psum(grad_w_out, "exp").astype(F32)
        grad_attn_gain = jnp.sum(d_normed_one * tokens * scale_one, axis=0)
        weighted_one = d_normed_one * gain_one
        grad_hidden = (
            d_middle
            + scale_one * weighted_one
            - tokens * scale_one**3 * jnp.mean(weighted_one * tokens, axis=-1, keepdims=True)
        )
        empty = jnp.zeros((width,), F32)
        grad_q_full = lax.dynamic_update_slice_in_dim(empty, grad_q_part, head_start, 0)
        grad_k_full = lax.dynamic_update_slice_in_dim(empty, grad_k_part, head_start, 0)
        parts = (grad_attn_gain, grad_q_full, grad_k_full, grad_moe_gain)
        summed = lax.psum(parts + (grad_router,), ALL)
    return (
        final.astype(BF16)[None],
        grad_hidden[None],
        summed[0],
        grad_qkv,
        summed[1],
        summed[2],
        grad_w_out,
        summed[3],
        summed[4].T,
        weight_grads[0][None],
        weight_grads[1][None],
        weight_grads[2][None],
    )


def solution(mesh):
    token_spec = P("exp", ("row", "col"), None)
    expert_spec = P(("row", "col", "exp"), None, None)
    in_specs = (
        token_spec,
        token_spec,
        P(),
        P("row", "col"),
        P(),
        P(),
        P("col", "row"),
        P(),
        P(),
        expert_spec,
        expert_spec,
        expert_spec,
        token_spec,
        P(),
    )
    out_specs = (
        token_spec,
        token_spec,
        P(),
        P("row", "col"),
        P(),
        P(),
        P("col", "row"),
        P(),
        P(),
        expert_spec,
        expert_spec,
        expert_spec,
    )
    return jax.shard_map(shards, mesh=mesh, in_specs=in_specs, out_specs=out_specs, check_vma=False)
```

```python
import functools
import math

import jax
import jax.numpy as jnp
from jax import lax
from jax.experimental import pallas as pl
from jax.experimental.pallas import tpu as pltpu
from jax.sharding import PartitionSpec as P

HD = 128
EPSILON = 1e-05
ROPE_BASE = 10000.0
MASKED = -1e30
BF16 = jnp.bfloat16
F32 = jnp.float32


def matmul(left, right):
    return jnp.dot(left, right, preferred_element_type=F32)


def contract_rows(left, right):
    return lax.dot_general(left, right, (((0,), (0,)), ((), ())), preferred_element_type=F32)


def contract_cols(left, right):
    return lax.dot_general(left, right, (((1,), (1,)), ((), ())), preferred_element_type=F32)


def rms_scale(values):
    return lax.rsqrt(jnp.mean(values * values, axis=-1, keepdims=True) + EPSILON)


def rope_tables(position, width):
    frequency = ROPE_BASE ** (-jnp.arange(0, width, 2, dtype=F32) / width)
    angle = position.astype(F32)[:, None] * frequency[None, :]
    return (
        jnp.concatenate([jnp.cos(angle)] * 2, axis=-1),
        jnp.concatenate([jnp.sin(angle)] * 2, axis=-1),
    )


def rotate(values, cosine, sine):
    half = values.shape[-1] // 2
    turned = jnp.concatenate([-values[..., half:], values[..., :half]], axis=-1)
    return values * cosine + turned * sine


def rotate_back(values, cosine, sine):
    half = values.shape[-1] // 2
    turned = values * sine
    return values * cosine + jnp.concatenate([turned[..., half:], -turned[..., :half]], axis=-1)


def doc_positions(places, cuts):
    first = (places >= cuts[0]).astype(jnp.int32)
    second = (places >= cuts[1]).astype(jnp.int32)
    start = first * cuts[0] + second * (cuts[1] - cuts[0])
    return (first + second, places - start)


def from_behind(value, axis, steps):
    count = lax.axis_size(axis)
    initial, last = (max(0, -steps), min(count, count - steps))
    return lax.ppermute(value, axis, [(source, source + steps) for source in range(initial, last)])


def rows_to_heads(values):
    count = lax.axis_size("row")
    rows, heads, width = values.shape
    moved = lax.all_to_all(values.transpose(1, 0, 2), "row", split_axis=0, concat_axis=0, tiled=True)
    return moved.reshape(count * rows, width)


def heads_to_rows(values):
    count = lax.axis_size("row")
    rows, width = values.shape
    moved = lax.all_to_all(
        values.reshape(count, rows // count, width), "row", split_axis=0, concat_axis=0, tiled=True
    )
    return moved.transpose(1, 0, 2)


def heads_to_tokens(values):
    row_count, col_count = lax.axis_size("row"), lax.axis_size("col")
    rows = values.shape[0] // (row_count * col_count)
    moved = lax.all_to_all(
        values.reshape(row_count * col_count, rows, HD),
        ("row", "col"),
        split_axis=0,
        concat_axis=0,
        tiled=True,
    )
    moved = moved.reshape(row_count, col_count, rows, HD).transpose(2, 1, 0, 3)
    return moved.reshape(rows, row_count * col_count * HD)


def tokens_to_heads(values):
    row_count, col_count = lax.axis_size("row"), lax.axis_size("col")
    rows = values.shape[0]
    parted = values.reshape(rows, col_count, row_count, HD).transpose(2, 1, 0, 3)
    moved = lax.all_to_all(
        parted.reshape(row_count * col_count, rows, HD),
        ("row", "col"),
        split_axis=0,
        concat_axis=0,
        tiled=True,
    )
    return moved.reshape(row_count * col_count * rows, HD)


MESH = pl.DeviceIdType.MESH
ALL = ("row", "col", "exp")


class Here:
    def __init__(self):
        self.row, self.col, self.core = (lax.axis_index(axis) for axis in ALL)
        self.across = self.row + 1 - 2 * (self.row % 2)
        self.along = (self.row + 2) % 4
        self.opposite = 3 - self.row
        self.rows = (self.row, self.across, self.along, self.opposite)
        half = self.col // 2
        self.near_first = [
            self.col,
            1 + self.col % 2,
            2 - self.col - self.col % 2 + 3 * half,
            3 - 3 * half,
        ]

    def at_row(self, row):
        return (row, self.col, self.core)

    def at_col(self, col):
        return (self.row, col, self.core)

    def other_core(self):
        return (self.row, self.col, 1 - self.core)

    def line_peers(self):
        return [self.at_col((self.col + step) % 4) for step in (1, 2, 3)]

    def group_peers(self):
        steps = range(1, 16)
        return [((self.row + s // 4) % 4, (self.col + s) % 4, self.core) for s in steps]

    def plane_peers(self):
        return [self.at_row(row) for row in self.rows[1:]]


def greet(peers):
    barrier = pltpu.get_barrier_semaphore()
    for peer in peers:
        pl.semaphore_signal(barrier, inc=1, device_id=peer, device_id_type=MESH)
    pl.semaphore_wait(barrier, len(peers))


def greet_near(here):
    barrier = pltpu.get_barrier_semaphore()
    col = here.col

    def signal(peer):
        pl.semaphore_signal(barrier, inc=1, device_id=peer, device_id_type=MESH)

    for peer in (here.other_core(), here.at_row(here.across), here.at_row(here.along)):
        signal(peer)

    @pl.when(col > 0)
    def _():
        signal(here.at_col(col - 1))

    @pl.when(col < 3)
    def _():
        signal(here.at_col(col + 1))

    pl.semaphore_wait(barrier, 3 + (col + 3) // 4 + (6 - col) // 4)


def remote(source, target, send, recv, device):
    return pltpu.make_async_remote_copy(
        src_ref=source,
        dst_ref=target,
        send_sem=send,
        recv_sem=recv,
        device_id=device,
        device_id_type=MESH,
    )


def arrived(target, recv):
    pltpu.make_async_copy(target, target, recv).wait()


def add_into(target, *terms):
    step = 16

    @pl.loop(0, target.shape[0] // step)
    def _(index):
        part = pl.ds(pl.multiple_of(index * step, step), step)
        value = target[part].astype(F32)
        for term in terms:
            value = value + term[part].astype(F32)
        target[part] = value.astype(target.dtype)


SPREAD_SEMS = [pltpu.SemaphoreType.DMA((4,))] * 11 + [pltpu.SemaphoreType.DMA((4, 4))] * 2


class Spread:
    def __init__(self, here, own, block, rows, sems, line=True, plane=True, core=True):
        self.here, self.own, self.block = here, own, block
        self.line, self.plane, self.core = line, plane, core
        (
            self.up_send, self.down_send, self.line_recv,
            self.across_send, self.across_recv, self.along_send, self.along_recv,
            self.one_send, self.one_recv, self.two_send, self.two_recv,
            self.core_send, self.core_recv,
        ) = sems
        self.first, self.second = pl.ds(0, rows // 2), pl.ds(rows // 2, rows // 2)
        self.order = here.near_first if line else [0]
        self.steps = len(self.order)

    def held(self, step):
        here = self.here
        return self.own if step == 0 else self.block(here.row, self.order[step], here.core)

    def up(self, step):
        here, place = self.here, self.order[step]
        target = self.block(here.row, place, here.core)
        recv = self.line_recv.at[place]
        return remote(self.held(step), target, self.up_send.at[place], recv, here.at_col(here.col + 1))

    def down(self, step):
        here, place = self.here, self.order[step]
        target = self.block(here.row, place, here.core)
        recv = self.line_recv.at[place]
        return remote(self.held(step), target, self.down_send.at[place], recv, here.at_col(here.col - 1))

    def to_across(self, step):
        here, place = self.here, self.order[step]
        target = self.block(here.row, place, here.core)
        sems = self.across_send.at[place], self.across_recv.at[place]
        return remote(self.held(step), target, *sems, here.at_row(here.across))

    def to_along(self, step):
        here, place = self.here, self.order[step]
        target = self.block(here.row, place, here.core)
        sems = self.along_send.at[place], self.along_recv.at[place]
        return remote(self.held(step), target, *sems, here.at_row(here.along))

    def corner_one(self, step):
        here, place = self.here, self.order[step]
        part = self.block(here.across, place, here.core).at[self.first]
        sems = self.one_send.at[place], self.one_recv.at[place]
        return remote(part, part, *sems, here.at_row(here.along))

    def corner_two(self, step):
        here, place = self.here, self.order[step]
        part = self.block(here.along, place, here.core).at[self.second]
        sems = self.two_send.at[place], self.two_recv.at[place]
        return remote(part, part, *sems, here.at_row(here.across))

    def to_core(self, which, step):
        here, place = self.here, self.order[step]
        target = self.block(here.rows[which], place, here.core)
        source = self.held(step) if which == 0 else target
        sems = self.core_send.at[which, place], self.core_recv.at[which, place]
        return remote(source, target, *sems, here.other_core())

    def line_step(self, step):
        here, place = self.here, self.order[step]
        if step > 0:
            arrived(self.held(step), self.line_recv.at[place])
        if self.line:

            @pl.when((place <= here.col) & (here.col < 3))
            def _():
                self.up(step).start()

            @pl.when((place >= here.col) & (here.col > 0))
            def _():
                self.down(step).start()

    def near_step(self, step):
        self.to_across(step).start()
        self.to_along(step).start()
        if self.core:
            self.to_core(0, step).start()

    def plane_step(self, step):
        here, place = self.here, self.order[step]
        arrived(self.block(here.across, place, here.core), self.across_recv.at[place])
        self.corner_one(step).start()
        if self.core:
            self.to_core(1, step).start()
        arrived(self.block(here.along, place, here.core), self.along_recv.at[place])
        self.corner_two(step).start()
        if self.core:
            self.to_core(2, step).start()

    def corner_step(self, step):
        here, place = self.here, self.order[step]
        target = self.block(here.opposite, place, here.core)
        arrived(target.at[self.first], self.one_recv.at[place])
        arrived(target.at[self.second], self.two_recv.at[place])
        if self.core:
            self.to_core(3, step).start()

    def step(self, index):
        if index < self.steps:
            self.line_step(index)
        if self.plane and 0 <= index - 1 < self.steps:
            self.plane_step(index - 1)
        if self.plane and index < self.steps:
            self.near_step(index)
        if self.plane and 0 <= index - 2 < self.steps:
            self.corner_step(index - 2)

    def core_arrived(self, which, step):
        here, place = self.here, self.order[step]
        target = self.block(here.rows[which], place, 1 - here.core)
        arrived(target, self.core_recv.at[which, place])

    def finish(self, arrivals=True):
        here = self.here
        for step in range(self.steps):
            place = self.order[step]
            if self.line:

                @pl.when((place <= here.col) & (here.col < 3))
                def _():
                    self.up(step).wait_send()

                @pl.when((place >= here.col) & (here.col > 0))
                def _():
                    self.down(step).wait_send()

            if self.plane:
                self.to_across(step).wait_send()
                self.to_along(step).wait_send()
                self.corner_one(step).wait_send()
                self.corner_two(step).wait_send()
                for which in range(4 if self.core else 0):
                    self.to_core(which, step).wait_send()
                    if arrivals:
                        self.core_arrived(which, step)


def rows_block(buffer, rows, row, place):
    return buffer.at[pl.ds(pl.multiple_of((row * 4 + place) * rows, rows), rows)]


def place_spread(here, buffer, rows, step, sems):
    def block(row, unused_place, unused_core):
        return rows_block(buffer, rows, row, here.near_first[step])

    return Spread(here, block(here.row, 0, 0), block, rows, sems, line=False, core=False)


COLLECT_SEMS = (
    [pltpu.SemaphoreType.DMA((4,))] * 4
    + [pltpu.SemaphoreType.DMA((2, 4))] * 4
    + [pltpu.SemaphoreType.DMA((4,))] * 2
    + [pltpu.SemaphoreType.DMA((5,))]
)


def collect_buffers(rows, width):
    return [
        pltpu.VMEM((4, 4, rows, width), BF16),
        pltpu.VMEM((4, rows // 2, width), BF16),
        pltpu.VMEM((4, rows // 2, width), BF16),
        pltpu.VMEM((4, rows, width), BF16),
        pltpu.VMEM((4, rows, width), BF16),
        pltpu.VMEM((5, rows, width), BF16),
    ]


class Collect:
    def __init__(self, here, buffers, sems):
        self.here = here
        self.mine, self.one, self.two, self.from_across, self.from_along, self.line = buffers
        (
            self.one_send, self.one_recv, self.two_send, self.two_recv,
            self.across_send, self.across_recv, self.along_send, self.along_recv,
            self.up_send, self.down_send, self.line_recv,
        ) = sems
        half = self.mine.shape[2] // 2
        self.halves = (pl.ds(0, half), pl.ds(half, half))

    def give_one(self, place):
        here = self.here
        return remote(
            self.mine.at[3, place, self.halves[0]], self.one.at[place],
            self.one_send.at[place], self.one_recv.at[place], here.at_row(here.across),
        )

    def give_two(self, place):
        here = self.here
        return remote(
            self.mine.at[3, place, self.halves[1]], self.two.at[place],
            self.two_send.at[place], self.two_recv.at[place], here.at_row(here.along),
        )

    def give_across(self, place, half):
        here, part = self.here, self.halves[half]
        return remote(
            self.mine.at[1, place, part], self.from_across.at[place, part],
            self.across_send.at[half, place], self.across_recv.at[half, place], here.at_row(here.across),
        )

    def give_along(self, place, half):
        here, part = self.here, self.halves[half]
        return remote(
            self.mine.at[2, place, part], self.from_along.at[place, part],
            self.along_send.at[half, place], self.along_recv.at[half, place], here.at_row(here.along),
        )

    def give_up(self, place):
        here = self.here
        sems = self.up_send.at[place], self.line_recv.at[place]
        return remote(self.mine.at[0, place], self.line.at[place], *sems, here.at_col(here.col + 1))

    def give_down(self, place, slot):
        here = self.here
        sems = self.down_send.at[place], self.line_recv.at[slot]
        return remote(self.mine.at[0, place], self.line.at[slot], *sems, here.at_col(here.col - 1))

    def start_far(self, place):
        self.give_one(place).start()
        self.give_two(place).start()
        self.give_along(place, 1).start()

    def start_near(self, place):
        self.give_across(place, 0).start()

    def corner_step(self, place):
        self.give_two(place).wait_recv()
        add_into(self.mine.at[1, place, self.halves[1]], self.two.at[place])
        self.give_across(place, 1).start()
        self.give_one(place).wait_recv()
        add_into(self.mine.at[2, place, self.halves[0]], self.one.at[place])
        self.give_along(place, 0).start()

    def plane_step(self, place):
        for half in range(2):
            self.give_across(place, half).wait_recv()
            self.give_along(place, half).wait_recv()
        add_into(self.mine.at[0, place], self.from_across.at[place], self.from_along.at[place])

    def line_step(self, place):
        col = self.here.col

        @pl.when((place > col) & (col > 0))
        def _():
            self.give_up(place).wait_recv()
            add_into(self.mine.at[0, place], self.line.at[place])

        @pl.when((place < col) & (col < 3))
        def _():
            self.give_down(place, place).wait_recv()
            add_into(self.mine.at[0, place], self.line.at[place])

        @pl.when(place > col)
        def _():
            self.give_up(place).start()

        @pl.when(place < col - 1)
        def _():
            self.give_down(place, place).start()

        @pl.when(place == col - 1)
        def _():
            self.give_down(place, 4).start()

    def own_step(self):
        col = self.here.col

        @pl.when(col > 0)
        def _():
            self.give_up(col).wait_recv()
            add_into(self.mine.at[0, col], self.line.at[col])

        @pl.when(col < 3)
        def _():
            self.give_down(col, 4).wait_recv()
            add_into(self.mine.at[0, col], self.line.at[4])

    def finish(self):
        col = self.here.col
        for place in range(4):
            self.give_one(place).wait_send()
            self.give_two(place).wait_send()
            for half in range(2):
                self.give_across(place, half).wait_send()
                self.give_along(place, half).wait_send()

            @pl.when(place > col)
            def _():
                self.give_up(place).wait_send()

            @pl.when(place < col)
            def _():
                self.give_down(place, place).wait_send()


def doc_start(places, cuts):
    return jnp.where(places >= cuts[1], cuts[1], jnp.where(places >= cuts[0], cuts[0], 0))


def key_blocks(cuts, first_query, rows, scores_of, block_fn):
    def scan(index, carry):
        start = pl.multiple_of(index * rows, rows)
        free = (start >= doc_start(first_query + rows - 1, cuts)) & (start + rows <= first_query + 1)

        @pl.when(free)
        def _():
            block_fn(start, scores_of(start))

        @pl.when(jnp.logical_not(free))
        def _():
            key_place = start + lax.broadcasted_iota(jnp.int32, (rows, rows), 0)
            place = first_query + lax.broadcasted_iota(jnp.int32, (1, rows), 1)
            allowed = (key_place <= place) & (key_place >= doc_start(place, cuts))
            block_fn(start, jnp.where(allowed, scores_of(start), MASKED))

        return carry

    lax.fori_loop(doc_start(first_query, cuts) // rows, first_query // rows + 1, scan, 0)


def attend_kernel(scale, group_tok, cuts, query, keys, values_t, mixed, total, top, summed, acc):
    rows = query.shape[0]
    side = lax.axis_index("exp") % 2
    first_query = side * group_tok + pl.program_id(0) * rows
    top[...] = jnp.full_like(top, MASKED)
    summed[...] = jnp.zeros_like(summed)
    acc[...] = jnp.zeros_like(acc)
    cut = (cuts[0, 0], cuts[0, 1])

    def scores_of(start):
        return contract_cols(keys[pl.ds(start, rows)], query[...]) * scale

    def block_fn(start, scores):
        old = top[...]
        new = jnp.maximum(old, jnp.max(scores, axis=0, keepdims=True))
        weights = jnp.exp(scores - new)
        decay = jnp.exp(old - new)
        top[...] = new
        summed[...] = summed[...] * decay + jnp.sum(weights, axis=0, keepdims=True)
        acc[...] = acc[...] * decay + matmul(values_t[:, pl.ds(start, rows)], weights.astype(BF16))

    key_blocks(cut, first_query, rows, scores_of, block_fn)
    mixed[...] = (acc[...] / summed[...]).T
    total[...] = top[...] + jnp.log(summed[...])


def attend(query, keys, values, cuts, scale, rows=512):
    group_tok, head_size = query.shape
    whole = lambda shape: pl.BlockSpec(shape, lambda i: (0, 0))
    return pl.pallas_call(
        functools.partial(attend_kernel, scale, group_tok),
        grid=(group_tok // rows,),
        in_specs=[
            pl.BlockSpec(memory_space=pltpu.SMEM),
            pl.BlockSpec((rows, head_size), lambda i: (i, 0)),
            whole(keys.shape),
            whole(values.shape[::-1]),
        ],
        out_specs=[
            pl.BlockSpec((rows, head_size), lambda i: (i, 0)),
            pl.BlockSpec((1, rows), lambda i: (0, i)),
        ],
        out_shape=[
            jax.ShapeDtypeStruct((group_tok, head_size), F32),
            jax.ShapeDtypeStruct((1, group_tok), F32),
        ],
        scratch_shapes=[
            pltpu.VMEM((1, rows), F32),
            pltpu.VMEM((1, rows), F32),
            pltpu.VMEM((head_size, rows), F32),
        ],
        compiler_params=pltpu.CompilerParams(vmem_limit_bytes=40 * 2**20),
        cost_estimate=pl.CostEstimate(
            flops=4 * 7 * 2**20 * head_size, bytes_accessed=2**23, transcendentals=7 * 2**20
        ),
    )(cuts[None], query, keys, values.T)


def attend_back_kernel(
    scale, group_tok, cuts, query, keys, keys_t, values, d_mixed, total, delta,
    d_query, d_keys, d_values, acc,
):
    rows = query.shape[0]
    side = lax.axis_index("exp") % 2
    first_query = side * group_tok + pl.program_id(0) * rows
    cut = (cuts[0, 0], cuts[0, 1])

    @pl.when(pl.program_id(0) == 0)
    def _():
        d_keys[...] = jnp.zeros_like(d_keys)
        d_values[...] = jnp.zeros_like(d_values)

    acc[...] = jnp.zeros_like(acc)

    def scores_of(start):
        return contract_cols(keys[pl.ds(start, rows)], query[...]) * scale

    def block_fn(start, scores):
        part = pl.ds(start, rows)
        weights = jnp.exp(scores - total[...])
        d_weights = contract_cols(values[part], d_mixed[...])
        d_scores = (weights * (d_weights - delta[...])).astype(BF16)
        d_values[part] += matmul(weights.astype(BF16), d_mixed[...])
        d_keys[part] += matmul(d_scores, query[...]) * scale
        acc[...] += matmul(keys_t[:, part], d_scores)

    key_blocks(cut, first_query, rows, scores_of, block_fn)
    d_query[...] = (acc[...] * scale).T


def attend_back(query, keys, values, d_mixed, mixed, total, cuts, scale, rows=512):
    group_tok, head_size = query.shape
    delta = jnp.sum(d_mixed.astype(F32) * mixed, axis=1)[None]
    whole = lambda shape: pl.BlockSpec(shape, lambda i: (0, 0))
    block = pl.BlockSpec((rows, head_size), lambda i: (i, 0))
    line = pl.BlockSpec((1, rows), lambda i: (0, i))
    return pl.pallas_call(
        functools.partial(attend_back_kernel, scale, group_tok),
        grid=(group_tok // rows,),
        in_specs=[
            pl.BlockSpec(memory_space=pltpu.SMEM),
            block,
            whole(keys.shape),
            whole(keys.shape[::-1]),
            whole(keys.shape),
            block,
            line,
            line,
        ],
        out_specs=[block, whole(keys.shape), whole(keys.shape)],
        out_shape=[
            jax.ShapeDtypeStruct((group_tok, head_size), F32),
            jax.ShapeDtypeStruct(keys.shape, F32),
            jax.ShapeDtypeStruct(keys.shape, F32),
        ],
        scratch_shapes=[pltpu.VMEM((head_size, rows), F32)],
        compiler_params=pltpu.CompilerParams(vmem_limit_bytes=48 * 2**20),
        cost_estimate=pl.CostEstimate(
            flops=10 * 7 * 2**20 * head_size, bytes_accessed=2**23, transcendentals=7 * 2**20
        ),
    )(cuts[None], query, keys, keys.T, values, d_mixed, total, delta)


def transposed_product(left, right):
    return jnp.dot(left.T, right, preferred_element_type=F32)


def column_of(line):
    return jnp.broadcast_to(line, (128, 128)).T[:, :1]


def line_of(column):
    return jnp.broadcast_to(column, (128, 128)).T[:1]


def expert_kernel(
    expert_count, normed, unused_grads, mask, gate_half, up_half, down_half,
    gate_other, up_other, down_other, router,
    rows_all, out_parts, total, inner_in, grads_all, grad_gate, grad_up, grad_down,
    their_gates, their_down,
    gate_w, up_w, down_w, masks, x_buf, d_buf, gates_t, weighteds_t, d_gates, d_ups, weighteds, out_buf,
    inner, sum_buf, sum_down, *rest,
):
    here = Here()
    row, col, core = here.row, here.col, here.core
    rows, width = normed.shape
    half = gate_half.shape[1]
    expert = row * 4 + col
    count = len(SPREAD_SEMS)
    collect = Collect(here, rest[:6], rest[6 : 6 + len(COLLECT_SEMS)])
    rest = rest[6 + len(COLLECT_SEMS) :]
    (
        weight_sem, load_sem, store_sem, tile_sem, give_send, give_recv, their_sem, sum_sem,
        inner_send, inner_recv,
    ) = rest[:10]
    sems = rest[10:]

    def x_block(of_row, place, unused_core):
        return rows_all.at[pl.ds(pl.multiple_of((of_row * 4 + place) * rows, rows), rows)]

    def d_block(of_row, place, unused_core):
        return grads_all.at[pl.ds(pl.multiple_of((of_row * 4 + place) * rows, rows), rows)]

    def m_block(of_row, place, unused_core):
        return masks.at[of_row, place]

    spread_x = Spread(here, normed, x_block, rows, sems[:count], core=False)
    spread_m = Spread(here, mask, m_block, mask.shape[0], sems[count : 2 * count], core=False)
    spread_d = place_spread(here, grads_all, rows, 2, sems[2 * count :])
    order = here.near_first

    own_half = pl.ds(pl.multiple_of(core * half, half), half)
    other_half = pl.ds(pl.multiple_of((1 - core) * half, half), half)
    keeps = [
        pltpu.make_async_copy(source, target, weight_sem.at[index])
        for index, (source, target) in enumerate(
            (
                (normed, x_block(row, col, 0)),
                (mask, m_block(row, col, 0)),
                (gate_half, gate_w.at[:, own_half]),
                (up_half, up_w.at[:, own_half]),
                (down_half, down_w.at[own_half]),
                (gate_other, gate_w.at[:, other_half]),
                (up_other, up_w.at[:, other_half]),
                (down_other, down_w.at[other_half]),
            )
        )
    ]
    greet(here.group_peers() + [here.other_core()])
    spread_x.step(0)
    spread_m.step(0)
    for keep in keeps:
        keep.start()

    turns = (3, 2, 1, 0)

    def loads(step):
        return [
            pltpu.make_async_copy(
                source(here.rows[which], order[step], 0),
                target.at[pl.ds(position * rows, rows)],
                load_sem.at[position, array],
            )
            for position, which in enumerate(turns)
            for array, (source, target) in enumerate(((x_block, x_buf), (d_block, d_buf)))
        ]

    def stores(step):
        return [
            pltpu.make_async_copy(
                out_buf.at[pl.ds(position * rows, rows)],
                out_parts.at[which, order[step]],
                store_sem.at[position],
            )
            for position, which in enumerate(turns)
        ]

    tile = 256

    def first_products(step):
        place = order[step]
        x = x_buf[...]
        lane = lax.broadcasted_iota(jnp.int32, (x.shape[0], router.shape[1]), 1)
        logits = jnp.where(lane < expert_count, matmul(x, router[...]), MASKED)
        raised = jnp.exp(logits - jnp.max(logits, axis=1, keepdims=True))
        picked = jnp.sum(jnp.where(lane == expert, raised, 0.0), axis=1, keepdims=True)
        routed = jnp.concatenate(
            [column_of(masks[here.rows[which], place, pl.ds(expert, 1)]) for which in turns]
        )
        gate = picked / jnp.sum(raised, axis=1, keepdims=True) * routed
        columns = [
            pl.ds(pl.multiple_of((here.rows[which] * 4 + place) * rows, rows), rows) for which in turns
        ]

        def tile_step(index, inner_sum):
            at = pl.ds(pl.multiple_of(index * tile, tile), tile)
            pre_gate = matmul(x_buf[...], gate_w[:, at])
            pre_up = matmul(x_buf[...], up_w[:, at])
            back = contract_cols(d_buf[...], down_w[at])
            sigmoid_gate = 1.0 / (1.0 + jnp.exp(-pre_gate))
            silu_gate = pre_gate * sigmoid_gate
            hidden = (silu_gate * pre_up).astype(BF16).astype(F32)
            d_hid = back * gate
            d_gate = (d_hid * pre_up * (sigmoid_gate + silu_gate * (1.0 - sigmoid_gate))).astype(BF16)
            d_up = (d_hid * silu_gate).astype(BF16)
            weight = (hidden * gate).astype(BF16)
            d_gates[:, at] = d_gate
            d_ups[:, at] = d_up
            weighteds[:, at] = weight
            side = index // (half // tile)
            first = pl.multiple_of(index % (half // tile) * tile, tile)
            for values, target in (
                (d_gate, gates_t.at[side, pl.ds(first, tile)]),
                (d_up, gates_t.at[side, pl.ds(first + half, tile)]),
                (weight, weighteds_t.at[at]),
            ):
                turned = values.T
                for position, column in enumerate(columns):
                    target[:, column] = turned[:, position * rows : (position + 1) * rows]
            return inner_sum + jnp.sum(hidden * back, axis=1, keepdims=True)

        start = jnp.zeros((x.shape[0], 1), F32)
        inner_sum = lax.fori_loop(0, gate_w.shape[1] // tile, tile_step, start, unroll=2)
        for position, which in enumerate(turns):
            part = slice(position * rows, (position + 1) * rows)
            inner[here.rows[which], place, 0:1] = line_of(inner_sum[part])

    def second_products(step):
        place = order[step]

        @pl.loop(0, width // tile, unroll=2)
        def _(index):
            at = pl.ds(pl.multiple_of(index * tile, tile), tile)
            out_buf[:, at] = matmul(weighteds[...], down_w[:, at]).astype(BF16)
            d_x = contract_cols(d_gates[...], gate_w[at]) + contract_cols(d_ups[...], up_w[at])
            d_x = d_x.astype(BF16)
            for position, which in enumerate(turns):
                collect.mine[which, place, :, at] = d_x[position * rows : (position + 1) * rows]

    for index in (1, 2):
        spread_x.step(index)
        spread_m.step(index)
    for keep in keeps:
        keep.wait()
    for copy in loads(0):
        copy.start()
    turn_order = (0, 1, 3, 2)
    ends = (col == 0) | (col == 3)

    def from_ends(step):
        @pl.when(ends)
        def _():
            collect.line_step(order[step])

    def from_inside(step):
        @pl.when(jnp.logical_not(ends))
        def _():
            collect.line_step(order[step])

    for turn, step in enumerate(turn_order):
        for copy in loads(step):
            copy.wait()
        first_products(step)
        if turn < 2:
            spread_x.step(turn + 3)
            spread_m.step(turn + 3)
        if turn == 1:
            spread_d.step(0)
        if turn == 2:
            spread_d.step(2)
        if turn in (0, 2):
            for copy in loads(turn_order[turn + 1]):
                copy.start()
        if turn > 0:
            for copy in stores(turn_order[turn - 1]):
                copy.wait()
            collect.corner_step(order[turn_order[turn - 1]])
        second_products(step)
        for copy in stores(step):
            copy.start()
        collect.start_far(order[step])
        collect.start_near(order[step])
        if turn == 1:
            spread_x.step(5)
            spread_m.step(5)
            spread_d.step(1)
            for copy in loads(turn_order[2]):
                copy.start()
        if turn > 0:
            collect.plane_step(order[turn_order[turn - 1]])
        if turn > 1:
            from_ends(turn_order[turn - 1])

    tiles = width // tile

    def tile_at(index):
        return pl.ds(pl.multiple_of(index * tile, tile), tile)

    def acts_of(kind, side):
        if kind == 0:
            return gates_t[side]
        return weighteds_t[pl.ds(pl.multiple_of(side * half, half), half)]

    counts = (2 * half, half)

    def slot_at(kind, slot):
        return pl.ds(pl.multiple_of((2 * kind + slot) * tile, tile), tile)

    def tile_buf(kind, slot):
        return gate_w.at[:, slot_at(kind, slot)]

    def give_buf(kind, slot):
        return up_w.at[pl.ds(0, counts[kind]), slot_at(kind, slot)]

    def their_buf(kind, slot):
        return up_w.at[pl.ds(width // 2, counts[kind]), slot_at(kind, slot)]

    theirs = (their_gates, their_down)

    def tile_load(kind, index, slot):
        source = (rows_all, grads_all)[kind]
        return pltpu.make_async_copy(
            source.at[:, tile_at(index)], tile_buf(kind, slot), tile_sem.at[slot]
        )

    def give(kind, index, slot):
        sems = give_send.at[slot, kind], give_recv.at[kind, index]
        return remote(give_buf(kind, slot), theirs[kind].at[:, tile_at(index)], *sems, here.other_core())

    def their_load(kind, index, slot):
        return pltpu.make_async_copy(
            theirs[kind].at[:, tile_at(index)],
            their_buf(kind, slot),
            their_sem.at[slot, kind],
        )

    def sum_stores(kind, index, slot):
        if kind == 1:
            target = grad_down.at[:, tile_at(index)]
            return [pltpu.make_async_copy(sum_down, target, sum_sem.at[0, 2])]
        return [
            pltpu.make_async_copy(
                sum_buf.at[slot, part], target.at[tile_at(index)], sum_sem.at[slot, part]
            )
            for part, target in enumerate((grad_gate, grad_up))
        ]

    def give_gradients(kind, start, stop):
        tile_load(kind, start, 0).start()

        @pl.loop(start, stop)
        def _(index):
            slot = index % 2

            @pl.when(index + 1 < stop)
            def _():
                tile_load(kind, index + 1, 1 - slot).start()

            tile_load(kind, index, slot).wait()
            product = matmul(acts_of(kind, 1 - core), tile_buf(kind, slot)[...])

            @pl.when(index >= 2)
            def _():
                give(kind, index - 2, slot).wait_send()

            give_buf(kind, slot)[...] = product.astype(BF16)
            give(kind, index, slot).start()

    def keep_gradients(kind, start, stop):
        tile_load(kind, start, 0).start()
        give(kind, start, 0).wait_recv()
        their_load(kind, start, 0).start()

        @pl.loop(start, stop)
        def _(index):
            slot = index % 2

            @pl.when(index + 1 < stop)
            def _():
                tile_load(kind, index + 1, 1 - slot).start()
                give(kind, index + 1, 1 - slot).wait_recv()
                their_load(kind, index + 1, 1 - slot).start()

            tile_load(kind, index, slot).wait()
            product = matmul(acts_of(kind, core), tile_buf(kind, slot)[...])
            their_load(kind, index, slot).wait()
            product = product + their_buf(kind, slot)[...].astype(F32)
            held = 2 - kind

            @pl.when(index >= held)
            def _():
                for copy in sum_stores(kind, index - held, slot):
                    copy.wait()

            if kind == 1:
                sum_down[...] = product
            else:
                sum_buf[slot, 0] = product[:half].T
                sum_buf[slot, 1] = product[half:].T
            for copy in sum_stores(kind, index, slot):
                copy.start()

    def give_inner(index):
        step = index + 1
        to_row, to_col = (row + step // 4) % 4, (col + step) % 4
        return remote(
            inner.at[to_row, to_col],
            inner_in.at[row, col],
            inner_send.at[index],
            inner_recv.at[row, col],
            (to_row, to_col, core),
        )

    for index in range(15):
        give_inner(index).start()
    inner_in[row, col] = inner[row, col]
    give_gradients(0, 0, tiles // 2)
    from_inside(3)
    collect.corner_step(order[2])
    give_gradients(0, tiles // 2, tiles)
    collect.plane_step(order[2])
    from_ends(2)
    give_gradients(1, 0, tiles)
    from_inside(2)
    keep_gradients(0, 0, tiles // 2)
    from_inside(1)
    keep_gradients(0, tiles // 2, tiles)
    keep_gradients(1, 0, tiles)
    collect.own_step()
    total[...] = collect.mine[0, col]

    for index in range(15):
        give_inner(index).wait_send()
        step = index + 1
        from_row, from_col = (row + 4 - step // 4) % 4, (col + 4 - step % 4) % 4
        arrived(inner_in.at[from_row, from_col], inner_recv.at[from_row, from_col])
    for copy in stores(turn_order[3]):
        copy.wait()
    for kind in range(2):
        for slot in range(2):
            give(kind, tiles - 2 + slot, slot).wait_send()
        for slot in range(2 - kind):
            for copy in sum_stores(kind, tiles - 2 + kind + slot, slot):
                copy.wait()
    spread_x.finish()
    spread_m.finish()
    spread_d.finish()
    collect.finish()


def expert_stage(normed, grads_all, mask, halves, others, router, collective_id):
    rows, width = normed.shape
    half = halves[0].shape[1]
    expert_count = router.shape[1]
    router = jnp.pad(router, ((0, 0), (0, 128 - expert_count)))
    tokens = 16 * rows
    tile = 256
    vmem = pl.BlockSpec(memory_space=pltpu.VMEM)
    hbm = pl.BlockSpec(memory_space=pl.ANY)
    dma = pltpu.SemaphoreType.DMA
    blocks = jax.ShapeDtypeStruct((4, 4, rows, width), BF16)
    got = pl.pallas_call(
        functools.partial(expert_kernel, expert_count),
        in_specs=[hbm] * 9 + [vmem],
        out_specs=[hbm] * 2 + [vmem] * 2 + [hbm] * 6,
        out_shape=[
            jax.ShapeDtypeStruct((tokens, width), BF16),
            blocks,
            jax.ShapeDtypeStruct((rows, width), BF16),
            jax.ShapeDtypeStruct((4, 4, 8, rows), F32),
            jax.ShapeDtypeStruct((tokens, width), BF16),
            jax.ShapeDtypeStruct((width, half), F32),
            jax.ShapeDtypeStruct((width, half), F32),
            jax.ShapeDtypeStruct((half, width), F32),
            jax.ShapeDtypeStruct((2 * half, width), BF16),
            jax.ShapeDtypeStruct((half, width), BF16),
        ],
        input_output_aliases={1: 4},
        scratch_shapes=[
            pltpu.VMEM((width, 2 * half), BF16),
            pltpu.VMEM((width, 2 * half), BF16),
            pltpu.VMEM((2 * half, width), BF16),
            pltpu.VMEM((4, 4) + mask.shape, F32),
            pltpu.VMEM((4 * rows, width), BF16),
            pltpu.VMEM((4 * rows, width), BF16),
            pltpu.VMEM((2, 2 * half, tokens), BF16),
            pltpu.VMEM((2 * half, tokens), BF16),
            pltpu.VMEM((4 * rows, 2 * half), BF16),
            pltpu.VMEM((4 * rows, 2 * half), BF16),
            pltpu.VMEM((4 * rows, 2 * half), BF16),
            pltpu.VMEM((4 * rows, width), BF16),
            pltpu.VMEM((4, 4, 8, rows), F32),
            pltpu.VMEM((2, 2, tile, half), F32),
            pltpu.VMEM((half, tile), F32),
        ]
        + collect_buffers(rows, width)
        + COLLECT_SEMS
        + [
            dma((8,)), dma((4, 2)), dma((4,)),
            dma((2,)), dma((2, 2)), dma((2, width // tile)), dma((2, 2)), dma((2, 3)),
            dma((15,)), dma((4, 4)),
        ]
        + SPREAD_SEMS * 3,
        compiler_params=pltpu.CompilerParams(
            collective_id=collective_id, has_side_effects=True, vmem_limit_bytes=61 * 2**20
        ),
        cost_estimate=pl.CostEstimate(
            flops=18 * 2 * tokens * width * half,
            bytes_accessed=2**26,
            transcendentals=2 * tokens * half,
        ),
    )(normed, grads_all, mask, *halves, *others, router)
    return got[1], got[2], got[3], got[5:8]


def project_kernel(
    hidden, gain, weights, q_gain, k_gain, cosine, sine, grads,
    normed, all_weights, qkv, totals, query, keys, values, grads_all,
    heads, stat, scale_q, scale_k, kept_sem, kept_grads_sem, kept_kv_sem,
    stat_send, stat_recv, head_send, head_recv, pair_send, pair_recv, *sems,
):
    here = Here()
    row, col, core = here.row, here.col, here.core
    count = len(SPREAD_SEMS)
    rows, width = hidden.shape
    depth = weights.shape[0]
    part = depth // 2

    def weight_block(of_row, unused_place, of_core):
        return all_weights.at[pl.ds(pl.multiple_of(of_row * depth + of_core * part, part), part)]

    def normed_block(unused_row, place, unused_core):
        return normed.at[pl.ds(pl.multiple_of(place * rows, rows), rows)]

    own_weight = weights.at[pl.ds(pl.multiple_of(core * part, part), part)]
    spread_w = Spread(here, own_weight, weight_block, part, sems[:count], line=False)
    spread_n = Spread(
        here, normed_block(row, col, core), normed_block, rows, sems[count : 2 * count], plane=False
    )

    def grads_block(of_row, place, unused_core):
        return rows_block(grads_all, rows, of_row, place)

    spread_d = Spread(here, grads, grads_block, rows, sems[2 * count : 3 * count], plane=False)
    spread_e = Spread(
        here, grads, lambda of_row, *unused: grads_block(of_row, col, 0), rows, sems[3 * count :],
        line=False, core=False,
    )
    keep_grads = pltpu.make_async_copy(grads, grads_block(row, col, 0), kept_grads_sem)
    keep_grads.start()
    greet(here.plane_peers() + here.line_peers() + [here.other_core()])
    spread_w.step(0)
    keep = pltpu.make_async_copy(own_weight, weight_block(row, 0, core), kept_sem)
    keep.start()

    values_in = hidden[...].astype(F32)
    scale_one = lax.rsqrt(jnp.mean(values_in * values_in, axis=1, keepdims=True) + EPSILON)
    own_rows = pl.ds(pl.multiple_of(col * rows, rows), rows)
    normed[own_rows] = (values_in * scale_one * gain[...].astype(F32)).astype(BF16)
    spread_n.step(0)
    spread_w.step(1)
    spread_n.step(1)
    spread_w.step(2)
    spread_n.step(2)
    spread_n.step(3)
    spread_d.step(0)
    spread_e.step(0)
    keep.wait()
    for which in range(4):
        spread_w.core_arrived(which, 0)

    columns = 256

    @pl.loop(0, qkv.shape[1] // columns)
    def _(index):
        at = pl.ds(pl.multiple_of(index * columns, columns), columns)
        qkv[:, at] = matmul(normed[...], all_weights[:, at])

    spread_e.step(1)

    plane = qkv.shape[1] // (3 * HD)
    for kind in range(2):
        square = jnp.zeros((qkv.shape[0], HD), F32)
        for head in range(plane):
            start = (head * 3 + kind) * HD
            raw = qkv[:, start : start + HD]
            square = square + raw * raw
        stat[col, kind : kind + 1] = jnp.sum(square.T, axis=0, keepdims=True)

    def give_stat(step):
        peer = here.line_peers()[step]
        return remote(stat.at[col], stat.at[col], stat_send.at[step], stat_recv.at[col], peer)

    for step in range(3):
        give_stat(step).start()
    spread_d.step(1)
    for step in range(3):
        place = (col + step + 1) % 4
        arrived(stat.at[place], stat_recv.at[place])
    total = stat[0] + stat[1] + stat[2] + stat[3]
    totals[...] = total
    for kind, target in enumerate((scale_q, scale_k)):
        line = lax.rsqrt(total[kind : kind + 1] / width + EPSILON)
        target[...] = jnp.broadcast_to(line, (HD, line.shape[1])).T

    chunk = 64

    @pl.loop(0, qkv.shape[0] // chunk)
    def _(index):
        at = pl.ds(pl.multiple_of(index * chunk, chunk), chunk)
        for head in range(plane):
            for kind, (scales, gains) in enumerate(((scale_q, q_gain), (scale_k, k_gain))):
                raw = qkv[at, pl.ds((head * 3 + kind) * HD, HD)]
                unit = raw * scales[at] * gains[:, head * HD : (head + 1) * HD]
                turned = pltpu.roll(unit, HD // 2, 1)
                heads[head, kind, at] = (unit * cosine[at] + turned * sine[at]).astype(BF16)
            heads[head, 2, at] = qkv[at, pl.ds((head * 3 + 2) * HD, HD)].astype(BF16)

    targets = (query.at[row], keys.at[1, row], values.at[1, row])

    def give_head(step, kind):
        dest = here.rows[step + 1]
        sems = head_send.at[step, kind], head_recv.at[kind, row]
        return remote(heads.at[dest, kind], targets[kind], *sems, here.at_row(dest))

    for kind in (1, 2, 0):
        for step in range(3):
            give_head(step, kind).start()

    def give_pair(source, kind):
        array = (keys, values)[kind]
        sems = pair_send.at[kind, source], pair_recv.at[kind, source]
        return remote(array.at[1, source], array.at[0, source], *sems, here.other_core())

    def keep_pair(source, kind):
        array = (keys, values)[kind]
        return pltpu.make_async_copy(
            array.at[1, source], array.at[0, source], kept_kv_sem.at[kind, source]
        )

    def pair_from(source):
        @pl.when(core == 0)
        def _():
            for kind in range(2):
                give_pair(source, kind).start()
                keep_pair(source, kind).start()

    for kind, array in ((1, keys), (2, values)):
        array[1, row] = heads[row, kind]
    query[row] = heads[row, 0]
    pair_from(row)
    spread_e.step(2)
    spread_d.step(2)
    for source in here.rows[1:]:
        arrived(keys.at[1, source], head_recv.at[1, source])
        arrived(values.at[1, source], head_recv.at[2, source])
        pair_from(source)
    for source in here.rows[1:]:
        arrived(query.at[source], head_recv.at[0, source])

    @pl.when(core == 0)
    def _():
        for source in range(4):
            for kind in range(2):
                give_pair(source, kind).wait_send()
                keep_pair(source, kind).wait()

    @pl.when(core == 1)
    def _():
        for source in range(4):
            for kind in range(2):
                give_pair(source, kind).wait_recv()

    for step in range(3):
        give_stat(step).wait_send()
        for kind in range(3):
            give_head(step, kind).wait_send()
    spread_d.step(3)
    keep_grads.wait()
    spread_d.finish()
    spread_e.finish()
    spread_w.finish(arrivals=False)
    spread_n.finish()


def project(hidden, gain, weights, q_gain, k_gain, cosine, sine, grads, collective_id):
    rows, width = hidden.shape
    depth, columns = weights.shape
    row_tok = 4 * rows
    plane = columns // (3 * HD)
    vmem = pl.BlockSpec(memory_space=pltpu.VMEM)
    hbm = pl.BlockSpec(memory_space=pl.ANY)
    return pl.pallas_call(
        project_kernel,
        in_specs=[vmem, vmem, hbm, vmem, vmem, vmem, vmem, hbm],
        out_specs=[vmem] * 7 + [hbm],
        out_shape=[
            jax.ShapeDtypeStruct((row_tok, width), BF16),
            jax.ShapeDtypeStruct((4 * depth, columns), BF16),
            jax.ShapeDtypeStruct((row_tok, columns), F32),
            jax.ShapeDtypeStruct((8, row_tok), F32),
            jax.ShapeDtypeStruct((4, row_tok, HD), BF16),
            jax.ShapeDtypeStruct((2, 4, row_tok, HD), BF16),
            jax.ShapeDtypeStruct((2, 4, row_tok, HD), BF16),
            jax.ShapeDtypeStruct((16 * rows, width), BF16),
        ],
        scratch_shapes=[
            pltpu.VMEM((plane, 3, row_tok, HD), BF16),
            pltpu.VMEM((4, 8, row_tok), F32),
            pltpu.VMEM((row_tok, HD), F32),
            pltpu.VMEM((row_tok, HD), F32),
            pltpu.SemaphoreType.DMA,
            pltpu.SemaphoreType.DMA,
            pltpu.SemaphoreType.DMA((2, 4)),
            pltpu.SemaphoreType.DMA((3,)),
            pltpu.SemaphoreType.DMA((4,)),
            pltpu.SemaphoreType.DMA((3, 3)),
            pltpu.SemaphoreType.DMA((3, 4)),
            pltpu.SemaphoreType.DMA((2, 4)),
            pltpu.SemaphoreType.DMA((2, 4)),
        ]
        + SPREAD_SEMS * 4,
        compiler_params=pltpu.CompilerParams(
            collective_id=collective_id, has_side_effects=True, vmem_limit_bytes=56 * 2**20
        ),
    )(hidden, gain[None], weights, q_gain, k_gain, cosine, sine, grads)


def attention_kernel(
    scale, cuts, query, keys, values, out_weights, hidden, gain, unused_grads,
    mixed, total, all_out, mixed_rows, middle, normed, grads_all,
    values_t, top, summed, acc, mixed_low, mixed_tok, kept_sem,
    row_send, row_recv, token_send, token_recv, *sems,
):
    here = Here()
    row, col, core = here.row, here.col, here.core
    rows = hidden.shape[0]
    row_tok = 4 * rows
    group_tok = 4 * row_tok
    side = out_weights.shape[0]

    def out_block(of_row, place, of_core):
        start = pl.multiple_of(place * side + of_core * (side // 2), side // 2)
        return all_out.at[pl.ds(start, side // 2), pl.ds(pl.multiple_of(of_row * side, side), side)]

    own_out = out_weights.at[pl.ds(pl.multiple_of(core * (side // 2), side // 2), side // 2)]
    count = len(SPREAD_SEMS)
    spread = Spread(here, own_out, out_block, side // 2, sems[:count])
    spread_d = place_spread(here, grads_all, rows, 1, sems[count : 2 * count])
    spread_e = place_spread(here, grads_all, rows, 3, sems[2 * count :])
    keep = pltpu.make_async_copy(own_out, out_block(row, col, core), kept_sem)
    keep.start()
    values_t[...] = values[...].T
    greet(here.plane_peers() + here.line_peers() + [here.other_core()])
    spread.step(0)
    cut = (cuts[0, 0], cuts[0, 1])
    last_query = 2 * group_tok - row_tok

    def queries(index):
        at = pl.ds(index * row_tok, row_tok)
        first_query = core * group_tok + index * row_tok
        top[...] = jnp.full_like(top, MASKED)
        summed[...] = jnp.zeros_like(summed)
        acc[...] = jnp.zeros_like(acc)

        def block_fn(part, scores):
            old = top[...]
            new = jnp.maximum(old, jnp.max(scores, axis=0, keepdims=True))
            weight = jnp.exp(scores - new)
            decay = jnp.exp(old - new)
            top[...] = new
            summed[...] = summed[...] * decay + jnp.sum(weight, axis=0, keepdims=True)
            acc[...] = acc[...] * decay + matmul(values_t[:, part], weight.astype(BF16))

        def scan(block, carry):
            first_key = block * row_tok
            part = pl.ds(pl.multiple_of(first_key, row_tok), row_tok)
            masked = (block == 0) | (first_key == first_query) | (first_query == last_query)

            @pl.when(jnp.logical_not(masked))
            def _():
                block_fn(part, contract_cols(keys[part], query[at]) * scale)

            @pl.when(masked)
            def _():
                key_place = first_key + lax.broadcasted_iota(jnp.int32, (row_tok, row_tok), 0)
                place = first_query + lax.broadcasted_iota(jnp.int32, (1, row_tok), 1)
                allowed = (key_place <= place) & (key_place >= doc_start(place, cut))
                scores = contract_cols(keys[part], query[at]) * scale
                block_fn(part, jnp.where(allowed, scores, MASKED))

            return carry

        lax.fori_loop(0, core * 4 + index + 1, scan, 0)
        got = (acc[...] / summed[...]).T
        mixed[at] = got
        mixed_low[index] = got.astype(BF16)
        total[:, at] = top[...] + jnp.log(summed[...])

        @pl.when(row != index)
        def _():
            give_row(index).start()

        @pl.when(row == index)
        def _():
            mixed_rows[row] = mixed_low[index]

    def give_row(index):
        sems_of = row_send.at[index], row_recv.at[row]
        return remote(mixed_low.at[index], mixed_rows.at[row], *sems_of, here.at_row(index))

    def give_token(step):
        place = (col + step) % 4
        part = pl.ds(pl.multiple_of(place * rows, rows), rows)
        sems_of = token_send.at[step], token_recv.at[col]
        return remote(mixed_rows.at[:, part], mixed_tok.at[col], *sems_of, here.at_col(place))

    for index in range(4):
        queries(index)
        spread.step(index + 1)
        if index == 1:
            spread_d.step(0)
    spread_d.step(1)
    for source in here.rows[1:]:
        arrived(mixed_rows.at[source], row_recv.at[source])
    for step in range(1, 4):
        give_token(step).start()
    mixed_tok[col] = mixed_rows[:, pl.ds(pl.multiple_of(col * rows, rows), rows)]
    spread.step(5)
    spread_e.step(0)
    spread_d.step(2)
    keep.wait()
    spread.finish()
    for step in range(1, 4):
        place = (col + 4 - step) % 4
        arrived(mixed_tok.at[place], token_recv.at[place])
    own = jnp.concatenate([mixed_tok[place, head] for place in range(4) for head in range(4)], axis=1)
    tile = 512

    @pl.loop(0, all_out.shape[1] // tile)
    def _(index):
        at = pl.ds(pl.multiple_of(index * tile, tile), tile)
        middle[:, at] = hidden[:, at].astype(F32) + matmul(own, all_out[:, at])

    values_in = middle[...]
    root = lax.rsqrt(jnp.mean(values_in * values_in, axis=1, keepdims=True) + EPSILON)
    normed[...] = (values_in * root * gain[...].astype(F32)).astype(BF16)
    spread_e.step(1)
    spread_e.step(2)
    spread_d.finish()
    spread_e.finish()
    for index in range(4):

        @pl.when(row != index)
        def _():
            give_row(index).wait_send()

    for step in range(1, 4):
        give_token(step).wait_send()


def attention_stage(
    query, keys, values, cuts, out_weights, hidden, gain, grads_all, scale, collective_id
):
    rows, width = hidden.shape
    row_tok, group_tok = 4 * rows, 16 * rows
    vmem, hbm = pl.BlockSpec(memory_space=pltpu.VMEM), pl.BlockSpec(memory_space=pl.ANY)
    dma = pltpu.SemaphoreType.DMA
    return pl.pallas_call(
        functools.partial(attention_kernel, scale),
        in_specs=[pl.BlockSpec(memory_space=pltpu.SMEM)] + [vmem] * 3 + [hbm] + [vmem] * 2 + [hbm],
        out_specs=[vmem] * 6 + [hbm],
        out_shape=[
            jax.ShapeDtypeStruct((group_tok, HD), F32),
            jax.ShapeDtypeStruct((1, group_tok), F32),
            jax.ShapeDtypeStruct((width, width), BF16),
            jax.ShapeDtypeStruct((4, row_tok, HD), BF16),
            jax.ShapeDtypeStruct((rows, width), F32),
            jax.ShapeDtypeStruct((rows, width), BF16),
            jax.ShapeDtypeStruct(grads_all.shape, BF16),
        ],
        input_output_aliases={7: 6},
        scratch_shapes=[
            pltpu.VMEM((HD, 2 * group_tok), BF16),
            pltpu.VMEM((1, row_tok), F32),
            pltpu.VMEM((1, row_tok), F32),
            pltpu.VMEM((HD, row_tok), F32),
            pltpu.VMEM((4, row_tok, HD), BF16),
            pltpu.VMEM((4, 4, rows, HD), BF16),
            dma, dma((4,)), dma((4,)), dma((4,)), dma((4,)),
        ]
        + SPREAD_SEMS * 3,
        compiler_params=pltpu.CompilerParams(
            collective_id=collective_id, has_side_effects=True, vmem_limit_bytes=40 * 2**20
        ),
    )(cuts[None], query, keys, values, out_weights, hidden, gain[None], grads_all)


class PairSum:
    def __init__(self, here, values, out, held, got, send, recv):
        self.here, self.values, self.out, self.held, self.got = here, values, out, held, got
        self.send, self.recv = send, recv
        col, half = here.col, values.shape[1] // 2
        self.own = pl.ds(pl.multiple_of(here.core * half, half), half)
        self.others = pl.ds(pl.multiple_of((1 - here.core) * half, half), half)
        self.peers = [
            here.at_row(here.across),
            here.at_row(here.along),
            here.at_col(col + 1 - 2 * (col % 2)),
            here.at_col((col + 2) % 4),
        ]

    def copy(self, step):
        here, sems = self.here, (self.send.at[step], self.recv.at[step])
        if step == 0:
            return remote(self.values.at[:, self.others], self.got.at[0], *sems, here.other_core())
        if step == 5:
            return remote(self.held.at[4], self.out.at[:, self.own], *sems, here.other_core())
        return remote(self.held.at[step - 1], self.got.at[step], *sems, self.peers[step - 1])

    def begin(self):
        self.copy(0).start()

    def step(self, index):
        if index == 5:
            arrived(self.out.at[:, self.others], self.recv.at[5])
            return
        self.copy(index).wait_recv()
        before = self.values[:, self.own] if index == 0 else self.held[index - 1]
        self.held[index] = before + self.got[index]
        if index == 4:
            self.out[:, self.own] = self.held[4]
        self.copy(index + 1).start()

    def finish(self):
        for index in range(6):
            self.copy(index).wait_send()


def pair_sum_buffers(rows, width):
    return [
        pltpu.VMEM((5, rows, width // 2), F32),
        pltpu.VMEM((5, rows, width // 2), F32),
        pltpu.SemaphoreType.DMA((6,)),
        pltpu.SemaphoreType.DMA((6,)),
    ]


def back_kernel(
    scale, cuts, d_attn, query, keys, values, mixed, total, out_weights, out_parts, early,
    d_attn_row, d_heads, out_total, early_sum,
    weights, d_mixed_give, d_mixed_row, d_mixed, keys_t, d_keys, d_values, acc, pair_out, pair_in,
    head_give, sum_held, sum_got, sum_send, sum_recv, weight_sem, load_sem,
    near_send, near_recv, head_send, head_recv, back_send, back_recv,
    pair_send, pair_recv, *rest,
):
    here = Here()
    row, col, core = here.row, here.col, here.core
    rows = d_attn.shape[0]
    row_tok = 4 * rows
    group_tok = 4 * row_tok
    plane = 4 * HD
    order = here.near_first[::-1]
    collect = Collect(here, rest[:6], rest[6 : 6 + len(COLLECT_SEMS)])
    sems = rest[6 + len(COLLECT_SEMS) :]

    def row_block(unused_row, place, unused_core):
        return d_attn_row.at[pl.ds(pl.multiple_of(place * rows, rows), rows)]

    spread = Spread(here, row_block(row, col, core), row_block, rows, sems, plane=False)
    pair_sum = PairSum(here, early, early_sum, sum_held, sum_got, sum_send, sum_recv)

    def load(which, place):
        return pltpu.make_async_copy(
            out_parts.at[which, place], collect.mine.at[which, place], load_sem.at[which, place]
        )

    load_weights = pltpu.make_async_copy(out_weights, weights, weight_sem)
    load_weights.start()
    for place in order:
        for which in (3, 2, 1, 0):
            load(which, place).start()
    keys_t[...] = keys[...].T
    d_attn_row[pl.ds(pl.multiple_of(col * rows, rows), rows)] = d_attn[...]
    greet(here.plane_peers() + here.line_peers() + [here.other_core()])

    def give_near(step):
        place = (col + step) % 4
        sems_of = near_send.at[step], near_recv.at[col]
        return remote(d_mixed_give.at[place], d_mixed_row.at[col], *sems_of, here.at_col(place))

    def give_head(step):
        dest = here.rows[step]
        part = pl.ds(pl.multiple_of(dest * HD, HD), HD)
        sems_of = head_send.at[step], head_recv.at[row]
        return remote(d_mixed_row.at[:, :, part], d_mixed.at[row], *sems_of, here.at_row(dest))

    def start(index):
        for which in (3, 2, 1):
            load(which, order[index]).wait()
        collect.start_far(order[index])
        collect.start_near(order[index])

    ends = (col == 0) | (col == 3)

    def from_ends(index):
        @pl.when(ends)
        def _():
            collect.line_step(order[index])

    def from_inside(index):
        @pl.when(jnp.logical_not(ends))
        def _():
            collect.line_step(order[index])

    def plane_part(index):
        load(0, order[index]).wait()
        collect.plane_step(order[index])

    start(0)
    pair_sum.begin()
    load_weights.wait()
    for step in (1, 2, 3, 0):
        place = (col + step) % 4
        part = pl.ds(pl.multiple_of(place * plane, plane), plane)
        product = contract_cols(d_attn[...], weights[part]).astype(BF16)
        if step == 0:
            d_mixed_row[col] = product
        else:
            d_mixed_give[place] = product
            give_near(step).start()
    spread.step(0)
    pair_sum.step(0)
    d_keys[...] = jnp.zeros_like(d_keys)
    d_values[...] = jnp.zeros_like(d_values)
    for step in range(1, 4):
        place = (col + 4 - step) % 4
        arrived(d_mixed_row.at[place], near_recv.at[place])
    for step in range(1, 4):
        give_head(step).start()
    d_mixed[row] = d_mixed_row[:, :, pl.ds(pl.multiple_of(row * HD, HD), HD)]
    collect.corner_step(order[0])
    start(1)
    pair_sum.step(1)
    spread.step(1)
    for source in here.rows[1:]:
        arrived(d_mixed.at[source], head_recv.at[source])

    cut = (cuts[0, 0], cuts[0, 1])
    last_query = 2 * group_tok - row_tok

    def queries(index):
        at = pl.ds(index * row_tok, row_tok)
        first_query = core * group_tok + index * row_tok
        gradient = d_mixed[index].reshape(row_tok, HD)
        delta = jnp.sum((gradient.astype(F32) * mixed[at]).T, axis=0, keepdims=True)
        sums = total[:, at]
        acc[...] = jnp.zeros_like(acc)

        def block_fn(part, scores):
            weight = jnp.exp(scores - sums)
            d_weight = contract_cols(values[part], gradient)
            d_scores = (weight * (d_weight - delta)).astype(BF16)
            d_values[part] += matmul(weight.astype(BF16), gradient)
            d_keys[part] += matmul(d_scores, query[at]) * scale
            acc[...] += matmul(keys_t[:, part], d_scores)

        def scan(block, carry):
            first_key = block * row_tok
            part = pl.ds(pl.multiple_of(first_key, row_tok), row_tok)
            masked = (block == 0) | (first_key == first_query) | (first_query == last_query)

            @pl.when(jnp.logical_not(masked))
            def _():
                block_fn(part, contract_cols(keys[part], query[at]) * scale)

            @pl.when(masked)
            def _():
                key_place = first_key + lax.broadcasted_iota(jnp.int32, (row_tok, row_tok), 0)
                place = first_query + lax.broadcasted_iota(jnp.int32, (1, row_tok), 1)
                allowed = (key_place <= place) & (key_place >= doc_start(place, cut))
                scores = contract_cols(keys[part], query[at]) * scale
                block_fn(part, jnp.where(allowed, scores, MASKED))

            return carry

        lax.fori_loop(0, core * 4 + index + 1, scan, 0)
        head_give[0, index] = (acc[...] * scale).T.astype(BF16)

    queries(0)
    plane_part(0)
    from_ends(0)
    collect.corner_step(order[1])
    start(2)
    spread.step(2)
    queries(1)
    from_inside(0)
    plane_part(1)
    from_ends(1)
    collect.corner_step(order[2])
    start(3)
    pair_sum.step(2)
    queries(2)
    from_inside(1)
    plane_part(2)
    from_ends(2)
    collect.corner_step(order[3])
    spread.step(3)
    queries(3)

    def give_back(step, kind):
        dest = here.rows[step]
        sems_of = back_send.at[step, kind], back_recv.at[kind, row]
        return remote(head_give.at[kind, dest], d_heads.at[row, kind], *sems_of, here.at_row(dest))

    def give_pair(kind):
        sems_of = pair_send.at[kind], pair_recv.at[kind]
        return remote(pair_out.at[kind], pair_in.at[kind], *sems_of, here.other_core())

    for step in range(1, 4):
        give_back(step, 0).start()
    d_heads[row, 0] = head_give[0, row]

    @pl.when(core == 1)
    def _():
        for kind, gradient in enumerate((d_keys, d_values)):
            pair_out[kind] = gradient[pl.ds(0, group_tok)].astype(BF16)
            give_pair(kind).start()
        for kind, gradient in enumerate((d_keys, d_values)):
            for part in range(4):
                at = pl.ds(group_tok + part * row_tok, row_tok)
                head_give[kind + 1, part] = gradient[at].astype(BF16)

    from_inside(2)
    plane_part(3)
    pair_sum.step(3)

    @pl.when(core == 0)
    def _():
        for kind, gradient in enumerate((d_keys, d_values)):
            give_pair(kind).wait_recv()
            for part in range(4):
                at = pl.ds(part * row_tok, row_tok)
                summed = gradient[at] + pair_in[kind, at].astype(F32)
                head_give[kind + 1, part] = summed.astype(BF16)

    for kind in (1, 2):
        for step in range(1, 4):
            give_back(step, kind).start()
        d_heads[row, kind] = head_give[kind, row]
    pair_sum.step(4)
    pair_sum.step(5)
    collect.own_step()
    out_total[...] = collect.mine[0, col]
    for source in here.rows[1:]:
        for kind in range(3):
            arrived(d_heads.at[source, kind], back_recv.at[kind, source])
    for step in range(1, 4):
        give_near(step).wait_send()
        give_head(step).wait_send()
        for kind in range(3):
            give_back(step, kind).wait_send()

    @pl.when(core == 1)
    def _():
        for kind in range(2):
            give_pair(kind).wait_send()

    pair_sum.finish()
    spread.finish()
    collect.finish()


def attend_back_stage(
    d_attn, query, keys, values, mixed, total, cuts, out_weights, out_parts, early, scale, collective_id
):
    rows, width = d_attn.shape
    row_tok, group_tok = 4 * rows, 16 * rows
    vmem, hbm = pl.BlockSpec(memory_space=pltpu.VMEM), pl.BlockSpec(memory_space=pl.ANY)
    dma = pltpu.SemaphoreType.DMA
    return pl.pallas_call(
        functools.partial(back_kernel, scale),
        in_specs=[pl.BlockSpec(memory_space=pltpu.SMEM)] + [vmem] * 6 + [hbm] * 2 + [vmem],
        out_specs=[vmem] * 4,
        out_shape=[
            jax.ShapeDtypeStruct((row_tok, width), BF16),
            jax.ShapeDtypeStruct((4, 3, row_tok, HD), BF16),
            jax.ShapeDtypeStruct((rows, width), BF16),
            jax.ShapeDtypeStruct(early.shape, F32),
        ],
        scratch_shapes=[
            pltpu.VMEM((width, width), BF16),
            pltpu.VMEM((4, rows, 4 * HD), BF16),
            pltpu.VMEM((4, rows, 4 * HD), BF16),
            pltpu.VMEM((4, 4, rows, HD), BF16),
            pltpu.VMEM((HD, 2 * group_tok), BF16),
            pltpu.VMEM((2 * group_tok, HD), F32),
            pltpu.VMEM((2 * group_tok, HD), F32),
            pltpu.VMEM((HD, row_tok), F32),
            pltpu.VMEM((2, group_tok, HD), BF16),
            pltpu.VMEM((2, group_tok, HD), BF16),
            pltpu.VMEM((3, 4, row_tok, HD), BF16),
        ]
        + pair_sum_buffers(*early.shape)
        + [
            dma, dma((4, 4)), dma((4,)), dma((4,)), dma((4,)), dma((4,)),
            dma((4, 3)), dma((3, 4)), dma((2,)), dma((2,)),
        ]
        + collect_buffers(rows, width)
        + COLLECT_SEMS
        + SPREAD_SEMS,
        compiler_params=pltpu.CompilerParams(
            collective_id=collective_id, has_side_effects=True, vmem_limit_bytes=58 * 2**20
        ),
    )(cuts[None], d_attn, query, keys, values, mixed, total, out_weights, out_parts, early)


def tail_kernel(
    d_heads, qkv, totals, q_gain, k_gain, cosine, sine, weights, normed, mixed_rows, d_attn,
    hidden, gain, d_middle,
    grad_hidden, grad_qkv, grad_out, late_sum,
    d_qkv, late, grads, mixed, units, stat, scales, sums, sum_held, sum_got, sum_send, sum_recv,
    stat_send, stat_recv,
    line, line_in, whole, give, other, plane, corner_one, corner_two, from_across, from_along,
    up_send, down_send, line_recv, other_send, other_recv,
    one_send, one_recv, two_send, two_recv, across_send, across_recv, along_send, along_recv,
    back_send, back_recv,
):
    here = Here()
    row, col, core = here.row, here.col, here.core
    rows = hidden.shape[0]
    depth, columns = grads.shape
    part = depth // 2
    first, second = pl.ds(0, part // 2), pl.ds(part // 2, part // 2)
    order = here.near_first[::-1]
    qkv_columns = d_qkv.shape[1]
    tile = 512

    def line_products():
        @pl.loop(0, weights.shape[0] // tile)
        def _(index):
            at = pl.ds(pl.multiple_of(index * tile, tile), tile)
            product = contract_cols(d_qkv[...], weights[at]).astype(BF16)
            line[:, :, at] = product.reshape(4, rows, tile)

    def give_up(place):
        sems = up_send.at[place], line_recv.at[place]
        return remote(line.at[place], line_in.at[place], *sems, here.at_col(col + 1))

    def give_down(place, slot):
        sems = down_send.at[place], line_recv.at[slot]
        return remote(line.at[place], line_in.at[slot], *sems, here.at_col(col - 1))

    def line_step(place):
        @pl.when((place > col) & (col > 0))
        def _():
            give_up(place).wait_recv()
            add_into(line.at[place], line_in.at[place])

        @pl.when((place < col) & (col < 3))
        def _():
            give_down(place, place).wait_recv()
            add_into(line.at[place], line_in.at[place])

        @pl.when(place > col)
        def _():
            give_up(place).start()

        @pl.when(place < col - 1)
        def _():
            give_down(place, place).start()

        @pl.when(place == col - 1)
        def _():
            give_down(place, 4).start()

    def row_product(which):
        of_row = here.rows[which]
        at = pl.ds(pl.multiple_of(of_row * depth, depth), depth)
        whole[:, pl.ds(0, qkv_columns)] = transposed_product(normed[:, at], d_qkv[...]).astype(BF16)
        whole[:, pl.ds(qkv_columns, columns - qkv_columns)] = transposed_product(
            mixed[...], d_attn[:, at]
        ).astype(BF16)
        plane[which] = whole[pl.ds(pl.multiple_of(core * part, part), part)]
        give[which] = whole[pl.ds(pl.multiple_of((1 - core) * part, part), part)]
        to_core(which).start()

    def to_core(which):
        sems = other_send.at[which], other_recv.at[which]
        return remote(give.at[which], other.at[which], *sems, here.other_core())

    def own_sum(which):
        to_core(which).wait_recv()
        add_into(plane.at[which], other.at[which])

    give_one = remote(
        plane.at[3, first], corner_one, one_send, one_recv, here.at_row(here.across)
    )
    give_two = remote(
        plane.at[3, second], corner_two, two_send, two_recv, here.at_row(here.along)
    )

    def give_across(index):
        at = (first, second)[index]
        sems = across_send.at[index], across_recv.at[index]
        return remote(plane.at[1, at], from_across.at[at], *sems, here.at_row(here.across))

    def give_along(index):
        at = (first, second)[index]
        sems = along_send.at[index], along_recv.at[index]
        return remote(plane.at[2, at], from_along.at[at], *sems, here.at_row(here.along))

    pair_sum = PairSum(here, late, late_sum, sum_held, sum_got, sum_send, sum_recv)
    greet(here.plane_peers() + here.line_peers() + [here.other_core()])

    width = hidden.shape[1]
    heads = d_heads.shape[0]
    row_tok = d_qkv.shape[0]
    late[...] = jnp.zeros_like(late)
    for kind in range(2):
        root = lax.rsqrt(totals[kind : kind + 1] / width + EPSILON)
        scales[kind] = jnp.broadcast_to(root, (HD, row_tok)).T
        square = jnp.zeros((row_tok, HD), F32)
        for head in range(heads):
            start = (head * 3 + kind) * HD
            raw = qkv[:, start : start + HD]
            given = d_heads[head, kind].astype(F32)
            unit = given * cosine[...] + pltpu.roll(given * sine[...], HD // 2, 1)
            gains = (q_gain, k_gain)[kind][:, head * HD : (head + 1) * HD]
            gain_sum = jnp.sum(unit * raw * scales[kind], axis=0, keepdims=True)
            place = pl.ds(pl.multiple_of((col * heads + head) * HD, HD), HD)
            late[kind + 1 : kind + 2, place] = gain_sum
            weighted = unit * gains
            square = square + weighted * raw
            units[kind, head] = weighted
        stat[col, kind : kind + 1] = jnp.sum(square.T, axis=0, keepdims=True)

    def give_stat(step):
        peer = here.line_peers()[step]
        return remote(stat.at[col], stat.at[col], stat_send.at[step], stat_recv.at[col], peer)

    for step in range(3):
        give_stat(step).start()
    for head in range(heads):
        d_qkv[:, (head * 3 + 2) * HD : (head * 3 + 3) * HD] = d_heads[head, 2]
        mixed[:, head * HD : (head + 1) * HD] = mixed_rows[head]
    for step in range(3):
        place = (col + step + 1) % 4
        arrived(stat.at[place], stat_recv.at[place])
    total = stat[0] + stat[1] + stat[2] + stat[3]
    for kind in range(2):
        sums[...] = jnp.broadcast_to(total[kind : kind + 1] / width, (HD, row_tok)).T
        for head in range(heads):
            start = (head * 3 + kind) * HD
            raw = qkv[:, start : start + HD]
            root = scales[kind]
            d_raw = root * units[kind, head] - raw * (root * root * root) * sums[...]
            d_qkv[:, start : start + HD] = d_raw.astype(BF16)
    ends = (col == 0) | (col == 3)
    line_products()

    @pl.when(ends)
    def _():
        for place in order[:3]:
            line_step(place)

    def inner_step(place):
        @pl.when(jnp.logical_not(ends))
        def _():
            line_step(place)

    row_product(3)
    row_product(1)
    inner_step(order[0])
    own_sum(3)
    give_one.start()
    give_two.start()
    row_product(2)
    own_sum(1)
    give_across(0).start()
    own_sum(2)
    give_along(1).start()
    inner_step(order[1])
    row_product(0)
    inner_step(order[2])
    give_two.wait_recv()
    add_into(plane.at[1, second], corner_two)
    give_across(1).start()
    give_one.wait_recv()
    add_into(plane.at[2, first], corner_one)
    give_along(0).start()
    own_sum(0)

    @pl.when(col > 0)
    def _():
        give_up(col).wait_recv()
        add_into(line.at[col], line_in.at[col])

    @pl.when(col < 3)
    def _():
        give_down(col, 4).wait_recv()
        add_into(line.at[col], line_in.at[4])

    given = line[col].astype(F32)
    tokens = hidden[...].astype(F32)
    root = lax.rsqrt(jnp.mean(tokens * tokens, axis=1, keepdims=True) + EPSILON)
    late[0:1] = jnp.sum(given * tokens * root, axis=0, keepdims=True)
    pair_sum.begin()
    weighted = given * gain[...].astype(F32)
    inner = jnp.mean(weighted * tokens, axis=1, keepdims=True)
    grad_hidden[...] = d_middle[...] + root * weighted - tokens * (root * root * root) * inner
    pair_sum.step(0)
    for index in range(2):
        give_across(index).wait_recv()
        give_along(index).wait_recv()
    add_into(plane.at[0], from_across, from_along)
    pair_sum.step(1)
    own_half = pl.ds(pl.multiple_of(core * part, part), part)
    give_back = remote(
        plane.at[0], grads.at[own_half], back_send, back_recv, here.other_core()
    )
    give_back.start()
    grads[own_half] = plane[0]
    other_half = grads.at[pl.ds(pl.multiple_of((1 - core) * part, part), part)]
    pair_sum.step(2)
    arrived(other_half, back_recv)
    grad_qkv[...] = grads[:, pl.ds(0, qkv_columns)].astype(F32)
    grad_out[...] = grads[:, pl.ds(qkv_columns, columns - qkv_columns)].astype(F32)
    for index in (3, 4, 5):
        pair_sum.step(index)
    pair_sum.finish()
    for step in range(3):
        give_stat(step).wait_send()
    give_back.wait_send()
    give_one.wait_send()
    give_two.wait_send()
    for index in range(2):
        give_across(index).wait_send()
        give_along(index).wait_send()
    for which in range(4):
        to_core(which).wait_send()
    for place in order:

        @pl.when(place > col)
        def _():
            give_up(place).wait_send()

        @pl.when(place < col)
        def _():
            give_down(place, place).wait_send()


def tail_stage(
    d_heads, qkv, totals, q_gain, k_gain, cosine, sine, weights, normed, mixed_rows, d_attn,
    hidden, gain, d_middle, collective_id,
):
    row_tok, qkv_columns = qkv.shape
    rows, width = hidden.shape
    depth = width // 4
    out_columns = width // 4
    columns = qkv_columns + out_columns
    part = depth // 2
    heads = d_heads.shape[0]
    vmem = pl.BlockSpec(memory_space=pltpu.VMEM)
    one, four = pltpu.SemaphoreType.DMA, pltpu.SemaphoreType.DMA((4,))
    two, five = pltpu.SemaphoreType.DMA((2,)), pltpu.SemaphoreType.DMA((5,))
    three = pltpu.SemaphoreType.DMA((3,))
    return pl.pallas_call(
        tail_kernel,
        in_specs=[vmem] * 14,
        out_specs=[vmem] * 4,
        out_shape=[
            jax.ShapeDtypeStruct((rows, width), F32),
            jax.ShapeDtypeStruct((depth, qkv_columns), F32),
            jax.ShapeDtypeStruct((depth, out_columns), F32),
            jax.ShapeDtypeStruct((8, width), F32),
        ],
        scratch_shapes=[
            pltpu.VMEM((row_tok, qkv_columns), BF16),
            pltpu.VMEM((8, width), F32),
            pltpu.VMEM((depth, columns), BF16),
            pltpu.VMEM((row_tok, heads * HD), BF16),
            pltpu.VMEM((2, heads, row_tok, HD), F32),
            pltpu.VMEM((4, 8, row_tok), F32),
            pltpu.VMEM((2, row_tok, HD), F32),
            pltpu.VMEM((row_tok, HD), F32),
        ]
        + pair_sum_buffers(8, width)
        + [
            three, four,
            pltpu.VMEM((4, rows, width), BF16),
            pltpu.VMEM((5, rows, width), BF16),
            pltpu.VMEM((depth, columns), BF16),
            pltpu.VMEM((4, part, columns), BF16),
            pltpu.VMEM((4, part, columns), BF16),
            pltpu.VMEM((4, part, columns), BF16),
            pltpu.VMEM((part // 2, columns), BF16),
            pltpu.VMEM((part // 2, columns), BF16),
            pltpu.VMEM((part, columns), BF16),
            pltpu.VMEM((part, columns), BF16),
            four, four, five, four, four,
            one, one, one, one, two, two, two, two,
            one, one,
        ],
        compiler_params=pltpu.CompilerParams(
            collective_id=collective_id, has_side_effects=True, vmem_limit_bytes=58 * 2**20
        ),
    )(
        d_heads, qkv, totals, q_gain, k_gain, cosine, sine, weights, normed, mixed_rows, d_attn,
        hidden, gain[None], d_middle,
    )


def expert_rows(rows, grads, gate, gate_w, up_w, down_w):
    pre_gate = matmul(rows, gate_w)
    pre_up = matmul(rows, up_w)
    back = contract_cols(grads, down_w)
    sigmoid_gate = jax.nn.sigmoid(pre_gate)
    silu_gate = pre_gate * sigmoid_gate
    hidden = (silu_gate * pre_up).astype(BF16)
    inner = jnp.sum(hidden.astype(F32) * back, axis=-1)
    weighted = (hidden.astype(F32) * gate).astype(BF16)
    d_hid = back * gate
    d_pregate = (d_hid * pre_up * (sigmoid_gate + silu_gate * (1.0 - sigmoid_gate))).astype(BF16)
    d_preup = (d_hid * silu_gate).astype(BF16)
    outputs = matmul(weighted, down_w).astype(BF16)
    d_rows = (contract_cols(d_pregate, gate_w) + contract_cols(d_preup, up_w)).astype(BF16)
    return (
        outputs,
        d_rows,
        inner,
        contract_rows(rows, d_pregate),
        contract_rows(rows, d_preup),
        contract_rows(weighted, grads),
    )


def experts(normed, grads, dense_gates, gate_w, up_w, down_w):
    rows_dev, width = normed.shape
    devices = math.prod(lax.axis_size(axis) for axis in ALL)
    expert_count = dense_gates.shape[1]
    expert = lax.axis_index(ALL) // 2
    parts = max(1, lax.axis_size("exp") // 2)
    step = rows_dev // parts

    def one_part(sums, piece):
        rows, grad_rows, gates = piece
        rows_all = lax.all_gather(rows, ALL, axis=0, tiled=True)
        grads_all = lax.all_gather(grad_rows, ALL, axis=0, tiled=True)
        gates_all = lax.all_gather(gates, ALL, axis=0, tiled=True)
        gate = lax.dynamic_slice_in_dim(gates_all, expert, 1, 1)
        got = expert_rows(rows_all, grads_all, gate, gate_w, up_w, down_w)
        outputs = lax.psum_scatter(got[0], ALL, scatter_dimension=0, tiled=True)
        d_rows = lax.psum_scatter(got[1], ALL, scatter_dimension=0, tiled=True)
        inner = lax.all_to_all(
            got[2].reshape(devices, step), ALL, split_axis=0, concat_axis=0, tiled=True
        )
        inner = inner.reshape(expert_count, 2, step).sum(axis=1).T
        sums = got[3:] if sums is None else tuple(a + b for a, b in zip(sums, got[3:]))
        return sums, (outputs, d_rows, inner)

    if parts == 1:
        sums, (outputs, d_rows, inner) = one_part(None, (normed, grads, dense_gates))
    else:
        start = tuple(jnp.zeros(w.shape, F32) for w in (gate_w, up_w, down_w))
        pieces = tuple(v.reshape(parts, step, -1) for v in (normed, grads, dense_gates))
        sums, got = lax.scan(one_part, start, pieces)
        outputs, d_rows, inner = (v.reshape(rows_dev, -1) for v in got)
    return outputs.astype(F32), d_rows.astype(F32), inner, sums


def experts_here(normed, grads_all, picks, router, halves, others):
    numbers = jnp.arange(router.shape[1], dtype=jnp.int32)
    mask = jnp.any(picks.T[None] == numbers[:, None, None], axis=1).astype(F32)
    out_parts, d_rows, inner, weights = expert_stage(
        normed, grads_all, mask, halves, others, router, 1
    )
    inner = inner[:, :, 0].reshape(router.shape[1], -1).T
    return out_parts, d_rows.astype(F32), inner, weights


def shards(
    hidden_in,
    out_grad,
    attn_gain,
    w_qkv,
    q_gain,
    k_gain,
    w_out,
    moe_gain,
    router,
    w_gate,
    w_up,
    w_down,
    routes,
    doc_cuts,
):
    row_count, col_count = lax.axis_size("row"), lax.axis_size("col")
    tokens = hidden_in[0].astype(F32)
    rows_dev, width = tokens.shape
    heads = w_qkv.shape[1] // (3 * HD)
    plane = heads * HD
    scale = HD ** (-0.5)
    side = lax.axis_index("exp") % 2
    row_tok = rows_dev * col_count
    group_tok = row_tok * row_count
    cuts = lax.dynamic_index_in_dim(doc_cuts, lax.axis_index("exp") // 2, 0, keepdims=False)

    here = (row_count, col_count, lax.axis_size("exp")) == (4, 4, 2)

    if here:
        other_w = [lax.ppermute(w[0], "exp", [(0, 1), (1, 0)]) for w in (w_gate, w_up, w_down)]

    gain_one = attn_gain.astype(F32)
    scale_one = rms_scale(tokens)
    head_start = lax.axis_index("col") * plane
    gain_q = lax.dynamic_slice_in_dim(q_gain, head_start, plane, 0).astype(F32)
    gain_k = lax.dynamic_slice_in_dim(k_gain, head_start, plane, 0).astype(F32)
    row_places = side * group_tok + lax.axis_index("row") * row_tok + jnp.arange(row_tok, dtype=jnp.int32)
    unused_doc, position = doc_positions(row_places, cuts)
    cosine, sine = rope_tables(position, HD)
    if here:
        signed = jnp.concatenate([-sine[:, : HD // 2], sine[:, HD // 2 :]], axis=1)
        normed_row, qkv_w, qkv, totals, query, keys, values, grads_all = project(
            hidden_in[0], attn_gain, w_qkv, gain_q[None], gain_k[None], cosine, signed, out_grad[0], 0
        )
        total_q, total_k = totals[0], totals[1]
        query = query.reshape(group_tok, HD)
        key_all, value_all = keys.reshape(-1, HD), values.reshape(-1, HD)
    else:
        normed_one = (tokens * scale_one * gain_one).astype(BF16)
        normed_row = lax.all_gather(normed_one, "col", axis=0, tiled=True)
        qkv_w = lax.all_gather(w_qkv, "row", axis=0, tiled=True)
        out_w = lax.all_gather(
            lax.all_gather(w_out, "row", axis=1, tiled=True), "col", axis=0, tiled=True
        )
        qkv = matmul(normed_row, qkv_w)
    qkv = qkv.reshape(row_tok, heads, 3, HD)
    query_raw, key_raw, value_raw = qkv[:, :, 0], qkv[:, :, 1], qkv[:, :, 2]
    if not here:
        total_q, total_k = lax.psum(
            (jnp.sum(query_raw * query_raw, axis=(1, 2)), jnp.sum(key_raw * key_raw, axis=(1, 2))),
            "col",
        )
    scale_q = lax.rsqrt(total_q / width + EPSILON)[:, None, None]
    scale_k = lax.rsqrt(total_k / width + EPSILON)[:, None, None]
    gain_q, gain_k = gain_q.reshape(heads, HD), gain_k.reshape(heads, HD)
    cosine, sine = cosine[:, None, :], sine[:, None, :]
    if not here:
        query = rotate(query_raw * scale_q * gain_q, cosine, sine).astype(BF16)
        key = rotate(key_raw * scale_k * gain_k, cosine, sine).astype(BF16)
        moved = rows_to_heads(jnp.concatenate([query, key, value_raw.astype(BF16)], axis=-1))
        query, own_pair = moved[:, :HD], moved[:, HD:]
        earlier_pair = from_behind(own_pair, "exp", 1)
        lower_pair = jnp.where(side == 0, own_pair, earlier_pair)
        upper_pair = jnp.where(side == 0, jnp.zeros_like(own_pair), own_pair)
        key_value = jnp.concatenate([lower_pair, upper_pair], axis=0)
        key_all, value_all = key_value[:, :HD], key_value[:, HD:]

    if here:
        mixed_wide, total, out_w, mixed_rows, middle, normed_two, grads_all = attention_stage(
            query, key_all, value_all, cuts, w_out, hidden_in[0], moe_gain, grads_all, scale, 4
        )
    else:
        mixed_wide, total = attend(query, key_all, value_all, cuts, scale)
        mixed = mixed_wide.astype(BF16)
        middle = tokens + matmul(heads_to_tokens(mixed), out_w)

    gain_two = moe_gain.astype(F32)
    scale_two = rms_scale(middle)
    if not here:
        normed_two = (middle * scale_two * gain_two).astype(BF16)
    gates_all = jax.nn.softmax(matmul(normed_two, router), axis=-1)
    picks = routes[0]
    chosen = jnp.any(
        picks[:, :, None] == jnp.arange(router.shape[1], dtype=jnp.int32)[None, None, :], axis=1
    )
    grad_out = out_grad[0].astype(F32)
    expert_w = (w_gate[0], w_up[0], w_down[0])
    if here:
        out_parts, d_normed_two, inner, weight_grads = experts_here(
            normed_two, grads_all, picks, router, expert_w, other_w
        )
    else:
        dense_gates = jnp.where(chosen, gates_all, 0.0)
        mixture, d_normed_two, inner, weight_grads = experts(
            normed_two, out_grad[0], dense_gates, *expert_w
        )
    dense = jnp.where(chosen, inner, 0.0)
    d_logits = (gates_all * (dense - jnp.sum(gates_all * dense, axis=-1, keepdims=True))).astype(BF16)
    grad_router = contract_rows(d_logits, normed_two)
    d_normed_two = d_normed_two + contract_cols(d_logits, router)
    grad_moe_gain = jnp.sum(d_normed_two * middle * scale_two, axis=0)
    weighted_two = d_normed_two * gain_two
    d_middle = (
        grad_out
        + scale_two * weighted_two
        - middle * scale_two**3 * jnp.mean(weighted_two * middle, axis=-1, keepdims=True)
    )

    d_attn = d_middle.astype(BF16)
    if here:
        early = jnp.concatenate([grad_moe_gain[None], jnp.zeros((7, width), F32), grad_router])
        d_attn_row, d_heads, mixture, early = attend_back_stage(
            d_attn, query, key_all, value_all, mixed_wide, total, cuts, out_w, out_parts, early, scale, 2
        )
        grad_hidden, grad_qkv, grad_w_out, late = tail_stage(
            d_heads, qkv.reshape(row_tok, -1), totals, gain_q.reshape(1, -1), gain_k.reshape(1, -1),
            cosine[:, 0], signed, qkv_w, normed_row, mixed_rows, d_attn_row,
            hidden_in[0], attn_gain, d_middle, 3,
        )
        final = middle + mixture.astype(F32)
        summed = (late[0], late[1], late[2], early[0], early[8:])
    else:
        final = middle + mixture
        mixed_row = heads_to_rows(mixed).reshape(row_tok, plane)
        d_mixed = tokens_to_heads(contract_cols(d_attn, out_w).astype(BF16))
        d_attn_row = lax.all_gather(d_attn, "col", axis=0, tiled=True)
        d_query, acc_key, acc_value = attend_back(
            query, key_all, value_all, d_mixed, mixed_wide, total, cuts, scale
        )
        accumulated = jnp.concatenate([acc_key, acc_value], axis=1)
        lower_acc, upper_acc = accumulated[:group_tok], accumulated[group_tok:]
        kept_acc = jnp.where(side == 0, lower_acc, upper_acc)
        later_acc = from_behind(lower_acc.astype(BF16), "exp", -1).astype(F32)
        summed_pair = kept_acc + jnp.where(side == 0, later_acc, jnp.zeros_like(later_acc))
        d_heads = heads_to_rows(jnp.concatenate([d_query, summed_pair], axis=1).astype(BF16)).astype(F32)
        d_q_unit = rotate_back(d_heads[:, :, :HD], cosine, sine)
        d_k_unit = rotate_back(d_heads[:, :, HD : 2 * HD], cosine, sine)
        d_value = d_heads[:, :, 2 * HD :]
        weighted_q = d_q_unit * gain_q
        weighted_k = d_k_unit * gain_k
        sum_q, sum_k = lax.psum(
            (jnp.sum(weighted_q * query_raw, axis=(1, 2)), jnp.sum(weighted_k * key_raw, axis=(1, 2))),
            "col",
        )
        d_query_raw = scale_q * weighted_q - query_raw * scale_q**3 * (sum_q / width)[:, None, None]
        d_key_raw = scale_k * weighted_k - key_raw * scale_k**3 * (sum_k / width)[:, None, None]
        grad_q_part = jnp.sum(d_q_unit * query_raw * scale_q, axis=0).reshape(plane)
        grad_k_part = jnp.sum(d_k_unit * key_raw * scale_k, axis=0).reshape(plane)
        d_qkv = jnp.concatenate([d_query_raw, d_key_raw, d_value], axis=2).astype(BF16)
        d_qkv = d_qkv.reshape(row_tok, heads * 3 * HD)
        d_normed_one = lax.psum_scatter(
            contract_cols(d_qkv, qkv_w).astype(BF16), "col", scatter_dimension=0, tiled=True
        ).astype(F32)
        grad_qkv = lax.psum_scatter(
            contract_rows(normed_row, d_qkv).astype(BF16), "row", scatter_dimension=0, tiled=True
        )
        grad_w_out = lax.psum_scatter(
            contract_rows(mixed_row, d_attn_row).astype(BF16), "row", scatter_dimension=1, tiled=True
        )
        grad_qkv = lax.psum(grad_qkv, "exp").astype(F32)
        grad_w_out = lax.psum(grad_w_out, "exp").astype(F32)
        grad_attn_gain = jnp.sum(d_normed_one * tokens * scale_one, axis=0)
        weighted_one = d_normed_one * gain_one
        grad_hidden = (
            d_middle
            + scale_one * weighted_one
            - tokens * scale_one**3 * jnp.mean(weighted_one * tokens, axis=-1, keepdims=True)
        )
        empty = jnp.zeros((width,), F32)
        grad_q_full = lax.dynamic_update_slice_in_dim(empty, grad_q_part, head_start, 0)
        grad_k_full = lax.dynamic_update_slice_in_dim(empty, grad_k_part, head_start, 0)
        parts = (grad_attn_gain, grad_q_full, grad_k_full, grad_moe_gain)
        summed = lax.psum(parts + (grad_router,), ALL)
    return (
        final.astype(BF16)[None],
        grad_hidden[None],
        summed[0],
        grad_qkv,
        summed[1],
        summed[2],
        grad_w_out,
        summed[3],
        summed[4].T,
        weight_grads[0][None],
        weight_grads[1][None],
        weight_grads[2][None],
    )


def solution(mesh):
    token_spec = P("exp", ("row", "col"), None)
    expert_spec = P(("row", "col", "exp"), None, None)
    in_specs = (
        token_spec,
        token_spec,
        P(),
        P("row", "col"),
        P(),
        P(),
        P("col", "row"),
        P(),
        P(),
        expert_spec,
        expert_spec,
        expert_spec,
        token_spec,
        P(),
    )
    out_specs = (
        token_spec,
        token_spec,
        P(),
        P("row", "col"),
        P(),
        P(),
        P("col", "row"),
        P(),
        P(),
        expert_spec,
        expert_spec,
        expert_spec,
    )
    return jax.shard_map(shards, mesh=mesh, in_specs=in_specs, out_specs=out_specs, check_vma=False)
```

```python
import functools
import math

import jax
import jax.numpy as jnp
from jax import lax
from jax.experimental import pallas as pl
from jax.experimental.pallas import tpu as pltpu
from jax.sharding import PartitionSpec as P

HD = 128
EPSILON = 1e-05
ROPE_BASE = 10000.0
MASKED = -1e30
BF16 = jnp.bfloat16
F32 = jnp.float32


def matmul(left, right):
    return jnp.dot(left, right, preferred_element_type=F32)


def contract_rows(left, right):
    return lax.dot_general(left, right, (((0,), (0,)), ((), ())), preferred_element_type=F32)


def contract_cols(left, right):
    return lax.dot_general(left, right, (((1,), (1,)), ((), ())), preferred_element_type=F32)


def rms_scale(values):
    return lax.rsqrt(jnp.mean(values * values, axis=-1, keepdims=True) + EPSILON)


def rope_tables(position, width):
    frequency = ROPE_BASE ** (-jnp.arange(0, width, 2, dtype=F32) / width)
    angle = position.astype(F32)[:, None] * frequency[None, :]
    return (
        jnp.concatenate([jnp.cos(angle)] * 2, axis=-1),
        jnp.concatenate([jnp.sin(angle)] * 2, axis=-1),
    )


def rotate(values, cosine, sine):
    half = values.shape[-1] // 2
    turned = jnp.concatenate([-values[..., half:], values[..., :half]], axis=-1)
    return values * cosine + turned * sine


def rotate_back(values, cosine, sine):
    half = values.shape[-1] // 2
    turned = values * sine
    return values * cosine + jnp.concatenate([turned[..., half:], -turned[..., :half]], axis=-1)


def doc_positions(places, cuts):
    first = (places >= cuts[0]).astype(jnp.int32)
    second = (places >= cuts[1]).astype(jnp.int32)
    start = first * cuts[0] + second * (cuts[1] - cuts[0])
    return (first + second, places - start)


def from_behind(value, axis, steps):
    count = lax.axis_size(axis)
    initial, last = (max(0, -steps), min(count, count - steps))
    return lax.ppermute(value, axis, [(source, source + steps) for source in range(initial, last)])


def rows_to_heads(values):
    count = lax.axis_size("row")
    rows, heads, width = values.shape
    moved = lax.all_to_all(values.transpose(1, 0, 2), "row", split_axis=0, concat_axis=0, tiled=True)
    return moved.reshape(count * rows, width)


def heads_to_rows(values):
    count = lax.axis_size("row")
    rows, width = values.shape
    moved = lax.all_to_all(
        values.reshape(count, rows // count, width), "row", split_axis=0, concat_axis=0, tiled=True
    )
    return moved.transpose(1, 0, 2)


def heads_to_tokens(values):
    row_count, col_count = lax.axis_size("row"), lax.axis_size("col")
    rows = values.shape[0] // (row_count * col_count)
    moved = lax.all_to_all(
        values.reshape(row_count * col_count, rows, HD),
        ("row", "col"),
        split_axis=0,
        concat_axis=0,
        tiled=True,
    )
    moved = moved.reshape(row_count, col_count, rows, HD).transpose(2, 1, 0, 3)
    return moved.reshape(rows, row_count * col_count * HD)


def tokens_to_heads(values):
    row_count, col_count = lax.axis_size("row"), lax.axis_size("col")
    rows = values.shape[0]
    parted = values.reshape(rows, col_count, row_count, HD).transpose(2, 1, 0, 3)
    moved = lax.all_to_all(
        parted.reshape(row_count * col_count, rows, HD),
        ("row", "col"),
        split_axis=0,
        concat_axis=0,
        tiled=True,
    )
    return moved.reshape(row_count * col_count * rows, HD)


MESH = pl.DeviceIdType.MESH
ALL = ("row", "col", "exp")


class Here:
    def __init__(self):
        self.row, self.col, self.core = (lax.axis_index(axis) for axis in ALL)
        self.across = self.row + 1 - 2 * (self.row % 2)
        self.along = (self.row + 2) % 4
        self.opposite = 3 - self.row
        self.rows = (self.row, self.across, self.along, self.opposite)
        half = self.col // 2
        self.near_first = [
            self.col,
            1 + self.col % 2,
            2 - self.col - self.col % 2 + 3 * half,
            3 - 3 * half,
        ]

    def at_row(self, row):
        return (row, self.col, self.core)

    def at_col(self, col):
        return (self.row, col, self.core)

    def other_core(self):
        return (self.row, self.col, 1 - self.core)

    def line_peers(self):
        return [self.at_col((self.col + step) % 4) for step in (1, 2, 3)]

    def group_peers(self):
        steps = range(1, 16)
        return [((self.row + s // 4) % 4, (self.col + s) % 4, self.core) for s in steps]

    def plane_peers(self):
        return [self.at_row(row) for row in self.rows[1:]]


def greet(peers):
    barrier = pltpu.get_barrier_semaphore()
    for peer in peers:
        pl.semaphore_signal(barrier, inc=1, device_id=peer, device_id_type=MESH)
    pl.semaphore_wait(barrier, len(peers))


def greet_near(here):
    barrier = pltpu.get_barrier_semaphore()
    col = here.col

    def signal(peer):
        pl.semaphore_signal(barrier, inc=1, device_id=peer, device_id_type=MESH)

    for peer in (here.other_core(), here.at_row(here.across), here.at_row(here.along)):
        signal(peer)

    @pl.when(col > 0)
    def _():
        signal(here.at_col(col - 1))

    @pl.when(col < 3)
    def _():
        signal(here.at_col(col + 1))

    pl.semaphore_wait(barrier, 3 + (col + 3) // 4 + (6 - col) // 4)


def remote(source, target, send, recv, device):
    return pltpu.make_async_remote_copy(
        src_ref=source,
        dst_ref=target,
        send_sem=send,
        recv_sem=recv,
        device_id=device,
        device_id_type=MESH,
    )


def arrived(target, recv):
    pltpu.make_async_copy(target, target, recv).wait()


def add_into(target, *terms):
    step = 16

    @pl.loop(0, target.shape[0] // step)
    def _(index):
        part = pl.ds(pl.multiple_of(index * step, step), step)
        value = target[part].astype(F32)
        for term in terms:
            value = value + term[part].astype(F32)
        target[part] = value.astype(target.dtype)


SPREAD_SEMS = [pltpu.SemaphoreType.DMA((4,))] * 11 + [pltpu.SemaphoreType.DMA((4, 4))] * 2


class Spread:
    def __init__(self, here, own, block, rows, sems, line=True, plane=True, core=True):
        self.here, self.own, self.block = here, own, block
        self.line, self.plane, self.core = line, plane, core
        (
            self.up_send, self.down_send, self.line_recv,
            self.across_send, self.across_recv, self.along_send, self.along_recv,
            self.one_send, self.one_recv, self.two_send, self.two_recv,
            self.core_send, self.core_recv,
        ) = sems
        self.first, self.second = pl.ds(0, rows // 2), pl.ds(rows // 2, rows // 2)
        self.order = here.near_first if line else [0]
        self.steps = len(self.order)

    def held(self, step):
        here = self.here
        return self.own if step == 0 else self.block(here.row, self.order[step], here.core)

    def up(self, step):
        here, place = self.here, self.order[step]
        target = self.block(here.row, place, here.core)
        recv = self.line_recv.at[place]
        return remote(self.held(step), target, self.up_send.at[place], recv, here.at_col(here.col + 1))

    def down(self, step):
        here, place = self.here, self.order[step]
        target = self.block(here.row, place, here.core)
        recv = self.line_recv.at[place]
        return remote(self.held(step), target, self.down_send.at[place], recv, here.at_col(here.col - 1))

    def to_across(self, step):
        here, place = self.here, self.order[step]
        target = self.block(here.row, place, here.core)
        sems = self.across_send.at[place], self.across_recv.at[place]
        return remote(self.held(step), target, *sems, here.at_row(here.across))

    def to_along(self, step):
        here, place = self.here, self.order[step]
        target = self.block(here.row, place, here.core)
        sems = self.along_send.at[place], self.along_recv.at[place]
        return remote(self.held(step), target, *sems, here.at_row(here.along))

    def corner_one(self, step):
        here, place = self.here, self.order[step]
        part = self.block(here.across, place, here.core).at[self.first]
        sems = self.one_send.at[place], self.one_recv.at[place]
        return remote(part, part, *sems, here.at_row(here.along))

    def corner_two(self, step):
        here, place = self.here, self.order[step]
        part = self.block(here.along, place, here.core).at[self.second]
        sems = self.two_send.at[place], self.two_recv.at[place]
        return remote(part, part, *sems, here.at_row(here.across))

    def to_core(self, which, step):
        here, place = self.here, self.order[step]
        target = self.block(here.rows[which], place, here.core)
        source = self.held(step) if which == 0 else target
        sems = self.core_send.at[which, place], self.core_recv.at[which, place]
        return remote(source, target, *sems, here.other_core())

    def line_step(self, step):
        here, place = self.here, self.order[step]
        if step > 0:
            arrived(self.held(step), self.line_recv.at[place])
        if self.line:

            @pl.when((place <= here.col) & (here.col < 3))
            def _():
                self.up(step).start()

            @pl.when((place >= here.col) & (here.col > 0))
            def _():
                self.down(step).start()

    def near_step(self, step):
        self.to_across(step).start()
        self.to_along(step).start()
        if self.core:
            self.to_core(0, step).start()

    def plane_step(self, step):
        here, place = self.here, self.order[step]
        arrived(self.block(here.across, place, here.core), self.across_recv.at[place])
        self.corner_one(step).start()
        if self.core:
            self.to_core(1, step).start()
        arrived(self.block(here.along, place, here.core), self.along_recv.at[place])
        self.corner_two(step).start()
        if self.core:
            self.to_core(2, step).start()

    def corner_step(self, step):
        here, place = self.here, self.order[step]
        target = self.block(here.opposite, place, here.core)
        arrived(target.at[self.first], self.one_recv.at[place])
        arrived(target.at[self.second], self.two_recv.at[place])
        if self.core:
            self.to_core(3, step).start()

    def step(self, index):
        if index < self.steps:
            self.line_step(index)
        if self.plane and 0 <= index - 1 < self.steps:
            self.plane_step(index - 1)
        if self.plane and index < self.steps:
            self.near_step(index)
        if self.plane and 0 <= index - 2 < self.steps:
            self.corner_step(index - 2)

    def core_arrived(self, which, step):
        here, place = self.here, self.order[step]
        target = self.block(here.rows[which], place, 1 - here.core)
        arrived(target, self.core_recv.at[which, place])

    def finish(self, arrivals=True):
        here = self.here
        for step in range(self.steps):
            place = self.order[step]
            if self.line:

                @pl.when((place <= here.col) & (here.col < 3))
                def _():
                    self.up(step).wait_send()

                @pl.when((place >= here.col) & (here.col > 0))
                def _():
                    self.down(step).wait_send()

            if self.plane:
                self.to_across(step).wait_send()
                self.to_along(step).wait_send()
                self.corner_one(step).wait_send()
                self.corner_two(step).wait_send()
                for which in range(4 if self.core else 0):
                    self.to_core(which, step).wait_send()
                    if arrivals:
                        self.core_arrived(which, step)


COLLECT_SEMS = (
    [pltpu.SemaphoreType.DMA((4,))] * 4
    + [pltpu.SemaphoreType.DMA((2, 4))] * 4
    + [pltpu.SemaphoreType.DMA((2, 4))] * 2
    + [pltpu.SemaphoreType.DMA((2, 5))]
)


def collect_buffers(rows, width):
    return [
        pltpu.VMEM((4, 4, rows, width), BF16),
        pltpu.VMEM((4, rows // 2, width), BF16),
        pltpu.VMEM((4, rows // 2, width), BF16),
        pltpu.VMEM((4, rows, width), BF16),
        pltpu.VMEM((4, rows, width), BF16),
        pltpu.VMEM((5, rows, width), BF16),
    ]


class Collect:
    def __init__(self, here, buffers, sems):
        self.here = here
        self.mine, self.one, self.two, self.from_across, self.from_along, self.line = buffers
        (
            self.one_send, self.one_recv, self.two_send, self.two_recv,
            self.across_send, self.across_recv, self.along_send, self.along_recv,
            self.up_send, self.down_send, self.line_recv,
        ) = sems
        half = self.mine.shape[2] // 2
        self.halves = (pl.ds(0, half), pl.ds(half, half))

    def give_one(self, place):
        here = self.here
        return remote(
            self.mine.at[3, place, self.halves[0]], self.one.at[place],
            self.one_send.at[place], self.one_recv.at[place], here.at_row(here.across),
        )

    def give_two(self, place):
        here = self.here
        return remote(
            self.mine.at[3, place, self.halves[1]], self.two.at[place],
            self.two_send.at[place], self.two_recv.at[place], here.at_row(here.along),
        )

    def give_across(self, place, half):
        here, part = self.here, self.halves[half]
        return remote(
            self.mine.at[1, place, part], self.from_across.at[place, part],
            self.across_send.at[half, place], self.across_recv.at[half, place], here.at_row(here.across),
        )

    def give_along(self, place, half):
        here, part = self.here, self.halves[half]
        return remote(
            self.mine.at[2, place, part], self.from_along.at[place, part],
            self.along_send.at[half, place], self.along_recv.at[half, place], here.at_row(here.along),
        )

    def give_up(self, place, half):
        here, part = self.here, self.halves[half]
        sems = self.up_send.at[half, place], self.line_recv.at[half, place]
        return remote(
            self.mine.at[0, place, part], self.line.at[place, part], *sems, here.at_col(here.col + 1)
        )

    def give_down(self, place, slot, half):
        here, part = self.here, self.halves[half]
        sems = self.down_send.at[half, place], self.line_recv.at[half, slot]
        return remote(
            self.mine.at[0, place, part], self.line.at[slot, part], *sems, here.at_col(here.col - 1)
        )

    def add_line(self, place, slot, half):
        part = self.halves[half]
        arrived(self.line.at[slot, part], self.line_recv.at[half, slot])
        add_into(self.mine.at[0, place, part], self.line.at[slot, part])

    def start_far(self, place):
        self.give_one(place).start()
        self.give_two(place).start()
        self.give_along(place, 1).start()

    def start_near(self, place):
        self.give_across(place, 0).start()

    def corner_step(self, place):
        self.give_two(place).wait_recv()
        add_into(self.mine.at[1, place, self.halves[1]], self.two.at[place])
        self.give_across(place, 1).start()
        self.give_one(place).wait_recv()
        add_into(self.mine.at[2, place, self.halves[0]], self.one.at[place])
        self.give_along(place, 0).start()

    def plane_step(self, place):
        for half in range(2):
            self.give_across(place, half).wait_recv()
            self.give_along(place, half).wait_recv()
        add_into(self.mine.at[0, place], self.from_across.at[place], self.from_along.at[place])

    def line_step(self, place):
        col = self.here.col
        for half in range(2):

            @pl.when(((place > col) & (col > 0)) | ((place < col) & (col < 3)))
            def _():
                self.add_line(place, place, half)

            @pl.when(place > col)
            def _():
                self.give_up(place, half).start()

            @pl.when(place < col - 1)
            def _():
                self.give_down(place, place, half).start()

            @pl.when(place == col - 1)
            def _():
                self.give_down(place, 4, half).start()

    def own_step(self):
        col = self.here.col
        for half in range(2):

            @pl.when(col > 0)
            def _():
                self.add_line(col, col, half)

            @pl.when(col < 3)
            def _():
                self.add_line(col, 4, half)

    def finish(self):
        col = self.here.col
        for place in range(4):
            self.give_one(place).wait_send()
            self.give_two(place).wait_send()
            for half in range(2):
                self.give_across(place, half).wait_send()
                self.give_along(place, half).wait_send()

                @pl.when(place > col)
                def _():
                    self.give_up(place, half).wait_send()

                @pl.when(place < col)
                def _():
                    self.give_down(place, place, half).wait_send()


def doc_start(places, cuts):
    return jnp.where(places >= cuts[1], cuts[1], jnp.where(places >= cuts[0], cuts[0], 0))


def key_blocks(cuts, first_query, rows, scores_of, block_fn):
    def scan(index, carry):
        start = pl.multiple_of(index * rows, rows)
        free = (start >= doc_start(first_query + rows - 1, cuts)) & (start + rows <= first_query + 1)

        @pl.when(free)
        def _():
            block_fn(start, scores_of(start))

        @pl.when(jnp.logical_not(free))
        def _():
            key_place = start + lax.broadcasted_iota(jnp.int32, (rows, rows), 0)
            place = first_query + lax.broadcasted_iota(jnp.int32, (1, rows), 1)
            allowed = (key_place <= place) & (key_place >= doc_start(place, cuts))
            block_fn(start, jnp.where(allowed, scores_of(start), MASKED))

        return carry

    lax.fori_loop(doc_start(first_query, cuts) // rows, first_query // rows + 1, scan, 0)


def attend_kernel(scale, group_tok, cuts, query, keys, values_t, mixed, total, top, summed, acc):
    rows = query.shape[0]
    side = lax.axis_index("exp") % 2
    first_query = side * group_tok + pl.program_id(0) * rows
    top[...] = jnp.full_like(top, MASKED)
    summed[...] = jnp.zeros_like(summed)
    acc[...] = jnp.zeros_like(acc)
    cut = (cuts[0, 0], cuts[0, 1])

    def scores_of(start):
        return contract_cols(keys[pl.ds(start, rows)], query[...]) * scale

    def block_fn(start, scores):
        old = top[...]
        new = jnp.maximum(old, jnp.max(scores, axis=0, keepdims=True))
        weights = jnp.exp(scores - new)
        decay = jnp.exp(old - new)
        top[...] = new
        summed[...] = summed[...] * decay + jnp.sum(weights, axis=0, keepdims=True)
        acc[...] = acc[...] * decay + matmul(values_t[:, pl.ds(start, rows)], weights.astype(BF16))

    key_blocks(cut, first_query, rows, scores_of, block_fn)
    mixed[...] = (acc[...] / summed[...]).T
    total[...] = top[...] + jnp.log(summed[...])


def attend(query, keys, values, cuts, scale, rows=512):
    group_tok, head_size = query.shape
    whole = lambda shape: pl.BlockSpec(shape, lambda i: (0, 0))
    return pl.pallas_call(
        functools.partial(attend_kernel, scale, group_tok),
        grid=(group_tok // rows,),
        in_specs=[
            pl.BlockSpec(memory_space=pltpu.SMEM),
            pl.BlockSpec((rows, head_size), lambda i: (i, 0)),
            whole(keys.shape),
            whole(values.shape[::-1]),
        ],
        out_specs=[
            pl.BlockSpec((rows, head_size), lambda i: (i, 0)),
            pl.BlockSpec((1, rows), lambda i: (0, i)),
        ],
        out_shape=[
            jax.ShapeDtypeStruct((group_tok, head_size), F32),
            jax.ShapeDtypeStruct((1, group_tok), F32),
        ],
        scratch_shapes=[
            pltpu.VMEM((1, rows), F32),
            pltpu.VMEM((1, rows), F32),
            pltpu.VMEM((head_size, rows), F32),
        ],
        compiler_params=pltpu.CompilerParams(vmem_limit_bytes=40 * 2**20),
        cost_estimate=pl.CostEstimate(
            flops=4 * 7 * 2**20 * head_size, bytes_accessed=2**23, transcendentals=7 * 2**20
        ),
    )(cuts[None], query, keys, values.T)


def attend_back_kernel(
    scale, group_tok, cuts, query, keys, keys_t, values, d_mixed, total, delta,
    d_query, d_keys, d_values, acc,
):
    rows = query.shape[0]
    side = lax.axis_index("exp") % 2
    first_query = side * group_tok + pl.program_id(0) * rows
    cut = (cuts[0, 0], cuts[0, 1])

    @pl.when(pl.program_id(0) == 0)
    def _():
        d_keys[...] = jnp.zeros_like(d_keys)
        d_values[...] = jnp.zeros_like(d_values)

    acc[...] = jnp.zeros_like(acc)

    def scores_of(start):
        return contract_cols(keys[pl.ds(start, rows)], query[...]) * scale

    def block_fn(start, scores):
        part = pl.ds(start, rows)
        weights = jnp.exp(scores - total[...])
        d_weights = contract_cols(values[part], d_mixed[...])
        d_scores = (weights * (d_weights - delta[...])).astype(BF16)
        d_values[part] += matmul(weights.astype(BF16), d_mixed[...])
        d_keys[part] += matmul(d_scores, query[...]) * scale
        acc[...] += matmul(keys_t[:, part], d_scores)

    key_blocks(cut, first_query, rows, scores_of, block_fn)
    d_query[...] = (acc[...] * scale).T


def attend_back(query, keys, values, d_mixed, mixed, total, cuts, scale, rows=512):
    group_tok, head_size = query.shape
    delta = jnp.sum(d_mixed.astype(F32) * mixed, axis=1)[None]
    whole = lambda shape: pl.BlockSpec(shape, lambda i: (0, 0))
    block = pl.BlockSpec((rows, head_size), lambda i: (i, 0))
    line = pl.BlockSpec((1, rows), lambda i: (0, i))
    return pl.pallas_call(
        functools.partial(attend_back_kernel, scale, group_tok),
        grid=(group_tok // rows,),
        in_specs=[
            pl.BlockSpec(memory_space=pltpu.SMEM),
            block,
            whole(keys.shape),
            whole(keys.shape[::-1]),
            whole(keys.shape),
            block,
            line,
            line,
        ],
        out_specs=[block, whole(keys.shape), whole(keys.shape)],
        out_shape=[
            jax.ShapeDtypeStruct((group_tok, head_size), F32),
            jax.ShapeDtypeStruct(keys.shape, F32),
            jax.ShapeDtypeStruct(keys.shape, F32),
        ],
        scratch_shapes=[pltpu.VMEM((head_size, rows), F32)],
        compiler_params=pltpu.CompilerParams(vmem_limit_bytes=48 * 2**20),
        cost_estimate=pl.CostEstimate(
            flops=10 * 7 * 2**20 * head_size, bytes_accessed=2**23, transcendentals=7 * 2**20
        ),
    )(cuts[None], query, keys, keys.T, values, d_mixed, total, delta)


def transposed_product(left, right):
    return jnp.dot(left.T, right, preferred_element_type=F32)


def column_of(line):
    return jnp.broadcast_to(line, (128, 128)).T[:, :1]


def line_of(column):
    return jnp.broadcast_to(column, (128, 128)).T[:1]


def expert_kernel(
    expert_count, normed, grads_all, mask, gate_half, up_half, down_half,
    gate_other, up_other, down_other, router,
    rows_all, out_parts, total, inner_in, grad_gate, grad_up, grad_down,
    their_gates, their_down,
    gate_w, up_w, down_w, masks, x_buf, d_buf, gates_t, weighteds_t, d_gates, d_ups, weighteds, out_buf,
    inner, sum_buf, sum_down, *rest,
):
    here = Here()
    row, col, core = here.row, here.col, here.core
    rows, width = normed.shape
    half = gate_half.shape[1]
    expert = row * 4 + col
    count = len(SPREAD_SEMS)
    collect = Collect(here, rest[:6], rest[6 : 6 + len(COLLECT_SEMS)])
    rest = rest[6 + len(COLLECT_SEMS) :]
    (
        weight_sem, load_sem, store_sem, tile_sem, give_send, give_recv, their_sem, sum_sem,
        inner_send, inner_recv,
    ) = rest[:10]
    sems = rest[10:]

    def x_block(of_row, place, unused_core):
        return rows_all.at[pl.ds(pl.multiple_of((of_row * 4 + place) * rows, rows), rows)]

    def d_block(of_row, place, unused_core):
        return grads_all.at[pl.ds(pl.multiple_of((of_row * 4 + place) * rows, rows), rows)]

    def m_block(of_row, place, unused_core):
        return masks.at[of_row, place]

    spread_x = Spread(here, normed, x_block, rows, sems[:count], core=False)
    spread_m = Spread(here, mask, m_block, mask.shape[0], sems[count:], core=False)
    order = here.near_first

    own_half = pl.ds(pl.multiple_of(core * half, half), half)
    other_half = pl.ds(pl.multiple_of((1 - core) * half, half), half)
    keeps = [
        pltpu.make_async_copy(source, target, weight_sem.at[index])
        for index, (source, target) in enumerate(
            (
                (normed, x_block(row, col, 0)),
                (mask, m_block(row, col, 0)),
                (gate_half, gate_w.at[:, own_half]),
                (up_half, up_w.at[:, own_half]),
                (down_half, down_w.at[own_half]),
                (gate_other, gate_w.at[:, other_half]),
                (up_other, up_w.at[:, other_half]),
                (down_other, down_w.at[other_half]),
            )
        )
    ]
    greet(here.group_peers() + [here.other_core()])
    spread_x.step(0)
    spread_m.step(0)
    for keep in keeps:
        keep.start()

    turns = (3, 2, 1, 0)

    def loads(step):
        return [
            pltpu.make_async_copy(
                source(here.rows[which], order[step], 0),
                target.at[pl.ds(position * rows, rows)],
                load_sem.at[position, array],
            )
            for position, which in enumerate(turns)
            for array, (source, target) in enumerate(((x_block, x_buf), (d_block, d_buf)))
        ]

    def stores(step):
        return [
            pltpu.make_async_copy(
                out_buf.at[pl.ds(position * rows, rows)],
                out_parts.at[which, order[step]],
                store_sem.at[position],
            )
            for position, which in enumerate(turns)
        ]

    tile = 256

    def first_products(step):
        place = order[step]
        x = x_buf[...]
        lane = lax.broadcasted_iota(jnp.int32, (x.shape[0], router.shape[1]), 1)
        logits = jnp.where(lane < expert_count, matmul(x, router[...]), MASKED)
        raised = jnp.exp(logits - jnp.max(logits, axis=1, keepdims=True))
        picked = jnp.sum(jnp.where(lane == expert, raised, 0.0), axis=1, keepdims=True)
        routed = jnp.concatenate(
            [column_of(masks[here.rows[which], place, pl.ds(expert, 1)]) for which in turns]
        )
        gate = picked / jnp.sum(raised, axis=1, keepdims=True) * routed
        columns = [
            pl.ds(pl.multiple_of((here.rows[which] * 4 + place) * rows, rows), rows) for which in turns
        ]

        def tile_step(index, inner_sum):
            at = pl.ds(pl.multiple_of(index * tile, tile), tile)
            pre_gate = matmul(x_buf[...], gate_w[:, at])
            pre_up = matmul(x_buf[...], up_w[:, at])
            back = contract_cols(d_buf[...], down_w[at])
            sigmoid_gate = 1.0 / (1.0 + jnp.exp(-pre_gate))
            silu_gate = pre_gate * sigmoid_gate
            hidden = (silu_gate * pre_up).astype(BF16).astype(F32)
            d_hid = back * gate
            d_gate = (d_hid * pre_up * (sigmoid_gate + silu_gate * (1.0 - sigmoid_gate))).astype(BF16)
            d_up = (d_hid * silu_gate).astype(BF16)
            weight = (hidden * gate).astype(BF16)
            d_gates[:, at] = d_gate
            d_ups[:, at] = d_up
            weighteds[:, at] = weight
            side = index // (half // tile)
            first = pl.multiple_of(index % (half // tile) * tile, tile)
            for values, target in (
                (d_gate, gates_t.at[side, pl.ds(first, tile)]),
                (d_up, gates_t.at[side, pl.ds(first + half, tile)]),
                (weight, weighteds_t.at[at]),
            ):
                turned = values.T
                for position, column in enumerate(columns):
                    target[:, column] = turned[:, position * rows : (position + 1) * rows]
            return inner_sum + jnp.sum(hidden * back, axis=1, keepdims=True)

        start = jnp.zeros((x.shape[0], 1), F32)
        inner_sum = lax.fori_loop(0, gate_w.shape[1] // tile, tile_step, start, unroll=2)
        for position, which in enumerate(turns):
            part = slice(position * rows, (position + 1) * rows)
            inner[here.rows[which], place, 0:1] = line_of(inner_sum[part])

    def second_products(step):
        place = order[step]

        @pl.loop(0, width // tile, unroll=2)
        def _(index):
            at = pl.ds(pl.multiple_of(index * tile, tile), tile)
            out_buf[:, at] = matmul(weighteds[...], down_w[:, at]).astype(BF16)
            d_x = contract_cols(d_gates[...], gate_w[at]) + contract_cols(d_ups[...], up_w[at])
            d_x = d_x.astype(BF16)
            for position, which in enumerate(turns):
                collect.mine[which, place, :, at] = d_x[position * rows : (position + 1) * rows]

    for index in (1, 2):
        spread_x.step(index)
        spread_m.step(index)
    for keep in keeps:
        keep.wait()
    for copy in loads(0):
        copy.start()
    turn_order = (0, 1, 3, 2)
    ends = (col == 0) | (col == 3)

    def from_ends(step):
        @pl.when(ends)
        def _():
            collect.line_step(order[step])

    def from_inside(step):
        @pl.when(jnp.logical_not(ends))
        def _():
            collect.line_step(order[step])

    for turn, step in enumerate(turn_order):
        for copy in loads(step):
            copy.wait()
        first_products(step)
        if turn < 2:
            spread_x.step(turn + 3)
            spread_m.step(turn + 3)
        if turn in (0, 2):
            for copy in loads(turn_order[turn + 1]):
                copy.start()
        if turn > 0:
            for copy in stores(turn_order[turn - 1]):
                copy.wait()
            collect.corner_step(order[turn_order[turn - 1]])
        second_products(step)
        for copy in stores(step):
            copy.start()
        collect.start_far(order[step])
        collect.start_near(order[step])
        if turn == 1:
            spread_x.step(5)
            spread_m.step(5)
            for copy in loads(turn_order[2]):
                copy.start()
        if turn > 0:
            collect.plane_step(order[turn_order[turn - 1]])
        if turn > 1:
            from_ends(turn_order[turn - 1])

    tiles = width // tile

    def tile_at(index):
        return pl.ds(pl.multiple_of(index * tile, tile), tile)

    def acts_of(kind, side):
        if kind == 0:
            return gates_t[side]
        return weighteds_t[pl.ds(pl.multiple_of(side * half, half), half)]

    counts = (2 * half, half)

    def slot_at(kind, slot):
        return pl.ds(pl.multiple_of((2 * kind + slot) * tile, tile), tile)

    def tile_buf(kind, slot):
        return gate_w.at[:, slot_at(kind, slot)]

    def give_buf(kind, slot):
        return up_w.at[pl.ds(0, counts[kind]), slot_at(kind, slot)]

    def their_buf(kind, slot):
        return up_w.at[pl.ds(width // 2, counts[kind]), slot_at(kind, slot)]

    theirs = (their_gates, their_down)

    def tile_load(kind, index, slot):
        source = (rows_all, grads_all)[kind]
        return pltpu.make_async_copy(
            source.at[:, tile_at(index)], tile_buf(kind, slot), tile_sem.at[slot]
        )

    def give(kind, index, slot):
        sems = give_send.at[slot, kind], give_recv.at[kind, index]
        return remote(give_buf(kind, slot), theirs[kind].at[:, tile_at(index)], *sems, here.other_core())

    def their_load(kind, index, slot):
        return pltpu.make_async_copy(
            theirs[kind].at[:, tile_at(index)],
            their_buf(kind, slot),
            their_sem.at[slot, kind],
        )

    def sum_stores(kind, index, slot):
        if kind == 1:
            target = grad_down.at[:, tile_at(index)]
            return [pltpu.make_async_copy(sum_down, target, sum_sem.at[0, 2])]
        return [
            pltpu.make_async_copy(
                sum_buf.at[slot, part], target.at[tile_at(index)], sum_sem.at[slot, part]
            )
            for part, target in enumerate((grad_gate, grad_up))
        ]

    def give_gradients(kind, start, stop):
        tile_load(kind, start, 0).start()

        @pl.loop(start, stop)
        def _(index):
            slot = index % 2

            @pl.when(index + 1 < stop)
            def _():
                tile_load(kind, index + 1, 1 - slot).start()

            tile_load(kind, index, slot).wait()
            product = matmul(acts_of(kind, 1 - core), tile_buf(kind, slot)[...])

            @pl.when(index >= 2)
            def _():
                give(kind, index - 2, slot).wait_send()

            give_buf(kind, slot)[...] = product.astype(BF16)
            give(kind, index, slot).start()

    def keep_gradients(kind, start, stop):
        tile_load(kind, start, 0).start()
        give(kind, start, 0).wait_recv()
        their_load(kind, start, 0).start()

        @pl.loop(start, stop)
        def _(index):
            slot = index % 2

            @pl.when(index + 1 < stop)
            def _():
                tile_load(kind, index + 1, 1 - slot).start()
                give(kind, index + 1, 1 - slot).wait_recv()
                their_load(kind, index + 1, 1 - slot).start()

            tile_load(kind, index, slot).wait()
            product = matmul(acts_of(kind, core), tile_buf(kind, slot)[...])
            their_load(kind, index, slot).wait()
            product = product + their_buf(kind, slot)[...].astype(F32)
            held = 2 - kind

            @pl.when(index >= held)
            def _():
                for copy in sum_stores(kind, index - held, slot):
                    copy.wait()

            if kind == 1:
                sum_down[...] = product
            else:
                sum_buf[slot, 0] = product[:half].T
                sum_buf[slot, 1] = product[half:].T
            for copy in sum_stores(kind, index, slot):
                copy.start()

    def give_inner(index):
        step = index + 1
        to_row, to_col = (row + step // 4) % 4, (col + step) % 4
        return remote(
            inner.at[to_row, to_col],
            inner_in.at[row, col],
            inner_send.at[index],
            inner_recv.at[row, col],
            (to_row, to_col, core),
        )

    for index in range(15):
        give_inner(index).start()
    inner_in[row, col] = inner[row, col]
    give_gradients(0, 0, tiles // 2)
    from_inside(3)
    collect.corner_step(order[2])
    give_gradients(0, tiles // 2, tiles)
    collect.plane_step(order[2])
    from_ends(2)
    give_gradients(1, 0, tiles)
    from_inside(2)
    keep_gradients(0, 0, tiles // 2)
    from_inside(1)
    keep_gradients(0, tiles // 2, tiles)
    keep_gradients(1, 0, tiles)
    collect.own_step()
    total[...] = collect.mine[0, col]

    for index in range(15):
        give_inner(index).wait_send()
        step = index + 1
        from_row, from_col = (row + 4 - step // 4) % 4, (col + 4 - step % 4) % 4
        arrived(inner_in.at[from_row, from_col], inner_recv.at[from_row, from_col])
    for copy in stores(turn_order[3]):
        copy.wait()
    for kind in range(2):
        for slot in range(2):
            give(kind, tiles - 2 + slot, slot).wait_send()
        for slot in range(2 - kind):
            for copy in sum_stores(kind, tiles - 2 + kind + slot, slot):
                copy.wait()
    spread_x.finish()
    spread_m.finish()
    collect.finish()


def expert_stage(normed, grads_all, mask, halves, others, router, collective_id):
    rows, width = normed.shape
    half = halves[0].shape[1]
    expert_count = router.shape[1]
    router = jnp.pad(router, ((0, 0), (0, 128 - expert_count)))
    tokens = 16 * rows
    tile = 256
    vmem = pl.BlockSpec(memory_space=pltpu.VMEM)
    hbm = pl.BlockSpec(memory_space=pl.ANY)
    dma = pltpu.SemaphoreType.DMA
    blocks = jax.ShapeDtypeStruct((4, 4, rows, width), BF16)
    got = pl.pallas_call(
        functools.partial(expert_kernel, expert_count),
        in_specs=[hbm] * 9 + [vmem],
        out_specs=[hbm] * 2 + [vmem] * 2 + [hbm] * 5,
        out_shape=[
            jax.ShapeDtypeStruct((tokens, width), BF16),
            blocks,
            jax.ShapeDtypeStruct((rows, width), BF16),
            jax.ShapeDtypeStruct((4, 4, 8, rows), F32),
            jax.ShapeDtypeStruct((width, half), F32),
            jax.ShapeDtypeStruct((width, half), F32),
            jax.ShapeDtypeStruct((half, width), F32),
            jax.ShapeDtypeStruct((2 * half, width), BF16),
            jax.ShapeDtypeStruct((half, width), BF16),
        ],
        scratch_shapes=[
            pltpu.VMEM((width, 2 * half), BF16),
            pltpu.VMEM((width, 2 * half), BF16),
            pltpu.VMEM((2 * half, width), BF16),
            pltpu.VMEM((4, 4) + mask.shape, F32),
            pltpu.VMEM((4 * rows, width), BF16),
            pltpu.VMEM((4 * rows, width), BF16),
            pltpu.VMEM((2, 2 * half, tokens), BF16),
            pltpu.VMEM((2 * half, tokens), BF16),
            pltpu.VMEM((4 * rows, 2 * half), BF16),
            pltpu.VMEM((4 * rows, 2 * half), BF16),
            pltpu.VMEM((4 * rows, 2 * half), BF16),
            pltpu.VMEM((4 * rows, width), BF16),
            pltpu.VMEM((4, 4, 8, rows), F32),
            pltpu.VMEM((2, 2, tile, half), F32),
            pltpu.VMEM((half, tile), F32),
        ]
        + collect_buffers(rows, width)
        + COLLECT_SEMS
        + [
            dma((8,)), dma((4, 2)), dma((4,)),
            dma((2,)), dma((2, 2)), dma((2, width // tile)), dma((2, 2)), dma((2, 3)),
            dma((15,)), dma((4, 4)),
        ]
        + SPREAD_SEMS * 2,
        compiler_params=pltpu.CompilerParams(
            collective_id=collective_id, has_side_effects=True, vmem_limit_bytes=61 * 2**20
        ),
        cost_estimate=pl.CostEstimate(
            flops=18 * 2 * tokens * width * half,
            bytes_accessed=2**26,
            transcendentals=2 * tokens * half,
        ),
    )(normed, grads_all, mask, *halves, *others, router)
    return got[1], got[2], got[3], got[4:7]


def project_kernel(
    hidden, gain, weights, q_gain, k_gain, cosine, sine,
    normed_out, weights_out, qkv_out, totals, query, keys, values,
    normed, all_weights, qkv, out_sem,
    heads, stat, scale_q, scale_k, kept_sem, kept_kv_sem,
    stat_send, stat_recv, head_send, head_recv, pair_send, pair_recv, *sems,
):
    here = Here()
    row, col, core = here.row, here.col, here.core
    count = len(SPREAD_SEMS)
    rows, width = hidden.shape
    depth = weights.shape[0]
    part = depth // 2

    def weight_block(of_row, unused_place, of_core):
        return all_weights.at[pl.ds(pl.multiple_of(of_row * depth + of_core * part, part), part)]

    def normed_block(unused_row, place, unused_core):
        return normed.at[pl.ds(pl.multiple_of(place * rows, rows), rows)]

    own_weight = weights.at[pl.ds(pl.multiple_of(core * part, part), part)]
    spread_w = Spread(here, own_weight, weight_block, part, sems[:count], line=False)
    spread_n = Spread(
        here, normed_block(row, col, core), normed_block, rows, sems[count:], plane=False
    )
    greet(here.plane_peers() + here.line_peers() + [here.other_core()])
    spread_w.step(0)
    keep = pltpu.make_async_copy(own_weight, weight_block(row, 0, core), kept_sem)
    keep.start()

    values_in = hidden[...].astype(F32)
    scale_one = lax.rsqrt(jnp.mean(values_in * values_in, axis=1, keepdims=True) + EPSILON)
    own_rows = pl.ds(pl.multiple_of(col * rows, rows), rows)
    normed[own_rows] = (values_in * scale_one * gain[...].astype(F32)).astype(BF16)
    spread_n.step(0)
    spread_w.step(1)
    spread_n.step(1)
    spread_w.step(2)
    spread_n.step(2)
    spread_n.step(3)
    keep.wait()
    for which in range(4):
        spread_w.core_arrived(which, 0)
    puts = [
        pltpu.make_async_copy(source, target, out_sem.at[index])
        for index, (source, target) in enumerate(
            ((normed, normed_out), (all_weights, weights_out), (qkv, qkv_out))
        )
    ]
    puts[0].start()
    puts[1].start()
    columns = 256

    @pl.loop(0, qkv.shape[1] // columns)
    def _(index):
        at = pl.ds(pl.multiple_of(index * columns, columns), columns)
        qkv[:, at] = matmul(normed[...], all_weights[:, at])

    puts[2].start()

    plane = qkv.shape[1] // (3 * HD)
    for kind in range(2):
        square = jnp.zeros((qkv.shape[0], HD), F32)
        for head in range(plane):
            start = (head * 3 + kind) * HD
            raw = qkv[:, start : start + HD]
            square = square + raw * raw
        stat[col, kind : kind + 1] = jnp.sum(square.T, axis=0, keepdims=True)

    def give_stat(step):
        peer = here.line_peers()[step]
        return remote(stat.at[col], stat.at[col], stat_send.at[step], stat_recv.at[col], peer)

    for step in range(3):
        give_stat(step).start()
    for step in range(3):
        place = (col + step + 1) % 4
        arrived(stat.at[place], stat_recv.at[place])
    total = stat[0] + stat[1] + stat[2] + stat[3]
    totals[...] = total
    for kind, target in enumerate((scale_q, scale_k)):
        line = lax.rsqrt(total[kind : kind + 1] / width + EPSILON)
        target[...] = jnp.broadcast_to(line, (HD, line.shape[1])).T

    chunk = 64

    @pl.loop(0, qkv.shape[0] // chunk)
    def _(index):
        at = pl.ds(pl.multiple_of(index * chunk, chunk), chunk)
        for head in range(plane):
            for kind, (scales, gains) in enumerate(((scale_q, q_gain), (scale_k, k_gain))):
                raw = qkv[at, pl.ds((head * 3 + kind) * HD, HD)]
                unit = raw * scales[at] * gains[:, head * HD : (head + 1) * HD]
                turned = pltpu.roll(unit, HD // 2, 1)
                heads[head, kind, at] = (unit * cosine[at] + turned * sine[at]).astype(BF16)
            heads[head, 2, at] = qkv[at, pl.ds((head * 3 + 2) * HD, HD)].astype(BF16)

    targets = (query.at[row], keys.at[1, row], values.at[1, row])

    def give_head(step, kind):
        dest = here.rows[step + 1]
        sems = head_send.at[step, kind], head_recv.at[kind, row]
        return remote(heads.at[dest, kind], targets[kind], *sems, here.at_row(dest))

    for kind in (1, 2, 0):
        for step in range(3):
            give_head(step, kind).start()

    def give_pair(source, kind):
        array = (keys, values)[kind]
        sems = pair_send.at[kind, source], pair_recv.at[kind, source]
        return remote(array.at[1, source], array.at[0, source], *sems, here.other_core())

    def keep_pair(source, kind):
        array = (keys, values)[kind]
        return pltpu.make_async_copy(
            array.at[1, source], array.at[0, source], kept_kv_sem.at[kind, source]
        )

    def pair_from(source):
        @pl.when(core == 0)
        def _():
            for kind in range(2):
                give_pair(source, kind).start()
                keep_pair(source, kind).start()

    for kind, array in ((1, keys), (2, values)):
        array[1, row] = heads[row, kind]
    query[row] = heads[row, 0]
    pair_from(row)
    for source in here.rows[1:]:
        arrived(keys.at[1, source], head_recv.at[1, source])
        arrived(values.at[1, source], head_recv.at[2, source])
        pair_from(source)
    for source in here.rows[1:]:
        arrived(query.at[source], head_recv.at[0, source])

    @pl.when(core == 0)
    def _():
        for source in range(4):
            for kind in range(2):
                give_pair(source, kind).wait_send()
                keep_pair(source, kind).wait()

    @pl.when(core == 1)
    def _():
        for source in range(4):
            for kind in range(2):
                give_pair(source, kind).wait_recv()

    for step in range(3):
        give_stat(step).wait_send()
        for kind in range(3):
            give_head(step, kind).wait_send()
    for put in puts:
        put.wait()
    spread_w.finish(arrivals=False)
    spread_n.finish()


def project(hidden, gain, weights, q_gain, k_gain, cosine, sine, collective_id):
    rows, width = hidden.shape
    depth, columns = weights.shape
    row_tok = 4 * rows
    plane = columns // (3 * HD)
    vmem = pl.BlockSpec(memory_space=pltpu.VMEM)
    hbm = pl.BlockSpec(memory_space=pl.ANY)
    return pl.pallas_call(
        project_kernel,
        in_specs=[vmem, vmem, hbm, vmem, vmem, vmem, vmem],
        out_specs=[hbm] * 3 + [vmem] * 4,
        out_shape=[
            jax.ShapeDtypeStruct((row_tok, width), BF16),
            jax.ShapeDtypeStruct((4 * depth, columns), BF16),
            jax.ShapeDtypeStruct((row_tok, columns), F32),
            jax.ShapeDtypeStruct((8, row_tok), F32),
            jax.ShapeDtypeStruct((4, row_tok, HD), BF16),
            jax.ShapeDtypeStruct((2, 4, row_tok, HD), BF16),
            jax.ShapeDtypeStruct((2, 4, row_tok, HD), BF16),
        ],
        scratch_shapes=[
            pltpu.VMEM((row_tok, width), BF16),
            pltpu.VMEM((4 * depth, columns), BF16),
            pltpu.VMEM((row_tok, columns), F32),
            pltpu.SemaphoreType.DMA((3,)),
            pltpu.VMEM((plane, 3, row_tok, HD), BF16),
            pltpu.VMEM((4, 8, row_tok), F32),
            pltpu.VMEM((row_tok, HD), F32),
            pltpu.VMEM((row_tok, HD), F32),
            pltpu.SemaphoreType.DMA,
            pltpu.SemaphoreType.DMA((2, 4)),
            pltpu.SemaphoreType.DMA((3,)),
            pltpu.SemaphoreType.DMA((4,)),
            pltpu.SemaphoreType.DMA((3, 3)),
            pltpu.SemaphoreType.DMA((3, 4)),
            pltpu.SemaphoreType.DMA((2, 4)),
            pltpu.SemaphoreType.DMA((2, 4)),
        ]
        + SPREAD_SEMS * 2,
        compiler_params=pltpu.CompilerParams(
            collective_id=collective_id, has_side_effects=True, vmem_limit_bytes=56 * 2**20
        ),
    )(hidden, gain[None], weights, q_gain, k_gain, cosine, sine)


def attention_kernel(
    scale, cuts, query, keys, values, out_weights, hidden, gain,
    mixed, total, whole_out, mixed_rows, middle, normed,
    all_out, put_sem, values_t, top, summed, acc, mixed_low, mixed_tok, kept_sem,
    row_send, row_recv, token_send, token_recv, *sems,
):
    here = Here()
    row, col, core = here.row, here.col, here.core
    rows = hidden.shape[0]
    row_tok = 4 * rows
    group_tok = 4 * row_tok
    side = out_weights.shape[0]

    def out_block(of_row, place, of_core):
        start = pl.multiple_of(place * side + of_core * (side // 2), side // 2)
        return all_out.at[pl.ds(start, side // 2), pl.ds(pl.multiple_of(of_row * side, side), side)]

    own_out = out_weights.at[pl.ds(pl.multiple_of(core * (side // 2), side // 2), side // 2)]
    spread = Spread(here, own_out, out_block, side // 2, sems)
    keep = pltpu.make_async_copy(own_out, out_block(row, col, core), kept_sem)
    keep.start()
    values_t[...] = values[...].T
    greet(here.plane_peers() + here.line_peers() + [here.other_core()])
    spread.step(0)
    cut = (cuts[0, 0], cuts[0, 1])
    last_query = 2 * group_tok - row_tok

    def queries(index):
        at = pl.ds(index * row_tok, row_tok)
        first_query = core * group_tok + index * row_tok
        top[...] = jnp.full_like(top, MASKED)
        summed[...] = jnp.zeros_like(summed)
        acc[...] = jnp.zeros_like(acc)

        def block_fn(part, scores):
            old = top[...]
            new = jnp.maximum(old, jnp.max(scores, axis=0, keepdims=True))
            weight = jnp.exp(scores - new)
            decay = jnp.exp(old - new)
            top[...] = new
            summed[...] = summed[...] * decay + jnp.sum(weight, axis=0, keepdims=True)
            acc[...] = acc[...] * decay + matmul(values_t[:, part], weight.astype(BF16))

        def scan(block, carry):
            first_key = block * row_tok
            part = pl.ds(pl.multiple_of(first_key, row_tok), row_tok)
            masked = (block == 0) | (first_key == first_query) | (first_query == last_query)

            @pl.when(jnp.logical_not(masked))
            def _():
                block_fn(part, contract_cols(keys[part], query[at]) * scale)

            @pl.when(masked)
            def _():
                key_place = first_key + lax.broadcasted_iota(jnp.int32, (row_tok, row_tok), 0)
                place = first_query + lax.broadcasted_iota(jnp.int32, (1, row_tok), 1)
                allowed = (key_place <= place) & (key_place >= doc_start(place, cut))
                scores = contract_cols(keys[part], query[at]) * scale
                block_fn(part, jnp.where(allowed, scores, MASKED))

            return carry

        lax.fori_loop(0, core * 4 + index + 1, scan, 0)
        got = (acc[...] / summed[...]).T
        mixed[at] = got
        mixed_low[index] = got.astype(BF16)
        total[:, at] = top[...] + jnp.log(summed[...])

        @pl.when(row != index)
        def _():
            give_row(index).start()

        @pl.when(row == index)
        def _():
            mixed_rows[row] = mixed_low[index]

    def give_row(index):
        sems_of = row_send.at[index], row_recv.at[row]
        return remote(mixed_low.at[index], mixed_rows.at[row], *sems_of, here.at_row(index))

    def give_token(step):
        place = (col + step) % 4
        part = pl.ds(pl.multiple_of(place * rows, rows), rows)
        sems_of = token_send.at[step], token_recv.at[col]
        return remote(mixed_rows.at[:, part], mixed_tok.at[col], *sems_of, here.at_col(place))

    for index in range(4):
        queries(index)
        spread.step(index + 1)
    for source in here.rows[1:]:
        arrived(mixed_rows.at[source], row_recv.at[source])
    for step in range(1, 4):
        give_token(step).start()
    mixed_tok[col] = mixed_rows[:, pl.ds(pl.multiple_of(col * rows, rows), rows)]
    spread.step(5)
    keep.wait()
    spread.finish()
    put = pltpu.make_async_copy(all_out, whole_out, put_sem)
    put.start()
    for step in range(1, 4):
        place = (col + 4 - step) % 4
        arrived(mixed_tok.at[place], token_recv.at[place])
    own = jnp.concatenate([mixed_tok[place, head] for place in range(4) for head in range(4)], axis=1)
    tile = 512

    @pl.loop(0, all_out.shape[1] // tile)
    def _(index):
        at = pl.ds(pl.multiple_of(index * tile, tile), tile)
        middle[:, at] = hidden[:, at].astype(F32) + matmul(own, all_out[:, at])

    values_in = middle[...]
    root = lax.rsqrt(jnp.mean(values_in * values_in, axis=1, keepdims=True) + EPSILON)
    normed[...] = (values_in * root * gain[...].astype(F32)).astype(BF16)
    put.wait()
    for index in range(4):

        @pl.when(row != index)
        def _():
            give_row(index).wait_send()

    for step in range(1, 4):
        give_token(step).wait_send()


def attention_stage(query, keys, values, cuts, out_weights, hidden, gain, scale, collective_id):
    rows, width = hidden.shape
    row_tok, group_tok = 4 * rows, 16 * rows
    vmem, hbm = pl.BlockSpec(memory_space=pltpu.VMEM), pl.BlockSpec(memory_space=pl.ANY)
    dma = pltpu.SemaphoreType.DMA
    return pl.pallas_call(
        functools.partial(attention_kernel, scale),
        in_specs=[pl.BlockSpec(memory_space=pltpu.SMEM)] + [vmem] * 3 + [hbm] + [vmem] * 2,
        out_specs=[vmem] * 2 + [hbm] + [vmem] * 3,
        out_shape=[
            jax.ShapeDtypeStruct((group_tok, HD), F32),
            jax.ShapeDtypeStruct((1, group_tok), F32),
            jax.ShapeDtypeStruct((width, width), BF16),
            jax.ShapeDtypeStruct((4, row_tok, HD), BF16),
            jax.ShapeDtypeStruct((rows, width), F32),
            jax.ShapeDtypeStruct((rows, width), BF16),
        ],
        scratch_shapes=[
            pltpu.VMEM((width, width), BF16),
            dma,
            pltpu.VMEM((HD, 2 * group_tok), BF16),
            pltpu.VMEM((1, row_tok), F32),
            pltpu.VMEM((1, row_tok), F32),
            pltpu.VMEM((HD, row_tok), F32),
            pltpu.VMEM((4, row_tok, HD), BF16),
            pltpu.VMEM((4, 4, rows, HD), BF16),
            dma, dma((4,)), dma((4,)), dma((4,)), dma((4,)),
        ]
        + SPREAD_SEMS,
        compiler_params=pltpu.CompilerParams(
            collective_id=collective_id, has_side_effects=True, vmem_limit_bytes=40 * 2**20
        ),
    )(cuts[None], query, keys, values, out_weights, hidden, gain[None])


class PairSum:
    def __init__(self, here, values, out, held, got, send, recv):
        self.here, self.values, self.out, self.held, self.got = here, values, out, held, got
        self.send, self.recv = send, recv
        col, half = here.col, values.shape[1] // 2
        self.own = pl.ds(pl.multiple_of(here.core * half, half), half)
        self.others = pl.ds(pl.multiple_of((1 - here.core) * half, half), half)
        self.peers = [
            here.at_row(here.across),
            here.at_row(here.along),
            here.at_col(col + 1 - 2 * (col % 2)),
            here.at_col((col + 2) % 4),
        ]

    def copy(self, step):
        here, sems = self.here, (self.send.at[step], self.recv.at[step])
        if step == 0:
            return remote(self.values.at[:, self.others], self.got.at[0], *sems, here.other_core())
        if step == 5:
            return remote(self.held.at[4], self.out.at[:, self.own], *sems, here.other_core())
        return remote(self.held.at[step - 1], self.got.at[step], *sems, self.peers[step - 1])

    def begin(self):
        self.copy(0).start()

    def step(self, index):
        if index == 5:
            arrived(self.out.at[:, self.others], self.recv.at[5])
            return
        self.copy(index).wait_recv()
        before = self.values[:, self.own] if index == 0 else self.held[index - 1]
        self.held[index] = before + self.got[index]
        if index == 4:
            self.out[:, self.own] = self.held[4]
        self.copy(index + 1).start()

    def finish(self):
        for index in range(6):
            self.copy(index).wait_send()


def pair_sum_buffers(rows, width):
    return [
        pltpu.VMEM((5, rows, width // 2), F32),
        pltpu.VMEM((5, rows, width // 2), F32),
        pltpu.SemaphoreType.DMA((6,)),
        pltpu.SemaphoreType.DMA((6,)),
    ]


def back_kernel(
    scale, cuts, d_attn, query, keys, values, mixed, total, out_weights, out_parts, early,
    d_attn_row, d_heads, out_total, early_sum,
    weights, d_mixed_give, d_mixed_row, d_mixed, keys_t, d_keys, d_values, acc, pair_out, pair_in,
    head_give, sum_held, sum_got, sum_send, sum_recv, weight_sem, load_sem,
    near_send, near_recv, head_send, head_recv, back_send, back_recv,
    pair_send, pair_recv, *rest,
):
    here = Here()
    row, col, core = here.row, here.col, here.core
    rows = d_attn.shape[0]
    row_tok = 4 * rows
    group_tok = 4 * row_tok
    plane = 4 * HD
    order = here.near_first[::-1]
    collect = Collect(here, rest[:6], rest[6 : 6 + len(COLLECT_SEMS)])
    sems = rest[6 + len(COLLECT_SEMS) :]

    def row_block(unused_row, place, unused_core):
        return d_attn_row.at[pl.ds(pl.multiple_of(place * rows, rows), rows)]

    spread = Spread(here, row_block(row, col, core), row_block, rows, sems, plane=False)
    pair_sum = PairSum(here, early, early_sum, sum_held, sum_got, sum_send, sum_recv)

    def load(which, place):
        return pltpu.make_async_copy(
            out_parts.at[which, place], collect.mine.at[which, place], load_sem.at[which, place]
        )

    load_weights = pltpu.make_async_copy(out_weights, weights, weight_sem)
    load_weights.start()
    for place in order:
        for which in (3, 2, 1, 0):
            load(which, place).start()
    keys_t[...] = keys[...].T
    d_attn_row[pl.ds(pl.multiple_of(col * rows, rows), rows)] = d_attn[...]
    greet(here.plane_peers() + here.line_peers() + [here.other_core()])

    def give_near(step):
        place = (col + step) % 4
        sems_of = near_send.at[step], near_recv.at[col]
        return remote(d_mixed_give.at[place], d_mixed_row.at[col], *sems_of, here.at_col(place))

    def give_head(step):
        dest = here.rows[step]
        part = pl.ds(pl.multiple_of(dest * HD, HD), HD)
        sems_of = head_send.at[step], head_recv.at[row]
        return remote(d_mixed_row.at[:, :, part], d_mixed.at[row], *sems_of, here.at_row(dest))

    def start(index):
        for which in (3, 2, 1):
            load(which, order[index]).wait()
        collect.start_far(order[index])
        collect.start_near(order[index])

    ends = (col == 0) | (col == 3)

    def from_ends(index):
        @pl.when(ends)
        def _():
            collect.line_step(order[index])

    def from_inside(index):
        @pl.when(jnp.logical_not(ends))
        def _():
            collect.line_step(order[index])

    def plane_part(index):
        load(0, order[index]).wait()
        collect.plane_step(order[index])

    start(0)
    pair_sum.begin()
    load_weights.wait()
    for step in (1, 2, 3, 0):
        place = (col + step) % 4
        part = pl.ds(pl.multiple_of(place * plane, plane), plane)
        product = contract_cols(d_attn[...], weights[part]).astype(BF16)
        if step == 0:
            d_mixed_row[col] = product
        else:
            d_mixed_give[place] = product
            give_near(step).start()
    spread.step(0)
    pair_sum.step(0)
    d_keys[...] = jnp.zeros_like(d_keys)
    d_values[...] = jnp.zeros_like(d_values)
    for step in range(1, 4):
        place = (col + 4 - step) % 4
        arrived(d_mixed_row.at[place], near_recv.at[place])
    for step in range(1, 4):
        give_head(step).start()
    d_mixed[row] = d_mixed_row[:, :, pl.ds(pl.multiple_of(row * HD, HD), HD)]
    collect.corner_step(order[0])
    start(1)
    pair_sum.step(1)
    spread.step(1)
    for source in here.rows[1:]:
        arrived(d_mixed.at[source], head_recv.at[source])

    cut = (cuts[0, 0], cuts[0, 1])
    last_query = 2 * group_tok - row_tok

    def queries(index):
        at = pl.ds(index * row_tok, row_tok)
        first_query = core * group_tok + index * row_tok
        gradient = d_mixed[index].reshape(row_tok, HD)
        delta = jnp.sum((gradient.astype(F32) * mixed[at]).T, axis=0, keepdims=True)
        sums = total[:, at]
        acc[...] = jnp.zeros_like(acc)

        def block_fn(part, scores):
            weight = jnp.exp(scores - sums)
            d_weight = contract_cols(values[part], gradient)
            d_scores = (weight * (d_weight - delta)).astype(BF16)
            d_values[part] += matmul(weight.astype(BF16), gradient)
            d_keys[part] += matmul(d_scores, query[at]) * scale
            acc[...] += matmul(keys_t[:, part], d_scores)

        def scan(block, carry):
            first_key = block * row_tok
            part = pl.ds(pl.multiple_of(first_key, row_tok), row_tok)
            masked = (block == 0) | (first_key == first_query) | (first_query == last_query)

            @pl.when(jnp.logical_not(masked))
            def _():
                block_fn(part, contract_cols(keys[part], query[at]) * scale)

            @pl.when(masked)
            def _():
                key_place = first_key + lax.broadcasted_iota(jnp.int32, (row_tok, row_tok), 0)
                place = first_query + lax.broadcasted_iota(jnp.int32, (1, row_tok), 1)
                allowed = (key_place <= place) & (key_place >= doc_start(place, cut))
                scores = contract_cols(keys[part], query[at]) * scale
                block_fn(part, jnp.where(allowed, scores, MASKED))

            return carry

        lax.fori_loop(0, core * 4 + index + 1, scan, 0)
        head_give[0, index] = (acc[...] * scale).T.astype(BF16)

    queries(0)
    plane_part(0)
    from_ends(0)
    collect.corner_step(order[1])
    start(2)
    spread.step(2)
    queries(1)
    from_inside(0)
    plane_part(1)
    from_ends(1)
    collect.corner_step(order[2])
    start(3)
    pair_sum.step(2)
    queries(2)
    from_inside(1)
    plane_part(2)
    from_ends(2)
    collect.corner_step(order[3])
    spread.step(3)
    queries(3)

    def give_back(step, kind):
        dest = here.rows[step]
        sems_of = back_send.at[step, kind], back_recv.at[kind, row]
        return remote(head_give.at[kind, dest], d_heads.at[row, kind], *sems_of, here.at_row(dest))

    def give_pair(kind):
        sems_of = pair_send.at[kind], pair_recv.at[kind]
        return remote(pair_out.at[kind], pair_in.at[kind], *sems_of, here.other_core())

    for step in range(1, 4):
        give_back(step, 0).start()
    d_heads[row, 0] = head_give[0, row]

    @pl.when(core == 1)
    def _():
        for kind, gradient in enumerate((d_keys, d_values)):
            pair_out[kind] = gradient[pl.ds(0, group_tok)].astype(BF16)
            give_pair(kind).start()
        for kind, gradient in enumerate((d_keys, d_values)):
            for part in range(4):
                at = pl.ds(group_tok + part * row_tok, row_tok)
                head_give[kind + 1, part] = gradient[at].astype(BF16)

    from_inside(2)
    plane_part(3)
    pair_sum.step(3)

    @pl.when(core == 0)
    def _():
        for kind, gradient in enumerate((d_keys, d_values)):
            give_pair(kind).wait_recv()
            for part in range(4):
                at = pl.ds(part * row_tok, row_tok)
                summed = gradient[at] + pair_in[kind, at].astype(F32)
                head_give[kind + 1, part] = summed.astype(BF16)

    for kind in (1, 2):
        for step in range(1, 4):
            give_back(step, kind).start()
        d_heads[row, kind] = head_give[kind, row]
    pair_sum.step(4)
    pair_sum.step(5)
    collect.own_step()
    out_total[...] = collect.mine[0, col]
    for source in here.rows[1:]:
        for kind in range(3):
            arrived(d_heads.at[source, kind], back_recv.at[kind, source])
    for step in range(1, 4):
        give_near(step).wait_send()
        give_head(step).wait_send()
        for kind in range(3):
            give_back(step, kind).wait_send()

    @pl.when(core == 1)
    def _():
        for kind in range(2):
            give_pair(kind).wait_send()

    pair_sum.finish()
    spread.finish()
    collect.finish()


def attend_back_stage(
    d_attn, query, keys, values, mixed, total, cuts, out_weights, out_parts, early, scale, collective_id
):
    rows, width = d_attn.shape
    row_tok, group_tok = 4 * rows, 16 * rows
    vmem, hbm = pl.BlockSpec(memory_space=pltpu.VMEM), pl.BlockSpec(memory_space=pl.ANY)
    dma = pltpu.SemaphoreType.DMA
    return pl.pallas_call(
        functools.partial(back_kernel, scale),
        in_specs=[pl.BlockSpec(memory_space=pltpu.SMEM)] + [vmem] * 6 + [hbm] * 2 + [vmem],
        out_specs=[vmem] * 4,
        out_shape=[
            jax.ShapeDtypeStruct((row_tok, width), BF16),
            jax.ShapeDtypeStruct((4, 3, row_tok, HD), BF16),
            jax.ShapeDtypeStruct((rows, width), BF16),
            jax.ShapeDtypeStruct(early.shape, F32),
        ],
        scratch_shapes=[
            pltpu.VMEM((width, width), BF16),
            pltpu.VMEM((4, rows, 4 * HD), BF16),
            pltpu.VMEM((4, rows, 4 * HD), BF16),
            pltpu.VMEM((4, 4, rows, HD), BF16),
            pltpu.VMEM((HD, 2 * group_tok), BF16),
            pltpu.VMEM((2 * group_tok, HD), F32),
            pltpu.VMEM((2 * group_tok, HD), F32),
            pltpu.VMEM((HD, row_tok), F32),
            pltpu.VMEM((2, group_tok, HD), BF16),
            pltpu.VMEM((2, group_tok, HD), BF16),
            pltpu.VMEM((3, 4, row_tok, HD), BF16),
        ]
        + pair_sum_buffers(*early.shape)
        + [
            dma, dma((4, 4)), dma((4,)), dma((4,)), dma((4,)), dma((4,)),
            dma((4, 3)), dma((3, 4)), dma((2,)), dma((2,)),
        ]
        + collect_buffers(rows, width)
        + COLLECT_SEMS
        + SPREAD_SEMS,
        compiler_params=pltpu.CompilerParams(
            collective_id=collective_id, has_side_effects=True, vmem_limit_bytes=58 * 2**20
        ),
    )(cuts[None], d_attn, query, keys, values, mixed, total, out_weights, out_parts, early)


def tail_kernel(
    d_heads, qkv, totals, q_gain, k_gain, cosine, sine, weights_in, normed_in, mixed_rows, d_attn_in,
    hidden, gain, d_middle,
    grad_hidden, grad_qkv, grad_out, late_sum, last_sum,
    weights, normed, d_attn, in_sem, last, last_got, last_send, last_recv, hop, hop_got, hop_send, hop_recv,
    d_qkv, late, grads, mixed, units, stat, scales, sums, sum_held, sum_got, sum_send, sum_recv,
    stat_send, stat_recv,
    line, line_in, whole, give, other, plane, corner_one, corner_two, from_across, from_along,
    up_send, down_send, line_recv, other_send, other_recv,
    one_send, one_recv, two_send, two_recv, across_send, across_recv, along_send, along_recv,
    back_send, back_recv,
):
    here = Here()
    row, col, core = here.row, here.col, here.core
    rows = hidden.shape[0]
    depth, columns = grads.shape
    part = depth // 2
    first, second = pl.ds(0, part // 2), pl.ds(part // 2, part // 2)
    order = here.near_first[::-1]
    qkv_columns = d_qkv.shape[1]
    tile = 512

    def line_products():
        @pl.loop(0, weights.shape[0] // tile)
        def _(index):
            at = pl.ds(pl.multiple_of(index * tile, tile), tile)
            product = contract_cols(d_qkv[...], weights[at]).astype(BF16)
            line[:, :, at] = product.reshape(4, rows, tile)

    line_halves = (pl.ds(0, rows // 2), pl.ds(rows // 2, rows // 2))

    def give_up(place, half):
        at = line_halves[half]
        sems = up_send.at[half, place], line_recv.at[half, place]
        return remote(line.at[place, at], line_in.at[place, at], *sems, here.at_col(col + 1))

    def give_down(place, slot, half):
        at = line_halves[half]
        sems = down_send.at[half, place], line_recv.at[half, slot]
        return remote(line.at[place, at], line_in.at[slot, at], *sems, here.at_col(col - 1))

    def add_line(place, slot, half):
        at = line_halves[half]
        arrived(line_in.at[slot, at], line_recv.at[half, slot])
        add_into(line.at[place, at], line_in.at[slot, at])

    def line_step(place):
        for half in range(2):

            @pl.when(((place > col) & (col > 0)) | ((place < col) & (col < 3)))
            def _():
                add_line(place, place, half)

            @pl.when(place > col)
            def _():
                give_up(place, half).start()

            @pl.when(place < col - 1)
            def _():
                give_down(place, place, half).start()

            @pl.when(place == col - 1)
            def _():
                give_down(place, 4, half).start()

    def row_product(which):
        of_row = here.rows[which]
        at = pl.ds(pl.multiple_of(of_row * depth, depth), depth)
        whole[:, pl.ds(0, qkv_columns)] = transposed_product(normed[:, at], d_qkv[...]).astype(BF16)
        whole[:, pl.ds(qkv_columns, columns - qkv_columns)] = transposed_product(
            mixed[...], d_attn[:, at]
        ).astype(BF16)
        plane[which] = whole[pl.ds(pl.multiple_of(core * part, part), part)]
        give[which] = whole[pl.ds(pl.multiple_of((1 - core) * part, part), part)]
        to_core(which).start()

    def to_core(which):
        sems = other_send.at[which], other_recv.at[which]
        return remote(give.at[which], other.at[which], *sems, here.other_core())

    def own_sum(which):
        to_core(which).wait_recv()
        add_into(plane.at[which], other.at[which])

    give_one = remote(
        plane.at[3, first], corner_one, one_send, one_recv, here.at_row(here.across)
    )
    give_two = remote(
        plane.at[3, second], corner_two, two_send, two_recv, here.at_row(here.along)
    )

    def give_across(index):
        at = (first, second)[index]
        sems = across_send.at[index], across_recv.at[index]
        return remote(plane.at[1, at], from_across.at[at], *sems, here.at_row(here.across))

    def give_along(index):
        at = (first, second)[index]
        sems = along_send.at[index], along_recv.at[index]
        return remote(plane.at[2, at], from_along.at[at], *sems, here.at_row(here.along))

    pair_sum = PairSum(here, late, late_sum, sum_held, sum_got, sum_send, sum_recv)
    takes = [
        pltpu.make_async_copy(source, target, in_sem.at[index])
        for index, (source, target) in enumerate(
            ((weights_in, weights), (normed_in, normed), (d_attn_in, d_attn))
        )
    ]
    for take in takes:
        take.start()
    near = [(step // 2, step % 2) for step in range(1, 8)]

    def near_device(step):
        which, swap = near[step]
        return (here.rows[which], col, (core + swap) % 2)

    greet([near_device(step) for step in range(7)] + here.line_peers())

    width = hidden.shape[1]
    heads = d_heads.shape[0]
    row_tok = d_qkv.shape[0]
    late[...] = jnp.zeros_like(late)
    for kind in range(2):
        root = lax.rsqrt(totals[kind : kind + 1] / width + EPSILON)
        scales[kind] = jnp.broadcast_to(root, (HD, row_tok)).T
        square = jnp.zeros((row_tok, HD), F32)
        for head in range(heads):
            start = (head * 3 + kind) * HD
            raw = qkv[:, start : start + HD]
            given = d_heads[head, kind].astype(F32)
            unit = given * cosine[...] + pltpu.roll(given * sine[...], HD // 2, 1)
            gains = (q_gain, k_gain)[kind][:, head * HD : (head + 1) * HD]
            gain_sum = jnp.sum(unit * raw * scales[kind], axis=0, keepdims=True)
            place = pl.ds(pl.multiple_of((col * heads + head) * HD, HD), HD)
            late[kind : kind + 1, place] = gain_sum
            weighted = unit * gains
            square = square + weighted * raw
            units[kind, head] = weighted
        stat[col, kind : kind + 1] = jnp.sum(square.T, axis=0, keepdims=True)

    def give_stat(step):
        peer = here.line_peers()[step]
        return remote(stat.at[col], stat.at[col], stat_send.at[step], stat_recv.at[col], peer)

    for step in range(3):
        give_stat(step).start()
    for head in range(heads):
        d_qkv[:, (head * 3 + 2) * HD : (head * 3 + 3) * HD] = d_heads[head, 2]
        mixed[:, head * HD : (head + 1) * HD] = mixed_rows[head]
    for step in range(3):
        place = (col + step + 1) % 4
        arrived(stat.at[place], stat_recv.at[place])
    total = stat[0] + stat[1] + stat[2] + stat[3]
    for kind in range(2):
        sums[...] = jnp.broadcast_to(total[kind : kind + 1] / width, (HD, row_tok)).T
        for head in range(heads):
            start = (head * 3 + kind) * HD
            raw = qkv[:, start : start + HD]
            root = scales[kind]
            d_raw = root * units[kind, head] - raw * (root * root * root) * sums[...]
            d_qkv[:, start : start + HD] = d_raw.astype(BF16)
    ends = (col == 0) | (col == 3)
    pair_sum.begin()
    for take in takes:
        take.wait()
    line_products()

    @pl.when(ends)
    def _():
        for place in order[:3]:
            line_step(place)

    def inner_step(place):
        @pl.when(jnp.logical_not(ends))
        def _():
            line_step(place)

    row_product(3)
    row_product(1)
    pair_sum.step(0)
    inner_step(order[0])
    own_sum(3)
    give_one.start()
    give_two.start()
    row_product(2)
    pair_sum.step(1)
    own_sum(1)
    give_across(0).start()
    own_sum(2)
    give_along(1).start()
    inner_step(order[1])
    row_product(0)
    pair_sum.step(2)
    inner_step(order[2])
    give_two.wait_recv()
    add_into(plane.at[1, second], corner_two)
    give_across(1).start()
    give_one.wait_recv()
    add_into(plane.at[2, first], corner_one)
    give_along(0).start()
    own_sum(0)

    for half in range(2):

        @pl.when(col > 0)
        def _():
            add_line(col, col, half)

        @pl.when(col < 3)
        def _():
            add_line(col, 4, half)

    given = line[col].astype(F32)
    tokens = hidden[...].astype(F32)
    root = lax.rsqrt(jnp.mean(tokens * tokens, axis=1, keepdims=True) + EPSILON)
    part_sum = jnp.sum(given * tokens * root, axis=0, keepdims=True)
    eighth = width // 8
    me = row * 2 + core
    for index in range(8):
        last[index : index + 1] = part_sum[:, index * eighth : (index + 1) * eighth]

    def give_last(step):
        sems = last_send.at[step], last_recv.at[me]
        return remote(last, last_got.at[me], *sems, near_device(step))

    def give_hop(step):
        sems = hop_send.at[step], hop_recv.at[col]
        return remote(hop, hop_got.at[col], *sems, here.line_peers()[step])

    for step in range(7):
        give_last(step).start()
    last_got[me] = last[...]
    weighted = given * gain[...].astype(F32)
    inner = jnp.mean(weighted * tokens, axis=1, keepdims=True)
    grad_hidden[...] = d_middle[...] + root * weighted - tokens * (root * root * root) * inner
    pair_sum.step(3)
    for step in range(7):
        which, swap = near[step]
        source = here.rows[which] * 2 + (core + swap) % 2
        arrived(last_got.at[source], last_recv.at[source])
    held = last_got[0]
    for index in range(1, 8):
        held = held + last_got[index]
    hop[...] = held
    hop_got[col] = held
    for step in range(3):
        give_hop(step).start()
    pair_sum.step(4)
    for index in range(2):
        give_across(index).wait_recv()
        give_along(index).wait_recv()
    add_into(plane.at[0], from_across, from_along)
    own_half = pl.ds(pl.multiple_of(core * part, part), part)
    give_back = remote(
        plane.at[0], grads.at[own_half], back_send, back_recv, here.other_core()
    )
    give_back.start()
    grads[own_half] = plane[0]
    other_half = grads.at[pl.ds(pl.multiple_of((1 - core) * part, part), part)]
    pair_sum.step(5)
    for step in range(3):
        place = (col + step + 1) % 4
        arrived(hop_got.at[place], hop_recv.at[place])
    last_sum[...] = hop_got[0] + hop_got[1] + hop_got[2] + hop_got[3]
    arrived(other_half, back_recv)
    grad_qkv[...] = grads[:, pl.ds(0, qkv_columns)].astype(F32)
    grad_out[...] = grads[:, pl.ds(qkv_columns, columns - qkv_columns)].astype(F32)
    for step in range(7):
        give_last(step).wait_send()
    for step in range(3):
        give_hop(step).wait_send()
    pair_sum.finish()
    for step in range(3):
        give_stat(step).wait_send()
    give_back.wait_send()
    give_one.wait_send()
    give_two.wait_send()
    for index in range(2):
        give_across(index).wait_send()
        give_along(index).wait_send()
    for which in range(4):
        to_core(which).wait_send()
    for place in order:
        for half in range(2):

            @pl.when(place > col)
            def _():
                give_up(place, half).wait_send()

            @pl.when(place < col)
            def _():
                give_down(place, place, half).wait_send()


def tail_stage(
    d_heads, qkv, totals, q_gain, k_gain, cosine, sine, weights, normed, mixed_rows, d_attn,
    hidden, gain, d_middle, collective_id,
):
    row_tok, qkv_columns = qkv.shape
    rows, width = hidden.shape
    depth = width // 4
    out_columns = width // 4
    columns = qkv_columns + out_columns
    part = depth // 2
    heads = d_heads.shape[0]
    vmem, hbm = pl.BlockSpec(memory_space=pltpu.VMEM), pl.BlockSpec(memory_space=pl.ANY)
    dma = pltpu.SemaphoreType.DMA
    eighth = (8, width // 8)
    one, four = pltpu.SemaphoreType.DMA, pltpu.SemaphoreType.DMA((4,))
    two = pltpu.SemaphoreType.DMA((2,))
    three = pltpu.SemaphoreType.DMA((3,))
    return pl.pallas_call(
        tail_kernel,
        in_specs=[vmem] * 7 + [hbm] * 2 + [vmem, hbm] + [vmem] * 3,
        out_specs=[vmem] * 5,
        out_shape=[
            jax.ShapeDtypeStruct((rows, width), F32),
            jax.ShapeDtypeStruct((depth, qkv_columns), F32),
            jax.ShapeDtypeStruct((depth, out_columns), F32),
            jax.ShapeDtypeStruct((8, width), F32),
            jax.ShapeDtypeStruct(eighth, F32),
        ],
        scratch_shapes=[
            pltpu.VMEM(weights.shape, BF16),
            pltpu.VMEM(normed.shape, BF16),
            pltpu.VMEM(d_attn.shape, BF16),
            dma((3,)),
            pltpu.VMEM(eighth, F32),
            pltpu.VMEM((8,) + eighth, F32),
            dma((7,)),
            dma((8,)),
            pltpu.VMEM(eighth, F32),
            pltpu.VMEM((4,) + eighth, F32),
            dma((3,)),
            dma((4,)),
            pltpu.VMEM((row_tok, qkv_columns), BF16),
            pltpu.VMEM((8, width), F32),
            pltpu.VMEM((depth, columns), BF16),
            pltpu.VMEM((row_tok, heads * HD), BF16),
            pltpu.VMEM((2, heads, row_tok, HD), F32),
            pltpu.VMEM((4, 8, row_tok), F32),
            pltpu.VMEM((2, row_tok, HD), F32),
            pltpu.VMEM((row_tok, HD), F32),
        ]
        + pair_sum_buffers(8, width)
        + [
            three, four,
            pltpu.VMEM((4, rows, width), BF16),
            pltpu.VMEM((5, rows, width), BF16),
            pltpu.VMEM((depth, columns), BF16),
            pltpu.VMEM((4, part, columns), BF16),
            pltpu.VMEM((4, part, columns), BF16),
            pltpu.VMEM((4, part, columns), BF16),
            pltpu.VMEM((part // 2, columns), BF16),
            pltpu.VMEM((part // 2, columns), BF16),
            pltpu.VMEM((part, columns), BF16),
            pltpu.VMEM((part, columns), BF16),
            dma((2, 4)), dma((2, 4)), dma((2, 5)), four, four,
            one, one, one, one, two, two, two, two,
            one, one,
        ],
        compiler_params=pltpu.CompilerParams(
            collective_id=collective_id, has_side_effects=True, vmem_limit_bytes=58 * 2**20
        ),
    )(
        d_heads, qkv, totals, q_gain, k_gain, cosine, sine, weights, normed, mixed_rows, d_attn,
        hidden, gain[None], d_middle,
    )


def expert_rows(rows, grads, gate, gate_w, up_w, down_w):
    pre_gate = matmul(rows, gate_w)
    pre_up = matmul(rows, up_w)
    back = contract_cols(grads, down_w)
    sigmoid_gate = jax.nn.sigmoid(pre_gate)
    silu_gate = pre_gate * sigmoid_gate
    hidden = (silu_gate * pre_up).astype(BF16)
    inner = jnp.sum(hidden.astype(F32) * back, axis=-1)
    weighted = (hidden.astype(F32) * gate).astype(BF16)
    d_hid = back * gate
    d_pregate = (d_hid * pre_up * (sigmoid_gate + silu_gate * (1.0 - sigmoid_gate))).astype(BF16)
    d_preup = (d_hid * silu_gate).astype(BF16)
    outputs = matmul(weighted, down_w).astype(BF16)
    d_rows = (contract_cols(d_pregate, gate_w) + contract_cols(d_preup, up_w)).astype(BF16)
    return (
        outputs,
        d_rows,
        inner,
        contract_rows(rows, d_pregate),
        contract_rows(rows, d_preup),
        contract_rows(weighted, grads),
    )


def experts(normed, grads, dense_gates, gate_w, up_w, down_w):
    rows_dev, width = normed.shape
    devices = math.prod(lax.axis_size(axis) for axis in ALL)
    expert_count = dense_gates.shape[1]
    expert = lax.axis_index(ALL) // 2
    parts = max(1, lax.axis_size("exp") // 2)
    step = rows_dev // parts

    def one_part(sums, piece):
        rows, grad_rows, gates = piece
        rows_all = lax.all_gather(rows, ALL, axis=0, tiled=True)
        grads_all = lax.all_gather(grad_rows, ALL, axis=0, tiled=True)
        gates_all = lax.all_gather(gates, ALL, axis=0, tiled=True)
        gate = lax.dynamic_slice_in_dim(gates_all, expert, 1, 1)
        got = expert_rows(rows_all, grads_all, gate, gate_w, up_w, down_w)
        outputs = lax.psum_scatter(got[0], ALL, scatter_dimension=0, tiled=True)
        d_rows = lax.psum_scatter(got[1], ALL, scatter_dimension=0, tiled=True)
        inner = lax.all_to_all(
            got[2].reshape(devices, step), ALL, split_axis=0, concat_axis=0, tiled=True
        )
        inner = inner.reshape(expert_count, 2, step).sum(axis=1).T
        sums = got[3:] if sums is None else tuple(a + b for a, b in zip(sums, got[3:]))
        return sums, (outputs, d_rows, inner)

    if parts == 1:
        sums, (outputs, d_rows, inner) = one_part(None, (normed, grads, dense_gates))
    else:
        start = tuple(jnp.zeros(w.shape, F32) for w in (gate_w, up_w, down_w))
        pieces = tuple(v.reshape(parts, step, -1) for v in (normed, grads, dense_gates))
        sums, got = lax.scan(one_part, start, pieces)
        outputs, d_rows, inner = (v.reshape(rows_dev, -1) for v in got)
    return outputs.astype(F32), d_rows.astype(F32), inner, sums


def experts_here(normed, grads_all, picks, router, halves, others):
    numbers = jnp.arange(router.shape[1], dtype=jnp.int32)
    mask = jnp.any(picks.T[None] == numbers[:, None, None], axis=1).astype(F32)
    out_parts, d_rows, inner, weights = expert_stage(
        normed, grads_all, mask, halves, others, router, 1
    )
    inner = inner[:, :, 0].reshape(router.shape[1], -1).T
    return out_parts, d_rows.astype(F32), inner, weights


def shards(
    hidden_in,
    out_grad,
    attn_gain,
    w_qkv,
    q_gain,
    k_gain,
    w_out,
    moe_gain,
    router,
    w_gate,
    w_up,
    w_down,
    routes,
    doc_cuts,
):
    row_count, col_count = lax.axis_size("row"), lax.axis_size("col")
    tokens = hidden_in[0].astype(F32)
    rows_dev, width = tokens.shape
    heads = w_qkv.shape[1] // (3 * HD)
    plane = heads * HD
    scale = HD ** (-0.5)
    side = lax.axis_index("exp") % 2
    row_tok = rows_dev * col_count
    group_tok = row_tok * row_count
    cuts = lax.dynamic_index_in_dim(doc_cuts, lax.axis_index("exp") // 2, 0, keepdims=False)

    here = (row_count, col_count, lax.axis_size("exp")) == (4, 4, 2)

    if here:
        grads_all = lax.all_gather(out_grad[0], ("row", "col"), axis=0, tiled=True)
        other_w = [lax.ppermute(w[0], "exp", [(0, 1), (1, 0)]) for w in (w_gate, w_up, w_down)]

    gain_one = attn_gain.astype(F32)
    scale_one = rms_scale(tokens)
    head_start = lax.axis_index("col") * plane
    gain_q = lax.dynamic_slice_in_dim(q_gain, head_start, plane, 0).astype(F32)
    gain_k = lax.dynamic_slice_in_dim(k_gain, head_start, plane, 0).astype(F32)
    row_places = side * group_tok + lax.axis_index("row") * row_tok + jnp.arange(row_tok, dtype=jnp.int32)
    unused_doc, position = doc_positions(row_places, cuts)
    cosine, sine = rope_tables(position, HD)
    if here:
        signed = jnp.concatenate([-sine[:, : HD // 2], sine[:, HD // 2 :]], axis=1)
        normed_row, qkv_w, qkv, totals, query, keys, values = project(
            hidden_in[0], attn_gain, w_qkv, gain_q[None], gain_k[None], cosine, signed, 0
        )
        total_q, total_k = totals[0], totals[1]
        query = query.reshape(group_tok, HD)
        key_all, value_all = keys.reshape(-1, HD), values.reshape(-1, HD)
    else:
        normed_one = (tokens * scale_one * gain_one).astype(BF16)
        normed_row = lax.all_gather(normed_one, "col", axis=0, tiled=True)
        qkv_w = lax.all_gather(w_qkv, "row", axis=0, tiled=True)
        out_w = lax.all_gather(
            lax.all_gather(w_out, "row", axis=1, tiled=True), "col", axis=0, tiled=True
        )
        qkv = matmul(normed_row, qkv_w)
    qkv = qkv.reshape(row_tok, heads, 3, HD)
    query_raw, key_raw, value_raw = qkv[:, :, 0], qkv[:, :, 1], qkv[:, :, 2]
    if not here:
        total_q, total_k = lax.psum(
            (jnp.sum(query_raw * query_raw, axis=(1, 2)), jnp.sum(key_raw * key_raw, axis=(1, 2))),
            "col",
        )
    scale_q = lax.rsqrt(total_q / width + EPSILON)[:, None, None]
    scale_k = lax.rsqrt(total_k / width + EPSILON)[:, None, None]
    gain_q, gain_k = gain_q.reshape(heads, HD), gain_k.reshape(heads, HD)
    cosine, sine = cosine[:, None, :], sine[:, None, :]
    if not here:
        query = rotate(query_raw * scale_q * gain_q, cosine, sine).astype(BF16)
        key = rotate(key_raw * scale_k * gain_k, cosine, sine).astype(BF16)
        moved = rows_to_heads(jnp.concatenate([query, key, value_raw.astype(BF16)], axis=-1))
        query, own_pair = moved[:, :HD], moved[:, HD:]
        earlier_pair = from_behind(own_pair, "exp", 1)
        lower_pair = jnp.where(side == 0, own_pair, earlier_pair)
        upper_pair = jnp.where(side == 0, jnp.zeros_like(own_pair), own_pair)
        key_value = jnp.concatenate([lower_pair, upper_pair], axis=0)
        key_all, value_all = key_value[:, :HD], key_value[:, HD:]

    if here:
        mixed_wide, total, out_w, mixed_rows, middle, normed_two = attention_stage(
            query, key_all, value_all, cuts, w_out, hidden_in[0], moe_gain, scale, 4
        )
    else:
        mixed_wide, total = attend(query, key_all, value_all, cuts, scale)
        mixed = mixed_wide.astype(BF16)
        middle = tokens + matmul(heads_to_tokens(mixed), out_w)

    gain_two = moe_gain.astype(F32)
    scale_two = rms_scale(middle)
    if not here:
        normed_two = (middle * scale_two * gain_two).astype(BF16)
    gates_all = jax.nn.softmax(matmul(normed_two, router), axis=-1)
    picks = routes[0]
    chosen = jnp.any(
        picks[:, :, None] == jnp.arange(router.shape[1], dtype=jnp.int32)[None, None, :], axis=1
    )
    grad_out = out_grad[0].astype(F32)
    expert_w = (w_gate[0], w_up[0], w_down[0])
    if here:
        out_parts, d_normed_two, inner, weight_grads = experts_here(
            normed_two, grads_all, picks, router, expert_w, other_w
        )
    else:
        dense_gates = jnp.where(chosen, gates_all, 0.0)
        mixture, d_normed_two, inner, weight_grads = experts(
            normed_two, out_grad[0], dense_gates, *expert_w
        )
    dense = jnp.where(chosen, inner, 0.0)
    d_logits = (gates_all * (dense - jnp.sum(gates_all * dense, axis=-1, keepdims=True))).astype(BF16)
    grad_router = contract_rows(d_logits, normed_two)
    d_normed_two = d_normed_two + contract_cols(d_logits, router)
    grad_moe_gain = jnp.sum(d_normed_two * middle * scale_two, axis=0)
    weighted_two = d_normed_two * gain_two
    d_middle = (
        grad_out
        + scale_two * weighted_two
        - middle * scale_two**3 * jnp.mean(weighted_two * middle, axis=-1, keepdims=True)
    )

    d_attn = d_middle.astype(BF16)
    if here:
        early = jnp.concatenate([grad_moe_gain[None], jnp.zeros((7, width), F32), grad_router])
        d_attn_row, d_heads, mixture, early = attend_back_stage(
            d_attn, query, key_all, value_all, mixed_wide, total, cuts, out_w, out_parts, early, scale, 2
        )
        grad_hidden, grad_qkv, grad_w_out, late, last = tail_stage(
            d_heads, qkv.reshape(row_tok, -1), totals, gain_q.reshape(1, -1), gain_k.reshape(1, -1),
            cosine[:, 0], signed, qkv_w, normed_row, mixed_rows, d_attn_row,
            hidden_in[0], attn_gain, d_middle, 3,
        )
        final = middle + mixture.astype(F32)
        summed = (last.reshape(-1), late[0], late[1], early[0], early[8:])
    else:
        final = middle + mixture
        mixed_row = heads_to_rows(mixed).reshape(row_tok, plane)
        d_mixed = tokens_to_heads(contract_cols(d_attn, out_w).astype(BF16))
        d_attn_row = lax.all_gather(d_attn, "col", axis=0, tiled=True)
        d_query, acc_key, acc_value = attend_back(
            query, key_all, value_all, d_mixed, mixed_wide, total, cuts, scale
        )
        accumulated = jnp.concatenate([acc_key, acc_value], axis=1)
        lower_acc, upper_acc = accumulated[:group_tok], accumulated[group_tok:]
        kept_acc = jnp.where(side == 0, lower_acc, upper_acc)
        later_acc = from_behind(lower_acc.astype(BF16), "exp", -1).astype(F32)
        summed_pair = kept_acc + jnp.where(side == 0, later_acc, jnp.zeros_like(later_acc))
        d_heads = heads_to_rows(jnp.concatenate([d_query, summed_pair], axis=1).astype(BF16)).astype(F32)
        d_q_unit = rotate_back(d_heads[:, :, :HD], cosine, sine)
        d_k_unit = rotate_back(d_heads[:, :, HD : 2 * HD], cosine, sine)
        d_value = d_heads[:, :, 2 * HD :]
        weighted_q = d_q_unit * gain_q
        weighted_k = d_k_unit * gain_k
        sum_q, sum_k = lax.psum(
            (jnp.sum(weighted_q * query_raw, axis=(1, 2)), jnp.sum(weighted_k * key_raw, axis=(1, 2))),
            "col",
        )
        d_query_raw = scale_q * weighted_q - query_raw * scale_q**3 * (sum_q / width)[:, None, None]
        d_key_raw = scale_k * weighted_k - key_raw * scale_k**3 * (sum_k / width)[:, None, None]
        grad_q_part = jnp.sum(d_q_unit * query_raw * scale_q, axis=0).reshape(plane)
        grad_k_part = jnp.sum(d_k_unit * key_raw * scale_k, axis=0).reshape(plane)
        d_qkv = jnp.concatenate([d_query_raw, d_key_raw, d_value], axis=2).astype(BF16)
        d_qkv = d_qkv.reshape(row_tok, heads * 3 * HD)
        d_normed_one = lax.psum_scatter(
            contract_cols(d_qkv, qkv_w).astype(BF16), "col", scatter_dimension=0, tiled=True
        ).astype(F32)
        grad_qkv = lax.psum_scatter(
            contract_rows(normed_row, d_qkv).astype(BF16), "row", scatter_dimension=0, tiled=True
        )
        grad_w_out = lax.psum_scatter(
            contract_rows(mixed_row, d_attn_row).astype(BF16), "row", scatter_dimension=1, tiled=True
        )
        grad_qkv = lax.psum(grad_qkv, "exp").astype(F32)
        grad_w_out = lax.psum(grad_w_out, "exp").astype(F32)
        grad_attn_gain = jnp.sum(d_normed_one * tokens * scale_one, axis=0)
        weighted_one = d_normed_one * gain_one
        grad_hidden = (
            d_middle
            + scale_one * weighted_one
            - tokens * scale_one**3 * jnp.mean(weighted_one * tokens, axis=-1, keepdims=True)
        )
        empty = jnp.zeros((width,), F32)
        grad_q_full = lax.dynamic_update_slice_in_dim(empty, grad_q_part, head_start, 0)
        grad_k_full = lax.dynamic_update_slice_in_dim(empty, grad_k_part, head_start, 0)
        parts = (grad_attn_gain, grad_q_full, grad_k_full, grad_moe_gain)
        summed = lax.psum(parts + (grad_router,), ALL)
    return (
        final.astype(BF16)[None],
        grad_hidden[None],
        summed[0],
        grad_qkv,
        summed[1],
        summed[2],
        grad_w_out,
        summed[3],
        summed[4].T,
        weight_grads[0][None],
        weight_grads[1][None],
        weight_grads[2][None],
    )


def solution(mesh):
    token_spec = P("exp", ("row", "col"), None)
    expert_spec = P(("row", "col", "exp"), None, None)
    in_specs = (
        token_spec,
        token_spec,
        P(),
        P("row", "col"),
        P(),
        P(),
        P("col", "row"),
        P(),
        P(),
        expert_spec,
        expert_spec,
        expert_spec,
        token_spec,
        P(),
    )
    out_specs = (
        token_spec,
        token_spec,
        P(),
        P("row", "col"),
        P(),
        P(),
        P("col", "row"),
        P(),
        P(),
        expert_spec,
        expert_spec,
        expert_spec,
    )
    return jax.shard_map(shards, mesh=mesh, in_specs=in_specs, out_specs=out_specs, check_vma=False)
```

```python
import functools
import math

import jax
import jax.numpy as jnp
from jax import lax
from jax.experimental import pallas as pl
from jax.experimental.pallas import tpu as pltpu
from jax.sharding import PartitionSpec as P

HD = 128
EPSILON = 1e-05
ROPE_BASE = 10000.0
MASKED = -1e30
BF16 = jnp.bfloat16
F32 = jnp.float32


def matmul(left, right):
    return jnp.dot(left, right, preferred_element_type=F32)


def contract_rows(left, right):
    return lax.dot_general(left, right, (((0,), (0,)), ((), ())), preferred_element_type=F32)


def contract_cols(left, right):
    return lax.dot_general(left, right, (((1,), (1,)), ((), ())), preferred_element_type=F32)


def rms_scale(values):
    return lax.rsqrt(jnp.mean(values * values, axis=-1, keepdims=True) + EPSILON)


def rope_tables(position, width):
    frequency = ROPE_BASE ** (-jnp.arange(0, width, 2, dtype=F32) / width)
    angle = position.astype(F32)[:, None] * frequency[None, :]
    return (
        jnp.concatenate([jnp.cos(angle)] * 2, axis=-1),
        jnp.concatenate([jnp.sin(angle)] * 2, axis=-1),
    )


def rotate(values, cosine, sine):
    half = values.shape[-1] // 2
    turned = jnp.concatenate([-values[..., half:], values[..., :half]], axis=-1)
    return values * cosine + turned * sine


def rotate_back(values, cosine, sine):
    half = values.shape[-1] // 2
    turned = values * sine
    return values * cosine + jnp.concatenate([turned[..., half:], -turned[..., :half]], axis=-1)


def doc_positions(places, cuts):
    first = (places >= cuts[0]).astype(jnp.int32)
    second = (places >= cuts[1]).astype(jnp.int32)
    start = first * cuts[0] + second * (cuts[1] - cuts[0])
    return (first + second, places - start)


def from_behind(value, axis, steps):
    count = lax.axis_size(axis)
    initial, last = (max(0, -steps), min(count, count - steps))
    return lax.ppermute(value, axis, [(source, source + steps) for source in range(initial, last)])


def rows_to_heads(values):
    count = lax.axis_size("row")
    rows, heads, width = values.shape
    moved = lax.all_to_all(values.transpose(1, 0, 2), "row", split_axis=0, concat_axis=0, tiled=True)
    return moved.reshape(count * rows, width)


def heads_to_rows(values):
    count = lax.axis_size("row")
    rows, width = values.shape
    moved = lax.all_to_all(
        values.reshape(count, rows // count, width), "row", split_axis=0, concat_axis=0, tiled=True
    )
    return moved.transpose(1, 0, 2)


def heads_to_tokens(values):
    row_count, col_count = lax.axis_size("row"), lax.axis_size("col")
    rows = values.shape[0] // (row_count * col_count)
    moved = lax.all_to_all(
        values.reshape(row_count * col_count, rows, HD),
        ("row", "col"),
        split_axis=0,
        concat_axis=0,
        tiled=True,
    )
    moved = moved.reshape(row_count, col_count, rows, HD).transpose(2, 1, 0, 3)
    return moved.reshape(rows, row_count * col_count * HD)


def tokens_to_heads(values):
    row_count, col_count = lax.axis_size("row"), lax.axis_size("col")
    rows = values.shape[0]
    parted = values.reshape(rows, col_count, row_count, HD).transpose(2, 1, 0, 3)
    moved = lax.all_to_all(
        parted.reshape(row_count * col_count, rows, HD),
        ("row", "col"),
        split_axis=0,
        concat_axis=0,
        tiled=True,
    )
    return moved.reshape(row_count * col_count * rows, HD)


MESH = pl.DeviceIdType.MESH
ALL = ("row", "col", "exp")


class Here:
    def __init__(self):
        self.row, self.col, self.core = (lax.axis_index(axis) for axis in ALL)
        self.across = self.row + 1 - 2 * (self.row % 2)
        self.along = (self.row + 2) % 4
        self.opposite = 3 - self.row
        self.rows = (self.row, self.across, self.along, self.opposite)
        half = self.col // 2
        self.near_first = [
            self.col,
            1 + self.col % 2,
            2 - self.col - self.col % 2 + 3 * half,
            3 - 3 * half,
        ]

    def at_row(self, row):
        return (row, self.col, self.core)

    def at_col(self, col):
        return (self.row, col, self.core)

    def other_core(self):
        return (self.row, self.col, 1 - self.core)

    def line_peers(self):
        return [self.at_col((self.col + step) % 4) for step in (1, 2, 3)]

    def group_peers(self):
        steps = range(1, 16)
        return [((self.row + s // 4) % 4, (self.col + s) % 4, self.core) for s in steps]

    def plane_peers(self):
        return [self.at_row(row) for row in self.rows[1:]]


def greet(peers):
    barrier = pltpu.get_barrier_semaphore()
    for peer in peers:
        pl.semaphore_signal(barrier, inc=1, device_id=peer, device_id_type=MESH)
    pl.semaphore_wait(barrier, len(peers))


def greet_near(here):
    barrier = pltpu.get_barrier_semaphore()
    col = here.col

    def signal(peer):
        pl.semaphore_signal(barrier, inc=1, device_id=peer, device_id_type=MESH)

    for peer in (here.other_core(), here.at_row(here.across), here.at_row(here.along)):
        signal(peer)

    @pl.when(col > 0)
    def _():
        signal(here.at_col(col - 1))

    @pl.when(col < 3)
    def _():
        signal(here.at_col(col + 1))

    pl.semaphore_wait(barrier, 3 + (col + 3) // 4 + (6 - col) // 4)


def remote(source, target, send, recv, device):
    return pltpu.make_async_remote_copy(
        src_ref=source,
        dst_ref=target,
        send_sem=send,
        recv_sem=recv,
        device_id=device,
        device_id_type=MESH,
    )


def arrived(target, recv):
    pltpu.make_async_copy(target, target, recv).wait()


def add_into(target, *terms):
    step = 16

    @pl.loop(0, target.shape[0] // step)
    def _(index):
        part = pl.ds(pl.multiple_of(index * step, step), step)
        value = target[part].astype(F32)
        for term in terms:
            value = value + term[part].astype(F32)
        target[part] = value.astype(target.dtype)


SPREAD_SEMS = [pltpu.SemaphoreType.DMA((4,))] * 11 + [pltpu.SemaphoreType.DMA((4, 4))] * 2


class Spread:
    def __init__(self, here, own, block, rows, sems, line=True, plane=True, core=True):
        self.here, self.own, self.block = here, own, block
        self.line, self.plane, self.core = line, plane, core
        (
            self.up_send, self.down_send, self.line_recv,
            self.across_send, self.across_recv, self.along_send, self.along_recv,
            self.one_send, self.one_recv, self.two_send, self.two_recv,
            self.core_send, self.core_recv,
        ) = sems
        self.first, self.second = pl.ds(0, rows // 2), pl.ds(rows // 2, rows // 2)
        self.order = here.near_first if line else [0]
        self.steps = len(self.order)

    def held(self, step):
        here = self.here
        return self.own if step == 0 else self.block(here.row, self.order[step], here.core)

    def up(self, step):
        here, place = self.here, self.order[step]
        target = self.block(here.row, place, here.core)
        recv = self.line_recv.at[place]
        return remote(self.held(step), target, self.up_send.at[place], recv, here.at_col(here.col + 1))

    def down(self, step):
        here, place = self.here, self.order[step]
        target = self.block(here.row, place, here.core)
        recv = self.line_recv.at[place]
        return remote(self.held(step), target, self.down_send.at[place], recv, here.at_col(here.col - 1))

    def to_across(self, step):
        here, place = self.here, self.order[step]
        target = self.block(here.row, place, here.core)
        sems = self.across_send.at[place], self.across_recv.at[place]
        return remote(self.held(step), target, *sems, here.at_row(here.across))

    def to_along(self, step):
        here, place = self.here, self.order[step]
        target = self.block(here.row, place, here.core)
        sems = self.along_send.at[place], self.along_recv.at[place]
        return remote(self.held(step), target, *sems, here.at_row(here.along))

    def corner_one(self, step):
        here, place = self.here, self.order[step]
        part = self.block(here.across, place, here.core).at[self.first]
        sems = self.one_send.at[place], self.one_recv.at[place]
        return remote(part, part, *sems, here.at_row(here.along))

    def corner_two(self, step):
        here, place = self.here, self.order[step]
        part = self.block(here.along, place, here.core).at[self.second]
        sems = self.two_send.at[place], self.two_recv.at[place]
        return remote(part, part, *sems, here.at_row(here.across))

    def to_core(self, which, step):
        here, place = self.here, self.order[step]
        target = self.block(here.rows[which], place, here.core)
        source = self.held(step) if which == 0 else target
        sems = self.core_send.at[which, place], self.core_recv.at[which, place]
        return remote(source, target, *sems, here.other_core())

    def line_step(self, step):
        here, place = self.here, self.order[step]
        if step > 0:
            arrived(self.held(step), self.line_recv.at[place])
        if self.line:

            @pl.when((place <= here.col) & (here.col < 3))
            def _():
                self.up(step).start()

            @pl.when((place >= here.col) & (here.col > 0))
            def _():
                self.down(step).start()

    def near_step(self, step):
        self.to_across(step).start()
        self.to_along(step).start()
        if self.core:
            self.to_core(0, step).start()

    def plane_step(self, step):
        here, place = self.here, self.order[step]
        arrived(self.block(here.across, place, here.core), self.across_recv.at[place])
        self.corner_one(step).start()
        if self.core:
            self.to_core(1, step).start()
        arrived(self.block(here.along, place, here.core), self.along_recv.at[place])
        self.corner_two(step).start()
        if self.core:
            self.to_core(2, step).start()

    def corner_step(self, step):
        here, place = self.here, self.order[step]
        target = self.block(here.opposite, place, here.core)
        arrived(target.at[self.first], self.one_recv.at[place])
        arrived(target.at[self.second], self.two_recv.at[place])
        if self.core:
            self.to_core(3, step).start()

    def step(self, index):
        if index < self.steps:
            self.line_step(index)
        if self.plane and 0 <= index - 1 < self.steps:
            self.plane_step(index - 1)
        if self.plane and index < self.steps:
            self.near_step(index)
        if self.plane and 0 <= index - 2 < self.steps:
            self.corner_step(index - 2)

    def core_arrived(self, which, step):
        here, place = self.here, self.order[step]
        target = self.block(here.rows[which], place, 1 - here.core)
        arrived(target, self.core_recv.at[which, place])

    def finish(self, arrivals=True):
        here = self.here
        for step in range(self.steps):
            place = self.order[step]
            if self.line:

                @pl.when((place <= here.col) & (here.col < 3))
                def _():
                    self.up(step).wait_send()

                @pl.when((place >= here.col) & (here.col > 0))
                def _():
                    self.down(step).wait_send()

            if self.plane:
                self.to_across(step).wait_send()
                self.to_along(step).wait_send()
                self.corner_one(step).wait_send()
                self.corner_two(step).wait_send()
                for which in range(4 if self.core else 0):
                    self.to_core(which, step).wait_send()
                    if arrivals:
                        self.core_arrived(which, step)


COLLECT_SEMS = (
    [pltpu.SemaphoreType.DMA((4,))] * 4
    + [pltpu.SemaphoreType.DMA((2, 4))] * 4
    + [pltpu.SemaphoreType.DMA((2, 4))] * 2
    + [pltpu.SemaphoreType.DMA((2, 5))]
)


def collect_buffers(rows, width):
    return [
        pltpu.VMEM((4, 4, rows, width), BF16),
        pltpu.VMEM((4, rows // 2, width), BF16),
        pltpu.VMEM((4, rows // 2, width), BF16),
        pltpu.VMEM((4, rows, width), BF16),
        pltpu.VMEM((4, rows, width), BF16),
        pltpu.VMEM((5, rows, width), BF16),
    ]


class Collect:
    def __init__(self, here, buffers, sems):
        self.here = here
        self.mine, self.one, self.two, self.from_across, self.from_along, self.line = buffers
        (
            self.one_send, self.one_recv, self.two_send, self.two_recv,
            self.across_send, self.across_recv, self.along_send, self.along_recv,
            self.up_send, self.down_send, self.line_recv,
        ) = sems
        half = self.mine.shape[2] // 2
        self.halves = (pl.ds(0, half), pl.ds(half, half))

    def give_one(self, place):
        here = self.here
        return remote(
            self.mine.at[3, place, self.halves[0]], self.one.at[place],
            self.one_send.at[place], self.one_recv.at[place], here.at_row(here.across),
        )

    def give_two(self, place):
        here = self.here
        return remote(
            self.mine.at[3, place, self.halves[1]], self.two.at[place],
            self.two_send.at[place], self.two_recv.at[place], here.at_row(here.along),
        )

    def give_across(self, place, half):
        here, part = self.here, self.halves[half]
        return remote(
            self.mine.at[1, place, part], self.from_across.at[place, part],
            self.across_send.at[half, place], self.across_recv.at[half, place], here.at_row(here.across),
        )

    def give_along(self, place, half):
        here, part = self.here, self.halves[half]
        return remote(
            self.mine.at[2, place, part], self.from_along.at[place, part],
            self.along_send.at[half, place], self.along_recv.at[half, place], here.at_row(here.along),
        )

    def give_up(self, place, half):
        here, part = self.here, self.halves[half]
        sems = self.up_send.at[half, place], self.line_recv.at[half, place]
        return remote(
            self.mine.at[0, place, part], self.line.at[place, part], *sems, here.at_col(here.col + 1)
        )

    def give_down(self, place, slot, half):
        here, part = self.here, self.halves[half]
        sems = self.down_send.at[half, place], self.line_recv.at[half, slot]
        return remote(
            self.mine.at[0, place, part], self.line.at[slot, part], *sems, here.at_col(here.col - 1)
        )

    def add_line(self, place, slot, half):
        part = self.halves[half]
        arrived(self.line.at[slot, part], self.line_recv.at[half, slot])
        add_into(self.mine.at[0, place, part], self.line.at[slot, part])

    def start_far(self, place):
        self.give_one(place).start()
        self.give_two(place).start()
        self.give_along(place, 1).start()

    def start_near(self, place):
        self.give_across(place, 0).start()

    def corner_step(self, place):
        self.give_two(place).wait_recv()
        add_into(self.mine.at[1, place, self.halves[1]], self.two.at[place])
        self.give_across(place, 1).start()
        self.give_one(place).wait_recv()
        add_into(self.mine.at[2, place, self.halves[0]], self.one.at[place])
        self.give_along(place, 0).start()

    def plane_step(self, place):
        for half in range(2):
            self.give_across(place, half).wait_recv()
            self.give_along(place, half).wait_recv()
        add_into(self.mine.at[0, place], self.from_across.at[place], self.from_along.at[place])

    def line_step(self, place):
        col = self.here.col
        for half in range(2):

            @pl.when(((place > col) & (col > 0)) | ((place < col) & (col < 3)))
            def _():
                self.add_line(place, place, half)

            @pl.when(place > col)
            def _():
                self.give_up(place, half).start()

            @pl.when(place < col - 1)
            def _():
                self.give_down(place, place, half).start()

            @pl.when(place == col - 1)
            def _():
                self.give_down(place, 4, half).start()

    def own_step(self):
        col = self.here.col
        for half in range(2):

            @pl.when(col > 0)
            def _():
                self.add_line(col, col, half)

            @pl.when(col < 3)
            def _():
                self.add_line(col, 4, half)

    def finish(self):
        col = self.here.col
        for place in range(4):
            self.give_one(place).wait_send()
            self.give_two(place).wait_send()
            for half in range(2):
                self.give_across(place, half).wait_send()
                self.give_along(place, half).wait_send()

                @pl.when(place > col)
                def _():
                    self.give_up(place, half).wait_send()

                @pl.when(place < col)
                def _():
                    self.give_down(place, place, half).wait_send()


def doc_start(places, cuts):
    return jnp.where(places >= cuts[1], cuts[1], jnp.where(places >= cuts[0], cuts[0], 0))


def key_blocks(cuts, first_query, rows, scores_of, block_fn):
    def scan(index, carry):
        start = pl.multiple_of(index * rows, rows)
        free = (start >= doc_start(first_query + rows - 1, cuts)) & (start + rows <= first_query + 1)

        @pl.when(free)
        def _():
            block_fn(start, scores_of(start))

        @pl.when(jnp.logical_not(free))
        def _():
            key_place = start + lax.broadcasted_iota(jnp.int32, (rows, rows), 0)
            place = first_query + lax.broadcasted_iota(jnp.int32, (1, rows), 1)
            allowed = (key_place <= place) & (key_place >= doc_start(place, cuts))
            block_fn(start, jnp.where(allowed, scores_of(start), MASKED))

        return carry

    lax.fori_loop(doc_start(first_query, cuts) // rows, first_query // rows + 1, scan, 0)


def attend_kernel(scale, group_tok, cuts, query, keys, values_t, mixed, total, top, summed, acc):
    rows = query.shape[0]
    side = lax.axis_index("exp") % 2
    first_query = side * group_tok + pl.program_id(0) * rows
    top[...] = jnp.full_like(top, MASKED)
    summed[...] = jnp.zeros_like(summed)
    acc[...] = jnp.zeros_like(acc)
    cut = (cuts[0, 0], cuts[0, 1])

    def scores_of(start):
        return contract_cols(keys[pl.ds(start, rows)], query[...]) * scale

    def block_fn(start, scores):
        old = top[...]
        new = jnp.maximum(old, jnp.max(scores, axis=0, keepdims=True))
        weights = jnp.exp(scores - new)
        decay = jnp.exp(old - new)
        top[...] = new
        summed[...] = summed[...] * decay + jnp.sum(weights, axis=0, keepdims=True)
        acc[...] = acc[...] * decay + matmul(values_t[:, pl.ds(start, rows)], weights.astype(BF16))

    key_blocks(cut, first_query, rows, scores_of, block_fn)
    mixed[...] = (acc[...] / summed[...]).T
    total[...] = top[...] + jnp.log(summed[...])


def attend(query, keys, values, cuts, scale, rows=512):
    group_tok, head_size = query.shape
    whole = lambda shape: pl.BlockSpec(shape, lambda i: (0, 0))
    return pl.pallas_call(
        functools.partial(attend_kernel, scale, group_tok),
        grid=(group_tok // rows,),
        in_specs=[
            pl.BlockSpec(memory_space=pltpu.SMEM),
            pl.BlockSpec((rows, head_size), lambda i: (i, 0)),
            whole(keys.shape),
            whole(values.shape[::-1]),
        ],
        out_specs=[
            pl.BlockSpec((rows, head_size), lambda i: (i, 0)),
            pl.BlockSpec((1, rows), lambda i: (0, i)),
        ],
        out_shape=[
            jax.ShapeDtypeStruct((group_tok, head_size), F32),
            jax.ShapeDtypeStruct((1, group_tok), F32),
        ],
        scratch_shapes=[
            pltpu.VMEM((1, rows), F32),
            pltpu.VMEM((1, rows), F32),
            pltpu.VMEM((head_size, rows), F32),
        ],
        compiler_params=pltpu.CompilerParams(vmem_limit_bytes=40 * 2**20),
        cost_estimate=pl.CostEstimate(
            flops=4 * 7 * 2**20 * head_size, bytes_accessed=2**23, transcendentals=7 * 2**20
        ),
    )(cuts[None], query, keys, values.T)


def attend_back_kernel(
    scale, group_tok, cuts, query, keys, keys_t, values, d_mixed, total, delta,
    d_query, d_keys, d_values, acc,
):
    rows = query.shape[0]
    side = lax.axis_index("exp") % 2
    first_query = side * group_tok + pl.program_id(0) * rows
    cut = (cuts[0, 0], cuts[0, 1])

    @pl.when(pl.program_id(0) == 0)
    def _():
        d_keys[...] = jnp.zeros_like(d_keys)
        d_values[...] = jnp.zeros_like(d_values)

    acc[...] = jnp.zeros_like(acc)

    def scores_of(start):
        return contract_cols(keys[pl.ds(start, rows)], query[...]) * scale

    def block_fn(start, scores):
        part = pl.ds(start, rows)
        weights = jnp.exp(scores - total[...])
        d_weights = contract_cols(values[part], d_mixed[...])
        d_scores = (weights * (d_weights - delta[...])).astype(BF16)
        d_values[part] += matmul(weights.astype(BF16), d_mixed[...])
        d_keys[part] += matmul(d_scores, query[...]) * scale
        acc[...] += matmul(keys_t[:, part], d_scores)

    key_blocks(cut, first_query, rows, scores_of, block_fn)
    d_query[...] = (acc[...] * scale).T


def attend_back(query, keys, values, d_mixed, mixed, total, cuts, scale, rows=512):
    group_tok, head_size = query.shape
    delta = jnp.sum(d_mixed.astype(F32) * mixed, axis=1)[None]
    whole = lambda shape: pl.BlockSpec(shape, lambda i: (0, 0))
    block = pl.BlockSpec((rows, head_size), lambda i: (i, 0))
    line = pl.BlockSpec((1, rows), lambda i: (0, i))
    return pl.pallas_call(
        functools.partial(attend_back_kernel, scale, group_tok),
        grid=(group_tok // rows,),
        in_specs=[
            pl.BlockSpec(memory_space=pltpu.SMEM),
            block,
            whole(keys.shape),
            whole(keys.shape[::-1]),
            whole(keys.shape),
            block,
            line,
            line,
        ],
        out_specs=[block, whole(keys.shape), whole(keys.shape)],
        out_shape=[
            jax.ShapeDtypeStruct((group_tok, head_size), F32),
            jax.ShapeDtypeStruct(keys.shape, F32),
            jax.ShapeDtypeStruct(keys.shape, F32),
        ],
        scratch_shapes=[pltpu.VMEM((head_size, rows), F32)],
        compiler_params=pltpu.CompilerParams(vmem_limit_bytes=48 * 2**20),
        cost_estimate=pl.CostEstimate(
            flops=10 * 7 * 2**20 * head_size, bytes_accessed=2**23, transcendentals=7 * 2**20
        ),
    )(cuts[None], query, keys, keys.T, values, d_mixed, total, delta)


def transposed_product(left, right):
    return jnp.dot(left.T, right, preferred_element_type=F32)


def column_of(line):
    return jnp.broadcast_to(line, (128, 128)).T[:, :1]


def line_of(column):
    return jnp.broadcast_to(column, (128, 128)).T[:1]


def expert_kernel(
    normed, grads_all, mask, gate_half, up_half, down_half,
    gate_other, up_other, down_other, router,
    rows_all, out_parts, total, inner_in, grad_gate, grad_up, grad_down,
    their_gates, their_down,
    gate_w, up_w, down_w, masks, x_buf, d_buf, gates_t, weighteds_t, d_gates, d_ups, weighteds, out_buf,
    inner, sum_buf, sum_down, *rest,
):
    here = Here()
    row, col, core = here.row, here.col, here.core
    rows, width = normed.shape
    half = gate_half.shape[1]
    expert = row * 4 + col
    count = len(SPREAD_SEMS)
    collect = Collect(here, rest[:6], rest[6 : 6 + len(COLLECT_SEMS)])
    rest = rest[6 + len(COLLECT_SEMS) :]
    (
        weight_sem, load_sem, store_sem, tile_sem, give_send, give_recv, their_sem, sum_sem,
        inner_send, inner_recv,
    ) = rest[:10]
    sems = rest[10:]

    def x_block(of_row, place, unused_core):
        return rows_all.at[pl.ds(pl.multiple_of((of_row * 4 + place) * rows, rows), rows)]

    def d_block(of_row, place, unused_core):
        return grads_all.at[pl.ds(pl.multiple_of((of_row * 4 + place) * rows, rows), rows)]

    def m_block(of_row, place, unused_core):
        return masks.at[of_row, place]

    spread_x = Spread(here, normed, x_block, rows, sems[:count], core=False)
    spread_m = Spread(here, mask, m_block, mask.shape[0], sems[count:], core=False)
    order = here.near_first

    own_half = pl.ds(pl.multiple_of(core * half, half), half)
    other_half = pl.ds(pl.multiple_of((1 - core) * half, half), half)
    keeps = [
        pltpu.make_async_copy(source, target, weight_sem.at[index])
        for index, (source, target) in enumerate(
            (
                (normed, x_block(row, col, 0)),
                (mask, m_block(row, col, 0)),
                (gate_half, gate_w.at[:, own_half]),
                (up_half, up_w.at[:, own_half]),
                (down_half, down_w.at[own_half]),
                (gate_other, gate_w.at[:, other_half]),
                (up_other, up_w.at[:, other_half]),
                (down_other, down_w.at[other_half]),
            )
        )
    ]
    greet(here.group_peers() + [here.other_core()])
    spread_x.step(0)
    spread_m.step(0)
    for keep in keeps:
        keep.start()

    turns = (3, 2, 1, 0)

    def loads(step):
        return [
            pltpu.make_async_copy(
                source(here.rows[which], order[step], 0),
                target.at[pl.ds(position * rows, rows)],
                load_sem.at[position, array],
            )
            for position, which in enumerate(turns)
            for array, (source, target) in enumerate(((x_block, x_buf), (d_block, d_buf)))
        ]

    def stores(step):
        return [
            pltpu.make_async_copy(
                out_buf.at[pl.ds(position * rows, rows)],
                out_parts.at[which, order[step]],
                store_sem.at[position],
            )
            for position, which in enumerate(turns)
        ]

    tile = 256

    def first_products(step):
        place = order[step]
        x = x_buf[...]
        lane = lax.broadcasted_iota(jnp.int32, (x.shape[0], router.shape[0]), 1)
        logits = contract_cols(x, router[...])
        raised = jnp.exp(logits - jnp.max(logits, axis=1, keepdims=True))
        picked = jnp.sum(jnp.where(lane == expert, raised, 0.0), axis=1, keepdims=True)
        routed = jnp.concatenate(
            [column_of(masks[here.rows[which], place, pl.ds(expert, 1)]) for which in turns]
        )
        gate = picked / jnp.sum(raised, axis=1, keepdims=True) * routed
        columns = [
            pl.ds(pl.multiple_of((here.rows[which] * 4 + place) * rows, rows), rows) for which in turns
        ]

        def tile_step(index, inner_sum):
            at = pl.ds(pl.multiple_of(index * tile, tile), tile)
            pre_gate = matmul(x_buf[...], gate_w[:, at])
            pre_up = matmul(x_buf[...], up_w[:, at])
            back = contract_cols(d_buf[...], down_w[at])
            sigmoid_gate = 0.5 * jnp.tanh(0.5 * pre_gate) + 0.5
            silu_gate = pre_gate * sigmoid_gate
            hidden = (silu_gate * pre_up).astype(BF16).astype(F32)
            d_hid = back * gate
            d_gate = (d_hid * pre_up * (sigmoid_gate + silu_gate * (1.0 - sigmoid_gate))).astype(BF16)
            d_up = (d_hid * silu_gate).astype(BF16)
            weight = (hidden * gate).astype(BF16)
            d_gates[:, at] = d_gate
            d_ups[:, at] = d_up
            weighteds[:, at] = weight
            side = index // (half // tile)
            first = pl.multiple_of(index % (half // tile) * tile, tile)
            for values, target in (
                (d_gate, gates_t.at[side, pl.ds(first, tile)]),
                (d_up, gates_t.at[side, pl.ds(first + half, tile)]),
                (weight, weighteds_t.at[at]),
            ):
                turned = values.T
                for position, column in enumerate(columns):
                    target[:, column] = turned[:, position * rows : (position + 1) * rows]
            return inner_sum + jnp.sum(hidden * back, axis=1, keepdims=True)

        start = jnp.zeros((x.shape[0], 1), F32)
        inner_sum = lax.fori_loop(0, gate_w.shape[1] // tile, tile_step, start, unroll=2)
        for position, which in enumerate(turns):
            part = slice(position * rows, (position + 1) * rows)
            inner[here.rows[which], place, 0:1] = line_of(inner_sum[part])

    def second_products(step):
        place = order[step]

        @pl.loop(0, width // tile, unroll=2)
        def _(index):
            at = pl.ds(pl.multiple_of(index * tile, tile), tile)
            out_buf[:, at] = matmul(weighteds[...], down_w[:, at]).astype(BF16)
            d_x = contract_cols(d_gates[...], gate_w[at]) + contract_cols(d_ups[...], up_w[at])
            d_x = d_x.astype(BF16)
            for position, which in enumerate(turns):
                collect.mine[which, place, :, at] = d_x[position * rows : (position + 1) * rows]

    for index in (1, 2):
        spread_x.step(index)
        spread_m.step(index)
    for keep in keeps:
        keep.wait()
    for copy in loads(0):
        copy.start()
    turn_order = (0, 1, 3, 2)
    ends = (col == 0) | (col == 3)

    def from_ends(step):
        @pl.when(ends)
        def _():
            collect.line_step(order[step])

    def from_inside(step):
        @pl.when(jnp.logical_not(ends))
        def _():
            collect.line_step(order[step])

    for turn, step in enumerate(turn_order):
        for copy in loads(step):
            copy.wait()
        first_products(step)
        if turn < 2:
            spread_x.step(turn + 3)
            spread_m.step(turn + 3)
        if turn in (0, 2):
            for copy in loads(turn_order[turn + 1]):
                copy.start()
        if turn > 0:
            for copy in stores(turn_order[turn - 1]):
                copy.wait()
            collect.corner_step(order[turn_order[turn - 1]])
        second_products(step)
        for copy in stores(step):
            copy.start()
        collect.start_far(order[step])
        collect.start_near(order[step])
        if turn == 1:
            spread_x.step(5)
            spread_m.step(5)
            for copy in loads(turn_order[2]):
                copy.start()
        if turn > 0:
            collect.plane_step(order[turn_order[turn - 1]])
        if turn > 1:
            from_ends(turn_order[turn - 1])

    tiles = width // tile

    def tile_at(index):
        return pl.ds(pl.multiple_of(index * tile, tile), tile)

    def acts_of(kind, side):
        if kind == 0:
            return gates_t[side]
        return weighteds_t[pl.ds(pl.multiple_of(side * half, half), half)]

    counts = (2 * half, half)

    def slot_at(kind, slot):
        return pl.ds(pl.multiple_of((2 * kind + slot) * tile, tile), tile)

    def tile_buf(kind, slot):
        return gate_w.at[:, slot_at(kind, slot)]

    def give_buf(kind, slot):
        return up_w.at[pl.ds(0, counts[kind]), slot_at(kind, slot)]

    def their_buf(kind, slot):
        return up_w.at[pl.ds(width // 2, counts[kind]), slot_at(kind, slot)]

    theirs = (their_gates, their_down)

    def tile_load(kind, index, slot):
        source = (rows_all, grads_all)[kind]
        return pltpu.make_async_copy(
            source.at[:, tile_at(index)], tile_buf(kind, slot), tile_sem.at[slot]
        )

    def give(kind, index, slot):
        sems = give_send.at[slot, kind], give_recv.at[kind, index]
        return remote(give_buf(kind, slot), theirs[kind].at[:, tile_at(index)], *sems, here.other_core())

    def their_load(kind, index, slot):
        return pltpu.make_async_copy(
            theirs[kind].at[:, tile_at(index)],
            their_buf(kind, slot),
            their_sem.at[slot, kind],
        )

    def sum_stores(kind, index, slot):
        if kind == 1:
            target = grad_down.at[:, tile_at(index)]
            return [pltpu.make_async_copy(sum_down, target, sum_sem.at[0, 2])]
        return [
            pltpu.make_async_copy(
                sum_buf.at[slot, part], target.at[tile_at(index)], sum_sem.at[slot, part]
            )
            for part, target in enumerate((grad_gate, grad_up))
        ]

    def give_gradients(kind, start, stop):
        tile_load(kind, start, 0).start()

        @pl.loop(start, stop)
        def _(index):
            slot = index % 2

            @pl.when(index + 1 < stop)
            def _():
                tile_load(kind, index + 1, 1 - slot).start()

            tile_load(kind, index, slot).wait()
            product = matmul(acts_of(kind, 1 - core), tile_buf(kind, slot)[...])

            @pl.when(index >= 2)
            def _():
                give(kind, index - 2, slot).wait_send()

            give_buf(kind, slot)[...] = product.astype(BF16)
            give(kind, index, slot).start()

    def keep_gradients(kind, start, stop):
        tile_load(kind, start, 0).start()
        give(kind, start, 0).wait_recv()
        their_load(kind, start, 0).start()

        @pl.loop(start, stop)
        def _(index):
            slot = index % 2

            @pl.when(index + 1 < stop)
            def _():
                tile_load(kind, index + 1, 1 - slot).start()
                give(kind, index + 1, 1 - slot).wait_recv()
                their_load(kind, index + 1, 1 - slot).start()

            tile_load(kind, index, slot).wait()
            product = matmul(acts_of(kind, core), tile_buf(kind, slot)[...])
            their_load(kind, index, slot).wait()
            product = product + their_buf(kind, slot)[...].astype(F32)
            held = 2 - kind

            @pl.when(index >= held)
            def _():
                for copy in sum_stores(kind, index - held, slot):
                    copy.wait()

            if kind == 1:
                sum_down[...] = product.astype(BF16)
            else:
                sum_buf[slot, 0] = product[:half].T.astype(BF16)
                sum_buf[slot, 1] = product[half:].T.astype(BF16)
            for copy in sum_stores(kind, index, slot):
                copy.start()

    def give_inner(index):
        step = index + 1
        to_row, to_col = (row + step // 4) % 4, (col + step) % 4
        return remote(
            inner.at[to_row, to_col],
            inner_in.at[row, col],
            inner_send.at[index],
            inner_recv.at[row, col],
            (to_row, to_col, core),
        )

    for index in range(15):
        give_inner(index).start()
    inner_in[row, col] = inner[row, col]
    give_gradients(0, 0, tiles // 2)
    from_inside(3)
    collect.corner_step(order[2])
    give_gradients(0, tiles // 2, tiles)
    collect.plane_step(order[2])
    from_ends(2)
    give_gradients(1, 0, tiles)
    from_inside(2)
    keep_gradients(0, 0, tiles // 2)
    from_inside(1)
    keep_gradients(0, tiles // 2, tiles)
    keep_gradients(1, 0, tiles)
    collect.own_step()
    total[...] = collect.mine[0, col]

    for index in range(15):
        give_inner(index).wait_send()
        step = index + 1
        from_row, from_col = (row + 4 - step // 4) % 4, (col + 4 - step % 4) % 4
        arrived(inner_in.at[from_row, from_col], inner_recv.at[from_row, from_col])
    for copy in stores(turn_order[3]):
        copy.wait()
    for kind in range(2):
        for slot in range(2):
            give(kind, tiles - 2 + slot, slot).wait_send()
        for slot in range(2 - kind):
            for copy in sum_stores(kind, tiles - 2 + kind + slot, slot):
                copy.wait()
    spread_x.finish()
    spread_m.finish()
    collect.finish()


def expert_stage(normed, grads_all, mask, halves, others, router, collective_id):
    rows, width = normed.shape
    half = halves[0].shape[1]
    tokens = 16 * rows
    tile = 256
    vmem = pl.BlockSpec(memory_space=pltpu.VMEM)
    hbm = pl.BlockSpec(memory_space=pl.ANY)
    dma = pltpu.SemaphoreType.DMA
    blocks = jax.ShapeDtypeStruct((4, 4, rows, width), BF16)
    got = pl.pallas_call(
        expert_kernel,
        in_specs=[hbm] * 9 + [vmem],
        out_specs=[hbm] * 2 + [vmem] * 2 + [hbm] * 5,
        out_shape=[
            jax.ShapeDtypeStruct((tokens, width), BF16),
            blocks,
            jax.ShapeDtypeStruct((rows, width), BF16),
            jax.ShapeDtypeStruct((4, 4, 8, rows), F32),
            jax.ShapeDtypeStruct((width, half), BF16),
            jax.ShapeDtypeStruct((width, half), BF16),
            jax.ShapeDtypeStruct((half, width), BF16),
            jax.ShapeDtypeStruct((2 * half, width), BF16),
            jax.ShapeDtypeStruct((half, width), BF16),
        ],
        scratch_shapes=[
            pltpu.VMEM((width, 2 * half), BF16),
            pltpu.VMEM((width, 2 * half), BF16),
            pltpu.VMEM((2 * half, width), BF16),
            pltpu.VMEM((4, 4) + mask.shape, F32),
            pltpu.VMEM((4 * rows, width), BF16),
            pltpu.VMEM((4 * rows, width), BF16),
            pltpu.VMEM((2, 2 * half, tokens), BF16),
            pltpu.VMEM((2 * half, tokens), BF16),
            pltpu.VMEM((4 * rows, 2 * half), BF16),
            pltpu.VMEM((4 * rows, 2 * half), BF16),
            pltpu.VMEM((4 * rows, 2 * half), BF16),
            pltpu.VMEM((4 * rows, width), BF16),
            pltpu.VMEM((4, 4, 8, rows), F32),
            pltpu.VMEM((2, 2, tile, half), BF16),
            pltpu.VMEM((half, tile), BF16),
        ]
        + collect_buffers(rows, width)
        + COLLECT_SEMS
        + [
            dma((8,)), dma((4, 2)), dma((4,)),
            dma((2,)), dma((2, 2)), dma((2, width // tile)), dma((2, 2)), dma((2, 3)),
            dma((15,)), dma((4, 4)),
        ]
        + SPREAD_SEMS * 2,
        compiler_params=pltpu.CompilerParams(
            collective_id=collective_id, has_side_effects=True, vmem_limit_bytes=61 * 2**20
        ),
        cost_estimate=pl.CostEstimate(
            flops=18 * 2 * tokens * width * half,
            bytes_accessed=2**26,
            transcendentals=2 * tokens * half,
        ),
    )(normed, grads_all, mask, *halves, *others, router.T)
    return got[1], got[2], got[3], got[4:7]


def project_kernel(
    hidden, all_gains, weights, cosine, sine,
    normed_out, weights_out, qkv_out, totals, query, keys, values,
    normed, all_weights, qkv, out_sem,
    heads, stat, scale_q, scale_k, kept_sem, kept_kv_sem,
    stat_send, stat_recv, head_send, head_recv, pair_send, pair_recv, *sems,
):
    here = Here()
    row, col, core = here.row, here.col, here.core
    count = len(SPREAD_SEMS)
    rows, width = hidden.shape
    depth = weights.shape[0]
    part = depth // 2

    def weight_block(of_row, unused_place, of_core):
        return all_weights.at[pl.ds(pl.multiple_of(of_row * depth + of_core * part, part), part)]

    def normed_block(unused_row, place, unused_core):
        return normed.at[pl.ds(pl.multiple_of(place * rows, rows), rows)]

    own_weight = weights.at[pl.ds(pl.multiple_of(core * part, part), part)]
    spread_w = Spread(here, own_weight, weight_block, part, sems[:count], line=False)
    spread_n = Spread(
        here, normed_block(row, col, core), normed_block, rows, sems[count:], plane=False
    )
    greet(here.plane_peers() + here.line_peers() + [here.other_core()])
    spread_w.step(0)
    keep = pltpu.make_async_copy(own_weight, weight_block(row, 0, core), kept_sem)
    keep.start()

    values_in = hidden[...].astype(F32)
    scale_one = lax.rsqrt(jnp.mean(values_in * values_in, axis=1, keepdims=True) + EPSILON)
    own_rows = pl.ds(pl.multiple_of(col * rows, rows), rows)
    normed[own_rows] = (values_in * scale_one * all_gains[0:1]).astype(BF16)
    spread_n.step(0)
    spread_w.step(1)
    spread_n.step(1)
    spread_w.step(2)
    spread_n.step(2)
    spread_n.step(3)
    keep.wait()
    for which in range(4):
        spread_w.core_arrived(which, 0)
    puts = [
        pltpu.make_async_copy(source, target, out_sem.at[index])
        for index, (source, target) in enumerate(
            ((normed, normed_out), (all_weights, weights_out), (qkv, qkv_out))
        )
    ]
    puts[0].start()
    puts[1].start()
    columns = 256

    @pl.loop(0, qkv.shape[1] // columns)
    def _(index):
        at = pl.ds(pl.multiple_of(index * columns, columns), columns)
        qkv[:, at] = matmul(normed[...], all_weights[:, at])

    puts[2].start()

    plane = qkv.shape[1] // (3 * HD)
    for kind in range(2):
        square = jnp.zeros((qkv.shape[0], HD), F32)
        for head in range(plane):
            start = (head * 3 + kind) * HD
            raw = qkv[:, start : start + HD]
            square = square + raw * raw
        stat[col, kind : kind + 1] = jnp.sum(square.T, axis=0, keepdims=True)

    def give_stat(step):
        peer = here.line_peers()[step]
        return remote(stat.at[col], stat.at[col], stat_send.at[step], stat_recv.at[col], peer)

    for step in range(3):
        give_stat(step).start()
    for step in range(3):
        place = (col + step + 1) % 4
        arrived(stat.at[place], stat_recv.at[place])
    total = stat[0] + stat[1] + stat[2] + stat[3]
    totals[...] = total
    for kind, target in enumerate((scale_q, scale_k)):
        line = lax.rsqrt(total[kind : kind + 1] / width + EPSILON)
        target[...] = jnp.broadcast_to(line, (HD, line.shape[1])).T

    chunk = 64

    @pl.loop(0, qkv.shape[0] // chunk)
    def _(index):
        at = pl.ds(pl.multiple_of(index * chunk, chunk), chunk)
        for head in range(plane):
            place = pl.ds(pl.multiple_of((col * plane + head) * HD, HD), HD)
            for kind, scales in enumerate((scale_q, scale_k)):
                raw = qkv[at, pl.ds((head * 3 + kind) * HD, HD)]
                unit = raw * scales[at] * all_gains[kind + 1 : kind + 2, place]
                turned = pltpu.roll(unit, HD // 2, 1)
                heads[head, kind, at] = (unit * cosine[at] + turned * sine[at]).astype(BF16)
            heads[head, 2, at] = qkv[at, pl.ds((head * 3 + 2) * HD, HD)].astype(BF16)

    targets = (query.at[row], keys.at[1, row], values.at[1, row])

    def give_head(step, kind):
        dest = here.rows[step + 1]
        sems = head_send.at[step, kind], head_recv.at[kind, row]
        return remote(heads.at[dest, kind], targets[kind], *sems, here.at_row(dest))

    for kind in (1, 2, 0):
        for step in range(3):
            give_head(step, kind).start()

    def give_pair(source, kind):
        array = (keys, values)[kind]
        sems = pair_send.at[kind, source], pair_recv.at[kind, source]
        return remote(array.at[1, source], array.at[0, source], *sems, here.other_core())

    def keep_pair(source, kind):
        array = (keys, values)[kind]
        return pltpu.make_async_copy(
            array.at[1, source], array.at[0, source], kept_kv_sem.at[kind, source]
        )

    def pair_from(source):
        @pl.when(core == 0)
        def _():
            for kind in range(2):
                give_pair(source, kind).start()
                keep_pair(source, kind).start()

    for kind, array in ((1, keys), (2, values)):
        array[1, row] = heads[row, kind]
    query[row] = heads[row, 0]
    pair_from(row)
    for source in here.rows[1:]:
        arrived(keys.at[1, source], head_recv.at[1, source])
        arrived(values.at[1, source], head_recv.at[2, source])
        pair_from(source)
    for source in here.rows[1:]:
        arrived(query.at[source], head_recv.at[0, source])

    @pl.when(core == 0)
    def _():
        for source in range(4):
            for kind in range(2):
                give_pair(source, kind).wait_send()
                keep_pair(source, kind).wait()

    @pl.when(core == 1)
    def _():
        for source in range(4):
            for kind in range(2):
                give_pair(source, kind).wait_recv()

    for step in range(3):
        give_stat(step).wait_send()
        for kind in range(3):
            give_head(step, kind).wait_send()
    for put in puts:
        put.wait()
    spread_w.finish(arrivals=False)
    spread_n.finish()


def project(hidden, gains, weights, cosine, sine, collective_id):
    rows, width = hidden.shape
    depth, columns = weights.shape
    row_tok = 4 * rows
    plane = columns // (3 * HD)
    vmem = pl.BlockSpec(memory_space=pltpu.VMEM)
    hbm = pl.BlockSpec(memory_space=pl.ANY)
    return pl.pallas_call(
        project_kernel,
        in_specs=[vmem, vmem, hbm, vmem, vmem],
        out_specs=[hbm] * 3 + [vmem] * 4,
        out_shape=[
            jax.ShapeDtypeStruct((row_tok, width), BF16),
            jax.ShapeDtypeStruct((4 * depth, columns), BF16),
            jax.ShapeDtypeStruct((row_tok, columns), F32),
            jax.ShapeDtypeStruct((8, row_tok), F32),
            jax.ShapeDtypeStruct((4, row_tok, HD), BF16),
            jax.ShapeDtypeStruct((2, 4, row_tok, HD), BF16),
            jax.ShapeDtypeStruct((2, 4, row_tok, HD), BF16),
        ],
        scratch_shapes=[
            pltpu.VMEM((row_tok, width), BF16),
            pltpu.VMEM((4 * depth, columns), BF16),
            pltpu.VMEM((row_tok, columns), F32),
            pltpu.SemaphoreType.DMA((3,)),
            pltpu.VMEM((plane, 3, row_tok, HD), BF16),
            pltpu.VMEM((4, 8, row_tok), F32),
            pltpu.VMEM((row_tok, HD), F32),
            pltpu.VMEM((row_tok, HD), F32),
            pltpu.SemaphoreType.DMA,
            pltpu.SemaphoreType.DMA((2, 4)),
            pltpu.SemaphoreType.DMA((3,)),
            pltpu.SemaphoreType.DMA((4,)),
            pltpu.SemaphoreType.DMA((3, 3)),
            pltpu.SemaphoreType.DMA((3, 4)),
            pltpu.SemaphoreType.DMA((2, 4)),
            pltpu.SemaphoreType.DMA((2, 4)),
        ]
        + SPREAD_SEMS * 2,
        compiler_params=pltpu.CompilerParams(
            collective_id=collective_id, has_side_effects=True, vmem_limit_bytes=56 * 2**20
        ),
    )(hidden, gains, weights, cosine, sine)


def attention_kernel(
    scale, cuts, query, keys, values, out_weights, hidden, all_gains,
    mixed, total, whole_out, mixed_rows, middle, normed,
    all_out, put_sem, values_t, top, summed, acc, mixed_low, mixed_tok, kept_sem,
    row_send, row_recv, token_send, token_recv, *sems,
):
    here = Here()
    row, col, core = here.row, here.col, here.core
    rows = hidden.shape[0]
    row_tok = 4 * rows
    group_tok = 4 * row_tok
    side = out_weights.shape[0]

    def out_block(of_row, place, of_core):
        start = pl.multiple_of(place * side + of_core * (side // 2), side // 2)
        return all_out.at[pl.ds(start, side // 2), pl.ds(pl.multiple_of(of_row * side, side), side)]

    own_out = out_weights.at[pl.ds(pl.multiple_of(core * (side // 2), side // 2), side // 2)]
    spread = Spread(here, own_out, out_block, side // 2, sems)
    keep = pltpu.make_async_copy(own_out, out_block(row, col, core), kept_sem)
    keep.start()
    values_t[...] = values[...].T
    greet(here.plane_peers() + here.line_peers() + [here.other_core()])
    spread.step(0)
    cut = (cuts[0, 0], cuts[0, 1])
    last_query = 2 * group_tok - row_tok

    def queries(index):
        at = pl.ds(index * row_tok, row_tok)
        first_query = core * group_tok + index * row_tok
        top[...] = jnp.full_like(top, MASKED)
        summed[...] = jnp.zeros_like(summed)
        acc[...] = jnp.zeros_like(acc)

        def block_fn(part, scores):
            old = top[...]
            new = jnp.maximum(old, jnp.max(scores, axis=0, keepdims=True))
            weight = jnp.exp(scores - new)
            decay = jnp.exp(old - new)
            top[...] = new
            summed[...] = summed[...] * decay + jnp.sum(weight, axis=0, keepdims=True)
            acc[...] = acc[...] * decay + matmul(values_t[:, part], weight.astype(BF16))

        def scan(block, carry):
            first_key = block * row_tok
            part = pl.ds(pl.multiple_of(first_key, row_tok), row_tok)
            masked = (block == 0) | (first_key == first_query) | (first_query == last_query)

            @pl.when(jnp.logical_not(masked))
            def _():
                block_fn(part, contract_cols(keys[part], query[at]) * scale)

            @pl.when(masked)
            def _():
                key_place = first_key + lax.broadcasted_iota(jnp.int32, (row_tok, row_tok), 0)
                place = first_query + lax.broadcasted_iota(jnp.int32, (1, row_tok), 1)
                allowed = (key_place <= place) & (key_place >= doc_start(place, cut))
                scores = contract_cols(keys[part], query[at]) * scale
                block_fn(part, jnp.where(allowed, scores, MASKED))

            return carry

        lax.fori_loop(0, core * 4 + index + 1, scan, 0)
        got = (acc[...] / summed[...]).T
        mixed[at] = got
        mixed_low[index] = got.astype(BF16)
        total[:, at] = top[...] + jnp.log(summed[...])

        @pl.when(row != index)
        def _():
            give_row(index).start()

        @pl.when(row == index)
        def _():
            mixed_rows[row] = mixed_low[index]

    def give_row(index):
        sems_of = row_send.at[index], row_recv.at[row]
        return remote(mixed_low.at[index], mixed_rows.at[row], *sems_of, here.at_row(index))

    def give_token(step):
        place = (col + step) % 4
        part = pl.ds(pl.multiple_of(place * rows, rows), rows)
        sems_of = token_send.at[step], token_recv.at[col]
        return remote(mixed_rows.at[:, part], mixed_tok.at[col], *sems_of, here.at_col(place))

    for index in range(4):
        queries(index)
        spread.step(index + 1)
    for source in here.rows[1:]:
        arrived(mixed_rows.at[source], row_recv.at[source])
    for step in range(1, 4):
        give_token(step).start()
    mixed_tok[col] = mixed_rows[:, pl.ds(pl.multiple_of(col * rows, rows), rows)]
    spread.step(5)
    keep.wait()
    spread.finish()
    put = pltpu.make_async_copy(all_out, whole_out, put_sem)
    put.start()
    for step in range(1, 4):
        place = (col + 4 - step) % 4
        arrived(mixed_tok.at[place], token_recv.at[place])
    own = jnp.concatenate([mixed_tok[place, head] for place in range(4) for head in range(4)], axis=1)
    tile = 512

    @pl.loop(0, all_out.shape[1] // tile)
    def _(index):
        at = pl.ds(pl.multiple_of(index * tile, tile), tile)
        middle[:, at] = hidden[:, at].astype(F32) + matmul(own, all_out[:, at])

    values_in = middle[...]
    root = lax.rsqrt(jnp.mean(values_in * values_in, axis=1, keepdims=True) + EPSILON)
    normed[...] = (values_in * root * all_gains[3:4]).astype(BF16)
    put.wait()
    for index in range(4):

        @pl.when(row != index)
        def _():
            give_row(index).wait_send()

    for step in range(1, 4):
        give_token(step).wait_send()


def attention_stage(query, keys, values, cuts, out_weights, hidden, gains, scale, collective_id):
    rows, width = hidden.shape
    row_tok, group_tok = 4 * rows, 16 * rows
    vmem, hbm = pl.BlockSpec(memory_space=pltpu.VMEM), pl.BlockSpec(memory_space=pl.ANY)
    dma = pltpu.SemaphoreType.DMA
    return pl.pallas_call(
        functools.partial(attention_kernel, scale),
        in_specs=[pl.BlockSpec(memory_space=pltpu.SMEM)] + [vmem] * 3 + [hbm] + [vmem] * 2,
        out_specs=[vmem] * 2 + [hbm] + [vmem] * 3,
        out_shape=[
            jax.ShapeDtypeStruct((group_tok, HD), F32),
            jax.ShapeDtypeStruct((1, group_tok), F32),
            jax.ShapeDtypeStruct((width, width), BF16),
            jax.ShapeDtypeStruct((4, row_tok, HD), BF16),
            jax.ShapeDtypeStruct((rows, width), F32),
            jax.ShapeDtypeStruct((rows, width), BF16),
        ],
        scratch_shapes=[
            pltpu.VMEM((width, width), BF16),
            dma,
            pltpu.VMEM((HD, 2 * group_tok), BF16),
            pltpu.VMEM((1, row_tok), F32),
            pltpu.VMEM((1, row_tok), F32),
            pltpu.VMEM((HD, row_tok), F32),
            pltpu.VMEM((4, row_tok, HD), BF16),
            pltpu.VMEM((4, 4, rows, HD), BF16),
            dma, dma((4,)), dma((4,)), dma((4,)), dma((4,)),
        ]
        + SPREAD_SEMS,
        compiler_params=pltpu.CompilerParams(
            collective_id=collective_id, has_side_effects=True, vmem_limit_bytes=40 * 2**20
        ),
    )(cuts, query, keys, values, out_weights, hidden, gains)


class PairSum:
    def __init__(self, here, values, out, held, got, send, recv):
        self.here, self.values, self.out, self.held, self.got = here, values, out, held, got
        self.send, self.recv = send, recv
        col, half = here.col, values.shape[1] // 2
        self.own = pl.ds(pl.multiple_of(here.core * half, half), half)
        self.others = pl.ds(pl.multiple_of((1 - here.core) * half, half), half)
        self.peers = [
            here.at_row(here.across),
            here.at_row(here.along),
            here.at_col(col + 1 - 2 * (col % 2)),
            here.at_col((col + 2) % 4),
        ]

    def copy(self, step):
        here, sems = self.here, (self.send.at[step], self.recv.at[step])
        if step == 0:
            return remote(self.values.at[:, self.others], self.got.at[0], *sems, here.other_core())
        if step == 5:
            return remote(self.held.at[4], self.out.at[:, self.own], *sems, here.other_core())
        return remote(self.held.at[step - 1], self.got.at[step], *sems, self.peers[step - 1])

    def begin(self):
        self.copy(0).start()

    def step(self, index):
        if index == 5:
            arrived(self.out.at[:, self.others], self.recv.at[5])
            return
        self.copy(index).wait_recv()
        before = self.values[:, self.own] if index == 0 else self.held[index - 1]
        self.held[index] = before + self.got[index]
        if index == 4:
            self.out[:, self.own] = self.held[4]
        self.copy(index + 1).start()

    def finish(self):
        for index in range(6):
            self.copy(index).wait_send()


def pair_sum_buffers(rows, width):
    return [
        pltpu.VMEM((5, rows, width // 2), F32),
        pltpu.VMEM((5, rows, width // 2), F32),
        pltpu.SemaphoreType.DMA((6,)),
        pltpu.SemaphoreType.DMA((6,)),
    ]


def back_kernel(
    scale, cuts, d_attn, query, keys, values, mixed, total, out_weights, out_parts, early,
    d_attn_row, d_heads, out_total, early_sum,
    weights, d_mixed_give, d_mixed_row, d_mixed, keys_t, d_keys, d_values, acc, pair_out, pair_in,
    head_give, sum_held, sum_got, sum_send, sum_recv, weight_sem, load_sem,
    near_send, near_recv, head_send, head_recv, back_send, back_recv,
    pair_send, pair_recv, *rest,
):
    here = Here()
    row, col, core = here.row, here.col, here.core
    rows = d_attn.shape[0]
    row_tok = 4 * rows
    group_tok = 4 * row_tok
    plane = 4 * HD
    order = here.near_first[::-1]
    collect = Collect(here, rest[:6], rest[6 : 6 + len(COLLECT_SEMS)])
    sems = rest[6 + len(COLLECT_SEMS) :]

    def row_block(unused_row, place, unused_core):
        return d_attn_row.at[pl.ds(pl.multiple_of(place * rows, rows), rows)]

    spread = Spread(here, row_block(row, col, core), row_block, rows, sems, plane=False)
    pair_sum = PairSum(here, early, early_sum, sum_held, sum_got, sum_send, sum_recv)

    def load(which, place):
        return pltpu.make_async_copy(
            out_parts.at[which, place], collect.mine.at[which, place], load_sem.at[which, place]
        )

    load_weights = pltpu.make_async_copy(out_weights, weights, weight_sem)
    load_weights.start()
    for place in order:
        for which in (3, 2, 1, 0):
            load(which, place).start()
    keys_t[...] = keys[...].T
    d_attn_row[pl.ds(pl.multiple_of(col * rows, rows), rows)] = d_attn[...]
    greet(here.plane_peers() + here.line_peers() + [here.other_core()])

    def give_near(step):
        place = (col + step) % 4
        sems_of = near_send.at[step], near_recv.at[col]
        return remote(d_mixed_give.at[place], d_mixed_row.at[col], *sems_of, here.at_col(place))

    def give_head(step):
        dest = here.rows[step]
        part = pl.ds(pl.multiple_of(dest * HD, HD), HD)
        sems_of = head_send.at[step], head_recv.at[row]
        return remote(d_mixed_row.at[:, :, part], d_mixed.at[row], *sems_of, here.at_row(dest))

    def start(index):
        for which in (3, 2, 1):
            load(which, order[index]).wait()
        collect.start_far(order[index])
        collect.start_near(order[index])

    ends = (col == 0) | (col == 3)

    def from_ends(index):
        @pl.when(ends)
        def _():
            collect.line_step(order[index])

    def from_inside(index):
        @pl.when(jnp.logical_not(ends))
        def _():
            collect.line_step(order[index])

    def plane_part(index):
        load(0, order[index]).wait()
        collect.plane_step(order[index])

    start(0)
    pair_sum.begin()
    load_weights.wait()
    for step in (1, 2, 3, 0):
        place = (col + step) % 4
        part = pl.ds(pl.multiple_of(place * plane, plane), plane)
        product = contract_cols(d_attn[...], weights[part]).astype(BF16)
        if step == 0:
            d_mixed_row[col] = product
        else:
            d_mixed_give[place] = product
            give_near(step).start()
    spread.step(0)
    pair_sum.step(0)
    d_keys[...] = jnp.zeros_like(d_keys)
    d_values[...] = jnp.zeros_like(d_values)
    for step in range(1, 4):
        place = (col + 4 - step) % 4
        arrived(d_mixed_row.at[place], near_recv.at[place])
    for step in range(1, 4):
        give_head(step).start()
    d_mixed[row] = d_mixed_row[:, :, pl.ds(pl.multiple_of(row * HD, HD), HD)]
    collect.corner_step(order[0])
    start(1)
    pair_sum.step(1)
    spread.step(1)
    for source in here.rows[1:]:
        arrived(d_mixed.at[source], head_recv.at[source])

    cut = (cuts[0, 0], cuts[0, 1])
    last_query = 2 * group_tok - row_tok

    def queries(index):
        at = pl.ds(index * row_tok, row_tok)
        first_query = core * group_tok + index * row_tok
        gradient = d_mixed[index].reshape(row_tok, HD)
        delta = jnp.sum((gradient.astype(F32) * mixed[at]).T, axis=0, keepdims=True)
        sums = total[:, at]
        acc[...] = jnp.zeros_like(acc)

        def block_fn(part, scores):
            weight = jnp.exp(scores - sums)
            d_weight = contract_cols(values[part], gradient)
            d_scores = (weight * (d_weight - delta)).astype(BF16)
            d_values[part] += matmul(weight.astype(BF16), gradient)
            d_keys[part] += matmul(d_scores, query[at]) * scale
            acc[...] += matmul(keys_t[:, part], d_scores)

        def scan(block, carry):
            first_key = block * row_tok
            part = pl.ds(pl.multiple_of(first_key, row_tok), row_tok)
            masked = (block == 0) | (first_key == first_query) | (first_query == last_query)

            @pl.when(jnp.logical_not(masked))
            def _():
                block_fn(part, contract_cols(keys[part], query[at]) * scale)

            @pl.when(masked)
            def _():
                key_place = first_key + lax.broadcasted_iota(jnp.int32, (row_tok, row_tok), 0)
                place = first_query + lax.broadcasted_iota(jnp.int32, (1, row_tok), 1)
                allowed = (key_place <= place) & (key_place >= doc_start(place, cut))
                scores = contract_cols(keys[part], query[at]) * scale
                block_fn(part, jnp.where(allowed, scores, MASKED))

            return carry

        lax.fori_loop(0, core * 4 + index + 1, scan, 0)
        head_give[0, index] = (acc[...] * scale).T.astype(BF16)

    queries(0)
    plane_part(0)
    from_ends(0)
    collect.corner_step(order[1])
    start(2)
    spread.step(2)
    queries(1)
    from_inside(0)
    plane_part(1)
    from_ends(1)
    collect.corner_step(order[2])
    start(3)
    pair_sum.step(2)
    queries(2)
    from_inside(1)
    plane_part(2)
    from_ends(2)
    collect.corner_step(order[3])
    spread.step(3)
    queries(3)

    def give_back(step, kind):
        dest = here.rows[step]
        sems_of = back_send.at[step, kind], back_recv.at[kind, row]
        return remote(head_give.at[kind, dest], d_heads.at[row, kind], *sems_of, here.at_row(dest))

    def give_pair(kind):
        sems_of = pair_send.at[kind], pair_recv.at[kind]
        return remote(pair_out.at[kind], pair_in.at[kind], *sems_of, here.other_core())

    for step in range(1, 4):
        give_back(step, 0).start()
    d_heads[row, 0] = head_give[0, row]

    @pl.when(core == 1)
    def _():
        for kind, gradient in enumerate((d_keys, d_values)):
            pair_out[kind] = gradient[pl.ds(0, group_tok)].astype(BF16)
            give_pair(kind).start()
        for kind, gradient in enumerate((d_keys, d_values)):
            for part in range(4):
                at = pl.ds(group_tok + part * row_tok, row_tok)
                head_give[kind + 1, part] = gradient[at].astype(BF16)

    from_inside(2)
    plane_part(3)
    pair_sum.step(3)

    @pl.when(core == 0)
    def _():
        for kind, gradient in enumerate((d_keys, d_values)):
            give_pair(kind).wait_recv()
            for part in range(4):
                at = pl.ds(part * row_tok, row_tok)
                summed = gradient[at] + pair_in[kind, at].astype(F32)
                head_give[kind + 1, part] = summed.astype(BF16)

    for kind in (1, 2):
        for step in range(1, 4):
            give_back(step, kind).start()
        d_heads[row, kind] = head_give[kind, row]
    pair_sum.step(4)
    pair_sum.step(5)
    collect.own_step()
    out_total[...] = collect.mine[0, col]
    for source in here.rows[1:]:
        for kind in range(3):
            arrived(d_heads.at[source, kind], back_recv.at[kind, source])
    for step in range(1, 4):
        give_near(step).wait_send()
        give_head(step).wait_send()
        for kind in range(3):
            give_back(step, kind).wait_send()

    @pl.when(core == 1)
    def _():
        for kind in range(2):
            give_pair(kind).wait_send()

    pair_sum.finish()
    spread.finish()
    collect.finish()


def attend_back_stage(
    d_attn, query, keys, values, mixed, total, cuts, out_weights, out_parts, early, scale, collective_id
):
    rows, width = d_attn.shape
    row_tok, group_tok = 4 * rows, 16 * rows
    vmem, hbm = pl.BlockSpec(memory_space=pltpu.VMEM), pl.BlockSpec(memory_space=pl.ANY)
    dma = pltpu.SemaphoreType.DMA
    return pl.pallas_call(
        functools.partial(back_kernel, scale),
        in_specs=[pl.BlockSpec(memory_space=pltpu.SMEM)] + [vmem] * 6 + [hbm] * 2 + [vmem],
        out_specs=[vmem] * 4,
        out_shape=[
            jax.ShapeDtypeStruct((row_tok, width), BF16),
            jax.ShapeDtypeStruct((4, 3, row_tok, HD), BF16),
            jax.ShapeDtypeStruct((rows, width), BF16),
            jax.ShapeDtypeStruct(early.shape, F32),
        ],
        scratch_shapes=[
            pltpu.VMEM((width, width), BF16),
            pltpu.VMEM((4, rows, 4 * HD), BF16),
            pltpu.VMEM((4, rows, 4 * HD), BF16),
            pltpu.VMEM((4, 4, rows, HD), BF16),
            pltpu.VMEM((HD, 2 * group_tok), BF16),
            pltpu.VMEM((2 * group_tok, HD), F32),
            pltpu.VMEM((2 * group_tok, HD), F32),
            pltpu.VMEM((HD, row_tok), F32),
            pltpu.VMEM((2, group_tok, HD), BF16),
            pltpu.VMEM((2, group_tok, HD), BF16),
            pltpu.VMEM((3, 4, row_tok, HD), BF16),
        ]
        + pair_sum_buffers(*early.shape)
        + [
            dma, dma((4, 4)), dma((4,)), dma((4,)), dma((4,)), dma((4,)),
            dma((4, 3)), dma((3, 4)), dma((2,)), dma((2,)),
        ]
        + collect_buffers(rows, width)
        + COLLECT_SEMS
        + SPREAD_SEMS,
        compiler_params=pltpu.CompilerParams(
            collective_id=collective_id, has_side_effects=True, vmem_limit_bytes=58 * 2**20
        ),
    )(cuts, d_attn, query, keys, values, mixed, total, out_weights, out_parts, early)


def tail_kernel(
    d_heads, qkv, totals, all_gains, cosine, sine, weights_in, normed_in, mixed_rows, d_attn_in,
    hidden,
    grad_hidden, grads, late_sum, last_sum,
    weights, normed, d_attn, in_sem, last, last_got, last_send, last_recv, hop, hop_got, hop_send, hop_recv,
    d_qkv, late, mixed, units, stat, scales, sums, sum_held, sum_got, sum_send, sum_recv,
    stat_send, stat_recv,
    line, line_in, whole, give, other, plane, corner_one, corner_two, from_across, from_along,
    up_send, down_send, line_recv, other_send, other_recv,
    one_send, one_recv, two_send, two_recv, across_send, across_recv, along_send, along_recv,
    back_send, back_recv,
):
    here = Here()
    row, col, core = here.row, here.col, here.core
    rows = hidden.shape[0]
    depth, columns = grads.shape
    part = depth // 2
    first, second = pl.ds(0, part // 2), pl.ds(part // 2, part // 2)
    order = here.near_first[::-1]
    qkv_columns = d_qkv.shape[1]
    tile = 512

    def line_products():
        @pl.loop(0, weights.shape[0] // tile)
        def _(index):
            at = pl.ds(pl.multiple_of(index * tile, tile), tile)
            product = contract_cols(d_qkv[...], weights[at]).astype(BF16)
            line[:, :, at] = product.reshape(4, rows, tile)

    line_halves = (pl.ds(0, rows // 2), pl.ds(rows // 2, rows // 2))

    def give_up(place, half):
        at = line_halves[half]
        sems = up_send.at[half, place], line_recv.at[half, place]
        return remote(line.at[place, at], line_in.at[place, at], *sems, here.at_col(col + 1))

    def give_down(place, slot, half):
        at = line_halves[half]
        sems = down_send.at[half, place], line_recv.at[half, slot]
        return remote(line.at[place, at], line_in.at[slot, at], *sems, here.at_col(col - 1))

    def add_line(place, slot, half):
        at = line_halves[half]
        arrived(line_in.at[slot, at], line_recv.at[half, slot])
        add_into(line.at[place, at], line_in.at[slot, at])

    def line_step(place):
        for half in range(2):

            @pl.when(((place > col) & (col > 0)) | ((place < col) & (col < 3)))
            def _():
                add_line(place, place, half)

            @pl.when(place > col)
            def _():
                give_up(place, half).start()

            @pl.when(place < col - 1)
            def _():
                give_down(place, place, half).start()

            @pl.when(place == col - 1)
            def _():
                give_down(place, 4, half).start()

    def row_product(which):
        of_row = here.rows[which]
        at = pl.ds(pl.multiple_of(of_row * depth, depth), depth)
        whole[:, pl.ds(0, qkv_columns)] = transposed_product(normed[:, at], d_qkv[...]).astype(BF16)
        whole[:, pl.ds(qkv_columns, columns - qkv_columns)] = transposed_product(
            mixed[...], d_attn[:, at]
        ).astype(BF16)
        plane[which] = whole[pl.ds(pl.multiple_of(core * part, part), part)]
        give[which] = whole[pl.ds(pl.multiple_of((1 - core) * part, part), part)]
        to_core(which).start()

    def to_core(which):
        sems = other_send.at[which], other_recv.at[which]
        return remote(give.at[which], other.at[which], *sems, here.other_core())

    def own_sum(which):
        to_core(which).wait_recv()
        add_into(plane.at[which], other.at[which])

    give_one = remote(
        plane.at[3, first], corner_one, one_send, one_recv, here.at_row(here.across)
    )
    give_two = remote(
        plane.at[3, second], corner_two, two_send, two_recv, here.at_row(here.along)
    )

    def give_across(index):
        at = (first, second)[index]
        sems = across_send.at[index], across_recv.at[index]
        return remote(plane.at[1, at], from_across.at[at], *sems, here.at_row(here.across))

    def give_along(index):
        at = (first, second)[index]
        sems = along_send.at[index], along_recv.at[index]
        return remote(plane.at[2, at], from_along.at[at], *sems, here.at_row(here.along))

    pair_sum = PairSum(here, late, late_sum, sum_held, sum_got, sum_send, sum_recv)
    takes = [
        pltpu.make_async_copy(source, target, in_sem.at[index])
        for index, (source, target) in enumerate(
            ((weights_in, weights), (normed_in, normed), (d_attn_in, d_attn))
        )
    ]
    for take in takes:
        take.start()
    near = [(step // 2, step % 2) for step in range(1, 8)]

    def near_device(step):
        which, swap = near[step]
        return (here.rows[which], col, (core + swap) % 2)

    greet([near_device(step) for step in range(7)] + here.line_peers())

    width = hidden.shape[1]
    heads = d_heads.shape[0]
    row_tok = d_qkv.shape[0]
    late[...] = jnp.zeros_like(late)
    for kind in range(2):
        root = lax.rsqrt(totals[kind : kind + 1] / width + EPSILON)
        scales[kind] = jnp.broadcast_to(root, (HD, row_tok)).T
        square = jnp.zeros((row_tok, HD), F32)
        for head in range(heads):
            start = (head * 3 + kind) * HD
            raw = qkv[:, start : start + HD]
            given = d_heads[head, kind].astype(F32)
            unit = given * cosine[...] + pltpu.roll(given * sine[...], HD // 2, 1)
            place = pl.ds(pl.multiple_of((col * heads + head) * HD, HD), HD)
            gains = all_gains[kind + 1 : kind + 2, place]
            gain_sum = jnp.sum(unit * raw * scales[kind], axis=0, keepdims=True)
            late[kind : kind + 1, place] = gain_sum
            weighted = unit * gains
            square = square + weighted * raw
            units[kind, head] = weighted
        stat[col, kind : kind + 1] = jnp.sum(square.T, axis=0, keepdims=True)

    def give_stat(step):
        peer = here.line_peers()[step]
        return remote(stat.at[col], stat.at[col], stat_send.at[step], stat_recv.at[col], peer)

    for step in range(3):
        give_stat(step).start()
    for head in range(heads):
        d_qkv[:, (head * 3 + 2) * HD : (head * 3 + 3) * HD] = d_heads[head, 2]
        mixed[:, head * HD : (head + 1) * HD] = mixed_rows[head]
    for step in range(3):
        place = (col + step + 1) % 4
        arrived(stat.at[place], stat_recv.at[place])
    total = stat[0] + stat[1] + stat[2] + stat[3]
    for kind in range(2):
        sums[...] = jnp.broadcast_to(total[kind : kind + 1] / width, (HD, row_tok)).T
        for head in range(heads):
            start = (head * 3 + kind) * HD
            raw = qkv[:, start : start + HD]
            root = scales[kind]
            d_raw = root * units[kind, head] - raw * (root * root * root) * sums[...]
            d_qkv[:, start : start + HD] = d_raw.astype(BF16)
    ends = (col == 0) | (col == 3)
    pair_sum.begin()
    for take in takes:
        take.wait()
    line_products()

    @pl.when(ends)
    def _():
        for place in order[:3]:
            line_step(place)

    def inner_step(place):
        @pl.when(jnp.logical_not(ends))
        def _():
            line_step(place)

    row_product(3)
    row_product(1)
    pair_sum.step(0)
    inner_step(order[0])
    own_sum(3)
    give_one.start()
    give_two.start()
    row_product(2)
    pair_sum.step(1)
    own_sum(1)
    give_across(0).start()
    own_sum(2)
    give_along(1).start()
    inner_step(order[1])
    row_product(0)
    pair_sum.step(2)
    inner_step(order[2])
    give_two.wait_recv()
    add_into(plane.at[1, second], corner_two)
    give_across(1).start()
    give_one.wait_recv()
    add_into(plane.at[2, first], corner_one)
    give_along(0).start()
    own_sum(0)

    for half in range(2):

        @pl.when(col > 0)
        def _():
            add_line(col, col, half)

        @pl.when(col < 3)
        def _():
            add_line(col, 4, half)

    given = line[col].astype(F32)
    tokens = hidden[...].astype(F32)
    root = lax.rsqrt(jnp.mean(tokens * tokens, axis=1, keepdims=True) + EPSILON)
    part_sum = jnp.sum(given * tokens * root, axis=0, keepdims=True)
    eighth = width // 8
    me = row * 2 + core
    for index in range(8):
        last[index : index + 1] = part_sum[:, index * eighth : (index + 1) * eighth]

    def give_last(step):
        sems = last_send.at[step], last_recv.at[me]
        return remote(last, last_got.at[me], *sems, near_device(step))

    def give_hop(step):
        sems = hop_send.at[step], hop_recv.at[col]
        return remote(hop, hop_got.at[col], *sems, here.line_peers()[step])

    for step in range(7):
        give_last(step).start()
    last_got[me] = last[...]
    weighted = given * all_gains[0:1]
    inner = jnp.mean(weighted * tokens, axis=1, keepdims=True)
    grad_hidden[...] = root * weighted - tokens * (root * root * root) * inner
    pair_sum.step(3)
    for step in range(7):
        which, swap = near[step]
        source = here.rows[which] * 2 + (core + swap) % 2
        arrived(last_got.at[source], last_recv.at[source])
    held = last_got[0]
    for index in range(1, 8):
        held = held + last_got[index]
    hop[...] = held
    hop_got[col] = held
    for step in range(3):
        give_hop(step).start()
    pair_sum.step(4)
    for index in range(2):
        give_across(index).wait_recv()
        give_along(index).wait_recv()
    add_into(plane.at[0], from_across, from_along)
    own_half = pl.ds(pl.multiple_of(core * part, part), part)
    give_back = remote(
        plane.at[0], grads.at[own_half], back_send, back_recv, here.other_core()
    )
    give_back.start()
    grads[own_half] = plane[0]
    other_half = grads.at[pl.ds(pl.multiple_of((1 - core) * part, part), part)]
    pair_sum.step(5)
    for step in range(3):
        place = (col + step + 1) % 4
        arrived(hop_got.at[place], hop_recv.at[place])
    last_sum[...] = hop_got[0] + hop_got[1] + hop_got[2] + hop_got[3]
    arrived(other_half, back_recv)
    for step in range(7):
        give_last(step).wait_send()
    for step in range(3):
        give_hop(step).wait_send()
    pair_sum.finish()
    for step in range(3):
        give_stat(step).wait_send()
    give_back.wait_send()
    give_one.wait_send()
    give_two.wait_send()
    for index in range(2):
        give_across(index).wait_send()
        give_along(index).wait_send()
    for which in range(4):
        to_core(which).wait_send()
    for place in order:
        for half in range(2):

            @pl.when(place > col)
            def _():
                give_up(place, half).wait_send()

            @pl.when(place < col)
            def _():
                give_down(place, place, half).wait_send()


def tail_stage(
    d_heads, qkv, totals, gains, cosine, sine, weights, normed, mixed_rows, d_attn, hidden, collective_id
):
    row_tok, qkv_columns = qkv.shape
    rows, width = hidden.shape
    depth = width // 4
    out_columns = width // 4
    columns = qkv_columns + out_columns
    part = depth // 2
    heads = d_heads.shape[0]
    vmem, hbm = pl.BlockSpec(memory_space=pltpu.VMEM), pl.BlockSpec(memory_space=pl.ANY)
    dma = pltpu.SemaphoreType.DMA
    eighth = (8, width // 8)
    one, four = pltpu.SemaphoreType.DMA, pltpu.SemaphoreType.DMA((4,))
    two = pltpu.SemaphoreType.DMA((2,))
    three = pltpu.SemaphoreType.DMA((3,))
    return pl.pallas_call(
        tail_kernel,
        in_specs=[vmem] * 6 + [hbm] * 2 + [vmem, hbm, vmem],
        out_specs=[vmem] * 4,
        out_shape=[
            jax.ShapeDtypeStruct((rows, width), F32),
            jax.ShapeDtypeStruct((depth, columns), BF16),
            jax.ShapeDtypeStruct((8, width), F32),
            jax.ShapeDtypeStruct(eighth, F32),
        ],
        scratch_shapes=[
            pltpu.VMEM(weights.shape, BF16),
            pltpu.VMEM(normed.shape, BF16),
            pltpu.VMEM(d_attn.shape, BF16),
            dma((3,)),
            pltpu.VMEM(eighth, F32),
            pltpu.VMEM((8,) + eighth, F32),
            dma((7,)),
            dma((8,)),
            pltpu.VMEM(eighth, F32),
            pltpu.VMEM((4,) + eighth, F32),
            dma((3,)),
            dma((4,)),
            pltpu.VMEM((row_tok, qkv_columns), BF16),
            pltpu.VMEM((8, width), F32),
            pltpu.VMEM((row_tok, heads * HD), BF16),
            pltpu.VMEM((2, heads, row_tok, HD), F32),
            pltpu.VMEM((4, 8, row_tok), F32),
            pltpu.VMEM((2, row_tok, HD), F32),
            pltpu.VMEM((row_tok, HD), F32),
        ]
        + pair_sum_buffers(8, width)
        + [
            three, four,
            pltpu.VMEM((4, rows, width), BF16),
            pltpu.VMEM((5, rows, width), BF16),
            pltpu.VMEM((depth, columns), BF16),
            pltpu.VMEM((4, part, columns), BF16),
            pltpu.VMEM((4, part, columns), BF16),
            pltpu.VMEM((4, part, columns), BF16),
            pltpu.VMEM((part // 2, columns), BF16),
            pltpu.VMEM((part // 2, columns), BF16),
            pltpu.VMEM((part, columns), BF16),
            pltpu.VMEM((part, columns), BF16),
            dma((2, 4)), dma((2, 4)), dma((2, 5)), four, four,
            one, one, one, one, two, two, two, two,
            one, one,
        ],
        compiler_params=pltpu.CompilerParams(
            collective_id=collective_id, has_side_effects=True, vmem_limit_bytes=58 * 2**20
        ),
    )(
        d_heads, qkv, totals, gains, cosine, sine, weights, normed, mixed_rows, d_attn, hidden
    )


def expert_rows(rows, grads, gate, gate_w, up_w, down_w):
    pre_gate = matmul(rows, gate_w)
    pre_up = matmul(rows, up_w)
    back = contract_cols(grads, down_w)
    sigmoid_gate = jax.nn.sigmoid(pre_gate)
    silu_gate = pre_gate * sigmoid_gate
    hidden = (silu_gate * pre_up).astype(BF16)
    inner = jnp.sum(hidden.astype(F32) * back, axis=-1)
    weighted = (hidden.astype(F32) * gate).astype(BF16)
    d_hid = back * gate
    d_pregate = (d_hid * pre_up * (sigmoid_gate + silu_gate * (1.0 - sigmoid_gate))).astype(BF16)
    d_preup = (d_hid * silu_gate).astype(BF16)
    outputs = matmul(weighted, down_w).astype(BF16)
    d_rows = (contract_cols(d_pregate, gate_w) + contract_cols(d_preup, up_w)).astype(BF16)
    return (
        outputs,
        d_rows,
        inner,
        contract_rows(rows, d_pregate),
        contract_rows(rows, d_preup),
        contract_rows(weighted, grads),
    )


def experts(normed, grads, dense_gates, gate_w, up_w, down_w):
    rows_dev, width = normed.shape
    devices = math.prod(lax.axis_size(axis) for axis in ALL)
    expert_count = dense_gates.shape[1]
    expert = lax.axis_index(ALL) // 2
    parts = max(1, lax.axis_size("exp") // 2)
    step = rows_dev // parts

    def one_part(sums, piece):
        rows, grad_rows, gates = piece
        rows_all = lax.all_gather(rows, ALL, axis=0, tiled=True)
        grads_all = lax.all_gather(grad_rows, ALL, axis=0, tiled=True)
        gates_all = lax.all_gather(gates, ALL, axis=0, tiled=True)
        gate = lax.dynamic_slice_in_dim(gates_all, expert, 1, 1)
        got = expert_rows(rows_all, grads_all, gate, gate_w, up_w, down_w)
        outputs = lax.psum_scatter(got[0], ALL, scatter_dimension=0, tiled=True)
        d_rows = lax.psum_scatter(got[1], ALL, scatter_dimension=0, tiled=True)
        inner = lax.all_to_all(
            got[2].reshape(devices, step), ALL, split_axis=0, concat_axis=0, tiled=True
        )
        inner = inner.reshape(expert_count, 2, step).sum(axis=1).T
        sums = got[3:] if sums is None else tuple(a + b for a, b in zip(sums, got[3:]))
        return sums, (outputs, d_rows, inner)

    if parts == 1:
        sums, (outputs, d_rows, inner) = one_part(None, (normed, grads, dense_gates))
    else:
        start = tuple(jnp.zeros(w.shape, F32) for w in (gate_w, up_w, down_w))
        pieces = tuple(v.reshape(parts, step, -1) for v in (normed, grads, dense_gates))
        sums, got = lax.scan(one_part, start, pieces)
        outputs, d_rows, inner = (v.reshape(rows_dev, -1) for v in got)
    return outputs.astype(F32), d_rows.astype(F32), inner, sums


def experts_here(normed, grads_all, picks, router, halves, others):
    numbers = jnp.arange(router.shape[1], dtype=jnp.int32)
    mask = jnp.any(picks.T[None] == numbers[:, None, None], axis=1).astype(F32)
    out_parts, d_rows, inner, weights = expert_stage(
        normed, grads_all, mask, halves, others, router, 1
    )
    inner = inner[:, :, 0].reshape(router.shape[1], -1).T
    return out_parts, d_rows.astype(F32), inner, weights


def shards(
    hidden_in,
    out_grad,
    attn_gain,
    w_qkv,
    q_gain,
    k_gain,
    w_out,
    moe_gain,
    router,
    w_gate,
    w_up,
    w_down,
    routes,
    doc_cuts,
):
    row_count, col_count = lax.axis_size("row"), lax.axis_size("col")
    tokens = hidden_in[0].astype(F32)
    rows_dev, width = tokens.shape
    heads = w_qkv.shape[1] // (3 * HD)
    plane = heads * HD
    scale = HD ** (-0.5)
    side = lax.axis_index("exp") % 2
    row_tok = rows_dev * col_count
    group_tok = row_tok * row_count
    here = (row_count, col_count, lax.axis_size("exp")) == (4, 4, 2)
    sequence = 0 if here else lax.axis_index("exp") // 2
    cuts = lax.dynamic_index_in_dim(doc_cuts, sequence, 0, keepdims=False)

    if here:
        grads_all = lax.all_gather(out_grad[0], ("row", "col"), axis=0, tiled=True)
        gains = jnp.stack([attn_gain, q_gain, k_gain, moe_gain]).astype(F32)
        other_w = [lax.ppermute(w[0], "exp", [(0, 1), (1, 0)]) for w in (w_gate, w_up, w_down)]

    gain_one = attn_gain.astype(F32)
    scale_one = rms_scale(tokens)
    head_start = lax.axis_index("col") * plane
    gain_q = lax.dynamic_slice_in_dim(q_gain, head_start, plane, 0).astype(F32)
    gain_k = lax.dynamic_slice_in_dim(k_gain, head_start, plane, 0).astype(F32)
    row_places = side * group_tok + lax.axis_index("row") * row_tok + jnp.arange(row_tok, dtype=jnp.int32)
    unused_doc, position = doc_positions(row_places, cuts)
    cosine, sine = rope_tables(position, HD)
    if here:
        signed = jnp.concatenate([-sine[:, : HD // 2], sine[:, HD // 2 :]], axis=1)
        normed_row, qkv_w, qkv, totals, query, keys, values = project(
            hidden_in[0], gains, w_qkv, cosine, signed, 0
        )
        total_q, total_k = totals[0], totals[1]
        query = query.reshape(group_tok, HD)
        key_all, value_all = keys.reshape(-1, HD), values.reshape(-1, HD)
    else:
        normed_one = (tokens * scale_one * gain_one).astype(BF16)
        normed_row = lax.all_gather(normed_one, "col", axis=0, tiled=True)
        qkv_w = lax.all_gather(w_qkv, "row", axis=0, tiled=True)
        out_w = lax.all_gather(
            lax.all_gather(w_out, "row", axis=1, tiled=True), "col", axis=0, tiled=True
        )
        qkv = matmul(normed_row, qkv_w)
    qkv = qkv.reshape(row_tok, heads, 3, HD)
    query_raw, key_raw, value_raw = qkv[:, :, 0], qkv[:, :, 1], qkv[:, :, 2]
    if not here:
        total_q, total_k = lax.psum(
            (jnp.sum(query_raw * query_raw, axis=(1, 2)), jnp.sum(key_raw * key_raw, axis=(1, 2))),
            "col",
        )
    scale_q = lax.rsqrt(total_q / width + EPSILON)[:, None, None]
    scale_k = lax.rsqrt(total_k / width + EPSILON)[:, None, None]
    gain_q, gain_k = gain_q.reshape(heads, HD), gain_k.reshape(heads, HD)
    cosine, sine = cosine[:, None, :], sine[:, None, :]
    if not here:
        query = rotate(query_raw * scale_q * gain_q, cosine, sine).astype(BF16)
        key = rotate(key_raw * scale_k * gain_k, cosine, sine).astype(BF16)
        moved = rows_to_heads(jnp.concatenate([query, key, value_raw.astype(BF16)], axis=-1))
        query, own_pair = moved[:, :HD], moved[:, HD:]
        earlier_pair = from_behind(own_pair, "exp", 1)
        lower_pair = jnp.where(side == 0, own_pair, earlier_pair)
        upper_pair = jnp.where(side == 0, jnp.zeros_like(own_pair), own_pair)
        key_value = jnp.concatenate([lower_pair, upper_pair], axis=0)
        key_all, value_all = key_value[:, :HD], key_value[:, HD:]

    if here:
        mixed_wide, total, out_w, mixed_rows, middle, normed_two = attention_stage(
            query, key_all, value_all, doc_cuts, w_out, hidden_in[0], gains, scale, 4
        )
    else:
        mixed_wide, total = attend(query, key_all, value_all, cuts, scale)
        mixed = mixed_wide.astype(BF16)
        middle = tokens + matmul(heads_to_tokens(mixed), out_w)

    gain_two = moe_gain.astype(F32)
    scale_two = rms_scale(middle)
    if not here:
        normed_two = (middle * scale_two * gain_two).astype(BF16)
    gates_all = jax.nn.softmax(matmul(normed_two, router), axis=-1)
    picks = routes[0]
    chosen = jnp.any(
        picks[:, :, None] == jnp.arange(router.shape[1], dtype=jnp.int32)[None, None, :], axis=1
    )
    grad_out = out_grad[0].astype(F32)
    expert_w = (w_gate[0], w_up[0], w_down[0])
    if here:
        out_parts, d_normed_two, inner, weight_grads = experts_here(
            normed_two, grads_all, picks, router, expert_w, other_w
        )
    else:
        dense_gates = jnp.where(chosen, gates_all, 0.0)
        mixture, d_normed_two, inner, weight_grads = experts(
            normed_two, out_grad[0], dense_gates, *expert_w
        )
    dense = jnp.where(chosen, inner, 0.0)
    d_logits = (gates_all * (dense - jnp.sum(gates_all * dense, axis=-1, keepdims=True))).astype(BF16)
    grad_router = contract_rows(d_logits, normed_two)
    d_normed_two = d_normed_two + contract_cols(d_logits, router)
    grad_moe_gain = jnp.sum(d_normed_two * middle * scale_two, axis=0)
    weighted_two = d_normed_two * gain_two
    d_middle = (
        grad_out
        + scale_two * weighted_two
        - middle * scale_two**3 * jnp.mean(weighted_two * middle, axis=-1, keepdims=True)
    )

    d_attn = d_middle.astype(BF16)
    if here:
        early = jnp.concatenate([grad_moe_gain[None], jnp.zeros((7, width), F32), grad_router])
        d_attn_row, d_heads, mixture, early = attend_back_stage(
            d_attn, query, key_all, value_all, mixed_wide, total, doc_cuts, out_w, out_parts, early, scale, 2
        )
        grad_hidden, grads, late, last = tail_stage(
            d_heads, qkv.reshape(row_tok, -1), totals, gains, cosine[:, 0], signed,
            qkv_w, normed_row, mixed_rows, d_attn_row, hidden_in[0], 3,
        )
        grad_hidden = d_middle + grad_hidden
        grad_qkv = grads[:, : 3 * plane].astype(F32)
        grad_w_out = grads[:, 3 * plane :].astype(F32)
        weight_grads = [value.astype(F32) for value in weight_grads]
        final = middle + mixture.astype(F32)
        summed = (last.reshape(-1), late[0], late[1], early[0], early[8:])
    else:
        final = middle + mixture
        mixed_row = heads_to_rows(mixed).reshape(row_tok, plane)
        d_mixed = tokens_to_heads(contract_cols(d_attn, out_w).astype(BF16))
        d_attn_row = lax.all_gather(d_attn, "col", axis=0, tiled=True)
        d_query, acc_key, acc_value = attend_back(
            query, key_all, value_all, d_mixed, mixed_wide, total, cuts, scale
        )
        accumulated = jnp.concatenate([acc_key, acc_value], axis=1)
        lower_acc, upper_acc = accumulated[:group_tok], accumulated[group_tok:]
        kept_acc = jnp.where(side == 0, lower_acc, upper_acc)
        later_acc = from_behind(lower_acc.astype(BF16), "exp", -1).astype(F32)
        summed_pair = kept_acc + jnp.where(side == 0, later_acc, jnp.zeros_like(later_acc))
        d_heads = heads_to_rows(jnp.concatenate([d_query, summed_pair], axis=1).astype(BF16)).astype(F32)
        d_q_unit = rotate_back(d_heads[:, :, :HD], cosine, sine)
        d_k_unit = rotate_back(d_heads[:, :, HD : 2 * HD], cosine, sine)
        d_value = d_heads[:, :, 2 * HD :]
        weighted_q = d_q_unit * gain_q
        weighted_k = d_k_unit * gain_k
        sum_q, sum_k = lax.psum(
            (jnp.sum(weighted_q * query_raw, axis=(1, 2)), jnp.sum(weighted_k * key_raw, axis=(1, 2))),
            "col",
        )
        d_query_raw = scale_q * weighted_q - query_raw * scale_q**3 * (sum_q / width)[:, None, None]
        d_key_raw = scale_k * weighted_k - key_raw * scale_k**3 * (sum_k / width)[:, None, None]
        grad_q_part = jnp.sum(d_q_unit * query_raw * scale_q, axis=0).reshape(plane)
        grad_k_part = jnp.sum(d_k_unit * key_raw * scale_k, axis=0).reshape(plane)
        d_qkv = jnp.concatenate([d_query_raw, d_key_raw, d_value], axis=2).astype(BF16)
        d_qkv = d_qkv.reshape(row_tok, heads * 3 * HD)
        d_normed_one = lax.psum_scatter(
            contract_cols(d_qkv, qkv_w).astype(BF16), "col", scatter_dimension=0, tiled=True
        ).astype(F32)
        grad_qkv = lax.psum_scatter(
            contract_rows(normed_row, d_qkv).astype(BF16), "row", scatter_dimension=0, tiled=True
        )
        grad_w_out = lax.psum_scatter(
            contract_rows(mixed_row, d_attn_row).astype(BF16), "row", scatter_dimension=1, tiled=True
        )
        grad_qkv = lax.psum(grad_qkv, "exp").astype(F32)
        grad_w_out = lax.psum(grad_w_out, "exp").astype(F32)
        grad_attn_gain = jnp.sum(d_normed_one * tokens * scale_one, axis=0)
        weighted_one = d_normed_one * gain_one
        grad_hidden = (
            d_middle
            + scale_one * weighted_one
            - tokens * scale_one**3 * jnp.mean(weighted_one * tokens, axis=-1, keepdims=True)
        )
        empty = jnp.zeros((width,), F32)
        grad_q_full = lax.dynamic_update_slice_in_dim(empty, grad_q_part, head_start, 0)
        grad_k_full = lax.dynamic_update_slice_in_dim(empty, grad_k_part, head_start, 0)
        parts = (grad_attn_gain, grad_q_full, grad_k_full, grad_moe_gain)
        summed = lax.psum(parts + (grad_router,), ALL)
    return (
        final.astype(BF16)[None],
        grad_hidden[None],
        summed[0],
        grad_qkv,
        summed[1],
        summed[2],
        grad_w_out,
        summed[3],
        summed[4].T,
        weight_grads[0][None],
        weight_grads[1][None],
        weight_grads[2][None],
    )


def solution(mesh):
    token_spec = P("exp", ("row", "col"), None)
    expert_spec = P(("row", "col", "exp"), None, None)
    in_specs = (
        token_spec,
        token_spec,
        P(),
        P("row", "col"),
        P(),
        P(),
        P("col", "row"),
        P(),
        P(),
        expert_spec,
        expert_spec,
        expert_spec,
        token_spec,
        P(),
    )
    out_specs = (
        token_spec,
        token_spec,
        P(),
        P("row", "col"),
        P(),
        P(),
        P("col", "row"),
        P(),
        P(),
        expert_spec,
        expert_spec,
        expert_spec,
    )
    return jax.shard_map(shards, mesh=mesh, in_specs=in_specs, out_specs=out_specs, check_vma=False)
```

```python
import functools
import math

import jax
import jax.numpy as jnp
from jax import lax
from jax.experimental import pallas as pl
from jax.experimental.pallas import tpu as pltpu
from jax.sharding import PartitionSpec as P

HD = 128
EPSILON = 1e-05
ROPE_BASE = 10000.0
MASKED = -1e30
BF16 = jnp.bfloat16
F32 = jnp.float32


def matmul(left, right):
    return jnp.dot(left, right, preferred_element_type=F32)


def contract_rows(left, right):
    return lax.dot_general(left, right, (((0,), (0,)), ((), ())), preferred_element_type=F32)


def contract_cols(left, right):
    return lax.dot_general(left, right, (((1,), (1,)), ((), ())), preferred_element_type=F32)


def rms_scale(values):
    return lax.rsqrt(jnp.mean(values * values, axis=-1, keepdims=True) + EPSILON)


def rope_tables(position, width):
    frequency = ROPE_BASE ** (-jnp.arange(0, width, 2, dtype=F32) / width)
    angle = position.astype(F32)[:, None] * frequency[None, :]
    return (
        jnp.concatenate([jnp.cos(angle)] * 2, axis=-1),
        jnp.concatenate([jnp.sin(angle)] * 2, axis=-1),
    )


def rotate(values, cosine, sine):
    half = values.shape[-1] // 2
    turned = jnp.concatenate([-values[..., half:], values[..., :half]], axis=-1)
    return values * cosine + turned * sine


def rotate_back(values, cosine, sine):
    half = values.shape[-1] // 2
    turned = values * sine
    return values * cosine + jnp.concatenate([turned[..., half:], -turned[..., :half]], axis=-1)


def doc_positions(places, cuts):
    first = (places >= cuts[0]).astype(jnp.int32)
    second = (places >= cuts[1]).astype(jnp.int32)
    start = first * cuts[0] + second * (cuts[1] - cuts[0])
    return (first + second, places - start)


def from_behind(value, axis, steps):
    count = lax.axis_size(axis)
    initial, last = (max(0, -steps), min(count, count - steps))
    return lax.ppermute(value, axis, [(source, source + steps) for source in range(initial, last)])


def rows_to_heads(values):
    count = lax.axis_size("row")
    rows, heads, width = values.shape
    moved = lax.all_to_all(values.transpose(1, 0, 2), "row", split_axis=0, concat_axis=0, tiled=True)
    return moved.reshape(count * rows, width)


def heads_to_rows(values):
    count = lax.axis_size("row")
    rows, width = values.shape
    moved = lax.all_to_all(
        values.reshape(count, rows // count, width), "row", split_axis=0, concat_axis=0, tiled=True
    )
    return moved.transpose(1, 0, 2)


def heads_to_tokens(values):
    row_count, col_count = lax.axis_size("row"), lax.axis_size("col")
    rows = values.shape[0] // (row_count * col_count)
    moved = lax.all_to_all(
        values.reshape(row_count * col_count, rows, HD),
        ("row", "col"),
        split_axis=0,
        concat_axis=0,
        tiled=True,
    )
    moved = moved.reshape(row_count, col_count, rows, HD).transpose(2, 1, 0, 3)
    return moved.reshape(rows, row_count * col_count * HD)


def tokens_to_heads(values):
    row_count, col_count = lax.axis_size("row"), lax.axis_size("col")
    rows = values.shape[0]
    parted = values.reshape(rows, col_count, row_count, HD).transpose(2, 1, 0, 3)
    moved = lax.all_to_all(
        parted.reshape(row_count * col_count, rows, HD),
        ("row", "col"),
        split_axis=0,
        concat_axis=0,
        tiled=True,
    )
    return moved.reshape(row_count * col_count * rows, HD)


MESH = pl.DeviceIdType.MESH
ALL = ("row", "col", "exp")


class Here:
    def __init__(self):
        self.row, self.col, self.core = (lax.axis_index(axis) for axis in ALL)
        self.across = self.row + 1 - 2 * (self.row % 2)
        self.along = (self.row + 2) % 4
        self.opposite = 3 - self.row
        self.rows = (self.row, self.across, self.along, self.opposite)
        half = self.col // 2
        self.near_first = [
            self.col,
            1 + self.col % 2,
            2 - self.col - self.col % 2 + 3 * half,
            3 - 3 * half,
        ]

    def at_row(self, row):
        return (row, self.col, self.core)

    def at_col(self, col):
        return (self.row, col, self.core)

    def other_core(self):
        return (self.row, self.col, 1 - self.core)

    def line_peers(self):
        return [self.at_col((self.col + step) % 4) for step in (1, 2, 3)]

    def group_peers(self):
        steps = range(1, 16)
        return [((self.row + s // 4) % 4, (self.col + s) % 4, self.core) for s in steps]

    def plane_peers(self):
        return [self.at_row(row) for row in self.rows[1:]]


def greet(peers):
    barrier = pltpu.get_barrier_semaphore()
    for peer in peers:
        pl.semaphore_signal(barrier, inc=1, device_id=peer, device_id_type=MESH)
    pl.semaphore_wait(barrier, len(peers))


def greet_near(here):
    barrier = pltpu.get_barrier_semaphore()
    col = here.col

    def signal(peer):
        pl.semaphore_signal(barrier, inc=1, device_id=peer, device_id_type=MESH)

    for peer in (here.other_core(), here.at_row(here.across), here.at_row(here.along)):
        signal(peer)

    @pl.when(col > 0)
    def _():
        signal(here.at_col(col - 1))

    @pl.when(col < 3)
    def _():
        signal(here.at_col(col + 1))

    pl.semaphore_wait(barrier, 3 + (col + 3) // 4 + (6 - col) // 4)


def remote(source, target, send, recv, device):
    return pltpu.make_async_remote_copy(
        src_ref=source,
        dst_ref=target,
        send_sem=send,
        recv_sem=recv,
        device_id=device,
        device_id_type=MESH,
    )


def arrived(target, recv):
    pltpu.make_async_copy(target, target, recv).wait()


def add_into(target, *terms):
    step = 16

    @pl.loop(0, target.shape[0] // step)
    def _(index):
        part = pl.ds(pl.multiple_of(index * step, step), step)
        value = target[part].astype(F32)
        for term in terms:
            value = value + term[part].astype(F32)
        target[part] = value.astype(target.dtype)


SPREAD_SEMS = [pltpu.SemaphoreType.DMA((4,))] * 11 + [pltpu.SemaphoreType.DMA((4, 4))] * 2


class Spread:
    def __init__(self, here, own, block, rows, sems, line=True, plane=True, core=True):
        self.here, self.own, self.block = here, own, block
        self.line, self.plane, self.core = line, plane, core
        (
            self.up_send, self.down_send, self.line_recv,
            self.across_send, self.across_recv, self.along_send, self.along_recv,
            self.one_send, self.one_recv, self.two_send, self.two_recv,
            self.core_send, self.core_recv,
        ) = sems
        self.first, self.second = pl.ds(0, rows // 2), pl.ds(rows // 2, rows // 2)
        self.order = here.near_first if line else [0]
        self.steps = len(self.order)

    def held(self, step):
        here = self.here
        return self.own if step == 0 else self.block(here.row, self.order[step], here.core)

    def up(self, step):
        here, place = self.here, self.order[step]
        target = self.block(here.row, place, here.core)
        recv = self.line_recv.at[place]
        return remote(self.held(step), target, self.up_send.at[place], recv, here.at_col(here.col + 1))

    def down(self, step):
        here, place = self.here, self.order[step]
        target = self.block(here.row, place, here.core)
        recv = self.line_recv.at[place]
        return remote(self.held(step), target, self.down_send.at[place], recv, here.at_col(here.col - 1))

    def to_across(self, step):
        here, place = self.here, self.order[step]
        target = self.block(here.row, place, here.core)
        sems = self.across_send.at[place], self.across_recv.at[place]
        return remote(self.held(step), target, *sems, here.at_row(here.across))

    def to_along(self, step):
        here, place = self.here, self.order[step]
        target = self.block(here.row, place, here.core)
        sems = self.along_send.at[place], self.along_recv.at[place]
        return remote(self.held(step), target, *sems, here.at_row(here.along))

    def corner_one(self, step):
        here, place = self.here, self.order[step]
        part = self.block(here.across, place, here.core).at[self.first]
        sems = self.one_send.at[place], self.one_recv.at[place]
        return remote(part, part, *sems, here.at_row(here.along))

    def corner_two(self, step):
        here, place = self.here, self.order[step]
        part = self.block(here.along, place, here.core).at[self.second]
        sems = self.two_send.at[place], self.two_recv.at[place]
        return remote(part, part, *sems, here.at_row(here.across))

    def to_core(self, which, step):
        here, place = self.here, self.order[step]
        target = self.block(here.rows[which], place, here.core)
        source = self.held(step) if which == 0 else target
        sems = self.core_send.at[which, place], self.core_recv.at[which, place]
        return remote(source, target, *sems, here.other_core())

    def line_step(self, step):
        here, place = self.here, self.order[step]
        if step > 0:
            arrived(self.held(step), self.line_recv.at[place])
        if self.line:

            @pl.when((place <= here.col) & (here.col < 3))
            def _():
                self.up(step).start()

            @pl.when((place >= here.col) & (here.col > 0))
            def _():
                self.down(step).start()

    def near_step(self, step):
        self.to_across(step).start()
        self.to_along(step).start()
        if self.core:
            self.to_core(0, step).start()

    def plane_step(self, step):
        here, place = self.here, self.order[step]
        arrived(self.block(here.across, place, here.core), self.across_recv.at[place])
        self.corner_one(step).start()
        if self.core:
            self.to_core(1, step).start()
        arrived(self.block(here.along, place, here.core), self.along_recv.at[place])
        self.corner_two(step).start()
        if self.core:
            self.to_core(2, step).start()

    def corner_step(self, step):
        here, place = self.here, self.order[step]
        target = self.block(here.opposite, place, here.core)
        arrived(target.at[self.first], self.one_recv.at[place])
        arrived(target.at[self.second], self.two_recv.at[place])
        if self.core:
            self.to_core(3, step).start()

    def step(self, index):
        if index < self.steps:
            self.line_step(index)
        if self.plane and 0 <= index - 1 < self.steps:
            self.plane_step(index - 1)
        if self.plane and index < self.steps:
            self.near_step(index)
        if self.plane and 0 <= index - 2 < self.steps:
            self.corner_step(index - 2)

    def core_arrived(self, which, step):
        here, place = self.here, self.order[step]
        target = self.block(here.rows[which], place, 1 - here.core)
        arrived(target, self.core_recv.at[which, place])

    def finish(self, arrivals=True):
        here = self.here
        for step in range(self.steps):
            place = self.order[step]
            if self.line:

                @pl.when((place <= here.col) & (here.col < 3))
                def _():
                    self.up(step).wait_send()

                @pl.when((place >= here.col) & (here.col > 0))
                def _():
                    self.down(step).wait_send()

            if self.plane:
                self.to_across(step).wait_send()
                self.to_along(step).wait_send()
                self.corner_one(step).wait_send()
                self.corner_two(step).wait_send()
                for which in range(4 if self.core else 0):
                    self.to_core(which, step).wait_send()
                    if arrivals:
                        self.core_arrived(which, step)


COLLECT_SEMS = (
    [pltpu.SemaphoreType.DMA((4,))] * 4
    + [pltpu.SemaphoreType.DMA((2, 4))] * 4
    + [pltpu.SemaphoreType.DMA((2, 4))] * 2
    + [pltpu.SemaphoreType.DMA((2, 5))]
)


def collect_buffers(rows, width):
    return [
        pltpu.VMEM((4, 4, rows, width), BF16),
        pltpu.VMEM((4, rows // 2, width), BF16),
        pltpu.VMEM((4, rows // 2, width), BF16),
        pltpu.VMEM((4, rows, width), BF16),
        pltpu.VMEM((4, rows, width), BF16),
        pltpu.VMEM((5, rows, width), BF16),
    ]


class Collect:
    def __init__(self, here, buffers, sems):
        self.here = here
        self.mine, self.one, self.two, self.from_across, self.from_along, self.line = buffers
        (
            self.one_send, self.one_recv, self.two_send, self.two_recv,
            self.across_send, self.across_recv, self.along_send, self.along_recv,
            self.up_send, self.down_send, self.line_recv,
        ) = sems
        half = self.mine.shape[2] // 2
        self.halves = (pl.ds(0, half), pl.ds(half, half))

    def give_one(self, place):
        here = self.here
        return remote(
            self.mine.at[3, place, self.halves[0]], self.one.at[place],
            self.one_send.at[place], self.one_recv.at[place], here.at_row(here.across),
        )

    def give_two(self, place):
        here = self.here
        return remote(
            self.mine.at[3, place, self.halves[1]], self.two.at[place],
            self.two_send.at[place], self.two_recv.at[place], here.at_row(here.along),
        )

    def give_across(self, place, half):
        here, part = self.here, self.halves[half]
        return remote(
            self.mine.at[1, place, part], self.from_across.at[place, part],
            self.across_send.at[half, place], self.across_recv.at[half, place], here.at_row(here.across),
        )

    def give_along(self, place, half):
        here, part = self.here, self.halves[half]
        return remote(
            self.mine.at[2, place, part], self.from_along.at[place, part],
            self.along_send.at[half, place], self.along_recv.at[half, place], here.at_row(here.along),
        )

    def give_up(self, place, half):
        here, part = self.here, self.halves[half]
        sems = self.up_send.at[half, place], self.line_recv.at[half, place]
        return remote(
            self.mine.at[0, place, part], self.line.at[place, part], *sems, here.at_col(here.col + 1)
        )

    def give_down(self, place, slot, half):
        here, part = self.here, self.halves[half]
        sems = self.down_send.at[half, place], self.line_recv.at[half, slot]
        return remote(
            self.mine.at[0, place, part], self.line.at[slot, part], *sems, here.at_col(here.col - 1)
        )

    def add_line(self, place, slot, half):
        part = self.halves[half]
        arrived(self.line.at[slot, part], self.line_recv.at[half, slot])
        add_into(self.mine.at[0, place, part], self.line.at[slot, part])

    def start_far(self, place):
        self.give_one(place).start()
        self.give_two(place).start()
        self.give_along(place, 1).start()

    def start_near(self, place):
        self.give_across(place, 0).start()

    def corner_step(self, place):
        self.give_two(place).wait_recv()
        add_into(self.mine.at[1, place, self.halves[1]], self.two.at[place])
        self.give_across(place, 1).start()
        self.give_one(place).wait_recv()
        add_into(self.mine.at[2, place, self.halves[0]], self.one.at[place])
        self.give_along(place, 0).start()

    def plane_step(self, place):
        for half in range(2):
            self.give_across(place, half).wait_recv()
            self.give_along(place, half).wait_recv()
        add_into(self.mine.at[0, place], self.from_across.at[place], self.from_along.at[place])

    def line_step(self, place):
        col = self.here.col
        for half in range(2):

            @pl.when(((place > col) & (col > 0)) | ((place < col) & (col < 3)))
            def _():
                self.add_line(place, place, half)

            @pl.when(place > col)
            def _():
                self.give_up(place, half).start()

            @pl.when(place < col - 1)
            def _():
                self.give_down(place, place, half).start()

            @pl.when(place == col - 1)
            def _():
                self.give_down(place, 4, half).start()

    def own_step(self):
        col = self.here.col
        for half in range(2):

            @pl.when(col > 0)
            def _():
                self.add_line(col, col, half)

            @pl.when(col < 3)
            def _():
                self.add_line(col, 4, half)

    def finish(self):
        col = self.here.col
        for place in range(4):
            self.give_one(place).wait_send()
            self.give_two(place).wait_send()
            for half in range(2):
                self.give_across(place, half).wait_send()
                self.give_along(place, half).wait_send()

                @pl.when(place > col)
                def _():
                    self.give_up(place, half).wait_send()

                @pl.when(place < col)
                def _():
                    self.give_down(place, place, half).wait_send()


def doc_start(places, cuts):
    return jnp.where(places >= cuts[1], cuts[1], jnp.where(places >= cuts[0], cuts[0], 0))


def key_blocks(cuts, first_query, rows, scores_of, block_fn):
    def scan(index, carry):
        start = pl.multiple_of(index * rows, rows)
        free = (start >= doc_start(first_query + rows - 1, cuts)) & (start + rows <= first_query + 1)

        @pl.when(free)
        def _():
            block_fn(start, scores_of(start))

        @pl.when(jnp.logical_not(free))
        def _():
            key_place = start + lax.broadcasted_iota(jnp.int32, (rows, rows), 0)
            place = first_query + lax.broadcasted_iota(jnp.int32, (1, rows), 1)
            allowed = (key_place <= place) & (key_place >= doc_start(place, cuts))
            block_fn(start, jnp.where(allowed, scores_of(start), MASKED))

        return carry

    lax.fori_loop(doc_start(first_query, cuts) // rows, first_query // rows + 1, scan, 0)


def attend_kernel(scale, group_tok, cuts, query, keys, values_t, mixed, total, top, summed, acc):
    rows = query.shape[0]
    side = lax.axis_index("exp") % 2
    first_query = side * group_tok + pl.program_id(0) * rows
    top[...] = jnp.full_like(top, MASKED)
    summed[...] = jnp.zeros_like(summed)
    acc[...] = jnp.zeros_like(acc)
    cut = (cuts[0, 0], cuts[0, 1])

    def scores_of(start):
        return contract_cols(keys[pl.ds(start, rows)], query[...]) * scale

    def block_fn(start, scores):
        old = top[...]
        new = jnp.maximum(old, jnp.max(scores, axis=0, keepdims=True))
        weights = jnp.exp(scores - new)
        decay = jnp.exp(old - new)
        top[...] = new
        summed[...] = summed[...] * decay + jnp.sum(weights, axis=0, keepdims=True)
        acc[...] = acc[...] * decay + matmul(values_t[:, pl.ds(start, rows)], weights.astype(BF16))

    key_blocks(cut, first_query, rows, scores_of, block_fn)
    mixed[...] = (acc[...] / summed[...]).T
    total[...] = top[...] + jnp.log(summed[...])


def attend(query, keys, values, cuts, scale, rows=512):
    group_tok, head_size = query.shape
    whole = lambda shape: pl.BlockSpec(shape, lambda i: (0, 0))
    return pl.pallas_call(
        functools.partial(attend_kernel, scale, group_tok),
        grid=(group_tok // rows,),
        in_specs=[
            pl.BlockSpec(memory_space=pltpu.SMEM),
            pl.BlockSpec((rows, head_size), lambda i: (i, 0)),
            whole(keys.shape),
            whole(values.shape[::-1]),
        ],
        out_specs=[
            pl.BlockSpec((rows, head_size), lambda i: (i, 0)),
            pl.BlockSpec((1, rows), lambda i: (0, i)),
        ],
        out_shape=[
            jax.ShapeDtypeStruct((group_tok, head_size), F32),
            jax.ShapeDtypeStruct((1, group_tok), F32),
        ],
        scratch_shapes=[
            pltpu.VMEM((1, rows), F32),
            pltpu.VMEM((1, rows), F32),
            pltpu.VMEM((head_size, rows), F32),
        ],
        compiler_params=pltpu.CompilerParams(vmem_limit_bytes=40 * 2**20),
        cost_estimate=pl.CostEstimate(
            flops=4 * 7 * 2**20 * head_size, bytes_accessed=2**23, transcendentals=7 * 2**20
        ),
    )(cuts[None], query, keys, values.T)


def attend_back_kernel(
    scale, group_tok, cuts, query, keys, keys_t, values, d_mixed, total, delta,
    d_query, d_keys, d_values, acc,
):
    rows = query.shape[0]
    side = lax.axis_index("exp") % 2
    first_query = side * group_tok + pl.program_id(0) * rows
    cut = (cuts[0, 0], cuts[0, 1])

    @pl.when(pl.program_id(0) == 0)
    def _():
        d_keys[...] = jnp.zeros_like(d_keys)
        d_values[...] = jnp.zeros_like(d_values)

    acc[...] = jnp.zeros_like(acc)

    def scores_of(start):
        return contract_cols(keys[pl.ds(start, rows)], query[...]) * scale

    def block_fn(start, scores):
        part = pl.ds(start, rows)
        weights = jnp.exp(scores - total[...])
        d_weights = contract_cols(values[part], d_mixed[...])
        d_scores = (weights * (d_weights - delta[...])).astype(BF16)
        d_values[part] += matmul(weights.astype(BF16), d_mixed[...])
        d_keys[part] += matmul(d_scores, query[...]) * scale
        acc[...] += matmul(keys_t[:, part], d_scores)

    key_blocks(cut, first_query, rows, scores_of, block_fn)
    d_query[...] = (acc[...] * scale).T


def attend_back(query, keys, values, d_mixed, mixed, total, cuts, scale, rows=512):
    group_tok, head_size = query.shape
    delta = jnp.sum(d_mixed.astype(F32) * mixed, axis=1)[None]
    whole = lambda shape: pl.BlockSpec(shape, lambda i: (0, 0))
    block = pl.BlockSpec((rows, head_size), lambda i: (i, 0))
    line = pl.BlockSpec((1, rows), lambda i: (0, i))
    return pl.pallas_call(
        functools.partial(attend_back_kernel, scale, group_tok),
        grid=(group_tok // rows,),
        in_specs=[
            pl.BlockSpec(memory_space=pltpu.SMEM),
            block,
            whole(keys.shape),
            whole(keys.shape[::-1]),
            whole(keys.shape),
            block,
            line,
            line,
        ],
        out_specs=[block, whole(keys.shape), whole(keys.shape)],
        out_shape=[
            jax.ShapeDtypeStruct((group_tok, head_size), F32),
            jax.ShapeDtypeStruct(keys.shape, F32),
            jax.ShapeDtypeStruct(keys.shape, F32),
        ],
        scratch_shapes=[pltpu.VMEM((head_size, rows), F32)],
        compiler_params=pltpu.CompilerParams(vmem_limit_bytes=48 * 2**20),
        cost_estimate=pl.CostEstimate(
            flops=10 * 7 * 2**20 * head_size, bytes_accessed=2**23, transcendentals=7 * 2**20
        ),
    )(cuts[None], query, keys, keys.T, values, d_mixed, total, delta)


def transposed_product(left, right):
    return jnp.dot(left.T, right, preferred_element_type=F32)


def column_of(line):
    return jnp.broadcast_to(line, (128, 128)).T[:, :1]


def line_of(column):
    return jnp.broadcast_to(column, (128, 128)).T[:1]


def expert_kernel(
    normed, grads_all, mask, gate_half, up_half, down_half,
    gate_other, up_other, down_other, router,
    rows_all, out_parts, total, inner_in, grad_gate, grad_up, grad_down,
    their_gates, their_down,
    gate_w, up_w, down_w, masks, x_buf, d_buf, gates_t, weighteds_t, d_gates, d_ups, weighteds, out_buf,
    inner, sum_buf, sum_down, *rest,
):
    here = Here()
    row, col, core = here.row, here.col, here.core
    rows, width = normed.shape
    half = gate_half.shape[1]
    expert = row * 4 + col
    count = len(SPREAD_SEMS)
    collect = Collect(here, rest[:6], rest[6 : 6 + len(COLLECT_SEMS)])
    rest = rest[6 + len(COLLECT_SEMS) :]
    (
        weight_sem, load_sem, store_sem, tile_sem, give_send, give_recv, their_sem, sum_sem,
        inner_send, inner_recv,
    ) = rest[:10]
    sems = rest[10:]

    def x_block(of_row, place, unused_core):
        return rows_all.at[pl.ds(pl.multiple_of((of_row * 4 + place) * rows, rows), rows)]

    def d_block(of_row, place, unused_core):
        return grads_all.at[pl.ds(pl.multiple_of((of_row * 4 + place) * rows, rows), rows)]

    def m_block(of_row, place, unused_core):
        return masks.at[of_row, place]

    spread_x = Spread(here, normed, x_block, rows, sems[:count], core=False)
    spread_m = Spread(here, mask, m_block, mask.shape[0], sems[count:], core=False)
    order = here.near_first

    own_half = pl.ds(pl.multiple_of(core * half, half), half)
    other_half = pl.ds(pl.multiple_of((1 - core) * half, half), half)
    keeps = [
        pltpu.make_async_copy(source, target, weight_sem.at[index])
        for index, (source, target) in enumerate(
            (
                (normed, x_block(row, col, 0)),
                (mask, m_block(row, col, 0)),
                (gate_half, gate_w.at[:, own_half]),
                (up_half, up_w.at[:, own_half]),
                (down_half, down_w.at[own_half]),
                (gate_other, gate_w.at[:, other_half]),
                (up_other, up_w.at[:, other_half]),
                (down_other, down_w.at[other_half]),
            )
        )
    ]
    greet(here.group_peers() + [here.other_core()])
    spread_x.step(0)
    spread_m.step(0)
    for keep in keeps:
        keep.start()

    turns = (3, 2, 1, 0)

    def loads(step):
        return [
            pltpu.make_async_copy(
                source(here.rows[which], order[step], 0),
                target.at[pl.ds(position * rows, rows)],
                load_sem.at[position, array],
            )
            for position, which in enumerate(turns)
            for array, (source, target) in enumerate(((x_block, x_buf), (d_block, d_buf)))
        ]

    def stores(step):
        return [
            pltpu.make_async_copy(
                out_buf.at[pl.ds(position * rows, rows)],
                out_parts.at[which, order[step]],
                store_sem.at[position],
            )
            for position, which in enumerate(turns)
        ]

    tile = 256

    def first_products(step):
        place = order[step]
        x = x_buf[...]
        lane = lax.broadcasted_iota(jnp.int32, (x.shape[0], router.shape[0]), 1)
        logits = contract_cols(x, router[...])
        raised = jnp.exp(logits - jnp.max(logits, axis=1, keepdims=True))
        picked = jnp.sum(jnp.where(lane == expert, raised, 0.0), axis=1, keepdims=True)
        routed = jnp.concatenate(
            [column_of(masks[here.rows[which], place, pl.ds(expert, 1)]) for which in turns]
        )
        gate = picked / jnp.sum(raised, axis=1, keepdims=True) * routed
        columns = [
            pl.ds(pl.multiple_of((here.rows[which] * 4 + place) * rows, rows), rows) for which in turns
        ]

        def tile_step(index, inner_sum):
            at = pl.ds(pl.multiple_of(index * tile, tile), tile)
            pre_gate = matmul(x_buf[...], gate_w[:, at])
            pre_up = matmul(x_buf[...], up_w[:, at])
            back = contract_cols(d_buf[...], down_w[at])
            sigmoid_gate = 0.5 * jnp.tanh(0.5 * pre_gate) + 0.5
            silu_gate = pre_gate * sigmoid_gate
            hidden = (silu_gate * pre_up).astype(BF16).astype(F32)
            d_hid = back * gate
            d_gate = (d_hid * pre_up * (sigmoid_gate + silu_gate * (1.0 - sigmoid_gate))).astype(BF16)
            d_up = (d_hid * silu_gate).astype(BF16)
            weight = (hidden * gate).astype(BF16)
            d_gates[:, at] = d_gate
            d_ups[:, at] = d_up
            weighteds[:, at] = weight
            side = index // (half // tile)
            first = pl.multiple_of(index % (half // tile) * tile, tile)
            for values, target in (
                (d_gate, gates_t.at[side, pl.ds(first, tile)]),
                (d_up, gates_t.at[side, pl.ds(first + half, tile)]),
                (weight, weighteds_t.at[at]),
            ):
                turned = values.T
                for position, column in enumerate(columns):
                    target[:, column] = turned[:, position * rows : (position + 1) * rows]
            return inner_sum + jnp.sum(hidden * back, axis=1, keepdims=True)

        start = jnp.zeros((x.shape[0], 1), F32)
        inner_sum = lax.fori_loop(0, gate_w.shape[1] // tile, tile_step, start, unroll=2)
        for position, which in enumerate(turns):
            part = slice(position * rows, (position + 1) * rows)
            inner[here.rows[which], place, 0:1] = line_of(inner_sum[part])

    def second_products(step):
        place = order[step]

        @pl.loop(0, width // tile, unroll=2)
        def _(index):
            at = pl.ds(pl.multiple_of(index * tile, tile), tile)
            out_buf[:, at] = matmul(weighteds[...], down_w[:, at]).astype(BF16)
            d_x = contract_cols(d_gates[...], gate_w[at]) + contract_cols(d_ups[...], up_w[at])
            d_x = d_x.astype(BF16)
            for position, which in enumerate(turns):
                collect.mine[which, place, :, at] = d_x[position * rows : (position + 1) * rows]

    for index in (1, 2):
        spread_x.step(index)
        spread_m.step(index)
    for keep in keeps:
        keep.wait()
    for copy in loads(0):
        copy.start()
    turn_order = (0, 1, 3, 2)
    ends = (col == 0) | (col == 3)

    def from_ends(step):
        @pl.when(ends)
        def _():
            collect.line_step(order[step])

    def from_inside(step):
        @pl.when(jnp.logical_not(ends))
        def _():
            collect.line_step(order[step])

    def start(step):
        collect.start_far(order[step])
        collect.start_near(order[step])

    for turn, step in enumerate(turn_order):
        for copy in loads(step):
            copy.wait()
        first_products(step)
        if turn < 2:
            spread_x.step(turn + 3)
            spread_m.step(turn + 3)
        if turn in (0, 2):
            for copy in loads(turn_order[turn + 1]):
                copy.start()
        if turn > 0:
            for copy in stores(turn_order[turn - 1]):
                copy.wait()
        if turn == 2:
            collect.corner_step(order[1])
        if turn == 3:
            collect.corner_step(order[3])
        second_products(step)
        for copy in stores(step):
            copy.start()
        if turn == 1:
            spread_x.step(5)
            spread_m.step(5)
            for copy in loads(turn_order[2]):
                copy.start()
            start(1)
            start(0)
        if turn == 2:
            start(3)
            collect.corner_step(order[0])
            collect.plane_step(order[1])
            from_ends(1)
        if turn == 3:
            start(2)
            collect.plane_step(order[3])
            from_ends(3)
            collect.plane_step(order[0])

    tiles = width // tile

    def tile_at(index):
        return pl.ds(pl.multiple_of(index * tile, tile), tile)

    def acts_of(kind, side):
        if kind == 0:
            return gates_t[side]
        return weighteds_t[pl.ds(pl.multiple_of(side * half, half), half)]

    counts = (2 * half, half)

    def slot_at(kind, slot):
        return pl.ds(pl.multiple_of((2 * kind + slot) * tile, tile), tile)

    def tile_buf(kind, slot):
        return gate_w.at[:, slot_at(kind, slot)]

    def give_buf(kind, slot):
        return up_w.at[pl.ds(0, counts[kind]), slot_at(kind, slot)]

    def their_buf(kind, slot):
        return up_w.at[pl.ds(width // 2, counts[kind]), slot_at(kind, slot)]

    theirs = (their_gates, their_down)

    def tile_load(kind, index, slot):
        source = (rows_all, grads_all)[kind]
        return pltpu.make_async_copy(
            source.at[:, tile_at(index)], tile_buf(kind, slot), tile_sem.at[slot]
        )

    def give(kind, index, slot):
        sems = give_send.at[slot, kind], give_recv.at[kind, index]
        return remote(give_buf(kind, slot), theirs[kind].at[:, tile_at(index)], *sems, here.other_core())

    def their_load(kind, index, slot):
        return pltpu.make_async_copy(
            theirs[kind].at[:, tile_at(index)],
            their_buf(kind, slot),
            their_sem.at[slot, kind],
        )

    def sum_stores(kind, index, slot):
        if kind == 1:
            target = grad_down.at[:, tile_at(index)]
            return [pltpu.make_async_copy(sum_down, target, sum_sem.at[0, 2])]
        return [
            pltpu.make_async_copy(
                sum_buf.at[slot, part], target.at[tile_at(index)], sum_sem.at[slot, part]
            )
            for part, target in enumerate((grad_gate, grad_up))
        ]

    def give_gradients(kind, start, stop):
        tile_load(kind, start, 0).start()

        @pl.loop(start, stop)
        def _(index):
            slot = index % 2

            @pl.when(index + 1 < stop)
            def _():
                tile_load(kind, index + 1, 1 - slot).start()

            tile_load(kind, index, slot).wait()
            product = matmul(acts_of(kind, 1 - core), tile_buf(kind, slot)[...])

            @pl.when(index >= 2)
            def _():
                give(kind, index - 2, slot).wait_send()

            give_buf(kind, slot)[...] = product.astype(BF16)
            give(kind, index, slot).start()

    def keep_gradients(kind, start, stop):
        tile_load(kind, start, 0).start()
        give(kind, start, 0).wait_recv()
        their_load(kind, start, 0).start()

        @pl.loop(start, stop)
        def _(index):
            slot = index % 2

            @pl.when(index + 1 < stop)
            def _():
                tile_load(kind, index + 1, 1 - slot).start()
                give(kind, index + 1, 1 - slot).wait_recv()
                their_load(kind, index + 1, 1 - slot).start()

            tile_load(kind, index, slot).wait()
            product = matmul(acts_of(kind, core), tile_buf(kind, slot)[...])
            their_load(kind, index, slot).wait()
            product = product + their_buf(kind, slot)[...].astype(F32)
            held = 2 - kind

            @pl.when(index >= held)
            def _():
                for copy in sum_stores(kind, index - held, slot):
                    copy.wait()

            if kind == 1:
                sum_down[...] = product.astype(BF16)
            else:
                sum_buf[slot, 0] = product[:half].T.astype(BF16)
                sum_buf[slot, 1] = product[half:].T.astype(BF16)
            for copy in sum_stores(kind, index, slot):
                copy.start()

    def give_inner(index):
        step = index + 1
        to_row, to_col = (row + step // 4) % 4, (col + step) % 4
        return remote(
            inner.at[to_row, to_col],
            inner_in.at[row, col],
            inner_send.at[index],
            inner_recv.at[row, col],
            (to_row, to_col, core),
        )

    for index in range(15):
        give_inner(index).start()
    inner_in[row, col] = inner[row, col]
    give_gradients(0, 0, tiles // 2)
    from_inside(3)
    collect.corner_step(order[2])
    give_gradients(0, tiles // 2, tiles)
    collect.plane_step(order[2])
    from_ends(2)
    give_gradients(1, 0, tiles)
    from_inside(2)
    keep_gradients(0, 0, tiles // 2)
    from_inside(1)
    keep_gradients(0, tiles // 2, tiles)
    keep_gradients(1, 0, tiles)
    collect.own_step()
    total[...] = collect.mine[0, col]

    for index in range(15):
        give_inner(index).wait_send()
        step = index + 1
        from_row, from_col = (row + 4 - step // 4) % 4, (col + 4 - step % 4) % 4
        arrived(inner_in.at[from_row, from_col], inner_recv.at[from_row, from_col])
    for copy in stores(turn_order[3]):
        copy.wait()
    for kind in range(2):
        for slot in range(2):
            give(kind, tiles - 2 + slot, slot).wait_send()
        for slot in range(2 - kind):
            for copy in sum_stores(kind, tiles - 2 + kind + slot, slot):
                copy.wait()
    spread_x.finish()
    spread_m.finish()
    collect.finish()


def expert_stage(normed, grads_all, mask, halves, others, router, collective_id):
    rows, width = normed.shape
    half = halves[0].shape[1]
    tokens = 16 * rows
    tile = 256
    vmem = pl.BlockSpec(memory_space=pltpu.VMEM)
    hbm = pl.BlockSpec(memory_space=pl.ANY)
    dma = pltpu.SemaphoreType.DMA
    blocks = jax.ShapeDtypeStruct((4, 4, rows, width), BF16)
    got = pl.pallas_call(
        expert_kernel,
        in_specs=[hbm] * 9 + [vmem],
        out_specs=[hbm] * 2 + [vmem] * 2 + [hbm] * 5,
        out_shape=[
            jax.ShapeDtypeStruct((tokens, width), BF16),
            blocks,
            jax.ShapeDtypeStruct((rows, width), BF16),
            jax.ShapeDtypeStruct((4, 4, 8, rows), F32),
            jax.ShapeDtypeStruct((width, half), BF16),
            jax.ShapeDtypeStruct((width, half), BF16),
            jax.ShapeDtypeStruct((half, width), BF16),
            jax.ShapeDtypeStruct((2 * half, width), BF16),
            jax.ShapeDtypeStruct((half, width), BF16),
        ],
        scratch_shapes=[
            pltpu.VMEM((width, 2 * half), BF16),
            pltpu.VMEM((width, 2 * half), BF16),
            pltpu.VMEM((2 * half, width), BF16),
            pltpu.VMEM((4, 4) + mask.shape, F32),
            pltpu.VMEM((4 * rows, width), BF16),
            pltpu.VMEM((4 * rows, width), BF16),
            pltpu.VMEM((2, 2 * half, tokens), BF16),
            pltpu.VMEM((2 * half, tokens), BF16),
            pltpu.VMEM((4 * rows, 2 * half), BF16),
            pltpu.VMEM((4 * rows, 2 * half), BF16),
            pltpu.VMEM((4 * rows, 2 * half), BF16),
            pltpu.VMEM((4 * rows, width), BF16),
            pltpu.VMEM((4, 4, 8, rows), F32),
            pltpu.VMEM((2, 2, tile, half), BF16),
            pltpu.VMEM((half, tile), BF16),
        ]
        + collect_buffers(rows, width)
        + COLLECT_SEMS
        + [
            dma((8,)), dma((4, 2)), dma((4,)),
            dma((2,)), dma((2, 2)), dma((2, width // tile)), dma((2, 2)), dma((2, 3)),
            dma((15,)), dma((4, 4)),
        ]
        + SPREAD_SEMS * 2,
        compiler_params=pltpu.CompilerParams(
            collective_id=collective_id, has_side_effects=True, vmem_limit_bytes=61 * 2**20
        ),
        cost_estimate=pl.CostEstimate(
            flops=18 * 2 * tokens * width * half,
            bytes_accessed=2**26,
            transcendentals=2 * tokens * half,
        ),
    )(normed, grads_all, mask, *halves, *others, router.T)
    return got[1], got[2], got[3], got[4:7]


def project_kernel(
    hidden, all_gains, weights, cosine, sine,
    normed_out, weights_out, qkv_out, totals, query, keys, values,
    normed, all_weights, qkv, out_sem,
    heads, stat, scale_q, scale_k, kept_sem, kept_kv_sem,
    stat_send, stat_recv, head_send, head_recv, pair_send, pair_recv, *sems,
):
    here = Here()
    row, col, core = here.row, here.col, here.core
    count = len(SPREAD_SEMS)
    rows, width = hidden.shape
    depth = weights.shape[0]
    part = depth // 2

    def weight_block(of_row, unused_place, of_core):
        return all_weights.at[pl.ds(pl.multiple_of(of_row * depth + of_core * part, part), part)]

    def normed_block(unused_row, place, unused_core):
        return normed.at[pl.ds(pl.multiple_of(place * rows, rows), rows)]

    own_weight = weights.at[pl.ds(pl.multiple_of(core * part, part), part)]
    spread_w = Spread(here, own_weight, weight_block, part, sems[:count], line=False)
    spread_n = Spread(
        here, normed_block(row, col, core), normed_block, rows, sems[count:], plane=False
    )
    greet(here.plane_peers() + here.line_peers() + [here.other_core()])
    spread_w.step(0)
    keep = pltpu.make_async_copy(own_weight, weight_block(row, 0, core), kept_sem)
    keep.start()

    values_in = hidden[...].astype(F32)
    scale_one = lax.rsqrt(jnp.mean(values_in * values_in, axis=1, keepdims=True) + EPSILON)
    own_rows = pl.ds(pl.multiple_of(col * rows, rows), rows)
    normed[own_rows] = (values_in * scale_one * all_gains[0:1]).astype(BF16)
    spread_n.step(0)
    spread_w.step(1)
    spread_n.step(1)
    spread_w.step(2)
    spread_n.step(2)
    spread_n.step(3)
    keep.wait()
    for which in range(4):
        spread_w.core_arrived(which, 0)
    puts = [
        pltpu.make_async_copy(source, target, out_sem.at[index])
        for index, (source, target) in enumerate(
            ((normed, normed_out), (all_weights, weights_out), (qkv, qkv_out))
        )
    ]
    puts[0].start()
    puts[1].start()
    columns = 256

    @pl.loop(0, qkv.shape[1] // columns)
    def _(index):
        at = pl.ds(pl.multiple_of(index * columns, columns), columns)
        qkv[:, at] = matmul(normed[...], all_weights[:, at])

    puts[2].start()

    plane = qkv.shape[1] // (3 * HD)
    for kind in range(2):
        square = jnp.zeros((qkv.shape[0], HD), F32)
        for head in range(plane):
            start = (head * 3 + kind) * HD
            raw = qkv[:, start : start + HD]
            square = square + raw * raw
        stat[col, kind : kind + 1] = jnp.sum(square.T, axis=0, keepdims=True)

    def give_stat(step):
        peer = here.line_peers()[step]
        return remote(stat.at[col], stat.at[col], stat_send.at[step], stat_recv.at[col], peer)

    for step in range(3):
        give_stat(step).start()
    for step in range(3):
        place = (col + step + 1) % 4
        arrived(stat.at[place], stat_recv.at[place])
    total = stat[0] + stat[1] + stat[2] + stat[3]
    totals[...] = total
    for kind, target in enumerate((scale_q, scale_k)):
        line = lax.rsqrt(total[kind : kind + 1] / width + EPSILON)
        target[...] = jnp.broadcast_to(line, (HD, line.shape[1])).T

    chunk = 64

    @pl.loop(0, qkv.shape[0] // chunk)
    def _(index):
        at = pl.ds(pl.multiple_of(index * chunk, chunk), chunk)
        for head in range(plane):
            place = pl.ds(pl.multiple_of((col * plane + head) * HD, HD), HD)
            for kind, scales in enumerate((scale_q, scale_k)):
                raw = qkv[at, pl.ds((head * 3 + kind) * HD, HD)]
                unit = raw * scales[at] * all_gains[kind + 1 : kind + 2, place]
                turned = pltpu.roll(unit, HD // 2, 1)
                heads[head, kind, at] = (unit * cosine[at] + turned * sine[at]).astype(BF16)
            heads[head, 2, at] = qkv[at, pl.ds((head * 3 + 2) * HD, HD)].astype(BF16)

    targets = (query.at[row], keys.at[1, row], values.at[1, row])

    def give_head(step, kind):
        dest = here.rows[step + 1]
        sems = head_send.at[step, kind], head_recv.at[kind, row]
        return remote(heads.at[dest, kind], targets[kind], *sems, here.at_row(dest))

    for kind in (1, 2, 0):
        for step in range(3):
            give_head(step, kind).start()

    def give_pair(source, kind):
        array = (keys, values)[kind]
        sems = pair_send.at[kind, source], pair_recv.at[kind, source]
        return remote(array.at[1, source], array.at[0, source], *sems, here.other_core())

    def keep_pair(source, kind):
        array = (keys, values)[kind]
        return pltpu.make_async_copy(
            array.at[1, source], array.at[0, source], kept_kv_sem.at[kind, source]
        )

    def pair_from(source):
        @pl.when(core == 0)
        def _():
            for kind in range(2):
                give_pair(source, kind).start()
                keep_pair(source, kind).start()

    for kind, array in ((1, keys), (2, values)):
        array[1, row] = heads[row, kind]
    query[row] = heads[row, 0]
    pair_from(row)
    for source in here.rows[1:]:
        arrived(keys.at[1, source], head_recv.at[1, source])
        arrived(values.at[1, source], head_recv.at[2, source])
        pair_from(source)
    for source in here.rows[1:]:
        arrived(query.at[source], head_recv.at[0, source])

    @pl.when(core == 0)
    def _():
        for source in range(4):
            for kind in range(2):
                give_pair(source, kind).wait_send()
                keep_pair(source, kind).wait()

    @pl.when(core == 1)
    def _():
        for source in range(4):
            for kind in range(2):
                give_pair(source, kind).wait_recv()

    for step in range(3):
        give_stat(step).wait_send()
        for kind in range(3):
            give_head(step, kind).wait_send()
    for put in puts:
        put.wait()
    spread_w.finish(arrivals=False)
    spread_n.finish()


def project(hidden, gains, weights, cosine, sine, collective_id):
    rows, width = hidden.shape
    depth, columns = weights.shape
    row_tok = 4 * rows
    plane = columns // (3 * HD)
    vmem = pl.BlockSpec(memory_space=pltpu.VMEM)
    hbm = pl.BlockSpec(memory_space=pl.ANY)
    return pl.pallas_call(
        project_kernel,
        in_specs=[vmem, vmem, hbm, vmem, vmem],
        out_specs=[hbm] * 3 + [vmem] * 4,
        out_shape=[
            jax.ShapeDtypeStruct((row_tok, width), BF16),
            jax.ShapeDtypeStruct((4 * depth, columns), BF16),
            jax.ShapeDtypeStruct((row_tok, columns), F32),
            jax.ShapeDtypeStruct((8, row_tok), F32),
            jax.ShapeDtypeStruct((4, row_tok, HD), BF16),
            jax.ShapeDtypeStruct((2, 4, row_tok, HD), BF16),
            jax.ShapeDtypeStruct((2, 4, row_tok, HD), BF16),
        ],
        scratch_shapes=[
            pltpu.VMEM((row_tok, width), BF16),
            pltpu.VMEM((4 * depth, columns), BF16),
            pltpu.VMEM((row_tok, columns), F32),
            pltpu.SemaphoreType.DMA((3,)),
            pltpu.VMEM((plane, 3, row_tok, HD), BF16),
            pltpu.VMEM((4, 8, row_tok), F32),
            pltpu.VMEM((row_tok, HD), F32),
            pltpu.VMEM((row_tok, HD), F32),
            pltpu.SemaphoreType.DMA,
            pltpu.SemaphoreType.DMA((2, 4)),
            pltpu.SemaphoreType.DMA((3,)),
            pltpu.SemaphoreType.DMA((4,)),
            pltpu.SemaphoreType.DMA((3, 3)),
            pltpu.SemaphoreType.DMA((3, 4)),
            pltpu.SemaphoreType.DMA((2, 4)),
            pltpu.SemaphoreType.DMA((2, 4)),
        ]
        + SPREAD_SEMS * 2,
        compiler_params=pltpu.CompilerParams(
            collective_id=collective_id, has_side_effects=True, vmem_limit_bytes=56 * 2**20
        ),
    )(hidden, gains, weights, cosine, sine)


def attention_kernel(
    scale, cuts, query, keys, values, out_weights, hidden, all_gains,
    mixed, total, whole_out, mixed_rows, middle, normed,
    all_out, put_sem, values_t, top, summed, acc, mixed_low, mixed_tok, kept_sem,
    row_send, row_recv, token_send, token_recv, *sems,
):
    here = Here()
    row, col, core = here.row, here.col, here.core
    rows = hidden.shape[0]
    row_tok = 4 * rows
    group_tok = 4 * row_tok
    side = out_weights.shape[0]

    def out_block(of_row, place, of_core):
        start = pl.multiple_of(place * side + of_core * (side // 2), side // 2)
        return all_out.at[pl.ds(start, side // 2), pl.ds(pl.multiple_of(of_row * side, side), side)]

    own_out = out_weights.at[pl.ds(pl.multiple_of(core * (side // 2), side // 2), side // 2)]
    spread = Spread(here, own_out, out_block, side // 2, sems)
    keep = pltpu.make_async_copy(own_out, out_block(row, col, core), kept_sem)
    keep.start()
    values_t[...] = values[...].T
    greet(here.plane_peers() + here.line_peers() + [here.other_core()])
    spread.step(0)
    cut = (cuts[0, 0], cuts[0, 1])
    last_query = 2 * group_tok - row_tok

    def queries(index):
        at = pl.ds(index * row_tok, row_tok)
        first_query = core * group_tok + index * row_tok
        top[...] = jnp.full_like(top, MASKED)
        summed[...] = jnp.zeros_like(summed)
        acc[...] = jnp.zeros_like(acc)

        def block_fn(part, scores):
            old = top[...]
            new = jnp.maximum(old, jnp.max(scores, axis=0, keepdims=True))
            weight = jnp.exp(scores - new)
            decay = jnp.exp(old - new)
            top[...] = new
            summed[...] = summed[...] * decay + jnp.sum(weight, axis=0, keepdims=True)
            acc[...] = acc[...] * decay + matmul(values_t[:, part], weight.astype(BF16))

        def scan(block, carry):
            first_key = block * row_tok
            part = pl.ds(pl.multiple_of(first_key, row_tok), row_tok)
            masked = (block == 0) | (first_key == first_query) | (first_query == last_query)

            @pl.when(jnp.logical_not(masked))
            def _():
                block_fn(part, contract_cols(keys[part], query[at]) * scale)

            @pl.when(masked)
            def _():
                key_place = first_key + lax.broadcasted_iota(jnp.int32, (row_tok, row_tok), 0)
                place = first_query + lax.broadcasted_iota(jnp.int32, (1, row_tok), 1)
                allowed = (key_place <= place) & (key_place >= doc_start(place, cut))
                scores = contract_cols(keys[part], query[at]) * scale
                block_fn(part, jnp.where(allowed, scores, MASKED))

            return carry

        lax.fori_loop(0, core * 4 + index + 1, scan, 0)
        got = (acc[...] / summed[...]).T
        mixed[at] = got
        mixed_low[index] = got.astype(BF16)
        total[:, at] = top[...] + jnp.log(summed[...])

        @pl.when(row != index)
        def _():
            give_row(index).start()

        @pl.when(row == index)
        def _():
            mixed_rows[row] = mixed_low[index]

    def give_row(index):
        sems_of = row_send.at[index], row_recv.at[row]
        return remote(mixed_low.at[index], mixed_rows.at[row], *sems_of, here.at_row(index))

    def give_token(step):
        place = (col + step) % 4
        part = pl.ds(pl.multiple_of(place * rows, rows), rows)
        sems_of = token_send.at[step], token_recv.at[col]
        return remote(mixed_rows.at[:, part], mixed_tok.at[col], *sems_of, here.at_col(place))

    for index in range(4):
        queries(index)
        spread.step(index + 1)
    for source in here.rows[1:]:
        arrived(mixed_rows.at[source], row_recv.at[source])
    for step in range(1, 4):
        give_token(step).start()
    mixed_tok[col] = mixed_rows[:, pl.ds(pl.multiple_of(col * rows, rows), rows)]
    spread.step(5)
    keep.wait()
    spread.finish()
    put = pltpu.make_async_copy(all_out, whole_out, put_sem)
    put.start()
    for step in range(1, 4):
        place = (col + 4 - step) % 4
        arrived(mixed_tok.at[place], token_recv.at[place])
    own = jnp.concatenate([mixed_tok[place, head] for place in range(4) for head in range(4)], axis=1)
    tile = 512

    @pl.loop(0, all_out.shape[1] // tile)
    def _(index):
        at = pl.ds(pl.multiple_of(index * tile, tile), tile)
        middle[:, at] = hidden[:, at].astype(F32) + matmul(own, all_out[:, at])

    values_in = middle[...]
    root = lax.rsqrt(jnp.mean(values_in * values_in, axis=1, keepdims=True) + EPSILON)
    normed[...] = (values_in * root * all_gains[3:4]).astype(BF16)
    put.wait()
    for index in range(4):

        @pl.when(row != index)
        def _():
            give_row(index).wait_send()

    for step in range(1, 4):
        give_token(step).wait_send()


def attention_stage(query, keys, values, cuts, out_weights, hidden, gains, scale, collective_id):
    rows, width = hidden.shape
    row_tok, group_tok = 4 * rows, 16 * rows
    vmem, hbm = pl.BlockSpec(memory_space=pltpu.VMEM), pl.BlockSpec(memory_space=pl.ANY)
    dma = pltpu.SemaphoreType.DMA
    return pl.pallas_call(
        functools.partial(attention_kernel, scale),
        in_specs=[pl.BlockSpec(memory_space=pltpu.SMEM)] + [vmem] * 3 + [hbm] + [vmem] * 2,
        out_specs=[vmem] * 2 + [hbm] + [vmem] * 3,
        out_shape=[
            jax.ShapeDtypeStruct((group_tok, HD), F32),
            jax.ShapeDtypeStruct((1, group_tok), F32),
            jax.ShapeDtypeStruct((width, width), BF16),
            jax.ShapeDtypeStruct((4, row_tok, HD), BF16),
            jax.ShapeDtypeStruct((rows, width), F32),
            jax.ShapeDtypeStruct((rows, width), BF16),
        ],
        scratch_shapes=[
            pltpu.VMEM((width, width), BF16),
            dma,
            pltpu.VMEM((HD, 2 * group_tok), BF16),
            pltpu.VMEM((1, row_tok), F32),
            pltpu.VMEM((1, row_tok), F32),
            pltpu.VMEM((HD, row_tok), F32),
            pltpu.VMEM((4, row_tok, HD), BF16),
            pltpu.VMEM((4, 4, rows, HD), BF16),
            dma, dma((4,)), dma((4,)), dma((4,)), dma((4,)),
        ]
        + SPREAD_SEMS,
        compiler_params=pltpu.CompilerParams(
            collective_id=collective_id, has_side_effects=True, vmem_limit_bytes=40 * 2**20
        ),
    )(cuts, query, keys, values, out_weights, hidden, gains)


class PairSum:
    def __init__(self, here, values, out, held, got, send, recv):
        self.here, self.values, self.out, self.held, self.got = here, values, out, held, got
        self.send, self.recv = send, recv
        col, half = here.col, values.shape[1] // 2
        self.own = pl.ds(pl.multiple_of(here.core * half, half), half)
        self.others = pl.ds(pl.multiple_of((1 - here.core) * half, half), half)
        self.peers = [
            here.at_row(here.across),
            here.at_row(here.along),
            here.at_col(col + 1 - 2 * (col % 2)),
            here.at_col((col + 2) % 4),
        ]

    def copy(self, step):
        here, sems = self.here, (self.send.at[step], self.recv.at[step])
        if step == 0:
            return remote(self.values.at[:, self.others], self.got.at[0], *sems, here.other_core())
        if step == 5:
            return remote(self.held.at[4], self.out.at[:, self.own], *sems, here.other_core())
        return remote(self.held.at[step - 1], self.got.at[step], *sems, self.peers[step - 1])

    def begin(self):
        self.copy(0).start()

    def step(self, index):
        if index == 5:
            arrived(self.out.at[:, self.others], self.recv.at[5])
            return
        self.copy(index).wait_recv()
        before = self.values[:, self.own] if index == 0 else self.held[index - 1]
        self.held[index] = before + self.got[index]
        if index == 4:
            self.out[:, self.own] = self.held[4]
        self.copy(index + 1).start()

    def finish(self):
        for index in range(6):
            self.copy(index).wait_send()


def pair_sum_buffers(rows, width):
    return [
        pltpu.VMEM((5, rows, width // 2), F32),
        pltpu.VMEM((5, rows, width // 2), F32),
        pltpu.SemaphoreType.DMA((6,)),
        pltpu.SemaphoreType.DMA((6,)),
    ]


def back_kernel(
    scale, cuts, d_attn, query, keys, values, mixed, total, out_weights, out_parts, early,
    d_attn_row, d_heads, out_total, early_sum,
    weights, d_mixed_give, d_mixed_row, d_mixed, keys_t, d_keys, d_values, acc, pair_out, pair_in,
    head_give, sum_held, sum_got, sum_send, sum_recv, weight_sem, load_sem,
    near_send, near_recv, head_send, head_recv, back_send, back_recv,
    pair_send, pair_recv, *rest,
):
    here = Here()
    row, col, core = here.row, here.col, here.core
    rows = d_attn.shape[0]
    row_tok = 4 * rows
    group_tok = 4 * row_tok
    plane = 4 * HD
    order = here.near_first[::-1]
    collect = Collect(here, rest[:6], rest[6 : 6 + len(COLLECT_SEMS)])
    sems = rest[6 + len(COLLECT_SEMS) :]

    def row_block(unused_row, place, unused_core):
        return d_attn_row.at[pl.ds(pl.multiple_of(place * rows, rows), rows)]

    spread = Spread(here, row_block(row, col, core), row_block, rows, sems, plane=False)
    pair_sum = PairSum(here, early, early_sum, sum_held, sum_got, sum_send, sum_recv)

    def load(which, place):
        return pltpu.make_async_copy(
            out_parts.at[which, place], collect.mine.at[which, place], load_sem.at[which, place]
        )

    load_weights = pltpu.make_async_copy(out_weights, weights, weight_sem)
    load_weights.start()
    for place in order:
        for which in (3, 2, 1, 0):
            load(which, place).start()
    keys_t[...] = keys[...].T
    d_attn_row[pl.ds(pl.multiple_of(col * rows, rows), rows)] = d_attn[...]
    greet(here.plane_peers() + here.line_peers() + [here.other_core()])

    def give_near(step):
        place = (col + step) % 4
        sems_of = near_send.at[step], near_recv.at[col]
        return remote(d_mixed_give.at[place], d_mixed_row.at[col], *sems_of, here.at_col(place))

    def give_head(step):
        dest = here.rows[step]
        part = pl.ds(pl.multiple_of(dest * HD, HD), HD)
        sems_of = head_send.at[step], head_recv.at[row]
        return remote(d_mixed_row.at[:, :, part], d_mixed.at[row], *sems_of, here.at_row(dest))

    def start(index):
        for which in (3, 2, 1):
            load(which, order[index]).wait()
        collect.start_far(order[index])
        collect.start_near(order[index])

    ends = (col == 0) | (col == 3)

    def from_ends(index):
        @pl.when(ends)
        def _():
            collect.line_step(order[index])

    def from_inside(index):
        @pl.when(jnp.logical_not(ends))
        def _():
            collect.line_step(order[index])

    def plane_part(index):
        load(0, order[index]).wait()
        collect.plane_step(order[index])

    start(0)
    pair_sum.begin()
    load_weights.wait()
    for step in (1, 2, 3, 0):
        place = (col + step) % 4
        part = pl.ds(pl.multiple_of(place * plane, plane), plane)
        product = contract_cols(d_attn[...], weights[part]).astype(BF16)
        if step == 0:
            d_mixed_row[col] = product
        else:
            d_mixed_give[place] = product
            give_near(step).start()
    spread.step(0)
    pair_sum.step(0)
    d_keys[...] = jnp.zeros_like(d_keys)
    d_values[...] = jnp.zeros_like(d_values)
    for step in range(1, 4):
        place = (col + 4 - step) % 4
        arrived(d_mixed_row.at[place], near_recv.at[place])
    for step in range(1, 4):
        give_head(step).start()
    d_mixed[row] = d_mixed_row[:, :, pl.ds(pl.multiple_of(row * HD, HD), HD)]
    collect.corner_step(order[0])
    start(1)
    pair_sum.step(1)
    spread.step(1)
    for source in here.rows[1:]:
        arrived(d_mixed.at[source], head_recv.at[source])

    cut = (cuts[0, 0], cuts[0, 1])
    last_query = 2 * group_tok - row_tok

    def queries(index):
        at = pl.ds(index * row_tok, row_tok)
        first_query = core * group_tok + index * row_tok
        gradient = d_mixed[index].reshape(row_tok, HD)
        delta = jnp.sum((gradient.astype(F32) * mixed[at]).T, axis=0, keepdims=True)
        sums = total[:, at]
        acc[...] = jnp.zeros_like(acc)

        def block_fn(part, scores):
            weight = jnp.exp(scores - sums)
            d_weight = contract_cols(values[part], gradient)
            d_scores = (weight * (d_weight - delta)).astype(BF16)
            d_values[part] += matmul(weight.astype(BF16), gradient)
            d_keys[part] += matmul(d_scores, query[at]) * scale
            acc[...] += matmul(keys_t[:, part], d_scores)

        def scan(block, carry):
            first_key = block * row_tok
            part = pl.ds(pl.multiple_of(first_key, row_tok), row_tok)
            masked = (block == 0) | (first_key == first_query) | (first_query == last_query)

            @pl.when(jnp.logical_not(masked))
            def _():
                block_fn(part, contract_cols(keys[part], query[at]) * scale)

            @pl.when(masked)
            def _():
                key_place = first_key + lax.broadcasted_iota(jnp.int32, (row_tok, row_tok), 0)
                place = first_query + lax.broadcasted_iota(jnp.int32, (1, row_tok), 1)
                allowed = (key_place <= place) & (key_place >= doc_start(place, cut))
                scores = contract_cols(keys[part], query[at]) * scale
                block_fn(part, jnp.where(allowed, scores, MASKED))

            return carry

        lax.fori_loop(0, core * 4 + index + 1, scan, 0)
        head_give[0, index] = (acc[...] * scale).T.astype(BF16)

    queries(0)
    plane_part(0)
    from_ends(0)
    collect.corner_step(order[1])
    start(2)
    spread.step(2)
    queries(1)
    from_inside(0)
    plane_part(1)
    from_ends(1)
    collect.corner_step(order[2])
    start(3)
    pair_sum.step(2)
    queries(2)
    from_inside(1)
    plane_part(2)
    from_ends(2)
    collect.corner_step(order[3])
    spread.step(3)
    queries(3)

    def give_back(step, kind):
        dest = here.rows[step]
        sems_of = back_send.at[step, kind], back_recv.at[kind, row]
        return remote(head_give.at[kind, dest], d_heads.at[row, kind], *sems_of, here.at_row(dest))

    def give_pair(kind):
        sems_of = pair_send.at[kind], pair_recv.at[kind]
        return remote(pair_out.at[kind], pair_in.at[kind], *sems_of, here.other_core())

    for step in range(1, 4):
        give_back(step, 0).start()
    d_heads[row, 0] = head_give[0, row]

    @pl.when(core == 1)
    def _():
        for kind, gradient in enumerate((d_keys, d_values)):
            pair_out[kind] = gradient[pl.ds(0, group_tok)].astype(BF16)
            give_pair(kind).start()
        for kind, gradient in enumerate((d_keys, d_values)):
            for part in range(4):
                at = pl.ds(group_tok + part * row_tok, row_tok)
                head_give[kind + 1, part] = gradient[at].astype(BF16)

    from_inside(2)
    plane_part(3)
    pair_sum.step(3)

    @pl.when(core == 0)
    def _():
        for kind, gradient in enumerate((d_keys, d_values)):
            give_pair(kind).wait_recv()
            for part in range(4):
                at = pl.ds(part * row_tok, row_tok)
                summed = gradient[at] + pair_in[kind, at].astype(F32)
                head_give[kind + 1, part] = summed.astype(BF16)

    for kind in (1, 2):
        for step in range(1, 4):
            give_back(step, kind).start()
        d_heads[row, kind] = head_give[kind, row]
    pair_sum.step(4)
    pair_sum.step(5)
    collect.own_step()
    out_total[...] = collect.mine[0, col]
    for source in here.rows[1:]:
        for kind in range(3):
            arrived(d_heads.at[source, kind], back_recv.at[kind, source])
    for step in range(1, 4):
        give_near(step).wait_send()
        give_head(step).wait_send()
        for kind in range(3):
            give_back(step, kind).wait_send()

    @pl.when(core == 1)
    def _():
        for kind in range(2):
            give_pair(kind).wait_send()

    pair_sum.finish()
    spread.finish()
    collect.finish()


def attend_back_stage(
    d_attn, query, keys, values, mixed, total, cuts, out_weights, out_parts, early, scale, collective_id
):
    rows, width = d_attn.shape
    row_tok, group_tok = 4 * rows, 16 * rows
    vmem, hbm = pl.BlockSpec(memory_space=pltpu.VMEM), pl.BlockSpec(memory_space=pl.ANY)
    dma = pltpu.SemaphoreType.DMA
    return pl.pallas_call(
        functools.partial(back_kernel, scale),
        in_specs=[pl.BlockSpec(memory_space=pltpu.SMEM)] + [vmem] * 6 + [hbm] * 2 + [vmem],
        out_specs=[vmem] * 4,
        out_shape=[
            jax.ShapeDtypeStruct((row_tok, width), BF16),
            jax.ShapeDtypeStruct((4, 3, row_tok, HD), BF16),
            jax.ShapeDtypeStruct((rows, width), BF16),
            jax.ShapeDtypeStruct(early.shape, F32),
        ],
        scratch_shapes=[
            pltpu.VMEM((width, width), BF16),
            pltpu.VMEM((4, rows, 4 * HD), BF16),
            pltpu.VMEM((4, rows, 4 * HD), BF16),
            pltpu.VMEM((4, 4, rows, HD), BF16),
            pltpu.VMEM((HD, 2 * group_tok), BF16),
            pltpu.VMEM((2 * group_tok, HD), F32),
            pltpu.VMEM((2 * group_tok, HD), F32),
            pltpu.VMEM((HD, row_tok), F32),
            pltpu.VMEM((2, group_tok, HD), BF16),
            pltpu.VMEM((2, group_tok, HD), BF16),
            pltpu.VMEM((3, 4, row_tok, HD), BF16),
        ]
        + pair_sum_buffers(*early.shape)
        + [
            dma, dma((4, 4)), dma((4,)), dma((4,)), dma((4,)), dma((4,)),
            dma((4, 3)), dma((3, 4)), dma((2,)), dma((2,)),
        ]
        + collect_buffers(rows, width)
        + COLLECT_SEMS
        + SPREAD_SEMS,
        compiler_params=pltpu.CompilerParams(
            collective_id=collective_id, has_side_effects=True, vmem_limit_bytes=58 * 2**20
        ),
    )(cuts, d_attn, query, keys, values, mixed, total, out_weights, out_parts, early)


def tail_kernel(
    d_heads, qkv, totals, all_gains, cosine, sine, weights_in, normed_in, mixed_rows, d_attn_in,
    hidden,
    grad_hidden, grads, late_sum, last_sum,
    weights, normed, d_attn, in_sem, last, last_got, last_send, last_recv, hop, hop_got, hop_send, hop_recv,
    d_qkv, late, mixed, units, stat, scales, sums, sum_held, sum_got, sum_send, sum_recv,
    stat_send, stat_recv,
    line, line_in, whole, give, other, plane, corner_one, corner_two, from_across, from_along,
    up_send, down_send, line_recv, other_send, other_recv,
    one_send, one_recv, two_send, two_recv, across_send, across_recv, along_send, along_recv,
    back_send, back_recv,
):
    here = Here()
    row, col, core = here.row, here.col, here.core
    rows = hidden.shape[0]
    depth, columns = grads.shape
    part = depth // 2
    first, second = pl.ds(0, part // 2), pl.ds(part // 2, part // 2)
    order = here.near_first[::-1]
    qkv_columns = d_qkv.shape[1]
    tile = 512

    def line_products():
        @pl.loop(0, weights.shape[0] // tile)
        def _(index):
            at = pl.ds(pl.multiple_of(index * tile, tile), tile)
            product = contract_cols(d_qkv[...], weights[at]).astype(BF16)
            line[:, :, at] = product.reshape(4, rows, tile)

    line_halves = (pl.ds(0, rows // 2), pl.ds(rows // 2, rows // 2))

    def give_up(place, half):
        at = line_halves[half]
        sems = up_send.at[half, place], line_recv.at[half, place]
        return remote(line.at[place, at], line_in.at[place, at], *sems, here.at_col(col + 1))

    def give_down(place, slot, half):
        at = line_halves[half]
        sems = down_send.at[half, place], line_recv.at[half, slot]
        return remote(line.at[place, at], line_in.at[slot, at], *sems, here.at_col(col - 1))

    def add_line(place, slot, half):
        at = line_halves[half]
        arrived(line_in.at[slot, at], line_recv.at[half, slot])
        add_into(line.at[place, at], line_in.at[slot, at])

    def line_step(place):
        for half in range(2):

            @pl.when(((place > col) & (col > 0)) | ((place < col) & (col < 3)))
            def _():
                add_line(place, place, half)

            @pl.when(place > col)
            def _():
                give_up(place, half).start()

            @pl.when(place < col - 1)
            def _():
                give_down(place, place, half).start()

            @pl.when(place == col - 1)
            def _():
                give_down(place, 4, half).start()

    def row_product(which):
        of_row = here.rows[which]
        at = pl.ds(pl.multiple_of(of_row * depth, depth), depth)
        whole[:, pl.ds(0, qkv_columns)] = transposed_product(normed[:, at], d_qkv[...]).astype(BF16)
        whole[:, pl.ds(qkv_columns, columns - qkv_columns)] = transposed_product(
            mixed[...], d_attn[:, at]
        ).astype(BF16)
        plane[which] = whole[pl.ds(pl.multiple_of(core * part, part), part)]
        give[which] = whole[pl.ds(pl.multiple_of((1 - core) * part, part), part)]
        to_core(which).start()

    def to_core(which):
        sems = other_send.at[which], other_recv.at[which]
        return remote(give.at[which], other.at[which], *sems, here.other_core())

    def own_sum(which):
        to_core(which).wait_recv()
        add_into(plane.at[which], other.at[which])

    give_one = remote(
        plane.at[3, first], corner_one, one_send, one_recv, here.at_row(here.across)
    )
    give_two = remote(
        plane.at[3, second], corner_two, two_send, two_recv, here.at_row(here.along)
    )

    def give_across(index):
        at = (first, second)[index]
        sems = across_send.at[index], across_recv.at[index]
        return remote(plane.at[1, at], from_across.at[at], *sems, here.at_row(here.across))

    def give_along(index):
        at = (first, second)[index]
        sems = along_send.at[index], along_recv.at[index]
        return remote(plane.at[2, at], from_along.at[at], *sems, here.at_row(here.along))

    pair_sum = PairSum(here, late, late_sum, sum_held, sum_got, sum_send, sum_recv)
    takes = [
        pltpu.make_async_copy(source, target, in_sem.at[index])
        for index, (source, target) in enumerate(
            ((weights_in, weights), (normed_in, normed), (d_attn_in, d_attn))
        )
    ]
    for take in takes:
        take.start()
    near = [(step // 2, step % 2) for step in range(1, 8)]

    def near_device(step):
        which, swap = near[step]
        return (here.rows[which], col, (core + swap) % 2)

    greet([near_device(step) for step in range(7)] + here.line_peers())

    width = hidden.shape[1]
    heads = d_heads.shape[0]
    row_tok = d_qkv.shape[0]
    late[...] = jnp.zeros_like(late)
    for kind in range(2):
        root = lax.rsqrt(totals[kind : kind + 1] / width + EPSILON)
        scales[kind] = jnp.broadcast_to(root, (HD, row_tok)).T
        square = jnp.zeros((row_tok, HD), F32)
        for head in range(heads):
            start = (head * 3 + kind) * HD
            raw = qkv[:, start : start + HD]
            given = d_heads[head, kind].astype(F32)
            unit = given * cosine[...] + pltpu.roll(given * sine[...], HD // 2, 1)
            place = pl.ds(pl.multiple_of((col * heads + head) * HD, HD), HD)
            gains = all_gains[kind + 1 : kind + 2, place]
            gain_sum = jnp.sum(unit * raw * scales[kind], axis=0, keepdims=True)
            late[kind : kind + 1, place] = gain_sum
            weighted = unit * gains
            square = square + weighted * raw
            units[kind, head] = weighted
        stat[col, kind : kind + 1] = jnp.sum(square.T, axis=0, keepdims=True)

    def give_stat(step):
        peer = here.line_peers()[step]
        return remote(stat.at[col], stat.at[col], stat_send.at[step], stat_recv.at[col], peer)

    for step in range(3):
        give_stat(step).start()
    for head in range(heads):
        d_qkv[:, (head * 3 + 2) * HD : (head * 3 + 3) * HD] = d_heads[head, 2]
        mixed[:, head * HD : (head + 1) * HD] = mixed_rows[head]
    for step in range(3):
        place = (col + step + 1) % 4
        arrived(stat.at[place], stat_recv.at[place])
    total = stat[0] + stat[1] + stat[2] + stat[3]
    for kind in range(2):
        sums[...] = jnp.broadcast_to(total[kind : kind + 1] / width, (HD, row_tok)).T
        for head in range(heads):
            start = (head * 3 + kind) * HD
            raw = qkv[:, start : start + HD]
            root = scales[kind]
            d_raw = root * units[kind, head] - raw * (root * root * root) * sums[...]
            d_qkv[:, start : start + HD] = d_raw.astype(BF16)
    ends = (col == 0) | (col == 3)
    pair_sum.begin()
    for take in takes:
        take.wait()
    line_products()

    @pl.when(ends)
    def _():
        for place in order[:3]:
            line_step(place)

    def inner_step(place):
        @pl.when(jnp.logical_not(ends))
        def _():
            line_step(place)

    row_product(3)
    row_product(1)
    pair_sum.step(0)
    inner_step(order[0])
    own_sum(3)
    give_one.start()
    give_two.start()
    row_product(2)
    pair_sum.step(1)
    own_sum(1)
    give_across(0).start()
    own_sum(2)
    give_along(1).start()
    inner_step(order[1])
    row_product(0)
    pair_sum.step(2)
    inner_step(order[2])
    give_two.wait_recv()
    add_into(plane.at[1, second], corner_two)
    give_across(1).start()
    give_one.wait_recv()
    add_into(plane.at[2, first], corner_one)
    give_along(0).start()
    own_sum(0)

    for half in range(2):

        @pl.when(col > 0)
        def _():
            add_line(col, col, half)

        @pl.when(col < 3)
        def _():
            add_line(col, 4, half)

    given = line[col].astype(F32)
    tokens = hidden[...].astype(F32)
    root = lax.rsqrt(jnp.mean(tokens * tokens, axis=1, keepdims=True) + EPSILON)
    part_sum = jnp.sum(given * tokens * root, axis=0, keepdims=True)
    eighth = width // 8
    me = row * 2 + core
    for index in range(8):
        last[index : index + 1] = part_sum[:, index * eighth : (index + 1) * eighth]

    def give_last(step):
        sems = last_send.at[step], last_recv.at[me]
        return remote(last, last_got.at[me], *sems, near_device(step))

    def give_hop(step):
        sems = hop_send.at[step], hop_recv.at[col]
        return remote(hop, hop_got.at[col], *sems, here.line_peers()[step])

    for step in range(7):
        give_last(step).start()
    last_got[me] = last[...]
    weighted = given * all_gains[0:1]
    inner = jnp.mean(weighted * tokens, axis=1, keepdims=True)
    grad_hidden[...] = root * weighted - tokens * (root * root * root) * inner
    pair_sum.step(3)
    for step in range(7):
        which, swap = near[step]
        source = here.rows[which] * 2 + (core + swap) % 2
        arrived(last_got.at[source], last_recv.at[source])
    held = last_got[0]
    for index in range(1, 8):
        held = held + last_got[index]
    hop[...] = held
    hop_got[col] = held
    for step in range(3):
        give_hop(step).start()
    pair_sum.step(4)
    for index in range(2):
        give_across(index).wait_recv()
        give_along(index).wait_recv()
    add_into(plane.at[0], from_across, from_along)
    own_half = pl.ds(pl.multiple_of(core * part, part), part)
    give_back = remote(
        plane.at[0], grads.at[own_half], back_send, back_recv, here.other_core()
    )
    give_back.start()
    grads[own_half] = plane[0]
    other_half = grads.at[pl.ds(pl.multiple_of((1 - core) * part, part), part)]
    pair_sum.step(5)
    for step in range(3):
        place = (col + step + 1) % 4
        arrived(hop_got.at[place], hop_recv.at[place])
    last_sum[...] = hop_got[0] + hop_got[1] + hop_got[2] + hop_got[3]
    arrived(other_half, back_recv)
    for step in range(7):
        give_last(step).wait_send()
    for step in range(3):
        give_hop(step).wait_send()
    pair_sum.finish()
    for step in range(3):
        give_stat(step).wait_send()
    give_back.wait_send()
    give_one.wait_send()
    give_two.wait_send()
    for index in range(2):
        give_across(index).wait_send()
        give_along(index).wait_send()
    for which in range(4):
        to_core(which).wait_send()
    for place in order:
        for half in range(2):

            @pl.when(place > col)
            def _():
                give_up(place, half).wait_send()

            @pl.when(place < col)
            def _():
                give_down(place, place, half).wait_send()


def tail_stage(
    d_heads, qkv, totals, gains, cosine, sine, weights, normed, mixed_rows, d_attn, hidden, collective_id
):
    row_tok, qkv_columns = qkv.shape
    rows, width = hidden.shape
    depth = width // 4
    out_columns = width // 4
    columns = qkv_columns + out_columns
    part = depth // 2
    heads = d_heads.shape[0]
    vmem, hbm = pl.BlockSpec(memory_space=pltpu.VMEM), pl.BlockSpec(memory_space=pl.ANY)
    dma = pltpu.SemaphoreType.DMA
    eighth = (8, width // 8)
    one, four = pltpu.SemaphoreType.DMA, pltpu.SemaphoreType.DMA((4,))
    two = pltpu.SemaphoreType.DMA((2,))
    three = pltpu.SemaphoreType.DMA((3,))
    return pl.pallas_call(
        tail_kernel,
        in_specs=[vmem] * 6 + [hbm] * 2 + [vmem, hbm, vmem],
        out_specs=[vmem] * 4,
        out_shape=[
            jax.ShapeDtypeStruct((rows, width), F32),
            jax.ShapeDtypeStruct((depth, columns), BF16),
            jax.ShapeDtypeStruct((8, width), F32),
            jax.ShapeDtypeStruct(eighth, F32),
        ],
        scratch_shapes=[
            pltpu.VMEM(weights.shape, BF16),
            pltpu.VMEM(normed.shape, BF16),
            pltpu.VMEM(d_attn.shape, BF16),
            dma((3,)),
            pltpu.VMEM(eighth, F32),
            pltpu.VMEM((8,) + eighth, F32),
            dma((7,)),
            dma((8,)),
            pltpu.VMEM(eighth, F32),
            pltpu.VMEM((4,) + eighth, F32),
            dma((3,)),
            dma((4,)),
            pltpu.VMEM((row_tok, qkv_columns), BF16),
            pltpu.VMEM((8, width), F32),
            pltpu.VMEM((row_tok, heads * HD), BF16),
            pltpu.VMEM((2, heads, row_tok, HD), F32),
            pltpu.VMEM((4, 8, row_tok), F32),
            pltpu.VMEM((2, row_tok, HD), F32),
            pltpu.VMEM((row_tok, HD), F32),
        ]
        + pair_sum_buffers(8, width)
        + [
            three, four,
            pltpu.VMEM((4, rows, width), BF16),
            pltpu.VMEM((5, rows, width), BF16),
            pltpu.VMEM((depth, columns), BF16),
            pltpu.VMEM((4, part, columns), BF16),
            pltpu.VMEM((4, part, columns), BF16),
            pltpu.VMEM((4, part, columns), BF16),
            pltpu.VMEM((part // 2, columns), BF16),
            pltpu.VMEM((part // 2, columns), BF16),
            pltpu.VMEM((part, columns), BF16),
            pltpu.VMEM((part, columns), BF16),
            dma((2, 4)), dma((2, 4)), dma((2, 5)), four, four,
            one, one, one, one, two, two, two, two,
            one, one,
        ],
        compiler_params=pltpu.CompilerParams(
            collective_id=collective_id, has_side_effects=True, vmem_limit_bytes=58 * 2**20
        ),
    )(
        d_heads, qkv, totals, gains, cosine, sine, weights, normed, mixed_rows, d_attn, hidden
    )


def expert_rows(rows, grads, gate, gate_w, up_w, down_w):
    pre_gate = matmul(rows, gate_w)
    pre_up = matmul(rows, up_w)
    back = contract_cols(grads, down_w)
    sigmoid_gate = jax.nn.sigmoid(pre_gate)
    silu_gate = pre_gate * sigmoid_gate
    hidden = (silu_gate * pre_up).astype(BF16)
    inner = jnp.sum(hidden.astype(F32) * back, axis=-1)
    weighted = (hidden.astype(F32) * gate).astype(BF16)
    d_hid = back * gate
    d_pregate = (d_hid * pre_up * (sigmoid_gate + silu_gate * (1.0 - sigmoid_gate))).astype(BF16)
    d_preup = (d_hid * silu_gate).astype(BF16)
    outputs = matmul(weighted, down_w).astype(BF16)
    d_rows = (contract_cols(d_pregate, gate_w) + contract_cols(d_preup, up_w)).astype(BF16)
    return (
        outputs,
        d_rows,
        inner,
        contract_rows(rows, d_pregate),
        contract_rows(rows, d_preup),
        contract_rows(weighted, grads),
    )


def experts(normed, grads, dense_gates, gate_w, up_w, down_w):
    rows_dev, width = normed.shape
    devices = math.prod(lax.axis_size(axis) for axis in ALL)
    expert_count = dense_gates.shape[1]
    expert = lax.axis_index(ALL) // 2
    parts = max(1, lax.axis_size("exp") // 2)
    step = rows_dev // parts

    def one_part(sums, piece):
        rows, grad_rows, gates = piece
        rows_all = lax.all_gather(rows, ALL, axis=0, tiled=True)
        grads_all = lax.all_gather(grad_rows, ALL, axis=0, tiled=True)
        gates_all = lax.all_gather(gates, ALL, axis=0, tiled=True)
        gate = lax.dynamic_slice_in_dim(gates_all, expert, 1, 1)
        got = expert_rows(rows_all, grads_all, gate, gate_w, up_w, down_w)
        outputs = lax.psum_scatter(got[0], ALL, scatter_dimension=0, tiled=True)
        d_rows = lax.psum_scatter(got[1], ALL, scatter_dimension=0, tiled=True)
        inner = lax.all_to_all(
            got[2].reshape(devices, step), ALL, split_axis=0, concat_axis=0, tiled=True
        )
        inner = inner.reshape(expert_count, 2, step).sum(axis=1).T
        sums = got[3:] if sums is None else tuple(a + b for a, b in zip(sums, got[3:]))
        return sums, (outputs, d_rows, inner)

    if parts == 1:
        sums, (outputs, d_rows, inner) = one_part(None, (normed, grads, dense_gates))
    else:
        start = tuple(jnp.zeros(w.shape, F32) for w in (gate_w, up_w, down_w))
        pieces = tuple(v.reshape(parts, step, -1) for v in (normed, grads, dense_gates))
        sums, got = lax.scan(one_part, start, pieces)
        outputs, d_rows, inner = (v.reshape(rows_dev, -1) for v in got)
    return outputs.astype(F32), d_rows.astype(F32), inner, sums


def experts_here(normed, grads_all, picks, router, halves, others):
    numbers = jnp.arange(router.shape[1], dtype=jnp.int32)
    mask = jnp.any(picks.T[None] == numbers[:, None, None], axis=1).astype(F32)
    out_parts, d_rows, inner, weights = expert_stage(
        normed, grads_all, mask, halves, others, router, 1
    )
    inner = inner[:, :, 0].reshape(router.shape[1], -1).T
    return out_parts, d_rows.astype(F32), inner, weights


def shards(
    hidden_in,
    out_grad,
    attn_gain,
    w_qkv,
    q_gain,
    k_gain,
    w_out,
    moe_gain,
    router,
    w_gate,
    w_up,
    w_down,
    routes,
    doc_cuts,
):
    row_count, col_count = lax.axis_size("row"), lax.axis_size("col")
    tokens = hidden_in[0].astype(F32)
    rows_dev, width = tokens.shape
    heads = w_qkv.shape[1] // (3 * HD)
    plane = heads * HD
    scale = HD ** (-0.5)
    side = lax.axis_index("exp") % 2
    row_tok = rows_dev * col_count
    group_tok = row_tok * row_count
    here = (row_count, col_count, lax.axis_size("exp")) == (4, 4, 2)
    sequence = 0 if here else lax.axis_index("exp") // 2
    cuts = lax.dynamic_index_in_dim(doc_cuts, sequence, 0, keepdims=False)

    if here:
        grads_all = lax.all_gather(out_grad[0], ("row", "col"), axis=0, tiled=True)
        gains = jnp.stack([attn_gain, q_gain, k_gain, moe_gain]).astype(F32)
        other_w = [lax.ppermute(w[0], "exp", [(0, 1), (1, 0)]) for w in (w_gate, w_up, w_down)]

    gain_one = attn_gain.astype(F32)
    scale_one = rms_scale(tokens)
    head_start = lax.axis_index("col") * plane
    gain_q = lax.dynamic_slice_in_dim(q_gain, head_start, plane, 0).astype(F32)
    gain_k = lax.dynamic_slice_in_dim(k_gain, head_start, plane, 0).astype(F32)
    row_places = side * group_tok + lax.axis_index("row") * row_tok + jnp.arange(row_tok, dtype=jnp.int32)
    unused_doc, position = doc_positions(row_places, cuts)
    cosine, sine = rope_tables(position, HD)
    if here:
        signed = jnp.concatenate([-sine[:, : HD // 2], sine[:, HD // 2 :]], axis=1)
        normed_row, qkv_w, qkv, totals, query, keys, values = project(
            hidden_in[0], gains, w_qkv, cosine, signed, 0
        )
        total_q, total_k = totals[0], totals[1]
        query = query.reshape(group_tok, HD)
        key_all, value_all = keys.reshape(-1, HD), values.reshape(-1, HD)
    else:
        normed_one = (tokens * scale_one * gain_one).astype(BF16)
        normed_row = lax.all_gather(normed_one, "col", axis=0, tiled=True)
        qkv_w = lax.all_gather(w_qkv, "row", axis=0, tiled=True)
        out_w = lax.all_gather(
            lax.all_gather(w_out, "row", axis=1, tiled=True), "col", axis=0, tiled=True
        )
        qkv = matmul(normed_row, qkv_w)
    qkv = qkv.reshape(row_tok, heads, 3, HD)
    query_raw, key_raw, value_raw = qkv[:, :, 0], qkv[:, :, 1], qkv[:, :, 2]
    if not here:
        total_q, total_k = lax.psum(
            (jnp.sum(query_raw * query_raw, axis=(1, 2)), jnp.sum(key_raw * key_raw, axis=(1, 2))),
            "col",
        )
    scale_q = lax.rsqrt(total_q / width + EPSILON)[:, None, None]
    scale_k = lax.rsqrt(total_k / width + EPSILON)[:, None, None]
    gain_q, gain_k = gain_q.reshape(heads, HD), gain_k.reshape(heads, HD)
    cosine, sine = cosine[:, None, :], sine[:, None, :]
    if not here:
        query = rotate(query_raw * scale_q * gain_q, cosine, sine).astype(BF16)
        key = rotate(key_raw * scale_k * gain_k, cosine, sine).astype(BF16)
        moved = rows_to_heads(jnp.concatenate([query, key, value_raw.astype(BF16)], axis=-1))
        query, own_pair = moved[:, :HD], moved[:, HD:]
        earlier_pair = from_behind(own_pair, "exp", 1)
        lower_pair = jnp.where(side == 0, own_pair, earlier_pair)
        upper_pair = jnp.where(side == 0, jnp.zeros_like(own_pair), own_pair)
        key_value = jnp.concatenate([lower_pair, upper_pair], axis=0)
        key_all, value_all = key_value[:, :HD], key_value[:, HD:]

    if here:
        mixed_wide, total, out_w, mixed_rows, middle, normed_two = attention_stage(
            query, key_all, value_all, doc_cuts, w_out, hidden_in[0], gains, scale, 4
        )
    else:
        mixed_wide, total = attend(query, key_all, value_all, cuts, scale)
        mixed = mixed_wide.astype(BF16)
        middle = tokens + matmul(heads_to_tokens(mixed), out_w)

    gain_two = moe_gain.astype(F32)
    scale_two = rms_scale(middle)
    if not here:
        normed_two = (middle * scale_two * gain_two).astype(BF16)
    gates_all = jax.nn.softmax(matmul(normed_two, router), axis=-1)
    picks = routes[0]
    chosen = jnp.any(
        picks[:, :, None] == jnp.arange(router.shape[1], dtype=jnp.int32)[None, None, :], axis=1
    )
    grad_out = out_grad[0].astype(F32)
    expert_w = (w_gate[0], w_up[0], w_down[0])
    if here:
        out_parts, d_normed_two, inner, weight_grads = experts_here(
            normed_two, grads_all, picks, router, expert_w, other_w
        )
    else:
        dense_gates = jnp.where(chosen, gates_all, 0.0)
        mixture, d_normed_two, inner, weight_grads = experts(
            normed_two, out_grad[0], dense_gates, *expert_w
        )
    dense = jnp.where(chosen, inner, 0.0)
    d_logits = (gates_all * (dense - jnp.sum(gates_all * dense, axis=-1, keepdims=True))).astype(BF16)
    grad_router = contract_rows(d_logits, normed_two)
    d_normed_two = d_normed_two + contract_cols(d_logits, router)
    grad_moe_gain = jnp.sum(d_normed_two * middle * scale_two, axis=0)
    weighted_two = d_normed_two * gain_two
    d_middle = (
        grad_out
        + scale_two * weighted_two
        - middle * scale_two**3 * jnp.mean(weighted_two * middle, axis=-1, keepdims=True)
    )

    d_attn = d_middle.astype(BF16)
    if here:
        early = jnp.concatenate([grad_moe_gain[None], jnp.zeros((7, width), F32), grad_router])
        d_attn_row, d_heads, mixture, early = attend_back_stage(
            d_attn, query, key_all, value_all, mixed_wide, total, doc_cuts, out_w, out_parts, early, scale, 2
        )
        grad_hidden, grads, late, last = tail_stage(
            d_heads, qkv.reshape(row_tok, -1), totals, gains, cosine[:, 0], signed,
            qkv_w, normed_row, mixed_rows, d_attn_row, hidden_in[0], 3,
        )
        grad_hidden = d_middle + grad_hidden
        grad_qkv = grads[:, : 3 * plane].astype(F32)
        grad_w_out = grads[:, 3 * plane :].astype(F32)
        weight_grads = [value.astype(F32) for value in weight_grads]
        final = middle + mixture.astype(F32)
        summed = (last.reshape(-1), late[0], late[1], early[0], early[8:])
    else:
        final = middle + mixture
        mixed_row = heads_to_rows(mixed).reshape(row_tok, plane)
        d_mixed = tokens_to_heads(contract_cols(d_attn, out_w).astype(BF16))
        d_attn_row = lax.all_gather(d_attn, "col", axis=0, tiled=True)
        d_query, acc_key, acc_value = attend_back(
            query, key_all, value_all, d_mixed, mixed_wide, total, cuts, scale
        )
        accumulated = jnp.concatenate([acc_key, acc_value], axis=1)
        lower_acc, upper_acc = accumulated[:group_tok], accumulated[group_tok:]
        kept_acc = jnp.where(side == 0, lower_acc, upper_acc)
        later_acc = from_behind(lower_acc.astype(BF16), "exp", -1).astype(F32)
        summed_pair = kept_acc + jnp.where(side == 0, later_acc, jnp.zeros_like(later_acc))
        d_heads = heads_to_rows(jnp.concatenate([d_query, summed_pair], axis=1).astype(BF16)).astype(F32)
        d_q_unit = rotate_back(d_heads[:, :, :HD], cosine, sine)
        d_k_unit = rotate_back(d_heads[:, :, HD : 2 * HD], cosine, sine)
        d_value = d_heads[:, :, 2 * HD :]
        weighted_q = d_q_unit * gain_q
        weighted_k = d_k_unit * gain_k
        sum_q, sum_k = lax.psum(
            (jnp.sum(weighted_q * query_raw, axis=(1, 2)), jnp.sum(weighted_k * key_raw, axis=(1, 2))),
            "col",
        )
        d_query_raw = scale_q * weighted_q - query_raw * scale_q**3 * (sum_q / width)[:, None, None]
        d_key_raw = scale_k * weighted_k - key_raw * scale_k**3 * (sum_k / width)[:, None, None]
        grad_q_part = jnp.sum(d_q_unit * query_raw * scale_q, axis=0).reshape(plane)
        grad_k_part = jnp.sum(d_k_unit * key_raw * scale_k, axis=0).reshape(plane)
        d_qkv = jnp.concatenate([d_query_raw, d_key_raw, d_value], axis=2).astype(BF16)
        d_qkv = d_qkv.reshape(row_tok, heads * 3 * HD)
        d_normed_one = lax.psum_scatter(
            contract_cols(d_qkv, qkv_w).astype(BF16), "col", scatter_dimension=0, tiled=True
        ).astype(F32)
        grad_qkv = lax.psum_scatter(
            contract_rows(normed_row, d_qkv).astype(BF16), "row", scatter_dimension=0, tiled=True
        )
        grad_w_out = lax.psum_scatter(
            contract_rows(mixed_row, d_attn_row).astype(BF16), "row", scatter_dimension=1, tiled=True
        )
        grad_qkv = lax.psum(grad_qkv, "exp").astype(F32)
        grad_w_out = lax.psum(grad_w_out, "exp").astype(F32)
        grad_attn_gain = jnp.sum(d_normed_one * tokens * scale_one, axis=0)
        weighted_one = d_normed_one * gain_one
        grad_hidden = (
            d_middle
            + scale_one * weighted_one
            - tokens * scale_one**3 * jnp.mean(weighted_one * tokens, axis=-1, keepdims=True)
        )
        empty = jnp.zeros((width,), F32)
        grad_q_full = lax.dynamic_update_slice_in_dim(empty, grad_q_part, head_start, 0)
        grad_k_full = lax.dynamic_update_slice_in_dim(empty, grad_k_part, head_start, 0)
        parts = (grad_attn_gain, grad_q_full, grad_k_full, grad_moe_gain)
        summed = lax.psum(parts + (grad_router,), ALL)
    return (
        final.astype(BF16)[None],
        grad_hidden[None],
        summed[0],
        grad_qkv,
        summed[1],
        summed[2],
        grad_w_out,
        summed[3],
        summed[4].T,
        weight_grads[0][None],
        weight_grads[1][None],
        weight_grads[2][None],
    )


def solution(mesh):
    token_spec = P("exp", ("row", "col"), None)
    expert_spec = P(("row", "col", "exp"), None, None)
    in_specs = (
        token_spec,
        token_spec,
        P(),
        P("row", "col"),
        P(),
        P(),
        P("col", "row"),
        P(),
        P(),
        expert_spec,
        expert_spec,
        expert_spec,
        token_spec,
        P(),
    )
    out_specs = (
        token_spec,
        token_spec,
        P(),
        P("row", "col"),
        P(),
        P(),
        P("col", "row"),
        P(),
        P(),
        expert_spec,
        expert_spec,
        expert_spec,
    )
    return jax.shard_map(shards, mesh=mesh, in_specs=in_specs, out_specs=out_specs, check_vma=False)
```

```python
import functools
import math

import jax
import jax.numpy as jnp
from jax import lax
from jax.experimental import pallas as pl
from jax.experimental.pallas import tpu as pltpu
from jax.sharding import PartitionSpec as P

HD = 128
EPSILON = 1e-05
ROPE_BASE = 10000.0
MASKED = -1e30
BF16 = jnp.bfloat16
F32 = jnp.float32


def matmul(left, right):
    return jnp.dot(left, right, preferred_element_type=F32)


def contract_rows(left, right):
    return lax.dot_general(left, right, (((0,), (0,)), ((), ())), preferred_element_type=F32)


def contract_cols(left, right):
    return lax.dot_general(left, right, (((1,), (1,)), ((), ())), preferred_element_type=F32)


def rms_scale(values):
    return lax.rsqrt(jnp.mean(values * values, axis=-1, keepdims=True) + EPSILON)


def rope_tables(position, width):
    frequency = ROPE_BASE ** (-jnp.arange(0, width, 2, dtype=F32) / width)
    angle = position.astype(F32)[:, None] * frequency[None, :]
    return (
        jnp.concatenate([jnp.cos(angle)] * 2, axis=-1),
        jnp.concatenate([jnp.sin(angle)] * 2, axis=-1),
    )


def rotate(values, cosine, sine):
    half = values.shape[-1] // 2
    turned = jnp.concatenate([-values[..., half:], values[..., :half]], axis=-1)
    return values * cosine + turned * sine


def rotate_back(values, cosine, sine):
    half = values.shape[-1] // 2
    turned = values * sine
    return values * cosine + jnp.concatenate([turned[..., half:], -turned[..., :half]], axis=-1)


def doc_positions(places, cuts):
    first = (places >= cuts[0]).astype(jnp.int32)
    second = (places >= cuts[1]).astype(jnp.int32)
    start = first * cuts[0] + second * (cuts[1] - cuts[0])
    return (first + second, places - start)


def from_behind(value, axis, steps):
    count = lax.axis_size(axis)
    initial, last = (max(0, -steps), min(count, count - steps))
    return lax.ppermute(value, axis, [(source, source + steps) for source in range(initial, last)])


def rows_to_heads(values):
    count = lax.axis_size("row")
    rows, heads, width = values.shape
    moved = lax.all_to_all(values.transpose(1, 0, 2), "row", split_axis=0, concat_axis=0, tiled=True)
    return moved.reshape(count * rows, width)


def heads_to_rows(values):
    count = lax.axis_size("row")
    rows, width = values.shape
    moved = lax.all_to_all(
        values.reshape(count, rows // count, width), "row", split_axis=0, concat_axis=0, tiled=True
    )
    return moved.transpose(1, 0, 2)


def heads_to_tokens(values):
    row_count, col_count = lax.axis_size("row"), lax.axis_size("col")
    rows = values.shape[0] // (row_count * col_count)
    moved = lax.all_to_all(
        values.reshape(row_count * col_count, rows, HD),
        ("row", "col"),
        split_axis=0,
        concat_axis=0,
        tiled=True,
    )
    moved = moved.reshape(row_count, col_count, rows, HD).transpose(2, 1, 0, 3)
    return moved.reshape(rows, row_count * col_count * HD)


def tokens_to_heads(values):
    row_count, col_count = lax.axis_size("row"), lax.axis_size("col")
    rows = values.shape[0]
    parted = values.reshape(rows, col_count, row_count, HD).transpose(2, 1, 0, 3)
    moved = lax.all_to_all(
        parted.reshape(row_count * col_count, rows, HD),
        ("row", "col"),
        split_axis=0,
        concat_axis=0,
        tiled=True,
    )
    return moved.reshape(row_count * col_count * rows, HD)


MESH = pl.DeviceIdType.MESH
ALL = ("row", "col", "exp")


class Here:
    def __init__(self):
        self.row, self.col, self.core = (lax.axis_index(axis) for axis in ALL)
        self.across = self.row + 1 - 2 * (self.row % 2)
        self.along = (self.row + 2) % 4
        self.opposite = 3 - self.row
        self.rows = (self.row, self.across, self.along, self.opposite)
        half = self.col // 2
        self.near_first = [
            self.col,
            1 + self.col % 2,
            2 - self.col - self.col % 2 + 3 * half,
            3 - 3 * half,
        ]

    def at_row(self, row):
        return (row, self.col, self.core)

    def at_col(self, col):
        return (self.row, col, self.core)

    def other_core(self):
        return (self.row, self.col, 1 - self.core)

    def line_peers(self):
        return [self.at_col((self.col + step) % 4) for step in (1, 2, 3)]

    def group_peers(self):
        steps = range(1, 16)
        return [((self.row + s // 4) % 4, (self.col + s) % 4, self.core) for s in steps]

    def plane_peers(self):
        return [self.at_row(row) for row in self.rows[1:]]


def greet(peers):
    barrier = pltpu.get_barrier_semaphore()
    for peer in peers:
        pl.semaphore_signal(barrier, inc=1, device_id=peer, device_id_type=MESH)
    pl.semaphore_wait(barrier, len(peers))


def greet_near(here):
    barrier = pltpu.get_barrier_semaphore()
    col = here.col

    def signal(peer):
        pl.semaphore_signal(barrier, inc=1, device_id=peer, device_id_type=MESH)

    for peer in (here.other_core(), here.at_row(here.across), here.at_row(here.along)):
        signal(peer)

    @pl.when(col > 0)
    def _():
        signal(here.at_col(col - 1))

    @pl.when(col < 3)
    def _():
        signal(here.at_col(col + 1))

    pl.semaphore_wait(barrier, 3 + (col + 3) // 4 + (6 - col) // 4)


def remote(source, target, send, recv, device):
    return pltpu.make_async_remote_copy(
        src_ref=source,
        dst_ref=target,
        send_sem=send,
        recv_sem=recv,
        device_id=device,
        device_id_type=MESH,
    )


def arrived(target, recv):
    pltpu.make_async_copy(target, target, recv).wait()


def add_into(target, *terms):
    step = 16

    @pl.loop(0, target.shape[0] // step)
    def _(index):
        part = pl.ds(pl.multiple_of(index * step, step), step)
        value = target[part].astype(F32)
        for term in terms:
            value = value + term[part].astype(F32)
        target[part] = value.astype(target.dtype)


SPREAD_SEMS = [pltpu.SemaphoreType.DMA((4,))] * 11 + [pltpu.SemaphoreType.DMA((4, 4))] * 2


class Spread:
    def __init__(self, here, own, block, rows, sems, line=True, plane=True, core=True):
        self.here, self.own, self.block = here, own, block
        self.line, self.plane, self.core = line, plane, core
        (
            self.up_send, self.down_send, self.line_recv,
            self.across_send, self.across_recv, self.along_send, self.along_recv,
            self.one_send, self.one_recv, self.two_send, self.two_recv,
            self.core_send, self.core_recv,
        ) = sems
        self.first, self.second = pl.ds(0, rows // 2), pl.ds(rows // 2, rows // 2)
        self.order = here.near_first if line else [0]
        self.steps = len(self.order)

    def held(self, step):
        here = self.here
        return self.own if step == 0 else self.block(here.row, self.order[step], here.core)

    def up(self, step):
        here, place = self.here, self.order[step]
        target = self.block(here.row, place, here.core)
        recv = self.line_recv.at[place]
        return remote(self.held(step), target, self.up_send.at[place], recv, here.at_col(here.col + 1))

    def down(self, step):
        here, place = self.here, self.order[step]
        target = self.block(here.row, place, here.core)
        recv = self.line_recv.at[place]
        return remote(self.held(step), target, self.down_send.at[place], recv, here.at_col(here.col - 1))

    def to_across(self, step):
        here, place = self.here, self.order[step]
        target = self.block(here.row, place, here.core)
        sems = self.across_send.at[place], self.across_recv.at[place]
        return remote(self.held(step), target, *sems, here.at_row(here.across))

    def to_along(self, step):
        here, place = self.here, self.order[step]
        target = self.block(here.row, place, here.core)
        sems = self.along_send.at[place], self.along_recv.at[place]
        return remote(self.held(step), target, *sems, here.at_row(here.along))

    def corner_one(self, step):
        here, place = self.here, self.order[step]
        part = self.block(here.across, place, here.core).at[self.first]
        sems = self.one_send.at[place], self.one_recv.at[place]
        return remote(part, part, *sems, here.at_row(here.along))

    def corner_two(self, step):
        here, place = self.here, self.order[step]
        part = self.block(here.along, place, here.core).at[self.second]
        sems = self.two_send.at[place], self.two_recv.at[place]
        return remote(part, part, *sems, here.at_row(here.across))

    def to_core(self, which, step):
        here, place = self.here, self.order[step]
        target = self.block(here.rows[which], place, here.core)
        source = self.held(step) if which == 0 else target
        sems = self.core_send.at[which, place], self.core_recv.at[which, place]
        return remote(source, target, *sems, here.other_core())

    def line_step(self, step):
        here, place = self.here, self.order[step]
        if step > 0:
            arrived(self.held(step), self.line_recv.at[place])
        if self.line:

            @pl.when((place <= here.col) & (here.col < 3))
            def _():
                self.up(step).start()

            @pl.when((place >= here.col) & (here.col > 0))
            def _():
                self.down(step).start()

    def near_step(self, step):
        self.to_across(step).start()
        self.to_along(step).start()
        if self.core:
            self.to_core(0, step).start()

    def plane_step(self, step):
        here, place = self.here, self.order[step]
        arrived(self.block(here.across, place, here.core), self.across_recv.at[place])
        self.corner_one(step).start()
        if self.core:
            self.to_core(1, step).start()
        arrived(self.block(here.along, place, here.core), self.along_recv.at[place])
        self.corner_two(step).start()
        if self.core:
            self.to_core(2, step).start()

    def corner_step(self, step):
        here, place = self.here, self.order[step]
        target = self.block(here.opposite, place, here.core)
        arrived(target.at[self.first], self.one_recv.at[place])
        arrived(target.at[self.second], self.two_recv.at[place])
        if self.core:
            self.to_core(3, step).start()

    def step(self, index):
        if index < self.steps:
            self.line_step(index)
        if self.plane and 0 <= index - 1 < self.steps:
            self.plane_step(index - 1)
        if self.plane and index < self.steps:
            self.near_step(index)
        if self.plane and 0 <= index - 2 < self.steps:
            self.corner_step(index - 2)

    def core_arrived(self, which, step):
        here, place = self.here, self.order[step]
        target = self.block(here.rows[which], place, 1 - here.core)
        arrived(target, self.core_recv.at[which, place])

    def finish(self, arrivals=True):
        here = self.here
        for step in range(self.steps):
            place = self.order[step]
            if self.line:

                @pl.when((place <= here.col) & (here.col < 3))
                def _():
                    self.up(step).wait_send()

                @pl.when((place >= here.col) & (here.col > 0))
                def _():
                    self.down(step).wait_send()

            if self.plane:
                self.to_across(step).wait_send()
                self.to_along(step).wait_send()
                self.corner_one(step).wait_send()
                self.corner_two(step).wait_send()
                for which in range(4 if self.core else 0):
                    self.to_core(which, step).wait_send()
                    if arrivals:
                        self.core_arrived(which, step)


COLLECT_SEMS = (
    [pltpu.SemaphoreType.DMA((4,))] * 4
    + [pltpu.SemaphoreType.DMA((2, 4))] * 4
    + [pltpu.SemaphoreType.DMA((2, 4))] * 2
    + [pltpu.SemaphoreType.DMA((2, 5))]
)


def collect_buffers(rows, width):
    return [
        pltpu.VMEM((4, 4, rows, width), BF16),
        pltpu.VMEM((4, rows // 2, width), BF16),
        pltpu.VMEM((4, rows // 2, width), BF16),
        pltpu.VMEM((4, rows, width), BF16),
        pltpu.VMEM((4, rows, width), BF16),
        pltpu.VMEM((5, rows, width), BF16),
    ]


class Collect:
    def __init__(self, here, buffers, sems):
        self.here = here
        self.mine, self.one, self.two, self.from_across, self.from_along, self.line = buffers
        (
            self.one_send, self.one_recv, self.two_send, self.two_recv,
            self.across_send, self.across_recv, self.along_send, self.along_recv,
            self.up_send, self.down_send, self.line_recv,
        ) = sems
        half = self.mine.shape[2] // 2
        self.halves = (pl.ds(0, half), pl.ds(half, half))

    def give_one(self, place):
        here = self.here
        return remote(
            self.mine.at[3, place, self.halves[0]], self.one.at[place],
            self.one_send.at[place], self.one_recv.at[place], here.at_row(here.across),
        )

    def give_two(self, place):
        here = self.here
        return remote(
            self.mine.at[3, place, self.halves[1]], self.two.at[place],
            self.two_send.at[place], self.two_recv.at[place], here.at_row(here.along),
        )

    def give_across(self, place, half):
        here, part = self.here, self.halves[half]
        return remote(
            self.mine.at[1, place, part], self.from_across.at[place, part],
            self.across_send.at[half, place], self.across_recv.at[half, place], here.at_row(here.across),
        )

    def give_along(self, place, half):
        here, part = self.here, self.halves[half]
        return remote(
            self.mine.at[2, place, part], self.from_along.at[place, part],
            self.along_send.at[half, place], self.along_recv.at[half, place], here.at_row(here.along),
        )

    def give_up(self, place, half):
        here, part = self.here, self.halves[half]
        sems = self.up_send.at[half, place], self.line_recv.at[half, place]
        return remote(
            self.mine.at[0, place, part], self.line.at[place, part], *sems, here.at_col(here.col + 1)
        )

    def give_down(self, place, slot, half):
        here, part = self.here, self.halves[half]
        sems = self.down_send.at[half, place], self.line_recv.at[half, slot]
        return remote(
            self.mine.at[0, place, part], self.line.at[slot, part], *sems, here.at_col(here.col - 1)
        )

    def add_line(self, place, slot, half):
        part = self.halves[half]
        arrived(self.line.at[slot, part], self.line_recv.at[half, slot])
        add_into(self.mine.at[0, place, part], self.line.at[slot, part])

    def start_far(self, place):
        self.give_one(place).start()
        self.give_two(place).start()
        self.give_along(place, 1).start()

    def start_near(self, place):
        self.give_across(place, 0).start()

    def corner_step(self, place):
        self.give_two(place).wait_recv()
        add_into(self.mine.at[1, place, self.halves[1]], self.two.at[place])
        self.give_across(place, 1).start()
        self.give_one(place).wait_recv()
        add_into(self.mine.at[2, place, self.halves[0]], self.one.at[place])
        self.give_along(place, 0).start()

    def plane_step(self, place):
        for half in range(2):
            self.give_across(place, half).wait_recv()
            self.give_along(place, half).wait_recv()
        add_into(self.mine.at[0, place], self.from_across.at[place], self.from_along.at[place])

    def line_step(self, place):
        col = self.here.col
        for half in range(2):

            @pl.when(((place > col) & (col > 0)) | ((place < col) & (col < 3)))
            def _():
                self.add_line(place, place, half)

            @pl.when(place > col)
            def _():
                self.give_up(place, half).start()

            @pl.when(place < col - 1)
            def _():
                self.give_down(place, place, half).start()

            @pl.when(place == col - 1)
            def _():
                self.give_down(place, 4, half).start()

    def own_step(self):
        col = self.here.col
        for half in range(2):

            @pl.when(col > 0)
            def _():
                self.add_line(col, col, half)

            @pl.when(col < 3)
            def _():
                self.add_line(col, 4, half)

    def finish(self):
        col = self.here.col
        for place in range(4):
            self.give_one(place).wait_send()
            self.give_two(place).wait_send()
            for half in range(2):
                self.give_across(place, half).wait_send()
                self.give_along(place, half).wait_send()

                @pl.when(place > col)
                def _():
                    self.give_up(place, half).wait_send()

                @pl.when(place < col)
                def _():
                    self.give_down(place, place, half).wait_send()


def doc_start(places, cuts):
    return jnp.where(places >= cuts[1], cuts[1], jnp.where(places >= cuts[0], cuts[0], 0))


def key_blocks(cuts, first_query, rows, scores_of, block_fn):
    def scan(index, carry):
        start = pl.multiple_of(index * rows, rows)
        free = (start >= doc_start(first_query + rows - 1, cuts)) & (start + rows <= first_query + 1)

        @pl.when(free)
        def _():
            block_fn(start, scores_of(start))

        @pl.when(jnp.logical_not(free))
        def _():
            key_place = start + lax.broadcasted_iota(jnp.int32, (rows, rows), 0)
            place = first_query + lax.broadcasted_iota(jnp.int32, (1, rows), 1)
            allowed = (key_place <= place) & (key_place >= doc_start(place, cuts))
            block_fn(start, jnp.where(allowed, scores_of(start), MASKED))

        return carry

    lax.fori_loop(doc_start(first_query, cuts) // rows, first_query // rows + 1, scan, 0)


def attend_kernel(scale, group_tok, cuts, query, keys, values_t, mixed, total, top, summed, acc):
    rows = query.shape[0]
    side = lax.axis_index("exp") % 2
    first_query = side * group_tok + pl.program_id(0) * rows
    top[...] = jnp.full_like(top, MASKED)
    summed[...] = jnp.zeros_like(summed)
    acc[...] = jnp.zeros_like(acc)
    cut = (cuts[0, 0], cuts[0, 1])

    def scores_of(start):
        return contract_cols(keys[pl.ds(start, rows)], query[...]) * scale

    def block_fn(start, scores):
        old = top[...]
        new = jnp.maximum(old, jnp.max(scores, axis=0, keepdims=True))
        weights = jnp.exp(scores - new)
        decay = jnp.exp(old - new)
        top[...] = new
        summed[...] = summed[...] * decay + jnp.sum(weights, axis=0, keepdims=True)
        acc[...] = acc[...] * decay + matmul(values_t[:, pl.ds(start, rows)], weights.astype(BF16))

    key_blocks(cut, first_query, rows, scores_of, block_fn)
    mixed[...] = (acc[...] / summed[...]).T
    total[...] = top[...] + jnp.log(summed[...])


def attend(query, keys, values, cuts, scale, rows=512):
    group_tok, head_size = query.shape
    whole = lambda shape: pl.BlockSpec(shape, lambda i: (0, 0))
    return pl.pallas_call(
        functools.partial(attend_kernel, scale, group_tok),
        grid=(group_tok // rows,),
        in_specs=[
            pl.BlockSpec(memory_space=pltpu.SMEM),
            pl.BlockSpec((rows, head_size), lambda i: (i, 0)),
            whole(keys.shape),
            whole(values.shape[::-1]),
        ],
        out_specs=[
            pl.BlockSpec((rows, head_size), lambda i: (i, 0)),
            pl.BlockSpec((1, rows), lambda i: (0, i)),
        ],
        out_shape=[
            jax.ShapeDtypeStruct((group_tok, head_size), F32),
            jax.ShapeDtypeStruct((1, group_tok), F32),
        ],
        scratch_shapes=[
            pltpu.VMEM((1, rows), F32),
            pltpu.VMEM((1, rows), F32),
            pltpu.VMEM((head_size, rows), F32),
        ],
        compiler_params=pltpu.CompilerParams(vmem_limit_bytes=40 * 2**20),
        cost_estimate=pl.CostEstimate(
            flops=4 * 7 * 2**20 * head_size, bytes_accessed=2**23, transcendentals=7 * 2**20
        ),
    )(cuts[None], query, keys, values.T)


def attend_back_kernel(
    scale, group_tok, cuts, query, keys, keys_t, values, d_mixed, total, delta,
    d_query, d_keys, d_values, acc,
):
    rows = query.shape[0]
    side = lax.axis_index("exp") % 2
    first_query = side * group_tok + pl.program_id(0) * rows
    cut = (cuts[0, 0], cuts[0, 1])

    @pl.when(pl.program_id(0) == 0)
    def _():
        d_keys[...] = jnp.zeros_like(d_keys)
        d_values[...] = jnp.zeros_like(d_values)

    acc[...] = jnp.zeros_like(acc)

    def scores_of(start):
        return contract_cols(keys[pl.ds(start, rows)], query[...]) * scale

    def block_fn(start, scores):
        part = pl.ds(start, rows)
        weights = jnp.exp(scores - total[...])
        d_weights = contract_cols(values[part], d_mixed[...])
        d_scores = (weights * (d_weights - delta[...])).astype(BF16)
        d_values[part] += matmul(weights.astype(BF16), d_mixed[...])
        d_keys[part] += matmul(d_scores, query[...]) * scale
        acc[...] += matmul(keys_t[:, part], d_scores)

    key_blocks(cut, first_query, rows, scores_of, block_fn)
    d_query[...] = (acc[...] * scale).T


def attend_back(query, keys, values, d_mixed, mixed, total, cuts, scale, rows=512):
    group_tok, head_size = query.shape
    delta = jnp.sum(d_mixed.astype(F32) * mixed, axis=1)[None]
    whole = lambda shape: pl.BlockSpec(shape, lambda i: (0, 0))
    block = pl.BlockSpec((rows, head_size), lambda i: (i, 0))
    line = pl.BlockSpec((1, rows), lambda i: (0, i))
    return pl.pallas_call(
        functools.partial(attend_back_kernel, scale, group_tok),
        grid=(group_tok // rows,),
        in_specs=[
            pl.BlockSpec(memory_space=pltpu.SMEM),
            block,
            whole(keys.shape),
            whole(keys.shape[::-1]),
            whole(keys.shape),
            block,
            line,
            line,
        ],
        out_specs=[block, whole(keys.shape), whole(keys.shape)],
        out_shape=[
            jax.ShapeDtypeStruct((group_tok, head_size), F32),
            jax.ShapeDtypeStruct(keys.shape, F32),
            jax.ShapeDtypeStruct(keys.shape, F32),
        ],
        scratch_shapes=[pltpu.VMEM((head_size, rows), F32)],
        compiler_params=pltpu.CompilerParams(vmem_limit_bytes=48 * 2**20),
        cost_estimate=pl.CostEstimate(
            flops=10 * 7 * 2**20 * head_size, bytes_accessed=2**23, transcendentals=7 * 2**20
        ),
    )(cuts[None], query, keys, keys.T, values, d_mixed, total, delta)


def transposed_product(left, right):
    return jnp.dot(left.T, right, preferred_element_type=F32)


def column_of(line):
    return jnp.broadcast_to(line, (128, 128)).T[:, :1]


def line_of(column):
    return jnp.broadcast_to(column, (128, 128)).T[:1]


def expert_kernel(
    normed, grads_all, mask, gate_half, up_half, down_half,
    gate_other, up_other, down_other, router,
    rows_all, out_parts, total, inner_in, grad_gate, grad_up, grad_down,
    their_gates, their_down,
    gate_w, up_w, down_w, masks, x_buf, d_buf, gates_t, weighteds_t, d_gates, d_ups, weighteds, out_buf,
    inner, sum_buf, sum_down, *rest,
):
    here = Here()
    row, col, core = here.row, here.col, here.core
    rows, width = normed.shape
    half = gate_half.shape[1]
    expert = row * 4 + col
    count = len(SPREAD_SEMS)
    collect = Collect(here, rest[:6], rest[6 : 6 + len(COLLECT_SEMS)])
    rest = rest[6 + len(COLLECT_SEMS) :]
    (
        weight_sem, load_sem, store_sem, tile_sem, give_send, give_recv, their_sem, sum_sem,
        inner_send, inner_recv,
    ) = rest[:10]
    sems = rest[10:]

    def x_block(of_row, place, unused_core):
        return rows_all.at[pl.ds(pl.multiple_of((of_row * 4 + place) * rows, rows), rows)]

    def d_block(of_row, place, unused_core):
        return grads_all.at[pl.ds(pl.multiple_of((of_row * 4 + place) * rows, rows), rows)]

    def m_block(of_row, place, unused_core):
        return masks.at[of_row, place]

    spread_x = Spread(here, normed, x_block, rows, sems[:count], core=False)
    spread_m = Spread(here, mask, m_block, mask.shape[0], sems[count:], core=False)
    order = here.near_first

    own_half = pl.ds(pl.multiple_of(core * half, half), half)
    other_half = pl.ds(pl.multiple_of((1 - core) * half, half), half)
    keeps = [
        pltpu.make_async_copy(source, target, weight_sem.at[index])
        for index, (source, target) in enumerate(
            (
                (normed, x_block(row, col, 0)),
                (mask, m_block(row, col, 0)),
                (gate_half, gate_w.at[:, own_half]),
                (up_half, up_w.at[:, own_half]),
                (down_half, down_w.at[own_half]),
                (gate_other, gate_w.at[:, other_half]),
                (up_other, up_w.at[:, other_half]),
                (down_other, down_w.at[other_half]),
            )
        )
    ]
    greet(here.group_peers() + [here.other_core()])
    spread_x.step(0)
    spread_m.step(0)
    for keep in keeps:
        keep.start()

    turns = (3, 2, 1, 0)

    def loads(step):
        return [
            pltpu.make_async_copy(
                source(here.rows[which], order[step], 0),
                target.at[pl.ds(position * rows, rows)],
                load_sem.at[position, array],
            )
            for position, which in enumerate(turns)
            for array, (source, target) in enumerate(((x_block, x_buf), (d_block, d_buf)))
        ]

    def stores(step):
        return [
            pltpu.make_async_copy(
                out_buf.at[pl.ds(position * rows, rows)],
                out_parts.at[which, order[step]],
                store_sem.at[position],
            )
            for position, which in enumerate(turns)
        ]

    tile = 256

    def first_products(step):
        place = order[step]
        x = x_buf[...]
        lane = lax.broadcasted_iota(jnp.int32, (x.shape[0], router.shape[0]), 1)
        logits = contract_cols(x, router[...])
        raised = jnp.exp(logits - jnp.max(logits, axis=1, keepdims=True))
        picked = jnp.sum(jnp.where(lane == expert, raised, 0.0), axis=1, keepdims=True)
        routed = jnp.concatenate(
            [column_of(masks[here.rows[which], place, pl.ds(expert, 1)]) for which in turns]
        )
        gate = picked / jnp.sum(raised, axis=1, keepdims=True) * routed
        columns = [
            pl.ds(pl.multiple_of((here.rows[which] * 4 + place) * rows, rows), rows) for which in turns
        ]

        def tile_step(index, inner_sum):
            at = pl.ds(pl.multiple_of(index * tile, tile), tile)
            pre_gate = matmul(x_buf[...], gate_w[:, at])
            pre_up = matmul(x_buf[...], up_w[:, at])
            back = contract_cols(d_buf[...], down_w[at])
            sigmoid_gate = 0.5 * jnp.tanh(0.5 * pre_gate) + 0.5
            silu_gate = pre_gate * sigmoid_gate
            hidden = (silu_gate * pre_up).astype(BF16).astype(F32)
            d_hid = back * gate
            d_gate = (d_hid * pre_up * (sigmoid_gate + silu_gate * (1.0 - sigmoid_gate))).astype(BF16)
            d_up = (d_hid * silu_gate).astype(BF16)
            weight = (hidden * gate).astype(BF16)
            d_gates[:, at] = d_gate
            d_ups[:, at] = d_up
            weighteds[:, at] = weight
            side = index // (half // tile)
            first = pl.multiple_of(index % (half // tile) * tile, tile)
            for values, target in (
                (d_gate, gates_t.at[side, pl.ds(first, tile)]),
                (d_up, gates_t.at[side, pl.ds(first + half, tile)]),
                (weight, weighteds_t.at[at]),
            ):
                turned = values.T
                for position, column in enumerate(columns):
                    target[:, column] = turned[:, position * rows : (position + 1) * rows]
            return inner_sum + jnp.sum(hidden * back, axis=1, keepdims=True)

        start = jnp.zeros((x.shape[0], 1), F32)
        inner_sum = lax.fori_loop(0, gate_w.shape[1] // tile, tile_step, start, unroll=2)
        for position, which in enumerate(turns):
            part = slice(position * rows, (position + 1) * rows)
            inner[here.rows[which], place, 0:1] = line_of(inner_sum[part])

    def second_products(step):
        place = order[step]
        wide = 512
        for index in range(width // wide):
            at = pl.ds(index * wide, wide)
            out_buf[:, at] = matmul(weighteds[...], down_w[:, at]).astype(BF16)
            d_x = contract_cols(d_gates[...], gate_w[at]) + contract_cols(d_ups[...], up_w[at])
            d_x = d_x.astype(BF16)
            for position, which in enumerate(turns):
                collect.mine[which, place, :, at] = d_x[position * rows : (position + 1) * rows]

    for index in (1, 2):
        spread_x.step(index)
        spread_m.step(index)
    for keep in keeps:
        keep.wait()
    for copy in loads(0):
        copy.start()
    turn_order = (0, 1, 3, 2)
    ends = (col == 0) | (col == 3)

    def from_ends(step):
        @pl.when(ends)
        def _():
            collect.line_step(order[step])

    def from_inside(step):
        @pl.when(jnp.logical_not(ends))
        def _():
            collect.line_step(order[step])

    def start(step):
        collect.start_far(order[step])
        collect.start_near(order[step])

    for turn, step in enumerate(turn_order):
        for copy in loads(step):
            copy.wait()
        first_products(step)
        if turn < 2:
            spread_x.step(turn + 3)
            spread_m.step(turn + 3)
        if turn in (0, 2):
            for copy in loads(turn_order[turn + 1]):
                copy.start()
        if turn > 0:
            for copy in stores(turn_order[turn - 1]):
                copy.wait()
        if turn == 2:
            collect.corner_step(order[1])
        if turn == 3:
            collect.corner_step(order[3])
        second_products(step)
        for copy in stores(step):
            copy.start()
        if turn == 1:
            spread_x.step(5)
            spread_m.step(5)
            for copy in loads(turn_order[2]):
                copy.start()
            start(1)
            start(0)
        if turn == 2:
            start(3)
            collect.corner_step(order[0])
            collect.plane_step(order[1])
            from_ends(1)
        if turn == 3:
            start(2)
            collect.plane_step(order[3])
            from_ends(3)
            collect.plane_step(order[0])

    tiles = width // tile

    def tile_at(index):
        return pl.ds(pl.multiple_of(index * tile, tile), tile)

    def acts_of(kind, side):
        if kind == 0:
            return gates_t[side]
        return weighteds_t[pl.ds(pl.multiple_of(side * half, half), half)]

    counts = (2 * half, half)

    def slot_at(kind, slot):
        return pl.ds(pl.multiple_of((2 * kind + slot) * tile, tile), tile)

    def tile_buf(kind, slot):
        return gate_w.at[:, slot_at(kind, slot)]

    def give_buf(kind, slot):
        return up_w.at[pl.ds(0, counts[kind]), slot_at(kind, slot)]

    def their_buf(kind, slot):
        return up_w.at[pl.ds(width // 2, counts[kind]), slot_at(kind, slot)]

    theirs = (their_gates, their_down)

    def tile_load(kind, index, slot):
        source = (rows_all, grads_all)[kind]
        return pltpu.make_async_copy(
            source.at[:, tile_at(index)], tile_buf(kind, slot), tile_sem.at[slot]
        )

    def give(kind, index, slot):
        sems = give_send.at[slot, kind], give_recv.at[kind, index]
        return remote(give_buf(kind, slot), theirs[kind].at[:, tile_at(index)], *sems, here.other_core())

    def their_load(kind, index, slot):
        return pltpu.make_async_copy(
            theirs[kind].at[:, tile_at(index)],
            their_buf(kind, slot),
            their_sem.at[slot, kind],
        )

    def sum_stores(kind, index, slot):
        if kind == 1:
            target = grad_down.at[:, tile_at(index)]
            return [pltpu.make_async_copy(sum_down, target, sum_sem.at[0, 2])]
        return [
            pltpu.make_async_copy(
                sum_buf.at[slot, part], target.at[tile_at(index)], sum_sem.at[slot, part]
            )
            for part, target in enumerate((grad_gate, grad_up))
        ]

    def give_gradients(kind, start, stop):
        tile_load(kind, start, 0).start()

        @pl.loop(start, stop)
        def _(index):
            slot = index % 2

            @pl.when(index + 1 < stop)
            def _():
                tile_load(kind, index + 1, 1 - slot).start()

            tile_load(kind, index, slot).wait()
            product = matmul(acts_of(kind, 1 - core), tile_buf(kind, slot)[...])

            @pl.when(index >= 2)
            def _():
                give(kind, index - 2, slot).wait_send()

            give_buf(kind, slot)[...] = product.astype(BF16)
            give(kind, index, slot).start()

    def keep_gradients(kind, start, stop):
        tile_load(kind, start, 0).start()
        give(kind, start, 0).wait_recv()
        their_load(kind, start, 0).start()

        @pl.loop(start, stop)
        def _(index):
            slot = index % 2

            @pl.when(index + 1 < stop)
            def _():
                tile_load(kind, index + 1, 1 - slot).start()
                give(kind, index + 1, 1 - slot).wait_recv()
                their_load(kind, index + 1, 1 - slot).start()

            tile_load(kind, index, slot).wait()
            product = matmul(acts_of(kind, core), tile_buf(kind, slot)[...])
            their_load(kind, index, slot).wait()
            product = product + their_buf(kind, slot)[...].astype(F32)
            held = 2 - kind

            @pl.when(index >= held)
            def _():
                for copy in sum_stores(kind, index - held, slot):
                    copy.wait()

            if kind == 1:
                sum_down[...] = product.astype(BF16)
            else:
                sum_buf[slot, 0] = product[:half].T.astype(BF16)
                sum_buf[slot, 1] = product[half:].T.astype(BF16)
            for copy in sum_stores(kind, index, slot):
                copy.start()

    def give_inner(index):
        step = index + 1
        to_row, to_col = (row + step // 4) % 4, (col + step) % 4
        return remote(
            inner.at[to_row, to_col],
            inner_in.at[row, col],
            inner_send.at[index],
            inner_recv.at[row, col],
            (to_row, to_col, core),
        )

    for index in range(15):
        give_inner(index).start()
    inner_in[row, col] = inner[row, col]
    give_gradients(0, 0, tiles // 2)
    from_inside(3)
    collect.corner_step(order[2])
    give_gradients(0, tiles // 2, tiles)
    collect.plane_step(order[2])
    from_ends(2)
    give_gradients(1, 0, tiles)
    from_inside(2)
    keep_gradients(0, 0, tiles // 2)
    from_inside(1)
    keep_gradients(0, tiles // 2, tiles)
    keep_gradients(1, 0, tiles)
    collect.own_step()
    total[...] = collect.mine[0, col]

    for index in range(15):
        give_inner(index).wait_send()
        step = index + 1
        from_row, from_col = (row + 4 - step // 4) % 4, (col + 4 - step % 4) % 4
        arrived(inner_in.at[from_row, from_col], inner_recv.at[from_row, from_col])
    for copy in stores(turn_order[3]):
        copy.wait()
    for kind in range(2):
        for slot in range(2):
            give(kind, tiles - 2 + slot, slot).wait_send()
        for slot in range(2 - kind):
            for copy in sum_stores(kind, tiles - 2 + kind + slot, slot):
                copy.wait()
    spread_x.finish()
    spread_m.finish()
    collect.finish()


def expert_stage(normed, grads_all, mask, halves, others, router, collective_id):
    rows, width = normed.shape
    half = halves[0].shape[1]
    tokens = 16 * rows
    tile = 256
    vmem = pl.BlockSpec(memory_space=pltpu.VMEM)
    hbm = pl.BlockSpec(memory_space=pl.ANY)
    dma = pltpu.SemaphoreType.DMA
    blocks = jax.ShapeDtypeStruct((4, 4, rows, width), BF16)
    got = pl.pallas_call(
        expert_kernel,
        in_specs=[hbm] * 9 + [vmem],
        out_specs=[hbm] * 2 + [vmem] * 2 + [hbm] * 5,
        out_shape=[
            jax.ShapeDtypeStruct((tokens, width), BF16),
            blocks,
            jax.ShapeDtypeStruct((rows, width), BF16),
            jax.ShapeDtypeStruct((4, 4, 8, rows), F32),
            jax.ShapeDtypeStruct((width, half), BF16),
            jax.ShapeDtypeStruct((width, half), BF16),
            jax.ShapeDtypeStruct((half, width), BF16),
            jax.ShapeDtypeStruct((2 * half, width), BF16),
            jax.ShapeDtypeStruct((half, width), BF16),
        ],
        scratch_shapes=[
            pltpu.VMEM((width, 2 * half), BF16),
            pltpu.VMEM((width, 2 * half), BF16),
            pltpu.VMEM((2 * half, width), BF16),
            pltpu.VMEM((4, 4) + mask.shape, F32),
            pltpu.VMEM((4 * rows, width), BF16),
            pltpu.VMEM((4 * rows, width), BF16),
            pltpu.VMEM((2, 2 * half, tokens), BF16),
            pltpu.VMEM((2 * half, tokens), BF16),
            pltpu.VMEM((4 * rows, 2 * half), BF16),
            pltpu.VMEM((4 * rows, 2 * half), BF16),
            pltpu.VMEM((4 * rows, 2 * half), BF16),
            pltpu.VMEM((4 * rows, width), BF16),
            pltpu.VMEM((4, 4, 8, rows), F32),
            pltpu.VMEM((2, 2, tile, half), BF16),
            pltpu.VMEM((half, tile), BF16),
        ]
        + collect_buffers(rows, width)
        + COLLECT_SEMS
        + [
            dma((8,)), dma((4, 2)), dma((4,)),
            dma((2,)), dma((2, 2)), dma((2, width // tile)), dma((2, 2)), dma((2, 3)),
            dma((15,)), dma((4, 4)),
        ]
        + SPREAD_SEMS * 2,
        compiler_params=pltpu.CompilerParams(
            collective_id=collective_id, has_side_effects=True, vmem_limit_bytes=61 * 2**20
        ),
        cost_estimate=pl.CostEstimate(
            flops=18 * 2 * tokens * width * half,
            bytes_accessed=2**26,
            transcendentals=2 * tokens * half,
        ),
    )(normed, grads_all, mask, *halves, *others, router.T)
    return got[1], got[2], got[3], got[4:7]


def project_kernel(
    hidden, all_gains, weights, cosine, sine,
    normed_out, weights_out, qkv_out, totals, query, keys, values,
    normed, all_weights, qkv, out_sem,
    heads, stat, scale_q, scale_k, kept_sem, kept_kv_sem,
    stat_send, stat_recv, head_send, head_recv, pair_send, pair_recv, *sems,
):
    here = Here()
    row, col, core = here.row, here.col, here.core
    count = len(SPREAD_SEMS)
    rows, width = hidden.shape
    depth = weights.shape[0]
    part = depth // 2

    def weight_block(of_row, unused_place, of_core):
        return all_weights.at[pl.ds(pl.multiple_of(of_row * depth + of_core * part, part), part)]

    def normed_block(unused_row, place, unused_core):
        return normed.at[pl.ds(pl.multiple_of(place * rows, rows), rows)]

    own_weight = weights.at[pl.ds(pl.multiple_of(core * part, part), part)]
    spread_w = Spread(here, own_weight, weight_block, part, sems[:count], line=False)
    spread_n = Spread(
        here, normed_block(row, col, core), normed_block, rows, sems[count:], plane=False
    )
    greet(here.plane_peers() + here.line_peers() + [here.other_core()])
    spread_w.step(0)
    keep = pltpu.make_async_copy(own_weight, weight_block(row, 0, core), kept_sem)
    keep.start()

    values_in = hidden[...].astype(F32)
    scale_one = lax.rsqrt(jnp.mean(values_in * values_in, axis=1, keepdims=True) + EPSILON)
    own_rows = pl.ds(pl.multiple_of(col * rows, rows), rows)
    normed[own_rows] = (values_in * scale_one * all_gains[0:1]).astype(BF16)
    spread_n.step(0)
    spread_w.step(1)
    spread_n.step(1)
    spread_w.step(2)
    spread_n.step(2)
    spread_n.step(3)
    keep.wait()
    for which in range(4):
        spread_w.core_arrived(which, 0)
    puts = [
        pltpu.make_async_copy(source, target, out_sem.at[index])
        for index, (source, target) in enumerate(
            ((normed, normed_out), (all_weights, weights_out), (qkv, qkv_out))
        )
    ]
    puts[0].start()
    puts[1].start()
    columns = 256

    @pl.loop(0, qkv.shape[1] // columns)
    def _(index):
        at = pl.ds(pl.multiple_of(index * columns, columns), columns)
        qkv[:, at] = matmul(normed[...], all_weights[:, at])

    puts[2].start()

    plane = qkv.shape[1] // (3 * HD)
    for kind in range(2):
        square = jnp.zeros((qkv.shape[0], HD), F32)
        for head in range(plane):
            start = (head * 3 + kind) * HD
            raw = qkv[:, start : start + HD]
            square = square + raw * raw
        stat[col, kind : kind + 1] = jnp.sum(square.T, axis=0, keepdims=True)

    def give_stat(step):
        peer = here.line_peers()[step]
        return remote(stat.at[col], stat.at[col], stat_send.at[step], stat_recv.at[col], peer)

    for step in range(3):
        give_stat(step).start()
    for step in range(3):
        place = (col + step + 1) % 4
        arrived(stat.at[place], stat_recv.at[place])
    total = stat[0] + stat[1] + stat[2] + stat[3]
    totals[...] = total
    for kind, target in enumerate((scale_q, scale_k)):
        line = lax.rsqrt(total[kind : kind + 1] / width + EPSILON)
        target[...] = jnp.broadcast_to(line, (HD, line.shape[1])).T

    chunk = 64

    @pl.loop(0, qkv.shape[0] // chunk)
    def _(index):
        at = pl.ds(pl.multiple_of(index * chunk, chunk), chunk)
        for head in range(plane):
            place = pl.ds(pl.multiple_of((col * plane + head) * HD, HD), HD)
            for kind, scales in enumerate((scale_q, scale_k)):
                raw = qkv[at, pl.ds((head * 3 + kind) * HD, HD)]
                unit = raw * scales[at] * all_gains[kind + 1 : kind + 2, place]
                turned = pltpu.roll(unit, HD // 2, 1)
                heads[head, kind, at] = (unit * cosine[at] + turned * sine[at]).astype(BF16)
            heads[head, 2, at] = qkv[at, pl.ds((head * 3 + 2) * HD, HD)].astype(BF16)

    targets = (query.at[row], keys.at[1, row], values.at[1, row])

    def give_head(step, kind):
        dest = here.rows[step + 1]
        sems = head_send.at[step, kind], head_recv.at[kind, row]
        return remote(heads.at[dest, kind], targets[kind], *sems, here.at_row(dest))

    for kind in (1, 2, 0):
        for step in range(3):
            give_head(step, kind).start()

    def give_pair(source, kind):
        array = (keys, values)[kind]
        sems = pair_send.at[kind, source], pair_recv.at[kind, source]
        return remote(array.at[1, source], array.at[0, source], *sems, here.other_core())

    def keep_pair(source, kind):
        array = (keys, values)[kind]
        return pltpu.make_async_copy(
            array.at[1, source], array.at[0, source], kept_kv_sem.at[kind, source]
        )

    def pair_from(source):
        @pl.when(core == 0)
        def _():
            for kind in range(2):
                give_pair(source, kind).start()
                keep_pair(source, kind).start()

    for kind, array in ((1, keys), (2, values)):
        array[1, row] = heads[row, kind]
    query[row] = heads[row, 0]
    pair_from(row)
    for source in here.rows[1:]:
        arrived(keys.at[1, source], head_recv.at[1, source])
        arrived(values.at[1, source], head_recv.at[2, source])
        pair_from(source)
    for source in here.rows[1:]:
        arrived(query.at[source], head_recv.at[0, source])

    @pl.when(core == 0)
    def _():
        for source in range(4):
            for kind in range(2):
                give_pair(source, kind).wait_send()
                keep_pair(source, kind).wait()

    @pl.when(core == 1)
    def _():
        for source in range(4):
            for kind in range(2):
                give_pair(source, kind).wait_recv()

    for step in range(3):
        give_stat(step).wait_send()
        for kind in range(3):
            give_head(step, kind).wait_send()
    for put in puts:
        put.wait()
    spread_w.finish(arrivals=False)
    spread_n.finish()


def project(hidden, gains, weights, cosine, sine, collective_id):
    rows, width = hidden.shape
    depth, columns = weights.shape
    row_tok = 4 * rows
    plane = columns // (3 * HD)
    vmem = pl.BlockSpec(memory_space=pltpu.VMEM)
    hbm = pl.BlockSpec(memory_space=pl.ANY)
    return pl.pallas_call(
        project_kernel,
        in_specs=[vmem, vmem, hbm, vmem, vmem],
        out_specs=[hbm] * 3 + [vmem] * 4,
        out_shape=[
            jax.ShapeDtypeStruct((row_tok, width), BF16),
            jax.ShapeDtypeStruct((4 * depth, columns), BF16),
            jax.ShapeDtypeStruct((row_tok, columns), F32),
            jax.ShapeDtypeStruct((8, row_tok), F32),
            jax.ShapeDtypeStruct((4, row_tok, HD), BF16),
            jax.ShapeDtypeStruct((2, 4, row_tok, HD), BF16),
            jax.ShapeDtypeStruct((2, 4, row_tok, HD), BF16),
        ],
        scratch_shapes=[
            pltpu.VMEM((row_tok, width), BF16),
            pltpu.VMEM((4 * depth, columns), BF16),
            pltpu.VMEM((row_tok, columns), F32),
            pltpu.SemaphoreType.DMA((3,)),
            pltpu.VMEM((plane, 3, row_tok, HD), BF16),
            pltpu.VMEM((4, 8, row_tok), F32),
            pltpu.VMEM((row_tok, HD), F32),
            pltpu.VMEM((row_tok, HD), F32),
            pltpu.SemaphoreType.DMA,
            pltpu.SemaphoreType.DMA((2, 4)),
            pltpu.SemaphoreType.DMA((3,)),
            pltpu.SemaphoreType.DMA((4,)),
            pltpu.SemaphoreType.DMA((3, 3)),
            pltpu.SemaphoreType.DMA((3, 4)),
            pltpu.SemaphoreType.DMA((2, 4)),
            pltpu.SemaphoreType.DMA((2, 4)),
        ]
        + SPREAD_SEMS * 2,
        compiler_params=pltpu.CompilerParams(
            collective_id=collective_id, has_side_effects=True, vmem_limit_bytes=56 * 2**20
        ),
    )(hidden, gains, weights, cosine, sine)


def attention_kernel(
    scale, cuts, query, keys, values, out_weights, hidden, all_gains,
    mixed, total, whole_out, mixed_rows, middle, normed,
    all_out, put_sem, values_t, top, summed, acc, mixed_low, mixed_tok, kept_sem,
    row_send, row_recv, token_send, token_recv, *sems,
):
    here = Here()
    row, col, core = here.row, here.col, here.core
    rows = hidden.shape[0]
    row_tok = 4 * rows
    group_tok = 4 * row_tok
    side = out_weights.shape[0]

    def out_block(of_row, place, of_core):
        start = pl.multiple_of(place * side + of_core * (side // 2), side // 2)
        return all_out.at[pl.ds(start, side // 2), pl.ds(pl.multiple_of(of_row * side, side), side)]

    own_out = out_weights.at[pl.ds(pl.multiple_of(core * (side // 2), side // 2), side // 2)]
    spread = Spread(here, own_out, out_block, side // 2, sems)
    keep = pltpu.make_async_copy(own_out, out_block(row, col, core), kept_sem)
    keep.start()
    values_t[...] = values[...].T
    greet(here.plane_peers() + here.line_peers() + [here.other_core()])
    spread.step(0)
    cut = (cuts[0, 0], cuts[0, 1])
    last_query = 2 * group_tok - row_tok

    def queries(index):
        at = pl.ds(index * row_tok, row_tok)
        first_query = core * group_tok + index * row_tok
        top[...] = jnp.full_like(top, MASKED)
        summed[...] = jnp.zeros_like(summed)
        acc[...] = jnp.zeros_like(acc)

        def block_fn(part, scores):
            old = top[...]
            new = jnp.maximum(old, jnp.max(scores, axis=0, keepdims=True))
            weight = jnp.exp(scores - new)
            decay = jnp.exp(old - new)
            top[...] = new
            summed[...] = summed[...] * decay + jnp.sum(weight, axis=0, keepdims=True)
            acc[...] = acc[...] * decay + matmul(values_t[:, part], weight.astype(BF16))

        def scan(block, carry):
            first_key = block * row_tok
            part = pl.ds(pl.multiple_of(first_key, row_tok), row_tok)
            masked = (block == 0) | (first_key == first_query) | (first_query == last_query)

            @pl.when(jnp.logical_not(masked))
            def _():
                block_fn(part, contract_cols(keys[part], query[at]) * scale)

            @pl.when(masked)
            def _():
                key_place = first_key + lax.broadcasted_iota(jnp.int32, (row_tok, row_tok), 0)
                place = first_query + lax.broadcasted_iota(jnp.int32, (1, row_tok), 1)
                allowed = (key_place <= place) & (key_place >= doc_start(place, cut))
                scores = contract_cols(keys[part], query[at]) * scale
                block_fn(part, jnp.where(allowed, scores, MASKED))

            return carry

        lax.fori_loop(0, core * 4 + index + 1, scan, 0)
        got = (acc[...] / summed[...]).T
        mixed[at] = got
        mixed_low[index] = got.astype(BF16)
        total[:, at] = top[...] + jnp.log(summed[...])

        @pl.when(row != index)
        def _():
            give_row(index).start()

        @pl.when(row == index)
        def _():
            mixed_rows[row] = mixed_low[index]

    def give_row(index):
        sems_of = row_send.at[index], row_recv.at[row]
        return remote(mixed_low.at[index], mixed_rows.at[row], *sems_of, here.at_row(index))

    def give_token(step):
        place = (col + step) % 4
        part = pl.ds(pl.multiple_of(place * rows, rows), rows)
        sems_of = token_send.at[step], token_recv.at[col]
        return remote(mixed_rows.at[:, part], mixed_tok.at[col], *sems_of, here.at_col(place))

    for index in range(4):
        queries(index)
        spread.step(index + 1)
    for source in here.rows[1:]:
        arrived(mixed_rows.at[source], row_recv.at[source])
    for step in range(1, 4):
        give_token(step).start()
    mixed_tok[col] = mixed_rows[:, pl.ds(pl.multiple_of(col * rows, rows), rows)]
    spread.step(5)
    keep.wait()
    spread.finish()
    put = pltpu.make_async_copy(all_out, whole_out, put_sem)
    put.start()
    for step in range(1, 4):
        place = (col + 4 - step) % 4
        arrived(mixed_tok.at[place], token_recv.at[place])
    own = jnp.concatenate([mixed_tok[place, head] for place in range(4) for head in range(4)], axis=1)
    tile = 512

    @pl.loop(0, all_out.shape[1] // tile)
    def _(index):
        at = pl.ds(pl.multiple_of(index * tile, tile), tile)
        middle[:, at] = hidden[:, at].astype(F32) + matmul(own, all_out[:, at])

    values_in = middle[...]
    root = lax.rsqrt(jnp.mean(values_in * values_in, axis=1, keepdims=True) + EPSILON)
    normed[...] = (values_in * root * all_gains[3:4]).astype(BF16)
    put.wait()
    for index in range(4):

        @pl.when(row != index)
        def _():
            give_row(index).wait_send()

    for step in range(1, 4):
        give_token(step).wait_send()


def attention_stage(query, keys, values, cuts, out_weights, hidden, gains, scale, collective_id):
    rows, width = hidden.shape
    row_tok, group_tok = 4 * rows, 16 * rows
    vmem, hbm = pl.BlockSpec(memory_space=pltpu.VMEM), pl.BlockSpec(memory_space=pl.ANY)
    dma = pltpu.SemaphoreType.DMA
    return pl.pallas_call(
        functools.partial(attention_kernel, scale),
        in_specs=[pl.BlockSpec(memory_space=pltpu.SMEM)] + [vmem] * 3 + [hbm] + [vmem] * 2,
        out_specs=[vmem] * 2 + [hbm] + [vmem] * 3,
        out_shape=[
            jax.ShapeDtypeStruct((group_tok, HD), F32),
            jax.ShapeDtypeStruct((1, group_tok), F32),
            jax.ShapeDtypeStruct((width, width), BF16),
            jax.ShapeDtypeStruct((4, row_tok, HD), BF16),
            jax.ShapeDtypeStruct((rows, width), F32),
            jax.ShapeDtypeStruct((rows, width), BF16),
        ],
        scratch_shapes=[
            pltpu.VMEM((width, width), BF16),
            dma,
            pltpu.VMEM((HD, 2 * group_tok), BF16),
            pltpu.VMEM((1, row_tok), F32),
            pltpu.VMEM((1, row_tok), F32),
            pltpu.VMEM((HD, row_tok), F32),
            pltpu.VMEM((4, row_tok, HD), BF16),
            pltpu.VMEM((4, 4, rows, HD), BF16),
            dma, dma((4,)), dma((4,)), dma((4,)), dma((4,)),
        ]
        + SPREAD_SEMS,
        compiler_params=pltpu.CompilerParams(
            collective_id=collective_id, has_side_effects=True, vmem_limit_bytes=40 * 2**20
        ),
    )(cuts, query, keys, values, out_weights, hidden, gains)


class PairSum:
    def __init__(self, here, values, out, held, got, send, recv):
        self.here, self.values, self.out, self.held, self.got = here, values, out, held, got
        self.send, self.recv = send, recv
        col, half = here.col, values.shape[1] // 2
        self.own = pl.ds(pl.multiple_of(here.core * half, half), half)
        self.others = pl.ds(pl.multiple_of((1 - here.core) * half, half), half)
        self.peers = [
            here.at_row(here.across),
            here.at_row(here.along),
            here.at_col(col + 1 - 2 * (col % 2)),
            here.at_col((col + 2) % 4),
        ]

    def copy(self, step):
        here, sems = self.here, (self.send.at[step], self.recv.at[step])
        if step == 0:
            return remote(self.values.at[:, self.others], self.got.at[0], *sems, here.other_core())
        if step == 5:
            return remote(self.held.at[4], self.out.at[:, self.own], *sems, here.other_core())
        return remote(self.held.at[step - 1], self.got.at[step], *sems, self.peers[step - 1])

    def begin(self):
        self.copy(0).start()

    def step(self, index):
        if index == 5:
            arrived(self.out.at[:, self.others], self.recv.at[5])
            return
        self.copy(index).wait_recv()
        before = self.values[:, self.own] if index == 0 else self.held[index - 1]
        self.held[index] = before + self.got[index]
        if index == 4:
            self.out[:, self.own] = self.held[4]
        self.copy(index + 1).start()

    def finish(self):
        for index in range(6):
            self.copy(index).wait_send()


def pair_sum_buffers(rows, width):
    return [
        pltpu.VMEM((5, rows, width // 2), F32),
        pltpu.VMEM((5, rows, width // 2), F32),
        pltpu.SemaphoreType.DMA((6,)),
        pltpu.SemaphoreType.DMA((6,)),
    ]


def back_kernel(
    scale, cuts, d_attn, query, keys, values, mixed, total, out_weights, out_parts, early,
    d_attn_row, d_heads, out_total, early_sum,
    weights, d_mixed_give, d_mixed_row, d_mixed, keys_t, d_keys, d_values, acc, pair_out, pair_in,
    head_give, sum_held, sum_got, sum_send, sum_recv, weight_sem, load_sem,
    near_send, near_recv, head_send, head_recv, back_send, back_recv,
    pair_send, pair_recv, *rest,
):
    here = Here()
    row, col, core = here.row, here.col, here.core
    rows = d_attn.shape[0]
    row_tok = 4 * rows
    group_tok = 4 * row_tok
    plane = 4 * HD
    order = here.near_first[::-1]
    collect = Collect(here, rest[:6], rest[6 : 6 + len(COLLECT_SEMS)])
    sems = rest[6 + len(COLLECT_SEMS) :]

    def row_block(unused_row, place, unused_core):
        return d_attn_row.at[pl.ds(pl.multiple_of(place * rows, rows), rows)]

    spread = Spread(here, row_block(row, col, core), row_block, rows, sems, plane=False)
    pair_sum = PairSum(here, early, early_sum, sum_held, sum_got, sum_send, sum_recv)

    def load(which, place):
        return pltpu.make_async_copy(
            out_parts.at[which, place], collect.mine.at[which, place], load_sem.at[which, place]
        )

    load_weights = pltpu.make_async_copy(out_weights, weights, weight_sem)
    load_weights.start()
    for place in order:
        for which in (3, 2, 1, 0):
            load(which, place).start()
    keys_t[...] = keys[...].T
    d_attn_row[pl.ds(pl.multiple_of(col * rows, rows), rows)] = d_attn[...]
    greet(here.plane_peers() + here.line_peers() + [here.other_core()])

    def give_near(step):
        place = (col + step) % 4
        sems_of = near_send.at[step], near_recv.at[col]
        return remote(d_mixed_give.at[place], d_mixed_row.at[col], *sems_of, here.at_col(place))

    def give_head(step):
        dest = here.rows[step]
        part = pl.ds(pl.multiple_of(dest * HD, HD), HD)
        sems_of = head_send.at[step], head_recv.at[row]
        return remote(d_mixed_row.at[:, :, part], d_mixed.at[row], *sems_of, here.at_row(dest))

    def start(index):
        for which in (3, 2, 1):
            load(which, order[index]).wait()
        collect.start_far(order[index])
        collect.start_near(order[index])

    ends = (col == 0) | (col == 3)

    def from_ends(index):
        @pl.when(ends)
        def _():
            collect.line_step(order[index])

    def from_inside(index):
        @pl.when(jnp.logical_not(ends))
        def _():
            collect.line_step(order[index])

    def plane_part(index):
        load(0, order[index]).wait()
        collect.plane_step(order[index])

    start(0)
    pair_sum.begin()
    load_weights.wait()
    for step in (1, 2, 3, 0):
        place = (col + step) % 4
        part = pl.ds(pl.multiple_of(place * plane, plane), plane)
        product = contract_cols(d_attn[...], weights[part]).astype(BF16)
        if step == 0:
            d_mixed_row[col] = product
        else:
            d_mixed_give[place] = product
            give_near(step).start()
    spread.step(0)
    pair_sum.step(0)
    d_keys[...] = jnp.zeros_like(d_keys)
    d_values[...] = jnp.zeros_like(d_values)
    for step in range(1, 4):
        place = (col + 4 - step) % 4
        arrived(d_mixed_row.at[place], near_recv.at[place])
    for step in range(1, 4):
        give_head(step).start()
    d_mixed[row] = d_mixed_row[:, :, pl.ds(pl.multiple_of(row * HD, HD), HD)]
    collect.corner_step(order[0])
    start(1)
    pair_sum.step(1)
    spread.step(1)
    for source in here.rows[1:]:
        arrived(d_mixed.at[source], head_recv.at[source])

    cut = (cuts[0, 0], cuts[0, 1])
    last_query = 2 * group_tok - row_tok

    def queries(index):
        at = pl.ds(index * row_tok, row_tok)
        first_query = core * group_tok + index * row_tok
        gradient = d_mixed[index].reshape(row_tok, HD)
        delta = jnp.sum((gradient.astype(F32) * mixed[at]).T, axis=0, keepdims=True)
        sums = total[:, at]
        acc[...] = jnp.zeros_like(acc)

        def block_fn(part, scores):
            weight = jnp.exp(scores - sums)
            d_weight = contract_cols(values[part], gradient)
            d_scores = (weight * (d_weight - delta)).astype(BF16)
            d_values[part] += matmul(weight.astype(BF16), gradient)
            d_keys[part] += matmul(d_scores, query[at]) * scale
            acc[...] += matmul(keys_t[:, part], d_scores)

        def scan(block, carry):
            first_key = block * row_tok
            part = pl.ds(pl.multiple_of(first_key, row_tok), row_tok)
            masked = (block == 0) | (first_key == first_query) | (first_query == last_query)

            @pl.when(jnp.logical_not(masked))
            def _():
                block_fn(part, contract_cols(keys[part], query[at]) * scale)

            @pl.when(masked)
            def _():
                key_place = first_key + lax.broadcasted_iota(jnp.int32, (row_tok, row_tok), 0)
                place = first_query + lax.broadcasted_iota(jnp.int32, (1, row_tok), 1)
                allowed = (key_place <= place) & (key_place >= doc_start(place, cut))
                scores = contract_cols(keys[part], query[at]) * scale
                block_fn(part, jnp.where(allowed, scores, MASKED))

            return carry

        lax.fori_loop(0, core * 4 + index + 1, scan, 0)
        head_give[0, index] = (acc[...] * scale).T.astype(BF16)

    queries(0)
    plane_part(0)
    from_ends(0)
    collect.corner_step(order[1])
    start(2)
    spread.step(2)
    queries(1)
    from_inside(0)
    plane_part(1)
    from_ends(1)
    collect.corner_step(order[2])
    start(3)
    pair_sum.step(2)
    queries(2)
    from_inside(1)
    plane_part(2)
    from_ends(2)
    collect.corner_step(order[3])
    spread.step(3)
    queries(3)

    def give_back(step, kind):
        dest = here.rows[step]
        sems_of = back_send.at[step, kind], back_recv.at[kind, row]
        return remote(head_give.at[kind, dest], d_heads.at[row, kind], *sems_of, here.at_row(dest))

    def give_pair(kind):
        sems_of = pair_send.at[kind], pair_recv.at[kind]
        return remote(pair_out.at[kind], pair_in.at[kind], *sems_of, here.other_core())

    for step in range(1, 4):
        give_back(step, 0).start()
    d_heads[row, 0] = head_give[0, row]

    @pl.when(core == 1)
    def _():
        for kind, gradient in enumerate((d_keys, d_values)):
            pair_out[kind] = gradient[pl.ds(0, group_tok)].astype(BF16)
            give_pair(kind).start()
        for kind, gradient in enumerate((d_keys, d_values)):
            for part in range(4):
                at = pl.ds(group_tok + part * row_tok, row_tok)
                head_give[kind + 1, part] = gradient[at].astype(BF16)

    from_inside(2)
    plane_part(3)
    pair_sum.step(3)

    @pl.when(core == 0)
    def _():
        for kind, gradient in enumerate((d_keys, d_values)):
            give_pair(kind).wait_recv()
            for part in range(4):
                at = pl.ds(part * row_tok, row_tok)
                summed = gradient[at] + pair_in[kind, at].astype(F32)
                head_give[kind + 1, part] = summed.astype(BF16)

    for kind in (1, 2):
        for step in range(1, 4):
            give_back(step, kind).start()
        d_heads[row, kind] = head_give[kind, row]
    pair_sum.step(4)
    pair_sum.step(5)
    collect.own_step()
    out_total[...] = collect.mine[0, col]
    for source in here.rows[1:]:
        for kind in range(3):
            arrived(d_heads.at[source, kind], back_recv.at[kind, source])
    for step in range(1, 4):
        give_near(step).wait_send()
        give_head(step).wait_send()
        for kind in range(3):
            give_back(step, kind).wait_send()

    @pl.when(core == 1)
    def _():
        for kind in range(2):
            give_pair(kind).wait_send()

    pair_sum.finish()
    spread.finish()
    collect.finish()


def attend_back_stage(
    d_attn, query, keys, values, mixed, total, cuts, out_weights, out_parts, early, scale, collective_id
):
    rows, width = d_attn.shape
    row_tok, group_tok = 4 * rows, 16 * rows
    vmem, hbm = pl.BlockSpec(memory_space=pltpu.VMEM), pl.BlockSpec(memory_space=pl.ANY)
    dma = pltpu.SemaphoreType.DMA
    return pl.pallas_call(
        functools.partial(back_kernel, scale),
        in_specs=[pl.BlockSpec(memory_space=pltpu.SMEM)] + [vmem] * 6 + [hbm] * 2 + [vmem],
        out_specs=[vmem] * 4,
        out_shape=[
            jax.ShapeDtypeStruct((row_tok, width), BF16),
            jax.ShapeDtypeStruct((4, 3, row_tok, HD), BF16),
            jax.ShapeDtypeStruct((rows, width), BF16),
            jax.ShapeDtypeStruct(early.shape, F32),
        ],
        scratch_shapes=[
            pltpu.VMEM((width, width), BF16),
            pltpu.VMEM((4, rows, 4 * HD), BF16),
            pltpu.VMEM((4, rows, 4 * HD), BF16),
            pltpu.VMEM((4, 4, rows, HD), BF16),
            pltpu.VMEM((HD, 2 * group_tok), BF16),
            pltpu.VMEM((2 * group_tok, HD), F32),
            pltpu.VMEM((2 * group_tok, HD), F32),
            pltpu.VMEM((HD, row_tok), F32),
            pltpu.VMEM((2, group_tok, HD), BF16),
            pltpu.VMEM((2, group_tok, HD), BF16),
            pltpu.VMEM((3, 4, row_tok, HD), BF16),
        ]
        + pair_sum_buffers(*early.shape)
        + [
            dma, dma((4, 4)), dma((4,)), dma((4,)), dma((4,)), dma((4,)),
            dma((4, 3)), dma((3, 4)), dma((2,)), dma((2,)),
        ]
        + collect_buffers(rows, width)
        + COLLECT_SEMS
        + SPREAD_SEMS,
        compiler_params=pltpu.CompilerParams(
            collective_id=collective_id, has_side_effects=True, vmem_limit_bytes=58 * 2**20
        ),
    )(cuts, d_attn, query, keys, values, mixed, total, out_weights, out_parts, early)


def tail_kernel(
    d_heads, qkv, totals, all_gains, cosine, sine, weights_in, normed_in, mixed_rows, d_attn_in,
    hidden,
    grad_hidden, grads, late_sum, last_sum,
    weights, normed, d_attn, in_sem, last, last_got, last_send, last_recv, hop, hop_got, hop_send, hop_recv,
    d_qkv, late, mixed, units, stat, scales, sums, sum_held, sum_got, sum_send, sum_recv,
    stat_send, stat_recv,
    line, line_in, whole, give, other, plane, corner_one, corner_two, from_across, from_along,
    up_send, down_send, line_recv, other_send, other_recv,
    one_send, one_recv, two_send, two_recv, across_send, across_recv, along_send, along_recv,
    back_send, back_recv,
):
    here = Here()
    row, col, core = here.row, here.col, here.core
    rows = hidden.shape[0]
    depth, columns = grads.shape
    part = depth // 2
    first, second = pl.ds(0, part // 2), pl.ds(part // 2, part // 2)
    order = here.near_first[::-1]
    qkv_columns = d_qkv.shape[1]
    tile = 512

    def line_products():
        @pl.loop(0, weights.shape[0] // tile)
        def _(index):
            at = pl.ds(pl.multiple_of(index * tile, tile), tile)
            product = contract_cols(d_qkv[...], weights[at]).astype(BF16)
            line[:, :, at] = product.reshape(4, rows, tile)

    line_halves = (pl.ds(0, rows // 2), pl.ds(rows // 2, rows // 2))

    def give_up(place, half):
        at = line_halves[half]
        sems = up_send.at[half, place], line_recv.at[half, place]
        return remote(line.at[place, at], line_in.at[place, at], *sems, here.at_col(col + 1))

    def give_down(place, slot, half):
        at = line_halves[half]
        sems = down_send.at[half, place], line_recv.at[half, slot]
        return remote(line.at[place, at], line_in.at[slot, at], *sems, here.at_col(col - 1))

    def add_line(place, slot, half):
        at = line_halves[half]
        arrived(line_in.at[slot, at], line_recv.at[half, slot])
        add_into(line.at[place, at], line_in.at[slot, at])

    def line_step(place):
        for half in range(2):

            @pl.when(((place > col) & (col > 0)) | ((place < col) & (col < 3)))
            def _():
                add_line(place, place, half)

            @pl.when(place > col)
            def _():
                give_up(place, half).start()

            @pl.when(place < col - 1)
            def _():
                give_down(place, place, half).start()

            @pl.when(place == col - 1)
            def _():
                give_down(place, 4, half).start()

    def row_product(which):
        of_row = here.rows[which]
        at = pl.ds(pl.multiple_of(of_row * depth, depth), depth)
        whole[:, pl.ds(0, qkv_columns)] = transposed_product(normed[:, at], d_qkv[...]).astype(BF16)
        whole[:, pl.ds(qkv_columns, columns - qkv_columns)] = transposed_product(
            mixed[...], d_attn[:, at]
        ).astype(BF16)
        plane[which] = whole[pl.ds(pl.multiple_of(core * part, part), part)]
        give[which] = whole[pl.ds(pl.multiple_of((1 - core) * part, part), part)]
        to_core(which).start()

    def to_core(which):
        sems = other_send.at[which], other_recv.at[which]
        return remote(give.at[which], other.at[which], *sems, here.other_core())

    def own_sum(which):
        to_core(which).wait_recv()
        add_into(plane.at[which], other.at[which])

    give_one = remote(
        plane.at[3, first], corner_one, one_send, one_recv, here.at_row(here.across)
    )
    give_two = remote(
        plane.at[3, second], corner_two, two_send, two_recv, here.at_row(here.along)
    )

    def give_across(index):
        at = (first, second)[index]
        sems = across_send.at[index], across_recv.at[index]
        return remote(plane.at[1, at], from_across.at[at], *sems, here.at_row(here.across))

    def give_along(index):
        at = (first, second)[index]
        sems = along_send.at[index], along_recv.at[index]
        return remote(plane.at[2, at], from_along.at[at], *sems, here.at_row(here.along))

    pair_sum = PairSum(here, late, late_sum, sum_held, sum_got, sum_send, sum_recv)
    takes = [
        pltpu.make_async_copy(source, target, in_sem.at[index])
        for index, (source, target) in enumerate(
            ((weights_in, weights), (normed_in, normed), (d_attn_in, d_attn))
        )
    ]
    for take in takes:
        take.start()
    near = [(step // 2, step % 2) for step in range(1, 8)]

    def near_device(step):
        which, swap = near[step]
        return (here.rows[which], col, (core + swap) % 2)

    greet([near_device(step) for step in range(7)] + here.line_peers())

    width = hidden.shape[1]
    heads = d_heads.shape[0]
    row_tok = d_qkv.shape[0]
    late[...] = jnp.zeros_like(late)
    for kind in range(2):
        root = lax.rsqrt(totals[kind : kind + 1] / width + EPSILON)
        scales[kind] = jnp.broadcast_to(root, (HD, row_tok)).T
        square = jnp.zeros((row_tok, HD), F32)
        for head in range(heads):
            start = (head * 3 + kind) * HD
            raw = qkv[:, start : start + HD]
            given = d_heads[head, kind].astype(F32)
            unit = given * cosine[...] + pltpu.roll(given * sine[...], HD // 2, 1)
            place = pl.ds(pl.multiple_of((col * heads + head) * HD, HD), HD)
            gains = all_gains[kind + 1 : kind + 2, place]
            gain_sum = jnp.sum(unit * raw * scales[kind], axis=0, keepdims=True)
            late[kind : kind + 1, place] = gain_sum
            weighted = unit * gains
            square = square + weighted * raw
            units[kind, head] = weighted
        stat[col, kind : kind + 1] = jnp.sum(square.T, axis=0, keepdims=True)

    def give_stat(step):
        peer = here.line_peers()[step]
        return remote(stat.at[col], stat.at[col], stat_send.at[step], stat_recv.at[col], peer)

    for step in range(3):
        give_stat(step).start()
    for head in range(heads):
        d_qkv[:, (head * 3 + 2) * HD : (head * 3 + 3) * HD] = d_heads[head, 2]
        mixed[:, head * HD : (head + 1) * HD] = mixed_rows[head]
    for step in range(3):
        place = (col + step + 1) % 4
        arrived(stat.at[place], stat_recv.at[place])
    total = stat[0] + stat[1] + stat[2] + stat[3]
    for kind in range(2):
        sums[...] = jnp.broadcast_to(total[kind : kind + 1] / width, (HD, row_tok)).T
        for head in range(heads):
            start = (head * 3 + kind) * HD
            raw = qkv[:, start : start + HD]
            root = scales[kind]
            d_raw = root * units[kind, head] - raw * (root * root * root) * sums[...]
            d_qkv[:, start : start + HD] = d_raw.astype(BF16)
    ends = (col == 0) | (col == 3)
    pair_sum.begin()
    for take in takes:
        take.wait()
    line_products()

    @pl.when(ends)
    def _():
        for place in order[:3]:
            line_step(place)

    def inner_step(place):
        @pl.when(jnp.logical_not(ends))
        def _():
            line_step(place)

    row_product(3)
    row_product(1)
    pair_sum.step(0)
    inner_step(order[0])
    own_sum(3)
    give_one.start()
    give_two.start()
    row_product(2)
    pair_sum.step(1)
    own_sum(1)
    give_across(0).start()
    own_sum(2)
    give_along(1).start()
    inner_step(order[1])
    row_product(0)
    pair_sum.step(2)
    inner_step(order[2])
    give_two.wait_recv()
    add_into(plane.at[1, second], corner_two)
    give_across(1).start()
    give_one.wait_recv()
    add_into(plane.at[2, first], corner_one)
    give_along(0).start()
    own_sum(0)

    for half in range(2):

        @pl.when(col > 0)
        def _():
            add_line(col, col, half)

        @pl.when(col < 3)
        def _():
            add_line(col, 4, half)

    given = line[col].astype(F32)
    tokens = hidden[...].astype(F32)
    root = lax.rsqrt(jnp.mean(tokens * tokens, axis=1, keepdims=True) + EPSILON)
    part_sum = jnp.sum(given * tokens * root, axis=0, keepdims=True)
    eighth = width // 8
    me = row * 2 + core
    for index in range(8):
        last[index : index + 1] = part_sum[:, index * eighth : (index + 1) * eighth]

    def give_last(step):
        sems = last_send.at[step], last_recv.at[me]
        return remote(last, last_got.at[me], *sems, near_device(step))

    def give_hop(step):
        sems = hop_send.at[step], hop_recv.at[col]
        return remote(hop, hop_got.at[col], *sems, here.line_peers()[step])

    for step in range(7):
        give_last(step).start()
    last_got[me] = last[...]
    weighted = given * all_gains[0:1]
    inner = jnp.mean(weighted * tokens, axis=1, keepdims=True)
    grad_hidden[...] = root * weighted - tokens * (root * root * root) * inner
    pair_sum.step(3)
    for step in range(7):
        which, swap = near[step]
        source = here.rows[which] * 2 + (core + swap) % 2
        arrived(last_got.at[source], last_recv.at[source])
    held = last_got[0]
    for index in range(1, 8):
        held = held + last_got[index]
    hop[...] = held
    hop_got[col] = held
    for step in range(3):
        give_hop(step).start()
    pair_sum.step(4)
    for index in range(2):
        give_across(index).wait_recv()
        give_along(index).wait_recv()
    add_into(plane.at[0], from_across, from_along)
    own_half = pl.ds(pl.multiple_of(core * part, part), part)
    give_back = remote(
        plane.at[0], grads.at[own_half], back_send, back_recv, here.other_core()
    )
    give_back.start()
    grads[own_half] = plane[0]
    other_half = grads.at[pl.ds(pl.multiple_of((1 - core) * part, part), part)]
    pair_sum.step(5)
    for step in range(3):
        place = (col + step + 1) % 4
        arrived(hop_got.at[place], hop_recv.at[place])
    last_sum[...] = hop_got[0] + hop_got[1] + hop_got[2] + hop_got[3]
    arrived(other_half, back_recv)
    for step in range(7):
        give_last(step).wait_send()
    for step in range(3):
        give_hop(step).wait_send()
    pair_sum.finish()
    for step in range(3):
        give_stat(step).wait_send()
    give_back.wait_send()
    give_one.wait_send()
    give_two.wait_send()
    for index in range(2):
        give_across(index).wait_send()
        give_along(index).wait_send()
    for which in range(4):
        to_core(which).wait_send()
    for place in order:
        for half in range(2):

            @pl.when(place > col)
            def _():
                give_up(place, half).wait_send()

            @pl.when(place < col)
            def _():
                give_down(place, place, half).wait_send()


def tail_stage(
    d_heads, qkv, totals, gains, cosine, sine, weights, normed, mixed_rows, d_attn, hidden, collective_id
):
    row_tok, qkv_columns = qkv.shape
    rows, width = hidden.shape
    depth = width // 4
    out_columns = width // 4
    columns = qkv_columns + out_columns
    part = depth // 2
    heads = d_heads.shape[0]
    vmem, hbm = pl.BlockSpec(memory_space=pltpu.VMEM), pl.BlockSpec(memory_space=pl.ANY)
    dma = pltpu.SemaphoreType.DMA
    eighth = (8, width // 8)
    one, four = pltpu.SemaphoreType.DMA, pltpu.SemaphoreType.DMA((4,))
    two = pltpu.SemaphoreType.DMA((2,))
    three = pltpu.SemaphoreType.DMA((3,))
    return pl.pallas_call(
        tail_kernel,
        in_specs=[vmem] * 6 + [hbm] * 2 + [vmem, hbm, vmem],
        out_specs=[vmem] * 4,
        out_shape=[
            jax.ShapeDtypeStruct((rows, width), F32),
            jax.ShapeDtypeStruct((depth, columns), BF16),
            jax.ShapeDtypeStruct((8, width), F32),
            jax.ShapeDtypeStruct(eighth, F32),
        ],
        scratch_shapes=[
            pltpu.VMEM(weights.shape, BF16),
            pltpu.VMEM(normed.shape, BF16),
            pltpu.VMEM(d_attn.shape, BF16),
            dma((3,)),
            pltpu.VMEM(eighth, F32),
            pltpu.VMEM((8,) + eighth, F32),
            dma((7,)),
            dma((8,)),
            pltpu.VMEM(eighth, F32),
            pltpu.VMEM((4,) + eighth, F32),
            dma((3,)),
            dma((4,)),
            pltpu.VMEM((row_tok, qkv_columns), BF16),
            pltpu.VMEM((8, width), F32),
            pltpu.VMEM((row_tok, heads * HD), BF16),
            pltpu.VMEM((2, heads, row_tok, HD), F32),
            pltpu.VMEM((4, 8, row_tok), F32),
            pltpu.VMEM((2, row_tok, HD), F32),
            pltpu.VMEM((row_tok, HD), F32),
        ]
        + pair_sum_buffers(8, width)
        + [
            three, four,
            pltpu.VMEM((4, rows, width), BF16),
            pltpu.VMEM((5, rows, width), BF16),
            pltpu.VMEM((depth, columns), BF16),
            pltpu.VMEM((4, part, columns), BF16),
            pltpu.VMEM((4, part, columns), BF16),
            pltpu.VMEM((4, part, columns), BF16),
            pltpu.VMEM((part // 2, columns), BF16),
            pltpu.VMEM((part // 2, columns), BF16),
            pltpu.VMEM((part, columns), BF16),
            pltpu.VMEM((part, columns), BF16),
            dma((2, 4)), dma((2, 4)), dma((2, 5)), four, four,
            one, one, one, one, two, two, two, two,
            one, one,
        ],
        compiler_params=pltpu.CompilerParams(
            collective_id=collective_id, has_side_effects=True, vmem_limit_bytes=58 * 2**20
        ),
    )(
        d_heads, qkv, totals, gains, cosine, sine, weights, normed, mixed_rows, d_attn, hidden
    )


def expert_rows(rows, grads, gate, gate_w, up_w, down_w):
    pre_gate = matmul(rows, gate_w)
    pre_up = matmul(rows, up_w)
    back = contract_cols(grads, down_w)
    sigmoid_gate = jax.nn.sigmoid(pre_gate)
    silu_gate = pre_gate * sigmoid_gate
    hidden = (silu_gate * pre_up).astype(BF16)
    inner = jnp.sum(hidden.astype(F32) * back, axis=-1)
    weighted = (hidden.astype(F32) * gate).astype(BF16)
    d_hid = back * gate
    d_pregate = (d_hid * pre_up * (sigmoid_gate + silu_gate * (1.0 - sigmoid_gate))).astype(BF16)
    d_preup = (d_hid * silu_gate).astype(BF16)
    outputs = matmul(weighted, down_w).astype(BF16)
    d_rows = (contract_cols(d_pregate, gate_w) + contract_cols(d_preup, up_w)).astype(BF16)
    return (
        outputs,
        d_rows,
        inner,
        contract_rows(rows, d_pregate),
        contract_rows(rows, d_preup),
        contract_rows(weighted, grads),
    )


def experts(normed, grads, dense_gates, gate_w, up_w, down_w):
    rows_dev, width = normed.shape
    devices = math.prod(lax.axis_size(axis) for axis in ALL)
    expert_count = dense_gates.shape[1]
    expert = lax.axis_index(ALL) // 2
    parts = max(1, lax.axis_size("exp") // 2)
    step = rows_dev // parts

    def one_part(sums, piece):
        rows, grad_rows, gates = piece
        rows_all = lax.all_gather(rows, ALL, axis=0, tiled=True)
        grads_all = lax.all_gather(grad_rows, ALL, axis=0, tiled=True)
        gates_all = lax.all_gather(gates, ALL, axis=0, tiled=True)
        gate = lax.dynamic_slice_in_dim(gates_all, expert, 1, 1)
        got = expert_rows(rows_all, grads_all, gate, gate_w, up_w, down_w)
        outputs = lax.psum_scatter(got[0], ALL, scatter_dimension=0, tiled=True)
        d_rows = lax.psum_scatter(got[1], ALL, scatter_dimension=0, tiled=True)
        inner = lax.all_to_all(
            got[2].reshape(devices, step), ALL, split_axis=0, concat_axis=0, tiled=True
        )
        inner = inner.reshape(expert_count, 2, step).sum(axis=1).T
        sums = got[3:] if sums is None else tuple(a + b for a, b in zip(sums, got[3:]))
        return sums, (outputs, d_rows, inner)

    if parts == 1:
        sums, (outputs, d_rows, inner) = one_part(None, (normed, grads, dense_gates))
    else:
        start = tuple(jnp.zeros(w.shape, F32) for w in (gate_w, up_w, down_w))
        pieces = tuple(v.reshape(parts, step, -1) for v in (normed, grads, dense_gates))
        sums, got = lax.scan(one_part, start, pieces)
        outputs, d_rows, inner = (v.reshape(rows_dev, -1) for v in got)
    return outputs.astype(F32), d_rows.astype(F32), inner, sums


def experts_here(normed, grads_all, picks, router, halves, others):
    numbers = jnp.arange(router.shape[1], dtype=jnp.int32)
    mask = jnp.any(picks.T[None] == numbers[:, None, None], axis=1).astype(F32)
    out_parts, d_rows, inner, weights = expert_stage(
        normed, grads_all, mask, halves, others, router, 1
    )
    inner = inner[:, :, 0].reshape(router.shape[1], -1).T
    return out_parts, d_rows.astype(F32), inner, weights


def shards(
    hidden_in,
    out_grad,
    attn_gain,
    w_qkv,
    q_gain,
    k_gain,
    w_out,
    moe_gain,
    router,
    w_gate,
    w_up,
    w_down,
    routes,
    doc_cuts,
):
    row_count, col_count = lax.axis_size("row"), lax.axis_size("col")
    tokens = hidden_in[0].astype(F32)
    rows_dev, width = tokens.shape
    heads = w_qkv.shape[1] // (3 * HD)
    plane = heads * HD
    scale = HD ** (-0.5)
    side = lax.axis_index("exp") % 2
    row_tok = rows_dev * col_count
    group_tok = row_tok * row_count
    here = (row_count, col_count, lax.axis_size("exp")) == (4, 4, 2)
    sequence = 0 if here else lax.axis_index("exp") // 2
    cuts = lax.dynamic_index_in_dim(doc_cuts, sequence, 0, keepdims=False)

    if here:
        grads_all = lax.all_gather(out_grad[0], ("row", "col"), axis=0, tiled=True)
        gains = jnp.stack([attn_gain, q_gain, k_gain, moe_gain]).astype(F32)
        other_w = [lax.ppermute(w[0], "exp", [(0, 1), (1, 0)]) for w in (w_gate, w_up, w_down)]

    gain_one = attn_gain.astype(F32)
    scale_one = rms_scale(tokens)
    head_start = lax.axis_index("col") * plane
    gain_q = lax.dynamic_slice_in_dim(q_gain, head_start, plane, 0).astype(F32)
    gain_k = lax.dynamic_slice_in_dim(k_gain, head_start, plane, 0).astype(F32)
    row_places = side * group_tok + lax.axis_index("row") * row_tok + jnp.arange(row_tok, dtype=jnp.int32)
    unused_doc, position = doc_positions(row_places, cuts)
    cosine, sine = rope_tables(position, HD)
    if here:
        signed = jnp.concatenate([-sine[:, : HD // 2], sine[:, HD // 2 :]], axis=1)
        normed_row, qkv_w, qkv, totals, query, keys, values = project(
            hidden_in[0], gains, w_qkv, cosine, signed, 0
        )
        total_q, total_k = totals[0], totals[1]
        query = query.reshape(group_tok, HD)
        key_all, value_all = keys.reshape(-1, HD), values.reshape(-1, HD)
    else:
        normed_one = (tokens * scale_one * gain_one).astype(BF16)
        normed_row = lax.all_gather(normed_one, "col", axis=0, tiled=True)
        qkv_w = lax.all_gather(w_qkv, "row", axis=0, tiled=True)
        out_w = lax.all_gather(
            lax.all_gather(w_out, "row", axis=1, tiled=True), "col", axis=0, tiled=True
        )
        qkv = matmul(normed_row, qkv_w)
    qkv = qkv.reshape(row_tok, heads, 3, HD)
    query_raw, key_raw, value_raw = qkv[:, :, 0], qkv[:, :, 1], qkv[:, :, 2]
    if not here:
        total_q, total_k = lax.psum(
            (jnp.sum(query_raw * query_raw, axis=(1, 2)), jnp.sum(key_raw * key_raw, axis=(1, 2))),
            "col",
        )
    scale_q = lax.rsqrt(total_q / width + EPSILON)[:, None, None]
    scale_k = lax.rsqrt(total_k / width + EPSILON)[:, None, None]
    gain_q, gain_k = gain_q.reshape(heads, HD), gain_k.reshape(heads, HD)
    cosine, sine = cosine[:, None, :], sine[:, None, :]
    if not here:
        query = rotate(query_raw * scale_q * gain_q, cosine, sine).astype(BF16)
        key = rotate(key_raw * scale_k * gain_k, cosine, sine).astype(BF16)
        moved = rows_to_heads(jnp.concatenate([query, key, value_raw.astype(BF16)], axis=-1))
        query, own_pair = moved[:, :HD], moved[:, HD:]
        earlier_pair = from_behind(own_pair, "exp", 1)
        lower_pair = jnp.where(side == 0, own_pair, earlier_pair)
        upper_pair = jnp.where(side == 0, jnp.zeros_like(own_pair), own_pair)
        key_value = jnp.concatenate([lower_pair, upper_pair], axis=0)
        key_all, value_all = key_value[:, :HD], key_value[:, HD:]

    if here:
        mixed_wide, total, out_w, mixed_rows, middle, normed_two = attention_stage(
            query, key_all, value_all, doc_cuts, w_out, hidden_in[0], gains, scale, 4
        )
    else:
        mixed_wide, total = attend(query, key_all, value_all, cuts, scale)
        mixed = mixed_wide.astype(BF16)
        middle = tokens + matmul(heads_to_tokens(mixed), out_w)

    gain_two = moe_gain.astype(F32)
    scale_two = rms_scale(middle)
    if not here:
        normed_two = (middle * scale_two * gain_two).astype(BF16)
    gates_all = jax.nn.softmax(matmul(normed_two, router), axis=-1)
    picks = routes[0]
    chosen = jnp.any(
        picks[:, :, None] == jnp.arange(router.shape[1], dtype=jnp.int32)[None, None, :], axis=1
    )
    grad_out = out_grad[0].astype(F32)
    expert_w = (w_gate[0], w_up[0], w_down[0])
    if here:
        out_parts, d_normed_two, inner, weight_grads = experts_here(
            normed_two, grads_all, picks, router, expert_w, other_w
        )
    else:
        dense_gates = jnp.where(chosen, gates_all, 0.0)
        mixture, d_normed_two, inner, weight_grads = experts(
            normed_two, out_grad[0], dense_gates, *expert_w
        )
    dense = jnp.where(chosen, inner, 0.0)
    d_logits = (gates_all * (dense - jnp.sum(gates_all * dense, axis=-1, keepdims=True))).astype(BF16)
    grad_router = contract_rows(d_logits, normed_two)
    d_normed_two = d_normed_two + contract_cols(d_logits, router)
    grad_moe_gain = jnp.sum(d_normed_two * middle * scale_two, axis=0)
    weighted_two = d_normed_two * gain_two
    d_middle = (
        grad_out
        + scale_two * weighted_two
        - middle * scale_two**3 * jnp.mean(weighted_two * middle, axis=-1, keepdims=True)
    )

    d_attn = d_middle.astype(BF16)
    if here:
        early = jnp.concatenate([grad_moe_gain[None], jnp.zeros((7, width), F32), grad_router])
        d_attn_row, d_heads, mixture, early = attend_back_stage(
            d_attn, query, key_all, value_all, mixed_wide, total, doc_cuts, out_w, out_parts, early, scale, 2
        )
        grad_hidden, grads, late, last = tail_stage(
            d_heads, qkv.reshape(row_tok, -1), totals, gains, cosine[:, 0], signed,
            qkv_w, normed_row, mixed_rows, d_attn_row, hidden_in[0], 3,
        )
        grad_hidden = d_middle + grad_hidden
        grad_qkv = grads[:, : 3 * plane].astype(F32)
        grad_w_out = grads[:, 3 * plane :].astype(F32)
        weight_grads = [value.astype(F32) for value in weight_grads]
        final = middle + mixture.astype(F32)
        summed = (last.reshape(-1), late[0], late[1], early[0], early[8:])
    else:
        final = middle + mixture
        mixed_row = heads_to_rows(mixed).reshape(row_tok, plane)
        d_mixed = tokens_to_heads(contract_cols(d_attn, out_w).astype(BF16))
        d_attn_row = lax.all_gather(d_attn, "col", axis=0, tiled=True)
        d_query, acc_key, acc_value = attend_back(
            query, key_all, value_all, d_mixed, mixed_wide, total, cuts, scale
        )
        accumulated = jnp.concatenate([acc_key, acc_value], axis=1)
        lower_acc, upper_acc = accumulated[:group_tok], accumulated[group_tok:]
        kept_acc = jnp.where(side == 0, lower_acc, upper_acc)
        later_acc = from_behind(lower_acc.astype(BF16), "exp", -1).astype(F32)
        summed_pair = kept_acc + jnp.where(side == 0, later_acc, jnp.zeros_like(later_acc))
        d_heads = heads_to_rows(jnp.concatenate([d_query, summed_pair], axis=1).astype(BF16)).astype(F32)
        d_q_unit = rotate_back(d_heads[:, :, :HD], cosine, sine)
        d_k_unit = rotate_back(d_heads[:, :, HD : 2 * HD], cosine, sine)
        d_value = d_heads[:, :, 2 * HD :]
        weighted_q = d_q_unit * gain_q
        weighted_k = d_k_unit * gain_k
        sum_q, sum_k = lax.psum(
            (jnp.sum(weighted_q * query_raw, axis=(1, 2)), jnp.sum(weighted_k * key_raw, axis=(1, 2))),
            "col",
        )
        d_query_raw = scale_q * weighted_q - query_raw * scale_q**3 * (sum_q / width)[:, None, None]
        d_key_raw = scale_k * weighted_k - key_raw * scale_k**3 * (sum_k / width)[:, None, None]
        grad_q_part = jnp.sum(d_q_unit * query_raw * scale_q, axis=0).reshape(plane)
        grad_k_part = jnp.sum(d_k_unit * key_raw * scale_k, axis=0).reshape(plane)
        d_qkv = jnp.concatenate([d_query_raw, d_key_raw, d_value], axis=2).astype(BF16)
        d_qkv = d_qkv.reshape(row_tok, heads * 3 * HD)
        d_normed_one = lax.psum_scatter(
            contract_cols(d_qkv, qkv_w).astype(BF16), "col", scatter_dimension=0, tiled=True
        ).astype(F32)
        grad_qkv = lax.psum_scatter(
            contract_rows(normed_row, d_qkv).astype(BF16), "row", scatter_dimension=0, tiled=True
        )
        grad_w_out = lax.psum_scatter(
            contract_rows(mixed_row, d_attn_row).astype(BF16), "row", scatter_dimension=1, tiled=True
        )
        grad_qkv = lax.psum(grad_qkv, "exp").astype(F32)
        grad_w_out = lax.psum(grad_w_out, "exp").astype(F32)
        grad_attn_gain = jnp.sum(d_normed_one * tokens * scale_one, axis=0)
        weighted_one = d_normed_one * gain_one
        grad_hidden = (
            d_middle
            + scale_one * weighted_one
            - tokens * scale_one**3 * jnp.mean(weighted_one * tokens, axis=-1, keepdims=True)
        )
        empty = jnp.zeros((width,), F32)
        grad_q_full = lax.dynamic_update_slice_in_dim(empty, grad_q_part, head_start, 0)
        grad_k_full = lax.dynamic_update_slice_in_dim(empty, grad_k_part, head_start, 0)
        parts = (grad_attn_gain, grad_q_full, grad_k_full, grad_moe_gain)
        summed = lax.psum(parts + (grad_router,), ALL)
    return (
        final.astype(BF16)[None],
        grad_hidden[None],
        summed[0],
        grad_qkv,
        summed[1],
        summed[2],
        grad_w_out,
        summed[3],
        summed[4].T,
        weight_grads[0][None],
        weight_grads[1][None],
        weight_grads[2][None],
    )


def solution(mesh):
    token_spec = P("exp", ("row", "col"), None)
    expert_spec = P(("row", "col", "exp"), None, None)
    in_specs = (
        token_spec,
        token_spec,
        P(),
        P("row", "col"),
        P(),
        P(),
        P("col", "row"),
        P(),
        P(),
        expert_spec,
        expert_spec,
        expert_spec,
        token_spec,
        P(),
    )
    out_specs = (
        token_spec,
        token_spec,
        P(),
        P("row", "col"),
        P(),
        P(),
        P("col", "row"),
        P(),
        P(),
        expert_spec,
        expert_spec,
        expert_spec,
    )
    return jax.shard_map(shards, mesh=mesh, in_specs=in_specs, out_specs=out_specs, check_vma=False)
```

```python
import functools
import math

import jax
import jax.numpy as jnp
from jax import lax
from jax.experimental import pallas as pl
from jax.experimental.pallas import tpu as pltpu
from jax.sharding import PartitionSpec as P

HD = 128
EPSILON = 1e-05
ROPE_BASE = 10000.0
MASKED = -1e30
BF16 = jnp.bfloat16
F32 = jnp.float32


def matmul(left, right):
    return jnp.dot(left, right, preferred_element_type=F32)


def contract_rows(left, right):
    return lax.dot_general(left, right, (((0,), (0,)), ((), ())), preferred_element_type=F32)


def contract_cols(left, right):
    return lax.dot_general(left, right, (((1,), (1,)), ((), ())), preferred_element_type=F32)


def rms_scale(values):
    return lax.rsqrt(jnp.mean(values * values, axis=-1, keepdims=True) + EPSILON)


def rope_tables(position, width):
    frequency = ROPE_BASE ** (-jnp.arange(0, width, 2, dtype=F32) / width)
    angle = position.astype(F32)[:, None] * frequency[None, :]
    return (
        jnp.concatenate([jnp.cos(angle)] * 2, axis=-1),
        jnp.concatenate([jnp.sin(angle)] * 2, axis=-1),
    )


def rotate(values, cosine, sine):
    half = values.shape[-1] // 2
    turned = jnp.concatenate([-values[..., half:], values[..., :half]], axis=-1)
    return values * cosine + turned * sine


def rotate_back(values, cosine, sine):
    half = values.shape[-1] // 2
    turned = values * sine
    return values * cosine + jnp.concatenate([turned[..., half:], -turned[..., :half]], axis=-1)


def doc_positions(places, cuts):
    first = (places >= cuts[0]).astype(jnp.int32)
    second = (places >= cuts[1]).astype(jnp.int32)
    start = first * cuts[0] + second * (cuts[1] - cuts[0])
    return (first + second, places - start)


def from_behind(value, axis, steps):
    count = lax.axis_size(axis)
    initial, last = (max(0, -steps), min(count, count - steps))
    return lax.ppermute(value, axis, [(source, source + steps) for source in range(initial, last)])


def rows_to_heads(values):
    count = lax.axis_size("row")
    rows, heads, width = values.shape
    moved = lax.all_to_all(values.transpose(1, 0, 2), "row", split_axis=0, concat_axis=0, tiled=True)
    return moved.reshape(count * rows, width)


def heads_to_rows(values):
    count = lax.axis_size("row")
    rows, width = values.shape
    moved = lax.all_to_all(
        values.reshape(count, rows // count, width), "row", split_axis=0, concat_axis=0, tiled=True
    )
    return moved.transpose(1, 0, 2)


def heads_to_tokens(values):
    row_count, col_count = lax.axis_size("row"), lax.axis_size("col")
    rows = values.shape[0] // (row_count * col_count)
    moved = lax.all_to_all(
        values.reshape(row_count * col_count, rows, HD),
        ("row", "col"),
        split_axis=0,
        concat_axis=0,
        tiled=True,
    )
    moved = moved.reshape(row_count, col_count, rows, HD).transpose(2, 1, 0, 3)
    return moved.reshape(rows, row_count * col_count * HD)


def tokens_to_heads(values):
    row_count, col_count = lax.axis_size("row"), lax.axis_size("col")
    rows = values.shape[0]
    parted = values.reshape(rows, col_count, row_count, HD).transpose(2, 1, 0, 3)
    moved = lax.all_to_all(
        parted.reshape(row_count * col_count, rows, HD),
        ("row", "col"),
        split_axis=0,
        concat_axis=0,
        tiled=True,
    )
    return moved.reshape(row_count * col_count * rows, HD)


MESH = pl.DeviceIdType.MESH
ALL = ("row", "col", "exp")


class Here:
    def __init__(self):
        self.row, self.col, self.core = (lax.axis_index(axis) for axis in ALL)
        self.across = self.row + 1 - 2 * (self.row % 2)
        self.along = (self.row + 2) % 4
        self.opposite = 3 - self.row
        self.rows = (self.row, self.across, self.along, self.opposite)
        half = self.col // 2
        self.near_first = [
            self.col,
            1 + self.col % 2,
            2 - self.col - self.col % 2 + 3 * half,
            3 - 3 * half,
        ]

    def at_row(self, row):
        return (row, self.col, self.core)

    def at_col(self, col):
        return (self.row, col, self.core)

    def other_core(self):
        return (self.row, self.col, 1 - self.core)

    def line_peers(self):
        return [self.at_col((self.col + step) % 4) for step in (1, 2, 3)]

    def group_peers(self):
        steps = range(1, 16)
        return [((self.row + s // 4) % 4, (self.col + s) % 4, self.core) for s in steps]

    def plane_peers(self):
        return [self.at_row(row) for row in self.rows[1:]]


def greet(peers):
    barrier = pltpu.get_barrier_semaphore()
    for peer in peers:
        pl.semaphore_signal(barrier, inc=1, device_id=peer, device_id_type=MESH)
    pl.semaphore_wait(barrier, len(peers))


def greet_near(here):
    barrier = pltpu.get_barrier_semaphore()
    col = here.col

    def signal(peer):
        pl.semaphore_signal(barrier, inc=1, device_id=peer, device_id_type=MESH)

    for peer in (here.other_core(), here.at_row(here.across), here.at_row(here.along)):
        signal(peer)

    @pl.when(col > 0)
    def _():
        signal(here.at_col(col - 1))

    @pl.when(col < 3)
    def _():
        signal(here.at_col(col + 1))

    pl.semaphore_wait(barrier, 3 + (col + 3) // 4 + (6 - col) // 4)


def remote(source, target, send, recv, device):
    return pltpu.make_async_remote_copy(
        src_ref=source,
        dst_ref=target,
        send_sem=send,
        recv_sem=recv,
        device_id=device,
        device_id_type=MESH,
    )


def arrived(target, recv):
    pltpu.make_async_copy(target, target, recv).wait()


def add_into(target, *terms):
    step = 16

    @pl.loop(0, target.shape[0] // step)
    def _(index):
        part = pl.ds(pl.multiple_of(index * step, step), step)
        value = target[part].astype(F32)
        for term in terms:
            value = value + term[part].astype(F32)
        target[part] = value.astype(target.dtype)


SPREAD_SEMS = [pltpu.SemaphoreType.DMA((4,))] * 11 + [pltpu.SemaphoreType.DMA((4, 4))] * 2


class Spread:
    def __init__(self, here, own, block, rows, sems, line=True, plane=True, core=True):
        self.here, self.own, self.block = here, own, block
        self.line, self.plane, self.core = line, plane, core
        (
            self.up_send, self.down_send, self.line_recv,
            self.across_send, self.across_recv, self.along_send, self.along_recv,
            self.one_send, self.one_recv, self.two_send, self.two_recv,
            self.core_send, self.core_recv,
        ) = sems
        self.first, self.second = pl.ds(0, rows // 2), pl.ds(rows // 2, rows // 2)
        self.order = here.near_first if line else [0]
        self.steps = len(self.order)

    def held(self, step):
        here = self.here
        return self.own if step == 0 else self.block(here.row, self.order[step], here.core)

    def up(self, step):
        here, place = self.here, self.order[step]
        target = self.block(here.row, place, here.core)
        recv = self.line_recv.at[place]
        return remote(self.held(step), target, self.up_send.at[place], recv, here.at_col(here.col + 1))

    def down(self, step):
        here, place = self.here, self.order[step]
        target = self.block(here.row, place, here.core)
        recv = self.line_recv.at[place]
        return remote(self.held(step), target, self.down_send.at[place], recv, here.at_col(here.col - 1))

    def to_across(self, step):
        here, place = self.here, self.order[step]
        target = self.block(here.row, place, here.core)
        sems = self.across_send.at[place], self.across_recv.at[place]
        return remote(self.held(step), target, *sems, here.at_row(here.across))

    def to_along(self, step):
        here, place = self.here, self.order[step]
        target = self.block(here.row, place, here.core)
        sems = self.along_send.at[place], self.along_recv.at[place]
        return remote(self.held(step), target, *sems, here.at_row(here.along))

    def corner_one(self, step):
        here, place = self.here, self.order[step]
        part = self.block(here.across, place, here.core).at[self.first]
        sems = self.one_send.at[place], self.one_recv.at[place]
        return remote(part, part, *sems, here.at_row(here.along))

    def corner_two(self, step):
        here, place = self.here, self.order[step]
        part = self.block(here.along, place, here.core).at[self.second]
        sems = self.two_send.at[place], self.two_recv.at[place]
        return remote(part, part, *sems, here.at_row(here.across))

    def to_core(self, which, step):
        here, place = self.here, self.order[step]
        target = self.block(here.rows[which], place, here.core)
        source = self.held(step) if which == 0 else target
        sems = self.core_send.at[which, place], self.core_recv.at[which, place]
        return remote(source, target, *sems, here.other_core())

    def line_step(self, step):
        here, place = self.here, self.order[step]
        if step > 0:
            arrived(self.held(step), self.line_recv.at[place])
        if self.line:

            @pl.when((place <= here.col) & (here.col < 3))
            def _():
                self.up(step).start()

            @pl.when((place >= here.col) & (here.col > 0))
            def _():
                self.down(step).start()

    def near_step(self, step):
        self.to_across(step).start()
        self.to_along(step).start()
        if self.core:
            self.to_core(0, step).start()

    def plane_step(self, step):
        here, place = self.here, self.order[step]
        arrived(self.block(here.across, place, here.core), self.across_recv.at[place])
        self.corner_one(step).start()
        if self.core:
            self.to_core(1, step).start()
        arrived(self.block(here.along, place, here.core), self.along_recv.at[place])
        self.corner_two(step).start()
        if self.core:
            self.to_core(2, step).start()

    def corner_step(self, step):
        here, place = self.here, self.order[step]
        target = self.block(here.opposite, place, here.core)
        arrived(target.at[self.first], self.one_recv.at[place])
        arrived(target.at[self.second], self.two_recv.at[place])
        if self.core:
            self.to_core(3, step).start()

    def step(self, index):
        if index < self.steps:
            self.line_step(index)
        if self.plane and 0 <= index - 1 < self.steps:
            self.plane_step(index - 1)
        if self.plane and index < self.steps:
            self.near_step(index)
        if self.plane and 0 <= index - 2 < self.steps:
            self.corner_step(index - 2)

    def core_arrived(self, which, step):
        here, place = self.here, self.order[step]
        target = self.block(here.rows[which], place, 1 - here.core)
        arrived(target, self.core_recv.at[which, place])

    def finish(self, arrivals=True):
        here = self.here
        for step in range(self.steps):
            place = self.order[step]
            if self.line:

                @pl.when((place <= here.col) & (here.col < 3))
                def _():
                    self.up(step).wait_send()

                @pl.when((place >= here.col) & (here.col > 0))
                def _():
                    self.down(step).wait_send()

            if self.plane:
                self.to_across(step).wait_send()
                self.to_along(step).wait_send()
                self.corner_one(step).wait_send()
                self.corner_two(step).wait_send()
                for which in range(4 if self.core else 0):
                    self.to_core(which, step).wait_send()
                    if arrivals:
                        self.core_arrived(which, step)


COLLECT_SEMS = (
    [pltpu.SemaphoreType.DMA((4,))] * 4
    + [pltpu.SemaphoreType.DMA((2, 4))] * 4
    + [pltpu.SemaphoreType.DMA((2, 4))] * 2
    + [pltpu.SemaphoreType.DMA((2, 5))]
)


def collect_buffers(rows, width):
    return [
        pltpu.VMEM((4, 4, rows, width), BF16),
        pltpu.VMEM((4, rows // 2, width), BF16),
        pltpu.VMEM((4, rows // 2, width), BF16),
        pltpu.VMEM((4, rows, width), BF16),
        pltpu.VMEM((4, rows, width), BF16),
        pltpu.VMEM((5, rows, width), BF16),
    ]


class Collect:
    def __init__(self, here, buffers, sems):
        self.here = here
        self.mine, self.one, self.two, self.from_across, self.from_along, self.line = buffers
        (
            self.one_send, self.one_recv, self.two_send, self.two_recv,
            self.across_send, self.across_recv, self.along_send, self.along_recv,
            self.up_send, self.down_send, self.line_recv,
        ) = sems
        half = self.mine.shape[2] // 2
        self.halves = (pl.ds(0, half), pl.ds(half, half))

    def give_one(self, place):
        here = self.here
        return remote(
            self.mine.at[3, place, self.halves[0]], self.one.at[place],
            self.one_send.at[place], self.one_recv.at[place], here.at_row(here.across),
        )

    def give_two(self, place):
        here = self.here
        return remote(
            self.mine.at[3, place, self.halves[1]], self.two.at[place],
            self.two_send.at[place], self.two_recv.at[place], here.at_row(here.along),
        )

    def give_across(self, place, half):
        here, part = self.here, self.halves[half]
        return remote(
            self.mine.at[1, place, part], self.from_across.at[place, part],
            self.across_send.at[half, place], self.across_recv.at[half, place], here.at_row(here.across),
        )

    def give_along(self, place, half):
        here, part = self.here, self.halves[half]
        return remote(
            self.mine.at[2, place, part], self.from_along.at[place, part],
            self.along_send.at[half, place], self.along_recv.at[half, place], here.at_row(here.along),
        )

    def give_up(self, place, half):
        here, part = self.here, self.halves[half]
        sems = self.up_send.at[half, place], self.line_recv.at[half, place]
        return remote(
            self.mine.at[0, place, part], self.line.at[place, part], *sems, here.at_col(here.col + 1)
        )

    def give_down(self, place, slot, half):
        here, part = self.here, self.halves[half]
        sems = self.down_send.at[half, place], self.line_recv.at[half, slot]
        return remote(
            self.mine.at[0, place, part], self.line.at[slot, part], *sems, here.at_col(here.col - 1)
        )

    def add_line(self, place, slot, half):
        part = self.halves[half]
        arrived(self.line.at[slot, part], self.line_recv.at[half, slot])
        add_into(self.mine.at[0, place, part], self.line.at[slot, part])

    def start_far(self, place):
        self.give_one(place).start()
        self.give_two(place).start()
        self.give_along(place, 1).start()

    def start_near(self, place):
        self.give_across(place, 0).start()

    def corner_step(self, place):
        self.give_two(place).wait_recv()
        add_into(self.mine.at[1, place, self.halves[1]], self.two.at[place])
        self.give_across(place, 1).start()
        self.give_one(place).wait_recv()
        add_into(self.mine.at[2, place, self.halves[0]], self.one.at[place])
        self.give_along(place, 0).start()

    def plane_step(self, place):
        for half in range(2):
            self.give_across(place, half).wait_recv()
            self.give_along(place, half).wait_recv()
        add_into(self.mine.at[0, place], self.from_across.at[place], self.from_along.at[place])

    def line_step(self, place):
        col = self.here.col
        for half in range(2):

            @pl.when(((place > col) & (col > 0)) | ((place < col) & (col < 3)))
            def _():
                self.add_line(place, place, half)

            @pl.when(place > col)
            def _():
                self.give_up(place, half).start()

            @pl.when(place < col - 1)
            def _():
                self.give_down(place, place, half).start()

            @pl.when(place == col - 1)
            def _():
                self.give_down(place, 4, half).start()

    def own_step(self):
        col = self.here.col
        for half in range(2):

            @pl.when(col > 0)
            def _():
                self.add_line(col, col, half)

            @pl.when(col < 3)
            def _():
                self.add_line(col, 4, half)

    def finish(self):
        col = self.here.col
        for place in range(4):
            self.give_one(place).wait_send()
            self.give_two(place).wait_send()
            for half in range(2):
                self.give_across(place, half).wait_send()
                self.give_along(place, half).wait_send()

                @pl.when(place > col)
                def _():
                    self.give_up(place, half).wait_send()

                @pl.when(place < col)
                def _():
                    self.give_down(place, place, half).wait_send()


def doc_start(places, cuts):
    return jnp.where(places >= cuts[1], cuts[1], jnp.where(places >= cuts[0], cuts[0], 0))


def key_blocks(cuts, first_query, rows, scores_of, block_fn):
    def scan(index, carry):
        start = pl.multiple_of(index * rows, rows)
        free = (start >= doc_start(first_query + rows - 1, cuts)) & (start + rows <= first_query + 1)

        @pl.when(free)
        def _():
            block_fn(start, scores_of(start))

        @pl.when(jnp.logical_not(free))
        def _():
            key_place = start + lax.broadcasted_iota(jnp.int32, (rows, rows), 0)
            place = first_query + lax.broadcasted_iota(jnp.int32, (1, rows), 1)
            allowed = (key_place <= place) & (key_place >= doc_start(place, cuts))
            block_fn(start, jnp.where(allowed, scores_of(start), MASKED))

        return carry

    lax.fori_loop(doc_start(first_query, cuts) // rows, first_query // rows + 1, scan, 0)


def attend_kernel(scale, group_tok, cuts, query, keys, values_t, mixed, total, top, summed, acc):
    rows = query.shape[0]
    side = lax.axis_index("exp") % 2
    first_query = side * group_tok + pl.program_id(0) * rows
    top[...] = jnp.full_like(top, MASKED)
    summed[...] = jnp.zeros_like(summed)
    acc[...] = jnp.zeros_like(acc)
    cut = (cuts[0, 0], cuts[0, 1])

    def scores_of(start):
        return contract_cols(keys[pl.ds(start, rows)], query[...]) * scale

    def block_fn(start, scores):
        old = top[...]
        new = jnp.maximum(old, jnp.max(scores, axis=0, keepdims=True))
        weights = jnp.exp(scores - new)
        decay = jnp.exp(old - new)
        top[...] = new
        summed[...] = summed[...] * decay + jnp.sum(weights, axis=0, keepdims=True)
        acc[...] = acc[...] * decay + matmul(values_t[:, pl.ds(start, rows)], weights.astype(BF16))

    key_blocks(cut, first_query, rows, scores_of, block_fn)
    mixed[...] = (acc[...] / summed[...]).T
    total[...] = top[...] + jnp.log(summed[...])


def attend(query, keys, values, cuts, scale, rows=512):
    group_tok, head_size = query.shape
    whole = lambda shape: pl.BlockSpec(shape, lambda i: (0, 0))
    return pl.pallas_call(
        functools.partial(attend_kernel, scale, group_tok),
        grid=(group_tok // rows,),
        in_specs=[
            pl.BlockSpec(memory_space=pltpu.SMEM),
            pl.BlockSpec((rows, head_size), lambda i: (i, 0)),
            whole(keys.shape),
            whole(values.shape[::-1]),
        ],
        out_specs=[
            pl.BlockSpec((rows, head_size), lambda i: (i, 0)),
            pl.BlockSpec((1, rows), lambda i: (0, i)),
        ],
        out_shape=[
            jax.ShapeDtypeStruct((group_tok, head_size), F32),
            jax.ShapeDtypeStruct((1, group_tok), F32),
        ],
        scratch_shapes=[
            pltpu.VMEM((1, rows), F32),
            pltpu.VMEM((1, rows), F32),
            pltpu.VMEM((head_size, rows), F32),
        ],
        compiler_params=pltpu.CompilerParams(vmem_limit_bytes=40 * 2**20),
        cost_estimate=pl.CostEstimate(
            flops=4 * 7 * 2**20 * head_size, bytes_accessed=2**23, transcendentals=7 * 2**20
        ),
    )(cuts[None], query, keys, values.T)


def attend_back_kernel(
    scale, group_tok, cuts, query, keys, keys_t, values, d_mixed, total, delta,
    d_query, d_keys, d_values, acc,
):
    rows = query.shape[0]
    side = lax.axis_index("exp") % 2
    first_query = side * group_tok + pl.program_id(0) * rows
    cut = (cuts[0, 0], cuts[0, 1])

    @pl.when(pl.program_id(0) == 0)
    def _():
        d_keys[...] = jnp.zeros_like(d_keys)
        d_values[...] = jnp.zeros_like(d_values)

    acc[...] = jnp.zeros_like(acc)

    def scores_of(start):
        return contract_cols(keys[pl.ds(start, rows)], query[...]) * scale

    def block_fn(start, scores):
        part = pl.ds(start, rows)
        weights = jnp.exp(scores - total[...])
        d_weights = contract_cols(values[part], d_mixed[...])
        d_scores = (weights * (d_weights - delta[...])).astype(BF16)
        d_values[part] += matmul(weights.astype(BF16), d_mixed[...])
        d_keys[part] += matmul(d_scores, query[...]) * scale
        acc[...] += matmul(keys_t[:, part], d_scores)

    key_blocks(cut, first_query, rows, scores_of, block_fn)
    d_query[...] = (acc[...] * scale).T


def attend_back(query, keys, values, d_mixed, mixed, total, cuts, scale, rows=512):
    group_tok, head_size = query.shape
    delta = jnp.sum(d_mixed.astype(F32) * mixed, axis=1)[None]
    whole = lambda shape: pl.BlockSpec(shape, lambda i: (0, 0))
    block = pl.BlockSpec((rows, head_size), lambda i: (i, 0))
    line = pl.BlockSpec((1, rows), lambda i: (0, i))
    return pl.pallas_call(
        functools.partial(attend_back_kernel, scale, group_tok),
        grid=(group_tok // rows,),
        in_specs=[
            pl.BlockSpec(memory_space=pltpu.SMEM),
            block,
            whole(keys.shape),
            whole(keys.shape[::-1]),
            whole(keys.shape),
            block,
            line,
            line,
        ],
        out_specs=[block, whole(keys.shape), whole(keys.shape)],
        out_shape=[
            jax.ShapeDtypeStruct((group_tok, head_size), F32),
            jax.ShapeDtypeStruct(keys.shape, F32),
            jax.ShapeDtypeStruct(keys.shape, F32),
        ],
        scratch_shapes=[pltpu.VMEM((head_size, rows), F32)],
        compiler_params=pltpu.CompilerParams(vmem_limit_bytes=48 * 2**20),
        cost_estimate=pl.CostEstimate(
            flops=10 * 7 * 2**20 * head_size, bytes_accessed=2**23, transcendentals=7 * 2**20
        ),
    )(cuts[None], query, keys, keys.T, values, d_mixed, total, delta)


def transposed_product(left, right):
    return jnp.dot(left.T, right, preferred_element_type=F32)


def column_of(line):
    return jnp.broadcast_to(line, (128, 128)).T[:, :1]


def line_of(column):
    return jnp.broadcast_to(column, (128, 128)).T[:1]


def expert_kernel(
    normed, grads_all, mask, gate_half, up_half, down_half,
    gate_other, up_other, down_other, router,
    rows_all, out_parts, total, inner_in, grad_gate, grad_up, grad_down,
    their_gates, their_down,
    gate_w, up_w, down_w, masks, x_buf, d_buf, gates_t, weighteds_t, d_gates, d_ups, weighteds, out_buf,
    inner, sum_buf, sum_down, *rest,
):
    here = Here()
    row, col, core = here.row, here.col, here.core
    rows, width = normed.shape
    half = gate_half.shape[1]
    expert = row * 4 + col
    count = len(SPREAD_SEMS)
    collect = Collect(here, rest[:6], rest[6 : 6 + len(COLLECT_SEMS)])
    rest = rest[6 + len(COLLECT_SEMS) :]
    (
        weight_sem, load_sem, store_sem, tile_sem, give_send, give_recv, their_sem, sum_sem,
        inner_send, inner_recv,
    ) = rest[:10]
    sems = rest[10:]

    def x_block(of_row, place, unused_core):
        return rows_all.at[pl.ds(pl.multiple_of((of_row * 4 + place) * rows, rows), rows)]

    def d_block(of_row, place, unused_core):
        return grads_all.at[pl.ds(pl.multiple_of((of_row * 4 + place) * rows, rows), rows)]

    def m_block(of_row, place, unused_core):
        return masks.at[of_row, place]

    spread_x = Spread(here, normed, x_block, rows, sems[:count], core=False)
    spread_m = Spread(here, mask, m_block, mask.shape[0], sems[count:], core=False)
    order = here.near_first

    own_half = pl.ds(pl.multiple_of(core * half, half), half)
    other_half = pl.ds(pl.multiple_of((1 - core) * half, half), half)
    keeps = [
        pltpu.make_async_copy(source, target, weight_sem.at[index])
        for index, (source, target) in enumerate(
            (
                (normed, x_block(row, col, 0)),
                (mask, m_block(row, col, 0)),
                (gate_half, gate_w.at[:, own_half]),
                (up_half, up_w.at[:, own_half]),
                (down_half, down_w.at[own_half]),
                (gate_other, gate_w.at[:, other_half]),
                (up_other, up_w.at[:, other_half]),
                (down_other, down_w.at[other_half]),
            )
        )
    ]
    greet(here.group_peers() + [here.other_core()])
    spread_x.step(0)
    spread_m.step(0)
    for keep in keeps:
        keep.start()

    turns = (3, 2, 1, 0)

    def loads(step):
        return [
            pltpu.make_async_copy(
                source(here.rows[which], order[step], 0),
                target.at[pl.ds(position * rows, rows)],
                load_sem.at[position, array],
            )
            for position, which in enumerate(turns)
            for array, (source, target) in enumerate(((x_block, x_buf), (d_block, d_buf)))
        ]

    def stores(step):
        return [
            pltpu.make_async_copy(
                out_buf.at[pl.ds(position * rows, rows)],
                out_parts.at[which, order[step]],
                store_sem.at[position],
            )
            for position, which in enumerate(turns)
        ]

    tile = 256

    def first_products(step):
        place = order[step]
        x = x_buf[...]
        lane = lax.broadcasted_iota(jnp.int32, (x.shape[0], router.shape[0]), 1)
        logits = contract_cols(x, router[...])
        raised = jnp.exp(logits - jnp.max(logits, axis=1, keepdims=True))
        picked = jnp.sum(jnp.where(lane == expert, raised, 0.0), axis=1, keepdims=True)
        routed = jnp.concatenate(
            [column_of(masks[here.rows[which], place, pl.ds(expert, 1)]) for which in turns]
        )
        gate = picked / jnp.sum(raised, axis=1, keepdims=True) * routed
        columns = [
            pl.ds(pl.multiple_of((here.rows[which] * 4 + place) * rows, rows), rows) for which in turns
        ]

        def tile_step(index, inner_sum):
            at = pl.ds(pl.multiple_of(index * tile, tile), tile)
            pre_gate = matmul(x_buf[...], gate_w[:, at])
            pre_up = matmul(x_buf[...], up_w[:, at])
            back = contract_cols(d_buf[...], down_w[at])
            sigmoid_gate = 0.5 * jnp.tanh(0.5 * pre_gate) + 0.5
            silu_gate = pre_gate * sigmoid_gate
            hidden = (silu_gate * pre_up).astype(BF16).astype(F32)
            d_hid = back * gate
            d_gate = (d_hid * pre_up * (sigmoid_gate + silu_gate * (1.0 - sigmoid_gate))).astype(BF16)
            d_up = (d_hid * silu_gate).astype(BF16)
            weight = (hidden * gate).astype(BF16)
            d_gates[:, at] = d_gate
            d_ups[:, at] = d_up
            weighteds[:, at] = weight
            side = index // (half // tile)
            first = pl.multiple_of(index % (half // tile) * tile, tile)
            for values, target in (
                (d_gate, gates_t.at[side, pl.ds(first, tile)]),
                (d_up, gates_t.at[side, pl.ds(first + half, tile)]),
                (weight, weighteds_t.at[at]),
            ):
                turned = values.T
                for position, column in enumerate(columns):
                    target[:, column] = turned[:, position * rows : (position + 1) * rows]
            return inner_sum + jnp.sum(hidden * back, axis=1, keepdims=True)

        start = jnp.zeros((x.shape[0], 1), F32)
        inner_sum = lax.fori_loop(0, gate_w.shape[1] // tile, tile_step, start, unroll=2)
        for position, which in enumerate(turns):
            part = slice(position * rows, (position + 1) * rows)
            inner[here.rows[which], place, 0:1] = line_of(inner_sum[part])

    def second_products(step):
        place = order[step]

        @pl.loop(0, width // tile, unroll=2)
        def _(index):
            at = pl.ds(pl.multiple_of(index * tile, tile), tile)
            out_buf[:, at] = matmul(weighteds[...], down_w[:, at]).astype(BF16)
            d_x = contract_cols(d_gates[...], gate_w[at]) + contract_cols(d_ups[...], up_w[at])
            d_x = d_x.astype(BF16)
            for position, which in enumerate(turns):
                collect.mine[which, place, :, at] = d_x[position * rows : (position + 1) * rows]

    for index in (1, 2):
        spread_x.step(index)
        spread_m.step(index)
    for keep in keeps:
        keep.wait()
    for copy in loads(0):
        copy.start()
    turn_order = (0, 1, 3, 2)
    ends = (col == 0) | (col == 3)

    def from_ends(step):
        @pl.when(ends)
        def _():
            collect.line_step(order[step])

    def from_inside(step):
        @pl.when(jnp.logical_not(ends))
        def _():
            collect.line_step(order[step])

    def start(step):
        collect.start_far(order[step])
        collect.start_near(order[step])

    for turn, step in enumerate(turn_order):
        for copy in loads(step):
            copy.wait()
        first_products(step)
        if turn < 2:
            spread_x.step(turn + 3)
            spread_m.step(turn + 3)
        if turn in (0, 2):
            for copy in loads(turn_order[turn + 1]):
                copy.start()
        if turn > 0:
            for copy in stores(turn_order[turn - 1]):
                copy.wait()
        if turn == 2:
            collect.corner_step(order[1])
        if turn == 3:
            collect.corner_step(order[3])
        second_products(step)
        for copy in stores(step):
            copy.start()
        if turn == 1:
            spread_x.step(5)
            spread_m.step(5)
            for copy in loads(turn_order[2]):
                copy.start()
            start(1)
            start(0)
        if turn == 2:
            start(3)
            collect.corner_step(order[0])
            collect.plane_step(order[1])
            from_ends(1)
        if turn == 3:
            start(2)
            collect.plane_step(order[3])
            from_ends(3)
            collect.plane_step(order[0])

    tiles = width // tile

    def tile_at(index):
        return pl.ds(pl.multiple_of(index * tile, tile), tile)

    def acts_of(kind, side):
        if kind == 0:
            return gates_t[side]
        return weighteds_t[pl.ds(pl.multiple_of(side * half, half), half)]

    counts = (2 * half, half)

    def slot_at(kind, slot):
        return pl.ds(pl.multiple_of((2 * kind + slot) * tile, tile), tile)

    def tile_buf(kind, slot):
        return gate_w.at[:, slot_at(kind, slot)]

    def give_buf(kind, slot):
        return up_w.at[pl.ds(0, counts[kind]), slot_at(kind, slot)]

    def their_buf(kind, slot):
        return up_w.at[pl.ds(width // 2, counts[kind]), slot_at(kind, slot)]

    theirs = (their_gates, their_down)

    def tile_load(kind, index, slot):
        source = (rows_all, grads_all)[kind]
        return pltpu.make_async_copy(
            source.at[:, tile_at(index)], tile_buf(kind, slot), tile_sem.at[slot]
        )

    def give(kind, index, slot):
        sems = give_send.at[slot, kind], give_recv.at[kind, index]
        return remote(give_buf(kind, slot), theirs[kind].at[:, tile_at(index)], *sems, here.other_core())

    def their_load(kind, index, slot):
        return pltpu.make_async_copy(
            theirs[kind].at[:, tile_at(index)],
            their_buf(kind, slot),
            their_sem.at[slot, kind],
        )

    def sum_stores(kind, index, slot):
        if kind == 1:
            target = grad_down.at[:, tile_at(index)]
            return [pltpu.make_async_copy(sum_down, target, sum_sem.at[0, 2])]
        return [
            pltpu.make_async_copy(
                sum_buf.at[slot, part], target.at[tile_at(index)], sum_sem.at[slot, part]
            )
            for part, target in enumerate((grad_gate, grad_up))
        ]

    def give_gradients(kind, start, stop):
        tile_load(kind, start, 0).start()

        @pl.loop(start, stop)
        def _(index):
            slot = index % 2

            @pl.when(index + 1 < stop)
            def _():
                tile_load(kind, index + 1, 1 - slot).start()

            tile_load(kind, index, slot).wait()
            product = matmul(acts_of(kind, 1 - core), tile_buf(kind, slot)[...])

            @pl.when(index >= 2)
            def _():
                give(kind, index - 2, slot).wait_send()

            give_buf(kind, slot)[...] = product.astype(BF16)
            give(kind, index, slot).start()

    def keep_gradients(kind, start, stop):
        tile_load(kind, start, 0).start()
        give(kind, start, 0).wait_recv()
        their_load(kind, start, 0).start()

        @pl.loop(start, stop)
        def _(index):
            slot = index % 2

            @pl.when(index + 1 < stop)
            def _():
                tile_load(kind, index + 1, 1 - slot).start()
                give(kind, index + 1, 1 - slot).wait_recv()
                their_load(kind, index + 1, 1 - slot).start()

            tile_load(kind, index, slot).wait()
            product = matmul(acts_of(kind, core), tile_buf(kind, slot)[...])
            their_load(kind, index, slot).wait()
            product = product + their_buf(kind, slot)[...].astype(F32)
            held = 2 - kind

            @pl.when(index >= held)
            def _():
                for copy in sum_stores(kind, index - held, slot):
                    copy.wait()

            if kind == 1:
                sum_down[...] = product.astype(BF16)
            else:
                sum_buf[slot, 0] = product[:half].T.astype(BF16)
                sum_buf[slot, 1] = product[half:].T.astype(BF16)
            for copy in sum_stores(kind, index, slot):
                copy.start()

    def give_inner(index):
        step = index + 1
        to_row, to_col = (row + step // 4) % 4, (col + step) % 4
        return remote(
            inner.at[to_row, to_col],
            inner_in.at[row, col],
            inner_send.at[index],
            inner_recv.at[row, col],
            (to_row, to_col, core),
        )

    for index in range(15):
        give_inner(index).start()
    inner_in[row, col] = inner[row, col]
    give_gradients(0, 0, tiles // 2)
    from_inside(3)
    collect.corner_step(order[2])
    give_gradients(0, tiles // 2, tiles)
    collect.plane_step(order[2])
    from_ends(2)
    give_gradients(1, 0, tiles)
    from_inside(2)
    keep_gradients(0, 0, tiles // 2)
    from_inside(1)
    keep_gradients(0, tiles // 2, tiles)
    keep_gradients(1, 0, tiles)
    collect.own_step()
    total[...] = collect.mine[0, col]

    for index in range(15):
        give_inner(index).wait_send()
        step = index + 1
        from_row, from_col = (row + 4 - step // 4) % 4, (col + 4 - step % 4) % 4
        arrived(inner_in.at[from_row, from_col], inner_recv.at[from_row, from_col])
    for copy in stores(turn_order[3]):
        copy.wait()
    for kind in range(2):
        for slot in range(2):
            give(kind, tiles - 2 + slot, slot).wait_send()
        for slot in range(2 - kind):
            for copy in sum_stores(kind, tiles - 2 + kind + slot, slot):
                copy.wait()
    spread_x.finish()
    spread_m.finish()
    collect.finish()


def expert_stage(normed, grads_all, mask, halves, others, router, collective_id):
    rows, width = normed.shape
    half = halves[0].shape[1]
    tokens = 16 * rows
    tile = 256
    vmem = pl.BlockSpec(memory_space=pltpu.VMEM)
    hbm = pl.BlockSpec(memory_space=pl.ANY)
    dma = pltpu.SemaphoreType.DMA
    blocks = jax.ShapeDtypeStruct((4, 4, rows, width), BF16)
    got = pl.pallas_call(
        expert_kernel,
        in_specs=[hbm] * 9 + [vmem],
        out_specs=[hbm] * 2 + [vmem] * 2 + [hbm] * 5,
        out_shape=[
            jax.ShapeDtypeStruct((tokens, width), BF16),
            blocks,
            jax.ShapeDtypeStruct((rows, width), BF16),
            jax.ShapeDtypeStruct((4, 4, 8, rows), F32),
            jax.ShapeDtypeStruct((width, half), BF16),
            jax.ShapeDtypeStruct((width, half), BF16),
            jax.ShapeDtypeStruct((half, width), BF16),
            jax.ShapeDtypeStruct((2 * half, width), BF16),
            jax.ShapeDtypeStruct((half, width), BF16),
        ],
        scratch_shapes=[
            pltpu.VMEM((width, 2 * half), BF16),
            pltpu.VMEM((width, 2 * half), BF16),
            pltpu.VMEM((2 * half, width), BF16),
            pltpu.VMEM((4, 4) + mask.shape, F32),
            pltpu.VMEM((4 * rows, width), BF16),
            pltpu.VMEM((4 * rows, width), BF16),
            pltpu.VMEM((2, 2 * half, tokens), BF16),
            pltpu.VMEM((2 * half, tokens), BF16),
            pltpu.VMEM((4 * rows, 2 * half), BF16),
            pltpu.VMEM((4 * rows, 2 * half), BF16),
            pltpu.VMEM((4 * rows, 2 * half), BF16),
            pltpu.VMEM((4 * rows, width), BF16),
            pltpu.VMEM((4, 4, 8, rows), F32),
            pltpu.VMEM((2, 2, tile, half), BF16),
            pltpu.VMEM((half, tile), BF16),
        ]
        + collect_buffers(rows, width)
        + COLLECT_SEMS
        + [
            dma((8,)), dma((4, 2)), dma((4,)),
            dma((2,)), dma((2, 2)), dma((2, width // tile)), dma((2, 2)), dma((2, 3)),
            dma((15,)), dma((4, 4)),
        ]
        + SPREAD_SEMS * 2,
        compiler_params=pltpu.CompilerParams(
            collective_id=collective_id, has_side_effects=True, vmem_limit_bytes=61 * 2**20
        ),
        cost_estimate=pl.CostEstimate(
            flops=18 * 2 * tokens * width * half,
            bytes_accessed=2**26,
            transcendentals=2 * tokens * half,
        ),
    )(normed, grads_all, mask, *halves, *others, router.T)
    return got[1], got[2], got[3], got[4:7]


def project_kernel(
    hidden, all_gains, weights, cosine, sine,
    normed_out, weights_out, qkv_out, totals, query, keys, values,
    normed, all_weights, qkv, out_sem,
    heads, stat, scale_q, scale_k, kept_sem, kept_kv_sem,
    stat_send, stat_recv, head_send, head_recv, pair_send, pair_recv, *sems,
):
    here = Here()
    row, col, core = here.row, here.col, here.core
    count = len(SPREAD_SEMS)
    rows, width = hidden.shape
    depth = weights.shape[0]
    part = depth // 2

    def weight_block(of_row, unused_place, of_core):
        return all_weights.at[pl.ds(pl.multiple_of(of_row * depth + of_core * part, part), part)]

    def normed_block(unused_row, place, unused_core):
        return normed.at[pl.ds(pl.multiple_of(place * rows, rows), rows)]

    own_weight = weights.at[pl.ds(pl.multiple_of(core * part, part), part)]
    spread_w = Spread(here, own_weight, weight_block, part, sems[:count], line=False)
    spread_n = Spread(
        here, normed_block(row, col, core), normed_block, rows, sems[count:], plane=False
    )
    greet(here.plane_peers() + here.line_peers() + [here.other_core()])
    spread_w.step(0)
    keep = pltpu.make_async_copy(own_weight, weight_block(row, 0, core), kept_sem)
    keep.start()

    values_in = hidden[...].astype(F32)
    scale_one = lax.rsqrt(jnp.mean(values_in * values_in, axis=1, keepdims=True) + EPSILON)
    own_rows = pl.ds(pl.multiple_of(col * rows, rows), rows)
    normed[own_rows] = (values_in * scale_one * all_gains[0:1]).astype(BF16)
    spread_n.step(0)
    spread_w.step(1)
    spread_n.step(1)
    spread_w.step(2)
    spread_n.step(2)
    spread_n.step(3)
    keep.wait()
    for which in range(4):
        spread_w.core_arrived(which, 0)
    puts = [
        pltpu.make_async_copy(source, target, out_sem.at[index])
        for index, (source, target) in enumerate(
            ((normed, normed_out), (all_weights, weights_out), (qkv, qkv_out))
        )
    ]
    puts[0].start()
    puts[1].start()
    columns = 256

    @pl.loop(0, qkv.shape[1] // columns)
    def _(index):
        at = pl.ds(pl.multiple_of(index * columns, columns), columns)
        qkv[:, at] = matmul(normed[...], all_weights[:, at])

    puts[2].start()

    plane = qkv.shape[1] // (3 * HD)
    for kind in range(2):
        square = jnp.zeros((qkv.shape[0], HD), F32)
        for head in range(plane):
            start = (head * 3 + kind) * HD
            raw = qkv[:, start : start + HD]
            square = square + raw * raw
        stat[col, kind : kind + 1] = jnp.sum(square.T, axis=0, keepdims=True)

    def give_stat(step):
        peer = here.line_peers()[step]
        return remote(stat.at[col], stat.at[col], stat_send.at[step], stat_recv.at[col], peer)

    for step in range(3):
        give_stat(step).start()
    for step in range(3):
        place = (col + step + 1) % 4
        arrived(stat.at[place], stat_recv.at[place])
    total = stat[0] + stat[1] + stat[2] + stat[3]
    totals[...] = total
    for kind, target in enumerate((scale_q, scale_k)):
        line = lax.rsqrt(total[kind : kind + 1] / width + EPSILON)
        target[...] = jnp.broadcast_to(line, (HD, line.shape[1])).T

    chunk = 64

    @pl.loop(0, qkv.shape[0] // chunk)
    def _(index):
        at = pl.ds(pl.multiple_of(index * chunk, chunk), chunk)
        for head in range(plane):
            place = pl.ds(pl.multiple_of((col * plane + head) * HD, HD), HD)
            for kind, scales in enumerate((scale_q, scale_k)):
                raw = qkv[at, pl.ds((head * 3 + kind) * HD, HD)]
                unit = raw * scales[at] * all_gains[kind + 1 : kind + 2, place]
                turned = pltpu.roll(unit, HD // 2, 1)
                heads[head, kind, at] = (unit * cosine[at] + turned * sine[at]).astype(BF16)
            heads[head, 2, at] = qkv[at, pl.ds((head * 3 + 2) * HD, HD)].astype(BF16)

    targets = (query.at[row], keys.at[1, row], values.at[1, row])

    def give_head(step, kind):
        dest = here.rows[step + 1]
        sems = head_send.at[step, kind], head_recv.at[kind, row]
        return remote(heads.at[dest, kind], targets[kind], *sems, here.at_row(dest))

    for kind in (1, 2, 0):
        for step in range(3):
            give_head(step, kind).start()

    def give_pair(source, kind):
        array = (keys, values)[kind]
        sems = pair_send.at[kind, source], pair_recv.at[kind, source]
        return remote(array.at[1, source], array.at[0, source], *sems, here.other_core())

    def keep_pair(source, kind):
        array = (keys, values)[kind]
        return pltpu.make_async_copy(
            array.at[1, source], array.at[0, source], kept_kv_sem.at[kind, source]
        )

    def pair_from(source):
        @pl.when(core == 0)
        def _():
            for kind in range(2):
                give_pair(source, kind).start()
                keep_pair(source, kind).start()

    for kind, array in ((1, keys), (2, values)):
        array[1, row] = heads[row, kind]
    query[row] = heads[row, 0]
    pair_from(row)
    for source in here.rows[1:]:
        arrived(keys.at[1, source], head_recv.at[1, source])
        arrived(values.at[1, source], head_recv.at[2, source])
        pair_from(source)
    for source in here.rows[1:]:
        arrived(query.at[source], head_recv.at[0, source])

    @pl.when(core == 0)
    def _():
        for source in range(4):
            for kind in range(2):
                give_pair(source, kind).wait_send()
                keep_pair(source, kind).wait()

    @pl.when(core == 1)
    def _():
        for source in range(4):
            for kind in range(2):
                give_pair(source, kind).wait_recv()

    for step in range(3):
        give_stat(step).wait_send()
        for kind in range(3):
            give_head(step, kind).wait_send()
    for put in puts:
        put.wait()
    spread_w.finish(arrivals=False)
    spread_n.finish()


def project(hidden, gains, weights, cosine, sine, collective_id):
    rows, width = hidden.shape
    depth, columns = weights.shape
    row_tok = 4 * rows
    plane = columns // (3 * HD)
    vmem = pl.BlockSpec(memory_space=pltpu.VMEM)
    hbm = pl.BlockSpec(memory_space=pl.ANY)
    return pl.pallas_call(
        project_kernel,
        in_specs=[vmem, vmem, hbm, vmem, vmem],
        out_specs=[hbm] * 3 + [vmem] * 4,
        out_shape=[
            jax.ShapeDtypeStruct((row_tok, width), BF16),
            jax.ShapeDtypeStruct((4 * depth, columns), BF16),
            jax.ShapeDtypeStruct((row_tok, columns), F32),
            jax.ShapeDtypeStruct((8, row_tok), F32),
            jax.ShapeDtypeStruct((4, row_tok, HD), BF16),
            jax.ShapeDtypeStruct((2, 4, row_tok, HD), BF16),
            jax.ShapeDtypeStruct((2, 4, row_tok, HD), BF16),
        ],
        scratch_shapes=[
            pltpu.VMEM((row_tok, width), BF16),
            pltpu.VMEM((4 * depth, columns), BF16),
            pltpu.VMEM((row_tok, columns), F32),
            pltpu.SemaphoreType.DMA((3,)),
            pltpu.VMEM((plane, 3, row_tok, HD), BF16),
            pltpu.VMEM((4, 8, row_tok), F32),
            pltpu.VMEM((row_tok, HD), F32),
            pltpu.VMEM((row_tok, HD), F32),
            pltpu.SemaphoreType.DMA,
            pltpu.SemaphoreType.DMA((2, 4)),
            pltpu.SemaphoreType.DMA((3,)),
            pltpu.SemaphoreType.DMA((4,)),
            pltpu.SemaphoreType.DMA((3, 3)),
            pltpu.SemaphoreType.DMA((3, 4)),
            pltpu.SemaphoreType.DMA((2, 4)),
            pltpu.SemaphoreType.DMA((2, 4)),
        ]
        + SPREAD_SEMS * 2,
        compiler_params=pltpu.CompilerParams(
            collective_id=collective_id, has_side_effects=True, vmem_limit_bytes=56 * 2**20
        ),
    )(hidden, gains, weights, cosine, sine)


def attention_kernel(
    scale, cuts, query, keys, values, out_weights, hidden, all_gains,
    mixed, total, whole_out, mixed_rows, middle, normed,
    all_out, put_sem, values_t, top, summed, acc, mixed_low, mixed_tok, kept_sem,
    row_send, row_recv, token_send, token_recv, *sems,
):
    here = Here()
    row, col, core = here.row, here.col, here.core
    rows = hidden.shape[0]
    row_tok = 4 * rows
    group_tok = 4 * row_tok
    side = out_weights.shape[0]

    def out_block(of_row, place, of_core):
        start = pl.multiple_of(place * side + of_core * (side // 2), side // 2)
        return all_out.at[pl.ds(start, side // 2), pl.ds(pl.multiple_of(of_row * side, side), side)]

    own_out = out_weights.at[pl.ds(pl.multiple_of(core * (side // 2), side // 2), side // 2)]
    spread = Spread(here, own_out, out_block, side // 2, sems)
    keep = pltpu.make_async_copy(own_out, out_block(row, col, core), kept_sem)
    keep.start()
    values_t[...] = values[...].T
    greet(here.plane_peers() + here.line_peers() + [here.other_core()])
    spread.step(0)
    cut = (cuts[0, 0], cuts[0, 1])
    last_query = 2 * group_tok - row_tok

    def queries(index):
        at = pl.ds(index * row_tok, row_tok)
        first_query = core * group_tok + index * row_tok
        top[...] = jnp.full_like(top, MASKED)
        summed[...] = jnp.zeros_like(summed)
        acc[...] = jnp.zeros_like(acc)

        def block_fn(part, scores):
            old = top[...]
            new = jnp.maximum(old, jnp.max(scores, axis=0, keepdims=True))
            weight = jnp.exp(scores - new)
            decay = jnp.exp(old - new)
            top[...] = new
            summed[...] = summed[...] * decay + jnp.sum(weight, axis=0, keepdims=True)
            acc[...] = acc[...] * decay + matmul(values_t[:, part], weight.astype(BF16))

        def scan(block, carry):
            first_key = block * row_tok
            part = pl.ds(pl.multiple_of(first_key, row_tok), row_tok)
            masked = (block == 0) | (first_key == first_query) | (first_query == last_query)

            @pl.when(jnp.logical_not(masked))
            def _():
                block_fn(part, contract_cols(keys[part], query[at]) * scale)

            @pl.when(masked)
            def _():
                key_place = first_key + lax.broadcasted_iota(jnp.int32, (row_tok, row_tok), 0)
                place = first_query + lax.broadcasted_iota(jnp.int32, (1, row_tok), 1)
                allowed = (key_place <= place) & (key_place >= doc_start(place, cut))
                scores = contract_cols(keys[part], query[at]) * scale
                block_fn(part, jnp.where(allowed, scores, MASKED))

            return carry

        lax.fori_loop(0, core * 4 + index + 1, scan, 0)
        got = (acc[...] / summed[...]).T
        mixed[at] = got
        mixed_low[index] = got.astype(BF16)
        total[:, at] = top[...] + jnp.log(summed[...])

        @pl.when(row != index)
        def _():
            give_row(index).start()

        @pl.when(row == index)
        def _():
            mixed_rows[row] = mixed_low[index]

    def give_row(index):
        sems_of = row_send.at[index], row_recv.at[row]
        return remote(mixed_low.at[index], mixed_rows.at[row], *sems_of, here.at_row(index))

    def give_token(step):
        place = (col + step) % 4
        part = pl.ds(pl.multiple_of(place * rows, rows), rows)
        sems_of = token_send.at[step], token_recv.at[col]
        return remote(mixed_rows.at[:, part], mixed_tok.at[col], *sems_of, here.at_col(place))

    for index in range(4):
        queries(index)
        spread.step(index + 1)
    for source in here.rows[1:]:
        arrived(mixed_rows.at[source], row_recv.at[source])
    for step in range(1, 4):
        give_token(step).start()
    mixed_tok[col] = mixed_rows[:, pl.ds(pl.multiple_of(col * rows, rows), rows)]
    spread.step(5)
    keep.wait()
    spread.finish()
    put = pltpu.make_async_copy(all_out, whole_out, put_sem)
    put.start()
    for step in range(1, 4):
        place = (col + 4 - step) % 4
        arrived(mixed_tok.at[place], token_recv.at[place])
    own = jnp.concatenate([mixed_tok[place, head] for place in range(4) for head in range(4)], axis=1)
    tile = 512

    @pl.loop(0, all_out.shape[1] // tile)
    def _(index):
        at = pl.ds(pl.multiple_of(index * tile, tile), tile)
        middle[:, at] = hidden[:, at].astype(F32) + matmul(own, all_out[:, at])

    values_in = middle[...]
    root = lax.rsqrt(jnp.mean(values_in * values_in, axis=1, keepdims=True) + EPSILON)
    normed[...] = (values_in * root * all_gains[3:4]).astype(BF16)
    put.wait()
    for index in range(4):

        @pl.when(row != index)
        def _():
            give_row(index).wait_send()

    for step in range(1, 4):
        give_token(step).wait_send()


def attention_stage(query, keys, values, cuts, out_weights, hidden, gains, scale, collective_id):
    rows, width = hidden.shape
    row_tok, group_tok = 4 * rows, 16 * rows
    vmem, hbm = pl.BlockSpec(memory_space=pltpu.VMEM), pl.BlockSpec(memory_space=pl.ANY)
    dma = pltpu.SemaphoreType.DMA
    return pl.pallas_call(
        functools.partial(attention_kernel, scale),
        in_specs=[pl.BlockSpec(memory_space=pltpu.SMEM)] + [vmem] * 3 + [hbm] + [vmem] * 2,
        out_specs=[vmem] * 2 + [hbm] + [vmem] * 3,
        out_shape=[
            jax.ShapeDtypeStruct((group_tok, HD), F32),
            jax.ShapeDtypeStruct((1, group_tok), F32),
            jax.ShapeDtypeStruct((width, width), BF16),
            jax.ShapeDtypeStruct((4, row_tok, HD), BF16),
            jax.ShapeDtypeStruct((rows, width), F32),
            jax.ShapeDtypeStruct((rows, width), BF16),
        ],
        scratch_shapes=[
            pltpu.VMEM((width, width), BF16),
            dma,
            pltpu.VMEM((HD, 2 * group_tok), BF16),
            pltpu.VMEM((1, row_tok), F32),
            pltpu.VMEM((1, row_tok), F32),
            pltpu.VMEM((HD, row_tok), F32),
            pltpu.VMEM((4, row_tok, HD), BF16),
            pltpu.VMEM((4, 4, rows, HD), BF16),
            dma, dma((4,)), dma((4,)), dma((4,)), dma((4,)),
        ]
        + SPREAD_SEMS,
        compiler_params=pltpu.CompilerParams(
            collective_id=collective_id, has_side_effects=True, vmem_limit_bytes=40 * 2**20
        ),
    )(cuts, query, keys, values, out_weights, hidden, gains)


class PairSum:
    def __init__(self, here, values, out, held, got, send, recv):
        self.here, self.values, self.out, self.held, self.got = here, values, out, held, got
        self.send, self.recv = send, recv
        col, half = here.col, values.shape[1] // 2
        self.own = pl.ds(pl.multiple_of(here.core * half, half), half)
        self.others = pl.ds(pl.multiple_of((1 - here.core) * half, half), half)
        self.peers = [
            here.at_row(here.across),
            here.at_row(here.along),
            here.at_col(col + 1 - 2 * (col % 2)),
            here.at_col((col + 2) % 4),
        ]

    def copy(self, step):
        here, sems = self.here, (self.send.at[step], self.recv.at[step])
        if step == 0:
            return remote(self.values.at[:, self.others], self.got.at[0], *sems, here.other_core())
        if step == 5:
            return remote(self.held.at[4], self.out.at[:, self.own], *sems, here.other_core())
        return remote(self.held.at[step - 1], self.got.at[step], *sems, self.peers[step - 1])

    def begin(self):
        self.copy(0).start()

    def step(self, index):
        if index == 5:
            arrived(self.out.at[:, self.others], self.recv.at[5])
            return
        self.copy(index).wait_recv()
        before = self.values[:, self.own] if index == 0 else self.held[index - 1]
        self.held[index] = before + self.got[index]
        if index == 4:
            self.out[:, self.own] = self.held[4]
        self.copy(index + 1).start()

    def finish(self):
        for index in range(6):
            self.copy(index).wait_send()


def pair_sum_buffers(rows, width):
    return [
        pltpu.VMEM((5, rows, width // 2), F32),
        pltpu.VMEM((5, rows, width // 2), F32),
        pltpu.SemaphoreType.DMA((6,)),
        pltpu.SemaphoreType.DMA((6,)),
    ]


def back_kernel(
    scale, cuts, d_attn, query, keys, values, mixed, total, out_weights, out_parts, early,
    d_attn_row, d_heads, out_total, early_sum,
    weights, d_mixed_give, d_mixed_row, d_mixed, keys_t, d_keys, d_values, acc, pair_out, pair_in,
    head_give, sum_held, sum_got, sum_send, sum_recv, weight_sem, load_sem,
    near_send, near_recv, head_send, head_recv, back_send, back_recv,
    pair_send, pair_recv, *rest,
):
    here = Here()
    row, col, core = here.row, here.col, here.core
    rows = d_attn.shape[0]
    row_tok = 4 * rows
    group_tok = 4 * row_tok
    plane = 4 * HD
    order = here.near_first[::-1]
    collect = Collect(here, rest[:6], rest[6 : 6 + len(COLLECT_SEMS)])
    sems = rest[6 + len(COLLECT_SEMS) :]

    def row_block(unused_row, place, unused_core):
        return d_attn_row.at[pl.ds(pl.multiple_of(place * rows, rows), rows)]

    spread = Spread(here, row_block(row, col, core), row_block, rows, sems, plane=False)
    pair_sum = PairSum(here, early, early_sum, sum_held, sum_got, sum_send, sum_recv)

    def load(which, place):
        return pltpu.make_async_copy(
            out_parts.at[which, place], collect.mine.at[which, place], load_sem.at[which, place]
        )

    load_weights = pltpu.make_async_copy(out_weights, weights, weight_sem)
    load_weights.start()
    for place in order:
        for which in (3, 2, 1, 0):
            load(which, place).start()
    keys_t[...] = keys[...].T
    d_attn_row[pl.ds(pl.multiple_of(col * rows, rows), rows)] = d_attn[...]
    greet(here.plane_peers() + here.line_peers() + [here.other_core()])

    def give_near(step):
        place = (col + step) % 4
        sems_of = near_send.at[step], near_recv.at[col]
        return remote(d_mixed_give.at[place], d_mixed_row.at[col], *sems_of, here.at_col(place))

    def give_head(step):
        dest = here.rows[step]
        part = pl.ds(pl.multiple_of(dest * HD, HD), HD)
        sems_of = head_send.at[step], head_recv.at[row]
        return remote(d_mixed_row.at[:, :, part], d_mixed.at[row], *sems_of, here.at_row(dest))

    def start(index):
        for which in (3, 2, 1):
            load(which, order[index]).wait()
        collect.start_far(order[index])
        collect.start_near(order[index])

    ends = (col == 0) | (col == 3)

    def from_ends(index):
        @pl.when(ends)
        def _():
            collect.line_step(order[index])

    def from_inside(index):
        @pl.when(jnp.logical_not(ends))
        def _():
            collect.line_step(order[index])

    def plane_part(index):
        load(0, order[index]).wait()
        collect.plane_step(order[index])

    start(0)
    pair_sum.begin()
    load_weights.wait()
    for step in (1, 2, 3, 0):
        place = (col + step) % 4
        part = pl.ds(pl.multiple_of(place * plane, plane), plane)
        product = contract_cols(d_attn[...], weights[part]).astype(BF16)
        if step == 0:
            d_mixed_row[col] = product
        else:
            d_mixed_give[place] = product
            give_near(step).start()
    spread.step(0)
    pair_sum.step(0)
    d_keys[...] = jnp.zeros_like(d_keys)
    d_values[...] = jnp.zeros_like(d_values)
    for step in range(1, 4):
        place = (col + 4 - step) % 4
        arrived(d_mixed_row.at[place], near_recv.at[place])
    for step in range(1, 4):
        give_head(step).start()
    d_mixed[row] = d_mixed_row[:, :, pl.ds(pl.multiple_of(row * HD, HD), HD)]
    collect.corner_step(order[0])
    pair_sum.step(1)
    spread.step(1)
    for source in here.rows[1:]:
        arrived(d_mixed.at[source], head_recv.at[source])
    start(1)

    cut = (cuts[0, 0], cuts[0, 1])
    last_query = 2 * group_tok - row_tok

    def queries(index):
        at = pl.ds(index * row_tok, row_tok)
        first_query = core * group_tok + index * row_tok
        gradient = d_mixed[index].reshape(row_tok, HD)
        delta = jnp.sum((gradient.astype(F32) * mixed[at]).T, axis=0, keepdims=True)
        sums = total[:, at]
        acc[...] = jnp.zeros_like(acc)

        def block_fn(part, scores):
            weight = jnp.exp(scores - sums)
            d_weight = contract_cols(values[part], gradient)
            d_scores = (weight * (d_weight - delta)).astype(BF16)
            d_values[part] += matmul(weight.astype(BF16), gradient)
            d_keys[part] += matmul(d_scores, query[at]) * scale
            acc[...] += matmul(keys_t[:, part], d_scores)

        def scan(block, carry):
            first_key = block * row_tok
            part = pl.ds(pl.multiple_of(first_key, row_tok), row_tok)
            masked = (block == 0) | (first_key == first_query) | (first_query == last_query)

            @pl.when(jnp.logical_not(masked))
            def _():
                block_fn(part, contract_cols(keys[part], query[at]) * scale)

            @pl.when(masked)
            def _():
                key_place = first_key + lax.broadcasted_iota(jnp.int32, (row_tok, row_tok), 0)
                place = first_query + lax.broadcasted_iota(jnp.int32, (1, row_tok), 1)
                allowed = (key_place <= place) & (key_place >= doc_start(place, cut))
                scores = contract_cols(keys[part], query[at]) * scale
                block_fn(part, jnp.where(allowed, scores, MASKED))

            return carry

        lax.fori_loop(0, core * 4 + index + 1, scan, 0)
        head_give[0, index] = (acc[...] * scale).T.astype(BF16)

    queries(0)
    plane_part(0)
    from_ends(0)
    collect.corner_step(order[1])
    start(2)
    spread.step(2)
    queries(1)
    from_inside(0)
    plane_part(1)
    from_ends(1)
    collect.corner_step(order[2])
    start(3)
    pair_sum.step(2)
    queries(2)
    from_inside(1)
    plane_part(2)
    from_ends(2)
    collect.corner_step(order[3])
    spread.step(3)
    queries(3)

    def give_back(step, kind):
        dest = here.rows[step]
        sems_of = back_send.at[step, kind], back_recv.at[kind, row]
        return remote(head_give.at[kind, dest], d_heads.at[row, kind], *sems_of, here.at_row(dest))

    def give_pair(kind):
        sems_of = pair_send.at[kind], pair_recv.at[kind]
        return remote(pair_out.at[kind], pair_in.at[kind], *sems_of, here.other_core())

    for step in range(1, 4):
        give_back(step, 0).start()
    d_heads[row, 0] = head_give[0, row]

    @pl.when(core == 1)
    def _():
        for kind, gradient in enumerate((d_keys, d_values)):
            pair_out[kind] = gradient[pl.ds(0, group_tok)].astype(BF16)
            give_pair(kind).start()
        for kind, gradient in enumerate((d_keys, d_values)):
            for part in range(4):
                at = pl.ds(group_tok + part * row_tok, row_tok)
                head_give[kind + 1, part] = gradient[at].astype(BF16)

    from_inside(2)
    plane_part(3)
    pair_sum.step(3)

    @pl.when(core == 0)
    def _():
        for kind, gradient in enumerate((d_keys, d_values)):
            give_pair(kind).wait_recv()
            for part in range(4):
                at = pl.ds(part * row_tok, row_tok)
                summed = gradient[at] + pair_in[kind, at].astype(F32)
                head_give[kind + 1, part] = summed.astype(BF16)

    for kind in (1, 2):
        for step in range(1, 4):
            give_back(step, kind).start()
        d_heads[row, kind] = head_give[kind, row]
    pair_sum.step(4)
    pair_sum.step(5)
    collect.own_step()
    out_total[...] = collect.mine[0, col]
    for source in here.rows[1:]:
        for kind in range(3):
            arrived(d_heads.at[source, kind], back_recv.at[kind, source])
    for step in range(1, 4):
        give_near(step).wait_send()
        give_head(step).wait_send()
        for kind in range(3):
            give_back(step, kind).wait_send()

    @pl.when(core == 1)
    def _():
        for kind in range(2):
            give_pair(kind).wait_send()

    pair_sum.finish()
    spread.finish()
    collect.finish()


def attend_back_stage(
    d_attn, query, keys, values, mixed, total, cuts, out_weights, out_parts, early, scale, collective_id
):
    rows, width = d_attn.shape
    row_tok, group_tok = 4 * rows, 16 * rows
    vmem, hbm = pl.BlockSpec(memory_space=pltpu.VMEM), pl.BlockSpec(memory_space=pl.ANY)
    dma = pltpu.SemaphoreType.DMA
    return pl.pallas_call(
        functools.partial(back_kernel, scale),
        in_specs=[pl.BlockSpec(memory_space=pltpu.SMEM)] + [vmem] * 6 + [hbm] * 2 + [vmem],
        out_specs=[vmem] * 4,
        out_shape=[
            jax.ShapeDtypeStruct((row_tok, width), BF16),
            jax.ShapeDtypeStruct((4, 3, row_tok, HD), BF16),
            jax.ShapeDtypeStruct((rows, width), BF16),
            jax.ShapeDtypeStruct(early.shape, F32),
        ],
        scratch_shapes=[
            pltpu.VMEM((width, width), BF16),
            pltpu.VMEM((4, rows, 4 * HD), BF16),
            pltpu.VMEM((4, rows, 4 * HD), BF16),
            pltpu.VMEM((4, 4, rows, HD), BF16),
            pltpu.VMEM((HD, 2 * group_tok), BF16),
            pltpu.VMEM((2 * group_tok, HD), F32),
            pltpu.VMEM((2 * group_tok, HD), F32),
            pltpu.VMEM((HD, row_tok), F32),
            pltpu.VMEM((2, group_tok, HD), BF16),
            pltpu.VMEM((2, group_tok, HD), BF16),
            pltpu.VMEM((3, 4, row_tok, HD), BF16),
        ]
        + pair_sum_buffers(*early.shape)
        + [
            dma, dma((4, 4)), dma((4,)), dma((4,)), dma((4,)), dma((4,)),
            dma((4, 3)), dma((3, 4)), dma((2,)), dma((2,)),
        ]
        + collect_buffers(rows, width)
        + COLLECT_SEMS
        + SPREAD_SEMS,
        compiler_params=pltpu.CompilerParams(
            collective_id=collective_id, has_side_effects=True, vmem_limit_bytes=58 * 2**20
        ),
    )(cuts, d_attn, query, keys, values, mixed, total, out_weights, out_parts, early)


def tail_kernel(
    d_heads, qkv, totals, all_gains, cosine, sine, weights_in, normed_in, mixed_rows, d_attn_in,
    hidden,
    grad_hidden, grads, late_sum, last_sum,
    weights, normed, d_attn, in_sem, last, last_got, last_send, last_recv, hop, hop_got, hop_send, hop_recv,
    d_qkv, late, mixed, units, stat, scales, sums, sum_held, sum_got, sum_send, sum_recv,
    stat_send, stat_recv,
    line, line_in, whole, give, other, plane, corner_one, corner_two, from_across, from_along,
    up_send, down_send, line_recv, other_send, other_recv,
    one_send, one_recv, two_send, two_recv, across_send, across_recv, along_send, along_recv,
    back_send, back_recv,
):
    here = Here()
    row, col, core = here.row, here.col, here.core
    rows = hidden.shape[0]
    depth, columns = grads.shape
    part = depth // 2
    first, second = pl.ds(0, part // 2), pl.ds(part // 2, part // 2)
    order = here.near_first[::-1]
    qkv_columns = d_qkv.shape[1]
    tile = 512

    def line_products():
        @pl.loop(0, weights.shape[0] // tile)
        def _(index):
            at = pl.ds(pl.multiple_of(index * tile, tile), tile)
            product = contract_cols(d_qkv[...], weights[at]).astype(BF16)
            line[:, :, at] = product.reshape(4, rows, tile)

    line_halves = (pl.ds(0, rows // 2), pl.ds(rows // 2, rows // 2))

    def give_up(place, half):
        at = line_halves[half]
        sems = up_send.at[half, place], line_recv.at[half, place]
        return remote(line.at[place, at], line_in.at[place, at], *sems, here.at_col(col + 1))

    def give_down(place, slot, half):
        at = line_halves[half]
        sems = down_send.at[half, place], line_recv.at[half, slot]
        return remote(line.at[place, at], line_in.at[slot, at], *sems, here.at_col(col - 1))

    def add_line(place, slot, half):
        at = line_halves[half]
        arrived(line_in.at[slot, at], line_recv.at[half, slot])
        add_into(line.at[place, at], line_in.at[slot, at])

    def line_step(place):
        for half in range(2):

            @pl.when(((place > col) & (col > 0)) | ((place < col) & (col < 3)))
            def _():
                add_line(place, place, half)

            @pl.when(place > col)
            def _():
                give_up(place, half).start()

            @pl.when(place < col - 1)
            def _():
                give_down(place, place, half).start()

            @pl.when(place == col - 1)
            def _():
                give_down(place, 4, half).start()

    def row_product(which):
        of_row = here.rows[which]
        at = pl.ds(pl.multiple_of(of_row * depth, depth), depth)
        whole[:, pl.ds(0, qkv_columns)] = transposed_product(normed[:, at], d_qkv[...]).astype(BF16)
        whole[:, pl.ds(qkv_columns, columns - qkv_columns)] = transposed_product(
            mixed[...], d_attn[:, at]
        ).astype(BF16)
        plane[which] = whole[pl.ds(pl.multiple_of(core * part, part), part)]
        give[which] = whole[pl.ds(pl.multiple_of((1 - core) * part, part), part)]
        to_core(which).start()

    def to_core(which):
        sems = other_send.at[which], other_recv.at[which]
        return remote(give.at[which], other.at[which], *sems, here.other_core())

    def own_sum(which):
        to_core(which).wait_recv()
        add_into(plane.at[which], other.at[which])

    give_one = remote(
        plane.at[3, first], corner_one, one_send, one_recv, here.at_row(here.across)
    )
    give_two = remote(
        plane.at[3, second], corner_two, two_send, two_recv, here.at_row(here.along)
    )

    def give_across(index):
        at = (first, second)[index]
        sems = across_send.at[index], across_recv.at[index]
        return remote(plane.at[1, at], from_across.at[at], *sems, here.at_row(here.across))

    def give_along(index):
        at = (first, second)[index]
        sems = along_send.at[index], along_recv.at[index]
        return remote(plane.at[2, at], from_along.at[at], *sems, here.at_row(here.along))

    pair_sum = PairSum(here, late, late_sum, sum_held, sum_got, sum_send, sum_recv)
    takes = [
        pltpu.make_async_copy(source, target, in_sem.at[index])
        for index, (source, target) in enumerate(
            ((weights_in, weights), (normed_in, normed), (d_attn_in, d_attn))
        )
    ]
    for take in takes:
        take.start()
    near = [(step // 2, step % 2) for step in range(1, 8)]

    def near_device(step):
        which, swap = near[step]
        return (here.rows[which], col, (core + swap) % 2)

    greet([near_device(step) for step in range(7)] + here.line_peers())

    width = hidden.shape[1]
    heads = d_heads.shape[0]
    row_tok = d_qkv.shape[0]
    late[...] = jnp.zeros_like(late)
    for kind in range(2):
        root = lax.rsqrt(totals[kind : kind + 1] / width + EPSILON)
        scales[kind] = jnp.broadcast_to(root, (HD, row_tok)).T
        square = jnp.zeros((row_tok, HD), F32)
        for head in range(heads):
            start = (head * 3 + kind) * HD
            raw = qkv[:, start : start + HD]
            given = d_heads[head, kind].astype(F32)
            unit = given * cosine[...] + pltpu.roll(given * sine[...], HD // 2, 1)
            place = pl.ds(pl.multiple_of((col * heads + head) * HD, HD), HD)
            gains = all_gains[kind + 1 : kind + 2, place]
            gain_sum = jnp.sum(unit * raw * scales[kind], axis=0, keepdims=True)
            late[kind : kind + 1, place] = gain_sum
            weighted = unit * gains
            square = square + weighted * raw
            units[kind, head] = weighted
        stat[col, kind : kind + 1] = jnp.sum(square.T, axis=0, keepdims=True)

    def give_stat(step):
        peer = here.line_peers()[step]
        return remote(stat.at[col], stat.at[col], stat_send.at[step], stat_recv.at[col], peer)

    for step in range(3):
        give_stat(step).start()
    for head in range(heads):
        d_qkv[:, (head * 3 + 2) * HD : (head * 3 + 3) * HD] = d_heads[head, 2]
        mixed[:, head * HD : (head + 1) * HD] = mixed_rows[head]
    for step in range(3):
        place = (col + step + 1) % 4
        arrived(stat.at[place], stat_recv.at[place])
    total = stat[0] + stat[1] + stat[2] + stat[3]
    for kind in range(2):
        sums[...] = jnp.broadcast_to(total[kind : kind + 1] / width, (HD, row_tok)).T
        for head in range(heads):
            start = (head * 3 + kind) * HD
            raw = qkv[:, start : start + HD]
            root = scales[kind]
            d_raw = root * units[kind, head] - raw * (root * root * root) * sums[...]
            d_qkv[:, start : start + HD] = d_raw.astype(BF16)
    ends = (col == 0) | (col == 3)
    pair_sum.begin()
    for take in takes:
        take.wait()
    line_products()

    @pl.when(ends)
    def _():
        for place in order[:3]:
            line_step(place)

    def inner_step(place):
        @pl.when(jnp.logical_not(ends))
        def _():
            line_step(place)

    row_product(3)
    row_product(1)
    pair_sum.step(0)
    inner_step(order[0])
    own_sum(3)
    give_one.start()
    give_two.start()
    row_product(2)
    pair_sum.step(1)
    own_sum(1)
    give_across(0).start()
    own_sum(2)
    give_along(1).start()
    inner_step(order[1])
    row_product(0)
    pair_sum.step(2)
    inner_step(order[2])
    give_two.wait_recv()
    add_into(plane.at[1, second], corner_two)
    give_across(1).start()
    give_one.wait_recv()
    add_into(plane.at[2, first], corner_one)
    give_along(0).start()
    own_sum(0)

    for half in range(2):

        @pl.when(col > 0)
        def _():
            add_line(col, col, half)

        @pl.when(col < 3)
        def _():
            add_line(col, 4, half)

    given = line[col].astype(F32)
    tokens = hidden[...].astype(F32)
    root = lax.rsqrt(jnp.mean(tokens * tokens, axis=1, keepdims=True) + EPSILON)
    part_sum = jnp.sum(given * tokens * root, axis=0, keepdims=True)
    eighth = width // 8
    me = row * 2 + core
    for index in range(8):
        last[index : index + 1] = part_sum[:, index * eighth : (index + 1) * eighth]

    def give_last(step):
        sems = last_send.at[step], last_recv.at[me]
        return remote(last, last_got.at[me], *sems, near_device(step))

    def give_hop(step):
        sems = hop_send.at[step], hop_recv.at[col]
        return remote(hop, hop_got.at[col], *sems, here.line_peers()[step])

    for step in range(7):
        give_last(step).start()
    last_got[me] = last[...]
    weighted = given * all_gains[0:1]
    inner = jnp.mean(weighted * tokens, axis=1, keepdims=True)
    grad_hidden[...] = root * weighted - tokens * (root * root * root) * inner
    pair_sum.step(3)
    for step in range(7):
        which, swap = near[step]
        source = here.rows[which] * 2 + (core + swap) % 2
        arrived(last_got.at[source], last_recv.at[source])
    held = last_got[0]
    for index in range(1, 8):
        held = held + last_got[index]
    hop[...] = held
    hop_got[col] = held
    for step in range(3):
        give_hop(step).start()
    pair_sum.step(4)
    for index in range(2):
        give_across(index).wait_recv()
        give_along(index).wait_recv()
    add_into(plane.at[0], from_across, from_along)
    own_half = pl.ds(pl.multiple_of(core * part, part), part)
    give_back = remote(
        plane.at[0], grads.at[own_half], back_send, back_recv, here.other_core()
    )
    give_back.start()
    grads[own_half] = plane[0]
    other_half = grads.at[pl.ds(pl.multiple_of((1 - core) * part, part), part)]
    pair_sum.step(5)
    for step in range(3):
        place = (col + step + 1) % 4
        arrived(hop_got.at[place], hop_recv.at[place])
    last_sum[...] = hop_got[0] + hop_got[1] + hop_got[2] + hop_got[3]
    arrived(other_half, back_recv)
    for step in range(7):
        give_last(step).wait_send()
    for step in range(3):
        give_hop(step).wait_send()
    pair_sum.finish()
    for step in range(3):
        give_stat(step).wait_send()
    give_back.wait_send()
    give_one.wait_send()
    give_two.wait_send()
    for index in range(2):
        give_across(index).wait_send()
        give_along(index).wait_send()
    for which in range(4):
        to_core(which).wait_send()
    for place in order:
        for half in range(2):

            @pl.when(place > col)
            def _():
                give_up(place, half).wait_send()

            @pl.when(place < col)
            def _():
                give_down(place, place, half).wait_send()


def tail_stage(
    d_heads, qkv, totals, gains, cosine, sine, weights, normed, mixed_rows, d_attn, hidden, collective_id
):
    row_tok, qkv_columns = qkv.shape
    rows, width = hidden.shape
    depth = width // 4
    out_columns = width // 4
    columns = qkv_columns + out_columns
    part = depth // 2
    heads = d_heads.shape[0]
    vmem, hbm = pl.BlockSpec(memory_space=pltpu.VMEM), pl.BlockSpec(memory_space=pl.ANY)
    dma = pltpu.SemaphoreType.DMA
    eighth = (8, width // 8)
    one, four = pltpu.SemaphoreType.DMA, pltpu.SemaphoreType.DMA((4,))
    two = pltpu.SemaphoreType.DMA((2,))
    three = pltpu.SemaphoreType.DMA((3,))
    return pl.pallas_call(
        tail_kernel,
        in_specs=[vmem] * 6 + [hbm] * 2 + [vmem, hbm, vmem],
        out_specs=[vmem] * 4,
        out_shape=[
            jax.ShapeDtypeStruct((rows, width), F32),
            jax.ShapeDtypeStruct((depth, columns), BF16),
            jax.ShapeDtypeStruct((8, width), F32),
            jax.ShapeDtypeStruct(eighth, F32),
        ],
        scratch_shapes=[
            pltpu.VMEM(weights.shape, BF16),
            pltpu.VMEM(normed.shape, BF16),
            pltpu.VMEM(d_attn.shape, BF16),
            dma((3,)),
            pltpu.VMEM(eighth, F32),
            pltpu.VMEM((8,) + eighth, F32),
            dma((7,)),
            dma((8,)),
            pltpu.VMEM(eighth, F32),
            pltpu.VMEM((4,) + eighth, F32),
            dma((3,)),
            dma((4,)),
            pltpu.VMEM((row_tok, qkv_columns), BF16),
            pltpu.VMEM((8, width), F32),
            pltpu.VMEM((row_tok, heads * HD), BF16),
            pltpu.VMEM((2, heads, row_tok, HD), F32),
            pltpu.VMEM((4, 8, row_tok), F32),
            pltpu.VMEM((2, row_tok, HD), F32),
            pltpu.VMEM((row_tok, HD), F32),
        ]
        + pair_sum_buffers(8, width)
        + [
            three, four,
            pltpu.VMEM((4, rows, width), BF16),
            pltpu.VMEM((5, rows, width), BF16),
            pltpu.VMEM((depth, columns), BF16),
            pltpu.VMEM((4, part, columns), BF16),
            pltpu.VMEM((4, part, columns), BF16),
            pltpu.VMEM((4, part, columns), BF16),
            pltpu.VMEM((part // 2, columns), BF16),
            pltpu.VMEM((part // 2, columns), BF16),
            pltpu.VMEM((part, columns), BF16),
            pltpu.VMEM((part, columns), BF16),
            dma((2, 4)), dma((2, 4)), dma((2, 5)), four, four,
            one, one, one, one, two, two, two, two,
            one, one,
        ],
        compiler_params=pltpu.CompilerParams(
            collective_id=collective_id, has_side_effects=True, vmem_limit_bytes=58 * 2**20
        ),
    )(
        d_heads, qkv, totals, gains, cosine, sine, weights, normed, mixed_rows, d_attn, hidden
    )


def expert_rows(rows, grads, gate, gate_w, up_w, down_w):
    pre_gate = matmul(rows, gate_w)
    pre_up = matmul(rows, up_w)
    back = contract_cols(grads, down_w)
    sigmoid_gate = jax.nn.sigmoid(pre_gate)
    silu_gate = pre_gate * sigmoid_gate
    hidden = (silu_gate * pre_up).astype(BF16)
    inner = jnp.sum(hidden.astype(F32) * back, axis=-1)
    weighted = (hidden.astype(F32) * gate).astype(BF16)
    d_hid = back * gate
    d_pregate = (d_hid * pre_up * (sigmoid_gate + silu_gate * (1.0 - sigmoid_gate))).astype(BF16)
    d_preup = (d_hid * silu_gate).astype(BF16)
    outputs = matmul(weighted, down_w).astype(BF16)
    d_rows = (contract_cols(d_pregate, gate_w) + contract_cols(d_preup, up_w)).astype(BF16)
    return (
        outputs,
        d_rows,
        inner,
        contract_rows(rows, d_pregate),
        contract_rows(rows, d_preup),
        contract_rows(weighted, grads),
    )


def experts(normed, grads, dense_gates, gate_w, up_w, down_w):
    rows_dev, width = normed.shape
    devices = math.prod(lax.axis_size(axis) for axis in ALL)
    expert_count = dense_gates.shape[1]
    expert = lax.axis_index(ALL) // 2
    parts = max(1, lax.axis_size("exp") // 2)
    step = rows_dev // parts

    def one_part(sums, piece):
        rows, grad_rows, gates = piece
        rows_all = lax.all_gather(rows, ALL, axis=0, tiled=True)
        grads_all = lax.all_gather(grad_rows, ALL, axis=0, tiled=True)
        gates_all = lax.all_gather(gates, ALL, axis=0, tiled=True)
        gate = lax.dynamic_slice_in_dim(gates_all, expert, 1, 1)
        got = expert_rows(rows_all, grads_all, gate, gate_w, up_w, down_w)
        outputs = lax.psum_scatter(got[0], ALL, scatter_dimension=0, tiled=True)
        d_rows = lax.psum_scatter(got[1], ALL, scatter_dimension=0, tiled=True)
        inner = lax.all_to_all(
            got[2].reshape(devices, step), ALL, split_axis=0, concat_axis=0, tiled=True
        )
        inner = inner.reshape(expert_count, 2, step).sum(axis=1).T
        sums = got[3:] if sums is None else tuple(a + b for a, b in zip(sums, got[3:]))
        return sums, (outputs, d_rows, inner)

    if parts == 1:
        sums, (outputs, d_rows, inner) = one_part(None, (normed, grads, dense_gates))
    else:
        start = tuple(jnp.zeros(w.shape, F32) for w in (gate_w, up_w, down_w))
        pieces = tuple(v.reshape(parts, step, -1) for v in (normed, grads, dense_gates))
        sums, got = lax.scan(one_part, start, pieces)
        outputs, d_rows, inner = (v.reshape(rows_dev, -1) for v in got)
    return outputs.astype(F32), d_rows.astype(F32), inner, sums


def experts_here(normed, grads_all, picks, router, halves, others):
    numbers = jnp.arange(router.shape[1], dtype=jnp.int32)
    mask = jnp.any(picks.T[None] == numbers[:, None, None], axis=1).astype(F32)
    out_parts, d_rows, inner, weights = expert_stage(
        normed, grads_all, mask, halves, others, router, 1
    )
    inner = inner[:, :, 0].reshape(router.shape[1], -1).T
    return out_parts, d_rows.astype(F32), inner, weights


def shards(
    hidden_in,
    out_grad,
    attn_gain,
    w_qkv,
    q_gain,
    k_gain,
    w_out,
    moe_gain,
    router,
    w_gate,
    w_up,
    w_down,
    routes,
    doc_cuts,
):
    row_count, col_count = lax.axis_size("row"), lax.axis_size("col")
    tokens = hidden_in[0].astype(F32)
    rows_dev, width = tokens.shape
    heads = w_qkv.shape[1] // (3 * HD)
    plane = heads * HD
    scale = HD ** (-0.5)
    side = lax.axis_index("exp") % 2
    row_tok = rows_dev * col_count
    group_tok = row_tok * row_count
    here = (row_count, col_count, lax.axis_size("exp")) == (4, 4, 2)
    sequence = 0 if here else lax.axis_index("exp") // 2
    cuts = lax.dynamic_index_in_dim(doc_cuts, sequence, 0, keepdims=False)

    if here:
        grads_all = lax.all_gather(out_grad[0], ("row", "col"), axis=0, tiled=True)
        gains = jnp.stack([attn_gain, q_gain, k_gain, moe_gain]).astype(F32)
        other_w = [lax.ppermute(w[0], "exp", [(0, 1), (1, 0)]) for w in (w_gate, w_up, w_down)]

    gain_one = attn_gain.astype(F32)
    scale_one = rms_scale(tokens)
    head_start = lax.axis_index("col") * plane
    gain_q = lax.dynamic_slice_in_dim(q_gain, head_start, plane, 0).astype(F32)
    gain_k = lax.dynamic_slice_in_dim(k_gain, head_start, plane, 0).astype(F32)
    row_places = side * group_tok + lax.axis_index("row") * row_tok + jnp.arange(row_tok, dtype=jnp.int32)
    unused_doc, position = doc_positions(row_places, cuts)
    cosine, sine = rope_tables(position, HD)
    if here:
        signed = jnp.concatenate([-sine[:, : HD // 2], sine[:, HD // 2 :]], axis=1)
        normed_row, qkv_w, qkv, totals, query, keys, values = project(
            hidden_in[0], gains, w_qkv, cosine, signed, 0
        )
        total_q, total_k = totals[0], totals[1]
        query = query.reshape(group_tok, HD)
        key_all, value_all = keys.reshape(-1, HD), values.reshape(-1, HD)
    else:
        normed_one = (tokens * scale_one * gain_one).astype(BF16)
        normed_row = lax.all_gather(normed_one, "col", axis=0, tiled=True)
        qkv_w = lax.all_gather(w_qkv, "row", axis=0, tiled=True)
        out_w = lax.all_gather(
            lax.all_gather(w_out, "row", axis=1, tiled=True), "col", axis=0, tiled=True
        )
        qkv = matmul(normed_row, qkv_w)
    qkv = qkv.reshape(row_tok, heads, 3, HD)
    query_raw, key_raw, value_raw = qkv[:, :, 0], qkv[:, :, 1], qkv[:, :, 2]
    if not here:
        total_q, total_k = lax.psum(
            (jnp.sum(query_raw * query_raw, axis=(1, 2)), jnp.sum(key_raw * key_raw, axis=(1, 2))),
            "col",
        )
    scale_q = lax.rsqrt(total_q / width + EPSILON)[:, None, None]
    scale_k = lax.rsqrt(total_k / width + EPSILON)[:, None, None]
    gain_q, gain_k = gain_q.reshape(heads, HD), gain_k.reshape(heads, HD)
    cosine, sine = cosine[:, None, :], sine[:, None, :]
    if not here:
        query = rotate(query_raw * scale_q * gain_q, cosine, sine).astype(BF16)
        key = rotate(key_raw * scale_k * gain_k, cosine, sine).astype(BF16)
        moved = rows_to_heads(jnp.concatenate([query, key, value_raw.astype(BF16)], axis=-1))
        query, own_pair = moved[:, :HD], moved[:, HD:]
        earlier_pair = from_behind(own_pair, "exp", 1)
        lower_pair = jnp.where(side == 0, own_pair, earlier_pair)
        upper_pair = jnp.where(side == 0, jnp.zeros_like(own_pair), own_pair)
        key_value = jnp.concatenate([lower_pair, upper_pair], axis=0)
        key_all, value_all = key_value[:, :HD], key_value[:, HD:]

    if here:
        mixed_wide, total, out_w, mixed_rows, middle, normed_two = attention_stage(
            query, key_all, value_all, doc_cuts, w_out, hidden_in[0], gains, scale, 4
        )
    else:
        mixed_wide, total = attend(query, key_all, value_all, cuts, scale)
        mixed = mixed_wide.astype(BF16)
        middle = tokens + matmul(heads_to_tokens(mixed), out_w)

    gain_two = moe_gain.astype(F32)
    scale_two = rms_scale(middle)
    if not here:
        normed_two = (middle * scale_two * gain_two).astype(BF16)
    gates_all = jax.nn.softmax(matmul(normed_two, router), axis=-1)
    picks = routes[0]
    chosen = jnp.any(
        picks[:, :, None] == jnp.arange(router.shape[1], dtype=jnp.int32)[None, None, :], axis=1
    )
    grad_out = out_grad[0].astype(F32)
    expert_w = (w_gate[0], w_up[0], w_down[0])
    if here:
        out_parts, d_normed_two, inner, weight_grads = experts_here(
            normed_two, grads_all, picks, router, expert_w, other_w
        )
    else:
        dense_gates = jnp.where(chosen, gates_all, 0.0)
        mixture, d_normed_two, inner, weight_grads = experts(
            normed_two, out_grad[0], dense_gates, *expert_w
        )
    dense = jnp.where(chosen, inner, 0.0)
    d_logits = (gates_all * (dense - jnp.sum(gates_all * dense, axis=-1, keepdims=True))).astype(BF16)
    grad_router = contract_rows(d_logits, normed_two)
    d_normed_two = d_normed_two + contract_cols(d_logits, router)
    grad_moe_gain = jnp.sum(d_normed_two * middle * scale_two, axis=0)
    weighted_two = d_normed_two * gain_two
    d_middle = (
        grad_out
        + scale_two * weighted_two
        - middle * scale_two**3 * jnp.mean(weighted_two * middle, axis=-1, keepdims=True)
    )

    d_attn = d_middle.astype(BF16)
    if here:
        early = jnp.concatenate([grad_moe_gain[None], jnp.zeros((7, width), F32), grad_router])
        d_attn_row, d_heads, mixture, early = attend_back_stage(
            d_attn, query, key_all, value_all, mixed_wide, total, doc_cuts, out_w, out_parts, early, scale, 2
        )
        grad_hidden, grads, late, last = tail_stage(
            d_heads, qkv.reshape(row_tok, -1), totals, gains, cosine[:, 0], signed,
            qkv_w, normed_row, mixed_rows, d_attn_row, hidden_in[0], 3,
        )
        grad_hidden = d_middle + grad_hidden
        grad_qkv = grads[:, : 3 * plane].astype(F32)
        grad_w_out = grads[:, 3 * plane :].astype(F32)
        weight_grads = [value.astype(F32) for value in weight_grads]
        final = middle + mixture.astype(F32)
        summed = (last.reshape(-1), late[0], late[1], early[0], early[8:])
    else:
        final = middle + mixture
        mixed_row = heads_to_rows(mixed).reshape(row_tok, plane)
        d_mixed = tokens_to_heads(contract_cols(d_attn, out_w).astype(BF16))
        d_attn_row = lax.all_gather(d_attn, "col", axis=0, tiled=True)
        d_query, acc_key, acc_value = attend_back(
            query, key_all, value_all, d_mixed, mixed_wide, total, cuts, scale
        )
        accumulated = jnp.concatenate([acc_key, acc_value], axis=1)
        lower_acc, upper_acc = accumulated[:group_tok], accumulated[group_tok:]
        kept_acc = jnp.where(side == 0, lower_acc, upper_acc)
        later_acc = from_behind(lower_acc.astype(BF16), "exp", -1).astype(F32)
        summed_pair = kept_acc + jnp.where(side == 0, later_acc, jnp.zeros_like(later_acc))
        d_heads = heads_to_rows(jnp.concatenate([d_query, summed_pair], axis=1).astype(BF16)).astype(F32)
        d_q_unit = rotate_back(d_heads[:, :, :HD], cosine, sine)
        d_k_unit = rotate_back(d_heads[:, :, HD : 2 * HD], cosine, sine)
        d_value = d_heads[:, :, 2 * HD :]
        weighted_q = d_q_unit * gain_q
        weighted_k = d_k_unit * gain_k
        sum_q, sum_k = lax.psum(
            (jnp.sum(weighted_q * query_raw, axis=(1, 2)), jnp.sum(weighted_k * key_raw, axis=(1, 2))),
            "col",
        )
        d_query_raw = scale_q * weighted_q - query_raw * scale_q**3 * (sum_q / width)[:, None, None]
        d_key_raw = scale_k * weighted_k - key_raw * scale_k**3 * (sum_k / width)[:, None, None]
        grad_q_part = jnp.sum(d_q_unit * query_raw * scale_q, axis=0).reshape(plane)
        grad_k_part = jnp.sum(d_k_unit * key_raw * scale_k, axis=0).reshape(plane)
        d_qkv = jnp.concatenate([d_query_raw, d_key_raw, d_value], axis=2).astype(BF16)
        d_qkv = d_qkv.reshape(row_tok, heads * 3 * HD)
        d_normed_one = lax.psum_scatter(
            contract_cols(d_qkv, qkv_w).astype(BF16), "col", scatter_dimension=0, tiled=True
        ).astype(F32)
        grad_qkv = lax.psum_scatter(
            contract_rows(normed_row, d_qkv).astype(BF16), "row", scatter_dimension=0, tiled=True
        )
        grad_w_out = lax.psum_scatter(
            contract_rows(mixed_row, d_attn_row).astype(BF16), "row", scatter_dimension=1, tiled=True
        )
        grad_qkv = lax.psum(grad_qkv, "exp").astype(F32)
        grad_w_out = lax.psum(grad_w_out, "exp").astype(F32)
        grad_attn_gain = jnp.sum(d_normed_one * tokens * scale_one, axis=0)
        weighted_one = d_normed_one * gain_one
        grad_hidden = (
            d_middle
            + scale_one * weighted_one
            - tokens * scale_one**3 * jnp.mean(weighted_one * tokens, axis=-1, keepdims=True)
        )
        empty = jnp.zeros((width,), F32)
        grad_q_full = lax.dynamic_update_slice_in_dim(empty, grad_q_part, head_start, 0)
        grad_k_full = lax.dynamic_update_slice_in_dim(empty, grad_k_part, head_start, 0)
        parts = (grad_attn_gain, grad_q_full, grad_k_full, grad_moe_gain)
        summed = lax.psum(parts + (grad_router,), ALL)
    return (
        final.astype(BF16)[None],
        grad_hidden[None],
        summed[0],
        grad_qkv,
        summed[1],
        summed[2],
        grad_w_out,
        summed[3],
        summed[4].T,
        weight_grads[0][None],
        weight_grads[1][None],
        weight_grads[2][None],
    )


def solution(mesh):
    token_spec = P("exp", ("row", "col"), None)
    expert_spec = P(("row", "col", "exp"), None, None)
    in_specs = (
        token_spec,
        token_spec,
        P(),
        P("row", "col"),
        P(),
        P(),
        P("col", "row"),
        P(),
        P(),
        expert_spec,
        expert_spec,
        expert_spec,
        token_spec,
        P(),
    )
    out_specs = (
        token_spec,
        token_spec,
        P(),
        P("row", "col"),
        P(),
        P(),
        P("col", "row"),
        P(),
        P(),
        expert_spec,
        expert_spec,
        expert_spec,
    )
    return jax.shard_map(shards, mesh=mesh, in_specs=in_specs, out_specs=out_specs, check_vma=False)
```
